128 devices in a mesh: wide: 16 (over y, x_lo, core), narrow: 8 (over z, x_hi).
Axes of the slice: x: 4 (x_hi: 2, x_lo: 2; x = x_hi * 2 + x_lo), y: 4, z: 4, core: 2. Of those that a mesh axis runs over, the one named last changes fastest.
Arguments:
- tokens: bfloat16 [2, 2048, 768], P(None, 'wide'), may hold values from -6 to 6
- scene_of_block: int32 [2, 32], replicated, may hold values from 0 to 3, as said below
- ln1_gain: float32 [768], replicated, may hold values from 0.1 to 1.9
- ln1_shift: float32 [768], replicated, may hold values from -3 to 3
- w_qkv: bfloat16 [768, 2304], replicated, may hold values from -0.21875 to 0.21875
- w_out: bfloat16 [768, 768], replicated, may hold values from -6 to 6
- ln2_gain: float32 [768], replicated, may hold values from 0.1 to 1.9
- ln2_shift: float32 [768], replicated, may hold values from -3 to 3
- w_up: bfloat16 [768, 3072], P(None, 'narrow'), may hold values from -0.21875 to 0.21875
- w_down: bfloat16 [3072, 768], P('narrow'), may hold values from -0.109375 to 0.109375
- out_grad: bfloat16 [2, 2048, 768], P(None, 'wide'), may hold values from -6 to 6
Outputs:
- result: bfloat16 [2, 2048, 768], P(None, 'wide')
- input_grad: float32 [2, 2048, 768], P(None, 'wide')
- qkv_grad: float32 [768, 2304], replicated
- out_proj_grad: float32 [768, 768], replicated
- ln1_gain_grad: float32 [768], replicated
- ln1_shift_grad: float32 [768], replicated
- ln2_gain_grad: float32 [768], replicated
- ln2_shift_grad: float32 [768], replicated
- up_grad: float32 [768, 3072], P(None, 'narrow')
- down_grad: float32 [3072, 768], P('narrow')
The draws below stay inside these ranges and needn't reach their ends.
Inputs may be any that keep to these rules, and one draw needn't show every extreme that they name: `scene_of_block`: in each micro-batch the scene ids never fall along the blocks, so each scene is one contiguous span of blocks. One scene, drawn from the seed, holds 32 - 3 * (4) blocks; each of the others holds 4 blocks.
All inputs are finite; a program needn't handle non-finite values.
Results may differ from the reference program's by a relative error of at most 0.023.
Values may be sent and summed in bfloat16 or wider, within the bound.
No kernel may reach another device: no remote copies, remote signals or barrier semaphores. Data moves between devices by JAX's collectives and lax.ppermute only.
A program may use at most 128 MiB of HBM per device.

```python
from functools import partial
import jax
import jax.numpy as jnp
from jax import lax

D = 768
HEADS = 12
HD = 64
FF = 3072
TOK_DEV = 128
MICRO = 2
SCENES = 4
SCENE_BLOCK = 64
MB_TOK = 2048
BLOCKS = 32
N_WIDE = 16


def draw_scene_of_block(key, part):
    key = jax.random.fold_in(key, 7)
    small = BLOCKS // (SCENES + 3)
    large = BLOCKS - (SCENES - 1) * small
    index = jnp.arange(BLOCKS, dtype=jnp.int32)
    rows = []
    for micro in range(MICRO):
        sub = jax.random.fold_in(key, micro)
        biggest = jax.random.randint(sub, (), 0, SCENES)
        sizes = jnp.where(jnp.arange(SCENES, dtype=jnp.int32) == biggest, large, small).astype(jnp.int32)
        ends = jnp.cumsum(sizes).astype(jnp.int32)
        labels = jnp.sum((index[:, None] >= ends[None, :]).astype(jnp.int32), axis=1)
        rows.append(labels)
    return jnp.stack(rows).astype(jnp.int32)


def block_scale(rng, shape, split, smallest, high):
    loudness = 1.0
    for dim, blocks in split:
        draws = jax.random.uniform(jax.random.fold_in(jax.random.fold_in(rng, 6), dim), (blocks,), jnp.float32, smallest / len(split), high / len(split))
        loudness = loudness * jnp.repeat(jnp.exp(draws), shape[dim] // blocks).reshape((-1,) + (1,) * (len(shape) - 1 - dim))
    return loudness


def centred(stream_key, dims, deviation, bound, pieces=(), held_as=jnp.bfloat16):
    result = deviation * jax.random.normal(stream_key, dims, jnp.float32)
    if pieces:
        result = result * block_scale(stream_key, dims, pieces, -0.22, 0.18)
    return jnp.clip(result, -bound, bound).astype(held_as)


def setup_inputs(seed: int = 0) -> dict:
    seeds = jax.random.split(jax.random.key(seed), 12)
    tokens = centred(seeds[0], (MICRO, MB_TOK, D), 1.0, 6.0, ((1, 16),))
    scene_of_block = draw_scene_of_block(jax.random.fold_in(seeds[11], 71), 0)
    ln1_gain = jnp.clip(1.0 + 0.18 * jax.random.normal(seeds[2], (D,), jnp.float32), 0.1, 1.9)
    ln1_shift = centred(seeds[3], (D,), 0.3, 3.0, (), jnp.float32)
    w_qkv = centred(seeds[4], (D, 3 * D), D ** -0.5, 0.21875)
    w_out = centred(seeds[5], (D, D), (max(1, (4 * D) // (TOK_DEV * N_WIDE))) ** -0.5, 6.0)
    ln2_gain = jnp.clip(1.0 + 0.18 * jax.random.normal(seeds[6], (D,), jnp.float32), 0.1, 1.9)
    ln2_shift = centred(seeds[7], (D,), 0.3, 3.0, (), jnp.float32)
    w_up = centred(seeds[8], (D, FF), D ** -0.5, 0.21875, ((1, 8),))
    w_down = centred(seeds[9], (FF, D), FF ** -0.5, 0.109375, ((0, 8),))
    out_grad = centred(seeds[10], (MICRO, MB_TOK, D), 1.0, 6.0, ((1, 16),))
    return dict(tokens=tokens, scene_of_block=scene_of_block, ln1_gain=ln1_gain, ln1_shift=ln1_shift, w_qkv=w_qkv, w_out=w_out, ln2_gain=ln2_gain, ln2_shift=ln2_shift, w_up=w_up, w_down=w_down, out_grad=out_grad)


@jax.custom_vjp
def low(v):
    return lax.optimization_barrier(v.astype(jnp.bfloat16)).astype(jnp.float32)

@jax.custom_vjp
def low_back(v):
    return v

def low_keep(v):
    return (low(v), None)

def low_pass(kept, grad):
    return (grad,)

def back_keep(v):
    return (v, None)

def back_low(kept, grad):
    return (low(grad),)
low.defvjp(low_keep, low_pass)
low_back.defvjp(back_keep, back_low)
EPS = 1e-05
HIGH = lax.Precision.HIGHEST

def layer_norm(values, gain, shift):
    center = values - lax.optimization_barrier(jnp.mean(values, axis=-1, keepdims=True))
    spread = lax.optimization_barrier(jnp.mean(center * center, axis=-1, keepdims=True))
    return center * lax.rsqrt(spread + EPS) * gain + shift

def head_mix(parts, same):
    query, keys, values = parts
    scores = low_back(jnp.dot(query, keys.T, precision=HIGH) * HD ** (-0.5))
    probs = jax.nn.softmax(jnp.where(same, scores, -1e+30), axis=-1)
    return jnp.dot(low(probs), values, precision=HIGH)

def micro_forward(inputs, scene_tok, params):
    ln1_gain, ln1_shift, w_qkv, w_out, ln2_gain, ln2_shift, w_up, w_down = params
    normed = low(layer_norm(inputs, ln1_gain, ln1_shift))
    qkv = low(low_back(jnp.dot(normed, w_qkv, precision=HIGH)))
    heads = []
    for index in range(3):
        block = qkv[:, index * D:(index + 1) * D].reshape(MB_TOK, HEADS, HD)
        heads.append(jnp.transpose(block, (1, 0, 2)))
    same = scene_tok[:, None] == scene_tok[None, :]
    mixed_heads = lax.map(jax.checkpoint(partial(head_mix, same=same)), (heads[0], heads[1], heads[2]))
    mixed = jnp.transpose(mixed_heads, (1, 0, 2)).reshape(MB_TOK, D)
    mixed = low(low_back(mixed))
    middle = inputs + low_back(jnp.dot(mixed, w_out, precision=HIGH))
    normed2 = low(layer_norm(middle, ln2_gain, ln2_shift))
    pre = low_back(jnp.dot(normed2, w_up, precision=HIGH))
    act = low(jax.nn.gelu(pre, approximate=False))
    return middle + low_back(jnp.dot(act, w_down, precision=HIGH))

def reference(tokens, scene_of_block, ln1_gain, ln1_shift, w_qkv, w_out, ln2_gain, ln2_shift, w_up, w_down, out_grad):
    scene_tok = jnp.repeat(scene_of_block, SCENE_BLOCK, axis=1).astype(jnp.int32)
    params = (ln1_gain, ln1_shift, w_qkv.astype(jnp.float32), w_out.astype(jnp.float32), ln2_gain, ln2_shift, w_up.astype(jnp.float32), w_down.astype(jnp.float32))
    inputs = tokens.astype(jnp.float32)

    def whole(values, weights):
        return jnp.stack([micro_forward(values[m], scene_tok[m], weights) for m in range(MICRO)])
    output, pullback = jax.vjp(whole, inputs, params)
    grad_in, grads = pullback(out_grad.astype(jnp.float32))
    g_ln1, s_ln1, g_qkv, g_out, g_ln2, s_ln2, g_up, g_down = grads
    return (output.astype(jnp.bfloat16), grad_in, g_qkv, g_out, g_ln1, s_ln1, g_ln2, s_ln2, g_up, g_down)
```

```python
import functools

import jax
import jax.numpy as jnp
from jax import lax
from jax.experimental import pallas as pl
from jax.experimental.pallas import tpu as pltpu
from jax.sharding import Mesh
from jax.sharding import PartitionSpec as P

D = 768
HD = 64
FFL = 384
TOK = 128
BLK = 32
EPS = 1e-05
BF = jnp.bfloat16
F32 = jnp.float32

CHIP = ("y", "xl")
CORE = "c"
MICRO = "zh"
GROUP = ("zl", "xh")
NARROW = (MICRO, *GROUP)
WIDE = (*CHIP, CORE)


def chip_index():
    return lax.axis_index("y") * 2 + lax.axis_index("xl")


def group_index():
    return lax.axis_index("zl") * 2 + lax.axis_index("xh")


def mm(left, right):
    return lax.dot_general(left, right, (((1,), (0,)), ((), ())), preferred_element_type=F32)


def mm_nt(left, right):
    return lax.dot_general(left, right, (((1,), (1,)), ((), ())), preferred_element_type=F32)


def mm_tn(left, right):
    return lax.dot_general(left, right, (((0,), (0,)), ((), ())), preferred_element_type=F32)


def normalized(values):
    center = values - jnp.mean(values, axis=-1, keepdims=True)
    spread = jnp.mean(center * center, axis=-1, keepdims=True)
    inverse = lax.rsqrt(spread + EPS)
    return center * inverse, inverse


def norm_back(grad, unit, inverse, gain):
    scaled = grad * gain
    first = jnp.mean(scaled, axis=-1, keepdims=True)
    second = jnp.mean(scaled * unit, axis=-1, keepdims=True)
    return inverse * (scaled - first - unit * second)


def halves(block):
    lane = lax.broadcasted_iota(jnp.int32, block.shape, 1)
    zero = jnp.zeros_like(block)
    return jnp.where(lane < HD, block, zero), jnp.where(lane < HD, zero, block)


def join(low, high):
    lane = lax.broadcasted_iota(jnp.int32, low.shape, 1)
    return jnp.where(lane < HD, low, high)


def span(scene_ref):
    micro = lax.axis_index(MICRO)
    own = scene_ref[micro, chip_index() * 4]
    first = jnp.int32(0)
    count = jnp.int32(0)
    for index in range(8):
        other = scene_ref[micro, index * 4]
        first += (other < own).astype(jnp.int32)
        count += (other == own).astype(jnp.int32)
    return first, count > 1


def three(value):
    a = value.astype(BF).astype(F32)
    b = (value - a).astype(BF).astype(F32)
    c = value - a - b
    return a, b, c


def put_columns(width, rows, start, columns):
    lane = lax.broadcasted_iota(jnp.int32, (rows, width), 1)
    out = jnp.zeros((rows, width), F32)
    for offset, column in enumerate(columns):
        out = jnp.where(lane == start + offset, column, out)
    return out


def call(kernel, outs, ins, cost, scratch=(), smem=0):
    specs = [pl.BlockSpec(memory_space=pltpu.SMEM)] * smem + [
        pl.BlockSpec(memory_space=pl.ANY) if any_space else pl.BlockSpec(memory_space=pltpu.VMEM)
        for any_space in [isinstance(value, tuple) for value in ins[smem:]]
    ]
    values = [value[0] if isinstance(value, tuple) else value for value in ins]
    return pl.pallas_call(
        kernel,
        out_shape=[jax.ShapeDtypeStruct(shape, dtype) for shape, dtype in outs],
        in_specs=specs,
        out_specs=[pl.BlockSpec(memory_space=pltpu.VMEM)] * len(outs),
        scratch_shapes=list(scratch),
        cost_estimate=pl.CostEstimate(flops=cost, bytes_accessed=2000000, transcendentals=0),
        compiler_params=pltpu.CompilerParams(vmem_limit_bytes=40 * 2**20),
    )(*values)


def project_kernel(tok_ref, gain_ref, shift_ref, w_ref, kv_ref, q_ref, normed_ref, x_buf, w_buf, x_sem, w_sem):
    micro = lax.axis_index(MICRO)
    group = group_index()
    copy_x = pltpu.make_async_copy(tok_ref.at[micro], x_buf, x_sem)
    copy_x.start()
    copies = []
    for slot, part in enumerate((1, 2, 0)):
        column = pl.multiple_of(part * D + (group // 2) * 384, 128)
        copy = pltpu.make_async_copy(w_ref.at[:, pl.ds(column, 384)], w_buf.at[slot], w_sem.at[slot])
        copy.start()
        copies.append(copy)
    copy_x.wait()
    unit, _ = normalized(x_buf[...].astype(F32))
    normed = (unit * gain_ref[...] + shift_ref[...]).astype(BF)
    normed_ref[...] = normed
    odd = (group % 2) == 1
    parts = []
    for slot in range(3):
        copies[slot].wait()
        full = mm(normed, w_buf[slot])
        parts.append(jnp.where(odd, full[:, 192:], full[:, :192]).astype(BF))
    kv = jnp.concatenate(parts[:2], axis=1)
    query = jnp.concatenate([parts[2], jnp.zeros((TOK, 64), BF)], axis=1)
    for chip in range(8):
        kv_ref[chip] = kv
        q_ref[chip] = query


def attend_kernel(scene_ref, q_ref, same_ref, other_ref, out_ref):
    first, big = span(scene_ref)

    def run(count):
        rows = count * TOK
        keys = jnp.concatenate(
            [ref[pl.ds(first, count)].reshape(rows, 384) for ref in (same_ref, other_ref)], axis=0
        )
        query = q_ref[0]
        q0, q1 = halves(query[:, :128])
        blocks = [keys[:, :128], keys[:, 128:256], keys[:, 256:]]
        mixed = []
        columns = []
        for qh, kb, vb in ((q0, 0, 1), (q1, 0, 2), (query[:, 128:], 1, 2)):
            scores = mm_nt(qh, blocks[kb]) * (HD**-0.5)
            top = jnp.max(scores, axis=-1, keepdims=True)
            weights = jnp.exp(scores - top)
            total = jnp.sum(weights, axis=-1, keepdims=True)
            probs = (weights * (1.0 / total)).astype(BF)
            mixed.append(mm(probs, blocks[vb]))
            columns += three(top + jnp.log(total))
        stats = put_columns(128, TOK, 0, columns)
        packed = jnp.concatenate([join(stats, mixed[0]), join(mixed[1], mixed[2])], axis=1).astype(BF)
        for index in range(8):
            out_ref[index] = packed

    @pl.when(big)
    def _():
        run(5)

    @pl.when(jnp.logical_not(big))
    def _():
        run(1)


def forward_kernel(
    mixed_ref, tok_ref, og_ref, wo_ref, gain_ref, shift_ref, up_ref, down_ref,
    out_ref, middle_ref, normed_ref, act_ref, gpre_ref,
):
    x = tok_ref[...].reshape(2 * TOK, D).astype(F32)
    total = x
    for group in range(4):
        rows = jnp.concatenate([mixed_ref[group], mixed_ref[4 + group]], axis=0)
        total = total + mm(rows, wo_ref[group])
    middle_ref[...] = total.reshape(8, BLK, D)
    unit, _ = normalized(total)
    normed = (unit * gain_ref[...] + shift_ref[...]).astype(BF)
    normed_ref[...] = normed
    pre = mm(normed, up_ref[...])
    cdf = 0.5 * (1.0 + lax.erf(pre * (0.5**0.5)))
    act = (pre * cdf).astype(BF)
    act_ref[...] = act
    slope = cdf + pre * jnp.exp(-0.5 * pre * pre) * 0.3989422804014327
    grad_out = og_ref[...].reshape(2 * TOK, D)
    gpre = (mm_nt(grad_out, down_ref[...]) * slope).astype(BF)
    gpre_ref[...] = gpre
    grad = mm_nt(gpre, up_ref[...]).astype(BF).reshape(8, BLK, D)
    branch = mm(act, down_ref[...]).astype(BF).reshape(8, BLK, D)
    out_ref[:, :BLK] = branch
    out_ref[:, BLK:] = grad


def ff_grads_kernel(normed_ref, act_ref, gpre_ref, og_ref, out_ref):
    up = mm_tn(normed_ref[...], gpre_ref[...]).astype(BF)
    grad_out = og_ref[...].reshape(2 * TOK, D)
    down = mm_tn(act_ref[...], grad_out).astype(BF)
    for tile in range(16):
        half = (tile % 2) * 384
        out_ref[tile, :, :384] = up[tile * 48:(tile + 1) * 48]
        out_ref[tile, :, 384:] = down[(tile // 2) * 48:(tile // 2 + 1) * 48, half:half + 384]


def middle_kernel(
    sums_ref, middle_ref, og_ref, mixed_ref, wo_ref, gain_ref, out_ref, rest_ref
):
    micro = lax.axis_index(MICRO)
    group = group_index()
    start = pl.multiple_of(group * BLK, BLK)
    total = sums_ref[0].astype(F32)
    for index in range(1, 8):
        total = total + sums_ref[index].astype(F32)
    branch, grad = total[:BLK], total[BLK:]
    middle = middle_ref[micro * 4 + group]
    unit, inverse = normalized(middle)
    grad_mid = og_ref[micro, pl.ds(start, BLK)].astype(F32) + norm_back(grad, unit, inverse, gain_ref[...])
    low = grad_mid.astype(BF)
    for head_group in range(4):
        mixed = mixed_ref[micro * 4 + head_group, pl.ds(start, BLK)].astype(F32)
        back = mm_nt(low, wo_ref[head_group]).astype(BF).astype(F32)
        lane = lax.broadcasted_iota(jnp.int32, (BLK, 256), 1)
        product = mixed * back
        columns = []
        for head in range(3):
            inside = (lane >= (head + 1) * HD) & (lane < (head + 2) * HD)
            columns += three(jnp.sum(jnp.where(inside, product, 0.0), axis=-1, keepdims=True))
        stats = put_columns(256, BLK, 9, columns)
        packed = jnp.where(lane < 9, mixed, jnp.where(lane < HD, stats, back)).astype(BF)
        for chip in range(8):
            out_ref[chip * 4 + head_group] = packed
    result = (middle + branch).astype(BF)
    gain_grad = jnp.sum(grad * unit, axis=0, keepdims=True)
    shift_grad = jnp.sum(grad, axis=0, keepdims=True)
    vectors = jnp.concatenate([gain_grad, shift_grad, jnp.zeros((14, D), F32)], axis=0).astype(BF)
    for index in range(8):
        rest_ref[index, :BLK] = result
        rest_ref[index, BLK:2 * BLK] = low
        rest_ref[index, 2 * BLK:] = vectors


def attend_back_kernel(
    scene_ref, kvs_ref, kvo_ref, qs_ref, qo_ref, gs_ref, go_ref, out_ref
):
    first, big = span(scene_ref)
    chip = chip_index()
    scale = HD**-0.5

    def run(count):
        rows = count * TOK

        def gathered(one, two, width):
            return jnp.concatenate(
                [ref[pl.ds(first, count)].reshape(rows, width) for ref in (one, two)], axis=0
            )

        def cut(value):
            return [value[:, at:at + 128] for at in range(0, value.shape[1], 128)]

        kv = cut(gathered(kvs_ref, kvo_ref, 384))
        query = cut(gathered(qs_ref, qo_ref, 256))
        grad = cut(gathered(gs_ref, go_ref, 256))
        kv_own = cut(kvs_ref[chip])
        q_own = cut(qs_ref[chip])
        g_own = cut(gs_ref[chip])
        q_heads = [*halves(q_own[0]), q_own[1]]
        g_heads = [halves(g_own[0])[1], *halves(g_own[1])]
        k_heads = [*halves(kv_own[0]), halves(kv_own[1])[0]]
        v_heads = [halves(kv_own[1])[1], *halves(kv_own[2])]
        own_stats = g_own[0].astype(F32)
        all_stats = grad[0].astype(F32).T

        def column(at):
            return own_stats[:, at:at + 1] + own_stats[:, at + 1:at + 2] + own_stats[:, at + 2:at + 3]

        def row(at):
            return all_stats[at:at + 1] + all_stats[at + 1:at + 2] + all_stats[at + 2:at + 3]

        dq, dk, dv = [], [], []
        for head, (kb, vb) in enumerate(((0, 1), (0, 2), (1, 2))):
            qb, gb = (0, 0, 1)[head], (0, 1, 1)[head]
            probs = jnp.exp(mm_nt(q_heads[head], kv[kb]) * scale - column(3 * head))
            gap = mm_nt(g_heads[head], kv[vb]) - column(9 + 3 * head)
            dq.append(mm((probs * gap).astype(BF), kv[kb]) * scale)
            probs = jnp.exp(mm_nt(k_heads[head], query[qb]) * scale - row(3 * head))
            gap = mm_nt(v_heads[head], grad[gb]) - row(9 + 3 * head)
            dv.append(mm(probs.astype(BF), grad[gb]))
            dk.append(mm((probs * gap).astype(BF), query[qb]) * scale)
        packed = jnp.concatenate(
            [join(dk[0], dk[1]), join(dk[2], dv[0]), join(dv[1], dv[2]), join(dq[0], dq[1]), dq[2][:, :HD]],
            axis=1,
        ).astype(BF)
        for index in range(8):
            out_ref[index] = packed

    @pl.when(big)
    def _():
        run(5)

    @pl.when(jnp.logical_not(big))
    def _():
        run(1)


def weight_grads_kernel(gqkv_ref, normed_ref, mixed_ref, rest_ref, out_ref):
    index = lax.axis_index(MICRO) * 4 + group_index()
    grad = mm_tn(normed_ref[...], gqkv_ref[0])
    low = jnp.concatenate([rest_ref[lax.axis_index(MICRO) * 4 + b, BLK:2 * BLK] for b in range(4)], axis=0)
    out = mm_tn(mixed_ref[index], low)[HD:]
    for tile in range(16):
        rows = grad[tile * 48:(tile + 1) * 48]
        at, column = (tile // 4) * 48, (tile % 4) * 192
        out_ref[2 * tile] = rows[:, :384].astype(BF)
        out_ref[2 * tile + 1] = jnp.concatenate(
            [rows[:, 384:], out[at:at + 48, column:column + 192]], axis=1
        ).astype(BF)


def sum_kernel(parts, copies, in_ref, out_ref):
    total = in_ref[0].astype(F32)
    for index in range(1, parts):
        total = total + in_ref[index].astype(F32)
    total = total.astype(BF)
    for index in range(copies):
        out_ref[index] = total


def spread_kernel(same_ref, other_ref, qkv_ref, out_ref):
    swapped = lax.axis_index(CORE) == 1
    same, other = same_ref[0], other_ref[0]
    for core in range(2):
        block = jnp.where(swapped, other, same) if core == 0 else jnp.where(swapped, same, other)
        block = block.astype(F32)
        rows = slice(core * 48, (core + 1) * 48)
        for part, half, at in ((1, 0, 0), (2, 0, 192), (0, 1, 0)):
            qkv_ref[rows, part * D:(part + 1) * D] = jnp.concatenate(
                [block[half * 4 + group][:, at:at + 192] for group in range(4)], axis=1
            )
        for group in range(4):
            out_ref[group, 0, :, core * 192:(core + 1) * 192] = block[4 + group][:, 192:]


def spread_ff_kernel(same_ref, other_ref, up_ref, down_ref):
    swapped = lax.axis_index(CORE) == 1
    for chip in range(8):
        same, other = same_ref[chip], other_ref[chip]
        for core in range(2):
            block = jnp.where(swapped, other, same) if core == 0 else jnp.where(swapped, same, other)
            block = block.astype(F32)
            tile = chip * 2 + core
            up_ref[tile * 48:(tile + 1) * 48] = block[:, :384]
            down_ref[chip * 48:(chip + 1) * 48, core * 384:(core + 1) * 384] = block[:, 384:]


def input_kernel(gqkv_ref, rest_ref, tok_ref, w_ref, gain_ref, grad_ref, result_ref, vec_ref):
    total = jnp.zeros((2 * TOK, D), F32)
    for part, at in ((1, 0), (2, 192), (0, 384)):
        for pair in range(2):
            rows = jnp.concatenate(
                [
                    jnp.concatenate(
                        [gqkv_ref[micro * 4 + pair * 2 + k][:, at:at + 192] for k in range(2)], axis=1
                    )
                    for micro in range(2)
                ],
                axis=0,
            )
            column = part * D + pair * 384
            total = total + mm_nt(rows, w_ref[:, column:column + 384])
    unit, inverse = normalized(tok_ref[...].reshape(2 * TOK, D).astype(F32))
    grad_mid = rest_ref[:, BLK:2 * BLK].reshape(2 * TOK, D).astype(F32)
    grad_ref[...] = (grad_mid + norm_back(total, unit, inverse, gain_ref[...])).reshape(2, TOK, D)
    result_ref[...] = rest_ref[:, :BLK].reshape(2, TOK, D)
    gain1 = jnp.sum(total * unit, axis=0, keepdims=True)
    shift1 = jnp.sum(total, axis=0, keepdims=True)
    second = rest_ref[:, 2 * BLK:].astype(F32)
    sums = second[0]
    for index in range(1, 8):
        sums = sums + second[index]
    vectors = jnp.concatenate([gain1, shift1, sums[:2], jnp.zeros((4, D), F32)], axis=0)
    for index in range(16):
        vec_ref[index] = vectors


def vectors_kernel(in_ref, a_ref, b_ref, c_ref, d_ref):
    total = in_ref[0]
    for index in range(1, 16):
        total = total + in_ref[index]
    for row, ref in enumerate((a_ref, b_ref, c_ref, d_ref)):
        ref[...] = total[row:row + 1]


def exchange(value, axes):
    return lax.all_to_all(value, axes, 0, 0, tiled=True)


def swap(value):
    return lax.ppermute(value, CORE, [(0, 1), (1, 0)])


def shards(
    tokens, scene_of_block, ln1_gain, ln1_shift, w_qkv, w_out, ln2_gain, ln2_shift, w_up, w_down, out_grad
):
    ln1_gain, ln1_shift, ln2_gain, ln2_shift = (
        value.reshape(1, D) for value in (ln1_gain, ln1_shift, ln2_gain, ln2_shift)
    )
    w_out_pad = jnp.pad(w_out.reshape(4, 192, D), ((0, 0), (HD, 0), (0, 0)))
    kv_send, q_send, normed = call(
        project_kernel,
        [((8, TOK, 384), BF), ((8, TOK, 256), BF), ((TOK, D), BF)],
        [(tokens,), ln1_gain, ln1_shift, (w_qkv,)],
        10**9,
        [
            pltpu.VMEM((TOK, D), BF),
            pltpu.VMEM((3, D, 384), BF),
            pltpu.SemaphoreType.DMA,
            pltpu.SemaphoreType.DMA((3,)),
        ],
    )
    kv_same = exchange(kv_send, CHIP)
    kv_other = swap(kv_same)
    (mixed_send,) = call(
        attend_kernel,
        [((8, TOK, 256), BF)],
        [scene_of_block, q_send, kv_same, kv_other],
        2 * 10**9,
        smem=1,
    )
    mixed = exchange(mixed_send, NARROW)
    q_send, _ = lax.optimization_barrier((q_send, mixed_send))
    q_same = exchange(q_send, CHIP)
    q_other = swap(q_same)
    ff_send, middle, normed2, act, grad_pre = call(
        forward_kernel,
        [
            ((8, 2 * BLK, D), BF),
            ((8, BLK, D), F32),
            ((2 * TOK, D), BF),
            ((2 * TOK, FFL), BF),
            ((2 * TOK, FFL), BF),
        ],
        [mixed, tokens, out_grad, w_out_pad, ln2_gain, ln2_shift, w_up, w_down],
        4 * 10**9,
    )
    ff_sums = exchange(ff_send, NARROW)
    (ff_grads,) = call(
        ff_grads_kernel, [((16, 48, D), BF)], [normed2, act, grad_pre, out_grad], 2 * 10**9
    )
    ff_grads = exchange(ff_grads, WIDE)
    grad_send, rest_send = call(
        middle_kernel,
        [((32, BLK, 256), BF), ((8, 80, D), BF)],
        [ff_sums, middle, out_grad, mixed, w_out_pad, ln2_gain],
        10**9,
    )
    grad_same = exchange(grad_send, (*CHIP, *GROUP)).reshape(8, TOK, 256)
    grad_other = swap(grad_same)
    rest_send, _ = lax.optimization_barrier((rest_send, grad_same))
    rest = exchange(rest_send, NARROW)
    (ff_total,) = call(functools.partial(sum_kernel, 16, 8), [((8, 48, D), BF)], [ff_grads], 10**8)
    ff_total, _ = lax.optimization_barrier((ff_total, grad_same))
    ff_same = exchange(ff_total, CHIP)
    ff_other = swap(ff_same)
    (gqkv_send,) = call(
        attend_back_kernel,
        [((8, TOK, 576), BF)],
        [scene_of_block, kv_same, kv_other, q_same, q_other, grad_same, grad_other],
        8 * 10**9,
        smem=1,
    )
    (weight_send,) = call(
        weight_grads_kernel, [((32, 48, 384), BF)], [gqkv_send, normed, mixed, rest], 10**9
    )
    weight_parts = exchange(weight_send, (*CHIP, CORE, MICRO))
    gqkv_send, _ = lax.optimization_barrier((gqkv_send, weight_send))
    gqkv = exchange(gqkv_send, NARROW)
    (weight_total,) = call(
        functools.partial(sum_kernel, 32, 64), [((64, 48, 384), BF)], [weight_parts], 10**8
    )
    weight_same = exchange(weight_total, (*CHIP, *NARROW)).reshape(8, 8, 48, 384)
    weight_other = swap(weight_same)
    input_grad, result, vector_send = call(
        input_kernel,
        [((2, TOK, D), F32), ((2, TOK, D), BF), ((16, 8, D), F32)],
        [gqkv, rest, tokens, w_qkv, ln1_gain],
        2 * 10**9,
    )
    vectors = exchange(vector_send, WIDE)
    gain1, shift1, gain2, shift2 = call(vectors_kernel, [((1, D), F32)] * 4, [vectors], 10**6)
    up_grad, down_grad = call(
        spread_ff_kernel, [((D, FFL), F32), ((FFL, D), F32)], [ff_same, ff_other], 10**7
    )
    qkv_grad, out_proj_grad = pl.pallas_call(
        spread_kernel,
        out_shape=[
            jax.ShapeDtypeStruct((D, 3 * D), F32),
            jax.ShapeDtypeStruct((4, 4, 48, D), F32),
        ],
        grid=(8,),
        in_specs=[pl.BlockSpec((1, 8, 48, 384), lambda p: (p, 0, 0, 0))] * 2,
        out_specs=[
            pl.BlockSpec((96, 3 * D), lambda p: (p, 0)),
            pl.BlockSpec((4, 1, 48, 384), lambda p: (0, p // 2, 0, p % 2)),
        ],
        cost_estimate=pl.CostEstimate(flops=10**7, bytes_accessed=15000000, transcendentals=0),
        compiler_params=pltpu.CompilerParams(vmem_limit_bytes=40 * 2**20),
    )(weight_same, weight_other)
    return (
        result,
        input_grad,
        qkv_grad,
        out_proj_grad.reshape(D, D),
        gain1.reshape(D),
        shift1.reshape(D),
        gain2.reshape(D),
        shift2.reshape(D),
        up_grad,
        down_grad,
    )


def solution(mesh):
    names = ("y", "xl", "c", "zh", "zl", "xh")
    fine = Mesh(mesh.devices.reshape(4, 2, 2, 2, 2, 2), names)
    tokens = P(None, WIDE, None)
    placed = (
        tokens, P(), P(), P(), P(), P(), P(), P(), P(None, NARROW), P(NARROW, None), tokens
    )
    return jax.shard_map(
        shards,
        mesh=fine,
        in_specs=placed,
        out_specs=(
            tokens, tokens, P(), P(), P(), P(), P(), P(), P(None, NARROW), P(NARROW, None)
        ),
        check_vma=False,
    )
```

```python
import functools

import jax
import jax.numpy as jnp
from jax import lax
from jax.experimental import pallas as pl
from jax.experimental.pallas import tpu as pltpu
from jax.sharding import Mesh
from jax.sharding import PartitionSpec as P

D = 768
HD = 64
FFL = 384
TOK = 128
BLK = 32
EPS = 1e-05
BF = jnp.bfloat16
F32 = jnp.float32

CHIP = ("y", "xl")
CORE = "c"
MICRO = "zh"
GROUP = ("zl", "xh")
NARROW = (MICRO, *GROUP)
WIDE = (*CHIP, CORE)


def chip_index():
    return lax.axis_index("y") * 2 + lax.axis_index("xl")


def group_index():
    return lax.axis_index("zl") * 2 + lax.axis_index("xh")


def mm(left, right):
    return lax.dot_general(left, right, (((1,), (0,)), ((), ())), preferred_element_type=F32)


def mm_nt(left, right):
    return lax.dot_general(left, right, (((1,), (1,)), ((), ())), preferred_element_type=F32)


def mm_tn(left, right):
    return lax.dot_general(left, right, (((0,), (0,)), ((), ())), preferred_element_type=F32)


def normalized(values):
    center = values - jnp.mean(values, axis=-1, keepdims=True)
    spread = jnp.mean(center * center, axis=-1, keepdims=True)
    inverse = lax.rsqrt(spread + EPS)
    return center * inverse, inverse


def norm_back(grad, unit, inverse, gain):
    scaled = grad * gain
    first = jnp.mean(scaled, axis=-1, keepdims=True)
    second = jnp.mean(scaled * unit, axis=-1, keepdims=True)
    return inverse * (scaled - first - unit * second)


def halves(block):
    lane = lax.broadcasted_iota(jnp.int32, block.shape, 1)
    zero = jnp.zeros_like(block)
    return jnp.where(lane < HD, block, zero), jnp.where(lane < HD, zero, block)


def join(low, high):
    lane = lax.broadcasted_iota(jnp.int32, low.shape, 1)
    return jnp.where(lane < HD, low, high)


def span(scene_ref):
    micro = lax.axis_index(MICRO)
    own = scene_ref[micro, chip_index() * 4]
    first = jnp.int32(0)
    count = jnp.int32(0)
    for index in range(8):
        other = scene_ref[micro, index * 4]
        first += (other < own).astype(jnp.int32)
        count += (other == own).astype(jnp.int32)
    return first, count > 1


def three(value):
    a = value.astype(BF).astype(F32)
    b = (value - a).astype(BF).astype(F32)
    c = value - a - b
    return a, b, c


def put_columns(width, rows, start, columns):
    lane = lax.broadcasted_iota(jnp.int32, (rows, width), 1)
    out = jnp.zeros((rows, width), F32)
    for offset, column in enumerate(columns):
        out = jnp.where(lane == start + offset, column, out)
    return out


def call(kernel, outs, ins, cost, scratch=(), vmem=16, aliases=None):
    places = {"V": pltpu.VMEM, "H": pltpu.HBM, "S": pltpu.SMEM}
    return pl.pallas_call(
        kernel,
        out_shape=[jax.ShapeDtypeStruct(shape, dtype) for shape, dtype, _ in outs],
        in_specs=[pl.BlockSpec(memory_space=places[place]) for _, place in ins],
        out_specs=[pl.BlockSpec(memory_space=places[place]) for _, _, place in outs],
        scratch_shapes=list(scratch),
        input_output_aliases=aliases or {},
        cost_estimate=pl.CostEstimate(flops=cost, bytes_accessed=2000000, transcendentals=0),
        compiler_params=pltpu.CompilerParams(vmem_limit_bytes=vmem * 2**20),
    )(*[value for value, _ in ins])


DMA = pltpu.SemaphoreType.DMA


def send_copies(source, target, indices, sem):
    copies = [pltpu.make_async_copy(source, target.at[index], sem.at[index]) for index in indices]
    for copy in copies:
        copy.start()
    return copies


def wait_all(copies):
    for copy in copies:
        copy.wait()


def weight_copies(w_ref, w_buf, w_sem):
    group = group_index()
    copies = []
    for slot, part in enumerate((1, 2, 0)):
        column = pl.multiple_of(part * D + (group // 2) * 384, 128)
        copy = pltpu.make_async_copy(w_ref.at[:, pl.ds(column, 384)], w_buf.at[slot], w_sem.at[slot])
        copy.start()
        copies.append(copy)
    return copies


def project_kernel(
    tok_ref, gain_ref, shift_ref, w_ref, kv_ref, q_ref, normed_ref, x_buf, w_buf, kv_buf, x_sem, w_sem, kv_sem
):
    copy_x = pltpu.make_async_copy(tok_ref.at[lax.axis_index(MICRO)], x_buf, x_sem)
    copy_x.start()
    copies = weight_copies(w_ref, w_buf, w_sem)
    copy_x.wait()
    unit, _ = normalized(x_buf[...].astype(F32))
    normed = (unit * gain_ref[...].reshape(1, D) + shift_ref[...].reshape(1, D)).astype(BF)
    odd = (group_index() % 2) == 1

    def part(slot):
        copies[slot].wait()
        full = mm(normed, w_buf[slot])
        return jnp.where(odd, full[:, 192:], full[:, :192]).astype(BF)

    kv_buf[...] = jnp.concatenate([part(0), part(1)], axis=1)
    sends = send_copies(kv_buf, kv_ref, range(8), kv_sem)
    normed_ref[...] = normed
    q_ref[...] = jnp.concatenate([part(2), jnp.zeros((TOK, HD), BF)], axis=1)
    wait_all(sends)


def attend_kernel(scene_ref, q_ref, same_ref, other_ref, out_ref, buf, sem):
    first, big = span(scene_ref)

    def run(count):
        rows = count * TOK
        keys = jnp.concatenate(
            [ref[pl.ds(first, count)].reshape(rows, 384) for ref in (same_ref, other_ref)], axis=0
        )
        query = q_ref[...]
        q0, q1 = halves(query[:, :128])
        blocks = [keys[:, :128], keys[:, 128:256], keys[:, 256:]]
        mixed = []
        columns = []
        for qh, kb, vb in ((q0, 0, 1), (q1, 0, 2), (query[:, 128:], 1, 2)):
            scores = mm_nt(qh, blocks[kb]) * (HD**-0.5)
            top = jnp.max(scores, axis=-1, keepdims=True)
            weights = jnp.exp(scores - top)
            total = jnp.sum(weights, axis=-1, keepdims=True)
            probs = (weights * (1.0 / total)).astype(BF)
            mixed.append(mm(probs, blocks[vb]))
            columns += three(top + jnp.log(total))
        stats = put_columns(128, TOK, 0, columns)
        buf[...] = jnp.concatenate([join(stats, mixed[0]), join(mixed[1], mixed[2])], axis=1).astype(BF)

    @pl.when(big)
    def _():
        run(5)

    @pl.when(jnp.logical_not(big))
    def _():
        run(1)

    wait_all(send_copies(buf, out_ref, range(8), sem))


def forward_kernel(
    mixed_ref, tok_ref, og_ref, wo_ref, gain_ref, shift_ref, up_ref, down_ref,
    out_ref, middle_ref, normed_ref, act_ref, gpre_ref, grad_buf, branch_buf, sem,
):
    total = tok_ref[...].reshape(2 * TOK, D).astype(F32)
    for group in range(4):
        rows = jnp.concatenate([mixed_ref[group], mixed_ref[4 + group]], axis=0)
        total = total + mm(rows, wo_ref[group])
    middle_ref[...] = total.reshape(8, BLK, D)
    unit, _ = normalized(total)
    normed = (unit * gain_ref[...].reshape(1, D) + shift_ref[...].reshape(1, D)).astype(BF)
    normed_ref[...] = normed
    pre = mm(normed, up_ref[...])
    cdf = 0.5 * (1.0 + lax.erf(pre * (0.5**0.5)))
    slope = cdf + pre * jnp.exp(-0.5 * pre * pre) * 0.3989422804014327
    grad_out = og_ref[...].reshape(2 * TOK, D)
    gpre = (mm_nt(grad_out, down_ref[...]) * slope).astype(BF)
    gpre_ref[...] = gpre
    grad_buf[...] = mm_nt(gpre, up_ref[...]).astype(BF).reshape(8, BLK, D)
    first = pltpu.make_async_copy(grad_buf, out_ref.at[:, pl.ds(BLK, BLK)], sem.at[0])
    first.start()
    act = (pre * cdf).astype(BF)
    act_ref[...] = act
    branch_buf[...] = mm(act, down_ref[...]).astype(BF).reshape(8, BLK, D)
    second = pltpu.make_async_copy(branch_buf, out_ref.at[:, pl.ds(0, BLK)], sem.at[1])
    second.start()
    first.wait()
    second.wait()


def ff_grads_kernel(normed_ref, act_ref, gpre_ref, og_ref, out_ref):
    up = mm_tn(normed_ref[...], gpre_ref[...]).astype(BF)
    grad_out = og_ref[...].reshape(2 * TOK, D)
    down = mm_tn(act_ref[...], grad_out).astype(BF)
    out_ref[:, :384] = up
    for tile in range(16):
        half = (tile % 2) * 384
        out_ref[tile * 48:(tile + 1) * 48, 384:] = down[
            (tile // 2) * 48:(tile // 2 + 1) * 48, half:half + 384
        ]


def middle_kernel(
    sums_ref, middle_ref, og_ref, mixed_ref, wo_ref, gain_ref,
    out_ref, low_ref, grad_ref, result_ref, vec_ref, buf, sem,
):
    micro = lax.axis_index(MICRO)
    group = group_index()
    start = pl.multiple_of(group * BLK, BLK)
    total = sums_ref[0].astype(F32)
    for index in range(1, 8):
        total = total + sums_ref[index].astype(F32)
    branch, grad = total[:BLK], total[BLK:]
    middle = middle_ref[micro * 4 + group]
    unit, inverse = normalized(middle)
    grad_mid = og_ref[micro, pl.ds(start, BLK)].astype(F32) + norm_back(
        grad, unit, inverse, gain_ref[...].reshape(1, D)
    )
    low = grad_mid.astype(BF)
    lane = lax.broadcasted_iota(jnp.int32, (BLK, 256), 1)
    sends = []
    for head_group in range(4):
        mixed = mixed_ref[micro * 4 + head_group, pl.ds(start, BLK)].astype(F32)
        back = mm_nt(low, wo_ref[head_group]).astype(BF).astype(F32)
        product = mixed * back
        columns = []
        for head in range(3):
            inside = (lane >= (head + 1) * HD) & (lane < (head + 2) * HD)
            columns += three(jnp.sum(jnp.where(inside, product, 0.0), axis=-1, keepdims=True))
        stats = put_columns(256, BLK, 9, columns)
        buf[head_group] = jnp.where(lane < 9, mixed, jnp.where(lane < HD, stats, back)).astype(BF)
        sends += send_copies(
            buf.at[head_group], out_ref, [chip * 4 + head_group for chip in range(8)], sem
        )
    low_ref[...] = low
    grad_ref[...] = grad_mid
    result_ref[...] = (middle + branch).astype(BF)
    gain_grad = jnp.sum(grad * unit, axis=0, keepdims=True)
    shift_grad = jnp.sum(grad, axis=0, keepdims=True)
    vec_ref[...] = jnp.concatenate([gain_grad, shift_grad, jnp.zeros((6, D), F32)], axis=0)
    wait_all(sends)


def attend_back_kernel(
    scene_ref, kvs_ref, kvo_ref, q_ref, gs_ref, go_ref, normed_ref, mixed_ref, low0_ref, low1_ref, low2_ref,
    low3_ref, gqkv_ref, keep_ref, send_ref, grad_buf,
):
    first, big = span(scene_ref)
    chip = chip_index()
    core = lax.axis_index(CORE)
    group = group_index()
    scale = HD**-0.5

    def run(count):
        rows = count * TOK

        def cut(value):
            return [value[:, at:at + 128] for at in range(0, value.shape[1], 128)]

        def gathered(one, two, width):
            return cut(jnp.concatenate(
                [ref[pl.ds(first, count)].reshape(rows, width) for ref in (one, two)], axis=0
            ))

        kv = gathered(kvs_ref, kvo_ref, 384)
        grad = gathered(gs_ref, go_ref, 256)
        query = cut(jnp.concatenate(
            [q_ref[pl.ds(first, count), which].reshape(rows, 256) for which in (core, 1 - core)], axis=0
        ))
        kv_own = cut(kvs_ref[chip])
        q_own = cut(q_ref[chip, core])
        g_own = cut(gs_ref[chip])
        q_heads = [*halves(q_own[0]), q_own[1]]
        g_heads = [halves(g_own[0])[1], *halves(g_own[1])]
        k_heads = [*halves(kv_own[0]), halves(kv_own[1])[0]]
        v_heads = [halves(kv_own[1])[1], *halves(kv_own[2])]
        own_stats = g_own[0].astype(F32)
        all_stats = grad[0].astype(F32).T

        def column(at):
            return own_stats[:, at:at + 1] + own_stats[:, at + 1:at + 2] + own_stats[:, at + 2:at + 3]

        def row(at):
            return all_stats[at:at + 1] + all_stats[at + 1:at + 2] + all_stats[at + 2:at + 3]

        dq, dk, dv = [], [], []
        for head, (kb, vb) in enumerate(((0, 1), (0, 2), (1, 2))):
            qb, gb = (0, 0, 1)[head], (0, 1, 1)[head]
            probs = jnp.exp(mm_nt(q_heads[head], kv[kb]) * scale - column(3 * head))
            gap = mm_nt(g_heads[head], kv[vb]) - column(9 + 3 * head)
            dq.append(mm((probs * gap).astype(BF), kv[kb]) * scale)
            probs = jnp.exp(mm_nt(k_heads[head], query[qb]) * scale - row(3 * head))
            gap = mm_nt(v_heads[head], grad[gb]) - row(9 + 3 * head)
            dv.append(mm(probs.astype(BF), grad[gb]))
            dk.append(mm((probs * gap).astype(BF), query[qb]) * scale)
        tail = dq[2]
        gqkv_ref[...] = jnp.concatenate(
            [join(dk[0], dk[1]), join(dk[2], dv[0]), join(dv[1], dv[2]), join(dq[0], dq[1]),
             join(tail, jnp.zeros_like(tail))],
            axis=1,
        ).astype(BF)

    @pl.when(big)
    def _():
        run(5)

    @pl.when(jnp.logical_not(big))
    def _():
        run(1)

    grad_buf[...] = mm_tn(normed_ref[...], gqkv_ref[...])
    index = lax.axis_index(MICRO) * 4 + group
    low = jnp.concatenate([ref[...] for ref in (low0_ref, low1_ref, low2_ref, low3_ref)], axis=0)
    mixed = jnp.concatenate(
        [mixed_ref[index, pl.ds(pl.multiple_of((group ^ k) * BLK, BLK), BLK)] for k in range(4)], axis=0
    )
    out = mm_tn(mixed, low)[HD:]
    for ref, owner in ((keep_ref, core), (send_ref, 1 - core)):
        for tile in range(8):
            rows = grad_buf[pl.ds(pl.multiple_of((2 * tile + owner) * 48, 16), 48)]
            at = (tile // 4) * 96
            pieces = [
                out[at + row * 48:at + (row + 1) * 48, (tile % 4) * 192:(tile % 4 + 1) * 192] for row in range(2)
            ]
            ref[2 * tile] = rows[:, :384].astype(BF)
            ref[2 * tile + 1] = jnp.concatenate(
                [rows[:, 384:576], jnp.where(owner == 1, pieces[1], pieces[0])], axis=1
            ).astype(BF)


def add_kernel(one_ref, two_ref, out_ref, buf, sem):
    buf[...] = (one_ref[...].astype(F32) + two_ref[...].astype(F32)).astype(BF)
    copy = pltpu.make_async_copy(buf, out_ref, sem)
    copy.start()
    copy.wait()


def sum_kernel(in_ref, out_ref, buf, sem):
    total = in_ref[0].astype(F32)
    for index in range(1, 16):
        total = total + in_ref[index].astype(F32)
    buf[...] = total.astype(BF)
    wait_all(send_copies(buf, out_ref, range(64), sem))


def spread_kernel(turn, in_ref, *refs):
    qkv_ref, out_ref, qkv_buf, out_buf, sem, out_sem = refs[-6:]
    owner = lax.axis_index(CORE)
    owner = 1 - owner if turn else owner
    copies = []
    for tile in range(8):
        block = [in_ref[tile, index].astype(F32) for index in range(8)]
        for part, half, at in ((1, 0, 0), (2, 0, 192), (0, 4, 0)):
            qkv_buf[tile, :, part * D:(part + 1) * D] = jnp.concatenate(
                [block[half + group][:, at:at + 192] for group in range(4)], axis=1
            )
        start = pl.multiple_of((2 * tile + owner) * 48, 16)
        copy = pltpu.make_async_copy(qkv_buf.at[tile], qkv_ref.at[pl.ds(start, 48)], sem.at[tile])
        copy.start()
        copies.append(copy)
        for group in range(4):
            out_buf[group, tile // 4, :, (tile % 4) * 192:(tile % 4 + 1) * 192] = block[4 + group][:, 192:]
    for group in range(4):
        for pair in range(2):
            start = pl.multiple_of(group * 192 + (pair * 2 + owner) * 48, 16)
            copy = pltpu.make_async_copy(
                out_buf.at[group, pair], out_ref.at[pl.ds(start, 48)], out_sem.at[group, pair]
            )
            copy.start()
            copies.append(copy)
    wait_all(copies)


def spread_ff_kernel(in_ref, up_ref, down_ref):
    up_ref[...] = in_ref[:, :384].astype(F32)
    for tile in range(16):
        half = (tile % 2) * 384
        down_ref[(tile // 2) * 48:(tile // 2 + 1) * 48, half:half + 384] = in_ref[
            tile * 48:(tile + 1) * 48, 384:
        ].astype(F32)


def normed_grad_kernel(gqkv_ref, w_ref, own_ref, one_ref, two_ref, three_ref, w_buf, buf, w_sem):
    copies = weight_copies(w_ref, w_buf, w_sem)
    group = group_index()
    odd = (group % 2) == 1
    total = jnp.zeros((TOK, D), F32)
    for slot in range(3):
        copies[slot].wait()
        part = gqkv_ref[:, slot * 192:(slot + 1) * 192]
        zero = jnp.zeros_like(part)
        wide = jnp.where(
            odd, jnp.concatenate([zero, part], axis=1), jnp.concatenate([part, zero], axis=1)
        )
        total = total + mm_nt(wide, w_buf[slot])
    buf[...] = total
    own_ref[...] = buf[pl.ds(pl.multiple_of(group * BLK, BLK), BLK)]
    for k, ref in ((1, one_ref), (2, two_ref), (3, three_ref)):
        ref[...] = buf[pl.ds(pl.multiple_of((group ^ k) * BLK, BLK), BLK)].astype(BF)


def input_kernel(
    own_ref, one_ref, two_ref, three_ref, tok_ref, gain_ref, grad_ref, result_ref, vec_ref, out_ref, x_buf, sem
):
    start = pl.multiple_of(group_index() * BLK, BLK)
    copy = pltpu.make_async_copy(tok_ref.at[lax.axis_index(MICRO), pl.ds(start, BLK)], x_buf, sem)
    copy.start()
    total = own_ref[...]
    for ref in (one_ref, two_ref, three_ref):
        total = total + ref[...].astype(F32)
    copy.wait()
    unit, inverse = normalized(x_buf[...].astype(F32))
    grad = grad_ref[...] + norm_back(total, unit, inverse, gain_ref[...].reshape(1, D))
    gain1 = jnp.sum(total * unit, axis=0, keepdims=True)
    shift1 = jnp.sum(total, axis=0, keepdims=True)
    vectors = jnp.concatenate([gain1, shift1, vec_ref[...][:2], jnp.zeros((12, D), F32)], axis=0)
    out_ref[:BLK] = grad.astype(BF)
    out_ref[BLK:2 * BLK] = result_ref[...]
    out_ref[2 * BLK:] = vectors.astype(BF)


def unpack_kernel(*refs):
    parts, (grad_ref, result_ref, vec_ref) = refs[:8], refs[8:]
    micro = lax.axis_index(MICRO)
    group = group_index()
    total = jnp.zeros((16, D), F32)
    for k, ref in enumerate(parts):
        rows = pl.ds(pl.multiple_of((group ^ (k % 4)) * BLK, BLK), BLK)
        where = micro ^ (k // 4)
        grad_ref[where, rows] = ref[:BLK].astype(F32)
        result_ref[where, rows] = ref[BLK:2 * BLK]
        total = total + ref[2 * BLK:].astype(F32)
    vec_ref[...] = total[:8]


def exchange(value, axes):
    return lax.all_to_all(value, axes, 0, 0, tiled=True)


def swap(value):
    return lax.ppermute(value, CORE, [(0, 1), (1, 0)])


def flip(value, axes, count, bits):
    return lax.ppermute(value, axes, [(index, index ^ bits) for index in range(count)])


def shards(
    tokens, scene_of_block, ln1_gain, ln1_shift, w_qkv, w_out, ln2_gain, ln2_shift, w_up, w_down, out_grad
):
    w_out_pad = jnp.pad(w_out.reshape(4, 192, D), ((0, 0), (HD, 0), (0, 0)))
    kv_send, query, normed = call(
        project_kernel,
        [((8, TOK, 384), BF, "H"), ((TOK, 256), BF, "V"), ((TOK, D), BF, "V")],
        [(tokens, "H"), (ln1_gain, "V"), (ln1_shift, "V"), (w_qkv, "H")],
        10**9,
        [
            pltpu.VMEM((TOK, D), BF), pltpu.VMEM((3, D, 384), BF), pltpu.VMEM((TOK, 384), BF),
            DMA, DMA((3,)), DMA((8,)),
        ],
    )
    kv_same = exchange(kv_send, CHIP)
    kv_other = swap(kv_same)
    (mixed_send,) = call(
        attend_kernel,
        [((8, TOK, 256), BF, "H")],
        [(scene_of_block, "S"), (query, "V"), (kv_same, "V"), (kv_other, "V")],
        2 * 10**9,
        [pltpu.VMEM((TOK, 256), BF), DMA((8,))],
    )
    mixed = exchange(mixed_send, NARROW)
    query, _ = lax.optimization_barrier((query, kv_same))
    queries = lax.all_gather(query, WIDE, axis=0, tiled=True).reshape(8, 2, TOK, 256)
    ff_send, middle, normed2, act, grad_pre = call(
        forward_kernel,
        [
            ((8, 2 * BLK, D), BF, "H"), ((8, BLK, D), F32, "V"), ((2 * TOK, D), BF, "V"),
            ((2 * TOK, FFL), BF, "V"), ((2 * TOK, FFL), BF, "V"),
        ],
        [
            (mixed, "V"), (tokens, "V"), (out_grad, "V"), (w_out_pad, "V"), (ln2_gain, "V"), (ln2_shift, "V"),
            (w_up, "V"), (w_down, "V"),
        ],
        4 * 10**9,
        [pltpu.VMEM((8, BLK, D), BF), pltpu.VMEM((8, BLK, D), BF), DMA((2,))],
    )
    ff_sums = exchange(ff_send, NARROW)
    (ff_grads,) = call(
        ff_grads_kernel,
        [((D, D), BF, "V")],
        [(normed2, "V"), (act, "V"), (grad_pre, "V"), (out_grad, "V")],
        2 * 10**9,
    )
    ff_part = lax.psum_scatter(ff_grads, WIDE, scatter_dimension=0, tiled=True)
    ff_all = lax.all_gather(ff_part, WIDE, axis=0, tiled=True)
    grad_send, low, grad_mid, result_part, vec2 = call(
        middle_kernel,
        [
            ((32, BLK, 256), BF, "H"), ((BLK, D), BF, "V"), ((BLK, D), F32, "V"), ((BLK, D), BF, "V"),
            ((8, D), F32, "V"),
        ],
        [(ff_sums, "V"), (middle, "V"), (out_grad, "V"), (mixed, "V"), (w_out_pad, "V"), (ln2_gain, "V")],
        10**9,
        [pltpu.VMEM((4, BLK, 256), BF), DMA((32,))],
    )
    grad_same = exchange(grad_send, (*CHIP, *GROUP)).reshape(8, TOK, 256)
    lows = [low] + [flip(low, GROUP, 4, k) for k in (1, 2, 3)]
    grad_other = swap(grad_same)
    gqkv, keep, send = call(
        attend_back_kernel,
        [((TOK, 640), BF, "V"), ((16, 48, 384), BF, "V"), ((16, 48, 384), BF, "V")],
        [
            (scene_of_block, "S"), (kv_same, "V"), (kv_other, "V"), (queries, "V"), (grad_same, "V"),
            (grad_other, "V"), (normed, "V"), (mixed, "V"), *[(value, "V") for value in lows],
        ],
        8 * 10**9,
        [pltpu.VMEM((D, 640), F32)],
        vmem=24,
    )
    (weight_send,) = call(
        add_kernel,
        [((16, 48, 384), BF, "H")],
        [(keep, "V"), (swap(send), "V")],
        10**8,
        [pltpu.VMEM((16, 48, 384), BF), DMA],
    )
    weight_parts = exchange(weight_send, (*CHIP, MICRO))
    own, *sends = call(
        normed_grad_kernel,
        [((BLK, D), F32, "V")] + [((BLK, D), BF, "V")] * 3,
        [(gqkv, "V"), (w_qkv, "H")],
        10**9,
        [pltpu.VMEM((3, D, 384), BF), pltpu.VMEM((TOK, D), F32), DMA((3,))],
    )
    parts = [flip(value, GROUP, 4, k + 1) for k, value in enumerate(sends)]
    (packed,) = call(
        input_kernel,
        [((80, D), BF, "V")],
        [
            (own, "V"), *[(value, "V") for value in parts], (tokens, "H"), (ln1_gain, "V"), (grad_mid, "V"),
            (result_part, "V"), (vec2, "V"),
        ],
        10**8,
        [pltpu.VMEM((BLK, D), BF), DMA],
    )
    everyone = [packed] + [flip(packed, NARROW, 8, k) for k in range(1, 8)]
    input_grad, result, vectors = call(
        unpack_kernel,
        [((2, TOK, D), F32, "V"), ((2, TOK, D), BF, "V"), ((8, D), F32, "V")],
        [(value, "V") for value in everyone],
        10**8,
    )
    (weight_total,) = call(
        sum_kernel,
        [((64, 48, 384), BF, "H")],
        [(weight_parts, "V")],
        10**8,
        [pltpu.VMEM((48, 384), BF), DMA((64,))],
    )
    weight_same = exchange(weight_total, (*CHIP, *NARROW)).reshape(8, 8, 48, 384)
    weight_other = swap(weight_same)
    vectors = vectors + swap(vectors)
    for bits in (1, 2, 4):
        vectors = vectors + flip(vectors, CHIP, 8, bits)
    up_grad, down_grad = call(
        spread_ff_kernel, [((D, FFL), F32, "V"), ((FFL, D), F32, "V")], [(ff_all, "V")], 10**7
    )
    scratch = [
        pltpu.VMEM((8, 48, 3 * D), F32), pltpu.VMEM((4, 2, 48, D), F32), DMA((8,)), DMA((4, 2)),
    ]
    grads = [((D, 3 * D), F32, "H"), ((D, D), F32, "H")]
    half = call(
        functools.partial(spread_kernel, False), grads, [(weight_same, "V")], 10**8, scratch
    )
    qkv_grad, out_proj_grad = call(
        functools.partial(spread_kernel, True),
        grads,
        [(weight_other, "V"), (half[0], "H"), (half[1], "H")],
        10**8,
        scratch,
        aliases={1: 0, 2: 1},
    )
    return (
        result, input_grad, qkv_grad, out_proj_grad, vectors[0], vectors[1], vectors[2], vectors[3], up_grad,
        down_grad,
    )


def solution(mesh):
    names = ("y", "xl", "c", "zh", "zl", "xh")
    fine = Mesh(mesh.devices.reshape(4, 2, 2, 2, 2, 2), names)
    tokens = P(None, WIDE, None)
    placed = (
        tokens, P(), P(), P(), P(), P(), P(), P(), P(None, NARROW), P(NARROW, None), tokens
    )
    return jax.shard_map(
        shards,
        mesh=fine,
        in_specs=placed,
        out_specs=(
            tokens, tokens, P(), P(), P(), P(), P(), P(), P(None, NARROW), P(NARROW, None)
        ),
        check_vma=False,
    )
```

```python
import functools

import jax
import jax.numpy as jnp
from jax import lax
from jax.experimental import pallas as pl
from jax.experimental.pallas import tpu as pltpu
from jax.sharding import Mesh
from jax.sharding import PartitionSpec as P

D = 768
HD = 64
FFL = 384
TOK = 128
BLK = 32
EPS = 1e-05
BF = jnp.bfloat16
F32 = jnp.float32

CHIP = ("y", "xl")
CORE = "c"
MICRO = "zh"
GROUP = ("zl", "xh")
NARROW = (MICRO, *GROUP)
WIDE = (*CHIP, CORE)


def chip_index():
    return lax.axis_index("y") * 2 + lax.axis_index("xl")


def group_index():
    return lax.axis_index("zl") * 2 + lax.axis_index("xh")


def mm(left, right):
    return lax.dot_general(left, right, (((1,), (0,)), ((), ())), preferred_element_type=F32)


def mm_nt(left, right):
    return lax.dot_general(left, right, (((1,), (1,)), ((), ())), preferred_element_type=F32)


def mm_tn(left, right):
    return lax.dot_general(left, right, (((0,), (0,)), ((), ())), preferred_element_type=F32)


def normalized(values):
    center = values - jnp.mean(values, axis=-1, keepdims=True)
    spread = jnp.mean(center * center, axis=-1, keepdims=True)
    inverse = lax.rsqrt(spread + EPS)
    return center * inverse, inverse


def norm_back(grad, unit, inverse, gain):
    scaled = grad * gain
    first = jnp.mean(scaled, axis=-1, keepdims=True)
    second = jnp.mean(scaled * unit, axis=-1, keepdims=True)
    return inverse * (scaled - first - unit * second)


def halves(block):
    lane = lax.broadcasted_iota(jnp.int32, block.shape, 1)
    zero = jnp.zeros_like(block)
    return jnp.where(lane < HD, block, zero), jnp.where(lane < HD, zero, block)


def join(low, high):
    lane = lax.broadcasted_iota(jnp.int32, low.shape, 1)
    return jnp.where(lane < HD, low, high)


def span(scene_ref):
    micro = lax.axis_index(MICRO)
    own = scene_ref[micro, chip_index() * 4]
    first = jnp.int32(0)
    count = jnp.int32(0)
    for index in range(8):
        other = scene_ref[micro, index * 4]
        first += (other < own).astype(jnp.int32)
        count += (other == own).astype(jnp.int32)
    return first, count > 1


def three(value):
    a = value.astype(BF).astype(F32)
    b = (value - a).astype(BF).astype(F32)
    c = value - a - b
    return a, b, c


def put_columns(width, rows, start, columns):
    lane = lax.broadcasted_iota(jnp.int32, (rows, width), 1)
    out = jnp.zeros((rows, width), F32)
    for offset, column in enumerate(columns):
        out = jnp.where(lane == start + offset, column, out)
    return out


def call(kernel, outs, ins, cost, scratch=(), vmem=16, aliases=None):
    places = {"V": pltpu.VMEM, "H": pltpu.HBM, "S": pltpu.SMEM}
    return pl.pallas_call(
        kernel,
        out_shape=[jax.ShapeDtypeStruct(shape, dtype) for shape, dtype, _ in outs],
        in_specs=[pl.BlockSpec(memory_space=places[place]) for _, place in ins],
        out_specs=[pl.BlockSpec(memory_space=places[place]) for _, _, place in outs],
        scratch_shapes=list(scratch),
        input_output_aliases=aliases or {},
        cost_estimate=pl.CostEstimate(flops=cost, bytes_accessed=2000000, transcendentals=0),
        compiler_params=pltpu.CompilerParams(vmem_limit_bytes=vmem * 2**20),
    )(*[value for value, _ in ins])


DMA = pltpu.SemaphoreType.DMA


def send_copies(source, target, indices, sem):
    copies = [pltpu.make_async_copy(source, target.at[index], sem.at[index]) for index in indices]
    for copy in copies:
        copy.start()
    return copies


def wait_all(copies):
    for copy in copies:
        copy.wait()


def weight_copies(w_ref, w_buf, w_sem):
    group = group_index()
    copies = []
    for slot, part in enumerate((1, 2, 0)):
        column = pl.multiple_of(part * D + (group // 2) * 384, 128)
        copy = pltpu.make_async_copy(w_ref.at[:, pl.ds(column, 384)], w_buf.at[slot], w_sem.at[slot])
        copy.start()
        copies.append(copy)
    return copies


def project_kernel(
    tok_ref, gain_ref, shift_ref, w_ref, kv_ref, q_ref, normed_ref,
    x_buf, w_buf, kv_buf, gain_buf, shift_buf, x_sem, w_sem, kv_sem, gain_sem, shift_sem,
):
    copy_x = pltpu.make_async_copy(tok_ref.at[lax.axis_index(MICRO)], x_buf, x_sem)
    copy_x.start()
    copy_gain = pltpu.make_async_copy(gain_ref, gain_buf, gain_sem)
    copy_gain.start()
    copy_shift = pltpu.make_async_copy(shift_ref, shift_buf, shift_sem)
    copy_shift.start()
    copies = weight_copies(w_ref, w_buf, w_sem)
    wait_all([copy_x, copy_gain, copy_shift])
    unit, _ = normalized(x_buf[...].astype(F32))
    normed = (unit * gain_buf[...].reshape(1, D) + shift_buf[...].reshape(1, D)).astype(BF)
    odd = (group_index() % 2) == 1

    def part(slot):
        copies[slot].wait()
        full = mm(normed, w_buf[slot])
        return jnp.where(odd, full[:, 192:], full[:, :192]).astype(BF)

    kv_buf[...] = jnp.concatenate([part(0), part(1)], axis=1)
    sends = send_copies(kv_buf, kv_ref, range(8), kv_sem)
    normed_ref[...] = normed
    q_ref[...] = jnp.concatenate([part(2), jnp.zeros((TOK, HD), BF)], axis=1)
    wait_all(sends)


def attend_kernel(scene_ref, q_ref, same_ref, other_ref, out_ref, buf, sem):
    first, big = span(scene_ref)

    def run(count):
        rows = count * TOK
        keys = jnp.concatenate(
            [ref[pl.ds(first, count)].reshape(rows, 384) for ref in (same_ref, other_ref)], axis=0
        )
        query = q_ref[...]
        q0, q1 = halves(query[:, :128])
        blocks = [keys[:, :128], keys[:, 128:256], keys[:, 256:]]
        mixed = []
        columns = []
        for qh, kb, vb in ((q0, 0, 1), (q1, 0, 2), (query[:, 128:], 1, 2)):
            scores = mm_nt(qh, blocks[kb]) * (HD**-0.5)
            top = jnp.max(scores, axis=-1, keepdims=True)
            weights = jnp.exp(scores - top)
            total = jnp.sum(weights, axis=-1, keepdims=True)
            probs = (weights * (1.0 / total)).astype(BF)
            mixed.append(mm(probs, blocks[vb]))
            columns += three(top + jnp.log(total))
        stats = put_columns(128, TOK, 0, columns)
        buf[...] = jnp.concatenate([join(stats, mixed[0]), join(mixed[1], mixed[2])], axis=1).astype(BF)

    @pl.when(big)
    def _():
        run(5)

    @pl.when(jnp.logical_not(big))
    def _():
        run(1)

    wait_all(send_copies(buf, out_ref, range(8), sem))


def forward_kernel(
    mixed_ref, tok_ref, og_ref, wo_ref, gain_ref, shift_ref, up_ref, down_ref,
    out_ref, middle_ref, normed_ref, act_ref, gpre_ref, grad_buf, branch_buf, sem,
):
    total = tok_ref[...].reshape(2 * TOK, D).astype(F32)
    for group in range(4):
        rows = jnp.concatenate([mixed_ref[group], mixed_ref[4 + group]], axis=0)
        total = total + mm(rows, wo_ref[group])
    middle_ref[...] = total.reshape(8, BLK, D)
    unit, _ = normalized(total)
    normed = (unit * gain_ref[...].reshape(1, D) + shift_ref[...].reshape(1, D)).astype(BF)
    normed_ref[...] = normed
    pre = mm(normed, up_ref[...])
    cdf = 0.5 * (1.0 + lax.erf(pre * (0.5**0.5)))
    slope = cdf + pre * jnp.exp(-0.5 * pre * pre) * 0.3989422804014327
    grad_out = og_ref[...].reshape(2 * TOK, D)
    gpre = (mm_nt(grad_out, down_ref[...]) * slope).astype(BF)
    gpre_ref[...] = gpre
    grad_buf[...] = mm_nt(gpre, up_ref[...]).astype(BF).reshape(8, BLK, D)
    first = pltpu.make_async_copy(grad_buf, out_ref.at[:, pl.ds(BLK, BLK)], sem.at[0])
    first.start()
    act = (pre * cdf).astype(BF)
    act_ref[...] = act
    branch_buf[...] = mm(act, down_ref[...]).astype(BF).reshape(8, BLK, D)
    second = pltpu.make_async_copy(branch_buf, out_ref.at[:, pl.ds(0, BLK)], sem.at[1])
    second.start()
    first.wait()
    second.wait()


def ff_grads_kernel(normed_ref, act_ref, gpre_ref, og_ref, keep_ref, send_ref, up_buf, down_buf):
    core = lax.axis_index(CORE)
    up_buf[...] = mm_tn(normed_ref[...], gpre_ref[...])
    down_buf[...] = mm_tn(act_ref[...], og_ref[...].reshape(2 * TOK, D))
    for ref, owner in ((keep_ref, core), (send_ref, 1 - core)):
        column = pl.multiple_of(owner * 384, 128)
        for tile in range(8):
            rows = pl.ds(pl.multiple_of((2 * tile + owner) * 48, 16), 48)
            ref[tile, :, :384] = up_buf[rows].astype(BF)
            ref[tile, :, 384:] = down_buf[tile * 48:(tile + 1) * 48, pl.ds(column, 384)].astype(BF)


def halve_kernel(bit_of, one_ref, two_ref, keep_ref, send_ref):
    bit = bit_of()
    for ref, owner in ((keep_ref, bit), (send_ref, 1 - bit)):
        for index in range(ref.shape[0]):
            at = 2 * index + owner
            ref[index] = (one_ref[at].astype(F32) + two_ref[at].astype(F32)).astype(BF)


def pair_kernel(one_ref, two_ref, out_ref):
    out_ref[...] = (one_ref[0].astype(F32) + two_ref[0].astype(F32)).astype(BF)


def middle_kernel(
    sums_ref, middle_ref, og_ref, mixed_ref, wo_ref, gain_ref,
    out_ref, low_ref, grad_ref, result_ref, vec_ref, buf, sem,
):
    micro = lax.axis_index(MICRO)
    group = group_index()
    start = pl.multiple_of(group * BLK, BLK)
    total = sums_ref[0].astype(F32)
    for index in range(1, 8):
        total = total + sums_ref[index].astype(F32)
    branch, grad = total[:BLK], total[BLK:]
    middle = middle_ref[micro * 4 + group]
    unit, inverse = normalized(middle)
    grad_mid = og_ref[micro, pl.ds(start, BLK)].astype(F32) + norm_back(
        grad, unit, inverse, gain_ref[...].reshape(1, D)
    )
    low = grad_mid.astype(BF)
    lane = lax.broadcasted_iota(jnp.int32, (BLK, 256), 1)
    sends = []
    for head_group in range(4):
        mixed = mixed_ref[micro * 4 + head_group, pl.ds(start, BLK)].astype(F32)
        back = mm_nt(low, wo_ref[head_group]).astype(BF).astype(F32)
        product = mixed * back
        columns = []
        for head in range(3):
            inside = (lane >= (head + 1) * HD) & (lane < (head + 2) * HD)
            columns += three(jnp.sum(jnp.where(inside, product, 0.0), axis=-1, keepdims=True))
        stats = put_columns(256, BLK, 9, columns)
        buf[head_group] = jnp.where(lane < 9, mixed, jnp.where(lane < HD, stats, back)).astype(BF)
        sends += send_copies(
            buf.at[head_group], out_ref, [chip * 4 + head_group for chip in range(8)], sem
        )
    low_ref[...] = low
    grad_ref[...] = grad_mid
    result_ref[...] = (middle + branch).astype(BF)
    gain_grad = jnp.sum(grad * unit, axis=0, keepdims=True)
    shift_grad = jnp.sum(grad, axis=0, keepdims=True)
    vec_ref[...] = jnp.concatenate([gain_grad, shift_grad, jnp.zeros((6, D), F32)], axis=0)
    wait_all(sends)


def attend_back_kernel(
    scene_ref, kvs_ref, kvo_ref, q_ref, gs_ref, go_ref, normed_ref, mixed_ref, low0_ref, low1_ref, low2_ref,
    low3_ref, gqkv_ref, keep_ref, send_ref, grad_buf,
):
    first, big = span(scene_ref)
    chip = chip_index()
    core = lax.axis_index(CORE)
    group = group_index()
    scale = HD**-0.5

    def run(count):
        rows = count * TOK

        def cut(value):
            return [value[:, at:at + 128] for at in range(0, value.shape[1], 128)]

        def gathered(one, two, width):
            return cut(jnp.concatenate(
                [ref[pl.ds(first, count)].reshape(rows, width) for ref in (one, two)], axis=0
            ))

        kv = gathered(kvs_ref, kvo_ref, 384)
        grad = gathered(gs_ref, go_ref, 256)
        query = cut(jnp.concatenate(
            [q_ref[pl.ds(first, count), which].reshape(rows, 256) for which in (core, 1 - core)], axis=0
        ))
        kv_own = cut(kvs_ref[chip])
        q_own = cut(q_ref[chip, core])
        g_own = cut(gs_ref[chip])
        q_heads = [*halves(q_own[0]), q_own[1]]
        g_heads = [halves(g_own[0])[1], *halves(g_own[1])]
        k_heads = [*halves(kv_own[0]), halves(kv_own[1])[0]]
        v_heads = [halves(kv_own[1])[1], *halves(kv_own[2])]
        own_stats = g_own[0].astype(F32)
        all_stats = grad[0].astype(F32).T

        def column(at):
            return own_stats[:, at:at + 1] + own_stats[:, at + 1:at + 2] + own_stats[:, at + 2:at + 3]

        def row(at):
            return all_stats[at:at + 1] + all_stats[at + 1:at + 2] + all_stats[at + 2:at + 3]

        dq, dk, dv = [], [], []
        for head, (kb, vb) in enumerate(((0, 1), (0, 2), (1, 2))):
            qb, gb = (0, 0, 1)[head], (0, 1, 1)[head]
            probs = jnp.exp(mm_nt(q_heads[head], kv[kb]) * scale - column(3 * head))
            gap = mm_nt(g_heads[head], kv[vb]) - column(9 + 3 * head)
            dq.append(mm((probs * gap).astype(BF), kv[kb]) * scale)
            probs = jnp.exp(mm_nt(k_heads[head], query[qb]) * scale - row(3 * head))
            gap = mm_nt(v_heads[head], grad[gb]) - row(9 + 3 * head)
            dv.append(mm(probs.astype(BF), grad[gb]))
            dk.append(mm((probs * gap).astype(BF), query[qb]) * scale)
        tail = dq[2]
        gqkv_ref[...] = jnp.concatenate(
            [join(dk[0], dk[1]), join(dk[2], dv[0]), join(dv[1], dv[2]), join(dq[0], dq[1]),
             join(tail, jnp.zeros_like(tail))],
            axis=1,
        ).astype(BF)

    @pl.when(big)
    def _():
        run(5)

    @pl.when(jnp.logical_not(big))
    def _():
        run(1)

    grad_buf[...] = mm_tn(normed_ref[...], gqkv_ref[...])
    index = lax.axis_index(MICRO) * 4 + group
    low = jnp.concatenate([ref[...] for ref in (low0_ref, low1_ref, low2_ref, low3_ref)], axis=0)
    mixed = jnp.concatenate(
        [mixed_ref[index, pl.ds(pl.multiple_of((group ^ k) * BLK, BLK), BLK)] for k in range(4)], axis=0
    )
    out = mm_tn(mixed, low)[HD:]
    for ref, owner in ((keep_ref, core), (send_ref, 1 - core)):
        for tile in range(8):
            rows = grad_buf[pl.ds(pl.multiple_of((2 * tile + owner) * 48, 16), 48)]
            at = (tile // 4) * 96
            pieces = [
                out[at + row * 48:at + (row + 1) * 48, (tile % 4) * 192:(tile % 4 + 1) * 192] for row in range(2)
            ]
            ref[2 * tile] = rows[:, :384].astype(BF)
            ref[2 * tile + 1] = jnp.concatenate(
                [rows[:, 384:576], jnp.where(owner == 1, pieces[1], pieces[0])], axis=1
            ).astype(BF)


def add_kernel(one_ref, two_ref, out_ref, buf, sem):
    buf[...] = (one_ref[...].astype(F32) + two_ref[...].astype(F32)).astype(BF)
    copy = pltpu.make_async_copy(buf, out_ref, sem)
    copy.start()
    copy.wait()


def sum_kernel(in_ref, out_ref, buf, sem):
    total = in_ref[0].astype(F32)
    for index in range(1, 16):
        total = total + in_ref[index].astype(F32)
    buf[...] = total.astype(BF)
    wait_all(send_copies(buf, out_ref, range(64), sem))


def spread_kernel(turn, in_ref, *refs):
    qkv_ref, out_ref, qkv_buf, out_buf, sem, out_sem = refs[-6:]
    owner = lax.axis_index(CORE)
    owner = 1 - owner if turn else owner
    copies = []
    for tile in range(8):
        block = [in_ref[tile, index].astype(F32) for index in range(8)]
        for part, half, at in ((1, 0, 0), (2, 0, 192), (0, 4, 0)):
            qkv_buf[tile, :, part * D:(part + 1) * D] = jnp.concatenate(
                [block[half + group][:, at:at + 192] for group in range(4)], axis=1
            )
        start = pl.multiple_of((2 * tile + owner) * 48, 16)
        copy = pltpu.make_async_copy(qkv_buf.at[tile], qkv_ref.at[pl.ds(start, 48)], sem.at[tile])
        copy.start()
        copies.append(copy)
        for group in range(4):
            out_buf[group, tile // 4, :, (tile % 4) * 192:(tile % 4 + 1) * 192] = block[4 + group][:, 192:]
    for group in range(4):
        for pair in range(2):
            start = pl.multiple_of(group * 192 + (pair * 2 + owner) * 48, 16)
            copy = pltpu.make_async_copy(
                out_buf.at[group, pair], out_ref.at[pl.ds(start, 48)], out_sem.at[group, pair]
            )
            copy.start()
            copies.append(copy)
    wait_all(copies)


def spread_ff_kernel(in_ref, up_ref, down_ref):
    up_ref[...] = in_ref[:, :384].astype(F32)
    for tile in range(16):
        half = (tile % 2) * 384
        down_ref[(tile // 2) * 48:(tile // 2 + 1) * 48, half:half + 384] = in_ref[
            tile * 48:(tile + 1) * 48, 384:
        ].astype(F32)


def normed_grad_kernel(gqkv_ref, w_ref, own_ref, one_ref, two_ref, three_ref, w_buf, buf, w_sem):
    copies = weight_copies(w_ref, w_buf, w_sem)
    group = group_index()
    odd = (group % 2) == 1
    total = jnp.zeros((TOK, D), F32)
    for slot in range(3):
        copies[slot].wait()
        part = gqkv_ref[:, slot * 192:(slot + 1) * 192]
        zero = jnp.zeros_like(part)
        wide = jnp.where(
            odd, jnp.concatenate([zero, part], axis=1), jnp.concatenate([part, zero], axis=1)
        )
        total = total + mm_nt(wide, w_buf[slot])
    buf[...] = total
    own_ref[...] = buf[pl.ds(pl.multiple_of(group * BLK, BLK), BLK)]
    for k, ref in ((1, one_ref), (2, two_ref), (3, three_ref)):
        ref[...] = buf[pl.ds(pl.multiple_of((group ^ k) * BLK, BLK), BLK)].astype(BF)


def input_kernel(
    own_ref, one_ref, two_ref, three_ref, tok_ref, gain_ref, grad_ref, result_ref, vec_ref, out_ref, x_buf, sem
):
    start = pl.multiple_of(group_index() * BLK, BLK)
    copy = pltpu.make_async_copy(tok_ref.at[lax.axis_index(MICRO), pl.ds(start, BLK)], x_buf, sem)
    copy.start()
    total = own_ref[...]
    for ref in (one_ref, two_ref, three_ref):
        total = total + ref[...].astype(F32)
    copy.wait()
    unit, inverse = normalized(x_buf[...].astype(F32))
    grad = grad_ref[...] + norm_back(total, unit, inverse, gain_ref[...].reshape(1, D))
    gain1 = jnp.sum(total * unit, axis=0, keepdims=True)
    shift1 = jnp.sum(total, axis=0, keepdims=True)
    vectors = jnp.concatenate([gain1, shift1, vec_ref[...][:2], jnp.zeros((12, D), F32)], axis=0)
    out_ref[:BLK] = grad.astype(BF)
    out_ref[BLK:2 * BLK] = result_ref[...]
    out_ref[2 * BLK:] = vectors.astype(BF)


def unpack_kernel(*refs):
    parts, (grad_ref, result_ref, vec_ref) = refs[:8], refs[8:]
    micro = lax.axis_index(MICRO)
    group = group_index()
    total = jnp.zeros((16, D), F32)
    for k, ref in enumerate(parts):
        rows = pl.ds(pl.multiple_of((group ^ (k % 4)) * BLK, BLK), BLK)
        where = micro ^ (k // 4)
        grad_ref[where, rows] = ref[:BLK].astype(F32)
        result_ref[where, rows] = ref[BLK:2 * BLK]
        total = total + ref[2 * BLK:].astype(F32)
    vec_ref[...] = total[:8]


def exchange(value, axes):
    return lax.all_to_all(value, axes, 0, 0, tiled=True)


def swap(value):
    return lax.ppermute(value, CORE, [(0, 1), (1, 0)])


def after(value, *others):
    return pl.pallas_call(
        lambda *refs: None,
        out_shape=jax.ShapeDtypeStruct(value.shape, value.dtype),
        in_specs=[pl.BlockSpec(memory_space=pl.ANY)] * (1 + len(others)),
        out_specs=pl.BlockSpec(memory_space=pl.ANY),
        input_output_aliases={0: 0},
        cost_estimate=pl.CostEstimate(flops=1, bytes_accessed=1, transcendentals=0),
        compiler_params=pltpu.CompilerParams(vmem_limit_bytes=2**20),
    )(value, *others)


def flip(value, axes, count, bits):
    return lax.ppermute(value, axes, [(index, index ^ bits) for index in range(count)])


def shards(
    tokens, scene_of_block, ln1_gain, ln1_shift, w_qkv, w_out, ln2_gain, ln2_shift, w_up, w_down, out_grad
):
    w_out_pad = jnp.pad(w_out.reshape(4, 192, D), ((0, 0), (HD, 0), (0, 0)))
    kv_send, query, normed = call(
        project_kernel,
        [((8, TOK, 384), BF, "H"), ((TOK, 256), BF, "V"), ((TOK, D), BF, "V")],
        [(tokens, "H"), (ln1_gain, "H"), (ln1_shift, "H"), (w_qkv, "H")],
        10**9,
        [
            pltpu.VMEM((TOK, D), BF), pltpu.VMEM((3, D, 384), BF), pltpu.VMEM((TOK, 384), BF),
            pltpu.VMEM((D,), F32), pltpu.VMEM((D,), F32), DMA, DMA((3,)), DMA((8,)), DMA, DMA,
        ],
        vmem=56,
    )
    kv_same = exchange(kv_send, CHIP)
    kv_other = swap(kv_same)
    (mixed_send,) = call(
        attend_kernel,
        [((8, TOK, 256), BF, "H")],
        [(scene_of_block, "S"), (query, "V"), (kv_same, "V"), (kv_other, "V")],
        2 * 10**9,
        [pltpu.VMEM((TOK, 256), BF), DMA((8,))],
    )
    mixed = exchange(mixed_send, NARROW)
    query, _ = lax.optimization_barrier((query, kv_same))
    queries = lax.all_gather(query, WIDE, axis=0, tiled=True).reshape(8, 2, TOK, 256)
    ff_send, middle, normed2, act, grad_pre = call(
        forward_kernel,
        [
            ((8, 2 * BLK, D), BF, "H"), ((8, BLK, D), F32, "V"), ((2 * TOK, D), BF, "V"),
            ((2 * TOK, FFL), BF, "V"), ((2 * TOK, FFL), BF, "V"),
        ],
        [
            (mixed, "V"), (tokens, "V"), (out_grad, "V"), (w_out_pad, "V"), (ln2_gain, "V"), (ln2_shift, "V"),
            (w_up, "V"), (w_down, "V"),
        ],
        4 * 10**9,
        [pltpu.VMEM((8, BLK, D), BF), pltpu.VMEM((8, BLK, D), BF), DMA((2,))],
    )
    ff_sums = exchange(ff_send, NARROW)
    keep, send = call(
        ff_grads_kernel,
        [((8, 48, D), BF, "V")] * 2,
        [(normed2, "V"), (act, "V"), (grad_pre, "V"), (out_grad, "V")],
        2 * 10**9,
        [pltpu.VMEM((D, FFL), F32), pltpu.VMEM((FFL, D), F32)],
    )
    pieces = [(keep, send)]
    for count, bit_of, move in (
        (4, lambda: lax.axis_index("xl"), swap),
        (2, lambda: lax.axis_index("y") % 2, lambda value: flip(value, "xl", 2, 1)),
        (1, lambda: lax.axis_index("y") // 2, lambda value: flip(value, "y", 4, 1)),
    ):
        keep, send = pieces[-1]
        pieces.append(
            call(
                functools.partial(halve_kernel, bit_of),
                [((count, 48, D), BF, "V")] * 2,
                [(keep, "V"), (move(send), "V")],
                10**8,
            )
        )
    ff_sums = after(ff_sums, pieces[2][0])
    keep, send = pieces[3]
    (ff_part,) = call(
        pair_kernel, [((48, D), BF, "V")], [(keep, "V"), (flip(send, "y", 4, 2), "V")], 10**7
    )
    ff_all = lax.all_gather(ff_part, WIDE, axis=0, tiled=True)
    grad_send, low, grad_mid, result_part, vec2 = call(
        middle_kernel,
        [
            ((32, BLK, 256), BF, "H"), ((BLK, D), BF, "V"), ((BLK, D), F32, "V"), ((BLK, D), BF, "V"),
            ((8, D), F32, "V"),
        ],
        [(ff_sums, "V"), (middle, "V"), (out_grad, "V"), (mixed, "V"), (w_out_pad, "V"), (ln2_gain, "V")],
        10**9,
        [pltpu.VMEM((4, BLK, 256), BF), DMA((32,))],
    )
    grad_same = exchange(grad_send, (*CHIP, *GROUP)).reshape(8, TOK, 256)
    lows = [low] + [flip(low, GROUP, 4, k) for k in (1, 2, 3)]
    grad_same = after(grad_same, *lows, ff_part)
    grad_other = swap(grad_same)
    gqkv, keep, send = call(
        attend_back_kernel,
        [((TOK, 640), BF, "V"), ((16, 48, 384), BF, "V"), ((16, 48, 384), BF, "V")],
        [
            (scene_of_block, "S"), (kv_same, "V"), (kv_other, "V"), (queries, "V"), (grad_same, "V"),
            (grad_other, "V"), (normed, "V"), (mixed, "V"), *[(value, "V") for value in lows],
        ],
        8 * 10**9,
        [pltpu.VMEM((D, 640), F32)],
        vmem=24,
    )
    (weight_send,) = call(
        add_kernel,
        [((16, 48, 384), BF, "H")],
        [(keep, "V"), (swap(send), "V")],
        10**8,
        [pltpu.VMEM((16, 48, 384), BF), DMA],
    )
    weight_parts = exchange(weight_send, (*CHIP, MICRO))
    own, *sends = call(
        normed_grad_kernel,
        [((BLK, D), F32, "V")] + [((BLK, D), BF, "V")] * 3,
        [(gqkv, "V"), (w_qkv, "H")],
        10**9,
        [pltpu.VMEM((3, D, 384), BF), pltpu.VMEM((TOK, D), F32), DMA((3,))],
    )
    parts = [flip(value, GROUP, 4, k + 1) for k, value in enumerate(sends)]
    (packed,) = call(
        input_kernel,
        [((80, D), BF, "V")],
        [
            (own, "V"), *[(value, "V") for value in parts], (tokens, "H"), (ln1_gain, "V"), (grad_mid, "V"),
            (result_part, "V"), (vec2, "V"),
        ],
        10**8,
        [pltpu.VMEM((BLK, D), BF), DMA],
    )
    everyone = [packed] + [flip(packed, NARROW, 8, k) for k in range(1, 8)]
    input_grad, result, vectors = call(
        unpack_kernel,
        [((2, TOK, D), F32, "V"), ((2, TOK, D), BF, "V"), ((8, D), F32, "V")],
        [(value, "V") for value in everyone],
        10**8,
    )
    weight_parts = after(weight_parts, packed)
    (weight_total,) = call(
        sum_kernel,
        [((64, 48, 384), BF, "H")],
        [(weight_parts, "V")],
        10**8,
        [pltpu.VMEM((48, 384), BF), DMA((64,))],
    )
    weight_same = exchange(weight_total, (*CHIP, *NARROW)).reshape(8, 8, 48, 384)
    vectors = vectors + swap(vectors)
    for bits in (1, 2, 4):
        vectors = vectors + flip(vectors, CHIP, 8, bits)
    up_grad, down_grad = call(
        spread_ff_kernel, [((D, FFL), F32, "V"), ((FFL, D), F32, "V")], [(ff_all, "V")], 10**7
    )
    weight_same = after(weight_same, vectors, input_grad, result, up_grad, down_grad)
    weight_other = swap(weight_same)
    scratch = [
        pltpu.VMEM((8, 48, 3 * D), F32), pltpu.VMEM((4, 2, 48, D), F32), DMA((8,)), DMA((4, 2)),
    ]
    grads = [((D, 3 * D), F32, "H"), ((D, D), F32, "H")]
    half = call(
        functools.partial(spread_kernel, False), grads, [(weight_same, "V")], 10**8, scratch
    )
    qkv_grad, out_proj_grad = call(
        functools.partial(spread_kernel, True),
        grads,
        [(weight_other, "V"), (half[0], "H"), (half[1], "H")],
        10**8,
        scratch,
        aliases={1: 0, 2: 1},
    )
    return (
        result, input_grad, qkv_grad, out_proj_grad, vectors[0], vectors[1], vectors[2], vectors[3], up_grad,
        down_grad,
    )


def solution(mesh):
    names = ("y", "xl", "c", "zh", "zl", "xh")
    fine = Mesh(mesh.devices.reshape(4, 2, 2, 2, 2, 2), names)
    tokens = P(None, WIDE, None)
    placed = (
        tokens, P(), P(), P(), P(), P(), P(), P(), P(None, NARROW), P(NARROW, None), tokens
    )
    return jax.shard_map(
        shards,
        mesh=fine,
        in_specs=placed,
        out_specs=(
            tokens, tokens, P(), P(), P(), P(), P(), P(), P(None, NARROW), P(NARROW, None)
        ),
        check_vma=False,
    )
```

```python
import functools

import jax
import jax.numpy as jnp
from jax import lax
from jax.experimental import pallas as pl
from jax.experimental.pallas import tpu as pltpu
from jax.sharding import Mesh
from jax.sharding import PartitionSpec as P

D = 768
HD = 64
FFL = 384
TOK = 128
BLK = 32
EPS = 1e-05
BF = jnp.bfloat16
F32 = jnp.float32

CHIP = ("y", "xl")
CORE = "c"
MICRO = "zh"
GROUP = ("zl", "xh")
NARROW = (MICRO, *GROUP)
WIDE = (*CHIP, CORE)


def chip_index():
    return lax.axis_index("y") * 2 + lax.axis_index("xl")


def group_index():
    return lax.axis_index("zl") * 2 + lax.axis_index("xh")


def mm(left, right):
    return lax.dot_general(left, right, (((1,), (0,)), ((), ())), preferred_element_type=F32)


def mm_nt(left, right):
    return lax.dot_general(left, right, (((1,), (1,)), ((), ())), preferred_element_type=F32)


def mm_tn(left, right):
    return lax.dot_general(left, right, (((0,), (0,)), ((), ())), preferred_element_type=F32)


def normalized(values):
    center = values - jnp.mean(values, axis=-1, keepdims=True)
    spread = jnp.mean(center * center, axis=-1, keepdims=True)
    inverse = lax.rsqrt(spread + EPS)
    return center * inverse, inverse


def norm_back(grad, unit, inverse, gain):
    scaled = grad * gain
    first = jnp.mean(scaled, axis=-1, keepdims=True)
    second = jnp.mean(scaled * unit, axis=-1, keepdims=True)
    return inverse * (scaled - first - unit * second)


def halves(block):
    lane = lax.broadcasted_iota(jnp.int32, block.shape, 1)
    zero = jnp.zeros_like(block)
    return jnp.where(lane < HD, block, zero), jnp.where(lane < HD, zero, block)


def join(low, high):
    lane = lax.broadcasted_iota(jnp.int32, low.shape, 1)
    return jnp.where(lane < HD, low, high)


def span(scene_ref):
    micro = lax.axis_index(MICRO)
    own = scene_ref[micro, chip_index() * 4]
    first = jnp.int32(0)
    count = jnp.int32(0)
    for index in range(8):
        other = scene_ref[micro, index * 4]
        first += (other < own).astype(jnp.int32)
        count += (other == own).astype(jnp.int32)
    return first, count > 1


def three(value):
    a = value.astype(BF).astype(F32)
    b = (value - a).astype(BF).astype(F32)
    c = value - a - b
    return a, b, c


def put_columns(width, rows, start, columns):
    lane = lax.broadcasted_iota(jnp.int32, (rows, width), 1)
    out = jnp.zeros((rows, width), F32)
    for offset, column in enumerate(columns):
        out = jnp.where(lane == start + offset, column, out)
    return out


def pin(value):
    return pltpu.with_memory_space_constraint(value, pltpu.HBM)


def call(kernel, outs, ins, cost, scratch=(), vmem=16, aliases=None):
    places = {"V": pltpu.VMEM, "H": pltpu.HBM, "S": pltpu.SMEM, "L": pltpu.VMEM}
    return pl.pallas_call(
        kernel,
        out_shape=[
            (pltpu.HBM if place in "HL" else jax.ShapeDtypeStruct)(shape, dtype) for shape, dtype, place in outs
        ],
        in_specs=[pl.BlockSpec(memory_space=places[place]) for _, place in ins],
        out_specs=[pl.BlockSpec(memory_space=places[place]) for _, _, place in outs],
        scratch_shapes=list(scratch),
        input_output_aliases=aliases or {},
        cost_estimate=pl.CostEstimate(flops=cost, bytes_accessed=2000000, transcendentals=0),
        compiler_params=pltpu.CompilerParams(vmem_limit_bytes=vmem * 2**20),
    )(*[pin(value) if place in "HL" else value for value, place in ins])


DMA = pltpu.SemaphoreType.DMA


def send_copies(source, target, indices, sem):
    copies = [pltpu.make_async_copy(source, target.at[index], sem.at[index]) for index in indices]
    for copy in copies:
        copy.start()
    return copies


def wait_all(copies):
    for copy in copies:
        copy.wait()


def weight_copies(w_ref, w_buf, w_sem):
    group = group_index()
    copies = []
    for slot, part in enumerate((1, 2, 0)):
        column = pl.multiple_of(part * D + (group // 2) * 384, 128)
        copy = pltpu.make_async_copy(w_ref.at[:, pl.ds(column, 384)], w_buf.at[slot], w_sem.at[slot])
        copy.start()
        copies.append(copy)
    return copies


def project_kernel(
    tok_ref, gain_ref, shift_ref, w_ref, kv_ref, q_ref, normed_ref,
    x_buf, w_buf, kv_buf, gain_buf, shift_buf, x_sem, w_sem, kv_sem, gain_sem, shift_sem,
):
    copy_x = pltpu.make_async_copy(tok_ref.at[lax.axis_index(MICRO)], x_buf, x_sem)
    copy_x.start()
    copy_gain = pltpu.make_async_copy(gain_ref, gain_buf, gain_sem)
    copy_gain.start()
    copy_shift = pltpu.make_async_copy(shift_ref, shift_buf, shift_sem)
    copy_shift.start()
    copies = weight_copies(w_ref, w_buf, w_sem)
    wait_all([copy_x, copy_gain, copy_shift])
    unit, _ = normalized(x_buf[...].astype(F32))
    normed = (unit * gain_buf[...].reshape(1, D) + shift_buf[...].reshape(1, D)).astype(BF)
    odd = (group_index() % 2) == 1

    def part(slot):
        copies[slot].wait()
        full = mm(normed, w_buf[slot])
        return jnp.where(odd, full[:, 192:], full[:, :192]).astype(BF)

    kv_buf[...] = jnp.concatenate([part(0), part(1)], axis=1)
    sends = send_copies(kv_buf, kv_ref, range(8), kv_sem)
    normed_ref[...] = normed
    q_ref[...] = jnp.concatenate([part(2), jnp.zeros((TOK, HD), BF)], axis=1)
    wait_all(sends)


def attend_kernel(scene_ref, q_ref, same_ref, other_ref, out_ref, buf, sem):
    first, big = span(scene_ref)

    def run(count):
        rows = count * TOK
        keys = jnp.concatenate(
            [ref[pl.ds(first, count)].reshape(rows, 384) for ref in (same_ref, other_ref)], axis=0
        )
        query = q_ref[...]
        q0, q1 = halves(query[:, :128])
        blocks = [keys[:, :128], keys[:, 128:256], keys[:, 256:]]
        mixed = []
        columns = []
        for qh, kb, vb in ((q0, 0, 1), (q1, 0, 2), (query[:, 128:], 1, 2)):
            scores = mm_nt(qh, blocks[kb]) * (HD**-0.5)
            top = jnp.max(scores, axis=-1, keepdims=True)
            weights = jnp.exp(scores - top)
            total = jnp.sum(weights, axis=-1, keepdims=True)
            probs = (weights * (1.0 / total)).astype(BF)
            mixed.append(mm(probs, blocks[vb]))
            columns += three(top + jnp.log(total))
        stats = put_columns(128, TOK, 0, columns)
        buf[...] = jnp.concatenate([join(stats, mixed[0]), join(mixed[1], mixed[2])], axis=1).astype(BF)

    @pl.when(big)
    def _():
        run(5)

    @pl.when(jnp.logical_not(big))
    def _():
        run(1)

    wait_all(send_copies(buf, out_ref, range(8), sem))


def forward_kernel(
    mixed_ref, tok_ref, og_ref, wo_ref, gain_ref, shift_ref, up_ref, down_ref,
    out_ref, middle_ref, normed_ref, act_ref, gpre_ref, grad_buf, branch_buf, sem,
):
    total = tok_ref[...].reshape(2 * TOK, D).astype(F32)
    for group in range(4):
        rows = jnp.concatenate([mixed_ref[group], mixed_ref[4 + group]], axis=0)
        total = total + mm(rows, wo_ref[group])
    middle_ref[...] = total.reshape(8, BLK, D)
    unit, _ = normalized(total)
    normed = (unit * gain_ref[...].reshape(1, D) + shift_ref[...].reshape(1, D)).astype(BF)
    normed_ref[...] = normed
    pre = mm(normed, up_ref[...])
    cdf = 0.5 * (1.0 + lax.erf(pre * (0.5**0.5)))
    slope = cdf + pre * jnp.exp(-0.5 * pre * pre) * 0.3989422804014327
    grad_out = og_ref[...].reshape(2 * TOK, D)
    gpre = (mm_nt(grad_out, down_ref[...]) * slope).astype(BF)
    gpre_ref[...] = gpre
    grad_buf[...] = mm_nt(gpre, up_ref[...]).astype(BF).reshape(8, BLK, D)
    first = pltpu.make_async_copy(grad_buf, out_ref.at[:, pl.ds(BLK, BLK)], sem.at[0])
    first.start()
    act = (pre * cdf).astype(BF)
    act_ref[...] = act
    branch_buf[...] = mm(act, down_ref[...]).astype(BF).reshape(8, BLK, D)
    second = pltpu.make_async_copy(branch_buf, out_ref.at[:, pl.ds(0, BLK)], sem.at[1])
    second.start()
    first.wait()
    second.wait()


def ff_grads_kernel(normed_ref, act_ref, gpre_ref, og_ref, keep_ref, send_ref, up_buf, down_buf):
    core = lax.axis_index(CORE)
    up_buf[...] = mm_tn(normed_ref[...], gpre_ref[...])
    down_buf[...] = mm_tn(act_ref[...], og_ref[...].reshape(2 * TOK, D))
    for ref, owner in ((keep_ref, core), (send_ref, 1 - core)):
        column = pl.multiple_of(owner * 384, 128)
        for tile in range(8):
            rows = pl.ds(pl.multiple_of((2 * tile + owner) * 48, 16), 48)
            ref[tile, :, :384] = up_buf[rows].astype(BF)
            ref[tile, :, 384:] = down_buf[tile * 48:(tile + 1) * 48, pl.ds(column, 384)].astype(BF)


def split_kernel(one_ref, two_ref, *refs):
    y = lax.axis_index("y")
    for k, ref in enumerate(refs):
        for xl in range(2):
            at = (y ^ k) * 2 + xl
            ref[xl] = (one_ref[at].astype(F32) + two_ref[at].astype(F32)).astype(BF)


def halve_kernel(*refs):
    parts, (keep_ref, send_ref) = refs[:4], refs[4:]
    xl = lax.axis_index("xl")
    for ref, at in ((keep_ref, xl), (send_ref, 1 - xl)):
        total = parts[0][at].astype(F32)
        for part in parts[1:]:
            total = total + part[at].astype(F32)
        ref[...] = total.astype(BF)


def pair_kernel(one_ref, two_ref, out_ref):
    out_ref[...] = (one_ref[...].astype(F32) + two_ref[...].astype(F32)).astype(BF)


def middle_kernel(
    sums_ref, middle_ref, og_ref, mixed_ref, wo_ref, gain_ref,
    out_ref, low_ref, grad_ref, result_ref, vec_ref, buf, sem,
):
    micro = lax.axis_index(MICRO)
    group = group_index()
    start = pl.multiple_of(group * BLK, BLK)
    total = sums_ref[0].astype(F32)
    for index in range(1, 8):
        total = total + sums_ref[index].astype(F32)
    branch, grad = total[:BLK], total[BLK:]
    middle = middle_ref[micro * 4 + group]
    unit, inverse = normalized(middle)
    grad_mid = og_ref[micro, pl.ds(start, BLK)].astype(F32) + norm_back(
        grad, unit, inverse, gain_ref[...].reshape(1, D)
    )
    low = grad_mid.astype(BF)
    lane = lax.broadcasted_iota(jnp.int32, (BLK, 256), 1)
    sends = []
    for head_group in range(4):
        mixed = mixed_ref[micro * 4 + head_group, pl.ds(start, BLK)].astype(F32)
        back = mm_nt(low, wo_ref[head_group]).astype(BF).astype(F32)
        product = mixed * back
        columns = []
        for head in range(3):
            inside = (lane >= (head + 1) * HD) & (lane < (head + 2) * HD)
            columns += three(jnp.sum(jnp.where(inside, product, 0.0), axis=-1, keepdims=True))
        stats = put_columns(256, BLK, 9, columns)
        buf[head_group] = jnp.where(lane < 9, mixed, jnp.where(lane < HD, stats, back)).astype(BF)
        sends += send_copies(
            buf.at[head_group], out_ref, [chip * 4 + head_group for chip in range(8)], sem
        )
    low_ref[...] = low
    grad_ref[...] = grad_mid
    result_ref[...] = (middle + branch).astype(BF)
    gain_grad = jnp.sum(grad * unit, axis=0, keepdims=True)
    shift_grad = jnp.sum(grad, axis=0, keepdims=True)
    vec_ref[...] = jnp.concatenate([gain_grad, shift_grad, jnp.zeros((6, D), F32)], axis=0)
    wait_all(sends)


def attend_back_kernel(
    scene_ref, kvs_ref, kvo_ref, q_ref, gs_ref, go_ref, normed_ref, mixed_ref, low0_ref, low1_ref, low2_ref,
    low3_ref, gqkv_ref, keep_ref, send_ref, grad_buf,
):
    first, big = span(scene_ref)
    chip = chip_index()
    core = lax.axis_index(CORE)
    group = group_index()
    scale = HD**-0.5

    def run(count):
        rows = count * TOK

        def cut(value):
            return [value[:, at:at + 128] for at in range(0, value.shape[1], 128)]

        def gathered(one, two, width):
            return cut(jnp.concatenate(
                [ref[pl.ds(first, count)].reshape(rows, width) for ref in (one, two)], axis=0
            ))

        kv = gathered(kvs_ref, kvo_ref, 384)
        grad = gathered(gs_ref, go_ref, 256)
        query = cut(jnp.concatenate(
            [q_ref[pl.ds(first, count), which].reshape(rows, 256) for which in (core, 1 - core)], axis=0
        ))
        kv_own = cut(kvs_ref[chip])
        q_own = cut(q_ref[chip, core])
        g_own = cut(gs_ref[chip])
        q_heads = [*halves(q_own[0]), q_own[1]]
        g_heads = [halves(g_own[0])[1], *halves(g_own[1])]
        k_heads = [*halves(kv_own[0]), halves(kv_own[1])[0]]
        v_heads = [halves(kv_own[1])[1], *halves(kv_own[2])]
        own_stats = g_own[0].astype(F32)
        all_stats = grad[0].astype(F32).T

        def column(at):
            return own_stats[:, at:at + 1] + own_stats[:, at + 1:at + 2] + own_stats[:, at + 2:at + 3]

        def row(at):
            return all_stats[at:at + 1] + all_stats[at + 1:at + 2] + all_stats[at + 2:at + 3]

        dq, dk, dv = [], [], []
        for head, (kb, vb) in enumerate(((0, 1), (0, 2), (1, 2))):
            qb, gb = (0, 0, 1)[head], (0, 1, 1)[head]
            probs = jnp.exp(mm_nt(q_heads[head], kv[kb]) * scale - column(3 * head))
            gap = mm_nt(g_heads[head], kv[vb]) - column(9 + 3 * head)
            dq.append(mm((probs * gap).astype(BF), kv[kb]) * scale)
            probs = jnp.exp(mm_nt(k_heads[head], query[qb]) * scale - row(3 * head))
            gap = mm_nt(v_heads[head], grad[gb]) - row(9 + 3 * head)
            dv.append(mm(probs.astype(BF), grad[gb]))
            dk.append(mm((probs * gap).astype(BF), query[qb]) * scale)
        tail = dq[2]
        gqkv_ref[...] = jnp.concatenate(
            [join(dk[0], dk[1]), join(dk[2], dv[0]), join(dv[1], dv[2]), join(dq[0], dq[1]),
             join(tail, jnp.zeros_like(tail))],
            axis=1,
        ).astype(BF)

    @pl.when(big)
    def _():
        run(5)

    @pl.when(jnp.logical_not(big))
    def _():
        run(1)

    grad_buf[...] = mm_tn(normed_ref[...], gqkv_ref[...])
    index = lax.axis_index(MICRO) * 4 + group
    low = jnp.concatenate([ref[...] for ref in (low0_ref, low1_ref, low2_ref, low3_ref)], axis=0)
    mixed = jnp.concatenate(
        [mixed_ref[index, pl.ds(pl.multiple_of((group ^ k) * BLK, BLK), BLK)] for k in range(4)], axis=0
    )
    out = mm_tn(mixed, low)[HD:]
    for ref, owner in ((keep_ref, core), (send_ref, 1 - core)):
        for tile in range(8):
            rows = grad_buf[pl.ds(pl.multiple_of((2 * tile + owner) * 48, 16), 48)]
            at = (tile // 4) * 96
            pieces = [
                out[at + row * 48:at + (row + 1) * 48, (tile % 4) * 192:(tile % 4 + 1) * 192] for row in range(2)
            ]
            ref[2 * tile] = rows[:, :384].astype(BF)
            ref[2 * tile + 1] = jnp.concatenate(
                [rows[:, 384:576], jnp.where(owner == 1, pieces[1], pieces[0])], axis=1
            ).astype(BF)


def add_kernel(one_ref, two_ref, out_ref, buf, sem):
    buf[...] = (one_ref[...].astype(F32) + two_ref[...].astype(F32)).astype(BF)
    copy = pltpu.make_async_copy(buf, out_ref, sem)
    copy.start()
    copy.wait()


def sum_kernel(in_ref, vec_ref, out_ref, buf, sem):
    total = in_ref[0].astype(F32)
    for index in range(1, 16):
        total = total + in_ref[index].astype(F32)
    vectors = vec_ref[...][:4]
    block = jnp.concatenate([total, vectors[:, :384], vectors[:, 384:]], axis=0).astype(BF)
    for index in range(8):
        buf[index] = block
    wait_all(send_copies(buf, out_ref, range(8), sem))


def spread_kernel(turn, in_ref, *refs):
    qkv_buf, out_buf, sem, out_sem = refs[-4:]
    qkv_ref, out_ref, *vec_refs = refs[3:-4] if turn else refs[:-4]
    owner = lax.axis_index(CORE)
    owner = 1 - owner if turn else owner
    copies = []
    vectors = jnp.zeros((8, 384), F32)
    for tile in range(8):
        whole = [in_ref[tile, index].astype(F32) for index in range(8)]
        block = [value[:48] for value in whole]
        for value in whole:
            vectors = vectors + value[48:]
        for part, half, at in ((1, 0, 0), (2, 0, 192), (0, 4, 0)):
            qkv_buf[tile, :, part * D:(part + 1) * D] = jnp.concatenate(
                [block[half + group][:, at:at + 192] for group in range(4)], axis=1
            )
        start = pl.multiple_of((2 * tile + owner) * 48, 16)
        copy = pltpu.make_async_copy(qkv_buf.at[tile], qkv_ref.at[pl.ds(start, 48)], sem.at[tile])
        copy.start()
        copies.append(copy)
        for group in range(4):
            out_buf[group, tile // 4, :, (tile % 4) * 192:(tile % 4 + 1) * 192] = block[4 + group][:, 192:]
    for group in range(4):
        for pair in range(2):
            start = pl.multiple_of(group * 192 + (pair * 2 + owner) * 48, 16)
            copy = pltpu.make_async_copy(
                out_buf.at[group, pair], out_ref.at[pl.ds(start, 48)], out_sem.at[group, pair]
            )
            copy.start()
            copies.append(copy)
    if turn:
        vectors = vectors + refs[0][...]
        for k, ref in enumerate(vec_refs):
            ref[...] = jnp.concatenate([vectors[k:k + 1], vectors[4 + k:5 + k]], axis=1).reshape(D)
    else:
        vec_refs[0][...] = vectors
    wait_all(copies)


def spread_ff_kernel(in_ref, up_ref, down_ref):
    up_ref[...] = in_ref[:, :384].astype(F32)
    for tile in range(16):
        half = (tile % 2) * 384
        down_ref[(tile // 2) * 48:(tile // 2 + 1) * 48, half:half + 384] = in_ref[
            tile * 48:(tile + 1) * 48, 384:
        ].astype(F32)


def normed_grad_kernel(gqkv_ref, w_ref, own_ref, one_ref, two_ref, three_ref, w_buf, buf, w_sem):
    copies = weight_copies(w_ref, w_buf, w_sem)
    group = group_index()
    odd = (group % 2) == 1
    total = jnp.zeros((TOK, D), F32)
    for slot in range(3):
        copies[slot].wait()
        part = gqkv_ref[:, slot * 192:(slot + 1) * 192]
        zero = jnp.zeros_like(part)
        wide = jnp.where(
            odd, jnp.concatenate([zero, part], axis=1), jnp.concatenate([part, zero], axis=1)
        )
        total = total + mm_nt(wide, w_buf[slot])
    buf[...] = total
    own_ref[...] = buf[pl.ds(pl.multiple_of(group * BLK, BLK), BLK)]
    for k, ref in ((1, one_ref), (2, two_ref), (3, three_ref)):
        ref[...] = buf[pl.ds(pl.multiple_of((group ^ k) * BLK, BLK), BLK)].astype(BF)


def input_kernel(
    own_ref, one_ref, two_ref, three_ref, tok_ref, gain_ref, grad_ref, result_ref, vec_ref, out_ref, sums_ref,
    x_buf, sem,
):
    start = pl.multiple_of(group_index() * BLK, BLK)
    copy = pltpu.make_async_copy(tok_ref.at[lax.axis_index(MICRO), pl.ds(start, BLK)], x_buf, sem)
    copy.start()
    total = own_ref[...]
    for ref in (one_ref, two_ref, three_ref):
        total = total + ref[...].astype(F32)
    copy.wait()
    unit, inverse = normalized(x_buf[...].astype(F32))
    grad = grad_ref[...] + norm_back(total, unit, inverse, gain_ref[...].reshape(1, D))
    gain1 = jnp.sum(total * unit, axis=0, keepdims=True)
    shift1 = jnp.sum(total, axis=0, keepdims=True)
    sums_ref[...] = jnp.concatenate([gain1, shift1, vec_ref[...][:2], jnp.zeros((4, D), F32)], axis=0)
    out_ref[:BLK] = grad.astype(BF)
    out_ref[BLK:] = result_ref[...]


def unpack_kernel(*refs):
    parts, (grad_ref, result_ref) = refs[:8], refs[9:]
    micro = lax.axis_index(MICRO)
    group = group_index()
    for k, ref in enumerate(parts):
        rows = pl.ds(pl.multiple_of((group ^ (k % 4)) * BLK, BLK), BLK)
        where = micro ^ (k // 4)
        grad_ref[where, rows] = ref[:BLK].astype(F32)
        result_ref[where, rows] = ref[BLK:]


def exchange(value, axes):
    return lax.all_to_all(value, axes, 0, 0, tiled=True)


def swap(value):
    return lax.ppermute(value, CORE, [(0, 1), (1, 0)])


def after(value, *others):
    return pl.pallas_call(
        lambda *refs: None,
        out_shape=jax.ShapeDtypeStruct(value.shape, value.dtype),
        in_specs=[pl.BlockSpec(memory_space=pl.ANY)] * (1 + len(others)),
        out_specs=pl.BlockSpec(memory_space=pl.ANY),
        input_output_aliases={0: 0},
        cost_estimate=pl.CostEstimate(flops=1, bytes_accessed=1, transcendentals=0),
        compiler_params=pltpu.CompilerParams(vmem_limit_bytes=2**20),
    )(value, *others)


def flip(value, axes, count, bits):
    return lax.ppermute(value, axes, [(index, index ^ bits) for index in range(count)])


def shards(
    tokens, scene_of_block, ln1_gain, ln1_shift, w_qkv, w_out, ln2_gain, ln2_shift, w_up, w_down, out_grad
):
    w_out_pad = jnp.pad(w_out.reshape(4, 192, D), ((0, 0), (HD, 0), (0, 0)))
    kv_send, query, normed = call(
        project_kernel,
        [((8, TOK, 384), BF, "H"), ((TOK, 256), BF, "L"), ((TOK, D), BF, "L")],
        [(tokens, "H"), (ln1_gain, "H"), (ln1_shift, "H"), (w_qkv, "H")],
        10**9,
        [
            pltpu.VMEM((TOK, D), BF), pltpu.VMEM((3, D, 384), BF), pltpu.VMEM((TOK, 384), BF),
            pltpu.VMEM((D,), F32), pltpu.VMEM((D,), F32), DMA, DMA((3,)), DMA((8,)), DMA, DMA,
        ],
    )
    kv_same = exchange(kv_send, CHIP)
    kv_other = swap(kv_same)
    (mixed_send,) = call(
        attend_kernel,
        [((8, TOK, 256), BF, "H")],
        [(scene_of_block, "S"), (query, "L"), (kv_same, "V"), (kv_other, "V")],
        2 * 10**9,
        [pltpu.VMEM((TOK, 256), BF), DMA((8,))],
    )
    mixed = exchange(mixed_send, NARROW)
    queries = lax.all_gather(query, WIDE, axis=0, tiled=True).reshape(8, 2, TOK, 256)
    ff_send, middle, normed2, act, grad_pre = call(
        forward_kernel,
        [
            ((8, 2 * BLK, D), BF, "H"), ((8, BLK, D), F32, "L"), ((2 * TOK, D), BF, "V"),
            ((2 * TOK, FFL), BF, "V"), ((2 * TOK, FFL), BF, "V"),
        ],
        [
            (mixed, "V"), (tokens, "L"), (out_grad, "L"), (w_out_pad, "L"), (ln2_gain, "L"), (ln2_shift, "L"),
            (w_up, "L"), (w_down, "L"),
        ],
        4 * 10**9,
        [pltpu.VMEM((8, BLK, D), BF), pltpu.VMEM((8, BLK, D), BF), DMA((2,))],
    )
    ff_sums = exchange(ff_send, NARROW)
    keep, send = call(
        ff_grads_kernel,
        [((8, 48, D), BF, "V")] * 2,
        [(normed2, "V"), (act, "V"), (grad_pre, "V"), (out_grad, "L")],
        2 * 10**9,
        [pltpu.VMEM((D, FFL), F32), pltpu.VMEM((FFL, D), F32)],
    )
    pieces = call(
        split_kernel, [((2, 48, D), BF, "L")] * 4, [(keep, "V"), (swap(send), "V")], 10**8
    )
    pieces = [pieces[0]] + [flip(pieces[k], "y", 4, k) for k in (1, 2, 3)]
    keep, send = call(
        halve_kernel, [((48, D), BF, "L")] * 2, [(pieces[0], "L")] + [(piece, "V") for piece in pieces[1:]], 10**8
    )
    ff_sums = after(ff_sums, pin(keep))
    (ff_part,) = call(
        pair_kernel, [((48, D), BF, "L")], [(keep, "L"), (flip(send, "xl", 2, 1), "V")], 10**7
    )
    ff_all = lax.all_gather(ff_part, WIDE, axis=0, tiled=True)
    grad_send, low, grad_mid, result_part, vec2 = call(
        middle_kernel,
        [
            ((32, BLK, 256), BF, "H"), ((BLK, D), BF, "L"), ((BLK, D), F32, "L"), ((BLK, D), BF, "L"),
            ((8, D), F32, "L"),
        ],
        [(ff_sums, "V"), (middle, "L"), (out_grad, "L"), (mixed, "L"), (w_out_pad, "L"), (ln2_gain, "L")],
        10**9,
        [pltpu.VMEM((4, BLK, 256), BF), DMA((32,))],
    )
    grad_same = exchange(grad_send, (*CHIP, *GROUP)).reshape(8, TOK, 256)
    lows = [flip(low, GROUP, 4, k) for k in (1, 2, 3)]
    grad_same = after(grad_same, *lows, pin(ff_part))
    grad_other = swap(grad_same)
    gqkv, keep, send = call(
        attend_back_kernel,
        [((TOK, 640), BF, "L"), ((16, 48, 384), BF, "V"), ((16, 48, 384), BF, "V")],
        [
            (scene_of_block, "S"), (kv_same, "L"), (kv_other, "L"), (queries, "L"), (grad_same, "V"),
            (grad_other, "V"), (normed, "L"), (mixed, "L"), (low, "L"), *[(value, "V") for value in lows],
        ],
        8 * 10**9,
        [pltpu.VMEM((D, 640), F32)],
    )
    (weight_send,) = call(
        add_kernel,
        [((16, 48, 384), BF, "H")],
        [(keep, "V"), (swap(send), "V")],
        10**8,
        [pltpu.VMEM((16, 48, 384), BF), DMA],
    )
    weight_parts = exchange(weight_send, (*CHIP, MICRO))
    own, *sends = call(
        normed_grad_kernel,
        [((BLK, D), F32, "L")] + [((BLK, D), BF, "L")] * 3,
        [(gqkv, "L"), (w_qkv, "H")],
        10**9,
        [pltpu.VMEM((3, D, 384), BF), pltpu.VMEM((TOK, D), F32), DMA((3,))],
    )
    parts = [flip(value, GROUP, 4, k + 1) for k, value in enumerate(sends)]
    packed, sums = call(
        input_kernel,
        [((2 * BLK, D), BF, "L"), ((8, D), F32, "L")],
        [
            (own, "L"), *[(value, "V") for value in parts], (tokens, "H"), (ln1_gain, "L"), (grad_mid, "L"),
            (result_part, "L"), (vec2, "L"),
        ],
        10**8,
        [pltpu.VMEM((BLK, D), BF), DMA],
    )
    everyone = [packed] + [flip(packed, NARROW, 8, k) for k in range(1, 8)]
    input_grad, result = call(
        unpack_kernel,
        [((2, TOK, D), F32, "L"), ((2, TOK, D), BF, "L")],
        [(packed, "L"), *[(value, "V") for value in everyone[1:]], (ff_all, "H")],
        10**8,
    )
    (weight_total,) = call(
        sum_kernel,
        [((8, 8, 56, 384), BF, "H")],
        [(weight_parts, "V"), (sums, "L")],
        10**8,
        [pltpu.VMEM((8, 56, 384), BF), DMA((8,))],
    )
    weight_same = exchange(weight_total.reshape(64, 56, 384), (*CHIP, *NARROW)).reshape(8, 8, 56, 384)
    up_grad, down_grad = call(
        spread_ff_kernel, [((D, FFL), F32, "L"), ((FFL, D), F32, "L")], [(ff_all, "L")], 10**7
    )
    weight_same = after(weight_same, *map(pin, (input_grad, result, up_grad, down_grad)))
    weight_other = swap(weight_same)
    scratch = [
        pltpu.VMEM((8, 48, 3 * D), F32), pltpu.VMEM((4, 2, 48, D), F32), DMA((8,)), DMA((4, 2)),
    ]
    grads = [((D, 3 * D), F32, "H"), ((D, D), F32, "H")]
    half = call(
        functools.partial(spread_kernel, False), grads + [((8, 384), F32, "V")], [(weight_same, "V")], 10**8, scratch
    )
    qkv_grad, out_proj_grad, *vectors = call(
        functools.partial(spread_kernel, True),
        grads + [((D,), F32, "L")] * 4,
        [(weight_other, "V"), (half[2], "V"), (half[0], "H"), (half[1], "H")],
        10**8,
        scratch,
        aliases={2: 0, 3: 1},
    )
    return (
        result, input_grad, qkv_grad, out_proj_grad, *vectors, up_grad, down_grad
    )


def solution(mesh):
    names = ("y", "xl", "c", "zh", "zl", "xh")
    fine = Mesh(mesh.devices.reshape(4, 2, 2, 2, 2, 2), names)
    tokens = P(None, WIDE, None)
    placed = (
        tokens, P(), P(), P(), P(), P(), P(), P(), P(None, NARROW), P(NARROW, None), tokens
    )
    return jax.shard_map(
        shards,
        mesh=fine,
        in_specs=placed,
        out_specs=(
            tokens, tokens, P(), P(), P(), P(), P(), P(), P(None, NARROW), P(NARROW, None)
        ),
        check_vma=False,
    )
```

```python
import functools

import jax
import jax.numpy as jnp
from jax import lax
from jax.experimental import pallas as pl
from jax.experimental.pallas import tpu as pltpu
from jax.sharding import Mesh
from jax.sharding import PartitionSpec as P

D = 768
HD = 64
FFL = 384
TOK = 128
BLK = 32
EPS = 1e-05
BF = jnp.bfloat16
F32 = jnp.float32

CHIP = ("y", "xl")
CORE = "c"
MICRO = "zh"
GROUP = ("zl", "xh")
NARROW = (MICRO, *GROUP)
WIDE = (*CHIP, CORE)


def chip_index():
    return lax.axis_index("y") * 2 + lax.axis_index("xl")


def group_index():
    return lax.axis_index("zl") * 2 + lax.axis_index("xh")


def mm(left, right):
    return lax.dot_general(left, right, (((1,), (0,)), ((), ())), preferred_element_type=F32)


def mm_nt(left, right):
    return lax.dot_general(left, right, (((1,), (1,)), ((), ())), preferred_element_type=F32)


def mm_tn(left, right):
    return lax.dot_general(left, right, (((0,), (0,)), ((), ())), preferred_element_type=F32)


def normalized(values):
    center = values - jnp.mean(values, axis=-1, keepdims=True)
    spread = jnp.mean(center * center, axis=-1, keepdims=True)
    inverse = lax.rsqrt(spread + EPS)
    return center * inverse, inverse


def norm_back(grad, unit, inverse, gain):
    scaled = grad * gain
    first = jnp.mean(scaled, axis=-1, keepdims=True)
    second = jnp.mean(scaled * unit, axis=-1, keepdims=True)
    return inverse * (scaled - first - unit * second)


def halves(block):
    lane = lax.broadcasted_iota(jnp.int32, block.shape, 1)
    zero = jnp.zeros_like(block)
    return jnp.where(lane < HD, block, zero), jnp.where(lane < HD, zero, block)


def join(low, high):
    lane = lax.broadcasted_iota(jnp.int32, low.shape, 1)
    return jnp.where(lane < HD, low, high)


def span(scene_ref):
    micro = lax.axis_index(MICRO)
    own = scene_ref[micro, chip_index() * 4]
    first = jnp.int32(0)
    count = jnp.int32(0)
    for index in range(8):
        other = scene_ref[micro, index * 4]
        first += (other < own).astype(jnp.int32)
        count += (other == own).astype(jnp.int32)
    return first, count > 1


def three(value):
    a = value.astype(BF).astype(F32)
    b = (value - a).astype(BF).astype(F32)
    c = value - a - b
    return a, b, c


def put_columns(width, rows, start, columns):
    lane = lax.broadcasted_iota(jnp.int32, (rows, width), 1)
    out = jnp.zeros((rows, width), F32)
    for offset, column in enumerate(columns):
        out = jnp.where(lane == start + offset, column, out)
    return out


def pin(value):
    return pltpu.with_memory_space_constraint(value, pltpu.HBM)


def call(kernel, outs, ins, cost, scratch=(), vmem=16, aliases=None):
    places = {"V": pltpu.VMEM, "H": pltpu.HBM, "S": pltpu.SMEM, "L": pltpu.VMEM}
    return pl.pallas_call(
        kernel,
        out_shape=[
            (pltpu.HBM if place in "HL" else jax.ShapeDtypeStruct)(shape, dtype) for shape, dtype, place in outs
        ],
        in_specs=[pl.BlockSpec(memory_space=places[place]) for _, place in ins],
        out_specs=[pl.BlockSpec(memory_space=places[place]) for _, _, place in outs],
        scratch_shapes=list(scratch),
        input_output_aliases=aliases or {},
        cost_estimate=pl.CostEstimate(flops=cost, bytes_accessed=2000000, transcendentals=0),
        compiler_params=pltpu.CompilerParams(vmem_limit_bytes=vmem * 2**20),
    )(*[pin(value) if place in "HL" else value for value, place in ins])


DMA = pltpu.SemaphoreType.DMA


def send_copies(source, target, indices, sem):
    copies = [pltpu.make_async_copy(source, target.at[index], sem.at[index]) for index in indices]
    for copy in copies:
        copy.start()
    return copies


def wait_all(copies):
    for copy in copies:
        copy.wait()


def weight_copies(w_ref, w_buf, w_sem):
    group = group_index()
    copies = []
    for slot, part in enumerate((1, 2, 0)):
        column = pl.multiple_of(part * D + (group // 2) * 384, 128)
        copy = pltpu.make_async_copy(w_ref.at[:, pl.ds(column, 384)], w_buf.at[slot], w_sem.at[slot])
        copy.start()
        copies.append(copy)
    return copies


def project_kernel(
    tok_ref, gain_ref, shift_ref, w_ref, kv_ref, normed_ref,
    x_buf, w_buf, kv_buf, gain_buf, shift_buf, x_sem, w_sem, kv_sem, gain_sem, shift_sem,
):
    copy_x = pltpu.make_async_copy(tok_ref.at[lax.axis_index(MICRO)], x_buf, x_sem)
    copy_x.start()
    copy_gain = pltpu.make_async_copy(gain_ref, gain_buf, gain_sem)
    copy_gain.start()
    copy_shift = pltpu.make_async_copy(shift_ref, shift_buf, shift_sem)
    copy_shift.start()
    copies = weight_copies(w_ref, w_buf, w_sem)
    wait_all([copy_x, copy_gain, copy_shift])
    unit, _ = normalized(x_buf[...].astype(F32))
    normed = (unit * gain_buf[...].reshape(1, D) + shift_buf[...].reshape(1, D)).astype(BF)
    odd = (group_index() % 2) == 1

    def part(slot):
        copies[slot].wait()
        full = mm(normed, w_buf[slot])
        return jnp.where(odd, full[:, 192:], full[:, :192]).astype(BF)

    kv_buf[...] = jnp.concatenate([part(0), part(1), part(2), jnp.zeros((TOK, HD), BF)], axis=1)
    sends = send_copies(kv_buf, kv_ref, range(8), kv_sem)
    normed_ref[...] = normed
    wait_all(sends)


def attend_kernel(scene_ref, same_ref, other_ref, out_ref, buf, sem):
    first, big = span(scene_ref)

    def run(count):
        rows = count * TOK
        keys = jnp.concatenate(
            [ref[pl.ds(first, count), :, :384].reshape(rows, 384) for ref in (same_ref, other_ref)], axis=0
        )
        query = same_ref[chip_index(), :, 384:]
        q0, q1 = halves(query[:, :128])
        blocks = [keys[:, :128], keys[:, 128:256], keys[:, 256:]]
        mixed = []
        columns = []
        for qh, kb, vb in ((q0, 0, 1), (q1, 0, 2), (query[:, 128:], 1, 2)):
            scores = mm_nt(qh, blocks[kb]) * (HD**-0.5)
            top = jnp.max(scores, axis=-1, keepdims=True)
            weights = jnp.exp(scores - top)
            total = jnp.sum(weights, axis=-1, keepdims=True)
            probs = (weights * (1.0 / total)).astype(BF)
            mixed.append(mm(probs, blocks[vb]))
            columns += three(top + jnp.log(total))
        stats = put_columns(128, TOK, 0, columns)
        buf[...] = jnp.concatenate([join(stats, mixed[0]), join(mixed[1], mixed[2])], axis=1).astype(BF)

    @pl.when(big)
    def _():
        run(5)

    @pl.when(jnp.logical_not(big))
    def _():
        run(1)

    wait_all(send_copies(buf, out_ref, range(8), sem))


def forward_kernel(
    mixed_ref, tok_ref, og_ref, wo_ref, gain_ref, shift_ref, up_ref, down_ref,
    out_ref, middle_ref, normed_ref, act_ref, gpre_ref, grad_buf, branch_buf, sem,
):
    total = tok_ref[...].reshape(2 * TOK, D).astype(F32)
    for group in range(4):
        rows = jnp.concatenate([mixed_ref[group], mixed_ref[4 + group]], axis=0)
        total = total + mm(rows, wo_ref[group])
    middle_ref[...] = total.reshape(8, BLK, D)
    unit, _ = normalized(total)
    normed = (unit * gain_ref[...].reshape(1, D) + shift_ref[...].reshape(1, D)).astype(BF)
    normed_ref[...] = normed
    pre = mm(normed, up_ref[...])
    cdf = 0.5 * (1.0 + lax.erf(pre * (0.5**0.5)))
    slope = cdf + pre * jnp.exp(-0.5 * pre * pre) * 0.3989422804014327
    grad_out = og_ref[...].reshape(2 * TOK, D)
    gpre = (mm_nt(grad_out, down_ref[...]) * slope).astype(BF)
    gpre_ref[...] = gpre
    grad_buf[...] = mm_nt(gpre, up_ref[...]).astype(BF).reshape(8, BLK, D)
    first = pltpu.make_async_copy(grad_buf, out_ref.at[:, pl.ds(BLK, BLK)], sem.at[0])
    first.start()
    act = (pre * cdf).astype(BF)
    act_ref[...] = act
    branch_buf[...] = mm(act, down_ref[...]).astype(BF).reshape(8, BLK, D)
    second = pltpu.make_async_copy(branch_buf, out_ref.at[:, pl.ds(0, BLK)], sem.at[1])
    second.start()
    first.wait()
    second.wait()


def ff_grads_kernel(normed_ref, act_ref, gpre_ref, og_ref, keep_ref, send_ref, up_buf, down_buf):
    core = lax.axis_index(CORE)
    up_buf[...] = mm_tn(normed_ref[...], gpre_ref[...])
    down_buf[...] = mm_tn(act_ref[...], og_ref[...].reshape(2 * TOK, D))
    for ref, owner in ((keep_ref, core), (send_ref, 1 - core)):
        column = pl.multiple_of(owner * 384, 128)
        for tile in range(8):
            rows = pl.ds(pl.multiple_of((2 * tile + owner) * 48, 16), 48)
            ref[tile, :, :384] = up_buf[rows].astype(BF)
            ref[tile, :, 384:] = down_buf[tile * 48:(tile + 1) * 48, pl.ds(column, 384)].astype(BF)


def split_kernel(one_ref, two_ref, *refs):
    y = lax.axis_index("y")
    for k, ref in enumerate(refs):
        for xl in range(2):
            at = (y ^ k) * 2 + xl
            ref[xl] = (one_ref[at].astype(F32) + two_ref[at].astype(F32)).astype(BF)


def halve_kernel(*refs):
    parts, (keep_ref, send_ref) = refs[:4], refs[4:]
    xl = lax.axis_index("xl")
    for ref, at in ((keep_ref, xl), (send_ref, 1 - xl)):
        total = parts[0][at].astype(F32)
        for part in parts[1:]:
            total = total + part[at].astype(F32)
        ref[...] = total.astype(BF)


def pair_kernel(one_ref, two_ref, out_ref):
    out_ref[...] = (one_ref[...].astype(F32) + two_ref[...].astype(F32)).astype(BF)


def middle_kernel(
    sums_ref, middle_ref, og_ref, tok_ref, mixed_ref, wo_ref, gain_ref,
    out_ref, low_ref, grad_ref, result_ref, vec_ref, x_ref, buf, middle_buf, og_buf, mixed_buf, x_sem, in_sem, sem,
):
    micro = lax.axis_index(MICRO)
    group = group_index()
    block = pl.ds(pl.multiple_of(group * BLK, BLK), BLK)
    loads = [
        pltpu.make_async_copy(middle_ref.at[micro * 4 + group], middle_buf, in_sem.at[0]),
        pltpu.make_async_copy(og_ref.at[micro, block], og_buf, in_sem.at[1]),
        pltpu.make_async_copy(mixed_ref.at[pl.ds(micro * 4, 4), block], mixed_buf, in_sem.at[2]),
        pltpu.make_async_copy(tok_ref.at[micro, block], x_ref, x_sem),
    ]
    for load in loads:
        load.start()
    total = sums_ref[0].astype(F32)
    for index in range(1, 8):
        total = total + sums_ref[index].astype(F32)
    branch, grad = total[:BLK], total[BLK:]
    wait_all(loads)
    middle = middle_buf[...]
    unit, inverse = normalized(middle)
    grad_mid = og_buf[...].astype(F32) + norm_back(grad, unit, inverse, gain_ref[...].reshape(1, D))
    low = grad_mid.astype(BF)
    lane = lax.broadcasted_iota(jnp.int32, (BLK, 256), 1)
    sends = []
    for head_group in range(4):
        mixed = mixed_buf[head_group].astype(F32)
        back = mm_nt(low, wo_ref[head_group]).astype(BF).astype(F32)
        product = mixed * back
        columns = []
        for head in range(3):
            inside = (lane >= (head + 1) * HD) & (lane < (head + 2) * HD)
            columns += three(jnp.sum(jnp.where(inside, product, 0.0), axis=-1, keepdims=True))
        stats = put_columns(256, BLK, 9, columns)
        buf[head_group] = jnp.where(lane < 9, mixed, jnp.where(lane < HD, stats, back)).astype(BF)
        sends += send_copies(
            buf.at[head_group], out_ref, [chip * 4 + head_group for chip in range(8)], sem
        )
    low_ref[...] = low
    grad_ref[...] = grad_mid
    result_ref[...] = (middle + branch).astype(BF)
    gain_grad = jnp.sum(grad * unit, axis=0, keepdims=True)
    shift_grad = jnp.sum(grad, axis=0, keepdims=True)
    vec_ref[...] = jnp.concatenate([gain_grad, shift_grad, jnp.zeros((6, D), F32)], axis=0)
    wait_all(sends)


def attend_back_kernel(
    scene_ref, kvs_ref, kvo_ref, gs_ref, go_ref, normed_ref, mixed_ref, low0_ref, low1_ref, low2_ref, low3_ref, w_ref,
    own_ref, one_ref, two_ref, three_ref, keep_ref, send_ref,
    kv_buf, gqkv_buf, grad_buf, part_buf, mixed_buf, w_buf, kv_sem, mixed_sem, w_sem,
):
    first, big = span(scene_ref)
    chip = chip_index()
    core = lax.axis_index(CORE)
    group = group_index()
    scale = HD**-0.5

    def run(count):
        rows = count * TOK
        loads = [
            pltpu.make_async_copy(ref.at[pl.ds(first, count)], kv_buf.at[slot, pl.ds(0, count)], kv_sem.at[slot])
            for slot, ref in enumerate((kvs_ref, kvo_ref))
        ]
        for load in loads:
            load.start()

        def cut(value):
            return [value[:, at:at + 128] for at in range(0, value.shape[1], 128)]

        grad = cut(jnp.concatenate(
            [ref[pl.ds(first, count)].reshape(rows, 256) for ref in (gs_ref, go_ref)], axis=0
        ))
        g_own = cut(gs_ref[chip])
        g_heads = [halves(g_own[0])[1], *halves(g_own[1])]
        own_stats = g_own[0].astype(F32)
        all_stats = grad[0].astype(F32).T
        wait_all(loads)
        every = cut(jnp.concatenate([kv_buf[slot, :count].reshape(rows, 640) for slot in range(2)], axis=0))
        kv, query = every[:3], every[3:]
        own = cut(kv_buf[0, chip - first])
        q_heads = [*halves(own[3]), own[4]]
        k_heads = [*halves(own[0]), halves(own[1])[0]]
        v_heads = [halves(own[1])[1], *halves(own[2])]

        def column(at):
            return own_stats[:, at:at + 1] + own_stats[:, at + 1:at + 2] + own_stats[:, at + 2:at + 3]

        def row(at):
            return all_stats[at:at + 1] + all_stats[at + 1:at + 2] + all_stats[at + 2:at + 3]

        dq, dk, dv = [], [], []
        for head, (kb, vb) in enumerate(((0, 1), (0, 2), (1, 2))):
            qb, gb = (0, 0, 1)[head], (0, 1, 1)[head]
            probs = jnp.exp(mm_nt(q_heads[head], kv[kb]) * scale - column(3 * head))
            gap = mm_nt(g_heads[head], kv[vb]) - column(9 + 3 * head)
            dq.append(mm((probs * gap).astype(BF), kv[kb]) * scale)
            probs = jnp.exp(mm_nt(k_heads[head], query[qb]) * scale - row(3 * head))
            gap = mm_nt(v_heads[head], grad[gb]) - row(9 + 3 * head)
            dv.append(mm(probs.astype(BF), grad[gb]))
            dk.append(mm((probs * gap).astype(BF), query[qb]) * scale)
        tail = dq[2]
        gqkv_buf[...] = jnp.concatenate(
            [join(dk[0], dk[1]), join(dk[2], dv[0]), join(dv[1], dv[2]), join(dq[0], dq[1]),
             join(tail, jnp.zeros_like(tail))],
            axis=1,
        ).astype(BF)

    index = lax.axis_index(MICRO) * 4 + group
    load_mixed = pltpu.make_async_copy(mixed_ref.at[index], mixed_buf, mixed_sem)
    load_mixed.start()
    loads = weight_copies(w_ref, w_buf, w_sem)

    @pl.when(big)
    def _():
        run(5)

    @pl.when(jnp.logical_not(big))
    def _():
        run(1)

    grad_buf[...] = mm_tn(normed_ref[...], gqkv_buf[...])
    load_mixed.wait()
    low = jnp.concatenate([ref[...] for ref in (low0_ref, low1_ref, low2_ref, low3_ref)], axis=0)
    mixed = jnp.concatenate(
        [mixed_buf[pl.ds(pl.multiple_of((group ^ k) * BLK, BLK), BLK)] for k in range(4)], axis=0
    )
    out = mm_tn(mixed, low)[HD:]
    for ref, owner in ((keep_ref, core), (send_ref, 1 - core)):
        for tile in range(8):
            rows = grad_buf[pl.ds(pl.multiple_of((2 * tile + owner) * 48, 16), 48)]
            at = (tile // 4) * 96
            pieces = [
                out[at + row * 48:at + (row + 1) * 48, (tile % 4) * 192:(tile % 4 + 1) * 192] for row in range(2)
            ]
            ref[2 * tile] = rows[:, :384].astype(BF)
            ref[2 * tile + 1] = jnp.concatenate(
                [rows[:, 384:576], jnp.where(owner == 1, pieces[1], pieces[0])], axis=1
            ).astype(BF)

    odd = (group % 2) == 1
    total = jnp.zeros((TOK, D), F32)
    for slot in range(3):
        loads[slot].wait()
        part = gqkv_buf[:, slot * 192:(slot + 1) * 192]
        zero = jnp.zeros_like(part)
        wide = jnp.where(
            odd, jnp.concatenate([zero, part], axis=1), jnp.concatenate([part, zero], axis=1)
        )
        total = total + mm_nt(wide, w_buf[slot])
    part_buf[...] = total
    own_ref[...] = part_buf[pl.ds(pl.multiple_of(group * BLK, BLK), BLK)]
    for k, ref in ((1, one_ref), (2, two_ref), (3, three_ref)):
        ref[...] = part_buf[pl.ds(pl.multiple_of((group ^ k) * BLK, BLK), BLK)].astype(BF)


def add_kernel(one_ref, two_ref, out_ref, buf, sem):
    buf[...] = (one_ref[...].astype(F32) + two_ref[...].astype(F32)).astype(BF)
    copy = pltpu.make_async_copy(buf, out_ref, sem)
    copy.start()
    copy.wait()


def sum_kernel(in_ref, vec_ref, out_ref, buf, sem):
    total = in_ref[0].astype(F32)
    for index in range(1, 16):
        total = total + in_ref[index].astype(F32)
    vectors = vec_ref[...][:4]
    block = jnp.concatenate([total, vectors[:, :384], vectors[:, 384:]], axis=0).astype(BF)
    for index in range(8):
        buf[index] = block
    wait_all(send_copies(buf, out_ref, range(8), sem))


def spread_kernel(turn, in_ref, *refs):
    qkv_buf, out_buf, sem, out_sem = refs[-4:]
    qkv_ref, out_ref, *vec_refs = refs[3:-4] if turn else refs[:-4]
    owner = lax.axis_index(CORE)
    owner = 1 - owner if turn else owner
    copies = []
    vectors = jnp.zeros((8, 384), F32)
    for tile in range(8):
        whole = [in_ref[tile, index].astype(F32) for index in range(8)]
        block = [value[:48] for value in whole]
        for value in whole:
            vectors = vectors + value[48:]
        for part, half, at in ((1, 0, 0), (2, 0, 192), (0, 4, 0)):
            qkv_buf[tile, :, part * D:(part + 1) * D] = jnp.concatenate(
                [block[half + group][:, at:at + 192] for group in range(4)], axis=1
            )
        start = pl.multiple_of((2 * tile + owner) * 48, 16)
        copy = pltpu.make_async_copy(qkv_buf.at[tile], qkv_ref.at[pl.ds(start, 48)], sem.at[tile])
        copy.start()
        copies.append(copy)
        for group in range(4):
            out_buf[group, tile // 4, :, (tile % 4) * 192:(tile % 4 + 1) * 192] = block[4 + group][:, 192:]
    for group in range(4):
        for pair in range(2):
            start = pl.multiple_of(group * 192 + (pair * 2 + owner) * 48, 16)
            copy = pltpu.make_async_copy(
                out_buf.at[group, pair], out_ref.at[pl.ds(start, 48)], out_sem.at[group, pair]
            )
            copy.start()
            copies.append(copy)
    if turn:
        vectors = vectors + refs[0][...]
        for k, ref in enumerate(vec_refs):
            ref[...] = jnp.concatenate([vectors[k:k + 1], vectors[4 + k:5 + k]], axis=1).reshape(D)
    else:
        vec_refs[0][...] = vectors
    wait_all(copies)


def stack_kernel(*refs):
    y = lax.axis_index("y")
    for k, ref in enumerate(refs[:4]):
        refs[4][y ^ k] = ref[...]


def spread_ff_kernel(*refs):
    up_ref, down_ref = refs[4:]
    xl, core = lax.axis_index("xl"), lax.axis_index(CORE)
    for index, ref in enumerate(refs[:4]):
        chip_xl = xl ^ (index % 2)
        owner = core ^ (index // 2)
        for y in range(4):
            chip = y * 2 + chip_xl
            block = ref[y].astype(F32)
            up_ref[pl.ds(pl.multiple_of((chip * 2 + owner) * 48, 16), 48)] = block[:, :384]
            down_ref[
                pl.ds(pl.multiple_of(chip * 48, 16), 48), pl.ds(pl.multiple_of(owner * 384, 128), 384)
            ] = block[:, 384:]


def input_kernel(
    own_ref, one_ref, two_ref, three_ref, x_ref, gain_ref, grad_ref, result_ref, vec_ref, out_ref, sums_ref
):
    total = own_ref[...]
    for ref in (one_ref, two_ref, three_ref):
        total = total + ref[...].astype(F32)
    unit, inverse = normalized(x_ref[...].astype(F32))
    grad = grad_ref[...] + norm_back(total, unit, inverse, gain_ref[...].reshape(1, D))
    gain1 = jnp.sum(total * unit, axis=0, keepdims=True)
    shift1 = jnp.sum(total, axis=0, keepdims=True)
    sums_ref[...] = jnp.concatenate([gain1, shift1, vec_ref[...][:2], jnp.zeros((4, D), F32)], axis=0)
    out_ref[:BLK] = grad.astype(BF)
    out_ref[BLK:] = result_ref[...]


def unpack_kernel(*refs):
    parts, (grad_ref, result_ref) = refs[:8], refs[8:]
    micro = lax.axis_index(MICRO)
    group = group_index()
    for k, ref in enumerate(parts):
        rows = pl.ds(pl.multiple_of((group ^ (k % 4)) * BLK, BLK), BLK)
        where = micro ^ (k // 4)
        grad_ref[where, rows] = ref[:BLK].astype(F32)
        result_ref[where, rows] = ref[BLK:]


def exchange(value, axes):
    return lax.all_to_all(value, axes, 0, 0, tiled=True)


def swap(value):
    return lax.ppermute(value, CORE, [(0, 1), (1, 0)])


def after(value, *others):
    return pl.pallas_call(
        lambda *refs: None,
        out_shape=jax.ShapeDtypeStruct(value.shape, value.dtype),
        in_specs=[pl.BlockSpec(memory_space=pl.ANY)] * (1 + len(others)),
        out_specs=pl.BlockSpec(memory_space=pl.ANY),
        input_output_aliases={0: 0},
        cost_estimate=pl.CostEstimate(flops=1, bytes_accessed=1, transcendentals=0),
        compiler_params=pltpu.CompilerParams(vmem_limit_bytes=2**20),
    )(value, *others)


def flip(value, axes, count, bits):
    return lax.ppermute(value, axes, [(index, index ^ bits) for index in range(count)])


def shards(
    tokens, scene_of_block, ln1_gain, ln1_shift, w_qkv, w_out, ln2_gain, ln2_shift, w_up, w_down, out_grad
):
    w_out_pad = jnp.pad(w_out.reshape(4, 192, D), ((0, 0), (HD, 0), (0, 0)))
    kv_send, normed = call(
        project_kernel,
        [((8, TOK, 640), BF, "H"), ((TOK, D), BF, "L")],
        [(tokens, "H"), (ln1_gain, "H"), (ln1_shift, "H"), (w_qkv, "H")],
        10**9,
        [
            pltpu.VMEM((TOK, D), BF), pltpu.VMEM((3, D, 384), BF), pltpu.VMEM((TOK, 640), BF),
            pltpu.VMEM((D,), F32), pltpu.VMEM((D,), F32), DMA, DMA((3,)), DMA((8,)), DMA, DMA,
        ],
    )
    kv_same = exchange(kv_send, CHIP)
    kv_other = swap(kv_same)
    (mixed_send,) = call(
        attend_kernel,
        [((8, TOK, 256), BF, "H")],
        [(scene_of_block, "S"), (kv_same, "V"), (kv_other, "V")],
        2 * 10**9,
        [pltpu.VMEM((TOK, 256), BF), DMA((8,))],
    )
    mixed = exchange(mixed_send, NARROW)
    ff_send, middle, normed2, act, grad_pre = call(
        forward_kernel,
        [
            ((8, 2 * BLK, D), BF, "H"), ((8, BLK, D), F32, "L"), ((2 * TOK, D), BF, "V"),
            ((2 * TOK, FFL), BF, "V"), ((2 * TOK, FFL), BF, "V"),
        ],
        [
            (mixed, "V"), (tokens, "V"), (out_grad, "V"), (w_out_pad, "V"), (ln2_gain, "L"), (ln2_shift, "L"),
            (w_up, "V"), (w_down, "V"),
        ],
        4 * 10**9,
        [pltpu.VMEM((8, BLK, D), BF), pltpu.VMEM((8, BLK, D), BF), DMA((2,))],
    )
    ff_sums = exchange(ff_send, NARROW)
    keep, send = call(
        ff_grads_kernel,
        [((8, 48, D), BF, "V")] * 2,
        [(normed2, "V"), (act, "V"), (grad_pre, "V"), (out_grad, "L")],
        2 * 10**9,
        [pltpu.VMEM((D, FFL), F32), pltpu.VMEM((FFL, D), F32)],
    )
    pieces = call(
        split_kernel, [((2, 48, D), BF, "L")] * 4, [(keep, "V"), (swap(send), "V")], 10**8
    )
    pieces = [pieces[0]] + [flip(pieces[k], "y", 4, k) for k in (1, 2, 3)]
    keep, send = call(
        halve_kernel,
        [((48, D), BF, "L")] * 2,
        [(pieces[0], "L")] + [(piece, "V") for piece in pieces[1:]],
        10**8,
    )
    ff_sums = after(ff_sums, pin(keep))
    grad_send, low, grad_mid, result_part, vec2, x_part = call(
        middle_kernel,
        [
            ((32, BLK, 256), BF, "H"), ((BLK, D), BF, "L"), ((BLK, D), F32, "L"), ((BLK, D), BF, "L"),
            ((8, D), F32, "L"), ((BLK, D), BF, "L"),
        ],
        [
            (ff_sums, "V"), (middle, "H"), (out_grad, "H"), (tokens, "H"), (mixed, "H"), (w_out_pad, "V"),
            (ln2_gain, "L"),
        ],
        10**9,
        [
            pltpu.VMEM((4, BLK, 256), BF), pltpu.VMEM((BLK, D), F32), pltpu.VMEM((BLK, D), BF),
            pltpu.VMEM((4, BLK, 256), BF), DMA, DMA((3,)), DMA((32,)),
        ],
    )
    (ff_part,) = call(
        pair_kernel, [((48, D), BF, "L")], [(keep, "L"), (flip(send, "xl", 2, 1), "V")], 10**7
    )
    ff_parts = [flip(ff_part, "y", 4, k) for k in (1, 2, 3)]
    grad_same = exchange(grad_send, (*CHIP, *GROUP)).reshape(8, TOK, 256)
    lows = [flip(low, GROUP, 4, k) for k in (1, 2, 3)]
    grad_same = after(grad_same, *lows, *ff_parts)
    grad_other = swap(grad_same)
    own, *sends, keep, send = call(
        attend_back_kernel,
        [((BLK, D), F32, "L")] + [((BLK, D), BF, "L")] * 3 + [((16, 48, 384), BF, "V")] * 2,
        [
            (scene_of_block, "S"), (kv_same, "H"), (kv_other, "H"), (grad_same, "V"), (grad_other, "V"),
            (normed, "L"), (mixed, "H"), (low, "L"), *[(value, "V") for value in lows], (w_qkv, "H"),
        ],
        8 * 10**9,
        [
            pltpu.VMEM((2, 5, TOK, 640), BF), pltpu.VMEM((TOK, 640), BF), pltpu.VMEM((D, 640), F32),
            pltpu.VMEM((TOK, D), F32), pltpu.VMEM((TOK, 256), BF), pltpu.VMEM((3, D, 384), BF),
            DMA((2,)), DMA, DMA((3,)),
        ],
        vmem=24,
    )
    (weight_send,) = call(
        add_kernel,
        [((16, 48, 384), BF, "H")],
        [(keep, "V"), (swap(send), "V")],
        10**8,
        [pltpu.VMEM((16, 48, 384), BF), DMA],
    )
    parts = [flip(value, GROUP, 4, k + 1) for k, value in enumerate(sends)]
    weight_parts = exchange(weight_send, (*CHIP, MICRO))
    (ff_near,) = call(
        stack_kernel,
        [((4, 48, D), BF, "L")],
        [(ff_part, "L"), *[(value, "V") for value in ff_parts]],
        10**7,
    )
    ff_far = flip(ff_near, "xl", 2, 1)
    packed, sums = call(
        input_kernel,
        [((2 * BLK, D), BF, "L"), ((8, D), F32, "L")],
        [
            (own, "L"), *[(value, "V") for value in parts], (x_part, "L"), (ln1_gain, "L"), (grad_mid, "L"),
            (result_part, "L"), (vec2, "L"),
        ],
        10**8,
    )
    weight_parts = after(weight_parts, ff_far, pin(sums))
    (weight_total,) = call(
        sum_kernel,
        [((8, 8, 56, 384), BF, "H")],
        [(weight_parts, "V"), (sums, "L")],
        10**8,
        [pltpu.VMEM((8, 56, 384), BF), DMA((8,))],
    )
    everyone = [packed] + [flip(packed, NARROW, 8, k) for k in range(1, 8)]
    input_grad, result = call(
        unpack_kernel,
        [((2, TOK, D), F32, "L"), ((2, TOK, D), BF, "L")],
        [(packed, "L"), *[(value, "V") for value in everyone[1:]]],
        10**8,
    )
    up_grad, down_grad = call(
        spread_ff_kernel,
        [((D, FFL), F32, "L"), ((FFL, D), F32, "L")],
        [(ff_near, "L"), (ff_far, "V"), (swap(ff_near), "V"), (swap(ff_far), "V")],
        10**7,
    )
    weight_same = exchange(weight_total.reshape(64, 56, 384), (*CHIP, *NARROW)).reshape(8, 8, 56, 384)
    weight_same = after(weight_same, *map(pin, (input_grad, result, up_grad, down_grad)))
    weight_other = swap(weight_same)
    scratch = [
        pltpu.VMEM((8, 48, 3 * D), F32), pltpu.VMEM((4, 2, 48, D), F32), DMA((8,)), DMA((4, 2)),
    ]
    grads = [((D, 3 * D), F32, "H"), ((D, D), F32, "H")]
    half = call(
        functools.partial(spread_kernel, False),
        grads + [((8, 384), F32, "V")],
        [(weight_same, "V")],
        10**8,
        scratch,
    )
    qkv_grad, out_proj_grad, *vectors = call(
        functools.partial(spread_kernel, True),
        grads + [((D,), F32, "L")] * 4,
        [(weight_other, "V"), (half[2], "V"), (half[0], "H"), (half[1], "H")],
        10**8,
        scratch,
        aliases={2: 0, 3: 1},
    )
    return (
        result, input_grad, qkv_grad, out_proj_grad, *vectors, up_grad, down_grad
    )


def solution(mesh):
    names = ("y", "xl", "c", "zh", "zl", "xh")
    fine = Mesh(mesh.devices.reshape(4, 2, 2, 2, 2, 2), names)
    tokens = P(None, WIDE, None)
    placed = (
        tokens, P(), P(), P(), P(), P(), P(), P(), P(None, NARROW), P(NARROW, None), tokens
    )
    return jax.shard_map(
        shards,
        mesh=fine,
        in_specs=placed,
        out_specs=(
            tokens, tokens, P(), P(), P(), P(), P(), P(), P(None, NARROW), P(NARROW, None)
        ),
        check_vma=False,
    )
```

```python
import functools

import jax
import jax.numpy as jnp
from jax import lax
from jax.experimental import pallas as pl
from jax.experimental.pallas import tpu as pltpu
from jax.sharding import Mesh
from jax.sharding import PartitionSpec as P

D = 768
HD = 64
FFL = 384
TOK = 128
BLK = 32
EPS = 1e-05
BF = jnp.bfloat16
F32 = jnp.float32

CHIP = ("y", "xl")
CORE = "c"
MICRO = "zh"
GROUP = ("zl", "xh")
NARROW = (MICRO, *GROUP)
WIDE = (*CHIP, CORE)


def chip_index():
    return lax.axis_index("y") * 2 + lax.axis_index("xl")


def group_index():
    return lax.axis_index("zl") * 2 + lax.axis_index("xh")


def mm(left, right):
    return lax.dot_general(left, right, (((1,), (0,)), ((), ())), preferred_element_type=F32)


def mm_nt(left, right):
    return lax.dot_general(left, right, (((1,), (1,)), ((), ())), preferred_element_type=F32)


def mm_tn(left, right):
    return lax.dot_general(left, right, (((0,), (0,)), ((), ())), preferred_element_type=F32)


def normalized(values):
    center = values - jnp.mean(values, axis=-1, keepdims=True)
    spread = jnp.mean(center * center, axis=-1, keepdims=True)
    inverse = lax.rsqrt(spread + EPS)
    return center * inverse, inverse


def norm_back(grad, unit, inverse, gain):
    scaled = grad * gain
    first = jnp.mean(scaled, axis=-1, keepdims=True)
    second = jnp.mean(scaled * unit, axis=-1, keepdims=True)
    return inverse * (scaled - first - unit * second)


def halves(block):
    lane = lax.broadcasted_iota(jnp.int32, block.shape, 1)
    zero = jnp.zeros_like(block)
    return jnp.where(lane < HD, block, zero), jnp.where(lane < HD, zero, block)


def join(low, high):
    lane = lax.broadcasted_iota(jnp.int32, low.shape, 1)
    return jnp.where(lane < HD, low, high)


def span(scene_ref):
    micro = lax.axis_index(MICRO)
    own = scene_ref[micro, chip_index() * 4]
    first = jnp.int32(0)
    count = jnp.int32(0)
    for index in range(8):
        other = scene_ref[micro, index * 4]
        first += (other < own).astype(jnp.int32)
        count += (other == own).astype(jnp.int32)
    return first, count > 1


def three(value):
    a = value.astype(BF).astype(F32)
    b = (value - a).astype(BF).astype(F32)
    c = value - a - b
    return a, b, c


def put_columns(width, rows, start, columns):
    lane = lax.broadcasted_iota(jnp.int32, (rows, width), 1)
    out = jnp.zeros((rows, width), F32)
    for offset, column in enumerate(columns):
        out = jnp.where(lane == start + offset, column, out)
    return out


def pin(value):
    return pltpu.with_memory_space_constraint(value, pltpu.HBM)


def call(kernel, outs, ins, cost, scratch=(), vmem=16, aliases=None):
    places = {"V": pltpu.VMEM, "H": pltpu.HBM, "S": pltpu.SMEM, "L": pltpu.VMEM}
    return pl.pallas_call(
        kernel,
        out_shape=[
            (pltpu.HBM if place in "HL" else jax.ShapeDtypeStruct)(shape, dtype) for shape, dtype, place in outs
        ],
        in_specs=[pl.BlockSpec(memory_space=places[place]) for _, place in ins],
        out_specs=[pl.BlockSpec(memory_space=places[place]) for _, _, place in outs],
        scratch_shapes=list(scratch),
        input_output_aliases=aliases or {},
        cost_estimate=pl.CostEstimate(flops=1000, bytes_accessed=1000, transcendentals=0),
        compiler_params=pltpu.CompilerParams(vmem_limit_bytes=vmem * 2**20),
    )(*[pin(value) if place in "HL" else value for value, place in ins])


DMA = pltpu.SemaphoreType.DMA


def send_copies(source, target, indices, sem):
    copies = [pltpu.make_async_copy(source, target.at[index], sem.at[index]) for index in indices]
    for copy in copies:
        copy.start()
    return copies


def wait_all(copies):
    for copy in copies:
        copy.wait()


def weight_copies(w_ref, w_buf, w_sem):
    group = group_index()
    copies = []
    for slot, part in enumerate((1, 2, 0)):
        column = pl.multiple_of(part * D + (group // 2) * 384, 128)
        copy = pltpu.make_async_copy(w_ref.at[:, pl.ds(column, 384)], w_buf.at[slot], w_sem.at[slot])
        copy.start()
        copies.append(copy)
    return copies


def project_kernel(
    tok_ref, gain_ref, shift_ref, w_ref, kv_ref, q_ref, normed_ref,
    x_buf, w_buf, kv_buf, gain_buf, shift_buf, x_sem, w_sem, kv_sem, gain_sem, shift_sem,
):
    copy_x = pltpu.make_async_copy(tok_ref.at[lax.axis_index(MICRO)], x_buf, x_sem)
    copy_x.start()
    copy_gain = pltpu.make_async_copy(gain_ref, gain_buf, gain_sem)
    copy_gain.start()
    copy_shift = pltpu.make_async_copy(shift_ref, shift_buf, shift_sem)
    copy_shift.start()
    copies = weight_copies(w_ref, w_buf, w_sem)
    wait_all([copy_x, copy_gain, copy_shift])
    unit, _ = normalized(x_buf[...].astype(F32))
    normed = (unit * gain_buf[...].reshape(1, D) + shift_buf[...].reshape(1, D)).astype(BF)
    odd = (group_index() % 2) == 1

    def part(slot):
        copies[slot].wait()
        full = mm(normed, w_buf[slot])
        return jnp.where(odd, full[:, 192:], full[:, :192]).astype(BF)

    kv_buf[...] = jnp.concatenate([part(0), part(1)], axis=1)
    sends = send_copies(kv_buf, kv_ref, range(8), kv_sem)
    normed_ref[...] = normed
    q_ref[...] = jnp.concatenate([part(2), jnp.zeros((TOK, HD), BF)], axis=1)
    wait_all(sends)


def attend_kernel(scene_ref, q_ref, same_ref, other_ref, out_ref, buf, sem):
    first, big = span(scene_ref)

    def run(count):
        rows = count * TOK
        keys = jnp.concatenate(
            [ref[pl.ds(first, count)].reshape(rows, 384) for ref in (same_ref, other_ref)], axis=0
        )
        query = q_ref[...]
        q0, q1 = halves(query[:, :128])
        blocks = [keys[:, :128], keys[:, 128:256], keys[:, 256:]]
        mixed = []
        columns = []
        for qh, kb, vb in ((q0, 0, 1), (q1, 0, 2), (query[:, 128:], 1, 2)):
            scores = mm_nt(qh, blocks[kb]) * (HD**-0.5)
            top = jnp.max(scores, axis=-1, keepdims=True)
            weights = jnp.exp(scores - top)
            total = jnp.sum(weights, axis=-1, keepdims=True)
            probs = (weights * (1.0 / total)).astype(BF)
            mixed.append(mm(probs, blocks[vb]))
            columns += three(top + jnp.log(total))
        stats = put_columns(128, TOK, 0, columns)
        buf[...] = jnp.concatenate([join(stats, mixed[0]), join(mixed[1], mixed[2])], axis=1).astype(BF)

    @pl.when(big)
    def _():
        run(5)

    @pl.when(jnp.logical_not(big))
    def _():
        run(1)

    wait_all(send_copies(buf, out_ref, range(8), sem))


def forward_kernel(
    mixed_ref, tok_ref, og_ref, wo_ref, gain_ref, shift_ref, up_ref, down_ref,
    out_ref, middle_ref, normed_ref, act_ref, gpre_ref, grad_buf, branch_buf, sem,
):
    total = tok_ref[...].reshape(2 * TOK, D).astype(F32)
    for group in range(4):
        rows = jnp.concatenate([mixed_ref[group], mixed_ref[4 + group]], axis=0)
        total = total + mm(rows, wo_ref[group])
    middle_ref[...] = total.reshape(8, BLK, D)
    unit, _ = normalized(total)
    normed = (unit * gain_ref[...].reshape(1, D) + shift_ref[...].reshape(1, D)).astype(BF)
    normed_ref[...] = normed
    pre = mm(normed, up_ref[...])
    cdf = 0.5 * (1.0 + lax.erf(pre * (0.5**0.5)))
    slope = cdf + pre * jnp.exp(-0.5 * pre * pre) * 0.3989422804014327
    grad_out = og_ref[...].reshape(2 * TOK, D)
    gpre = (mm_nt(grad_out, down_ref[...]) * slope).astype(BF)
    gpre_ref[...] = gpre
    grad_buf[...] = mm_nt(gpre, up_ref[...]).astype(BF).reshape(8, BLK, D)
    first = pltpu.make_async_copy(grad_buf, out_ref.at[:, pl.ds(BLK, BLK)], sem.at[0])
    first.start()
    act = (pre * cdf).astype(BF)
    act_ref[...] = act
    branch_buf[...] = mm(act, down_ref[...]).astype(BF).reshape(8, BLK, D)
    second = pltpu.make_async_copy(branch_buf, out_ref.at[:, pl.ds(0, BLK)], sem.at[1])
    second.start()
    first.wait()
    second.wait()


def ff_grads_kernel(normed_ref, act_ref, gpre_ref, og_ref, out_ref):
    up = mm_tn(normed_ref[...], gpre_ref[...]).astype(BF)
    grad_out = og_ref[...].reshape(2 * TOK, D)
    down = mm_tn(act_ref[...], grad_out).astype(BF)
    out_ref[:, :384] = up
    for tile in range(16):
        half = (tile % 2) * 384
        out_ref[tile * 48:(tile + 1) * 48, 384:] = down[
            (tile // 2) * 48:(tile // 2 + 1) * 48, half:half + 384
        ]


def middle_kernel(
    sums_ref, middle_ref, og_ref, tok_ref, mixed_ref, wo_ref, gain_ref,
    out_ref, low_ref, grad_ref, result_ref, vec_ref, x_ref, buf, middle_buf, og_buf, mixed_buf, x_sem, in_sem, sem,
):
    micro = lax.axis_index(MICRO)
    group = group_index()
    block = pl.ds(pl.multiple_of(group * BLK, BLK), BLK)
    loads = [
        pltpu.make_async_copy(middle_ref.at[micro * 4 + group], middle_buf, in_sem.at[0]),
        pltpu.make_async_copy(og_ref.at[micro, block], og_buf, in_sem.at[1]),
        pltpu.make_async_copy(mixed_ref.at[pl.ds(micro * 4, 4), block], mixed_buf, in_sem.at[2]),
        pltpu.make_async_copy(tok_ref.at[micro, block], x_ref, x_sem),
    ]
    for load in loads:
        load.start()
    total = sums_ref[0].astype(F32)
    for index in range(1, 8):
        total = total + sums_ref[index].astype(F32)
    branch, grad = total[:BLK], total[BLK:]
    wait_all(loads)
    middle = middle_buf[...]
    unit, inverse = normalized(middle)
    grad_mid = og_buf[...].astype(F32) + norm_back(grad, unit, inverse, gain_ref[...].reshape(1, D))
    low = grad_mid.astype(BF)
    lane = lax.broadcasted_iota(jnp.int32, (BLK, 256), 1)
    sends = []
    for head_group in range(4):
        mixed = mixed_buf[head_group].astype(F32)
        back = mm_nt(low, wo_ref[head_group]).astype(BF).astype(F32)
        product = mixed * back
        columns = []
        for head in range(3):
            inside = (lane >= (head + 1) * HD) & (lane < (head + 2) * HD)
            columns += three(jnp.sum(jnp.where(inside, product, 0.0), axis=-1, keepdims=True))
        stats = put_columns(256, BLK, 9, columns)
        buf[head_group] = jnp.where(lane < 9, mixed, jnp.where(lane < HD, stats, back)).astype(BF)
        sends += send_copies(
            buf.at[head_group], out_ref, [chip * 4 + head_group for chip in range(8)], sem
        )
    low_ref[...] = low
    grad_ref[...] = grad_mid
    result_ref[...] = (middle + branch).astype(BF)
    gain_grad = jnp.sum(grad * unit, axis=0, keepdims=True)
    shift_grad = jnp.sum(grad, axis=0, keepdims=True)
    vec_ref[...] = jnp.concatenate([gain_grad, shift_grad, jnp.zeros((6, D), F32)], axis=0)
    wait_all(sends)


def attend_back_kernel(
    scene_ref, kvs_ref, kvo_ref, q_ref, gs_ref, go_ref, normed_ref, mixed_ref, low0_ref, low1_ref, low2_ref, low3_ref, w_ref,
    own_ref, one_ref, two_ref, three_ref, keep_ref, send_ref,
    kv_buf, q_buf, gqkv_buf, grad_buf, part_buf, mixed_buf, w_buf, kv_sem, q_sem, mixed_sem, w_sem,
):
    first, big = span(scene_ref)
    chip = chip_index()
    core = lax.axis_index(CORE)
    group = group_index()
    scale = HD**-0.5

    def run(count):
        rows = count * TOK
        loads = [
            pltpu.make_async_copy(ref.at[pl.ds(first, count)], kv_buf.at[slot, pl.ds(0, count)], kv_sem.at[slot])
            for slot, ref in enumerate((kvs_ref, kvo_ref))
        ] + [
            pltpu.make_async_copy(
                q_ref.at[pl.ds(first, count), which], q_buf.at[slot, pl.ds(0, count)], q_sem.at[slot]
            )
            for slot, which in enumerate((core, 1 - core))
        ]
        for load in loads:
            load.start()

        def cut(value):
            return [value[:, at:at + 128] for at in range(0, value.shape[1], 128)]

        grad = cut(jnp.concatenate(
            [ref[pl.ds(first, count)].reshape(rows, 256) for ref in (gs_ref, go_ref)], axis=0
        ))
        g_own = cut(gs_ref[chip])
        g_heads = [halves(g_own[0])[1], *halves(g_own[1])]
        own_stats = g_own[0].astype(F32)
        all_stats = grad[0].astype(F32).T
        wait_all(loads)
        kv = cut(jnp.concatenate([kv_buf[slot, :count].reshape(rows, 384) for slot in range(2)], axis=0))
        query = cut(jnp.concatenate([q_buf[slot, :count].reshape(rows, 256) for slot in range(2)], axis=0))
        own = cut(kv_buf[0, chip - first]) + cut(q_buf[0, chip - first])
        q_heads = [*halves(own[3]), own[4]]
        k_heads = [*halves(own[0]), halves(own[1])[0]]
        v_heads = [halves(own[1])[1], *halves(own[2])]

        def column(at):
            return own_stats[:, at:at + 1] + own_stats[:, at + 1:at + 2] + own_stats[:, at + 2:at + 3]

        def row(at):
            return all_stats[at:at + 1] + all_stats[at + 1:at + 2] + all_stats[at + 2:at + 3]

        dq, dk, dv = [], [], []
        for head, (kb, vb) in enumerate(((0, 1), (0, 2), (1, 2))):
            qb, gb = (0, 0, 1)[head], (0, 1, 1)[head]
            probs = jnp.exp(mm_nt(q_heads[head], kv[kb]) * scale - column(3 * head))
            gap = mm_nt(g_heads[head], kv[vb]) - column(9 + 3 * head)
            dq.append(mm((probs * gap).astype(BF), kv[kb]) * scale)
            probs = jnp.exp(mm_nt(k_heads[head], query[qb]) * scale - row(3 * head))
            gap = mm_nt(v_heads[head], grad[gb]) - row(9 + 3 * head)
            dv.append(mm(probs.astype(BF), grad[gb]))
            dk.append(mm((probs * gap).astype(BF), query[qb]) * scale)
        tail = dq[2]
        gqkv_buf[...] = jnp.concatenate(
            [join(dk[0], dk[1]), join(dk[2], dv[0]), join(dv[1], dv[2]), join(dq[0], dq[1]),
             join(tail, jnp.zeros_like(tail))],
            axis=1,
        ).astype(BF)

    index = lax.axis_index(MICRO) * 4 + group
    load_mixed = pltpu.make_async_copy(mixed_ref.at[index], mixed_buf, mixed_sem)
    load_mixed.start()
    loads = weight_copies(w_ref, w_buf, w_sem)

    @pl.when(big)
    def _():
        run(5)

    @pl.when(jnp.logical_not(big))
    def _():
        run(1)

    grad_buf[...] = mm_tn(normed_ref[...], gqkv_buf[...])
    load_mixed.wait()
    low = jnp.concatenate([ref[...] for ref in (low0_ref, low1_ref, low2_ref, low3_ref)], axis=0)
    mixed = jnp.concatenate(
        [mixed_buf[pl.ds(pl.multiple_of((group ^ k) * BLK, BLK), BLK)] for k in range(4)], axis=0
    )
    out = mm_tn(mixed, low)[HD:]
    for ref, owner in ((keep_ref, core), (send_ref, 1 - core)):
        for tile in range(8):
            rows = grad_buf[pl.ds(pl.multiple_of((2 * tile + owner) * 48, 16), 48)]
            at = (tile // 4) * 96
            pieces = [
                out[at + row * 48:at + (row + 1) * 48, (tile % 4) * 192:(tile % 4 + 1) * 192] for row in range(2)
            ]
            ref[2 * tile] = rows[:, :384].astype(BF)
            ref[2 * tile + 1] = jnp.concatenate(
                [rows[:, 384:576], jnp.where(owner == 1, pieces[1], pieces[0])], axis=1
            ).astype(BF)

    odd = (group % 2) == 1
    total = jnp.zeros((TOK, D), F32)
    for slot in range(3):
        loads[slot].wait()
        part = gqkv_buf[:, slot * 192:(slot + 1) * 192]
        zero = jnp.zeros_like(part)
        wide = jnp.where(
            odd, jnp.concatenate([zero, part], axis=1), jnp.concatenate([part, zero], axis=1)
        )
        total = total + mm_nt(wide, w_buf[slot])
    part_buf[...] = total
    own_ref[...] = part_buf[pl.ds(pl.multiple_of(group * BLK, BLK), BLK)]
    for k, ref in ((1, one_ref), (2, two_ref), (3, three_ref)):
        ref[...] = part_buf[pl.ds(pl.multiple_of((group ^ k) * BLK, BLK), BLK)].astype(BF)


def add_kernel(one_ref, two_ref, out_ref, buf, sem):
    buf[...] = (one_ref[...].astype(F32) + two_ref[...].astype(F32)).astype(BF)
    copy = pltpu.make_async_copy(buf, out_ref, sem)
    copy.start()
    copy.wait()


def sum_kernel(in_ref, vec_ref, out_ref, buf, sem):
    total = in_ref[0].astype(F32)
    for index in range(1, 16):
        total = total + in_ref[index].astype(F32)
    vectors = vec_ref[...][:4]
    block = jnp.concatenate([total, vectors[:, :384], vectors[:, 384:]], axis=0).astype(BF)
    for index in range(8):
        buf[index] = block
    wait_all(send_copies(buf, out_ref, range(8), sem))


def spread_kernel(turn, in_ref, *refs):
    qkv_buf, out_buf, sem, out_sem = refs[-4:]
    qkv_ref, out_ref, *vec_refs = refs[3:-4] if turn else refs[:-4]
    owner = lax.axis_index(CORE)
    owner = 1 - owner if turn else owner
    copies = []
    vectors = jnp.zeros((8, 384), F32)
    for tile in range(8):
        whole = [in_ref[tile, index].astype(F32) for index in range(8)]
        block = [value[:48] for value in whole]
        for value in whole:
            vectors = vectors + value[48:]
        for part, half, at in ((1, 0, 0), (2, 0, 192), (0, 4, 0)):
            qkv_buf[tile, :, part * D:(part + 1) * D] = jnp.concatenate(
                [block[half + group][:, at:at + 192] for group in range(4)], axis=1
            )
        start = pl.multiple_of((2 * tile + owner) * 48, 16)
        copy = pltpu.make_async_copy(qkv_buf.at[tile], qkv_ref.at[pl.ds(start, 48)], sem.at[tile])
        copy.start()
        copies.append(copy)
        for group in range(4):
            out_buf[group, tile // 4, :, (tile % 4) * 192:(tile % 4 + 1) * 192] = block[4 + group][:, 192:]
    for group in range(4):
        for pair in range(2):
            start = pl.multiple_of(group * 192 + (pair * 2 + owner) * 48, 16)
            copy = pltpu.make_async_copy(
                out_buf.at[group, pair], out_ref.at[pl.ds(start, 48)], out_sem.at[group, pair]
            )
            copy.start()
            copies.append(copy)
    if turn:
        vectors = vectors + refs[0][...]
        for k, ref in enumerate(vec_refs):
            ref[...] = jnp.concatenate([vectors[k:k + 1], vectors[4 + k:5 + k]], axis=1).reshape(D)
    else:
        vec_refs[0][...] = vectors
    wait_all(copies)


def spread_ff_kernel(in_ref, up_ref, down_ref):
    up_ref[...] = in_ref[:, :384].astype(F32)
    for tile in range(16):
        half = (tile % 2) * 384
        down_ref[(tile // 2) * 48:(tile // 2 + 1) * 48, half:half + 384] = in_ref[
            tile * 48:(tile + 1) * 48, 384:
        ].astype(F32)


def input_kernel(
    own_ref, one_ref, two_ref, three_ref, x_ref, gain_ref, grad_ref, result_ref, vec_ref, out_ref, sums_ref
):
    total = own_ref[...]
    for ref in (one_ref, two_ref, three_ref):
        total = total + ref[...].astype(F32)
    unit, inverse = normalized(x_ref[...].astype(F32))
    grad = grad_ref[...] + norm_back(total, unit, inverse, gain_ref[...].reshape(1, D))
    gain1 = jnp.sum(total * unit, axis=0, keepdims=True)
    shift1 = jnp.sum(total, axis=0, keepdims=True)
    sums_ref[...] = jnp.concatenate([gain1, shift1, vec_ref[...][:2], jnp.zeros((4, D), F32)], axis=0)
    out_ref[:BLK] = grad.astype(BF)
    out_ref[BLK:] = result_ref[...]


def unpack_kernel(*refs):
    parts, (grad_ref, result_ref) = refs[:8], refs[8:]
    micro = lax.axis_index(MICRO)
    group = group_index()
    for k, ref in enumerate(parts):
        rows = pl.ds(pl.multiple_of((group ^ (k % 4)) * BLK, BLK), BLK)
        where = micro ^ (k // 4)
        grad_ref[where, rows] = ref[:BLK].astype(F32)
        result_ref[where, rows] = ref[BLK:]


def exchange(value, axes):
    return lax.all_to_all(value, axes, 0, 0, tiled=True)


def swap(value):
    return lax.ppermute(value, CORE, [(0, 1), (1, 0)])


def after(value, *others):
    return pl.pallas_call(
        lambda *refs: None,
        out_shape=jax.ShapeDtypeStruct(value.shape, value.dtype),
        in_specs=[pl.BlockSpec(memory_space=pl.ANY)] * (1 + len(others)),
        out_specs=pl.BlockSpec(memory_space=pl.ANY),
        input_output_aliases={0: 0},
        cost_estimate=pl.CostEstimate(flops=1, bytes_accessed=1, transcendentals=0),
        compiler_params=pltpu.CompilerParams(vmem_limit_bytes=2**20),
    )(value, *others)


def flip(value, axes, count, bits):
    return lax.ppermute(value, axes, [(index, index ^ bits) for index in range(count)])


def shards(
    tokens, scene_of_block, ln1_gain, ln1_shift, w_qkv, w_out, ln2_gain, ln2_shift, w_up, w_down, out_grad
):
    w_out_pad = jnp.pad(w_out.reshape(4, 192, D), ((0, 0), (HD, 0), (0, 0)))
    kv_send, query, normed = call(
        project_kernel,
        [((8, TOK, 384), BF, "H"), ((TOK, 256), BF, "L"), ((TOK, D), BF, "L")],
        [(tokens, "H"), (ln1_gain, "H"), (ln1_shift, "H"), (w_qkv, "H")],
        10**9,
        [
            pltpu.VMEM((TOK, D), BF), pltpu.VMEM((3, D, 384), BF), pltpu.VMEM((TOK, 384), BF),
            pltpu.VMEM((D,), F32), pltpu.VMEM((D,), F32), DMA, DMA((3,)), DMA((8,)), DMA, DMA,
        ],
    )
    kv_same = exchange(kv_send, CHIP)
    kv_other = swap(kv_same)
    (mixed_send,) = call(
        attend_kernel,
        [((8, TOK, 256), BF, "H")],
        [(scene_of_block, "S"), (query, "L"), (kv_same, "V"), (kv_other, "V")],
        2 * 10**9,
        [pltpu.VMEM((TOK, 256), BF), DMA((8,))],
    )
    mixed = exchange(mixed_send, NARROW)
    queries = lax.all_gather(after(pin(query), kv_same), WIDE, axis=0, tiled=True).reshape(8, 2, TOK, 256)
    ff_send, middle, normed2, act, grad_pre = call(
        forward_kernel,
        [
            ((8, 2 * BLK, D), BF, "H"), ((8, BLK, D), F32, "L"), ((2 * TOK, D), BF, "L"),
            ((2 * TOK, FFL), BF, "L"), ((2 * TOK, FFL), BF, "L"),
        ],
        [
            (mixed, "V"), (tokens, "V"), (out_grad, "V"), (w_out_pad, "V"), (ln2_gain, "L"), (ln2_shift, "L"),
            (w_up, "V"), (w_down, "V"),
        ],
        4 * 10**9,
        [pltpu.VMEM((8, BLK, D), BF), pltpu.VMEM((8, BLK, D), BF), DMA((2,))],
    )
    ff_sums = exchange(ff_send, NARROW)
    (ff_grads,) = call(
        ff_grads_kernel,
        [((D, D), BF, "L")],
        [(normed2, "L"), (act, "L"), (grad_pre, "L"), (out_grad, "L")],
        2 * 10**9,
    )
    ff_part = lax.psum_scatter(ff_grads, WIDE, scatter_dimension=0, tiled=True)
    ff_all = lax.all_gather(ff_part, WIDE, axis=0, tiled=True)
    ff_sums = after(ff_sums, pin(ff_grads))
    grad_send, low, grad_mid, result_part, vec2, x_part = call(
        middle_kernel,
        [
            ((32, BLK, 256), BF, "H"), ((BLK, D), BF, "L"), ((BLK, D), F32, "L"), ((BLK, D), BF, "L"),
            ((8, D), F32, "L"), ((BLK, D), BF, "L"),
        ],
        [
            (ff_sums, "V"), (middle, "H"), (out_grad, "H"), (tokens, "H"), (mixed, "H"), (w_out_pad, "V"),
            (ln2_gain, "L"),
        ],
        10**9,
        [
            pltpu.VMEM((4, BLK, 256), BF), pltpu.VMEM((BLK, D), F32), pltpu.VMEM((BLK, D), BF),
            pltpu.VMEM((4, BLK, 256), BF), DMA, DMA((3,)), DMA((32,)),
        ],
    )
    grad_same = exchange(grad_send, (*CHIP, *GROUP)).reshape(8, TOK, 256)
    lows = [flip(low, GROUP, 4, k) for k in (1, 2, 3)]
    grad_same = after(grad_same, *lows)
    grad_other = swap(grad_same)
    own, *sends, keep, send = call(
        attend_back_kernel,
        [((BLK, D), F32, "L")] + [((BLK, D), BF, "L")] * 3 + [((16, 48, 384), BF, "V")] * 2,
        [
            (scene_of_block, "S"), (kv_same, "H"), (kv_other, "H"), (queries, "H"), (grad_same, "V"), (grad_other, "V"),
            (normed, "L"), (mixed, "H"), (low, "L"), *[(value, "V") for value in lows],
            (w_qkv, "H"),
        ],
        8 * 10**9,
        [
            pltpu.VMEM((2, 5, TOK, 384), BF), pltpu.VMEM((2, 5, TOK, 256), BF), pltpu.VMEM((TOK, 640), BF),
            pltpu.VMEM((D, 640), F32),
            pltpu.VMEM((TOK, D), F32), pltpu.VMEM((TOK, 256), BF), pltpu.VMEM((3, D, 384), BF),
            DMA((2,)), DMA((2,)), DMA, DMA((3,)),
        ],
        vmem=24,
    )
    (weight_send,) = call(
        add_kernel,
        [((16, 48, 384), BF, "H")],
        [(keep, "V"), (swap(send), "V")],
        10**8,
        [pltpu.VMEM((16, 48, 384), BF), DMA],
    )
    parts = [flip(value, GROUP, 4, k + 1) for k, value in enumerate(sends)]
    weight_parts = exchange(weight_send, (*CHIP, MICRO))
    packed, sums = call(
        input_kernel,
        [((2 * BLK, D), BF, "L"), ((8, D), F32, "L")],
        [
            (own, "L"), *[(value, "V") for value in parts], (x_part, "L"), (ln1_gain, "L"), (grad_mid, "L"),
            (result_part, "L"), (vec2, "L"),
        ],
        10**8,
    )
    weight_parts = after(weight_parts, pin(sums), pin(ff_part))
    (weight_total,) = call(
        sum_kernel,
        [((8, 8, 56, 384), BF, "H")],
        [(weight_parts, "V"), (sums, "L")],
        10**8,
        [pltpu.VMEM((8, 56, 384), BF), DMA((8,))],
    )
    everyone = [packed] + [flip(packed, NARROW, 8, k) for k in range(1, 8)]
    input_grad, result = call(
        unpack_kernel,
        [((2, TOK, D), F32, "L"), ((2, TOK, D), BF, "L")],
        [(packed, "L"), *[(value, "V") for value in everyone[1:]]],
        10**8,
    )
    up_grad, down_grad = call(
        spread_ff_kernel, [((D, FFL), F32, "L"), ((FFL, D), F32, "L")], [(ff_all, "L")], 10**7
    )
    weight_same = exchange(weight_total.reshape(64, 56, 384), (*CHIP, *NARROW)).reshape(8, 8, 56, 384)
    weight_same = after(weight_same, *map(pin, (input_grad, result, up_grad, down_grad)))
    weight_other = swap(weight_same)
    scratch = [
        pltpu.VMEM((8, 48, 3 * D), F32), pltpu.VMEM((4, 2, 48, D), F32), DMA((8,)), DMA((4, 2)),
    ]
    grads = [((D, 3 * D), F32, "H"), ((D, D), F32, "H")]
    half = call(
        functools.partial(spread_kernel, False),
        grads + [((8, 384), F32, "V")],
        [(weight_same, "V")],
        10**8,
        scratch,
    )
    qkv_grad, out_proj_grad, *vectors = call(
        functools.partial(spread_kernel, True),
        grads + [((D,), F32, "L")] * 4,
        [(weight_other, "V"), (half[2], "V"), (half[0], "H"), (half[1], "H")],
        10**8,
        scratch,
        aliases={2: 0, 3: 1},
    )
    return (
        result, input_grad, qkv_grad, out_proj_grad, *vectors, up_grad, down_grad
    )


def solution(mesh):
    names = ("y", "xl", "c", "zh", "zl", "xh")
    fine = Mesh(mesh.devices.reshape(4, 2, 2, 2, 2, 2), names)
    tokens = P(None, WIDE, None)
    placed = (
        tokens, P(), P(), P(), P(), P(), P(), P(), P(None, NARROW), P(NARROW, None), tokens
    )
    return jax.shard_map(
        shards,
        mesh=fine,
        in_specs=placed,
        out_specs=(
            tokens, tokens, P(), P(), P(), P(), P(), P(), P(None, NARROW), P(NARROW, None)
        ),
        check_vma=False,
    )
```

```python
import functools

import jax
import jax.numpy as jnp
from jax import lax
from jax.experimental import pallas as pl
from jax.experimental.pallas import tpu as pltpu
from jax.sharding import Mesh
from jax.sharding import PartitionSpec as P

D = 768
HD = 64
FFL = 384
TOK = 128
BLK = 32
EPS = 1e-05
BF = jnp.bfloat16
F32 = jnp.float32

CHIP = ("y", "xl")
CORE = "c"
MICRO = "zh"
GROUP = ("zl", "xh")
NARROW = (MICRO, *GROUP)
WIDE = (*CHIP, CORE)


def chip_index():
    return lax.axis_index("y") * 2 + lax.axis_index("xl")


def group_index():
    return lax.axis_index("zl") * 2 + lax.axis_index("xh")


def mm(left, right):
    return lax.dot_general(left, right, (((1,), (0,)), ((), ())), preferred_element_type=F32)


def mm_nt(left, right):
    return lax.dot_general(left, right, (((1,), (1,)), ((), ())), preferred_element_type=F32)


def mm_tn(left, right):
    return lax.dot_general(left, right, (((0,), (0,)), ((), ())), preferred_element_type=F32)


def normalized(values):
    center = values - jnp.mean(values, axis=-1, keepdims=True)
    spread = jnp.mean(center * center, axis=-1, keepdims=True)
    inverse = lax.rsqrt(spread + EPS)
    return center * inverse, inverse


def norm_back(grad, unit, inverse, gain):
    scaled = grad * gain
    first = jnp.mean(scaled, axis=-1, keepdims=True)
    second = jnp.mean(scaled * unit, axis=-1, keepdims=True)
    return inverse * (scaled - first - unit * second)


def halves(block):
    lane = lax.broadcasted_iota(jnp.int32, block.shape, 1)
    zero = jnp.zeros_like(block)
    return jnp.where(lane < HD, block, zero), jnp.where(lane < HD, zero, block)


def join(low, high):
    lane = lax.broadcasted_iota(jnp.int32, low.shape, 1)
    return jnp.where(lane < HD, low, high)


def span(scene_ref):
    micro = lax.axis_index(MICRO)
    own = scene_ref[micro, chip_index() * 4]
    first = jnp.int32(0)
    count = jnp.int32(0)
    for index in range(8):
        other = scene_ref[micro, index * 4]
        first += (other < own).astype(jnp.int32)
        count += (other == own).astype(jnp.int32)
    return first, count > 1


def three(value):
    a = value.astype(BF).astype(F32)
    b = (value - a).astype(BF).astype(F32)
    c = value - a - b
    return a, b, c


def put_columns(width, rows, start, columns):
    lane = lax.broadcasted_iota(jnp.int32, (rows, width), 1)
    out = jnp.zeros((rows, width), F32)
    for offset, column in enumerate(columns):
        out = jnp.where(lane == start + offset, column, out)
    return out


def pin(value):
    return pltpu.with_memory_space_constraint(value, pltpu.HBM)


def call(kernel, outs, ins, cost, scratch=(), vmem=16, aliases=None):
    places = {"V": pltpu.VMEM, "H": pltpu.HBM, "S": pltpu.SMEM, "L": pltpu.VMEM}
    return pl.pallas_call(
        kernel,
        out_shape=[
            (pltpu.HBM if place in "HL" else jax.ShapeDtypeStruct)(shape, dtype) for shape, dtype, place in outs
        ],
        in_specs=[pl.BlockSpec(memory_space=places[place]) for _, place in ins],
        out_specs=[pl.BlockSpec(memory_space=places[place]) for _, _, place in outs],
        scratch_shapes=list(scratch),
        input_output_aliases=aliases or {},
        cost_estimate=pl.CostEstimate(flops=1000, bytes_accessed=1000, transcendentals=0),
        compiler_params=pltpu.CompilerParams(vmem_limit_bytes=vmem * 2**20),
    )(*[pin(value) if place in "HL" else value for value, place in ins])


DMA = pltpu.SemaphoreType.DMA


def send_copies(source, target, indices, sem):
    copies = [pltpu.make_async_copy(source, target.at[index], sem.at[index]) for index in indices]
    for copy in copies:
        copy.start()
    return copies


def wait_all(copies):
    for copy in copies:
        copy.wait()


def weight_copies(w_ref, w_buf, w_sem):
    group = group_index()
    copies = []
    for slot, part in enumerate((1, 2, 0)):
        column = pl.multiple_of(part * D + (group // 2) * 384, 128)
        copy = pltpu.make_async_copy(w_ref.at[:, pl.ds(column, 384)], w_buf.at[slot], w_sem.at[slot])
        copy.start()
        copies.append(copy)
    return copies


def project_kernel(
    tok_ref, gain_ref, shift_ref, w_ref, kv_ref, normed_ref,
    x_buf, w_buf, kv_buf, gain_buf, shift_buf, x_sem, w_sem, kv_sem, gain_sem, shift_sem,
):
    copy_x = pltpu.make_async_copy(tok_ref.at[lax.axis_index(MICRO)], x_buf, x_sem)
    copy_x.start()
    copy_gain = pltpu.make_async_copy(gain_ref, gain_buf, gain_sem)
    copy_gain.start()
    copy_shift = pltpu.make_async_copy(shift_ref, shift_buf, shift_sem)
    copy_shift.start()
    copies = weight_copies(w_ref, w_buf, w_sem)
    wait_all([copy_x, copy_gain, copy_shift])
    unit, _ = normalized(x_buf[...].astype(F32))
    normed = (unit * gain_buf[...].reshape(1, D) + shift_buf[...].reshape(1, D)).astype(BF)
    odd = (group_index() % 2) == 1

    def part(slot):
        copies[slot].wait()
        full = mm(normed, w_buf[slot])
        return jnp.where(odd, full[:, 192:], full[:, :192]).astype(BF)

    kv_buf[...] = jnp.concatenate([part(0), part(1), part(2), jnp.zeros((TOK, HD), BF)], axis=1)
    sends = send_copies(kv_buf, kv_ref, range(8), kv_sem)
    normed_ref[...] = normed
    wait_all(sends)


def attend_kernel(scene_ref, same_ref, other_ref, out_ref, buf, sem):
    first, big = span(scene_ref)

    def run(count):
        rows = count * TOK
        keys = jnp.concatenate(
            [ref[pl.ds(first, count), :, :384].reshape(rows, 384) for ref in (same_ref, other_ref)], axis=0
        )
        query = same_ref[chip_index(), :, 384:]
        q0, q1 = halves(query[:, :128])
        blocks = [keys[:, :128], keys[:, 128:256], keys[:, 256:]]
        mixed = []
        columns = []
        for qh, kb, vb in ((q0, 0, 1), (q1, 0, 2), (query[:, 128:], 1, 2)):
            scores = mm_nt(qh, blocks[kb]) * (HD**-0.5)
            top = jnp.max(scores, axis=-1, keepdims=True)
            weights = jnp.exp(scores - top)
            total = jnp.sum(weights, axis=-1, keepdims=True)
            probs = (weights * (1.0 / total)).astype(BF)
            mixed.append(mm(probs, blocks[vb]))
            columns += three(top + jnp.log(total))
        stats = put_columns(128, TOK, 0, columns)
        buf[...] = jnp.concatenate([join(stats, mixed[0]), join(mixed[1], mixed[2])], axis=1).astype(BF)

    @pl.when(big)
    def _():
        run(5)

    @pl.when(jnp.logical_not(big))
    def _():
        run(1)

    wait_all(send_copies(buf, out_ref, range(8), sem))


def forward_kernel(
    mixed_ref, tok_ref, og_ref, wo_ref, gain_ref, shift_ref, up_ref, down_ref,
    out_ref, middle_ref, normed_ref, act_ref, gpre_ref,
    tok_buf, og_buf, up_buf, down_buf, grad_buf, branch_buf, in_sem, sem,
):
    loads = [
        pltpu.make_async_copy(ref, buf, in_sem.at[index])
        for index, (ref, buf) in enumerate(
            ((tok_ref, tok_buf), (up_ref, up_buf), (og_ref, og_buf), (down_ref, down_buf))
        )
    ]
    for load in loads:
        load.start()
    total = jnp.zeros((2 * TOK, D), F32)
    for group in range(4):
        rows = jnp.concatenate([mixed_ref[group], mixed_ref[4 + group]], axis=0)
        total = total + mm(rows, wo_ref[group])
    loads[0].wait()
    total = total + tok_buf[...].reshape(2 * TOK, D).astype(F32)
    middle_ref[...] = total.reshape(8, BLK, D)
    unit, _ = normalized(total)
    normed = (unit * gain_ref[...].reshape(1, D) + shift_ref[...].reshape(1, D)).astype(BF)
    normed_ref[...] = normed
    loads[1].wait()
    pre = mm(normed, up_buf[...])
    cdf = 0.5 * (1.0 + lax.erf(pre * (0.5**0.5)))
    slope = cdf + pre * jnp.exp(-0.5 * pre * pre) * 0.3989422804014327
    loads[2].wait()
    loads[3].wait()
    grad_out = og_buf[...].reshape(2 * TOK, D)
    gpre = (mm_nt(grad_out, down_buf[...]) * slope).astype(BF)
    gpre_ref[...] = gpre
    grad_buf[...] = mm_nt(gpre, up_buf[...]).astype(BF).reshape(8, BLK, D)
    first = pltpu.make_async_copy(grad_buf, out_ref.at[:, pl.ds(BLK, BLK)], sem.at[0])
    first.start()
    act = (pre * cdf).astype(BF)
    act_ref[...] = act
    branch_buf[...] = mm(act, down_buf[...]).astype(BF).reshape(8, BLK, D)
    second = pltpu.make_async_copy(branch_buf, out_ref.at[:, pl.ds(0, BLK)], sem.at[1])
    second.start()
    first.wait()
    second.wait()


def ff_grads_kernel(normed_ref, act_ref, gpre_ref, og_ref, keep_ref, send_ref, up_buf, down_buf):
    core = lax.axis_index(CORE)
    up_buf[...] = mm_tn(normed_ref[...], gpre_ref[...])
    down_buf[...] = mm_tn(act_ref[...], og_ref[...].reshape(2 * TOK, D))
    for ref, owner in ((keep_ref, core), (send_ref, 1 - core)):
        column = pl.multiple_of(owner * 384, 128)
        for tile in range(8):
            rows = pl.ds(pl.multiple_of((2 * tile + owner) * 48, 16), 48)
            ref[tile, :, :384] = up_buf[rows].astype(BF)
            ref[tile, :, 384:] = down_buf[tile * 48:(tile + 1) * 48, pl.ds(column, 384)].astype(BF)


def split_kernel(one_ref, two_ref, *refs):
    y = lax.axis_index("y")
    for k, ref in enumerate(refs):
        for xl in range(2):
            at = (y ^ k) * 2 + xl
            ref[xl] = (one_ref[at].astype(F32) + two_ref[at].astype(F32)).astype(BF)


def halve_kernel(*refs):
    parts, (keep_ref, send_ref) = refs[:4], refs[4:]
    xl = lax.axis_index("xl")
    for ref, at in ((keep_ref, xl), (send_ref, 1 - xl)):
        total = parts[0][at].astype(F32)
        for part in parts[1:]:
            total = total + part[at].astype(F32)
        ref[...] = total.astype(BF)


def pair_kernel(one_ref, two_ref, out_ref):
    total = (one_ref[...].astype(F32) + two_ref[...].astype(F32)).astype(BF)
    out_ref[0] = total[:, :384]
    out_ref[1] = total[:, 384:]


def middle_kernel(
    sums_ref, middle_ref, og_ref, tok_ref, mixed_ref, wo_ref, gain_ref,
    out_ref, low_ref, grad_ref, result_ref, vec_ref, x_ref, buf, middle_buf, og_buf, mixed_buf, x_sem, in_sem, sem,
):
    micro = lax.axis_index(MICRO)
    group = group_index()
    block = pl.ds(pl.multiple_of(group * BLK, BLK), BLK)
    loads = [
        pltpu.make_async_copy(middle_ref.at[micro * 4 + group], middle_buf, in_sem.at[0]),
        pltpu.make_async_copy(og_ref.at[micro, block], og_buf, in_sem.at[1]),
        pltpu.make_async_copy(mixed_ref.at[pl.ds(micro * 4, 4), block], mixed_buf, in_sem.at[2]),
        pltpu.make_async_copy(tok_ref.at[micro, block], x_ref, x_sem),
    ]
    for load in loads:
        load.start()
    total = sums_ref[0].astype(F32)
    for index in range(1, 8):
        total = total + sums_ref[index].astype(F32)
    branch, grad = total[:BLK], total[BLK:]
    wait_all(loads)
    middle = middle_buf[...]
    unit, inverse = normalized(middle)
    grad_mid = og_buf[...].astype(F32) + norm_back(grad, unit, inverse, gain_ref[...].reshape(1, D))
    low = grad_mid.astype(BF)
    lane = lax.broadcasted_iota(jnp.int32, (BLK, 256), 1)
    for head_group in range(4):
        mixed = mixed_buf[head_group].astype(F32)
        back = mm_nt(low, wo_ref[head_group]).astype(BF).astype(F32)
        product = mixed * back
        columns = []
        for head in range(3):
            inside = (lane >= (head + 1) * HD) & (lane < (head + 2) * HD)
            columns += three(jnp.sum(jnp.where(inside, product, 0.0), axis=-1, keepdims=True))
        stats = put_columns(256, BLK, 9, columns)
        buf[head_group] = jnp.where(lane < 9, mixed, jnp.where(lane < HD, stats, back)).astype(BF)
    sends = send_copies(buf, out_ref, range(8), sem)
    low_ref[...] = low
    grad_ref[...] = grad_mid
    result_ref[...] = (middle + branch).astype(BF)
    gain_grad = jnp.sum(grad * unit, axis=0, keepdims=True)
    shift_grad = jnp.sum(grad, axis=0, keepdims=True)
    vec_ref[...] = jnp.concatenate([gain_grad, shift_grad, jnp.zeros((6, D), F32)], axis=0)
    wait_all(sends)


def attend_back_kernel(
    scene_ref, kvs_ref, kvo_ref, gs_ref, go_ref, normed_ref, mixed_ref, low0_ref, low1_ref, low2_ref, low3_ref,
    gqkv_ref, keep_ref, send_ref, kv_buf, grad_buf, mixed_buf, kv_sem, mixed_sem,
):
    first, big = span(scene_ref)
    chip = chip_index()
    core = lax.axis_index(CORE)
    group = group_index()
    scale = HD**-0.5

    def run(count):
        rows = count * TOK
        loads = [
            pltpu.make_async_copy(ref.at[pl.ds(first, count)], kv_buf.at[slot, pl.ds(0, count)], kv_sem.at[slot])
            for slot, ref in enumerate((kvs_ref, kvo_ref))
        ]
        for load in loads:
            load.start()

        def cut(value):
            return [value[:, at:at + 128] for at in range(0, value.shape[1], 128)]

        grad = cut(jnp.concatenate(
            [ref[pl.ds(first, count)].reshape(rows, 256) for ref in (gs_ref, go_ref)], axis=0
        ))
        g_own = cut(gs_ref[chip])
        g_heads = [halves(g_own[0])[1], *halves(g_own[1])]
        own_stats = g_own[0].astype(F32)
        all_stats = grad[0].astype(F32).T
        wait_all(loads)
        every = cut(jnp.concatenate([kv_buf[slot, :count].reshape(rows, 640) for slot in range(2)], axis=0))
        kv, query = every[:3], every[3:]
        own = cut(kv_buf[0, chip - first])
        q_heads = [*halves(own[3]), own[4]]
        k_heads = [*halves(own[0]), halves(own[1])[0]]
        v_heads = [halves(own[1])[1], *halves(own[2])]

        def column(at):
            return own_stats[:, at:at + 1] + own_stats[:, at + 1:at + 2] + own_stats[:, at + 2:at + 3]

        def row(at):
            return all_stats[at:at + 1] + all_stats[at + 1:at + 2] + all_stats[at + 2:at + 3]

        dq, dk, dv = [], [], []
        for head, (kb, vb) in enumerate(((0, 1), (0, 2), (1, 2))):
            qb, gb = (0, 0, 1)[head], (0, 1, 1)[head]
            probs = jnp.exp(mm_nt(q_heads[head], kv[kb]) * scale - column(3 * head))
            gap = mm_nt(g_heads[head], kv[vb]) - column(9 + 3 * head)
            dq.append(mm((probs * gap).astype(BF), kv[kb]) * scale)
            probs = jnp.exp(mm_nt(k_heads[head], query[qb]) * scale - row(3 * head))
            gap = mm_nt(v_heads[head], grad[gb]) - row(9 + 3 * head)
            dv.append(mm(probs.astype(BF), grad[gb]))
            dk.append(mm((probs * gap).astype(BF), query[qb]) * scale)
        tail = dq[2]
        gqkv_ref[...] = jnp.concatenate(
            [join(dk[0], dk[1]), join(dk[2], dv[0]), join(dv[1], dv[2]), join(dq[0], dq[1]),
             join(tail, jnp.zeros_like(tail))],
            axis=1,
        ).astype(BF)

    index = lax.axis_index(MICRO) * 4 + group
    load_mixed = pltpu.make_async_copy(mixed_ref.at[index], mixed_buf, mixed_sem)
    load_mixed.start()

    @pl.when(big)
    def _():
        run(5)

    @pl.when(jnp.logical_not(big))
    def _():
        run(1)

    grad_buf[...] = mm_tn(normed_ref[...], gqkv_ref[...])
    load_mixed.wait()
    low = jnp.concatenate([ref[...] for ref in (low0_ref, low1_ref, low2_ref, low3_ref)], axis=0)
    mixed = jnp.concatenate(
        [mixed_buf[pl.ds(pl.multiple_of((group ^ k) * BLK, BLK), BLK)] for k in range(4)], axis=0
    )
    out = mm_tn(mixed, low)[HD:]
    for ref, owner in ((keep_ref, core), (send_ref, 1 - core)):
        for tile in range(8):
            rows = grad_buf[pl.ds(pl.multiple_of((2 * tile + owner) * 48, 16), 48)]
            at = (tile // 4) * 96
            pieces = [
                out[at + row * 48:at + (row + 1) * 48, (tile % 4) * 192:(tile % 4 + 1) * 192] for row in range(2)
            ]
            ref[2 * tile] = rows[:, :384].astype(BF)
            ref[2 * tile + 1] = jnp.concatenate(
                [rows[:, 384:576], jnp.where(owner == 1, pieces[1], pieces[0])], axis=1
            ).astype(BF)

def normed_grad_kernel(
    gqkv_ref, tok_ref, w_ref, vec_ref, own_ref, one_ref, two_ref, three_ref, sums_ref,
    x_buf, part_buf, w_buf, x_sem, w_sem,
):
    load = pltpu.make_async_copy(tok_ref.at[lax.axis_index(MICRO)], x_buf, x_sem)
    load.start()
    loads = weight_copies(w_ref, w_buf, w_sem)
    group = group_index()
    odd = (group % 2) == 1
    load.wait()
    unit, _ = normalized(x_buf[...].astype(F32))
    total = jnp.zeros((TOK, D), F32)
    for slot in range(3):
        part = gqkv_ref[:, slot * 192:(slot + 1) * 192]
        zero = jnp.zeros_like(part)
        wide = jnp.where(
            odd, jnp.concatenate([zero, part], axis=1), jnp.concatenate([part, zero], axis=1)
        )
        loads[slot].wait()
        total = total + mm_nt(wide, w_buf[slot])
    part_buf[...] = total
    own_ref[...] = part_buf[pl.ds(pl.multiple_of(group * BLK, BLK), BLK)]
    for k, ref in ((1, one_ref), (2, two_ref), (3, three_ref)):
        ref[...] = part_buf[pl.ds(pl.multiple_of((group ^ k) * BLK, BLK), BLK)].astype(BF)
    gain1 = jnp.sum(total * unit, axis=0, keepdims=True)
    shift1 = jnp.sum(total, axis=0, keepdims=True)
    sums_ref[...] = jnp.concatenate([gain1, shift1, vec_ref[...][:2], jnp.zeros((4, D), F32)], axis=0)


def add_kernel(one_ref, two_ref, ff_ref, out_ref, buf, sem, ff_sem):
    micro = lax.axis_index(MICRO)
    copies = []
    for chip in range(8):
        for half in range(2):
            copy = pltpu.make_async_copy(
                ff_ref.at[half], out_ref.at[2 * chip + micro, pl.ds(48 * (1 + half), 48)], ff_sem.at[chip, half]
            )
            copy.start()
            copies.append(copy)
    buf[...] = (one_ref[...].astype(F32) + two_ref[...].astype(F32)).astype(BF)
    copy = pltpu.make_async_copy(buf, out_ref.at[:, pl.ds(0, 48)], sem)
    copy.start()
    copies.append(copy)
    wait_all(copies)


def pick_kernel(in_ref, out_ref):
    micro = lax.axis_index(MICRO)
    for chip in range(8):
        out_ref[chip] = in_ref[2 * chip + micro, 48:]


def sum_kernel(in_ref, vec_ref, out_ref, buf, sem):
    total = in_ref[0, :48].astype(F32)
    for index in range(1, 16):
        total = total + in_ref[index, :48].astype(F32)
    vectors = vec_ref[...][:4]
    block = jnp.concatenate([total, vectors[:, :384], vectors[:, 384:]], axis=0).astype(BF)
    for index in range(8):
        buf[index] = block
    wait_all(send_copies(buf, out_ref, range(8), sem))


def spread_kernel(turn, in_ref, *refs):
    qkv_buf, out_buf, sem, out_sem = refs[-4:]
    qkv_ref, out_ref, *vec_refs = refs[3:-4] if turn else refs[:-4]
    owner = lax.axis_index(CORE)
    owner = 1 - owner if turn else owner
    copies = []
    vectors = jnp.zeros((8, 384), F32)
    for tile in range(8):
        whole = [in_ref[tile, index].astype(F32) for index in range(8)]
        block = [value[:48] for value in whole]
        for value in whole:
            vectors = vectors + value[48:]
        for part, half, at in ((1, 0, 0), (2, 0, 192), (0, 4, 0)):
            qkv_buf[tile, :, part * D:(part + 1) * D] = jnp.concatenate(
                [block[half + group][:, at:at + 192] for group in range(4)], axis=1
            )
        start = pl.multiple_of((2 * tile + owner) * 48, 16)
        copy = pltpu.make_async_copy(qkv_buf.at[tile], qkv_ref.at[pl.ds(start, 48)], sem.at[tile])
        copy.start()
        copies.append(copy)
        for group in range(4):
            out_buf[group, tile // 4, :, (tile % 4) * 192:(tile % 4 + 1) * 192] = block[4 + group][:, 192:]
    for group in range(4):
        for pair in range(2):
            start = pl.multiple_of(group * 192 + (pair * 2 + owner) * 48, 16)
            copy = pltpu.make_async_copy(
                out_buf.at[group, pair], out_ref.at[pl.ds(start, 48)], out_sem.at[group, pair]
            )
            copy.start()
            copies.append(copy)
    if turn:
        vectors = vectors + refs[0][...]
        for k, ref in enumerate(vec_refs):
            ref[...] = jnp.concatenate([vectors[k:k + 1], vectors[4 + k:5 + k]], axis=1).reshape(D)
    else:
        vec_refs[0][...] = vectors
    wait_all(copies)


def spread_ff_kernel(same_ref, other_ref, up_ref, down_ref):
    core = lax.axis_index(CORE)
    for ref, owner in ((same_ref, core), (other_ref, 1 - core)):
        for chip in range(8):
            up_ref[pl.ds(pl.multiple_of((chip * 2 + owner) * 48, 16), 48)] = ref[chip, :48].astype(F32)
            down_ref[chip * 48:(chip + 1) * 48, pl.ds(pl.multiple_of(owner * 384, 128), 384)] = ref[
                chip, 48:
            ].astype(F32)


def input_kernel(
    own_ref, one_ref, two_ref, three_ref, x_ref, gain_ref, grad_ref, result_ref, out_ref
):
    total = own_ref[...]
    for ref in (one_ref, two_ref, three_ref):
        total = total + ref[...].astype(F32)
    unit, inverse = normalized(x_ref[...].astype(F32))
    grad = grad_ref[...] + norm_back(total, unit, inverse, gain_ref[...].reshape(1, D))
    out_ref[:BLK] = grad.astype(BF)
    out_ref[BLK:] = result_ref[...]


def unpack_kernel(*refs):
    parts, (grad_ref, result_ref) = refs[:8], refs[8:]
    micro = lax.axis_index(MICRO)
    group = group_index()
    for k, ref in enumerate(parts):
        rows = pl.ds(pl.multiple_of((group ^ (k % 4)) * BLK, BLK), BLK)
        where = micro ^ (k // 4)
        grad_ref[where, rows] = ref[:BLK].astype(F32)
        result_ref[where, rows] = ref[BLK:]


def exchange(value, axes):
    return lax.all_to_all(value, axes, 0, 0, tiled=True)


def swap(value):
    return lax.ppermute(value, CORE, [(0, 1), (1, 0)])


def after(value, *others):
    return pl.pallas_call(
        lambda *refs: None,
        out_shape=jax.ShapeDtypeStruct(value.shape, value.dtype),
        in_specs=[pl.BlockSpec(memory_space=pl.ANY)] * (1 + len(others)),
        out_specs=pl.BlockSpec(memory_space=pl.ANY),
        input_output_aliases={0: 0},
        cost_estimate=pl.CostEstimate(flops=1, bytes_accessed=1, transcendentals=0),
        compiler_params=pltpu.CompilerParams(vmem_limit_bytes=2**20),
    )(value, *others)


def flip(value, axes, count, bits):
    return lax.ppermute(value, axes, [(index, index ^ bits) for index in range(count)])


def shards(
    tokens, scene_of_block, ln1_gain, ln1_shift, w_qkv, w_out, ln2_gain, ln2_shift, w_up, w_down, out_grad
):
    w_out_pad = jnp.pad(w_out.reshape(4, 192, D), ((0, 0), (HD, 0), (0, 0)))
    kv_send, normed = call(
        project_kernel,
        [((8, TOK, 640), BF, "H"), ((TOK, D), BF, "L")],
        [(tokens, "H"), (ln1_gain, "H"), (ln1_shift, "H"), (w_qkv, "H")],
        10**9,
        [
            pltpu.VMEM((TOK, D), BF), pltpu.VMEM((3, D, 384), BF), pltpu.VMEM((TOK, 640), BF),
            pltpu.VMEM((D,), F32), pltpu.VMEM((D,), F32), DMA, DMA((3,)), DMA((8,)), DMA, DMA,
        ],
    )
    kv_same = exchange(kv_send, CHIP)
    kv_other = swap(kv_same)
    (mixed_send,) = call(
        attend_kernel,
        [((8, TOK, 256), BF, "H")],
        [(scene_of_block, "S"), (kv_same, "V"), (kv_other, "V")],
        2 * 10**9,
        [pltpu.VMEM((TOK, 256), BF), DMA((8,))],
    )
    mixed = exchange(mixed_send, NARROW)
    ff_send, middle, normed2, act, grad_pre = call(
        forward_kernel,
        [
            ((8, 2 * BLK, D), BF, "H"), ((8, BLK, D), F32, "L"), ((2 * TOK, D), BF, "V"),
            ((2 * TOK, FFL), BF, "V"), ((2 * TOK, FFL), BF, "V"),
        ],
        [
            (mixed, "V"), (tokens, "H"), (out_grad, "H"), (w_out_pad, "V"), (ln2_gain, "L"), (ln2_shift, "L"),
            (w_up, "H"), (w_down, "H"),
        ],
        4 * 10**9,
        [
            pltpu.VMEM((2, TOK, D), BF), pltpu.VMEM((2, TOK, D), BF), pltpu.VMEM((D, FFL), BF),
            pltpu.VMEM((FFL, D), BF), pltpu.VMEM((8, BLK, D), BF), pltpu.VMEM((8, BLK, D), BF), DMA((4,)), DMA((2,)),
        ],
    )
    ff_sums = exchange(ff_send, NARROW)
    keep, send = call(
        ff_grads_kernel,
        [((8, 48, D), BF, "V")] * 2,
        [(normed2, "V"), (act, "V"), (grad_pre, "V"), (out_grad, "L")],
        2 * 10**9,
        [pltpu.VMEM((D, FFL), F32), pltpu.VMEM((FFL, D), F32)],
    )
    pieces = call(
        split_kernel, [((2, 48, D), BF, "L")] * 4, [(keep, "V"), (swap(send), "V")], 10**8
    )
    pieces = [pieces[0]] + [flip(pieces[k], "y", 4, k) for k in (1, 2, 3)]
    keep, send = call(
        halve_kernel,
        [((48, D), BF, "L")] * 2,
        [(pieces[0], "L")] + [(piece, "V") for piece in pieces[1:]],
        10**8,
    )
    ff_sums = after(ff_sums, pin(keep))
    grad_send, low, grad_mid, result_part, vec2, x_part = call(
        middle_kernel,
        [
            ((8, 4, BLK, 256), BF, "H"), ((BLK, D), BF, "L"), ((BLK, D), F32, "L"), ((BLK, D), BF, "L"),
            ((8, D), F32, "L"), ((BLK, D), BF, "L"),
        ],
        [
            (ff_sums, "V"), (middle, "H"), (out_grad, "H"), (tokens, "H"), (mixed, "H"), (w_out_pad, "V"),
            (ln2_gain, "L"),
        ],
        10**9,
        [
            pltpu.VMEM((4, BLK, 256), BF), pltpu.VMEM((BLK, D), F32), pltpu.VMEM((BLK, D), BF),
            pltpu.VMEM((4, BLK, 256), BF), DMA, DMA((3,)), DMA((8,)),
        ],
    )
    (ff_part,) = call(
        pair_kernel, [((2, 48, 384), BF, "L")], [(keep, "L"), (flip(send, "xl", 2, 1), "V")], 10**7
    )
    grad_same = exchange(grad_send.reshape(32, BLK, 256), (*CHIP, *GROUP)).reshape(8, TOK, 256)
    lows = [flip(low, GROUP, 4, k) for k in (1, 2, 3)]
    grad_same = after(grad_same, *lows, pin(ff_part))
    grad_other = swap(grad_same)
    gqkv, keep, send = call(
        attend_back_kernel,
        [((TOK, 640), BF, "L")] + [((16, 48, 384), BF, "V")] * 2,
        [
            (scene_of_block, "S"), (kv_same, "H"), (kv_other, "H"), (grad_same, "V"), (grad_other, "V"),
            (normed, "L"), (mixed, "H"), (low, "L"), *[(value, "V") for value in lows],
        ],
        8 * 10**9,
        [
            pltpu.VMEM((2, 5, TOK, 640), BF), pltpu.VMEM((D, 640), F32), pltpu.VMEM((TOK, 256), BF), DMA((2,)), DMA,
        ],
        vmem=24,
    )
    (weight_send,) = call(
        add_kernel,
        [((16, 144, 384), BF, "H")],
        [(keep, "V"), (swap(send), "V"), (ff_part, "L")],
        10**8,
        [pltpu.VMEM((16, 48, 384), BF), DMA, DMA((8, 2))],
    )
    weight_parts = exchange(weight_send, (*CHIP, MICRO))
    own, *sends, sums = call(
        normed_grad_kernel,
        [((BLK, D), F32, "L")] + [((BLK, D), BF, "L")] * 3 + [((8, D), F32, "L")],
        [(gqkv, "L"), (tokens, "H"), (w_qkv, "H"), (vec2, "L")],
        10**9,
        [pltpu.VMEM((TOK, D), BF), pltpu.VMEM((TOK, D), F32), pltpu.VMEM((3, D, 384), BF), DMA, DMA((3,))],
    )
    parts = [flip(value, GROUP, 4, k + 1) for k, value in enumerate(sends)]
    weight_parts = after(weight_parts, pin(sums), *parts)
    (weight_total,) = call(
        sum_kernel,
        [((8, 8, 56, 384), BF, "H")],
        [(weight_parts, "V"), (sums, "L")],
        10**8,
        [pltpu.VMEM((8, 56, 384), BF), DMA((8,))],
    )
    (packed,) = call(
        input_kernel,
        [((2 * BLK, D), BF, "L")],
        [
            (own, "L"), *[(value, "V") for value in parts], (x_part, "L"), (ln1_gain, "L"), (grad_mid, "L"),
            (result_part, "L"),
        ],
        10**8,
    )
    others = {k: flip(packed, NARROW, 8, k) for k in (7, 5, 6, 3, 1, 4, 2)}
    input_grad, result = call(
        unpack_kernel,
        [((2, TOK, D), F32, "L"), ((2, TOK, D), BF, "L")],
        [(packed, "L"), *[(others[k], "V") for k in range(1, 8)]],
        10**8,
    )
    (ff_same,) = call(pick_kernel, [((8, 96, 384), BF, "V")], [(weight_parts, "V")], 10**7)
    up_grad, down_grad = call(
        spread_ff_kernel,
        [((D, FFL), F32, "L"), ((FFL, D), F32, "L")],
        [(ff_same, "V"), (swap(ff_same), "V")],
        10**7,
    )
    weight_same = exchange(weight_total.reshape(64, 56, 384), (*CHIP, *NARROW)).reshape(8, 8, 56, 384)
    weight_same = after(weight_same, *map(pin, (input_grad, result, up_grad, down_grad)))
    weight_other = swap(weight_same)
    scratch = [
        pltpu.VMEM((8, 48, 3 * D), F32), pltpu.VMEM((4, 2, 48, D), F32), DMA((8,)), DMA((4, 2)),
    ]
    grads = [((D, 3 * D), F32, "H"), ((D, D), F32, "H")]
    half = call(
        functools.partial(spread_kernel, False),
        grads + [((8, 384), F32, "V")],
        [(weight_same, "V")],
        10**8,
        scratch,
    )
    qkv_grad, out_proj_grad, *vectors = call(
        functools.partial(spread_kernel, True),
        grads + [((D,), F32, "L")] * 4,
        [(weight_other, "V"), (half[2], "V"), (half[0], "H"), (half[1], "H")],
        10**8,
        scratch,
        aliases={2: 0, 3: 1},
    )
    return (
        result, input_grad, qkv_grad, out_proj_grad, *vectors, up_grad, down_grad
    )


def solution(mesh):
    names = ("y", "xl", "c", "zh", "zl", "xh")
    fine = Mesh(mesh.devices.reshape(4, 2, 2, 2, 2, 2), names)
    tokens = P(None, WIDE, None)
    placed = (
        tokens, P(), P(), P(), P(), P(), P(), P(), P(None, NARROW), P(NARROW, None), tokens
    )
    return jax.shard_map(
        shards,
        mesh=fine,
        in_specs=placed,
        out_specs=(
            tokens, tokens, P(), P(), P(), P(), P(), P(), P(None, NARROW), P(NARROW, None)
        ),
        check_vma=False,
    )
```

```python
import functools

import jax
import jax.numpy as jnp
from jax import lax
from jax.experimental import pallas as pl
from jax.experimental.pallas import tpu as pltpu
from jax.sharding import Mesh
from jax.sharding import PartitionSpec as P

D = 768
HD = 64
FFL = 384
TOK = 128
BLK = 32
EPS = 1e-05
BF = jnp.bfloat16
F32 = jnp.float32

CHIP = ("y", "xl")
CORE = "c"
MICRO = "zh"
GROUP = ("zl", "xh")
NARROW = (MICRO, *GROUP)
WIDE = (*CHIP, CORE)


def chip_index():
    return lax.axis_index("y") * 2 + lax.axis_index("xl")


def group_index():
    return lax.axis_index("zl") * 2 + lax.axis_index("xh")


def mm(left, right):
    return lax.dot_general(left, right, (((1,), (0,)), ((), ())), preferred_element_type=F32)


def mm_nt(left, right):
    return lax.dot_general(left, right, (((1,), (1,)), ((), ())), preferred_element_type=F32)


def mm_tn(left, right):
    return lax.dot_general(left, right, (((0,), (0,)), ((), ())), preferred_element_type=F32)


def normalized(values):
    center = values - jnp.mean(values, axis=-1, keepdims=True)
    spread = jnp.mean(center * center, axis=-1, keepdims=True)
    inverse = lax.rsqrt(spread + EPS)
    return center * inverse, inverse


def norm_back(grad, unit, inverse, gain):
    scaled = grad * gain
    first = jnp.mean(scaled, axis=-1, keepdims=True)
    second = jnp.mean(scaled * unit, axis=-1, keepdims=True)
    return inverse * (scaled - first - unit * second)


def halves(block):
    lane = lax.broadcasted_iota(jnp.int32, block.shape, 1)
    zero = jnp.zeros_like(block)
    return jnp.where(lane < HD, block, zero), jnp.where(lane < HD, zero, block)


def join(low, high):
    lane = lax.broadcasted_iota(jnp.int32, low.shape, 1)
    return jnp.where(lane < HD, low, high)


def span(scene_ref):
    micro = lax.axis_index(MICRO)
    own = scene_ref[micro, chip_index() * 4]
    first = jnp.int32(0)
    count = jnp.int32(0)
    for index in range(8):
        other = scene_ref[micro, index * 4]
        first += (other < own).astype(jnp.int32)
        count += (other == own).astype(jnp.int32)
    return first, count > 1


def three(value):
    a = value.astype(BF).astype(F32)
    b = (value - a).astype(BF).astype(F32)
    c = value - a - b
    return a, b, c


def put_columns(width, rows, start, columns):
    lane = lax.broadcasted_iota(jnp.int32, (rows, width), 1)
    out = jnp.zeros((rows, width), F32)
    for offset, column in enumerate(columns):
        out = jnp.where(lane == start + offset, column, out)
    return out


def pin(value):
    return pltpu.with_memory_space_constraint(value, pltpu.HBM)


def call(kernel, outs, ins, cost, scratch=(), vmem=16, aliases=None):
    places = {"V": pltpu.VMEM, "H": pltpu.HBM, "S": pltpu.SMEM, "L": pltpu.VMEM}
    return pl.pallas_call(
        kernel,
        out_shape=[
            (pltpu.HBM if place in "HL" else jax.ShapeDtypeStruct)(shape, dtype) for shape, dtype, place in outs
        ],
        in_specs=[pl.BlockSpec(memory_space=places[place]) for _, place in ins],
        out_specs=[pl.BlockSpec(memory_space=places[place]) for _, _, place in outs],
        scratch_shapes=list(scratch),
        input_output_aliases=aliases or {},
        cost_estimate=pl.CostEstimate(flops=1000, bytes_accessed=1000, transcendentals=0),
        compiler_params=pltpu.CompilerParams(vmem_limit_bytes=vmem * 2**20),
    )(*[pin(value) if place in "HL" else value for value, place in ins])


DMA = pltpu.SemaphoreType.DMA


def send_copies(source, target, indices, sem):
    copies = [pltpu.make_async_copy(source, target.at[index], sem.at[index]) for index in indices]
    for copy in copies:
        copy.start()
    return copies


def wait_all(copies):
    for copy in copies:
        copy.wait()


def weight_copies(w_ref, w_buf, w_sem):
    group = group_index()
    copies = []
    for slot, part in enumerate((1, 2, 0)):
        column = pl.multiple_of(part * D + (group // 2) * 384, 128)
        copy = pltpu.make_async_copy(w_ref.at[:, pl.ds(column, 384)], w_buf.at[slot], w_sem.at[slot])
        copy.start()
        copies.append(copy)
    return copies


def project_kernel(
    tok_ref, gain_ref, shift_ref, w_ref, kv_ref, q_ref, normed_ref,
    x_buf, w_buf, kv_buf, gain_buf, shift_buf, x_sem, w_sem, kv_sem, gain_sem, shift_sem,
):
    copy_x = pltpu.make_async_copy(tok_ref.at[lax.axis_index(MICRO)], x_buf, x_sem)
    copy_x.start()
    copy_gain = pltpu.make_async_copy(gain_ref, gain_buf, gain_sem)
    copy_gain.start()
    copy_shift = pltpu.make_async_copy(shift_ref, shift_buf, shift_sem)
    copy_shift.start()
    copies = weight_copies(w_ref, w_buf, w_sem)
    wait_all([copy_x, copy_gain, copy_shift])
    unit, _ = normalized(x_buf[...].astype(F32))
    normed = (unit * gain_buf[...].reshape(1, D) + shift_buf[...].reshape(1, D)).astype(BF)
    odd = (group_index() % 2) == 1

    def part(slot):
        copies[slot].wait()
        full = mm(normed, w_buf[slot])
        return jnp.where(odd, full[:, 192:], full[:, :192]).astype(BF)

    kv_buf[...] = jnp.concatenate([part(0), part(1)], axis=1)
    sends = send_copies(kv_buf, kv_ref, range(8), kv_sem)
    normed_ref[...] = normed
    q_ref[...] = jnp.concatenate([part(2), jnp.zeros((TOK, HD), BF)], axis=1)
    wait_all(sends)


def attend_kernel(scene_ref, q_ref, same_ref, other_ref, out_ref, buf, sem):
    first, big = span(scene_ref)

    def run(count):
        rows = count * TOK
        keys = jnp.concatenate(
            [ref[pl.ds(first, count)].reshape(rows, 384) for ref in (same_ref, other_ref)], axis=0
        )
        query = q_ref[...]
        q0, q1 = halves(query[:, :128])
        blocks = [keys[:, :128], keys[:, 128:256], keys[:, 256:]]
        mixed = []
        columns = []
        for qh, kb, vb in ((q0, 0, 1), (q1, 0, 2), (query[:, 128:], 1, 2)):
            scores = mm_nt(qh, blocks[kb]) * (HD**-0.5)
            top = jnp.max(scores, axis=-1, keepdims=True)
            weights = jnp.exp(scores - top)
            total = jnp.sum(weights, axis=-1, keepdims=True)
            probs = (weights * (1.0 / total)).astype(BF)
            mixed.append(mm(probs, blocks[vb]))
            columns += three(top + jnp.log(total))
        stats = put_columns(128, TOK, 0, columns)
        buf[...] = jnp.concatenate([join(stats, mixed[0]), join(mixed[1], mixed[2])], axis=1).astype(BF)

    @pl.when(big)
    def _():
        run(5)

    @pl.when(jnp.logical_not(big))
    def _():
        run(1)

    wait_all(send_copies(buf, out_ref, range(8), sem))


def forward_kernel(
    mixed_ref, tok_ref, og_ref, wo_ref, gain_ref, shift_ref, up_ref, down_ref,
    out_ref, middle_ref, normed_ref, act_ref, gpre_ref,
    tok_buf, og_buf, up_buf, down_buf, grad_buf, branch_buf, in_sem, sem,
):
    loads = [
        pltpu.make_async_copy(ref, buf, in_sem.at[index])
        for index, (ref, buf) in enumerate(
            ((tok_ref, tok_buf), (up_ref, up_buf), (og_ref, og_buf), (down_ref, down_buf))
        )
    ]
    for load in loads:
        load.start()
    total = jnp.zeros((2 * TOK, D), F32)
    for group in range(4):
        rows = jnp.concatenate([mixed_ref[group], mixed_ref[4 + group]], axis=0)
        total = total + mm(rows, wo_ref[group])
    loads[0].wait()
    total = total + tok_buf[...].reshape(2 * TOK, D).astype(F32)
    middle_ref[...] = total.reshape(8, BLK, D)
    unit, _ = normalized(total)
    normed = (unit * gain_ref[...].reshape(1, D) + shift_ref[...].reshape(1, D)).astype(BF)
    normed_ref[...] = normed
    loads[1].wait()
    pre = mm(normed, up_buf[...])
    cdf = 0.5 * (1.0 + lax.erf(pre * (0.5**0.5)))
    slope = cdf + pre * jnp.exp(-0.5 * pre * pre) * 0.3989422804014327
    loads[2].wait()
    loads[3].wait()
    grad_out = og_buf[...].reshape(2 * TOK, D)
    gpre = (mm_nt(grad_out, down_buf[...]) * slope).astype(BF)
    gpre_ref[...] = gpre
    grad_buf[...] = mm_nt(gpre, up_buf[...]).astype(BF).reshape(8, BLK, D)
    first = pltpu.make_async_copy(grad_buf, out_ref.at[:, pl.ds(BLK, BLK)], sem.at[0])
    first.start()
    act = (pre * cdf).astype(BF)
    act_ref[...] = act
    branch_buf[...] = mm(act, down_buf[...]).astype(BF).reshape(8, BLK, D)
    second = pltpu.make_async_copy(branch_buf, out_ref.at[:, pl.ds(0, BLK)], sem.at[1])
    second.start()
    first.wait()
    second.wait()


def ff_grads_kernel(normed_ref, act_ref, gpre_ref, og_ref, keep_ref, send_ref, up_buf, down_buf):
    core = lax.axis_index(CORE)
    up_buf[...] = mm_tn(normed_ref[...], gpre_ref[...])
    down_buf[...] = mm_tn(act_ref[...], og_ref[...].reshape(2 * TOK, D))
    for ref, owner in ((keep_ref, core), (send_ref, 1 - core)):
        column = pl.multiple_of(owner * 384, 128)
        for tile in range(8):
            rows = pl.ds(pl.multiple_of((2 * tile + owner) * 48, 16), 48)
            ref[tile, :, :384] = up_buf[rows].astype(BF)
            ref[tile, :, 384:] = down_buf[tile * 48:(tile + 1) * 48, pl.ds(column, 384)].astype(BF)


def split_kernel(one_ref, two_ref, *refs):
    y = lax.axis_index("y")
    for k, ref in enumerate(refs):
        for xl in range(2):
            at = (y ^ k) * 2 + xl
            ref[xl] = (one_ref[at].astype(F32) + two_ref[at].astype(F32)).astype(BF)


def halve_kernel(*refs):
    parts, (keep_ref, send_ref) = refs[:4], refs[4:]
    xl = lax.axis_index("xl")
    for ref, at in ((keep_ref, xl), (send_ref, 1 - xl)):
        total = parts[0][at].astype(F32)
        for part in parts[1:]:
            total = total + part[at].astype(F32)
        ref[...] = total.astype(BF)


def pair_kernel(one_ref, two_ref, out_ref):
    out_ref[...] = (one_ref[...].astype(F32) + two_ref[...].astype(F32)).astype(BF)


def middle_kernel(
    sums_ref, middle_ref, og_ref, tok_ref, mixed_ref, wo_ref, gain_ref,
    out_ref, low_ref, grad_ref, result_ref, vec_ref, x_ref, buf, middle_buf, og_buf, mixed_buf, x_sem, in_sem, sem,
):
    micro = lax.axis_index(MICRO)
    group = group_index()
    block = pl.ds(pl.multiple_of(group * BLK, BLK), BLK)
    loads = [
        pltpu.make_async_copy(middle_ref.at[micro * 4 + group], middle_buf, in_sem.at[0]),
        pltpu.make_async_copy(og_ref.at[micro, block], og_buf, in_sem.at[1]),
        pltpu.make_async_copy(mixed_ref.at[pl.ds(micro * 4, 4), block], mixed_buf, in_sem.at[2]),
        pltpu.make_async_copy(tok_ref.at[micro, block], x_ref, x_sem),
    ]
    for load in loads:
        load.start()
    total = sums_ref[0].astype(F32)
    for index in range(1, 8):
        total = total + sums_ref[index].astype(F32)
    branch, grad = total[:BLK], total[BLK:]
    wait_all(loads)
    middle = middle_buf[...]
    unit, inverse = normalized(middle)
    grad_mid = og_buf[...].astype(F32) + norm_back(grad, unit, inverse, gain_ref[...].reshape(1, D))
    low = grad_mid.astype(BF)
    lane = lax.broadcasted_iota(jnp.int32, (BLK, 256), 1)
    for head_group in range(4):
        mixed = mixed_buf[head_group].astype(F32)
        back = mm_nt(low, wo_ref[head_group]).astype(BF).astype(F32)
        product = mixed * back
        columns = []
        for head in range(3):
            inside = (lane >= (head + 1) * HD) & (lane < (head + 2) * HD)
            columns += three(jnp.sum(jnp.where(inside, product, 0.0), axis=-1, keepdims=True))
        stats = put_columns(256, BLK, 9, columns)
        buf[head_group] = jnp.where(lane < 9, mixed, jnp.where(lane < HD, stats, back)).astype(BF)
    sends = send_copies(buf, out_ref, range(8), sem)
    low_ref[...] = low
    grad_ref[...] = grad_mid
    result_ref[...] = (middle + branch).astype(BF)
    gain_grad = jnp.sum(grad * unit, axis=0, keepdims=True)
    shift_grad = jnp.sum(grad, axis=0, keepdims=True)
    vec_ref[...] = jnp.concatenate([gain_grad, shift_grad, jnp.zeros((6, D), F32)], axis=0)
    wait_all(sends)


def attend_back_kernel(
    scene_ref, kvs_ref, kvo_ref, q_ref, gs_ref, go_ref, normed_ref, mixed_ref, low0_ref, low1_ref, low2_ref, low3_ref,
    gqkv_ref, keep_ref, send_ref, kv_buf, q_buf, grad_buf, mixed_buf, kv_sem, q_sem, mixed_sem,
):
    first, big = span(scene_ref)
    chip = chip_index()
    core = lax.axis_index(CORE)
    group = group_index()
    scale = HD**-0.5

    def run(count):
        rows = count * TOK
        loads = [
            pltpu.make_async_copy(ref.at[pl.ds(first, count)], kv_buf.at[slot, pl.ds(0, count)], kv_sem.at[slot])
            for slot, ref in enumerate((kvs_ref, kvo_ref))
        ] + [
            pltpu.make_async_copy(
                q_ref.at[pl.ds(first, count), which], q_buf.at[slot, pl.ds(0, count)], q_sem.at[slot]
            )
            for slot, which in enumerate((core, 1 - core))
        ]
        for load in loads:
            load.start()

        def cut(value):
            return [value[:, at:at + 128] for at in range(0, value.shape[1], 128)]

        grad = cut(jnp.concatenate(
            [ref[pl.ds(first, count)].reshape(rows, 256) for ref in (gs_ref, go_ref)], axis=0
        ))
        g_own = cut(gs_ref[chip])
        g_heads = [halves(g_own[0])[1], *halves(g_own[1])]
        own_stats = g_own[0].astype(F32)
        all_stats = grad[0].astype(F32).T
        wait_all(loads)
        kv = cut(jnp.concatenate([kv_buf[slot, :count].reshape(rows, 384) for slot in range(2)], axis=0))
        query = cut(jnp.concatenate([q_buf[slot, :count].reshape(rows, 256) for slot in range(2)], axis=0))
        own = cut(kv_buf[0, chip - first]) + cut(q_buf[0, chip - first])
        q_heads = [*halves(own[3]), own[4]]
        k_heads = [*halves(own[0]), halves(own[1])[0]]
        v_heads = [halves(own[1])[1], *halves(own[2])]

        def column(at):
            return own_stats[:, at:at + 1] + own_stats[:, at + 1:at + 2] + own_stats[:, at + 2:at + 3]

        def row(at):
            return all_stats[at:at + 1] + all_stats[at + 1:at + 2] + all_stats[at + 2:at + 3]

        dq, dk, dv = [], [], []
        for head, (kb, vb) in enumerate(((0, 1), (0, 2), (1, 2))):
            qb, gb = (0, 0, 1)[head], (0, 1, 1)[head]
            probs = jnp.exp(mm_nt(q_heads[head], kv[kb]) * scale - column(3 * head))
            gap = mm_nt(g_heads[head], kv[vb]) - column(9 + 3 * head)
            dq.append(mm((probs * gap).astype(BF), kv[kb]) * scale)
            probs = jnp.exp(mm_nt(k_heads[head], query[qb]) * scale - row(3 * head))
            gap = mm_nt(v_heads[head], grad[gb]) - row(9 + 3 * head)
            dv.append(mm(probs.astype(BF), grad[gb]))
            dk.append(mm((probs * gap).astype(BF), query[qb]) * scale)
        tail = dq[2]
        gqkv_ref[...] = jnp.concatenate(
            [join(dk[0], dk[1]), join(dk[2], dv[0]), join(dv[1], dv[2]), join(dq[0], dq[1]),
             join(tail, jnp.zeros_like(tail))],
            axis=1,
        ).astype(BF)

    index = lax.axis_index(MICRO) * 4 + group
    load_mixed = pltpu.make_async_copy(mixed_ref.at[index], mixed_buf, mixed_sem)
    load_mixed.start()

    @pl.when(big)
    def _():
        run(5)

    @pl.when(jnp.logical_not(big))
    def _():
        run(1)

    grad_buf[...] = mm_tn(normed_ref[...], gqkv_ref[...])
    load_mixed.wait()
    low = jnp.concatenate([ref[...] for ref in (low0_ref, low1_ref, low2_ref, low3_ref)], axis=0)
    mixed = jnp.concatenate(
        [mixed_buf[pl.ds(pl.multiple_of((group ^ k) * BLK, BLK), BLK)] for k in range(4)], axis=0
    )
    out = mm_tn(mixed, low)[HD:]
    for ref, owner in ((keep_ref, core), (send_ref, 1 - core)):
        for tile in range(8):
            rows = grad_buf[pl.ds(pl.multiple_of((2 * tile + owner) * 48, 16), 48)]
            at = (tile // 4) * 96
            pieces = [
                out[at + row * 48:at + (row + 1) * 48, (tile % 4) * 192:(tile % 4 + 1) * 192] for row in range(2)
            ]
            ref[2 * tile] = rows[:, :384].astype(BF)
            ref[2 * tile + 1] = jnp.concatenate(
                [rows[:, 384:576], jnp.where(owner == 1, pieces[1], pieces[0])], axis=1
            ).astype(BF)

def normed_grad_kernel(
    gqkv_ref, tok_ref, w_ref, vec_ref, own_ref, one_ref, two_ref, three_ref, sums_ref,
    x_buf, part_buf, w_buf, x_sem, w_sem,
):
    load = pltpu.make_async_copy(tok_ref.at[lax.axis_index(MICRO)], x_buf, x_sem)
    load.start()
    loads = weight_copies(w_ref, w_buf, w_sem)
    group = group_index()
    odd = (group % 2) == 1
    load.wait()
    unit, _ = normalized(x_buf[...].astype(F32))
    total = jnp.zeros((TOK, D), F32)
    for slot in range(3):
        part = gqkv_ref[:, slot * 192:(slot + 1) * 192]
        zero = jnp.zeros_like(part)
        wide = jnp.where(
            odd, jnp.concatenate([zero, part], axis=1), jnp.concatenate([part, zero], axis=1)
        )
        loads[slot].wait()
        total = total + mm_nt(wide, w_buf[slot])
    part_buf[...] = total
    own_ref[...] = part_buf[pl.ds(pl.multiple_of(group * BLK, BLK), BLK)]
    for k, ref in ((1, one_ref), (2, two_ref), (3, three_ref)):
        ref[...] = part_buf[pl.ds(pl.multiple_of((group ^ k) * BLK, BLK), BLK)].astype(BF)
    gain1 = jnp.sum(total * unit, axis=0, keepdims=True)
    shift1 = jnp.sum(total, axis=0, keepdims=True)
    sums_ref[...] = jnp.concatenate([gain1, shift1, vec_ref[...][:2], jnp.zeros((4, D), F32)], axis=0)


def add_kernel(one_ref, two_ref, out_ref, buf, sem):
    buf[...] = (one_ref[...].astype(F32) + two_ref[...].astype(F32)).astype(BF)
    copy = pltpu.make_async_copy(buf, out_ref, sem)
    copy.start()
    copy.wait()


def sum_kernel(in_ref, vec_ref, out_ref, buf, sem):
    total = in_ref[0].astype(F32)
    for index in range(1, 16):
        total = total + in_ref[index].astype(F32)
    vectors = vec_ref[...][:4]
    block = jnp.concatenate([total, vectors[:, :384], vectors[:, 384:]], axis=0).astype(BF)
    for index in range(8):
        buf[index] = block
    wait_all(send_copies(buf, out_ref, range(8), sem))


def spread_kernel(turn, in_ref, *refs):
    qkv_buf, out_buf, sem, out_sem = refs[-4:]
    qkv_ref, out_ref, *vec_refs = refs[3:-4] if turn else refs[:-4]
    owner = lax.axis_index(CORE)
    owner = 1 - owner if turn else owner
    copies = []
    vectors = jnp.zeros((8, 384), F32)
    for tile in range(8):
        whole = [in_ref[tile, index].astype(F32) for index in range(8)]
        block = [value[:48] for value in whole]
        for value in whole:
            vectors = vectors + value[48:]
        for part, half, at in ((1, 0, 0), (2, 0, 192), (0, 4, 0)):
            qkv_buf[tile, :, part * D:(part + 1) * D] = jnp.concatenate(
                [block[half + group][:, at:at + 192] for group in range(4)], axis=1
            )
        start = pl.multiple_of((2 * tile + owner) * 48, 16)
        copy = pltpu.make_async_copy(qkv_buf.at[tile], qkv_ref.at[pl.ds(start, 48)], sem.at[tile])
        copy.start()
        copies.append(copy)
        for group in range(4):
            out_buf[group, tile // 4, :, (tile % 4) * 192:(tile % 4 + 1) * 192] = block[4 + group][:, 192:]
    for group in range(4):
        for pair in range(2):
            start = pl.multiple_of(group * 192 + (pair * 2 + owner) * 48, 16)
            copy = pltpu.make_async_copy(
                out_buf.at[group, pair], out_ref.at[pl.ds(start, 48)], out_sem.at[group, pair]
            )
            copy.start()
            copies.append(copy)
    if turn:
        vectors = vectors + refs[0][...]
        for k, ref in enumerate(vec_refs):
            ref[...] = jnp.concatenate([vectors[k:k + 1], vectors[4 + k:5 + k]], axis=1).reshape(D)
    else:
        vec_refs[0][...] = vectors
    wait_all(copies)


def spread_ff_kernel(in_ref, up_ref, down_ref):
    up_ref[...] = in_ref[:, :384].astype(F32)
    for tile in range(16):
        half = (tile % 2) * 384
        down_ref[(tile // 2) * 48:(tile // 2 + 1) * 48, half:half + 384] = in_ref[
            tile * 48:(tile + 1) * 48, 384:
        ].astype(F32)


def input_kernel(
    own_ref, one_ref, two_ref, three_ref, x_ref, gain_ref, grad_ref, result_ref, out_ref, buf, sem
):
    total = own_ref[...]
    for ref in (one_ref, two_ref, three_ref):
        total = total + ref[...].astype(F32)
    unit, inverse = normalized(x_ref[...].astype(F32))
    grad = grad_ref[...] + norm_back(total, unit, inverse, gain_ref[...].reshape(1, D))
    buf[:BLK] = grad.astype(BF)
    buf[BLK:] = result_ref[...]
    wait_all(send_copies(buf, out_ref, range(8), sem))


def unpack_kernel(in_ref, unused_ref, grad_ref, result_ref):
    for index in range(8):
        rows = slice(index % 4 * BLK, (index % 4 + 1) * BLK)
        grad_ref[index // 4, rows] = in_ref[index, :BLK].astype(F32)
        result_ref[index // 4, rows] = in_ref[index, BLK:]


def exchange(value, axes):
    return lax.all_to_all(value, axes, 0, 0, tiled=True)


def swap(value):
    return lax.ppermute(value, CORE, [(0, 1), (1, 0)])


def after(value, *others):
    return pl.pallas_call(
        lambda *refs: None,
        out_shape=jax.ShapeDtypeStruct(value.shape, value.dtype),
        in_specs=[pl.BlockSpec(memory_space=pl.ANY)] * (1 + len(others)),
        out_specs=pl.BlockSpec(memory_space=pl.ANY),
        input_output_aliases={0: 0},
        cost_estimate=pl.CostEstimate(flops=1, bytes_accessed=1, transcendentals=0),
        compiler_params=pltpu.CompilerParams(vmem_limit_bytes=2**20),
    )(value, *others)


def flip(value, axes, count, bits):
    return lax.ppermute(value, axes, [(index, index ^ bits) for index in range(count)])


def shards(
    tokens, scene_of_block, ln1_gain, ln1_shift, w_qkv, w_out, ln2_gain, ln2_shift, w_up, w_down, out_grad
):
    w_out_pad = jnp.pad(w_out.reshape(4, 192, D), ((0, 0), (HD, 0), (0, 0)))
    kv_send, query, normed = call(
        project_kernel,
        [((8, TOK, 384), BF, "H"), ((TOK, 256), BF, "L"), ((TOK, D), BF, "L")],
        [(tokens, "H"), (ln1_gain, "H"), (ln1_shift, "H"), (w_qkv, "H")],
        10**9,
        [
            pltpu.VMEM((TOK, D), BF), pltpu.VMEM((3, D, 384), BF), pltpu.VMEM((TOK, 384), BF),
            pltpu.VMEM((D,), F32), pltpu.VMEM((D,), F32), DMA, DMA((3,)), DMA((8,)), DMA, DMA,
        ],
    )
    kv_same = exchange(kv_send, CHIP)
    kv_other = swap(kv_same)
    (mixed_send,) = call(
        attend_kernel,
        [((8, TOK, 256), BF, "H")],
        [(scene_of_block, "S"), (query, "L"), (kv_same, "V"), (kv_other, "V")],
        2 * 10**9,
        [pltpu.VMEM((TOK, 256), BF), DMA((8,))],
    )
    mixed = exchange(mixed_send, NARROW)
    queries = lax.all_gather(after(pin(query), kv_same), WIDE, axis=0, tiled=True).reshape(8, 2, TOK, 256)
    ff_send, middle, normed2, act, grad_pre = call(
        forward_kernel,
        [
            ((8, 2 * BLK, D), BF, "H"), ((8, BLK, D), F32, "L"), ((2 * TOK, D), BF, "V"),
            ((2 * TOK, FFL), BF, "V"), ((2 * TOK, FFL), BF, "V"),
        ],
        [
            (mixed, "V"), (tokens, "H"), (out_grad, "H"), (w_out_pad, "V"), (ln2_gain, "L"), (ln2_shift, "L"),
            (w_up, "H"), (w_down, "H"),
        ],
        4 * 10**9,
        [
            pltpu.VMEM((2, TOK, D), BF), pltpu.VMEM((2, TOK, D), BF), pltpu.VMEM((D, FFL), BF),
            pltpu.VMEM((FFL, D), BF), pltpu.VMEM((8, BLK, D), BF), pltpu.VMEM((8, BLK, D), BF), DMA((4,)), DMA((2,)),
        ],
    )
    ff_sums = exchange(ff_send, NARROW)
    keep, send = call(
        ff_grads_kernel,
        [((8, 48, D), BF, "V")] * 2,
        [(normed2, "V"), (act, "V"), (grad_pre, "V"), (out_grad, "L")],
        2 * 10**9,
        [pltpu.VMEM((D, FFL), F32), pltpu.VMEM((FFL, D), F32)],
    )
    pieces = call(
        split_kernel, [((2, 48, D), BF, "L")] * 4, [(keep, "V"), (swap(send), "V")], 10**8
    )
    pieces = [pieces[0]] + [flip(pieces[k], "y", 4, k) for k in (1, 2, 3)]
    keep, send = call(
        halve_kernel,
        [((48, D), BF, "L")] * 2,
        [(pieces[0], "L")] + [(piece, "V") for piece in pieces[1:]],
        10**8,
    )
    ff_sums = after(ff_sums, pin(keep))
    grad_send, low, grad_mid, result_part, vec2, x_part = call(
        middle_kernel,
        [
            ((8, 4, BLK, 256), BF, "H"), ((BLK, D), BF, "L"), ((BLK, D), F32, "L"), ((BLK, D), BF, "L"),
            ((8, D), F32, "L"), ((BLK, D), BF, "L"),
        ],
        [
            (ff_sums, "V"), (middle, "H"), (out_grad, "H"), (tokens, "H"), (mixed, "H"), (w_out_pad, "V"),
            (ln2_gain, "L"),
        ],
        10**9,
        [
            pltpu.VMEM((4, BLK, 256), BF), pltpu.VMEM((BLK, D), F32), pltpu.VMEM((BLK, D), BF),
            pltpu.VMEM((4, BLK, 256), BF), DMA, DMA((3,)), DMA((8,)),
        ],
    )
    (ff_part,) = call(
        pair_kernel, [((48, D), BF, "L")], [(keep, "L"), (flip(send, "xl", 2, 1), "V")], 10**7
    )
    ff_all = lax.all_gather(ff_part, WIDE, axis=0, tiled=True)
    grad_same = exchange(grad_send.reshape(32, BLK, 256), (*CHIP, *GROUP)).reshape(8, TOK, 256)
    lows = [flip(low, GROUP, 4, k) for k in (1, 2, 3)]
    grad_same = after(grad_same, *lows, pin(ff_part))
    grad_other = swap(grad_same)
    gqkv, keep, send = call(
        attend_back_kernel,
        [((TOK, 640), BF, "L")] + [((16, 48, 384), BF, "V")] * 2,
        [
            (scene_of_block, "S"), (kv_same, "H"), (kv_other, "H"), (queries, "H"), (grad_same, "V"), (grad_other, "V"),
            (normed, "L"), (mixed, "H"), (low, "L"), *[(value, "V") for value in lows],
        ],
        8 * 10**9,
        [
            pltpu.VMEM((2, 5, TOK, 384), BF), pltpu.VMEM((2, 5, TOK, 256), BF), pltpu.VMEM((D, 640), F32),
            pltpu.VMEM((TOK, 256), BF), DMA((2,)), DMA((2,)), DMA,
        ],
        vmem=24,
    )
    (weight_send,) = call(
        add_kernel,
        [((16, 48, 384), BF, "H")],
        [(keep, "V"), (swap(send), "V")],
        10**8,
        [pltpu.VMEM((16, 48, 384), BF), DMA],
    )
    weight_parts = exchange(weight_send, (*CHIP, MICRO))
    own, *sends, sums = call(
        normed_grad_kernel,
        [((BLK, D), F32, "L")] + [((BLK, D), BF, "L")] * 3 + [((8, D), F32, "L")],
        [(gqkv, "L"), (tokens, "H"), (w_qkv, "H"), (vec2, "L")],
        10**9,
        [pltpu.VMEM((TOK, D), BF), pltpu.VMEM((TOK, D), F32), pltpu.VMEM((3, D, 384), BF), DMA, DMA((3,))],
    )
    parts = [flip(value, GROUP, 4, k + 1) for k, value in enumerate(sends)]
    weight_parts = after(weight_parts, pin(sums))
    (weight_total,) = call(
        sum_kernel,
        [((8, 8, 56, 384), BF, "H")],
        [(weight_parts, "V"), (sums, "L")],
        10**8,
        [pltpu.VMEM((8, 56, 384), BF), DMA((8,))],
    )
    (packed,) = call(
        input_kernel,
        [((8, 2 * BLK, D), BF, "H")],
        [
            (own, "L"), *[(value, "V") for value in parts], (x_part, "L"), (ln1_gain, "L"), (grad_mid, "L"),
            (result_part, "L"),
        ],
        10**8,
        [pltpu.VMEM((2 * BLK, D), BF), DMA((8,))],
    )
    up_grad, down_grad = call(
        spread_ff_kernel, [((D, FFL), F32, "L"), ((FFL, D), F32, "L")], [(ff_all, "L")], 10**7
    )
    weight_same = exchange(weight_total.reshape(64, 56, 384), (*CHIP, *NARROW)).reshape(8, 8, 56, 384)
    weight_same = after(weight_same, pin(packed), pin(up_grad), pin(down_grad))
    everyone = exchange(after(pin(packed), weight_same), NARROW)
    weight_other = swap(weight_same)
    scratch = [
        pltpu.VMEM((8, 48, 3 * D), F32), pltpu.VMEM((4, 2, 48, D), F32), DMA((8,)), DMA((4, 2)),
    ]
    grads = [((D, 3 * D), F32, "H"), ((D, D), F32, "H")]
    half = call(
        functools.partial(spread_kernel, False),
        grads + [((8, 384), F32, "V")],
        [(weight_same, "V")],
        10**8,
        scratch,
    )
    qkv_grad, out_proj_grad, *vectors = call(
        functools.partial(spread_kernel, True),
        grads + [((D,), F32, "L")] * 4,
        [(weight_other, "V"), (half[2], "V"), (half[0], "H"), (half[1], "H")],
        10**8,
        scratch,
        aliases={2: 0, 3: 1},
    )
    input_grad, result = call(
        unpack_kernel, [((2, TOK, D), F32, "L"), ((2, TOK, D), BF, "L")], [(everyone, "V"), (vectors[0], "H")], 10**8
    )
    return (
        result, input_grad, qkv_grad, out_proj_grad, *vectors, up_grad, down_grad
    )


def solution(mesh):
    names = ("y", "xl", "c", "zh", "zl", "xh")
    fine = Mesh(mesh.devices.reshape(4, 2, 2, 2, 2, 2), names)
    tokens = P(None, WIDE, None)
    placed = (
        tokens, P(), P(), P(), P(), P(), P(), P(), P(None, NARROW), P(NARROW, None), tokens
    )
    return jax.shard_map(
        shards,
        mesh=fine,
        in_specs=placed,
        out_specs=(
            tokens, tokens, P(), P(), P(), P(), P(), P(), P(None, NARROW), P(NARROW, None)
        ),
        check_vma=False,
    )
```

```python
import functools

import jax
import jax.numpy as jnp
from jax import lax
from jax.experimental import pallas as pl
from jax.experimental.pallas import tpu as pltpu
from jax.sharding import Mesh
from jax.sharding import PartitionSpec as P

D = 768
HD = 64
FFL = 384
TOK = 128
BLK = 32
EPS = 1e-05
BF = jnp.bfloat16
F32 = jnp.float32

CHIP = ("y", "xl")
CORE = "c"
MICRO = "zh"
GROUP = ("zl", "xh")
NARROW = (MICRO, *GROUP)
WIDE = (*CHIP, CORE)


def chip_index():
    return lax.axis_index("y") * 2 + lax.axis_index("xl")


def group_index():
    return lax.axis_index("zl") * 2 + lax.axis_index("xh")


def mm(left, right):
    return lax.dot_general(left, right, (((1,), (0,)), ((), ())), preferred_element_type=F32)


def mm_nt(left, right):
    return lax.dot_general(left, right, (((1,), (1,)), ((), ())), preferred_element_type=F32)


def mm_tn(left, right):
    return lax.dot_general(left, right, (((0,), (0,)), ((), ())), preferred_element_type=F32)


def normalized(values):
    center = values - jnp.mean(values, axis=-1, keepdims=True)
    spread = jnp.mean(center * center, axis=-1, keepdims=True)
    inverse = lax.rsqrt(spread + EPS)
    return center * inverse, inverse


def norm_back(grad, unit, inverse, gain):
    scaled = grad * gain
    first = jnp.mean(scaled, axis=-1, keepdims=True)
    second = jnp.mean(scaled * unit, axis=-1, keepdims=True)
    return inverse * (scaled - first - unit * second)


def halves(block):
    lane = lax.broadcasted_iota(jnp.int32, block.shape, 1)
    zero = jnp.zeros_like(block)
    return jnp.where(lane < HD, block, zero), jnp.where(lane < HD, zero, block)


def join(low, high):
    lane = lax.broadcasted_iota(jnp.int32, low.shape, 1)
    return jnp.where(lane < HD, low, high)


def span(scene_ref):
    micro = lax.axis_index(MICRO)
    own = scene_ref[micro, chip_index() * 4]
    first = jnp.int32(0)
    count = jnp.int32(0)
    for index in range(8):
        other = scene_ref[micro, index * 4]
        first += (other < own).astype(jnp.int32)
        count += (other == own).astype(jnp.int32)
    return first, count > 1


def three(value):
    a = value.astype(BF).astype(F32)
    b = (value - a).astype(BF).astype(F32)
    c = value - a - b
    return a, b, c


def put_columns(width, rows, start, columns):
    lane = lax.broadcasted_iota(jnp.int32, (rows, width), 1)
    out = jnp.zeros((rows, width), F32)
    for offset, column in enumerate(columns):
        out = jnp.where(lane == start + offset, column, out)
    return out


def pin(value):
    return pltpu.with_memory_space_constraint(value, pltpu.HBM)


def call(kernel, outs, ins, cost, scratch=(), vmem=16, aliases=None):
    places = {"V": pltpu.VMEM, "H": pltpu.HBM, "S": pltpu.SMEM, "L": pltpu.VMEM}
    return pl.pallas_call(
        kernel,
        out_shape=[
            (pltpu.HBM if place in "HL" else jax.ShapeDtypeStruct)(shape, dtype) for shape, dtype, place in outs
        ],
        in_specs=[pl.BlockSpec(memory_space=places[place]) for _, place in ins],
        out_specs=[pl.BlockSpec(memory_space=places[place]) for _, _, place in outs],
        scratch_shapes=list(scratch),
        input_output_aliases=aliases or {},
        cost_estimate=pl.CostEstimate(flops=1000, bytes_accessed=1000, transcendentals=0),
        compiler_params=pltpu.CompilerParams(vmem_limit_bytes=vmem * 2**20),
    )(*[pin(value) if place in "HL" else value for value, place in ins])


DMA = pltpu.SemaphoreType.DMA


def send_copies(source, target, indices, sem):
    copies = [pltpu.make_async_copy(source, target.at[index], sem.at[index]) for index in indices]
    for copy in copies:
        copy.start()
    return copies


def wait_all(copies):
    for copy in copies:
        copy.wait()


def weight_copies(w_ref, w_buf, w_sem, parts=(1, 2, 0)):
    group = group_index()
    copies = []
    for slot, part in enumerate(parts):
        column = pl.multiple_of(part * D + (group // 2) * 384, 128)
        copy = pltpu.make_async_copy(w_ref.at[:, pl.ds(column, 384)], w_buf.at[slot], w_sem.at[slot])
        copy.start()
        copies.append(copy)
    return copies


def own_heads(full):
    odd = (group_index() % 2) == 1
    return jnp.where(odd, full[:, 192:], full[:, :192]).astype(BF)


def project_kernel(
    tok_ref, gain_ref, shift_ref, w_ref, kv_ref, normed_ref,
    x_buf, w_buf, kv_buf, gain_buf, shift_buf, x_sem, w_sem, kv_sem, gain_sem, shift_sem,
):
    copy_x = pltpu.make_async_copy(tok_ref.at[lax.axis_index(MICRO)], x_buf, x_sem)
    copy_x.start()
    copy_gain = pltpu.make_async_copy(gain_ref, gain_buf, gain_sem)
    copy_gain.start()
    copy_shift = pltpu.make_async_copy(shift_ref, shift_buf, shift_sem)
    copy_shift.start()
    copies = weight_copies(w_ref, w_buf, w_sem, (1, 2))
    wait_all([copy_x, copy_gain, copy_shift])
    unit, _ = normalized(x_buf[...].astype(F32))
    normed = (unit * gain_buf[...].reshape(1, D) + shift_buf[...].reshape(1, D)).astype(BF)
    normed_ref[...] = normed
    parts = []
    for slot in range(2):
        copies[slot].wait()
        parts.append(own_heads(mm(normed, w_buf[slot])))
    kv_buf[...] = jnp.concatenate(parts, axis=1)
    wait_all(send_copies(kv_buf, kv_ref, range(8), kv_sem))


def query_kernel(normed_ref, w_ref, q_ref, w_buf, w_sem):
    weight_copies(w_ref, w_buf, w_sem, (0,))[0].wait()
    part = own_heads(mm(normed_ref[...], w_buf[0]))
    q_ref[...] = jnp.concatenate([part, jnp.zeros((TOK, HD), BF)], axis=1)


def attend_kernel(scene_ref, q_ref, same_ref, other_ref, out_ref, buf, sem):
    first, big = span(scene_ref)

    def run(count):
        rows = count * TOK
        keys = jnp.concatenate(
            [ref[pl.ds(first, count)].reshape(rows, 384) for ref in (same_ref, other_ref)], axis=0
        )
        query = q_ref[...]
        q0, q1 = halves(query[:, :128])
        blocks = [keys[:, :128], keys[:, 128:256], keys[:, 256:]]
        mixed = []
        columns = []
        for qh, kb, vb in ((q0, 0, 1), (q1, 0, 2), (query[:, 128:], 1, 2)):
            scores = mm_nt(qh, blocks[kb]) * (HD**-0.5)
            top = jnp.max(scores, axis=-1, keepdims=True)
            weights = jnp.exp(scores - top)
            total = jnp.sum(weights, axis=-1, keepdims=True)
            probs = (weights * (1.0 / total)).astype(BF)
            mixed.append(mm(probs, blocks[vb]))
            columns += three(top + jnp.log(total))
        stats = put_columns(128, TOK, 0, columns)
        buf[...] = jnp.concatenate([join(stats, mixed[0]), join(mixed[1], mixed[2])], axis=1).astype(BF)

    @pl.when(big)
    def _():
        run(5)

    @pl.when(jnp.logical_not(big))
    def _():
        run(1)

    wait_all(send_copies(buf, out_ref, range(8), sem))


def forward_kernel(
    mixed_ref, tok_ref, og_ref, wo_ref, gain_ref, shift_ref, up_ref, down_ref,
    out_ref, middle_ref, normed_ref, act_ref, gpre_ref,
    tok_buf, og_buf, up_buf, down_buf, grad_buf, branch_buf, middle_buf, in_sem, sem,
):
    loads = [
        pltpu.make_async_copy(ref, buf, in_sem.at[index])
        for index, (ref, buf) in enumerate(
            ((tok_ref, tok_buf), (up_ref, up_buf), (og_ref, og_buf), (down_ref, down_buf))
        )
    ]
    for load in loads:
        load.start()
    total = jnp.zeros((2 * TOK, D), F32)
    for group in range(4):
        rows = jnp.concatenate([mixed_ref[group], mixed_ref[4 + group]], axis=0)
        total = total + mm(rows, wo_ref[group])
    loads[0].wait()
    total = total + tok_buf[...].reshape(2 * TOK, D).astype(F32)
    middle_buf[...] = total.reshape(8, BLK, D)
    middle_ref[...] = middle_buf[lax.axis_index(MICRO) * 4 + group_index()]
    unit, _ = normalized(total)
    normed = (unit * gain_ref[...].reshape(1, D) + shift_ref[...].reshape(1, D)).astype(BF)
    normed_ref[...] = normed
    loads[1].wait()
    pre = mm(normed, up_buf[...])
    cdf = 0.5 * (1.0 + lax.erf(pre * (0.5**0.5)))
    slope = cdf + pre * jnp.exp(-0.5 * pre * pre) * 0.3989422804014327
    loads[2].wait()
    loads[3].wait()
    grad_out = og_buf[...].reshape(2 * TOK, D)
    gpre = (mm_nt(grad_out, down_buf[...]) * slope).astype(BF)
    gpre_ref[...] = gpre
    grad_buf[...] = mm_nt(gpre, up_buf[...]).astype(BF).reshape(8, BLK, D)
    first = pltpu.make_async_copy(grad_buf, out_ref.at[:, pl.ds(BLK, BLK)], sem.at[0])
    first.start()
    act = (pre * cdf).astype(BF)
    act_ref[...] = act
    branch_buf[...] = mm(act, down_buf[...]).astype(BF).reshape(8, BLK, D)
    second = pltpu.make_async_copy(branch_buf, out_ref.at[:, pl.ds(0, BLK)], sem.at[1])
    second.start()
    first.wait()
    second.wait()


def ff_grads_kernel(normed_ref, act_ref, gpre_ref, og_ref, keep_ref, send_ref, up_buf, down_buf):
    core = lax.axis_index(CORE)
    up_buf[...] = mm_tn(normed_ref[...], gpre_ref[...])
    down_buf[...] = mm_tn(act_ref[...], og_ref[...].reshape(2 * TOK, D))
    for ref, owner in ((keep_ref, core), (send_ref, 1 - core)):
        column = pl.multiple_of(owner * 384, 128)
        for tile in range(8):
            rows = pl.ds(pl.multiple_of((2 * tile + owner) * 48, 16), 48)
            ref[tile, :, :384] = up_buf[rows].astype(BF)
            ref[tile, :, 384:] = down_buf[tile * 48:(tile + 1) * 48, pl.ds(column, 384)].astype(BF)


def split_kernel(one_ref, two_ref, *refs):
    y = lax.axis_index("y")
    for k, ref in enumerate(refs):
        for xl in range(2):
            at = (y ^ k) * 2 + xl
            ref[xl] = (one_ref[at].astype(F32) + two_ref[at].astype(F32)).astype(BF)


def halve_kernel(*refs):
    parts, (keep_ref, send_ref) = refs[:4], refs[4:]
    xl = lax.axis_index("xl")
    for ref, at in ((keep_ref, xl), (send_ref, 1 - xl)):
        total = parts[0][at].astype(F32)
        for part in parts[1:]:
            total = total + part[at].astype(F32)
        ref[...] = total.astype(BF)


def pair_kernel(one_ref, two_ref, out_ref):
    out_ref[...] = (one_ref[...].astype(F32) + two_ref[...].astype(F32)).astype(BF)


def middle_kernel(
    sums_ref, middle_ref, og_ref, tok_ref, mixed_ref, wo_ref, gain_ref,
    out_ref, low_ref, grad_ref, result_ref, vec_ref, x_ref, buf, middle_buf, og_buf, mixed_buf, x_sem, in_sem, sem,
):
    micro = lax.axis_index(MICRO)
    group = group_index()
    block = pl.ds(pl.multiple_of(group * BLK, BLK), BLK)
    loads = [
        pltpu.make_async_copy(middle_ref, middle_buf, in_sem.at[0]),
        pltpu.make_async_copy(og_ref.at[micro, block], og_buf, in_sem.at[1]),
        pltpu.make_async_copy(mixed_ref.at[pl.ds(micro * 4, 4), block], mixed_buf, in_sem.at[2]),
        pltpu.make_async_copy(tok_ref.at[micro, block], x_ref, x_sem),
    ]
    for load in loads:
        load.start()
    total = sums_ref[0].astype(F32)
    for index in range(1, 8):
        total = total + sums_ref[index].astype(F32)
    branch, grad = total[:BLK], total[BLK:]
    wait_all(loads)
    middle = middle_buf[...]
    unit, inverse = normalized(middle)
    grad_mid = og_buf[...].astype(F32) + norm_back(grad, unit, inverse, gain_ref[...].reshape(1, D))
    low = grad_mid.astype(BF)
    lane = lax.broadcasted_iota(jnp.int32, (BLK, 256), 1)
    for head_group in range(4):
        mixed = mixed_buf[head_group].astype(F32)
        back = mm_nt(low, wo_ref[head_group]).astype(BF).astype(F32)
        product = mixed * back
        columns = []
        for head in range(3):
            inside = (lane >= (head + 1) * HD) & (lane < (head + 2) * HD)
            columns += three(jnp.sum(jnp.where(inside, product, 0.0), axis=-1, keepdims=True))
        stats = put_columns(256, BLK, 9, columns)
        buf[head_group] = jnp.where(lane < 9, mixed, jnp.where(lane < HD, stats, back)).astype(BF)
    sends = send_copies(buf, out_ref, range(8), sem)
    low_ref[...] = low
    grad_ref[...] = grad_mid
    result_ref[...] = (middle + branch).astype(BF)
    gain_grad = jnp.sum(grad * unit, axis=0, keepdims=True)
    shift_grad = jnp.sum(grad, axis=0, keepdims=True)
    vec_ref[...] = jnp.concatenate([gain_grad, shift_grad, jnp.zeros((6, D), F32)], axis=0)
    wait_all(sends)


def attend_back_kernel(
    scene_ref, kvs_ref, kvo_ref, q_ref, gs_ref, go_ref, normed_ref, mixed_ref, low0_ref, low1_ref, low2_ref, low3_ref,
    gqkv_ref, keep_ref, send_ref, kv_buf, q_buf, grad_buf, mixed_buf, kv_sem, q_sem, mixed_sem,
):
    first, big = span(scene_ref)
    chip = chip_index()
    core = lax.axis_index(CORE)
    group = group_index()
    scale = HD**-0.5

    def run(count):
        rows = count * TOK
        loads = [
            pltpu.make_async_copy(ref.at[pl.ds(first, count)], kv_buf.at[slot, pl.ds(0, count)], kv_sem.at[slot])
            for slot, ref in enumerate((kvs_ref, kvo_ref))
        ] + [
            pltpu.make_async_copy(
                q_ref.at[pl.ds(first, count), which], q_buf.at[slot, pl.ds(0, count)], q_sem.at[slot]
            )
            for slot, which in enumerate((core, 1 - core))
        ]
        for load in loads:
            load.start()

        def cut(value):
            return [value[:, at:at + 128] for at in range(0, value.shape[1], 128)]

        grad = cut(jnp.concatenate(
            [ref[pl.ds(first, count)].reshape(rows, 256) for ref in (gs_ref, go_ref)], axis=0
        ))
        g_own = cut(gs_ref[chip])
        g_heads = [halves(g_own[0])[1], *halves(g_own[1])]
        own_stats = g_own[0].astype(F32)
        all_stats = grad[0].astype(F32).T
        wait_all(loads)
        kv = cut(jnp.concatenate([kv_buf[slot, :count].reshape(rows, 384) for slot in range(2)], axis=0))
        query = cut(jnp.concatenate([q_buf[slot, :count].reshape(rows, 256) for slot in range(2)], axis=0))
        own = cut(kv_buf[0, chip - first]) + cut(q_buf[0, chip - first])
        q_heads = [*halves(own[3]), own[4]]
        k_heads = [*halves(own[0]), halves(own[1])[0]]
        v_heads = [halves(own[1])[1], *halves(own[2])]

        def column(at):
            return own_stats[:, at:at + 1] + own_stats[:, at + 1:at + 2] + own_stats[:, at + 2:at + 3]

        def row(at):
            return all_stats[at:at + 1] + all_stats[at + 1:at + 2] + all_stats[at + 2:at + 3]

        dq, dk, dv = [], [], []
        for head, (kb, vb) in enumerate(((0, 1), (0, 2), (1, 2))):
            qb, gb = (0, 0, 1)[head], (0, 1, 1)[head]
            probs = jnp.exp(mm_nt(q_heads[head], kv[kb]) * scale - column(3 * head))
            gap = mm_nt(g_heads[head], kv[vb]) - column(9 + 3 * head)
            dq.append(mm((probs * gap).astype(BF), kv[kb]) * scale)
            probs = jnp.exp(mm_nt(k_heads[head], query[qb]) * scale - row(3 * head))
            gap = mm_nt(v_heads[head], grad[gb]) - row(9 + 3 * head)
            dv.append(mm(probs.astype(BF), grad[gb]))
            dk.append(mm((probs * gap).astype(BF), query[qb]) * scale)
        tail = dq[2]
        gqkv_ref[...] = jnp.concatenate(
            [join(dk[0], dk[1]), join(dk[2], dv[0]), join(dv[1], dv[2]), join(dq[0], dq[1]),
             join(tail, jnp.zeros_like(tail))],
            axis=1,
        ).astype(BF)

    index = lax.axis_index(MICRO) * 4 + group
    load_mixed = pltpu.make_async_copy(mixed_ref.at[index], mixed_buf, mixed_sem)
    load_mixed.start()

    @pl.when(big)
    def _():
        run(5)

    @pl.when(jnp.logical_not(big))
    def _():
        run(1)

    grad_buf[...] = mm_tn(normed_ref[...], gqkv_ref[...])
    load_mixed.wait()
    low = jnp.concatenate([ref[...] for ref in (low0_ref, low1_ref, low2_ref, low3_ref)], axis=0)
    mixed = jnp.concatenate(
        [mixed_buf[pl.ds(pl.multiple_of((group ^ k) * BLK, BLK), BLK)] for k in range(4)], axis=0
    )
    out = mm_tn(mixed, low)[HD:]
    for ref, owner in ((keep_ref, core), (send_ref, 1 - core)):
        for tile in range(8):
            rows = grad_buf[pl.ds(pl.multiple_of((2 * tile + owner) * 48, 16), 48)]
            at = (tile // 4) * 96
            pieces = [
                out[at + row * 48:at + (row + 1) * 48, (tile % 4) * 192:(tile % 4 + 1) * 192] for row in range(2)
            ]
            ref[2 * tile] = rows[:, :384].astype(BF)
            ref[2 * tile + 1] = jnp.concatenate(
                [rows[:, 384:576], jnp.where(owner == 1, pieces[1], pieces[0])], axis=1
            ).astype(BF)

def normed_grad_kernel(
    gqkv_ref, tok_ref, w_ref, vec_ref, own_ref, one_ref, two_ref, three_ref, sums_ref,
    x_buf, part_buf, w_buf, x_sem, w_sem,
):
    load = pltpu.make_async_copy(tok_ref.at[lax.axis_index(MICRO)], x_buf, x_sem)
    load.start()
    loads = weight_copies(w_ref, w_buf, w_sem)
    group = group_index()
    odd = (group % 2) == 1
    load.wait()
    unit, _ = normalized(x_buf[...].astype(F32))
    total = jnp.zeros((TOK, D), F32)
    for slot in range(3):
        part = gqkv_ref[:, slot * 192:(slot + 1) * 192]
        zero = jnp.zeros_like(part)
        wide = jnp.where(
            odd, jnp.concatenate([zero, part], axis=1), jnp.concatenate([part, zero], axis=1)
        )
        loads[slot].wait()
        total = total + mm_nt(wide, w_buf[slot])
    part_buf[...] = total
    own_ref[...] = part_buf[pl.ds(pl.multiple_of(group * BLK, BLK), BLK)]
    for k, ref in ((1, one_ref), (2, two_ref), (3, three_ref)):
        ref[...] = part_buf[pl.ds(pl.multiple_of((group ^ k) * BLK, BLK), BLK)].astype(BF)
    gain1 = jnp.sum(total * unit, axis=0, keepdims=True)
    shift1 = jnp.sum(total, axis=0, keepdims=True)
    sums_ref[...] = jnp.concatenate([gain1, shift1, vec_ref[...][:2], jnp.zeros((4, D), F32)], axis=0)


def add_kernel(one_ref, two_ref, out_ref, buf, sem):
    buf[...] = (one_ref[...].astype(F32) + two_ref[...].astype(F32)).astype(BF)
    copy = pltpu.make_async_copy(buf, out_ref, sem)
    copy.start()
    copy.wait()


def sum_kernel(in_ref, vec_ref, out_ref, buf, sem):
    total = in_ref[0].astype(F32)
    for index in range(1, 16):
        total = total + in_ref[index].astype(F32)
    vectors = vec_ref[...][:4]
    block = jnp.concatenate([total, vectors[:, :384], vectors[:, 384:]], axis=0).astype(BF)
    for index in range(8):
        buf[index] = block
    wait_all(send_copies(buf, out_ref, range(8), sem))


def spread_kernel(turn, in_ref, *refs):
    qkv_buf, out_buf, sem, out_sem = refs[-4:]
    qkv_ref, out_ref, *vec_refs = refs[3:-4] if turn else refs[:-4]
    owner = lax.axis_index(CORE)
    owner = 1 - owner if turn else owner
    copies = []
    vectors = jnp.zeros((8, 384), F32)
    for tile in range(8):
        whole = [in_ref[tile, index].astype(F32) for index in range(8)]
        block = [value[:48] for value in whole]
        for value in whole:
            vectors = vectors + value[48:]
        for part, half, at in ((1, 0, 0), (2, 0, 192), (0, 4, 0)):
            qkv_buf[tile, :, part * D:(part + 1) * D] = jnp.concatenate(
                [block[half + group][:, at:at + 192] for group in range(4)], axis=1
            )
        start = pl.multiple_of((2 * tile + owner) * 48, 16)
        copy = pltpu.make_async_copy(qkv_buf.at[tile], qkv_ref.at[pl.ds(start, 48)], sem.at[tile])
        copy.start()
        copies.append(copy)
        for group in range(4):
            out_buf[group, tile // 4, :, (tile % 4) * 192:(tile % 4 + 1) * 192] = block[4 + group][:, 192:]
    for group in range(4):
        for pair in range(2):
            start = pl.multiple_of(group * 192 + (pair * 2 + owner) * 48, 16)
            copy = pltpu.make_async_copy(
                out_buf.at[group, pair], out_ref.at[pl.ds(start, 48)], out_sem.at[group, pair]
            )
            copy.start()
            copies.append(copy)
    if turn:
        vectors = vectors + refs[0][...]
        for k, ref in enumerate(vec_refs):
            ref[...] = jnp.concatenate([vectors[k:k + 1], vectors[4 + k:5 + k]], axis=1).reshape(D)
    else:
        vec_refs[0][...] = vectors
    wait_all(copies)


def spread_ff_kernel(in_ref, up_ref, down_ref):
    up_ref[...] = in_ref[:, :384].astype(F32)
    for tile in range(16):
        half = (tile % 2) * 384
        down_ref[(tile // 2) * 48:(tile // 2 + 1) * 48, half:half + 384] = in_ref[
            tile * 48:(tile + 1) * 48, 384:
        ].astype(F32)


def input_kernel(
    own_ref, one_ref, two_ref, three_ref, x_ref, gain_ref, grad_ref, result_ref, out_ref, buf, sem
):
    total = own_ref[...]
    for ref in (one_ref, two_ref, three_ref):
        total = total + ref[...].astype(F32)
    unit, inverse = normalized(x_ref[...].astype(F32))
    grad = grad_ref[...] + norm_back(total, unit, inverse, gain_ref[...].reshape(1, D))
    buf[:BLK] = grad.astype(BF)
    buf[BLK:] = result_ref[...]
    wait_all(send_copies(buf, out_ref, range(8), sem))


def unpack_kernel(in_ref, unused_ref, grad_ref, result_ref):
    for index in range(8):
        rows = slice(index % 4 * BLK, (index % 4 + 1) * BLK)
        grad_ref[index // 4, rows] = in_ref[index, :BLK].astype(F32)
        result_ref[index // 4, rows] = in_ref[index, BLK:]


def exchange(value, axes):
    return lax.all_to_all(value, axes, 0, 0, tiled=True)


def swap(value):
    return lax.ppermute(value, CORE, [(0, 1), (1, 0)])


def after(value, *others):
    return pl.pallas_call(
        lambda *refs: None,
        out_shape=jax.ShapeDtypeStruct(value.shape, value.dtype),
        in_specs=[pl.BlockSpec(memory_space=pl.ANY)] * (1 + len(others)),
        out_specs=pl.BlockSpec(memory_space=pl.ANY),
        input_output_aliases={0: 0},
        cost_estimate=pl.CostEstimate(flops=1, bytes_accessed=1, transcendentals=0),
        compiler_params=pltpu.CompilerParams(vmem_limit_bytes=2**20),
    )(value, *others)


def flip(value, axes, count, bits):
    return lax.ppermute(value, axes, [(index, index ^ bits) for index in range(count)])


def shards(
    tokens, scene_of_block, ln1_gain, ln1_shift, w_qkv, w_out, ln2_gain, ln2_shift, w_up, w_down, out_grad
):
    w_out_pad = jnp.pad(w_out.reshape(4, 192, D), ((0, 0), (HD, 0), (0, 0)))
    kv_send, normed = call(
        project_kernel,
        [((8, TOK, 384), BF, "H"), ((TOK, D), BF, "L")],
        [(tokens, "H"), (ln1_gain, "H"), (ln1_shift, "H"), (w_qkv, "H")],
        10**9,
        [
            pltpu.VMEM((TOK, D), BF), pltpu.VMEM((2, D, 384), BF), pltpu.VMEM((TOK, 384), BF),
            pltpu.VMEM((D,), F32), pltpu.VMEM((D,), F32), DMA, DMA((2,)), DMA((8,)), DMA, DMA,
        ],
    )
    (query,) = call(
        query_kernel,
        [((TOK, 256), BF, "L")],
        [(normed, "L"), (w_qkv, "H")],
        10**8,
        [pltpu.VMEM((1, D, 384), BF), DMA((1,))],
    )
    kv_same = exchange(kv_send, CHIP)
    kv_same = after(kv_same, pin(query))
    kv_other = swap(kv_same)
    (mixed_send,) = call(
        attend_kernel,
        [((8, TOK, 256), BF, "H")],
        [(scene_of_block, "S"), (query, "L"), (kv_same, "V"), (kv_other, "V")],
        2 * 10**9,
        [pltpu.VMEM((TOK, 256), BF), DMA((8,))],
    )
    mixed = exchange(mixed_send, NARROW)
    queries = lax.all_gather(after(pin(query), kv_same), WIDE, axis=0, tiled=True).reshape(8, 2, TOK, 256)
    ff_send, middle, normed2, act, grad_pre = call(
        forward_kernel,
        [
            ((8, 2 * BLK, D), BF, "H"), ((BLK, D), F32, "L"), ((2 * TOK, D), BF, "V"),
            ((2 * TOK, FFL), BF, "V"), ((2 * TOK, FFL), BF, "V"),
        ],
        [
            (mixed, "V"), (tokens, "H"), (out_grad, "H"), (w_out_pad, "V"), (ln2_gain, "L"), (ln2_shift, "L"),
            (w_up, "H"), (w_down, "H"),
        ],
        4 * 10**9,
        [
            pltpu.VMEM((2, TOK, D), BF), pltpu.VMEM((2, TOK, D), BF), pltpu.VMEM((D, FFL), BF),
            pltpu.VMEM((FFL, D), BF), pltpu.VMEM((8, BLK, D), BF), pltpu.VMEM((8, BLK, D), BF),
            pltpu.VMEM((8, BLK, D), F32), DMA((4,)), DMA((2,)),
        ],
    )
    ff_sums = exchange(ff_send, NARROW)
    keep, send = call(
        ff_grads_kernel,
        [((8, 48, D), BF, "V")] * 2,
        [(normed2, "V"), (act, "V"), (grad_pre, "V"), (out_grad, "L")],
        2 * 10**9,
        [pltpu.VMEM((D, FFL), F32), pltpu.VMEM((FFL, D), F32)],
    )
    pieces = call(
        split_kernel, [((2, 48, D), BF, "L")] * 4, [(keep, "V"), (swap(send), "V")], 10**8
    )
    pieces = [pieces[0]] + [flip(pieces[k], "y", 4, k) for k in (1, 2, 3)]
    keep, send = call(
        halve_kernel,
        [((48, D), BF, "L")] * 2,
        [(pieces[0], "L")] + [(piece, "V") for piece in pieces[1:]],
        10**8,
    )
    ff_sums = after(ff_sums, pin(keep))
    grad_send, low, grad_mid, result_part, vec2, x_part = call(
        middle_kernel,
        [
            ((8, 4, BLK, 256), BF, "H"), ((BLK, D), BF, "L"), ((BLK, D), F32, "L"), ((BLK, D), BF, "L"),
            ((8, D), F32, "L"), ((BLK, D), BF, "L"),
        ],
        [
            (ff_sums, "V"), (middle, "H"), (out_grad, "H"), (tokens, "H"), (mixed, "H"), (w_out_pad, "V"),
            (ln2_gain, "L"),
        ],
        10**9,
        [
            pltpu.VMEM((4, BLK, 256), BF), pltpu.VMEM((BLK, D), F32), pltpu.VMEM((BLK, D), BF),
            pltpu.VMEM((4, BLK, 256), BF), DMA, DMA((3,)), DMA((8,)),
        ],
    )
    send = after(pin(send), pin(low))
    (ff_part,) = call(
        pair_kernel, [((48, D), BF, "L")], [(keep, "L"), (flip(send, "xl", 2, 1), "V")], 10**7
    )
    ff_all = lax.all_gather(ff_part, WIDE, axis=0, tiled=True)
    grad_same = exchange(grad_send.reshape(32, BLK, 256), (*CHIP, *GROUP)).reshape(8, TOK, 256)
    lows = [flip(low, GROUP, 4, k) for k in (1, 2, 3)]
    grad_same = after(grad_same, *lows, pin(ff_part))
    grad_other = swap(grad_same)
    gqkv, keep, send = call(
        attend_back_kernel,
        [((TOK, 640), BF, "L")] + [((16, 48, 384), BF, "V")] * 2,
        [
            (scene_of_block, "S"), (kv_same, "H"), (kv_other, "H"), (queries, "H"), (grad_same, "V"), (grad_other, "V"),
            (normed, "L"), (mixed, "H"), (low, "L"), *[(value, "V") for value in lows],
        ],
        8 * 10**9,
        [
            pltpu.VMEM((2, 5, TOK, 384), BF), pltpu.VMEM((2, 5, TOK, 256), BF), pltpu.VMEM((D, 640), F32),
            pltpu.VMEM((TOK, 256), BF), DMA((2,)), DMA((2,)), DMA,
        ],
        vmem=24,
    )
    (weight_send,) = call(
        add_kernel,
        [((16, 48, 384), BF, "H")],
        [(keep, "V"), (swap(send), "V")],
        10**8,
        [pltpu.VMEM((16, 48, 384), BF), DMA],
    )
    weight_parts = exchange(weight_send, (*CHIP, MICRO))
    own, *sends, sums = call(
        normed_grad_kernel,
        [((BLK, D), F32, "L")] + [((BLK, D), BF, "L")] * 3 + [((8, D), F32, "L")],
        [(gqkv, "L"), (tokens, "H"), (w_qkv, "H"), (vec2, "L")],
        10**9,
        [pltpu.VMEM((TOK, D), BF), pltpu.VMEM((TOK, D), F32), pltpu.VMEM((3, D, 384), BF), DMA, DMA((3,))],
    )
    parts = [flip(value, GROUP, 4, k + 1) for k, value in enumerate(sends)]
    weight_parts = after(weight_parts, pin(sums), *parts, pin(ff_all))
    (weight_total,) = call(
        sum_kernel,
        [((8, 8, 56, 384), BF, "H")],
        [(weight_parts, "V"), (sums, "L")],
        10**8,
        [pltpu.VMEM((8, 56, 384), BF), DMA((8,))],
    )
    (packed,) = call(
        input_kernel,
        [((8, 2 * BLK, D), BF, "H")],
        [
            (own, "L"), *[(value, "V") for value in parts], (x_part, "L"), (ln1_gain, "L"), (grad_mid, "L"),
            (result_part, "L"),
        ],
        10**8,
        [pltpu.VMEM((2 * BLK, D), BF), DMA((8,))],
    )
    up_grad, down_grad = call(
        spread_ff_kernel, [((D, FFL), F32, "L"), ((FFL, D), F32, "L")], [(ff_all, "L")], 10**7
    )
    weight_same = exchange(weight_total.reshape(64, 56, 384), (*CHIP, *NARROW)).reshape(8, 8, 56, 384)
    weight_same = after(weight_same, pin(packed), pin(up_grad), pin(down_grad))
    everyone = exchange(after(pin(packed), weight_same), NARROW)
    weight_other = swap(weight_same)
    scratch = [
        pltpu.VMEM((8, 48, 3 * D), F32), pltpu.VMEM((4, 2, 48, D), F32), DMA((8,)), DMA((4, 2)),
    ]
    grads = [((D, 3 * D), F32, "H"), ((D, D), F32, "H")]
    half = call(
        functools.partial(spread_kernel, False),
        grads + [((8, 384), F32, "V")],
        [(weight_same, "V")],
        10**8,
        scratch,
    )
    qkv_grad, out_proj_grad, *vectors = call(
        functools.partial(spread_kernel, True),
        grads + [((D,), F32, "L")] * 4,
        [(weight_other, "V"), (half[2], "V"), (half[0], "H"), (half[1], "H")],
        10**8,
        scratch,
        aliases={2: 0, 3: 1},
    )
    input_grad, result = call(
        unpack_kernel, [((2, TOK, D), F32, "L"), ((2, TOK, D), BF, "L")], [(everyone, "V"), (vectors[0], "H")], 10**8
    )
    return (
        result, input_grad, qkv_grad, out_proj_grad, *vectors, up_grad, down_grad
    )


def solution(mesh):
    names = ("y", "xl", "c", "zh", "zl", "xh")
    fine = Mesh(mesh.devices.reshape(4, 2, 2, 2, 2, 2), names)
    tokens = P(None, WIDE, None)
    placed = (
        tokens, P(), P(), P(), P(), P(), P(), P(), P(None, NARROW), P(NARROW, None), tokens
    )
    return jax.shard_map(
        shards,
        mesh=fine,
        in_specs=placed,
        out_specs=(
            tokens, tokens, P(), P(), P(), P(), P(), P(), P(None, NARROW), P(NARROW, None)
        ),
        check_vma=False,
    )
```

```python
import functools

import jax
import jax.numpy as jnp
from jax import lax
from jax.experimental import pallas as pl
from jax.experimental.pallas import tpu as pltpu
from jax.sharding import Mesh
from jax.sharding import PartitionSpec as P

D = 768
HD = 64
FFL = 384
TOK = 128
BLK = 32
EPS = 1e-05
BF = jnp.bfloat16
F32 = jnp.float32

CHIP = ("y", "xl")
CORE = "c"
MICRO = "zh"
GROUP = ("zl", "xh")
NARROW = (MICRO, *GROUP)
WIDE = (*CHIP, CORE)


def chip_index():
    return lax.axis_index("y") * 2 + lax.axis_index("xl")


def group_index():
    return lax.axis_index("zl") * 2 + lax.axis_index("xh")


def mm(left, right):
    return lax.dot_general(left, right, (((1,), (0,)), ((), ())), preferred_element_type=F32)


def mm_nt(left, right):
    return lax.dot_general(left, right, (((1,), (1,)), ((), ())), preferred_element_type=F32)


def mm_tn(left, right):
    return lax.dot_general(left, right, (((0,), (0,)), ((), ())), preferred_element_type=F32)


def normalized(values):
    center = values - jnp.mean(values, axis=-1, keepdims=True)
    spread = jnp.mean(center * center, axis=-1, keepdims=True)
    inverse = lax.rsqrt(spread + EPS)
    return center * inverse, inverse


def norm_back(grad, unit, inverse, gain):
    scaled = grad * gain
    first = jnp.mean(scaled, axis=-1, keepdims=True)
    second = jnp.mean(scaled * unit, axis=-1, keepdims=True)
    return inverse * (scaled - first - unit * second)


def halves(block):
    lane = lax.broadcasted_iota(jnp.int32, block.shape, 1)
    zero = jnp.zeros_like(block)
    return jnp.where(lane < HD, block, zero), jnp.where(lane < HD, zero, block)


def join(low, high):
    lane = lax.broadcasted_iota(jnp.int32, low.shape, 1)
    return jnp.where(lane < HD, low, high)


def span(scene_ref):
    micro = lax.axis_index(MICRO)
    own = scene_ref[micro, chip_index() * 4]
    first = jnp.int32(0)
    count = jnp.int32(0)
    for index in range(8):
        other = scene_ref[micro, index * 4]
        first += (other < own).astype(jnp.int32)
        count += (other == own).astype(jnp.int32)
    return first, count > 1


def three(value):
    a = value.astype(BF).astype(F32)
    b = (value - a).astype(BF).astype(F32)
    c = value - a - b
    return a, b, c


def put_columns(width, rows, start, columns):
    lane = lax.broadcasted_iota(jnp.int32, (rows, width), 1)
    out = jnp.zeros((rows, width), F32)
    for offset, column in enumerate(columns):
        out = jnp.where(lane == start + offset, column, out)
    return out


def pin(value):
    return pltpu.with_memory_space_constraint(value, pltpu.HBM)


def call(kernel, outs, ins, cost, scratch=(), vmem=16, aliases=None):
    places = {"V": pltpu.VMEM, "H": pltpu.HBM, "S": pltpu.SMEM, "L": pltpu.VMEM}
    return pl.pallas_call(
        kernel,
        out_shape=[
            (pltpu.HBM if place in "HL" else jax.ShapeDtypeStruct)(shape, dtype) for shape, dtype, place in outs
        ],
        in_specs=[pl.BlockSpec(memory_space=places[place]) for _, place in ins],
        out_specs=[pl.BlockSpec(memory_space=places[place]) for _, _, place in outs],
        scratch_shapes=list(scratch),
        input_output_aliases=aliases or {},
        cost_estimate=pl.CostEstimate(flops=cost, bytes_accessed=1000, transcendentals=0),
        compiler_params=pltpu.CompilerParams(vmem_limit_bytes=vmem * 2**20),
    )(*[pin(value) if place in "HL" else value for value, place in ins])


DMA = pltpu.SemaphoreType.DMA


def send_copies(source, target, indices, sem):
    copies = [pltpu.make_async_copy(source, target.at[index], sem.at[index]) for index in indices]
    for copy in copies:
        copy.start()
    return copies


def wait_all(copies):
    for copy in copies:
        copy.wait()


def weight_copies(w_ref, w_buf, w_sem, parts=(1, 2, 0)):
    group = group_index()
    copies = []
    for slot, part in enumerate(parts):
        column = pl.multiple_of(part * D + (group // 2) * 384, 128)
        copy = pltpu.make_async_copy(w_ref.at[:, pl.ds(column, 384)], w_buf.at[slot], w_sem.at[slot])
        copy.start()
        copies.append(copy)
    return copies


def own_heads(full):
    odd = (group_index() % 2) == 1
    return jnp.where(odd, full[:, 192:], full[:, :192]).astype(BF)


def project_kernel(
    tok_ref, gain_ref, shift_ref, w_ref, kv_ref, normed_ref,
    x_buf, w_buf, kv_buf, gain_buf, shift_buf, x_sem, w_sem, kv_sem, gain_sem, shift_sem,
):
    copy_x = pltpu.make_async_copy(tok_ref.at[lax.axis_index(MICRO)], x_buf, x_sem)
    copy_x.start()
    copy_gain = pltpu.make_async_copy(gain_ref, gain_buf, gain_sem)
    copy_gain.start()
    copy_shift = pltpu.make_async_copy(shift_ref, shift_buf, shift_sem)
    copy_shift.start()
    copies = weight_copies(w_ref, w_buf, w_sem, (1, 2))
    wait_all([copy_x, copy_gain, copy_shift])
    unit, _ = normalized(x_buf[...].astype(F32))
    normed = (unit * gain_buf[...].reshape(1, D) + shift_buf[...].reshape(1, D)).astype(BF)
    normed_ref[...] = normed
    parts = []
    for slot in range(2):
        copies[slot].wait()
        parts.append(own_heads(mm(normed, w_buf[slot])))
    kv_buf[...] = jnp.concatenate(parts, axis=1)
    wait_all(send_copies(kv_buf, kv_ref, range(8), kv_sem))


def query_kernel(normed_ref, w_ref, q_ref, w_buf, w_sem):
    weight_copies(w_ref, w_buf, w_sem, (0,))[0].wait()
    part = own_heads(mm(normed_ref[...], w_buf[0]))
    q_ref[...] = jnp.concatenate([part, jnp.zeros((TOK, HD), BF)], axis=1)


def attend_kernel(scene_ref, q_ref, same_ref, other_ref, out_ref, buf, q_buf, sem, q_sem):
    load = pltpu.make_async_copy(q_ref, q_buf, q_sem)
    load.start()
    first, big = span(scene_ref)

    def run(count):
        rows = count * TOK
        keys = jnp.concatenate(
            [ref[pl.ds(first, count)].reshape(rows, 384) for ref in (same_ref, other_ref)], axis=0
        )
        load.wait()
        query = q_buf[...]
        q0, q1 = halves(query[:, :128])
        blocks = [keys[:, :128], keys[:, 128:256], keys[:, 256:]]
        mixed = []
        columns = []
        for qh, kb, vb in ((q0, 0, 1), (q1, 0, 2), (query[:, 128:], 1, 2)):
            scores = mm_nt(qh, blocks[kb]) * (HD**-0.5)
            top = jnp.max(scores, axis=-1, keepdims=True)
            weights = jnp.exp(scores - top)
            total = jnp.sum(weights, axis=-1, keepdims=True)
            probs = (weights * (1.0 / total)).astype(BF)
            mixed.append(mm(probs, blocks[vb]))
            columns += three(top + jnp.log(total))
        stats = put_columns(128, TOK, 0, columns)
        buf[...] = jnp.concatenate([join(stats, mixed[0]), join(mixed[1], mixed[2])], axis=1).astype(BF)

    @pl.when(big)
    def _():
        run(5)

    @pl.when(jnp.logical_not(big))
    def _():
        run(1)

    wait_all(send_copies(buf, out_ref, range(8), sem))


def forward_kernel(
    mixed_ref, tok_ref, og_ref, wo_ref, gain_ref, shift_ref, up_ref, down_ref,
    out_ref, middle_ref, normed_ref, act_ref, gpre_ref,
    tok_buf, og_buf, up_buf, down_buf, gain_buf, shift_buf, grad_buf, branch_buf, middle_buf, in_sem, sem,
):
    loads = [
        pltpu.make_async_copy(ref, buf, in_sem.at[index])
        for index, (ref, buf) in enumerate(
            (
                (tok_ref, tok_buf), (up_ref, up_buf), (og_ref, og_buf), (down_ref, down_buf), (gain_ref, gain_buf),
                (shift_ref, shift_buf),
            )
        )
    ]
    for load in loads:
        load.start()
    total = jnp.zeros((2 * TOK, D), F32)
    for group in range(4):
        rows = jnp.concatenate([mixed_ref[group], mixed_ref[4 + group]], axis=0)
        total = total + mm(rows, wo_ref[group])
    loads[0].wait()
    total = total + tok_buf[...].reshape(2 * TOK, D).astype(F32)
    middle_buf[...] = total.reshape(8, BLK, D)
    third = pltpu.make_async_copy(
        middle_buf.at[lax.axis_index(MICRO) * 4 + group_index()], middle_ref, sem.at[2]
    )
    third.start()
    unit, _ = normalized(total)
    wait_all(loads[4:])
    normed = (unit * gain_buf[...].reshape(1, D) + shift_buf[...].reshape(1, D)).astype(BF)
    normed_ref[...] = normed
    loads[1].wait()
    pre = mm(normed, up_buf[...])
    cdf = 0.5 * (1.0 + lax.erf(pre * (0.5**0.5)))
    slope = cdf + pre * jnp.exp(-0.5 * pre * pre) * 0.3989422804014327
    loads[2].wait()
    loads[3].wait()
    grad_out = og_buf[...].reshape(2 * TOK, D)
    gpre = (mm_nt(grad_out, down_buf[...]) * slope).astype(BF)
    gpre_ref[...] = gpre
    grad_buf[...] = mm_nt(gpre, up_buf[...]).astype(BF).reshape(8, BLK, D)
    first = pltpu.make_async_copy(grad_buf, out_ref.at[:, pl.ds(BLK, BLK)], sem.at[0])
    first.start()
    act = (pre * cdf).astype(BF)
    act_ref[...] = act
    branch_buf[...] = mm(act, down_buf[...]).astype(BF).reshape(8, BLK, D)
    second = pltpu.make_async_copy(branch_buf, out_ref.at[:, pl.ds(0, BLK)], sem.at[1])
    second.start()
    wait_all([first, second, third])


def ff_grads_kernel(normed_ref, act_ref, gpre_ref, og_ref, keep_ref, send_ref, up_buf, down_buf):
    core = lax.axis_index(CORE)
    up_buf[...] = mm_tn(normed_ref[...], gpre_ref[...])
    down_buf[...] = mm_tn(act_ref[...], og_ref[...].reshape(2 * TOK, D))
    for ref, owner in ((keep_ref, core), (send_ref, 1 - core)):
        column = pl.multiple_of(owner * 384, 128)
        for tile in range(8):
            rows = pl.ds(pl.multiple_of((2 * tile + owner) * 48, 16), 48)
            ref[tile, :, :384] = up_buf[rows].astype(BF)
            ref[tile, :, 384:] = down_buf[tile * 48:(tile + 1) * 48, pl.ds(column, 384)].astype(BF)


def split_kernel(one_ref, two_ref, *refs):
    y = lax.axis_index("y")
    for k, ref in enumerate(refs):
        for xl in range(2):
            at = (y ^ k) * 2 + xl
            ref[xl] = (one_ref[at].astype(F32) + two_ref[at].astype(F32)).astype(BF)


def halve_kernel(*refs):
    parts, (keep_ref, send_ref) = refs[:4], refs[4:]
    xl = lax.axis_index("xl")
    for ref, at in ((keep_ref, xl), (send_ref, 1 - xl)):
        total = parts[0][at].astype(F32)
        for part in parts[1:]:
            total = total + part[at].astype(F32)
        ref[...] = total.astype(BF)


def pair_kernel(one_ref, two_ref, out_ref):
    out_ref[...] = (one_ref[...].astype(F32) + two_ref[...].astype(F32)).astype(BF)


def middle_kernel(
    sums_ref, middle_ref, og_ref, mixed_ref, wo_ref, gain_ref,
    out_ref, low_ref, grad_ref, result_ref, vec_ref,
    buf, middle_buf, og_buf, mixed_buf, gain_buf, low_buf, grad_buf, result_buf, vec_buf, in_sem, sem, rest_sem,
):
    micro = lax.axis_index(MICRO)
    group = group_index()
    block = pl.ds(pl.multiple_of(group * BLK, BLK), BLK)
    loads = [
        pltpu.make_async_copy(middle_ref, middle_buf, in_sem.at[0]),
        pltpu.make_async_copy(og_ref.at[micro, block], og_buf, in_sem.at[1]),
        pltpu.make_async_copy(mixed_ref.at[pl.ds(micro * 4, 4), block], mixed_buf, in_sem.at[2]),
        pltpu.make_async_copy(gain_ref, gain_buf, in_sem.at[3]),
    ]
    for load in loads:
        load.start()
    total = sums_ref[0].astype(F32)
    for index in range(1, 8):
        total = total + sums_ref[index].astype(F32)
    branch, grad = total[:BLK], total[BLK:]
    wait_all(loads)
    middle = middle_buf[...]
    unit, inverse = normalized(middle)
    grad_mid = og_buf[...].astype(F32) + norm_back(grad, unit, inverse, gain_buf[...].reshape(1, D))
    low = grad_mid.astype(BF)
    low_buf[...] = low
    grad_buf[...] = grad_mid
    result_buf[...] = (middle + branch).astype(BF)
    gain_grad = jnp.sum(grad * unit, axis=0, keepdims=True)
    shift_grad = jnp.sum(grad, axis=0, keepdims=True)
    vec_buf[...] = jnp.concatenate([gain_grad, shift_grad, jnp.zeros((6, D), F32)], axis=0)
    stores = [
        pltpu.make_async_copy(source, target, rest_sem.at[index])
        for index, (source, target) in enumerate(
            ((low_buf, low_ref), (grad_buf, grad_ref), (result_buf, result_ref), (vec_buf, vec_ref))
        )
    ]
    for store in stores:
        store.start()
    lane = lax.broadcasted_iota(jnp.int32, (BLK, 256), 1)
    for head_group in range(4):
        mixed = mixed_buf[head_group].astype(F32)
        back = mm_nt(low, wo_ref[head_group]).astype(BF).astype(F32)
        product = mixed * back
        columns = []
        for head in range(3):
            inside = (lane >= (head + 1) * HD) & (lane < (head + 2) * HD)
            columns += three(jnp.sum(jnp.where(inside, product, 0.0), axis=-1, keepdims=True))
        stats = put_columns(256, BLK, 9, columns)
        buf[head_group] = jnp.where(lane < 9, mixed, jnp.where(lane < HD, stats, back)).astype(BF)
    sends = send_copies(buf, out_ref, range(8), sem)
    wait_all(stores)
    wait_all(sends)


def attend_back_kernel(
    scene_ref, kvs_ref, kvo_ref, q_ref, gs_ref, go_ref, normed_ref, mixed_ref, low_ref, low1_ref, low2_ref, low3_ref,
    gqkv_ref, keep_ref, send_ref,
    kv_buf, q_buf, gqkv_buf, grad_buf, mixed_buf, normed_buf, low_buf, kv_sem, q_sem, in_sem, out_sem,
):
    first, big = span(scene_ref)
    chip = chip_index()
    core = lax.axis_index(CORE)
    group = group_index()
    index = lax.axis_index(MICRO) * 4 + group
    first_loads = [
        pltpu.make_async_copy(source, target, in_sem.at[slot])
        for slot, (source, target) in enumerate(
            ((normed_ref, normed_buf), (mixed_ref.at[index], mixed_buf), (low_ref, low_buf))
        )
    ]
    scale = HD**-0.5

    def run(count):
        rows = count * TOK
        loads = [
            pltpu.make_async_copy(ref.at[pl.ds(first, count)], kv_buf.at[slot, pl.ds(0, count)], kv_sem.at[slot])
            for slot, ref in enumerate((kvs_ref, kvo_ref))
        ] + [
            pltpu.make_async_copy(
                q_ref.at[pl.ds(first, count), which], q_buf.at[slot, pl.ds(0, count)], q_sem.at[slot]
            )
            for slot, which in enumerate((core, 1 - core))
        ]
        for load in loads + first_loads:
            load.start()

        def cut(value):
            return [value[:, at:at + 128] for at in range(0, value.shape[1], 128)]

        grad = cut(jnp.concatenate(
            [ref[pl.ds(first, count)].reshape(rows, 256) for ref in (gs_ref, go_ref)], axis=0
        ))
        g_own = cut(gs_ref[chip])
        g_heads = [halves(g_own[0])[1], *halves(g_own[1])]
        own_stats = g_own[0].astype(F32)
        all_stats = grad[0].astype(F32).T
        wait_all(loads)
        kv = cut(jnp.concatenate([kv_buf[slot, :count].reshape(rows, 384) for slot in range(2)], axis=0))
        query = cut(jnp.concatenate([q_buf[slot, :count].reshape(rows, 256) for slot in range(2)], axis=0))
        own = cut(kv_buf[0, chip - first]) + cut(q_buf[0, chip - first])
        q_heads = [*halves(own[3]), own[4]]
        k_heads = [*halves(own[0]), halves(own[1])[0]]
        v_heads = [halves(own[1])[1], *halves(own[2])]

        def column(at):
            return own_stats[:, at:at + 1] + own_stats[:, at + 1:at + 2] + own_stats[:, at + 2:at + 3]

        def row(at):
            return all_stats[at:at + 1] + all_stats[at + 1:at + 2] + all_stats[at + 2:at + 3]

        dq, dk, dv = [], [], []
        for head, (kb, vb) in enumerate(((0, 1), (0, 2), (1, 2))):
            qb, gb = (0, 0, 1)[head], (0, 1, 1)[head]
            probs = jnp.exp(mm_nt(q_heads[head], kv[kb]) * scale - column(3 * head))
            gap = mm_nt(g_heads[head], kv[vb]) - column(9 + 3 * head)
            dq.append(mm((probs * gap).astype(BF), kv[kb]) * scale)
            probs = jnp.exp(mm_nt(k_heads[head], query[qb]) * scale - row(3 * head))
            gap = mm_nt(v_heads[head], grad[gb]) - row(9 + 3 * head)
            dv.append(mm(probs.astype(BF), grad[gb]))
            dk.append(mm((probs * gap).astype(BF), query[qb]) * scale)
        tail = dq[2]
        gqkv_buf[...] = jnp.concatenate(
            [join(dk[0], dk[1]), join(dk[2], dv[0]), join(dv[1], dv[2]), join(dq[0], dq[1]),
             join(tail, jnp.zeros_like(tail))],
            axis=1,
        ).astype(BF)


    @pl.when(big)
    def _():
        run(5)

    @pl.when(jnp.logical_not(big))
    def _():
        run(1)

    store = pltpu.make_async_copy(gqkv_buf, gqkv_ref, out_sem)
    store.start()
    wait_all(first_loads)

    grad_buf[...] = mm_tn(normed_buf[...], gqkv_buf[...])
    low = jnp.concatenate([ref[...] for ref in (low_buf, low1_ref, low2_ref, low3_ref)], axis=0)
    mixed = jnp.concatenate(
        [mixed_buf[pl.ds(pl.multiple_of((group ^ k) * BLK, BLK), BLK)] for k in range(4)], axis=0
    )
    out = mm_tn(mixed, low)[HD:]
    for ref, owner in ((keep_ref, core), (send_ref, 1 - core)):
        for tile in range(8):
            rows = grad_buf[pl.ds(pl.multiple_of((2 * tile + owner) * 48, 16), 48)]
            at = (tile // 4) * 96
            pieces = [
                out[at + row * 48:at + (row + 1) * 48, (tile % 4) * 192:(tile % 4 + 1) * 192] for row in range(2)
            ]
            ref[2 * tile] = rows[:, :384].astype(BF)
            ref[2 * tile + 1] = jnp.concatenate(
                [rows[:, 384:576], jnp.where(owner == 1, pieces[1], pieces[0])], axis=1
            ).astype(BF)
    store.wait()


def normed_grad_kernel(
    gqkv_ref, tok_ref, w_ref, vec_ref, own_ref, one_ref, two_ref, three_ref, sums_ref,
    x_buf, part_buf, w_buf, x_sem, w_sem,
):
    load = pltpu.make_async_copy(tok_ref.at[lax.axis_index(MICRO)], x_buf, x_sem)
    load.start()
    loads = weight_copies(w_ref, w_buf, w_sem)
    group = group_index()
    odd = (group % 2) == 1
    load.wait()
    unit, _ = normalized(x_buf[...].astype(F32))
    total = jnp.zeros((TOK, D), F32)
    for slot in range(3):
        part = gqkv_ref[:, slot * 192:(slot + 1) * 192]
        zero = jnp.zeros_like(part)
        wide = jnp.where(
            odd, jnp.concatenate([zero, part], axis=1), jnp.concatenate([part, zero], axis=1)
        )
        loads[slot].wait()
        total = total + mm_nt(wide, w_buf[slot])
    part_buf[...] = total
    own_ref[...] = part_buf[pl.ds(pl.multiple_of(group * BLK, BLK), BLK)]
    for k, ref in ((1, one_ref), (2, two_ref), (3, three_ref)):
        ref[...] = part_buf[pl.ds(pl.multiple_of((group ^ k) * BLK, BLK), BLK)].astype(BF)
    gain1 = jnp.sum(total * unit, axis=0, keepdims=True)
    shift1 = jnp.sum(total, axis=0, keepdims=True)
    sums_ref[...] = jnp.concatenate([gain1, shift1, vec_ref[...][:2], jnp.zeros((4, D), F32)], axis=0)


def add_kernel(one_ref, two_ref, out_ref, buf, sem):
    buf[...] = (one_ref[...].astype(F32) + two_ref[...].astype(F32)).astype(BF)
    copy = pltpu.make_async_copy(buf, out_ref, sem)
    copy.start()
    copy.wait()


def sum_kernel(in_ref, vec_ref, out_ref, buf, vec_buf, sem, vec_sem):
    load = pltpu.make_async_copy(vec_ref, vec_buf, vec_sem)
    load.start()
    total = in_ref[0].astype(F32)
    for index in range(1, 16):
        total = total + in_ref[index].astype(F32)
    load.wait()
    vectors = vec_buf[...][:4]
    block = jnp.concatenate([total, vectors[:, :384], vectors[:, 384:]], axis=0).astype(BF)
    for index in range(8):
        buf[index] = block
    wait_all(send_copies(buf, out_ref, range(8), sem))


def spread_kernel(turn, in_ref, *refs):
    qkv_buf, out_buf, sem, out_sem = refs[-4:]
    qkv_ref, out_ref, *vec_refs = refs[3:-4] if turn else refs[:-4]
    owner = lax.axis_index(CORE)
    owner = 1 - owner if turn else owner
    copies = []
    vectors = jnp.zeros((8, 384), F32)
    for tile in range(8):
        whole = [in_ref[tile, index].astype(F32) for index in range(8)]
        block = [value[:48] for value in whole]
        for value in whole:
            vectors = vectors + value[48:]
        for part, half, at in ((1, 0, 0), (2, 0, 192), (0, 4, 0)):
            qkv_buf[tile, :, part * D:(part + 1) * D] = jnp.concatenate(
                [block[half + group][:, at:at + 192] for group in range(4)], axis=1
            )
        start = pl.multiple_of((2 * tile + owner) * 48, 16)
        copy = pltpu.make_async_copy(qkv_buf.at[tile], qkv_ref.at[pl.ds(start, 48)], sem.at[tile])
        copy.start()
        copies.append(copy)
        for group in range(4):
            out_buf[group, tile // 4, :, (tile % 4) * 192:(tile % 4 + 1) * 192] = block[4 + group][:, 192:]
    for group in range(4):
        for pair in range(2):
            start = pl.multiple_of(group * 192 + (pair * 2 + owner) * 48, 16)
            copy = pltpu.make_async_copy(
                out_buf.at[group, pair], out_ref.at[pl.ds(start, 48)], out_sem.at[group, pair]
            )
            copy.start()
            copies.append(copy)
    if turn:
        vectors = vectors + refs[0][...]
        for k, ref in enumerate(vec_refs):
            ref[...] = jnp.concatenate([vectors[k:k + 1], vectors[4 + k:5 + k]], axis=1).reshape(D)
    else:
        vec_refs[0][...] = vectors
    wait_all(copies)


def spread_ff_kernel(in_ref, up_ref, down_ref):
    up_ref[...] = in_ref[:, :384].astype(F32)
    for tile in range(16):
        half = (tile % 2) * 384
        down_ref[(tile // 2) * 48:(tile // 2 + 1) * 48, half:half + 384] = in_ref[
            tile * 48:(tile + 1) * 48, 384:
        ].astype(F32)


def input_kernel(
    own_ref, one_ref, two_ref, three_ref, tok_ref, gain_ref, grad_ref, result_ref, out_ref, buf, x_buf, sem, x_sem
):
    start = pl.multiple_of(group_index() * BLK, BLK)
    load = pltpu.make_async_copy(tok_ref.at[lax.axis_index(MICRO), pl.ds(start, BLK)], x_buf, x_sem)
    load.start()
    load.wait()
    total = own_ref[...]
    for ref in (one_ref, two_ref, three_ref):
        total = total + ref[...].astype(F32)
    unit, inverse = normalized(x_buf[...].astype(F32))
    grad = grad_ref[...] + norm_back(total, unit, inverse, gain_ref[...].reshape(1, D))
    buf[:BLK] = grad.astype(BF)
    buf[BLK:] = result_ref[...]
    wait_all(send_copies(buf, out_ref, range(8), sem))


def unpack_kernel(in_ref, unused_ref, grad_ref, result_ref):
    for index in range(8):
        rows = slice(index % 4 * BLK, (index % 4 + 1) * BLK)
        grad_ref[index // 4, rows] = in_ref[index, :BLK].astype(F32)
        result_ref[index // 4, rows] = in_ref[index, BLK:]


def exchange(value, axes):
    return lax.all_to_all(value, axes, 0, 0, tiled=True)


def swap(value):
    return lax.ppermute(value, CORE, [(0, 1), (1, 0)])


def after(value, *others):
    return pl.pallas_call(
        lambda *refs: None,
        out_shape=jax.ShapeDtypeStruct(value.shape, value.dtype),
        in_specs=[pl.BlockSpec(memory_space=pl.ANY)] * (1 + len(others)),
        out_specs=pl.BlockSpec(memory_space=pl.ANY),
        input_output_aliases={0: 0},
        cost_estimate=pl.CostEstimate(flops=1, bytes_accessed=1, transcendentals=0),
        compiler_params=pltpu.CompilerParams(vmem_limit_bytes=2**20),
    )(value, *others)


def flip(value, axes, count, bits):
    return lax.ppermute(value, axes, [(index, index ^ bits) for index in range(count)])


def shards(
    tokens, scene_of_block, ln1_gain, ln1_shift, w_qkv, w_out, ln2_gain, ln2_shift, w_up, w_down, out_grad
):
    w_out_pad = jnp.pad(w_out.reshape(4, 192, D), ((0, 0), (HD, 0), (0, 0)))
    kv_send, normed = call(
        project_kernel,
        [((8, TOK, 384), BF, "H"), ((TOK, D), BF, "L")],
        [(tokens, "H"), (ln1_gain, "H"), (ln1_shift, "H"), (w_qkv, "H")],
        1000,
        [
            pltpu.VMEM((TOK, D), BF), pltpu.VMEM((2, D, 384), BF), pltpu.VMEM((TOK, 384), BF),
            pltpu.VMEM((D,), F32), pltpu.VMEM((D,), F32), DMA, DMA((2,)), DMA((8,)), DMA, DMA,
        ],
    )
    (query,) = call(
        query_kernel,
        [((TOK, 256), BF, "L")],
        [(normed, "L"), (w_qkv, "H")],
        1000,
        [pltpu.VMEM((1, D, 384), BF), DMA((1,))],
    )
    kv_same = exchange(kv_send, CHIP)
    kv_same = after(kv_same, pin(query))
    kv_other = swap(kv_same)
    (mixed_send,) = call(
        attend_kernel,
        [((8, TOK, 256), BF, "H")],
        [(scene_of_block, "S"), (query, "H"), (kv_same, "V"), (kv_other, "V")],
        1000,
        [pltpu.VMEM((TOK, 256), BF), pltpu.VMEM((TOK, 256), BF), DMA((8,)), DMA],
    )
    mixed = exchange(mixed_send, NARROW)
    queries = lax.all_gather(after(pin(query), kv_same), WIDE, axis=0, tiled=True).reshape(8, 2, TOK, 256)
    ff_send, middle, normed2, act, grad_pre = call(
        forward_kernel,
        [
            ((8, 2 * BLK, D), BF, "H"), ((BLK, D), F32, "H"), ((2 * TOK, D), BF, "V"),
            ((2 * TOK, FFL), BF, "V"), ((2 * TOK, FFL), BF, "V"),
        ],
        [
            (mixed, "V"), (tokens, "H"), (out_grad, "H"), (w_out_pad, "V"), (ln2_gain, "H"), (ln2_shift, "H"),
            (w_up, "H"), (w_down, "H"),
        ],
        1000,
        [
            pltpu.VMEM((2, TOK, D), BF), pltpu.VMEM((2, TOK, D), BF), pltpu.VMEM((D, FFL), BF),
            pltpu.VMEM((FFL, D), BF), pltpu.VMEM((D,), F32), pltpu.VMEM((D,), F32), pltpu.VMEM((8, BLK, D), BF),
            pltpu.VMEM((8, BLK, D), BF), pltpu.VMEM((8, BLK, D), F32), DMA((6,)), DMA((3,)),
        ],
    )
    ff_sums = exchange(ff_send, NARROW)
    keep, send = call(
        ff_grads_kernel,
        [((8, 48, D), BF, "V")] * 2,
        [(normed2, "V"), (act, "V"), (grad_pre, "V"), (out_grad, "L")],
        1000,
        [pltpu.VMEM((D, FFL), F32), pltpu.VMEM((FFL, D), F32)],
    )
    pieces = call(
        split_kernel, [((2, 48, D), BF, "L")] * 4, [(keep, "V"), (swap(send), "V")], 1000
    )
    pieces = [pieces[0]] + [flip(pieces[k], "y", 4, k) for k in (1, 2, 3)]
    keep, send = call(
        halve_kernel,
        [((48, D), BF, "L")] * 2,
        [(pieces[0], "L")] + [(piece, "V") for piece in pieces[1:]],
        1000,
    )
    ff_sums = after(ff_sums, pin(keep))
    grad_send, low, grad_mid, result_part, vec2 = call(
        middle_kernel,
        [
            ((8, 4, BLK, 256), BF, "H"), ((BLK, D), BF, "H"), ((BLK, D), F32, "H"), ((BLK, D), BF, "H"),
            ((8, D), F32, "H"),
        ],
        [
            (ff_sums, "V"), (middle, "H"), (out_grad, "H"), (mixed, "H"), (w_out_pad, "V"), (ln2_gain, "H"),
        ],
        1000,
        [
            pltpu.VMEM((4, BLK, 256), BF), pltpu.VMEM((BLK, D), F32), pltpu.VMEM((BLK, D), BF),
            pltpu.VMEM((4, BLK, 256), BF), pltpu.VMEM((D,), F32), pltpu.VMEM((BLK, D), BF), pltpu.VMEM((BLK, D), F32),
            pltpu.VMEM((BLK, D), BF), pltpu.VMEM((8, D), F32), DMA((4,)), DMA((8,)), DMA((4,)),
        ],
    )
    send = after(pin(send), pin(low))
    (ff_part,) = call(
        pair_kernel, [((48, D), BF, "L")], [(keep, "L"), (flip(send, "xl", 2, 1), "V")], 1000
    )
    ff_all = lax.all_gather(ff_part, WIDE, axis=0, tiled=True)
    grad_same = exchange(grad_send.reshape(32, BLK, 256), (*CHIP, *GROUP)).reshape(8, TOK, 256)
    lows = [flip(low, GROUP, 4, k) for k in (1, 2, 3)]
    grad_same = after(grad_same, *lows, pin(ff_part))
    grad_other = swap(grad_same)
    gqkv, keep, send = call(
        attend_back_kernel,
        [((TOK, 640), BF, "H")] + [((16, 48, 384), BF, "V")] * 2,
        [
            (scene_of_block, "S"), (kv_same, "H"), (kv_other, "H"), (queries, "H"), (grad_same, "V"), (grad_other, "V"),
            (normed, "H"), (mixed, "H"), (low, "H"), *[(value, "V") for value in lows],
        ],
        10**9,
        [
            pltpu.VMEM((2, 5, TOK, 384), BF), pltpu.VMEM((2, 5, TOK, 256), BF), pltpu.VMEM((TOK, 640), BF),
            pltpu.VMEM((D, 640), F32), pltpu.VMEM((TOK, 256), BF), pltpu.VMEM((TOK, D), BF), pltpu.VMEM((BLK, D), BF),
            DMA((2,)), DMA((2,)), DMA((3,)), DMA,
        ],
        vmem=24,
    )
    (weight_send,) = call(
        add_kernel,
        [((16, 48, 384), BF, "H")],
        [(keep, "V"), (swap(send), "V")],
        1000,
        [pltpu.VMEM((16, 48, 384), BF), DMA],
    )
    weight_parts = exchange(weight_send, (*CHIP, MICRO))
    own, *sends, sums = call(
        normed_grad_kernel,
        [((BLK, D), F32, "L")] + [((BLK, D), BF, "L")] * 3 + [((8, D), F32, "L")],
        [(gqkv, "L"), (tokens, "H"), (w_qkv, "H"), (vec2, "L")],
        1000,
        [pltpu.VMEM((TOK, D), BF), pltpu.VMEM((TOK, D), F32), pltpu.VMEM((3, D, 384), BF), DMA, DMA((3,))],
    )
    parts = [flip(value, GROUP, 4, k + 1) for k, value in enumerate(sends)]
    weight_parts = after(weight_parts, pin(sums), *parts, pin(ff_all))
    (weight_total,) = call(
        sum_kernel,
        [((8, 8, 56, 384), BF, "H")],
        [(weight_parts, "V"), (sums, "H")],
        1000,
        [pltpu.VMEM((8, 56, 384), BF), pltpu.VMEM((8, D), F32), DMA((8,)), DMA],
    )
    (packed,) = call(
        input_kernel,
        [((8, 2 * BLK, D), BF, "H")],
        [
            (own, "L"), *[(value, "V") for value in parts], (tokens, "H"), (ln1_gain, "L"), (grad_mid, "L"),
            (result_part, "L"),
        ],
        1000,
        [pltpu.VMEM((2 * BLK, D), BF), pltpu.VMEM((BLK, D), BF), DMA((8,)), DMA],
    )
    up_grad, down_grad = call(
        spread_ff_kernel, [((D, FFL), F32, "L"), ((FFL, D), F32, "L")], [(ff_all, "L")], 1000
    )
    weight_same = exchange(weight_total.reshape(64, 56, 384), (*CHIP, *NARROW)).reshape(8, 8, 56, 384)
    weight_same = after(weight_same, pin(packed), pin(up_grad), pin(down_grad))
    everyone = exchange(after(pin(packed), weight_same), NARROW)
    weight_other = swap(weight_same)
    scratch = [
        pltpu.VMEM((8, 48, 3 * D), F32), pltpu.VMEM((4, 2, 48, D), F32), DMA((8,)), DMA((4, 2)),
    ]
    grads = [((D, 3 * D), F32, "H"), ((D, D), F32, "H")]
    half = call(
        functools.partial(spread_kernel, False),
        grads + [((8, 384), F32, "V")],
        [(weight_same, "V")],
        1000,
        scratch,
    )
    qkv_grad, out_proj_grad, *vectors = call(
        functools.partial(spread_kernel, True),
        grads + [((D,), F32, "L")] * 4,
        [(weight_other, "V"), (half[2], "V"), (half[0], "H"), (half[1], "H")],
        1000,
        scratch,
        aliases={2: 0, 3: 1},
    )
    input_grad, result = call(
        unpack_kernel, [((2, TOK, D), F32, "L"), ((2, TOK, D), BF, "L")], [(everyone, "V"), (vectors[0], "H")], 1000
    )
    return (
        result, input_grad, qkv_grad, out_proj_grad, *vectors, up_grad, down_grad
    )


def solution(mesh):
    names = ("y", "xl", "c", "zh", "zl", "xh")
    fine = Mesh(mesh.devices.reshape(4, 2, 2, 2, 2, 2), names)
    tokens = P(None, WIDE, None)
    placed = (
        tokens, P(), P(), P(), P(), P(), P(), P(), P(None, NARROW), P(NARROW, None), tokens
    )
    return jax.shard_map(
        shards,
        mesh=fine,
        in_specs=placed,
        out_specs=(
            tokens, tokens, P(), P(), P(), P(), P(), P(), P(None, NARROW), P(NARROW, None)
        ),
        check_vma=False,
    )
```

```python
import functools

import jax
import jax.numpy as jnp
from jax import lax
from jax.experimental import pallas as pl
from jax.experimental.pallas import tpu as pltpu
from jax.sharding import Mesh
from jax.sharding import PartitionSpec as P

D = 768
HD = 64
FFL = 384
TOK = 128
BLK = 32
EPS = 1e-05
BF = jnp.bfloat16
F32 = jnp.float32

CHIP = ("y", "xl")
CORE = "c"
MICRO = "zh"
GROUP = ("zl", "xh")
NARROW = (MICRO, *GROUP)
WIDE = (*CHIP, CORE)


def chip_index():
    return lax.axis_index("y") * 2 + lax.axis_index("xl")


def group_index():
    return lax.axis_index("zl") * 2 + lax.axis_index("xh")


def mm(left, right):
    return lax.dot_general(left, right, (((1,), (0,)), ((), ())), preferred_element_type=F32)


def mm_nt(left, right):
    return lax.dot_general(left, right, (((1,), (1,)), ((), ())), preferred_element_type=F32)


def mm_tn(left, right):
    return lax.dot_general(left, right, (((0,), (0,)), ((), ())), preferred_element_type=F32)


def normalized(values):
    center = values - jnp.mean(values, axis=-1, keepdims=True)
    spread = jnp.mean(center * center, axis=-1, keepdims=True)
    inverse = lax.rsqrt(spread + EPS)
    return center * inverse, inverse


def norm_back(grad, unit, inverse, gain):
    scaled = grad * gain
    first = jnp.mean(scaled, axis=-1, keepdims=True)
    second = jnp.mean(scaled * unit, axis=-1, keepdims=True)
    return inverse * (scaled - first - unit * second)


def halves(block):
    lane = lax.broadcasted_iota(jnp.int32, block.shape, 1)
    zero = jnp.zeros_like(block)
    return jnp.where(lane < HD, block, zero), jnp.where(lane < HD, zero, block)


def join(low, high):
    lane = lax.broadcasted_iota(jnp.int32, low.shape, 1)
    return jnp.where(lane < HD, low, high)


def span(scene_ref):
    micro = lax.axis_index(MICRO)
    own = scene_ref[micro, chip_index() * 4]
    first = jnp.int32(0)
    count = jnp.int32(0)
    for index in range(8):
        other = scene_ref[micro, index * 4]
        first += (other < own).astype(jnp.int32)
        count += (other == own).astype(jnp.int32)
    return first, count > 1


def three(value):
    a = value.astype(BF).astype(F32)
    b = (value - a).astype(BF).astype(F32)
    c = value - a - b
    return a, b, c


def put_columns(width, rows, start, columns):
    lane = lax.broadcasted_iota(jnp.int32, (rows, width), 1)
    out = jnp.zeros((rows, width), F32)
    for offset, column in enumerate(columns):
        out = jnp.where(lane == start + offset, column, out)
    return out


def pin(value):
    return pltpu.with_memory_space_constraint(value, pltpu.HBM)


def call(kernel, outs, ins, cost, scratch=(), vmem=16, aliases=None):
    places = {"V": pltpu.VMEM, "H": pltpu.HBM, "S": pltpu.SMEM, "L": pltpu.VMEM}
    return pl.pallas_call(
        kernel,
        out_shape=[
            (pltpu.HBM if place in "HL" else jax.ShapeDtypeStruct)(shape, dtype) for shape, dtype, place in outs
        ],
        in_specs=[pl.BlockSpec(memory_space=places[place]) for _, place in ins],
        out_specs=[pl.BlockSpec(memory_space=places[place]) for _, _, place in outs],
        scratch_shapes=list(scratch),
        input_output_aliases=aliases or {},
        cost_estimate=pl.CostEstimate(flops=cost, bytes_accessed=1000, transcendentals=0),
        compiler_params=pltpu.CompilerParams(vmem_limit_bytes=vmem * 2**20),
    )(*[pin(value) if place in "HL" else value for value, place in ins])


DMA = pltpu.SemaphoreType.DMA


def send_copies(source, target, indices, sem):
    copies = [pltpu.make_async_copy(source, target.at[index], sem.at[index]) for index in indices]
    for copy in copies:
        copy.start()
    return copies


def wait_all(copies):
    for copy in copies:
        copy.wait()


def weight_copies(w_ref, w_buf, w_sem, parts=(1, 2, 0), start=True):
    group = group_index()
    copies = []
    for slot, part in enumerate(parts):
        column = pl.multiple_of(part * D + (group // 2) * 384, 128)
        copy = pltpu.make_async_copy(w_ref.at[:, pl.ds(column, 384)], w_buf.at[slot], w_sem.at[slot])
        if start:
            copy.start()
        copies.append(copy)
    return copies


def own_heads(full):
    odd = (group_index() % 2) == 1
    return jnp.where(odd, full[:, 192:], full[:, :192]).astype(BF)


def project_kernel(
    tok_ref, gain_ref, shift_ref, w_ref, kv_ref, normed_ref,
    x_buf, w_buf, kv_buf, gain_buf, shift_buf, x_sem, w_sem, kv_sem, gain_sem, shift_sem,
):
    copy_x = pltpu.make_async_copy(tok_ref.at[lax.axis_index(MICRO)], x_buf, x_sem)
    copy_x.start()
    copy_gain = pltpu.make_async_copy(gain_ref, gain_buf, gain_sem)
    copy_gain.start()
    copy_shift = pltpu.make_async_copy(shift_ref, shift_buf, shift_sem)
    copy_shift.start()
    copies = weight_copies(w_ref, w_buf, w_sem, (1, 2))
    wait_all([copy_x, copy_gain, copy_shift])
    unit, _ = normalized(x_buf[...].astype(F32))
    normed = (unit * gain_buf[...].reshape(1, D) + shift_buf[...].reshape(1, D)).astype(BF)
    normed_ref[...] = normed
    parts = []
    for slot in range(2):
        copies[slot].wait()
        parts.append(own_heads(mm(normed, w_buf[slot])))
    kv_buf[...] = jnp.concatenate(parts, axis=1)
    wait_all(send_copies(kv_buf, kv_ref, range(8), kv_sem))


def query_kernel(normed_ref, w_ref, q_ref, w_buf, w_sem):
    weight_copies(w_ref, w_buf, w_sem, (0,))[0].wait()
    part = own_heads(mm(normed_ref[...], w_buf[0]))
    q_ref[...] = jnp.concatenate([part, jnp.zeros((TOK, HD), BF)], axis=1)


def attend_kernel(scene_ref, q_ref, same_ref, other_ref, out_ref, buf, q_buf, sem, q_sem):
    load = pltpu.make_async_copy(q_ref, q_buf, q_sem)
    load.start()
    first, big = span(scene_ref)

    def run(count):
        rows = count * TOK
        keys = jnp.concatenate(
            [ref[pl.ds(first, count)].reshape(rows, 384) for ref in (same_ref, other_ref)], axis=0
        )
        load.wait()
        query = q_buf[...]
        q0, q1 = halves(query[:, :128])
        blocks = [keys[:, :128], keys[:, 128:256], keys[:, 256:]]
        mixed = []
        columns = []
        for qh, kb, vb in ((q0, 0, 1), (q1, 0, 2), (query[:, 128:], 1, 2)):
            scores = mm_nt(qh, blocks[kb]) * (HD**-0.5)
            top = jnp.max(scores, axis=-1, keepdims=True)
            weights = jnp.exp(scores - top)
            total = jnp.sum(weights, axis=-1, keepdims=True)
            probs = (weights * (1.0 / total)).astype(BF)
            mixed.append(mm(probs, blocks[vb]))
            columns += three(top + jnp.log(total))
        stats = put_columns(128, TOK, 0, columns)
        buf[...] = jnp.concatenate([join(stats, mixed[0]), join(mixed[1], mixed[2])], axis=1).astype(BF)

    @pl.when(big)
    def _():
        run(5)

    @pl.when(jnp.logical_not(big))
    def _():
        run(1)

    wait_all(send_copies(buf, out_ref, range(8), sem))


def forward_kernel(
    mixed_ref, tok_ref, og_ref, wo_ref, gain_ref, shift_ref, up_ref, down_ref,
    out_ref, middle_ref, normed_ref, act_ref, gpre_ref,
    tok_buf, og_buf, up_buf, down_buf, gain_buf, shift_buf, grad_buf, branch_buf, middle_buf, in_sem, sem,
):
    loads = [
        pltpu.make_async_copy(ref, buf, in_sem.at[index])
        for index, (ref, buf) in enumerate(
            (
                (tok_ref, tok_buf), (up_ref, up_buf), (og_ref, og_buf), (down_ref, down_buf), (gain_ref, gain_buf),
                (shift_ref, shift_buf),
            )
        )
    ]
    for load in loads:
        load.start()
    total = jnp.zeros((2 * TOK, D), F32)
    for group in range(4):
        rows = jnp.concatenate([mixed_ref[group], mixed_ref[4 + group]], axis=0)
        total = total + mm(rows, wo_ref[group])
    loads[0].wait()
    total = total + tok_buf[...].reshape(2 * TOK, D).astype(F32)
    middle_buf[...] = total.reshape(8, BLK, D)
    third = pltpu.make_async_copy(
        middle_buf.at[lax.axis_index(MICRO) * 4 + group_index()], middle_ref, sem.at[2]
    )
    third.start()
    unit, _ = normalized(total)
    wait_all(loads[4:])
    normed = (unit * gain_buf[...].reshape(1, D) + shift_buf[...].reshape(1, D)).astype(BF)
    normed_ref[...] = normed
    loads[1].wait()
    pre = mm(normed, up_buf[...])
    cdf = 0.5 * (1.0 + lax.erf(pre * (0.5**0.5)))
    slope = cdf + pre * jnp.exp(-0.5 * pre * pre) * 0.3989422804014327
    loads[2].wait()
    loads[3].wait()
    grad_out = og_buf[...].reshape(2 * TOK, D)
    gpre = (mm_nt(grad_out, down_buf[...]) * slope).astype(BF)
    gpre_ref[...] = gpre
    grad_buf[...] = mm_nt(gpre, up_buf[...]).astype(BF).reshape(8, BLK, D)
    first = pltpu.make_async_copy(grad_buf, out_ref.at[:, pl.ds(BLK, BLK)], sem.at[0])
    first.start()
    act = (pre * cdf).astype(BF)
    act_ref[...] = act
    branch_buf[...] = mm(act, down_buf[...]).astype(BF).reshape(8, BLK, D)
    second = pltpu.make_async_copy(branch_buf, out_ref.at[:, pl.ds(0, BLK)], sem.at[1])
    second.start()
    wait_all([first, second, third])


def ff_grads_kernel(normed_ref, act_ref, gpre_ref, og_ref, keep_ref, send_ref, up_buf, down_buf):
    core = lax.axis_index(CORE)
    up_buf[...] = mm_tn(normed_ref[...], gpre_ref[...])
    down_buf[...] = mm_tn(act_ref[...], og_ref[...].reshape(2 * TOK, D))
    for ref, owner in ((keep_ref, core), (send_ref, 1 - core)):
        column = pl.multiple_of(owner * 384, 128)
        for tile in range(8):
            rows = pl.ds(pl.multiple_of((2 * tile + owner) * 48, 16), 48)
            ref[tile, :, :384] = up_buf[rows].astype(BF)
            ref[tile, :, 384:] = down_buf[tile * 48:(tile + 1) * 48, pl.ds(column, 384)].astype(BF)


def split_kernel(one_ref, two_ref, *refs):
    y = lax.axis_index("y")
    for k, ref in enumerate(refs):
        for xl in range(2):
            at = (y ^ k) * 2 + xl
            ref[xl] = (one_ref[at].astype(F32) + two_ref[at].astype(F32)).astype(BF)


def halve_kernel(*refs):
    parts, (keep_ref, send_ref) = refs[:4], refs[4:]
    xl = lax.axis_index("xl")
    for ref, at in ((keep_ref, xl), (send_ref, 1 - xl)):
        total = parts[0][at].astype(F32)
        for part in parts[1:]:
            total = total + part[at].astype(F32)
        ref[...] = total.astype(BF)


def pair_kernel(one_ref, two_ref, out_ref):
    out_ref[...] = (one_ref[...].astype(F32) + two_ref[...].astype(F32)).astype(BF)


def middle_kernel(
    sums_ref, middle_ref, og_ref, mixed_ref, wo_ref, gain_ref,
    out_ref, low_ref, grad_ref, result_ref, vec_ref,
    buf, middle_buf, og_buf, mixed_buf, gain_buf, low_buf, grad_buf, result_buf, vec_buf, in_sem, sem, rest_sem,
):
    micro = lax.axis_index(MICRO)
    group = group_index()
    block = pl.ds(pl.multiple_of(group * BLK, BLK), BLK)
    loads = [
        pltpu.make_async_copy(middle_ref, middle_buf, in_sem.at[0]),
        pltpu.make_async_copy(og_ref.at[micro, block], og_buf, in_sem.at[1]),
        pltpu.make_async_copy(mixed_ref.at[pl.ds(micro * 4, 4), block], mixed_buf, in_sem.at[2]),
        pltpu.make_async_copy(gain_ref, gain_buf, in_sem.at[3]),
    ]
    for load in loads:
        load.start()
    total = sums_ref[0].astype(F32)
    for index in range(1, 8):
        total = total + sums_ref[index].astype(F32)
    branch, grad = total[:BLK], total[BLK:]
    wait_all(loads)
    middle = middle_buf[...]
    unit, inverse = normalized(middle)
    grad_mid = og_buf[...].astype(F32) + norm_back(grad, unit, inverse, gain_buf[...].reshape(1, D))
    low = grad_mid.astype(BF)
    low_buf[...] = low
    grad_buf[...] = grad_mid
    result_buf[...] = (middle + branch).astype(BF)
    gain_grad = jnp.sum(grad * unit, axis=0, keepdims=True)
    shift_grad = jnp.sum(grad, axis=0, keepdims=True)
    vec_buf[...] = jnp.concatenate([gain_grad, shift_grad, jnp.zeros((6, D), F32)], axis=0)
    stores = [
        pltpu.make_async_copy(source, target, rest_sem.at[index])
        for index, (source, target) in enumerate(
            ((low_buf, low_ref), (grad_buf, grad_ref), (result_buf, result_ref), (vec_buf, vec_ref))
        )
    ]
    for store in stores:
        store.start()
    lane = lax.broadcasted_iota(jnp.int32, (BLK, 256), 1)
    for head_group in range(4):
        mixed = mixed_buf[head_group].astype(F32)
        back = mm_nt(low, wo_ref[head_group]).astype(BF).astype(F32)
        product = mixed * back
        columns = []
        for head in range(3):
            inside = (lane >= (head + 1) * HD) & (lane < (head + 2) * HD)
            columns += three(jnp.sum(jnp.where(inside, product, 0.0), axis=-1, keepdims=True))
        stats = put_columns(256, BLK, 9, columns)
        buf[head_group] = jnp.where(lane < 9, mixed, jnp.where(lane < HD, stats, back)).astype(BF)
    sends = send_copies(buf, out_ref, range(8), sem)
    wait_all(stores)
    wait_all(sends)


def attend_back_kernel(
    scene_ref, kvs_ref, kvo_ref, q_ref, gs_ref, go_ref, normed_ref, mixed_ref, low_ref, low1_ref, low2_ref, low3_ref,
    w_ref, gqkv_ref, w_out_ref, keep_ref, send_ref,
    kv_buf, q_buf, grad_buf, mixed_buf, normed_buf, low_buf, kv_sem, q_sem, in_sem, w_sem,
):
    first, big = span(scene_ref)
    chip = chip_index()
    core = lax.axis_index(CORE)
    group = group_index()
    index = lax.axis_index(MICRO) * 4 + group
    first_loads = [
        pltpu.make_async_copy(source, target, in_sem.at[slot])
        for slot, (source, target) in enumerate(
            ((normed_ref, normed_buf), (mixed_ref.at[index], mixed_buf), (low_ref, low_buf))
        )
    ]
    scale = HD**-0.5

    def run(count):
        rows = count * TOK
        loads = [
            pltpu.make_async_copy(ref.at[pl.ds(first, count)], kv_buf.at[slot, pl.ds(0, count)], kv_sem.at[slot])
            for slot, ref in enumerate((kvs_ref, kvo_ref))
        ] + [
            pltpu.make_async_copy(
                q_ref.at[pl.ds(first, count), which], q_buf.at[slot, pl.ds(0, count)], q_sem.at[slot]
            )
            for slot, which in enumerate((core, 1 - core))
        ]
        for load in loads + first_loads:
            load.start()
        weight_copies(w_ref, w_out_ref, w_sem)

        def cut(value):
            return [value[:, at:at + 128] for at in range(0, value.shape[1], 128)]

        grad = cut(jnp.concatenate(
            [ref[pl.ds(first, count)].reshape(rows, 256) for ref in (gs_ref, go_ref)], axis=0
        ))
        g_own = cut(gs_ref[chip])
        g_heads = [halves(g_own[0])[1], *halves(g_own[1])]
        own_stats = g_own[0].astype(F32)
        all_stats = grad[0].astype(F32).T
        wait_all(loads)
        kv = cut(jnp.concatenate([kv_buf[slot, :count].reshape(rows, 384) for slot in range(2)], axis=0))
        query = cut(jnp.concatenate([q_buf[slot, :count].reshape(rows, 256) for slot in range(2)], axis=0))
        own = cut(kv_buf[0, chip - first]) + cut(q_buf[0, chip - first])
        q_heads = [*halves(own[3]), own[4]]
        k_heads = [*halves(own[0]), halves(own[1])[0]]
        v_heads = [halves(own[1])[1], *halves(own[2])]

        def column(at):
            return own_stats[:, at:at + 1] + own_stats[:, at + 1:at + 2] + own_stats[:, at + 2:at + 3]

        def row(at):
            return all_stats[at:at + 1] + all_stats[at + 1:at + 2] + all_stats[at + 2:at + 3]

        dq, dk, dv = [], [], []
        for head, (kb, vb) in enumerate(((0, 1), (0, 2), (1, 2))):
            qb, gb = (0, 0, 1)[head], (0, 1, 1)[head]
            probs = jnp.exp(mm_nt(q_heads[head], kv[kb]) * scale - column(3 * head))
            gap = mm_nt(g_heads[head], kv[vb]) - column(9 + 3 * head)
            dq.append(mm((probs * gap).astype(BF), kv[kb]) * scale)
            probs = jnp.exp(mm_nt(k_heads[head], query[qb]) * scale - row(3 * head))
            gap = mm_nt(v_heads[head], grad[gb]) - row(9 + 3 * head)
            dv.append(mm(probs.astype(BF), grad[gb]))
            dk.append(mm((probs * gap).astype(BF), query[qb]) * scale)
        tail = dq[2]
        gqkv_ref[...] = jnp.concatenate(
            [join(dk[0], dk[1]), join(dk[2], dv[0]), join(dv[1], dv[2]), join(dq[0], dq[1]),
             join(tail, jnp.zeros_like(tail))],
            axis=1,
        ).astype(BF)


    @pl.when(big)
    def _():
        run(5)

    @pl.when(jnp.logical_not(big))
    def _():
        run(1)

    wait_all(first_loads)

    grad_buf[...] = mm_tn(normed_buf[...], gqkv_ref[...])
    low = jnp.concatenate([ref[...] for ref in (low_buf, low1_ref, low2_ref, low3_ref)], axis=0)
    mixed = jnp.concatenate(
        [mixed_buf[pl.ds(pl.multiple_of((group ^ k) * BLK, BLK), BLK)] for k in range(4)], axis=0
    )
    out = mm_tn(mixed, low)[HD:]
    for ref, owner in ((keep_ref, core), (send_ref, 1 - core)):
        for tile in range(8):
            rows = grad_buf[pl.ds(pl.multiple_of((2 * tile + owner) * 48, 16), 48)]
            at = (tile // 4) * 96
            pieces = [
                out[at + row * 48:at + (row + 1) * 48, (tile % 4) * 192:(tile % 4 + 1) * 192] for row in range(2)
            ]
            ref[2 * tile] = rows[:, :384].astype(BF)
            ref[2 * tile + 1] = jnp.concatenate(
                [rows[:, 384:576], jnp.where(owner == 1, pieces[1], pieces[0])], axis=1
            ).astype(BF)
    wait_all(weight_copies(w_ref, w_out_ref, w_sem, start=False))


def normed_grad_kernel(
    gqkv_ref, w_ref, tok_ref, vec_ref, own_ref, one_ref, two_ref, three_ref, sums_ref,
    x_buf, vec_buf, part_buf, low_buf, sums_buf, in_sem, out_sem,
):
    loads = [
        pltpu.make_async_copy(tok_ref.at[lax.axis_index(MICRO)], x_buf, in_sem.at[0]),
        pltpu.make_async_copy(vec_ref, vec_buf, in_sem.at[1]),
    ]
    for load in loads:
        load.start()
    group = group_index()
    odd = (group % 2) == 1
    total = jnp.zeros((TOK, D), F32)
    for slot in range(3):
        part = gqkv_ref[:, slot * 192:(slot + 1) * 192]
        zero = jnp.zeros_like(part)
        wide = jnp.where(
            odd, jnp.concatenate([zero, part], axis=1), jnp.concatenate([part, zero], axis=1)
        )
        total = total + mm_nt(wide, w_ref[slot])
    part_buf[...] = total
    low_buf[...] = total.astype(BF)
    stores = []
    for k, ref in enumerate((own_ref, one_ref, two_ref, three_ref)):
        rows = pl.ds(pl.multiple_of((group ^ k) * BLK, BLK), BLK)
        stores.append(pltpu.make_async_copy((low_buf if k else part_buf).at[rows], ref, out_sem.at[k]))
        stores[-1].start()
    wait_all(loads)
    unit, _ = normalized(x_buf[...].astype(F32))
    gain1 = jnp.sum(total * unit, axis=0, keepdims=True)
    shift1 = jnp.sum(total, axis=0, keepdims=True)
    sums_buf[...] = jnp.concatenate([gain1, shift1, vec_buf[...][:2], jnp.zeros((4, D), F32)], axis=0)
    stores.append(pltpu.make_async_copy(sums_buf, sums_ref, out_sem.at[4]))
    stores[-1].start()
    wait_all(stores)


def add_kernel(one_ref, two_ref, unused_ref, out_ref, buf, sem):
    buf[...] = (one_ref[...].astype(F32) + two_ref[...].astype(F32)).astype(BF)
    copy = pltpu.make_async_copy(buf, out_ref, sem)
    copy.start()
    copy.wait()


def sum_kernel(in_ref, vec_ref, out_ref, buf, vec_buf, sem, vec_sem):
    load = pltpu.make_async_copy(vec_ref, vec_buf, vec_sem)
    load.start()
    total = in_ref[0].astype(F32)
    for index in range(1, 16):
        total = total + in_ref[index].astype(F32)
    load.wait()
    vectors = vec_buf[...][:4]
    block = jnp.concatenate([total, vectors[:, :384], vectors[:, 384:]], axis=0).astype(BF)
    for index in range(8):
        buf[index] = block
    wait_all(send_copies(buf, out_ref, range(8), sem))


def spread_kernel(turn, in_ref, *refs):
    qkv_buf, out_buf, sem, out_sem = refs[-4:]
    qkv_ref, out_ref, *vec_refs = refs[3:-4] if turn else refs[:-4]
    owner = lax.axis_index(CORE)
    owner = 1 - owner if turn else owner
    copies = []
    vectors = jnp.zeros((8, 384), F32)
    for tile in range(8):
        whole = [in_ref[tile, index].astype(F32) for index in range(8)]
        block = [value[:48] for value in whole]
        for value in whole:
            vectors = vectors + value[48:]
        for part, half, at in ((1, 0, 0), (2, 0, 192), (0, 4, 0)):
            qkv_buf[tile, :, part * D:(part + 1) * D] = jnp.concatenate(
                [block[half + group][:, at:at + 192] for group in range(4)], axis=1
            )
        start = pl.multiple_of((2 * tile + owner) * 48, 16)
        copy = pltpu.make_async_copy(qkv_buf.at[tile], qkv_ref.at[pl.ds(start, 48)], sem.at[tile])
        copy.start()
        copies.append(copy)
        for group in range(4):
            out_buf[group, tile // 4, :, (tile % 4) * 192:(tile % 4 + 1) * 192] = block[4 + group][:, 192:]
    for group in range(4):
        for pair in range(2):
            start = pl.multiple_of(group * 192 + (pair * 2 + owner) * 48, 16)
            copy = pltpu.make_async_copy(
                out_buf.at[group, pair], out_ref.at[pl.ds(start, 48)], out_sem.at[group, pair]
            )
            copy.start()
            copies.append(copy)
    if turn:
        vectors = vectors + refs[0][...]
        for k, ref in enumerate(vec_refs):
            ref[...] = jnp.concatenate([vectors[k:k + 1], vectors[4 + k:5 + k]], axis=1).reshape(D)
    else:
        vec_refs[0][...] = vectors
    wait_all(copies)


def spread_ff_kernel(in_ref, up_ref, down_ref):
    up_ref[...] = in_ref[:, :384].astype(F32)
    for tile in range(16):
        half = (tile % 2) * 384
        down_ref[(tile // 2) * 48:(tile // 2 + 1) * 48, half:half + 384] = in_ref[
            tile * 48:(tile + 1) * 48, 384:
        ].astype(F32)


def input_kernel(
    own_ref, one_ref, two_ref, three_ref, tok_ref, gain_ref, grad_ref, result_ref, unused_ref, out_ref, buf, x_buf, sem, x_sem
):
    start = pl.multiple_of(group_index() * BLK, BLK)
    load = pltpu.make_async_copy(tok_ref.at[lax.axis_index(MICRO), pl.ds(start, BLK)], x_buf, x_sem)
    load.start()
    load.wait()
    total = own_ref[...]
    for ref in (one_ref, two_ref, three_ref):
        total = total + ref[...].astype(F32)
    unit, inverse = normalized(x_buf[...].astype(F32))
    grad = grad_ref[...] + norm_back(total, unit, inverse, gain_ref[...].reshape(1, D))
    buf[:BLK] = grad.astype(BF)
    buf[BLK:] = result_ref[...]
    wait_all(send_copies(buf, out_ref, range(8), sem))


def unpack_kernel(in_ref, unused_ref, grad_ref, result_ref):
    for index in range(8):
        rows = slice(index % 4 * BLK, (index % 4 + 1) * BLK)
        grad_ref[index // 4, rows] = in_ref[index, :BLK].astype(F32)
        result_ref[index // 4, rows] = in_ref[index, BLK:]


def exchange(value, axes):
    return lax.all_to_all(value, axes, 0, 0, tiled=True)


def swap(value):
    return lax.ppermute(value, CORE, [(0, 1), (1, 0)])


def after(value, *others):
    return pl.pallas_call(
        lambda *refs: None,
        out_shape=jax.ShapeDtypeStruct(value.shape, value.dtype),
        in_specs=[pl.BlockSpec(memory_space=pl.ANY)] * (1 + len(others)),
        out_specs=pl.BlockSpec(memory_space=pl.ANY),
        input_output_aliases={0: 0},
        cost_estimate=pl.CostEstimate(flops=1, bytes_accessed=1, transcendentals=0),
        compiler_params=pltpu.CompilerParams(vmem_limit_bytes=2**20),
    )(value, *others)


def flip(value, axes, count, bits):
    return lax.ppermute(value, axes, [(index, index ^ bits) for index in range(count)])


def shards(
    tokens, scene_of_block, ln1_gain, ln1_shift, w_qkv, w_out, ln2_gain, ln2_shift, w_up, w_down, out_grad
):
    w_out_pad = jnp.pad(w_out.reshape(4, 192, D), ((0, 0), (HD, 0), (0, 0)))
    kv_send, normed = call(
        project_kernel,
        [((8, TOK, 384), BF, "H"), ((TOK, D), BF, "L")],
        [(tokens, "H"), (ln1_gain, "H"), (ln1_shift, "H"), (w_qkv, "H")],
        1000,
        [
            pltpu.VMEM((TOK, D), BF), pltpu.VMEM((2, D, 384), BF), pltpu.VMEM((TOK, 384), BF),
            pltpu.VMEM((D,), F32), pltpu.VMEM((D,), F32), DMA, DMA((2,)), DMA((8,)), DMA, DMA,
        ],
    )
    (query,) = call(
        query_kernel,
        [((TOK, 256), BF, "L")],
        [(normed, "L"), (w_qkv, "H")],
        1000,
        [pltpu.VMEM((1, D, 384), BF), DMA((1,))],
    )
    kv_same = exchange(kv_send, CHIP)
    kv_same = after(kv_same, pin(query))
    kv_other = swap(kv_same)
    (mixed_send,) = call(
        attend_kernel,
        [((8, TOK, 256), BF, "H")],
        [(scene_of_block, "S"), (query, "H"), (kv_same, "V"), (kv_other, "V")],
        1000,
        [pltpu.VMEM((TOK, 256), BF), pltpu.VMEM((TOK, 256), BF), DMA((8,)), DMA],
    )
    mixed = exchange(mixed_send, NARROW)
    queries = lax.all_gather(after(pin(query), kv_same), WIDE, axis=0, tiled=True).reshape(8, 2, TOK, 256)
    ff_send, middle, normed2, act, grad_pre = call(
        forward_kernel,
        [
            ((8, 2 * BLK, D), BF, "H"), ((BLK, D), F32, "H"), ((2 * TOK, D), BF, "V"),
            ((2 * TOK, FFL), BF, "V"), ((2 * TOK, FFL), BF, "V"),
        ],
        [
            (mixed, "V"), (tokens, "H"), (out_grad, "H"), (w_out_pad, "V"), (ln2_gain, "H"), (ln2_shift, "H"),
            (w_up, "H"), (w_down, "H"),
        ],
        1000,
        [
            pltpu.VMEM((2, TOK, D), BF), pltpu.VMEM((2, TOK, D), BF), pltpu.VMEM((D, FFL), BF),
            pltpu.VMEM((FFL, D), BF), pltpu.VMEM((D,), F32), pltpu.VMEM((D,), F32), pltpu.VMEM((8, BLK, D), BF),
            pltpu.VMEM((8, BLK, D), BF), pltpu.VMEM((8, BLK, D), F32), DMA((6,)), DMA((3,)),
        ],
    )
    ff_sums = exchange(ff_send, NARROW)
    keep, send = call(
        ff_grads_kernel,
        [((8, 48, D), BF, "V")] * 2,
        [(normed2, "V"), (act, "V"), (grad_pre, "V"), (out_grad, "L")],
        1000,
        [pltpu.VMEM((D, FFL), F32), pltpu.VMEM((FFL, D), F32)],
    )
    pieces = call(
        split_kernel, [((2, 48, D), BF, "L")] * 4, [(keep, "V"), (swap(send), "V")], 1000
    )
    pieces = [pieces[0]] + [flip(pieces[k], "y", 4, k) for k in (1, 2, 3)]
    ff_keep, ff_send = call(
        halve_kernel,
        [((48, D), BF, "L")] * 2,
        [(pieces[0], "L")] + [(piece, "V") for piece in pieces[1:]],
        1000,
    )
    grad_send, low, grad_mid, result_part, vec2 = call(
        middle_kernel,
        [
            ((8, 4, BLK, 256), BF, "H"), ((BLK, D), BF, "H"), ((BLK, D), F32, "H"), ((BLK, D), BF, "H"),
            ((8, D), F32, "H"),
        ],
        [
            (ff_sums, "V"), (middle, "H"), (out_grad, "H"), (mixed, "H"), (w_out_pad, "V"), (ln2_gain, "H"),
        ],
        1000,
        [
            pltpu.VMEM((4, BLK, 256), BF), pltpu.VMEM((BLK, D), F32), pltpu.VMEM((BLK, D), BF),
            pltpu.VMEM((4, BLK, 256), BF), pltpu.VMEM((D,), F32), pltpu.VMEM((BLK, D), BF), pltpu.VMEM((BLK, D), F32),
            pltpu.VMEM((BLK, D), BF), pltpu.VMEM((8, D), F32), DMA((4,)), DMA((8,)), DMA((4,)),
        ],
    )
    grad_send = after(pin(grad_send), *pieces[1:])
    grad_same = exchange(grad_send.reshape(32, BLK, 256), (*CHIP, *GROUP)).reshape(8, TOK, 256)
    lows = [flip(low, GROUP, 4, k) for k in (1, 2, 3)]
    grad_same = after(grad_same, *lows, pin(ff_send))
    grad_other = swap(grad_same)
    far = flip(ff_send, "xl", 2, 1)
    gqkv, w_own, keep, send = call(
        attend_back_kernel,
        [((TOK, 640), BF, "V"), ((3, D, 384), BF, "V")] + [((16, 48, 384), BF, "V")] * 2,
        [
            (scene_of_block, "S"), (kv_same, "H"), (kv_other, "H"), (queries, "H"), (grad_same, "V"), (grad_other, "V"),
            (normed, "H"), (mixed, "H"), (low, "H"), *[(value, "V") for value in lows], (w_qkv, "H"),
        ],
        10**9,
        [
            pltpu.VMEM((2, 5, TOK, 384), BF), pltpu.VMEM((2, 5, TOK, 256), BF), pltpu.VMEM((D, 640), F32),
            pltpu.VMEM((TOK, 256), BF), pltpu.VMEM((TOK, D), BF), pltpu.VMEM((BLK, D), BF),
            DMA((2,)), DMA((2,)), DMA((3,)), DMA((3,)),
        ],
        vmem=24,
    )
    own, *sends, sums = call(
        normed_grad_kernel,
        [((BLK, D), F32, "H")] + [((BLK, D), BF, "H")] * 3 + [((8, D), F32, "H")],
        [(gqkv, "V"), (w_own, "V"), (tokens, "H"), (vec2, "H")],
        1000,
        [
            pltpu.VMEM((TOK, D), BF), pltpu.VMEM((8, D), F32), pltpu.VMEM((TOK, D), F32), pltpu.VMEM((TOK, D), BF),
            pltpu.VMEM((8, D), F32), DMA((2,)), DMA((5,)),
        ],
    )
    (weight_send,) = call(
        add_kernel,
        [((16, 48, 384), BF, "H")],
        [(keep, "V"), (swap(send), "V"), (own, "H")],
        1000,
        [pltpu.VMEM((16, 48, 384), BF), DMA],
    )
    (ff_part,) = call(pair_kernel, [((48, D), BF, "L")], [(ff_keep, "L"), (far, "V")], 1000)
    ff_all = lax.all_gather(ff_part, WIDE, axis=0, tiled=True)
    weight_parts = exchange(weight_send, (*CHIP, MICRO))
    parts = [flip(value, GROUP, 4, k + 1) for k, value in enumerate(sends)]
    weight_parts = after(weight_parts, pin(sums), *parts)
    (weight_total,) = call(
        sum_kernel,
        [((8, 8, 56, 384), BF, "H")],
        [(weight_parts, "V"), (sums, "H")],
        4 * 10**10,
        [pltpu.VMEM((8, 56, 384), BF), pltpu.VMEM((8, D), F32), DMA((8,)), DMA],
    )
    (packed,) = call(
        input_kernel,
        [((8, 2 * BLK, D), BF, "H")],
        [
            (own, "L"), *[(value, "V") for value in parts], (tokens, "H"), (ln1_gain, "L"), (grad_mid, "L"),
            (result_part, "L"), (weight_total, "H"),
        ],
        1000,
        [pltpu.VMEM((2 * BLK, D), BF), pltpu.VMEM((BLK, D), BF), DMA((8,)), DMA],
    )
    up_grad, down_grad = call(
        spread_ff_kernel, [((D, FFL), F32, "L"), ((FFL, D), F32, "L")], [(ff_all, "L")], 5 * 10**10
    )
    weight_same = exchange(weight_total.reshape(64, 56, 384), (*CHIP, *NARROW)).reshape(8, 8, 56, 384)
    weight_same = after(weight_same, pin(packed), pin(up_grad), pin(down_grad))
    everyone = exchange(after(pin(packed), weight_same), NARROW)
    weight_other = swap(weight_same)
    scratch = [
        pltpu.VMEM((8, 48, 3 * D), F32), pltpu.VMEM((4, 2, 48, D), F32), DMA((8,)), DMA((4, 2)),
    ]
    grads = [((D, 3 * D), F32, "H"), ((D, D), F32, "H")]
    half = call(
        functools.partial(spread_kernel, False),
        grads + [((8, 384), F32, "V")],
        [(weight_same, "V")],
        1000,
        scratch,
    )
    qkv_grad, out_proj_grad, *vectors = call(
        functools.partial(spread_kernel, True),
        grads + [((D,), F32, "L")] * 4,
        [(weight_other, "V"), (half[2], "V"), (half[0], "H"), (half[1], "H")],
        1000,
        scratch,
        aliases={2: 0, 3: 1},
    )
    input_grad, result = call(
        unpack_kernel, [((2, TOK, D), F32, "L"), ((2, TOK, D), BF, "L")], [(everyone, "V"), (vectors[0], "H")], 1000
    )
    return (
        result, input_grad, qkv_grad, out_proj_grad, *vectors, up_grad, down_grad
    )


def solution(mesh):
    names = ("y", "xl", "c", "zh", "zl", "xh")
    fine = Mesh(mesh.devices.reshape(4, 2, 2, 2, 2, 2), names)
    tokens = P(None, WIDE, None)
    placed = (
        tokens, P(), P(), P(), P(), P(), P(), P(), P(None, NARROW), P(NARROW, None), tokens
    )
    return jax.shard_map(
        shards,
        mesh=fine,
        in_specs=placed,
        out_specs=(
            tokens, tokens, P(), P(), P(), P(), P(), P(), P(None, NARROW), P(NARROW, None)
        ),
        check_vma=False,
    )
```

```python
import functools

import jax
import jax.numpy as jnp
from jax import lax
from jax.experimental import pallas as pl
from jax.experimental.pallas import tpu as pltpu
from jax.sharding import Mesh
from jax.sharding import PartitionSpec as P

D = 768
HD = 64
FFL = 384
TOK = 128
BLK = 32
EPS = 1e-05
BF = jnp.bfloat16
F32 = jnp.float32

CHIP = ("y", "xl")
CORE = "c"
MICRO = "zh"
GROUP = ("zl", "xh")
NARROW = (MICRO, *GROUP)
WIDE = (*CHIP, CORE)


def chip_index():
    return lax.axis_index("y") * 2 + lax.axis_index("xl")


def group_index():
    return lax.axis_index("zl") * 2 + lax.axis_index("xh")


def mm(left, right):
    return lax.dot_general(left, right, (((1,), (0,)), ((), ())), preferred_element_type=F32)


def mm_nt(left, right):
    return lax.dot_general(left, right, (((1,), (1,)), ((), ())), preferred_element_type=F32)


def mm_tn(left, right):
    return lax.dot_general(left, right, (((0,), (0,)), ((), ())), preferred_element_type=F32)


def normalized(values):
    center = values - jnp.mean(values, axis=-1, keepdims=True)
    spread = jnp.mean(center * center, axis=-1, keepdims=True)
    inverse = lax.rsqrt(spread + EPS)
    return center * inverse, inverse


def norm_back(grad, unit, inverse, gain):
    scaled = grad * gain
    first = jnp.mean(scaled, axis=-1, keepdims=True)
    second = jnp.mean(scaled * unit, axis=-1, keepdims=True)
    return inverse * (scaled - first - unit * second)


def halves(block):
    lane = lax.broadcasted_iota(jnp.int32, block.shape, 1)
    zero = jnp.zeros_like(block)
    return jnp.where(lane < HD, block, zero), jnp.where(lane < HD, zero, block)


def join(low, high):
    lane = lax.broadcasted_iota(jnp.int32, low.shape, 1)
    return jnp.where(lane < HD, low, high)


def span(scene_ref):
    micro = lax.axis_index(MICRO)
    own = scene_ref[micro, chip_index() * 4]
    first = jnp.int32(0)
    count = jnp.int32(0)
    for index in range(8):
        other = scene_ref[micro, index * 4]
        first += (other < own).astype(jnp.int32)
        count += (other == own).astype(jnp.int32)
    return first, count > 1


def three(value):
    a = value.astype(BF).astype(F32)
    b = (value - a).astype(BF).astype(F32)
    c = value - a - b
    return a, b, c


def put_columns(width, rows, start, columns):
    lane = lax.broadcasted_iota(jnp.int32, (rows, width), 1)
    out = jnp.zeros((rows, width), F32)
    for offset, column in enumerate(columns):
        out = jnp.where(lane == start + offset, column, out)
    return out


def pin(value):
    return pltpu.with_memory_space_constraint(value, pltpu.HBM)


def call(kernel, outs, ins, cost, scratch=(), vmem=16, aliases=None):
    places = {"V": pltpu.VMEM, "H": pltpu.HBM, "S": pltpu.SMEM, "L": pltpu.VMEM}
    return pl.pallas_call(
        kernel,
        out_shape=[
            (pltpu.HBM if place in "HL" else jax.ShapeDtypeStruct)(shape, dtype) for shape, dtype, place in outs
        ],
        in_specs=[pl.BlockSpec(memory_space=places[place]) for _, place in ins],
        out_specs=[pl.BlockSpec(memory_space=places[place]) for _, _, place in outs],
        scratch_shapes=list(scratch),
        input_output_aliases=aliases or {},
        cost_estimate=pl.CostEstimate(flops=cost, bytes_accessed=1000, transcendentals=0),
        compiler_params=pltpu.CompilerParams(vmem_limit_bytes=vmem * 2**20),
    )(*[pin(value) if place in "HL" else value for value, place in ins])


DMA = pltpu.SemaphoreType.DMA


def send_copies(source, target, indices, sem):
    copies = [pltpu.make_async_copy(source, target.at[index], sem.at[index]) for index in indices]
    for copy in copies:
        copy.start()
    return copies


def wait_all(copies):
    for copy in copies:
        copy.wait()


def weight_copies(w_ref, w_buf, w_sem, parts=(1, 2, 0), start=True):
    group = group_index()
    copies = []
    for slot, part in enumerate(parts):
        column = pl.multiple_of(part * D + (group // 2) * 384, 128)
        copy = pltpu.make_async_copy(w_ref.at[:, pl.ds(column, 384)], w_buf.at[slot], w_sem.at[slot])
        if start:
            copy.start()
        copies.append(copy)
    return copies


def own_heads(full):
    odd = (group_index() % 2) == 1
    return jnp.where(odd, full[:, 192:], full[:, :192]).astype(BF)


def project_kernel(
    tok_ref, gain_ref, shift_ref, w_ref, kv_ref, normed_ref,
    x_buf, w_buf, kv_buf, gain_buf, shift_buf, x_sem, w_sem, kv_sem, gain_sem, shift_sem,
):
    copy_x = pltpu.make_async_copy(tok_ref.at[lax.axis_index(MICRO)], x_buf, x_sem)
    copy_x.start()
    copy_gain = pltpu.make_async_copy(gain_ref, gain_buf, gain_sem)
    copy_gain.start()
    copy_shift = pltpu.make_async_copy(shift_ref, shift_buf, shift_sem)
    copy_shift.start()
    copies = weight_copies(w_ref, w_buf, w_sem, (1, 2))
    wait_all([copy_x, copy_gain, copy_shift])
    unit, _ = normalized(x_buf[...].astype(F32))
    normed = (unit * gain_buf[...].reshape(1, D) + shift_buf[...].reshape(1, D)).astype(BF)
    normed_ref[...] = normed
    parts = []
    for slot in range(2):
        copies[slot].wait()
        parts.append(own_heads(mm(normed, w_buf[slot])))
    kv_buf[...] = jnp.concatenate(parts, axis=1)
    wait_all(send_copies(kv_buf, kv_ref, range(8), kv_sem))


def query_kernel(normed_ref, w_ref, q_ref, w_buf, w_sem):
    weight_copies(w_ref, w_buf, w_sem, (0,))[0].wait()
    part = own_heads(mm(normed_ref[...], w_buf[0]))
    q_ref[...] = jnp.concatenate([part, jnp.zeros((TOK, HD), BF)], axis=1)


def attend_kernel(scene_ref, q_ref, same_ref, other_ref, out_ref, buf, q_buf, sem, q_sem):
    load = pltpu.make_async_copy(q_ref, q_buf, q_sem)
    load.start()
    first, big = span(scene_ref)

    def run(count):
        rows = count * TOK
        keys = jnp.concatenate(
            [ref[pl.ds(first, count)].reshape(rows, 384) for ref in (same_ref, other_ref)], axis=0
        )
        load.wait()
        query = q_buf[...]
        q0, q1 = halves(query[:, :128])
        blocks = [keys[:, :128], keys[:, 128:256], keys[:, 256:]]
        mixed = []
        columns = []
        for qh, kb, vb in ((q0, 0, 1), (q1, 0, 2), (query[:, 128:], 1, 2)):
            scores = mm_nt(qh, blocks[kb]) * (HD**-0.5)
            top = jnp.max(scores, axis=-1, keepdims=True)
            weights = jnp.exp(scores - top)
            total = jnp.sum(weights, axis=-1, keepdims=True)
            probs = (weights * (1.0 / total)).astype(BF)
            mixed.append(mm(probs, blocks[vb]))
            columns += three(top + jnp.log(total))
        stats = put_columns(128, TOK, 0, columns)
        buf[...] = jnp.concatenate([join(stats, mixed[0]), join(mixed[1], mixed[2])], axis=1).astype(BF)

    @pl.when(big)
    def _():
        run(5)

    @pl.when(jnp.logical_not(big))
    def _():
        run(1)

    wait_all(send_copies(buf, out_ref, range(8), sem))


def forward_kernel(
    mixed_ref, tok_ref, og_ref, wo_ref, gain_ref, shift_ref, up_ref, down_ref,
    out_ref, middle_ref, normed_ref, act_ref, gpre_ref,
    tok_buf, og_buf, up_buf, down_buf, gain_buf, shift_buf, grad_buf, branch_buf, middle_buf, in_sem, sem,
):
    loads = [
        pltpu.make_async_copy(ref, buf, in_sem.at[index])
        for index, (ref, buf) in enumerate(
            (
                (tok_ref, tok_buf), (up_ref, up_buf), (og_ref, og_buf), (down_ref, down_buf), (gain_ref, gain_buf),
                (shift_ref, shift_buf),
            )
        )
    ]
    for load in loads:
        load.start()
    total = jnp.zeros((2 * TOK, D), F32)
    for group in range(4):
        rows = jnp.concatenate([mixed_ref[group], mixed_ref[4 + group]], axis=0)
        total = total + mm(rows, wo_ref[group])
    loads[0].wait()
    total = total + tok_buf[...].reshape(2 * TOK, D).astype(F32)
    middle_buf[...] = total.reshape(8, BLK, D)
    third = pltpu.make_async_copy(
        middle_buf.at[lax.axis_index(MICRO) * 4 + group_index()], middle_ref, sem.at[2]
    )
    third.start()
    unit, _ = normalized(total)
    wait_all(loads[4:])
    normed = (unit * gain_buf[...].reshape(1, D) + shift_buf[...].reshape(1, D)).astype(BF)
    normed_ref[...] = normed
    loads[1].wait()
    pre = mm(normed, up_buf[...])
    cdf = 0.5 * (1.0 + lax.erf(pre * (0.5**0.5)))
    slope = cdf + pre * jnp.exp(-0.5 * pre * pre) * 0.3989422804014327
    loads[2].wait()
    loads[3].wait()
    grad_out = og_buf[...].reshape(2 * TOK, D)
    gpre = (mm_nt(grad_out, down_buf[...]) * slope).astype(BF)
    gpre_ref[...] = gpre
    grad_buf[...] = mm_nt(gpre, up_buf[...]).astype(BF).reshape(8, BLK, D)
    first = pltpu.make_async_copy(grad_buf, out_ref.at[:, pl.ds(BLK, BLK)], sem.at[0])
    first.start()
    act = (pre * cdf).astype(BF)
    act_ref[...] = act
    branch_buf[...] = mm(act, down_buf[...]).astype(BF).reshape(8, BLK, D)
    second = pltpu.make_async_copy(branch_buf, out_ref.at[:, pl.ds(0, BLK)], sem.at[1])
    second.start()
    wait_all([first, second, third])


def ff_grads_kernel(normed_ref, act_ref, gpre_ref, og_ref, keep_ref, send_ref, up_buf, down_buf):
    core = lax.axis_index(CORE)
    up_buf[...] = mm_tn(normed_ref[...], gpre_ref[...])
    down_buf[...] = mm_tn(act_ref[...], og_ref[...].reshape(2 * TOK, D))
    for ref, owner in ((keep_ref, core), (send_ref, 1 - core)):
        column = pl.multiple_of(owner * 384, 128)
        for tile in range(8):
            rows = pl.ds(pl.multiple_of((2 * tile + owner) * 48, 16), 48)
            ref[tile, :, :384] = up_buf[rows].astype(BF)
            ref[tile, :, 384:] = down_buf[tile * 48:(tile + 1) * 48, pl.ds(column, 384)].astype(BF)


def split_kernel(one_ref, two_ref, *refs):
    y = lax.axis_index("y")
    for k, ref in enumerate(refs):
        for xl in range(2):
            at = (y ^ k) * 2 + xl
            ref[xl] = (one_ref[at].astype(F32) + two_ref[at].astype(F32)).astype(BF)


def halve_kernel(*refs):
    parts, (keep_ref, send_ref) = refs[:4], refs[4:]
    xl = lax.axis_index("xl")
    for ref, at in ((keep_ref, xl), (send_ref, 1 - xl)):
        total = parts[0][at].astype(F32)
        for part in parts[1:]:
            total = total + part[at].astype(F32)
        ref[...] = total.astype(BF)


def pair_kernel(one_ref, two_ref, out_ref):
    out_ref[...] = (one_ref[...].astype(F32) + two_ref[...].astype(F32)).astype(BF)


def middle_kernel(
    sums_ref, middle_ref, og_ref, mixed_ref, wo_ref, gain_ref,
    out_ref, low_ref, grad_ref, result_ref, vec_ref,
    buf, middle_buf, og_buf, mixed_buf, gain_buf, low_buf, grad_buf, result_buf, vec_buf, in_sem, sem, rest_sem,
):
    micro = lax.axis_index(MICRO)
    group = group_index()
    block = pl.ds(pl.multiple_of(group * BLK, BLK), BLK)
    loads = [
        pltpu.make_async_copy(middle_ref, middle_buf, in_sem.at[0]),
        pltpu.make_async_copy(og_ref.at[micro, block], og_buf, in_sem.at[1]),
        pltpu.make_async_copy(mixed_ref.at[pl.ds(micro * 4, 4), block], mixed_buf, in_sem.at[2]),
        pltpu.make_async_copy(gain_ref, gain_buf, in_sem.at[3]),
    ]
    for load in loads:
        load.start()
    total = sums_ref[0].astype(F32)
    for index in range(1, 8):
        total = total + sums_ref[index].astype(F32)
    branch, grad = total[:BLK], total[BLK:]
    wait_all(loads)
    middle = middle_buf[...]
    unit, inverse = normalized(middle)
    grad_mid = og_buf[...].astype(F32) + norm_back(grad, unit, inverse, gain_buf[...].reshape(1, D))
    low = grad_mid.astype(BF)
    low_buf[...] = low
    grad_buf[...] = grad_mid
    result_buf[...] = (middle + branch).astype(BF)
    gain_grad = jnp.sum(grad * unit, axis=0, keepdims=True)
    shift_grad = jnp.sum(grad, axis=0, keepdims=True)
    vec_buf[...] = jnp.concatenate([gain_grad, shift_grad, jnp.zeros((6, D), F32)], axis=0)
    stores = [
        pltpu.make_async_copy(source, target, rest_sem.at[index])
        for index, (source, target) in enumerate(
            ((low_buf, low_ref), (grad_buf, grad_ref), (result_buf, result_ref), (vec_buf, vec_ref))
        )
    ]
    for store in stores:
        store.start()
    lane = lax.broadcasted_iota(jnp.int32, (BLK, 256), 1)
    for head_group in range(4):
        mixed = mixed_buf[head_group].astype(F32)
        back = mm_nt(low, wo_ref[head_group]).astype(BF).astype(F32)
        product = mixed * back
        columns = []
        for head in range(3):
            inside = (lane >= (head + 1) * HD) & (lane < (head + 2) * HD)
            columns += three(jnp.sum(jnp.where(inside, product, 0.0), axis=-1, keepdims=True))
        stats = put_columns(256, BLK, 9, columns)
        buf[head_group] = jnp.where(lane < 9, mixed, jnp.where(lane < HD, stats, back)).astype(BF)
    sends = send_copies(buf, out_ref, range(8), sem)
    wait_all(stores)
    wait_all(sends)


def attend_back_kernel(
    scene_ref, kvs_ref, kvo_ref, q_ref, gs_ref, go_ref, normed_ref, mixed_ref, low_ref, low1_ref, low2_ref, low3_ref,
    w_ref, gqkv_ref, w_out_ref, keep_ref, send_ref,
    kv_buf, q_buf, grad_buf, mixed_buf, normed_buf, low_buf, kv_sem, q_sem, in_sem, w_sem,
):
    first, big = span(scene_ref)
    chip = chip_index()
    core = lax.axis_index(CORE)
    group = group_index()
    index = lax.axis_index(MICRO) * 4 + group
    first_loads = [
        pltpu.make_async_copy(source, target, in_sem.at[slot])
        for slot, (source, target) in enumerate(
            ((normed_ref, normed_buf), (mixed_ref.at[index], mixed_buf), (low_ref, low_buf))
        )
    ]
    scale = HD**-0.5

    def run(count):
        rows = count * TOK
        loads = [
            pltpu.make_async_copy(ref.at[pl.ds(first, count)], kv_buf.at[slot, pl.ds(0, count)], kv_sem.at[slot])
            for slot, ref in enumerate((kvs_ref, kvo_ref))
        ] + [
            pltpu.make_async_copy(
                q_ref.at[pl.ds(first, count), which], q_buf.at[slot, pl.ds(0, count)], q_sem.at[slot]
            )
            for slot, which in enumerate((core, 1 - core))
        ]
        for load in loads + first_loads:
            load.start()
        weight_copies(w_ref, w_out_ref, w_sem)

        def cut(value):
            return [value[:, at:at + 128] for at in range(0, value.shape[1], 128)]

        grad = cut(jnp.concatenate(
            [ref[pl.ds(first, count)].reshape(rows, 256) for ref in (gs_ref, go_ref)], axis=0
        ))
        g_own = cut(gs_ref[chip])
        g_heads = [halves(g_own[0])[1], *halves(g_own[1])]
        own_stats = g_own[0].astype(F32)
        all_stats = grad[0].astype(F32).T
        wait_all(loads)
        kv = cut(jnp.concatenate([kv_buf[slot, :count].reshape(rows, 384) for slot in range(2)], axis=0))
        query = cut(jnp.concatenate([q_buf[slot, :count].reshape(rows, 256) for slot in range(2)], axis=0))
        own = cut(kv_buf[0, chip - first]) + cut(q_buf[0, chip - first])
        q_heads = [*halves(own[3]), own[4]]
        k_heads = [*halves(own[0]), halves(own[1])[0]]
        v_heads = [halves(own[1])[1], *halves(own[2])]

        def column(at):
            return own_stats[:, at:at + 1] + own_stats[:, at + 1:at + 2] + own_stats[:, at + 2:at + 3]

        def row(at):
            return all_stats[at:at + 1] + all_stats[at + 1:at + 2] + all_stats[at + 2:at + 3]

        dq, dk, dv = [], [], []
        for head, (kb, vb) in enumerate(((0, 1), (0, 2), (1, 2))):
            qb, gb = (0, 0, 1)[head], (0, 1, 1)[head]
            probs = jnp.exp(mm_nt(q_heads[head], kv[kb]) * scale - column(3 * head))
            gap = mm_nt(g_heads[head], kv[vb]) - column(9 + 3 * head)
            dq.append(mm((probs * gap).astype(BF), kv[kb]) * scale)
            probs = jnp.exp(mm_nt(k_heads[head], query[qb]) * scale - row(3 * head))
            gap = mm_nt(v_heads[head], grad[gb]) - row(9 + 3 * head)
            dv.append(mm(probs.astype(BF), grad[gb]))
            dk.append(mm((probs * gap).astype(BF), query[qb]) * scale)
        tail = dq[2]
        gqkv_ref[...] = jnp.concatenate(
            [join(dk[0], dk[1]), join(dk[2], dv[0]), join(dv[1], dv[2]), join(dq[0], dq[1]),
             join(tail, jnp.zeros_like(tail))],
            axis=1,
        ).astype(BF)


    @pl.when(big)
    def _():
        run(5)

    @pl.when(jnp.logical_not(big))
    def _():
        run(1)

    wait_all(first_loads)

    grad_buf[...] = mm_tn(normed_buf[...], gqkv_ref[...])
    low = jnp.concatenate([ref[...] for ref in (low_buf, low1_ref, low2_ref, low3_ref)], axis=0)
    mixed = jnp.concatenate(
        [mixed_buf[pl.ds(pl.multiple_of((group ^ k) * BLK, BLK), BLK)] for k in range(4)], axis=0
    )
    out = mm_tn(mixed, low)[HD:]
    for ref, owner in ((keep_ref, core), (send_ref, 1 - core)):
        for tile in range(8):
            rows = grad_buf[pl.ds(pl.multiple_of((2 * tile + owner) * 48, 16), 48)]
            at = (tile // 4) * 96
            pieces = [
                out[at + row * 48:at + (row + 1) * 48, (tile % 4) * 192:(tile % 4 + 1) * 192] for row in range(2)
            ]
            ref[2 * tile] = rows[:, :384].astype(BF)
            ref[2 * tile + 1] = jnp.concatenate(
                [rows[:, 384:576], jnp.where(owner == 1, pieces[1], pieces[0])], axis=1
            ).astype(BF)
    wait_all(weight_copies(w_ref, w_out_ref, w_sem, start=False))


def normed_grad_kernel(
    gqkv_ref, w_ref, tok_ref, vec_ref, own_ref, one_ref, two_ref, three_ref, sums_ref,
    x_buf, vec_buf, part_buf, low_buf, sums_buf, in_sem, out_sem,
):
    loads = [
        pltpu.make_async_copy(tok_ref.at[lax.axis_index(MICRO)], x_buf, in_sem.at[0]),
        pltpu.make_async_copy(vec_ref, vec_buf, in_sem.at[1]),
    ]
    for load in loads:
        load.start()
    group = group_index()
    odd = (group % 2) == 1
    total = jnp.zeros((TOK, D), F32)
    for slot in range(3):
        part = gqkv_ref[:, slot * 192:(slot + 1) * 192]
        zero = jnp.zeros_like(part)
        wide = jnp.where(
            odd, jnp.concatenate([zero, part], axis=1), jnp.concatenate([part, zero], axis=1)
        )
        total = total + mm_nt(wide, w_ref[slot])
    part_buf[...] = total
    low_buf[...] = total.astype(BF)
    stores = []
    for k, ref in enumerate((own_ref, one_ref, two_ref, three_ref)):
        rows = pl.ds(pl.multiple_of((group ^ k) * BLK, BLK), BLK)
        stores.append(pltpu.make_async_copy((low_buf if k else part_buf).at[rows], ref, out_sem.at[k]))
        stores[-1].start()
    wait_all(loads)
    unit, _ = normalized(x_buf[...].astype(F32))
    gain1 = jnp.sum(total * unit, axis=0, keepdims=True)
    shift1 = jnp.sum(total, axis=0, keepdims=True)
    sums_buf[...] = jnp.concatenate([gain1, shift1, vec_buf[...][:2], jnp.zeros((4, D), F32)], axis=0)
    stores.append(pltpu.make_async_copy(sums_buf, sums_ref, out_sem.at[4]))
    stores[-1].start()
    wait_all(stores)


def add_kernel(one_ref, two_ref, unused_ref, out_ref, buf, sem):
    buf[...] = (one_ref[...].astype(F32) + two_ref[...].astype(F32)).astype(BF)
    copy = pltpu.make_async_copy(buf, out_ref, sem)
    copy.start()
    copy.wait()


def sum_kernel(in_ref, vec_ref, out_ref, buf, vec_buf, sem, vec_sem):
    load = pltpu.make_async_copy(vec_ref, vec_buf, vec_sem)
    load.start()
    total = in_ref[0].astype(F32)
    for index in range(1, 16):
        total = total + in_ref[index].astype(F32)
    load.wait()
    vectors = vec_buf[...][:4]
    block = jnp.concatenate([total, vectors[:, :384], vectors[:, 384:]], axis=0).astype(BF)
    for index in range(8):
        buf[index] = block
    wait_all(send_copies(buf, out_ref, range(8), sem))


def spread_kernel(turn, in_ref, *refs):
    qkv_buf, out_buf, sem, out_sem = refs[-4:]
    qkv_ref, out_ref, *vec_refs = refs[3:-4] if turn else refs[:-4]
    owner = lax.axis_index(CORE)
    owner = 1 - owner if turn else owner
    copies = []
    vectors = jnp.zeros((8, 384), F32)
    for tile in range(8):
        whole = [in_ref[tile, index].astype(F32) for index in range(8)]
        block = [value[:48] for value in whole]
        for value in whole:
            vectors = vectors + value[48:]
        for part, half, at in ((1, 0, 0), (2, 0, 192), (0, 4, 0)):
            qkv_buf[tile, :, part * D:(part + 1) * D] = jnp.concatenate(
                [block[half + group][:, at:at + 192] for group in range(4)], axis=1
            )
        start = pl.multiple_of((2 * tile + owner) * 48, 16)
        copy = pltpu.make_async_copy(qkv_buf.at[tile], qkv_ref.at[pl.ds(start, 48)], sem.at[tile])
        copy.start()
        copies.append(copy)
        for group in range(4):
            out_buf[group, tile // 4, :, (tile % 4) * 192:(tile % 4 + 1) * 192] = block[4 + group][:, 192:]
    for group in range(4):
        for pair in range(2):
            start = pl.multiple_of(group * 192 + (pair * 2 + owner) * 48, 16)
            copy = pltpu.make_async_copy(
                out_buf.at[group, pair], out_ref.at[pl.ds(start, 48)], out_sem.at[group, pair]
            )
            copy.start()
            copies.append(copy)
    if turn:
        vectors = vectors + refs[0][...]
        for k, ref in enumerate(vec_refs):
            ref[...] = jnp.concatenate([vectors[k:k + 1], vectors[4 + k:5 + k]], axis=1).reshape(D)
    else:
        vec_refs[0][...] = vectors
    wait_all(copies)


def spread_ff_kernel(in_ref, up_ref, down_ref):
    up_ref[...] = in_ref[:, :384].astype(F32)
    for tile in range(16):
        half = (tile % 2) * 384
        down_ref[(tile // 2) * 48:(tile // 2 + 1) * 48, half:half + 384] = in_ref[
            tile * 48:(tile + 1) * 48, 384:
        ].astype(F32)


def input_kernel(
    own_ref, one_ref, two_ref, three_ref, tok_ref, gain_ref, grad_ref, result_ref, unused_ref, out_ref, buf, x_buf, sem, x_sem
):
    start = pl.multiple_of(group_index() * BLK, BLK)
    load = pltpu.make_async_copy(tok_ref.at[lax.axis_index(MICRO), pl.ds(start, BLK)], x_buf, x_sem)
    load.start()
    load.wait()
    total = own_ref[...]
    for ref in (one_ref, two_ref, three_ref):
        total = total + ref[...].astype(F32)
    unit, inverse = normalized(x_buf[...].astype(F32))
    grad = grad_ref[...] + norm_back(total, unit, inverse, gain_ref[...].reshape(1, D))
    buf[:BLK] = grad.astype(BF)
    buf[BLK:] = result_ref[...]
    wait_all(send_copies(buf, out_ref, range(8), sem))


def unpack_kernel(in_ref, unused_ref, grad_ref, result_ref):
    for index in range(8):
        rows = slice(index % 4 * BLK, (index % 4 + 1) * BLK)
        grad_ref[index // 4, rows] = in_ref[index, :BLK].astype(F32)
        result_ref[index // 4, rows] = in_ref[index, BLK:]


def exchange(value, axes):
    return lax.all_to_all(value, axes, 0, 0, tiled=True)


def swap(value):
    return lax.ppermute(value, CORE, [(0, 1), (1, 0)])


def after(value, *others):
    return pl.pallas_call(
        lambda *refs: None,
        out_shape=jax.ShapeDtypeStruct(value.shape, value.dtype),
        in_specs=[pl.BlockSpec(memory_space=pl.ANY)] * (1 + len(others)),
        out_specs=pl.BlockSpec(memory_space=pl.ANY),
        input_output_aliases={0: 0},
        cost_estimate=pl.CostEstimate(flops=1, bytes_accessed=1, transcendentals=0),
        compiler_params=pltpu.CompilerParams(vmem_limit_bytes=2**20),
    )(value, *others)


def flip(value, axes, count, bits):
    return lax.ppermute(value, axes, [(index, index ^ bits) for index in range(count)])


def shards(
    tokens, scene_of_block, ln1_gain, ln1_shift, w_qkv, w_out, ln2_gain, ln2_shift, w_up, w_down, out_grad
):
    w_out_pad = jnp.pad(w_out.reshape(4, 192, D), ((0, 0), (HD, 0), (0, 0)))
    kv_send, normed = call(
        project_kernel,
        [((8, TOK, 384), BF, "H"), ((TOK, D), BF, "L")],
        [(tokens, "H"), (ln1_gain, "H"), (ln1_shift, "H"), (w_qkv, "H")],
        1000,
        [
            pltpu.VMEM((TOK, D), BF), pltpu.VMEM((2, D, 384), BF), pltpu.VMEM((TOK, 384), BF),
            pltpu.VMEM((D,), F32), pltpu.VMEM((D,), F32), DMA, DMA((2,)), DMA((8,)), DMA, DMA,
        ],
    )
    (query,) = call(
        query_kernel,
        [((TOK, 256), BF, "L")],
        [(normed, "L"), (w_qkv, "H")],
        1000,
        [pltpu.VMEM((1, D, 384), BF), DMA((1,))],
    )
    kv_same = exchange(kv_send, CHIP)
    kv_same = after(kv_same, pin(query))
    kv_other = swap(kv_same)
    (mixed_send,) = call(
        attend_kernel,
        [((8, TOK, 256), BF, "H")],
        [(scene_of_block, "S"), (query, "H"), (kv_same, "V"), (kv_other, "V")],
        1000,
        [pltpu.VMEM((TOK, 256), BF), pltpu.VMEM((TOK, 256), BF), DMA((8,)), DMA],
    )
    mixed = exchange(mixed_send, NARROW)
    queries = lax.all_gather(after(pin(query), kv_same), WIDE, axis=0, tiled=True).reshape(8, 2, TOK, 256)
    ff_send, middle, normed2, act, grad_pre = call(
        forward_kernel,
        [
            ((8, 2 * BLK, D), BF, "H"), ((BLK, D), F32, "H"), ((2 * TOK, D), BF, "V"),
            ((2 * TOK, FFL), BF, "V"), ((2 * TOK, FFL), BF, "V"),
        ],
        [
            (mixed, "V"), (tokens, "H"), (out_grad, "H"), (w_out_pad, "V"), (ln2_gain, "H"), (ln2_shift, "H"),
            (w_up, "H"), (w_down, "H"),
        ],
        1000,
        [
            pltpu.VMEM((2, TOK, D), BF), pltpu.VMEM((2, TOK, D), BF), pltpu.VMEM((D, FFL), BF),
            pltpu.VMEM((FFL, D), BF), pltpu.VMEM((D,), F32), pltpu.VMEM((D,), F32), pltpu.VMEM((8, BLK, D), BF),
            pltpu.VMEM((8, BLK, D), BF), pltpu.VMEM((8, BLK, D), F32), DMA((6,)), DMA((3,)),
        ],
    )
    ff_sums = exchange(ff_send, NARROW)
    keep, send = call(
        ff_grads_kernel,
        [((8, 48, D), BF, "V")] * 2,
        [(normed2, "V"), (act, "V"), (grad_pre, "V"), (out_grad, "L")],
        1000,
        [pltpu.VMEM((D, FFL), F32), pltpu.VMEM((FFL, D), F32)],
    )
    pieces = call(
        split_kernel, [((2, 48, D), BF, "L")] * 4, [(keep, "V"), (swap(send), "V")], 1000
    )
    pieces = [pieces[0]] + [flip(pieces[k], "y", 4, k) for k in (1, 2, 3)]
    ff_keep, ff_send = call(
        halve_kernel,
        [((48, D), BF, "L")] * 2,
        [(pieces[0], "L")] + [(piece, "V") for piece in pieces[1:]],
        1000,
    )
    ff_sums = after(ff_sums, pin(ff_keep))
    grad_send, low, grad_mid, result_part, vec2 = call(
        middle_kernel,
        [
            ((8, 4, BLK, 256), BF, "H"), ((BLK, D), BF, "H"), ((BLK, D), F32, "H"), ((BLK, D), BF, "H"),
            ((8, D), F32, "H"),
        ],
        [
            (ff_sums, "V"), (middle, "H"), (out_grad, "H"), (mixed, "H"), (w_out_pad, "V"), (ln2_gain, "H"),
        ],
        1000,
        [
            pltpu.VMEM((4, BLK, 256), BF), pltpu.VMEM((BLK, D), F32), pltpu.VMEM((BLK, D), BF),
            pltpu.VMEM((4, BLK, 256), BF), pltpu.VMEM((D,), F32), pltpu.VMEM((BLK, D), BF), pltpu.VMEM((BLK, D), F32),
            pltpu.VMEM((BLK, D), BF), pltpu.VMEM((8, D), F32), DMA((4,)), DMA((8,)), DMA((4,)),
        ],
    )
    far = flip(after(pin(ff_send), pin(low)), "xl", 2, 1)
    (ff_part,) = call(pair_kernel, [((48, D), BF, "L")], [(ff_keep, "L"), (far, "V")], 1000)
    ff_all = lax.all_gather(ff_part, WIDE, axis=0, tiled=True)
    grad_same = exchange(grad_send.reshape(32, BLK, 256), (*CHIP, *GROUP)).reshape(8, TOK, 256)
    lows = [flip(low, GROUP, 4, k) for k in (1, 2, 3)]
    grad_same = after(grad_same, *lows, pin(ff_part))
    grad_other = swap(grad_same)
    gqkv, w_own, keep, send = call(
        attend_back_kernel,
        [((TOK, 640), BF, "V"), ((3, D, 384), BF, "V")] + [((16, 48, 384), BF, "V")] * 2,
        [
            (scene_of_block, "S"), (kv_same, "H"), (kv_other, "H"), (queries, "H"), (grad_same, "V"), (grad_other, "V"),
            (normed, "H"), (mixed, "H"), (low, "H"), *[(value, "V") for value in lows], (w_qkv, "H"),
        ],
        10**9,
        [
            pltpu.VMEM((2, 5, TOK, 384), BF), pltpu.VMEM((2, 5, TOK, 256), BF), pltpu.VMEM((D, 640), F32),
            pltpu.VMEM((TOK, 256), BF), pltpu.VMEM((TOK, D), BF), pltpu.VMEM((BLK, D), BF),
            DMA((2,)), DMA((2,)), DMA((3,)), DMA((3,)),
        ],
        vmem=24,
    )
    own, *sends, sums = call(
        normed_grad_kernel,
        [((BLK, D), F32, "H")] + [((BLK, D), BF, "H")] * 3 + [((8, D), F32, "H")],
        [(gqkv, "V"), (w_own, "V"), (tokens, "H"), (vec2, "H")],
        1000,
        [
            pltpu.VMEM((TOK, D), BF), pltpu.VMEM((8, D), F32), pltpu.VMEM((TOK, D), F32), pltpu.VMEM((TOK, D), BF),
            pltpu.VMEM((8, D), F32), DMA((2,)), DMA((5,)),
        ],
    )
    (weight_send,) = call(
        add_kernel,
        [((16, 48, 384), BF, "H")],
        [(keep, "V"), (swap(send), "V"), (own, "H")],
        1000,
        [pltpu.VMEM((16, 48, 384), BF), DMA],
    )
    weight_parts = exchange(weight_send, (*CHIP, MICRO))
    parts = [flip(value, GROUP, 4, k + 1) for k, value in enumerate(sends)]
    weight_parts = after(weight_parts, pin(sums), *parts, pin(ff_all))
    (weight_total,) = call(
        sum_kernel,
        [((8, 8, 56, 384), BF, "H")],
        [(weight_parts, "V"), (sums, "H")],
        1000,
        [pltpu.VMEM((8, 56, 384), BF), pltpu.VMEM((8, D), F32), DMA((8,)), DMA],
    )
    (packed,) = call(
        input_kernel,
        [((8, 2 * BLK, D), BF, "H")],
        [
            (own, "L"), *[(value, "V") for value in parts], (tokens, "H"), (ln1_gain, "L"), (grad_mid, "L"),
            (result_part, "L"), (weight_total, "H"),
        ],
        1000,
        [pltpu.VMEM((2 * BLK, D), BF), pltpu.VMEM((BLK, D), BF), DMA((8,)), DMA],
    )
    up_grad, down_grad = call(
        spread_ff_kernel, [((D, FFL), F32, "L"), ((FFL, D), F32, "L")], [(ff_all, "L")], 1000
    )
    weight_same = exchange(weight_total.reshape(64, 56, 384), (*CHIP, *NARROW)).reshape(8, 8, 56, 384)
    weight_same = after(weight_same, pin(packed), pin(up_grad), pin(down_grad))
    everyone = exchange(after(pin(packed), weight_same), NARROW)
    weight_other = swap(weight_same)
    scratch = [
        pltpu.VMEM((8, 48, 3 * D), F32), pltpu.VMEM((4, 2, 48, D), F32), DMA((8,)), DMA((4, 2)),
    ]
    grads = [((D, 3 * D), F32, "H"), ((D, D), F32, "H")]
    half = call(
        functools.partial(spread_kernel, False),
        grads + [((8, 384), F32, "V")],
        [(weight_same, "V")],
        1000,
        scratch,
    )
    qkv_grad, out_proj_grad, *vectors = call(
        functools.partial(spread_kernel, True),
        grads + [((D,), F32, "L")] * 4,
        [(weight_other, "V"), (half[2], "V"), (half[0], "H"), (half[1], "H")],
        1000,
        scratch,
        aliases={2: 0, 3: 1},
    )
    input_grad, result = call(
        unpack_kernel, [((2, TOK, D), F32, "L"), ((2, TOK, D), BF, "L")], [(everyone, "V"), (vectors[0], "H")], 1000
    )
    return (
        result, input_grad, qkv_grad, out_proj_grad, *vectors, up_grad, down_grad
    )


def solution(mesh):
    names = ("y", "xl", "c", "zh", "zl", "xh")
    fine = Mesh(mesh.devices.reshape(4, 2, 2, 2, 2, 2), names)
    tokens = P(None, WIDE, None)
    placed = (
        tokens, P(), P(), P(), P(), P(), P(), P(), P(None, NARROW), P(NARROW, None), tokens
    )
    return jax.shard_map(
        shards,
        mesh=fine,
        in_specs=placed,
        out_specs=(
            tokens, tokens, P(), P(), P(), P(), P(), P(), P(None, NARROW), P(NARROW, None)
        ),
        check_vma=False,
    )
```

```python
import functools

import jax
import jax.numpy as jnp
from jax import lax
from jax.experimental import pallas as pl
from jax.experimental.pallas import tpu as pltpu
from jax.sharding import Mesh
from jax.sharding import PartitionSpec as P

D = 768
HD = 64
FFL = 384
TOK = 128
BLK = 32
EPS = 1e-05
BF = jnp.bfloat16
F32 = jnp.float32

CHIP = ("y", "xl")
CORE = "c"
MICRO = "zh"
GROUP = ("zl", "xh")
NARROW = (MICRO, *GROUP)
WIDE = (*CHIP, CORE)


def chip_index():
    return lax.axis_index("y") * 2 + lax.axis_index("xl")


def group_index():
    return lax.axis_index("zl") * 2 + lax.axis_index("xh")


def mm(left, right):
    return lax.dot_general(left, right, (((1,), (0,)), ((), ())), preferred_element_type=F32)


def mm_nt(left, right):
    return lax.dot_general(left, right, (((1,), (1,)), ((), ())), preferred_element_type=F32)


def mm_tn(left, right):
    return lax.dot_general(left, right, (((0,), (0,)), ((), ())), preferred_element_type=F32)


def normalized(values):
    center = values - jnp.mean(values, axis=-1, keepdims=True)
    spread = jnp.mean(center * center, axis=-1, keepdims=True)
    inverse = lax.rsqrt(spread + EPS)
    return center * inverse, inverse


def norm_back(grad, unit, inverse, gain):
    scaled = grad * gain
    first = jnp.mean(scaled, axis=-1, keepdims=True)
    second = jnp.mean(scaled * unit, axis=-1, keepdims=True)
    return inverse * (scaled - first - unit * second)


def halves(block):
    lane = lax.broadcasted_iota(jnp.int32, block.shape, 1)
    zero = jnp.zeros_like(block)
    return jnp.where(lane < HD, block, zero), jnp.where(lane < HD, zero, block)


def join(low, high):
    lane = lax.broadcasted_iota(jnp.int32, low.shape, 1)
    return jnp.where(lane < HD, low, high)


def span(scene_ref):
    micro = lax.axis_index(MICRO)
    own = scene_ref[micro, chip_index() * 4]
    first = jnp.int32(0)
    count = jnp.int32(0)
    for index in range(8):
        other = scene_ref[micro, index * 4]
        first += (other < own).astype(jnp.int32)
        count += (other == own).astype(jnp.int32)
    return first, count > 1


def three(value):
    a = value.astype(BF).astype(F32)
    b = (value - a).astype(BF).astype(F32)
    c = value - a - b
    return a, b, c


def put_columns(width, rows, start, columns):
    lane = lax.broadcasted_iota(jnp.int32, (rows, width), 1)
    out = jnp.zeros((rows, width), F32)
    for offset, column in enumerate(columns):
        out = jnp.where(lane == start + offset, column, out)
    return out


def pin(value):
    return pltpu.with_memory_space_constraint(value, pltpu.HBM)


def call(kernel, outs, ins, cost, scratch=(), vmem=16, aliases=None):
    places = {"V": pltpu.VMEM, "H": pltpu.HBM, "S": pltpu.SMEM, "L": pltpu.VMEM}
    return pl.pallas_call(
        kernel,
        out_shape=[
            (pltpu.HBM if place in "HL" else jax.ShapeDtypeStruct)(shape, dtype) for shape, dtype, place in outs
        ],
        in_specs=[pl.BlockSpec(memory_space=places[place]) for _, place in ins],
        out_specs=[pl.BlockSpec(memory_space=places[place]) for _, _, place in outs],
        scratch_shapes=list(scratch),
        input_output_aliases=aliases or {},
        cost_estimate=pl.CostEstimate(flops=cost, bytes_accessed=1000, transcendentals=0),
        compiler_params=pltpu.CompilerParams(vmem_limit_bytes=vmem * 2**20),
    )(*[pin(value) if place in "HL" else value for value, place in ins])


DMA = pltpu.SemaphoreType.DMA


def send_copies(source, target, indices, sem):
    copies = [pltpu.make_async_copy(source, target.at[index], sem.at[index]) for index in indices]
    for copy in copies:
        copy.start()
    return copies


def wait_all(copies):
    for copy in copies:
        copy.wait()


def weight_copies(w_ref, w_buf, w_sem, parts=(1, 2, 0), start=True):
    group = group_index()
    copies = []
    for slot, part in enumerate(parts):
        column = pl.multiple_of(part * D + (group // 2) * 384, 128)
        copy = pltpu.make_async_copy(w_ref.at[:, pl.ds(column, 384)], w_buf.at[slot], w_sem.at[slot])
        if start:
            copy.start()
        copies.append(copy)
    return copies


def own_heads(full):
    odd = (group_index() % 2) == 1
    return jnp.where(odd, full[:, 192:], full[:, :192]).astype(BF)


def project_kernel(
    tok_ref, gain_ref, shift_ref, w_ref, kv_ref, normed_ref,
    x_buf, w_buf, kv_buf, gain_buf, shift_buf, x_sem, w_sem, kv_sem, gain_sem, shift_sem,
):
    copy_x = pltpu.make_async_copy(tok_ref.at[lax.axis_index(MICRO)], x_buf, x_sem)
    copy_x.start()
    copy_gain = pltpu.make_async_copy(gain_ref, gain_buf, gain_sem)
    copy_gain.start()
    copy_shift = pltpu.make_async_copy(shift_ref, shift_buf, shift_sem)
    copy_shift.start()
    copies = weight_copies(w_ref, w_buf, w_sem, (1, 2))
    wait_all([copy_x, copy_gain, copy_shift])
    unit, _ = normalized(x_buf[...].astype(F32))
    normed = (unit * gain_buf[...].reshape(1, D) + shift_buf[...].reshape(1, D)).astype(BF)
    normed_ref[...] = normed
    parts = []
    for slot in range(2):
        copies[slot].wait()
        parts.append(own_heads(mm(normed, w_buf[slot])))
    kv_buf[...] = jnp.concatenate(parts, axis=1)
    wait_all(send_copies(kv_buf, kv_ref, range(8), kv_sem))


def query_kernel(normed_ref, w_ref, q_ref, w_buf, w_sem):
    weight_copies(w_ref, w_buf, w_sem, (0,))[0].wait()
    part = own_heads(mm(normed_ref[...], w_buf[0]))
    q_ref[...] = jnp.concatenate([part, jnp.zeros((TOK, HD), BF)], axis=1)


def block_query_kernel(normed_ref, w_ref, out_ref, x_buf, w_buf, x_sem, w_sem):
    block = pl.ds(pl.multiple_of(group_index() * BLK, BLK), BLK)
    loads = [
        pltpu.make_async_copy(normed_ref.at[block], x_buf, x_sem),
        pltpu.make_async_copy(w_ref.at[:, pl.ds(0, D)], w_buf, w_sem),
    ]
    for load in loads:
        load.start()
    wait_all(loads)
    query = mm(x_buf[...], w_buf[...]).astype(BF)
    zero = jnp.zeros((BLK, HD), BF)
    for group in range(4):
        out_ref[group] = jnp.concatenate([query[:, group * 192:(group + 1) * 192], zero], axis=1)


def attend_kernel(scene_ref, q_ref, same_ref, other_ref, out_ref, buf, q_buf, sem, q_sem):
    load = pltpu.make_async_copy(q_ref, q_buf, q_sem)
    load.start()
    first, big = span(scene_ref)

    def run(count):
        rows = count * TOK
        keys = jnp.concatenate(
            [ref[pl.ds(first, count)].reshape(rows, 384) for ref in (same_ref, other_ref)], axis=0
        )
        load.wait()
        query = q_buf[...]
        q0, q1 = halves(query[:, :128])
        blocks = [keys[:, :128], keys[:, 128:256], keys[:, 256:]]
        mixed = []
        columns = []
        for qh, kb, vb in ((q0, 0, 1), (q1, 0, 2), (query[:, 128:], 1, 2)):
            scores = mm_nt(qh, blocks[kb]) * (HD**-0.5)
            top = jnp.max(scores, axis=-1, keepdims=True)
            weights = jnp.exp(scores - top)
            total = jnp.sum(weights, axis=-1, keepdims=True)
            probs = (weights * (1.0 / total)).astype(BF)
            mixed.append(mm(probs, blocks[vb]))
            columns += three(top + jnp.log(total))
        stats = put_columns(128, TOK, 0, columns)
        buf[...] = jnp.concatenate([join(stats, mixed[0]), join(mixed[1], mixed[2])], axis=1).astype(BF)

    @pl.when(big)
    def _():
        run(5)

    @pl.when(jnp.logical_not(big))
    def _():
        run(1)

    wait_all(send_copies(buf, out_ref, range(8), sem))


def forward_kernel(
    mixed_ref, tok_ref, og_ref, wo_ref, gain_ref, shift_ref, up_ref, down_ref,
    out_ref, middle_ref, normed_ref, act_ref, gpre_ref,
    tok_buf, og_buf, up_buf, down_buf, gain_buf, shift_buf, grad_buf, branch_buf, middle_buf, in_sem, sem,
):
    loads = [
        pltpu.make_async_copy(ref, buf, in_sem.at[index])
        for index, (ref, buf) in enumerate(
            (
                (tok_ref, tok_buf), (up_ref, up_buf), (og_ref, og_buf), (down_ref, down_buf), (gain_ref, gain_buf),
                (shift_ref, shift_buf),
            )
        )
    ]
    for load in loads:
        load.start()
    total = jnp.zeros((2 * TOK, D), F32)
    for group in range(4):
        rows = jnp.concatenate([mixed_ref[group], mixed_ref[4 + group]], axis=0)
        total = total + mm(rows, wo_ref[group])
    loads[0].wait()
    total = total + tok_buf[...].reshape(2 * TOK, D).astype(F32)
    middle_buf[...] = total.reshape(8, BLK, D)
    third = pltpu.make_async_copy(
        middle_buf.at[lax.axis_index(MICRO) * 4 + group_index()], middle_ref, sem.at[2]
    )
    third.start()
    unit, _ = normalized(total)
    wait_all(loads[4:])
    normed = (unit * gain_buf[...].reshape(1, D) + shift_buf[...].reshape(1, D)).astype(BF)
    normed_ref[...] = normed
    loads[1].wait()
    pre = mm(normed, up_buf[...])
    cdf = 0.5 * (1.0 + lax.erf(pre * (0.5**0.5)))
    slope = cdf + pre * jnp.exp(-0.5 * pre * pre) * 0.3989422804014327
    loads[2].wait()
    loads[3].wait()
    grad_out = og_buf[...].reshape(2 * TOK, D)
    gpre = (mm_nt(grad_out, down_buf[...]) * slope).astype(BF)
    gpre_ref[...] = gpre
    grad_buf[...] = mm_nt(gpre, up_buf[...]).astype(BF).reshape(8, BLK, D)
    first = pltpu.make_async_copy(grad_buf, out_ref.at[:, pl.ds(BLK, BLK)], sem.at[0])
    first.start()
    act = (pre * cdf).astype(BF)
    act_ref[...] = act
    branch_buf[...] = mm(act, down_buf[...]).astype(BF).reshape(8, BLK, D)
    second = pltpu.make_async_copy(branch_buf, out_ref.at[:, pl.ds(0, BLK)], sem.at[1])
    second.start()
    wait_all([first, second, third])


def ff_grads_kernel(normed_ref, act_ref, gpre_ref, og_ref, keep_ref, send_ref, up_buf, down_buf):
    core = lax.axis_index(CORE)
    up_buf[...] = mm_tn(normed_ref[...], gpre_ref[...])
    down_buf[...] = mm_tn(act_ref[...], og_ref[...].reshape(2 * TOK, D))
    for ref, owner in ((keep_ref, core), (send_ref, 1 - core)):
        column = pl.multiple_of(owner * 384, 128)
        for tile in range(8):
            rows = pl.ds(pl.multiple_of((2 * tile + owner) * 48, 16), 48)
            ref[tile, :, :384] = up_buf[rows].astype(BF)
            ref[tile, :, 384:] = down_buf[tile * 48:(tile + 1) * 48, pl.ds(column, 384)].astype(BF)


def split_kernel(one_ref, two_ref, *refs):
    y = lax.axis_index("y")
    for k, ref in enumerate(refs):
        for xl in range(2):
            at = (y ^ k) * 2 + xl
            ref[xl] = (one_ref[at].astype(F32) + two_ref[at].astype(F32)).astype(BF)


def halve_kernel(*refs):
    parts, (keep_ref, send_ref) = refs[:4], refs[4:]
    xl = lax.axis_index("xl")
    for ref, at in ((keep_ref, xl), (send_ref, 1 - xl)):
        total = parts[0][at].astype(F32)
        for part in parts[1:]:
            total = total + part[at].astype(F32)
        ref[...] = total.astype(BF)


def pair_kernel(one_ref, two_ref, out_ref):
    out_ref[...] = (one_ref[...].astype(F32) + two_ref[...].astype(F32)).astype(BF)


def middle_kernel(
    sums_ref, middle_ref, og_ref, mixed_ref, wo_ref, gain_ref, query_ref,
    out_ref, low_ref, grad_ref, result_ref, vec_ref,
    buf, middle_buf, og_buf, mixed_buf, gain_buf, query_buf, low_buf, grad_buf, result_buf, vec_buf, in_sem, sem, rest_sem,
):
    micro = lax.axis_index(MICRO)
    group = group_index()
    block = pl.ds(pl.multiple_of(group * BLK, BLK), BLK)
    loads = [
        pltpu.make_async_copy(middle_ref, middle_buf, in_sem.at[0]),
        pltpu.make_async_copy(og_ref.at[micro, block], og_buf, in_sem.at[1]),
        pltpu.make_async_copy(mixed_ref.at[pl.ds(micro * 4, 4), block], mixed_buf, in_sem.at[2]),
        pltpu.make_async_copy(gain_ref, gain_buf, in_sem.at[3]),
        pltpu.make_async_copy(query_ref, query_buf, in_sem.at[4]),
    ]
    for load in loads:
        load.start()
    total = sums_ref[0].astype(F32)
    for index in range(1, 8):
        total = total + sums_ref[index].astype(F32)
    branch, grad = total[:BLK], total[BLK:]
    wait_all(loads)
    middle = middle_buf[...]
    unit, inverse = normalized(middle)
    grad_mid = og_buf[...].astype(F32) + norm_back(grad, unit, inverse, gain_buf[...].reshape(1, D))
    low = grad_mid.astype(BF)
    low_buf[...] = low
    grad_buf[...] = grad_mid
    result_buf[...] = (middle + branch).astype(BF)
    gain_grad = jnp.sum(grad * unit, axis=0, keepdims=True)
    shift_grad = jnp.sum(grad, axis=0, keepdims=True)
    vec_buf[...] = jnp.concatenate([gain_grad, shift_grad, jnp.zeros((6, D), F32)], axis=0)
    stores = [
        pltpu.make_async_copy(source, target, rest_sem.at[index])
        for index, (source, target) in enumerate(
            ((low_buf, low_ref), (grad_buf, grad_ref), (result_buf, result_ref), (vec_buf, vec_ref))
        )
    ]
    for store in stores:
        store.start()
    lane = lax.broadcasted_iota(jnp.int32, (BLK, 256), 1)
    for head_group in range(4):
        mixed = mixed_buf[head_group].astype(F32)
        back = mm_nt(low, wo_ref[head_group]).astype(BF).astype(F32)
        product = mixed * back
        columns = []
        for head in range(3):
            inside = (lane >= (head + 1) * HD) & (lane < (head + 2) * HD)
            columns += three(jnp.sum(jnp.where(inside, product, 0.0), axis=-1, keepdims=True))
        stats = put_columns(256, BLK, 9, columns)
        buf[head_group, :, :256] = jnp.where(lane < 9, mixed, jnp.where(lane < HD, stats, back)).astype(BF)
        buf[head_group, :, 256:] = query_buf[head_group]
    sends = send_copies(buf, out_ref, range(8), sem)
    wait_all(stores)
    wait_all(sends)


def attend_back_kernel(
    scene_ref, kvs_ref, kvo_ref, gs_ref, go_ref, normed_ref, mixed_ref, low_ref, low1_ref, low2_ref, low3_ref,
    w_ref, gqkv_ref, w_out_ref, keep_ref, send_ref,
    kv_buf, grad_buf, mixed_buf, normed_buf, low_buf, kv_sem, in_sem, w_sem,
):
    first, big = span(scene_ref)
    chip = chip_index()
    core = lax.axis_index(CORE)
    group = group_index()
    index = lax.axis_index(MICRO) * 4 + group
    first_loads = [
        pltpu.make_async_copy(source, target, in_sem.at[slot])
        for slot, (source, target) in enumerate(
            ((normed_ref, normed_buf), (mixed_ref.at[index], mixed_buf), (low_ref, low_buf))
        )
    ]
    scale = HD**-0.5

    def run(count):
        rows = count * TOK
        loads = [
            pltpu.make_async_copy(ref.at[pl.ds(first, count)], kv_buf.at[slot, pl.ds(0, count)], kv_sem.at[slot])
            for slot, ref in enumerate((kvs_ref, kvo_ref))
        ]
        for load in loads + first_loads:
            load.start()
        weight_copies(w_ref, w_out_ref, w_sem)

        def cut(value):
            return [value[:, at:at + 128] for at in range(0, value.shape[1], 128)]

        every = cut(jnp.concatenate(
            [ref[pl.ds(first, count)].reshape(rows, 512) for ref in (gs_ref, go_ref)], axis=0
        ))
        grad, query = every[:2], every[2:]
        g_own = cut(gs_ref[chip])
        g_heads = [halves(g_own[0])[1], *halves(g_own[1])]
        own_stats = g_own[0].astype(F32)
        all_stats = grad[0].astype(F32).T
        wait_all(loads)
        kv = cut(jnp.concatenate([kv_buf[slot, :count].reshape(rows, 384) for slot in range(2)], axis=0))
        own = cut(kv_buf[0, chip - first]) + g_own[2:]
        q_heads = [*halves(own[3]), own[4]]
        k_heads = [*halves(own[0]), halves(own[1])[0]]
        v_heads = [halves(own[1])[1], *halves(own[2])]

        def column(at):
            return own_stats[:, at:at + 1] + own_stats[:, at + 1:at + 2] + own_stats[:, at + 2:at + 3]

        def row(at):
            return all_stats[at:at + 1] + all_stats[at + 1:at + 2] + all_stats[at + 2:at + 3]

        dq, dk, dv = [], [], []
        for head, (kb, vb) in enumerate(((0, 1), (0, 2), (1, 2))):
            qb, gb = (0, 0, 1)[head], (0, 1, 1)[head]
            probs = jnp.exp(mm_nt(q_heads[head], kv[kb]) * scale - column(3 * head))
            gap = mm_nt(g_heads[head], kv[vb]) - column(9 + 3 * head)
            dq.append(mm((probs * gap).astype(BF), kv[kb]) * scale)
            probs = jnp.exp(mm_nt(k_heads[head], query[qb]) * scale - row(3 * head))
            gap = mm_nt(v_heads[head], grad[gb]) - row(9 + 3 * head)
            dv.append(mm(probs.astype(BF), grad[gb]))
            dk.append(mm((probs * gap).astype(BF), query[qb]) * scale)
        tail = dq[2]
        gqkv_ref[...] = jnp.concatenate(
            [join(dk[0], dk[1]), join(dk[2], dv[0]), join(dv[1], dv[2]), join(dq[0], dq[1]),
             join(tail, jnp.zeros_like(tail))],
            axis=1,
        ).astype(BF)


    @pl.when(big)
    def _():
        run(5)

    @pl.when(jnp.logical_not(big))
    def _():
        run(1)

    wait_all(first_loads)

    grad_buf[...] = mm_tn(normed_buf[...], gqkv_ref[...])
    low = jnp.concatenate([ref[...] for ref in (low_buf, low1_ref, low2_ref, low3_ref)], axis=0)
    mixed = jnp.concatenate(
        [mixed_buf[pl.ds(pl.multiple_of((group ^ k) * BLK, BLK), BLK)] for k in range(4)], axis=0
    )
    out = mm_tn(mixed, low)[HD:]
    for ref, owner in ((keep_ref, core), (send_ref, 1 - core)):
        for tile in range(8):
            rows = grad_buf[pl.ds(pl.multiple_of((2 * tile + owner) * 48, 16), 48)]
            at = (tile // 4) * 96
            pieces = [
                out[at + row * 48:at + (row + 1) * 48, (tile % 4) * 192:(tile % 4 + 1) * 192] for row in range(2)
            ]
            ref[2 * tile] = rows[:, :384].astype(BF)
            ref[2 * tile + 1] = jnp.concatenate(
                [rows[:, 384:576], jnp.where(owner == 1, pieces[1], pieces[0])], axis=1
            ).astype(BF)
    wait_all(weight_copies(w_ref, w_out_ref, w_sem, start=False))


def normed_grad_kernel(
    gqkv_ref, w_ref, tok_ref, vec_ref, own_ref, one_ref, two_ref, three_ref, sums_ref,
    x_buf, vec_buf, part_buf, low_buf, sums_buf, in_sem, out_sem,
):
    loads = [
        pltpu.make_async_copy(tok_ref.at[lax.axis_index(MICRO)], x_buf, in_sem.at[0]),
        pltpu.make_async_copy(vec_ref, vec_buf, in_sem.at[1]),
    ]
    for load in loads:
        load.start()
    group = group_index()
    odd = (group % 2) == 1
    total = jnp.zeros((TOK, D), F32)
    for slot in range(3):
        part = gqkv_ref[:, slot * 192:(slot + 1) * 192]
        zero = jnp.zeros_like(part)
        wide = jnp.where(
            odd, jnp.concatenate([zero, part], axis=1), jnp.concatenate([part, zero], axis=1)
        )
        total = total + mm_nt(wide, w_ref[slot])
    part_buf[...] = total
    low_buf[...] = total.astype(BF)
    stores = []
    for k, ref in enumerate((own_ref, one_ref, two_ref, three_ref)):
        rows = pl.ds(pl.multiple_of((group ^ k) * BLK, BLK), BLK)
        stores.append(pltpu.make_async_copy((low_buf if k else part_buf).at[rows], ref, out_sem.at[k]))
        stores[-1].start()
    wait_all(loads)
    unit, _ = normalized(x_buf[...].astype(F32))
    gain1 = jnp.sum(total * unit, axis=0, keepdims=True)
    shift1 = jnp.sum(total, axis=0, keepdims=True)
    sums_buf[...] = jnp.concatenate([gain1, shift1, vec_buf[...][:2], jnp.zeros((4, D), F32)], axis=0)
    stores.append(pltpu.make_async_copy(sums_buf, sums_ref, out_sem.at[4]))
    stores[-1].start()
    wait_all(stores)


def add_kernel(one_ref, two_ref, unused_ref, out_ref, buf, sem):
    buf[...] = (one_ref[...].astype(F32) + two_ref[...].astype(F32)).astype(BF)
    copy = pltpu.make_async_copy(buf, out_ref, sem)
    copy.start()
    copy.wait()


def sum_kernel(in_ref, vec_ref, out_ref, buf, vec_buf, sem, vec_sem):
    load = pltpu.make_async_copy(vec_ref, vec_buf, vec_sem)
    load.start()
    total = in_ref[0].astype(F32)
    for index in range(1, 16):
        total = total + in_ref[index].astype(F32)
    load.wait()
    vectors = vec_buf[...][:4]
    block = jnp.concatenate([total, vectors[:, :384], vectors[:, 384:]], axis=0).astype(BF)
    for index in range(8):
        buf[index] = block
    wait_all(send_copies(buf, out_ref, range(8), sem))


def spread_kernel(turn, in_ref, *refs):
    qkv_buf, out_buf, sem, out_sem = refs[-4:]
    qkv_ref, out_ref, *vec_refs = refs[3:-4] if turn else refs[:-4]
    owner = lax.axis_index(CORE)
    owner = 1 - owner if turn else owner
    copies = []
    vectors = jnp.zeros((8, 384), F32)
    for tile in range(8):
        whole = [in_ref[tile, index].astype(F32) for index in range(8)]
        block = [value[:48] for value in whole]
        for value in whole:
            vectors = vectors + value[48:]
        for part, half, at in ((1, 0, 0), (2, 0, 192), (0, 4, 0)):
            qkv_buf[tile, :, part * D:(part + 1) * D] = jnp.concatenate(
                [block[half + group][:, at:at + 192] for group in range(4)], axis=1
            )
        start = pl.multiple_of((2 * tile + owner) * 48, 16)
        copy = pltpu.make_async_copy(qkv_buf.at[tile], qkv_ref.at[pl.ds(start, 48)], sem.at[tile])
        copy.start()
        copies.append(copy)
        for group in range(4):
            out_buf[group, tile // 4, :, (tile % 4) * 192:(tile % 4 + 1) * 192] = block[4 + group][:, 192:]
    for group in range(4):
        for pair in range(2):
            start = pl.multiple_of(group * 192 + (pair * 2 + owner) * 48, 16)
            copy = pltpu.make_async_copy(
                out_buf.at[group, pair], out_ref.at[pl.ds(start, 48)], out_sem.at[group, pair]
            )
            copy.start()
            copies.append(copy)
    if turn:
        vectors = vectors + refs[0][...]
        for k, ref in enumerate(vec_refs):
            ref[...] = jnp.concatenate([vectors[k:k + 1], vectors[4 + k:5 + k]], axis=1).reshape(D)
    else:
        vec_refs[0][...] = vectors
    wait_all(copies)


def stack_kernel(*refs):
    y = lax.axis_index("y")
    for k, ref in enumerate(refs[:4]):
        refs[4][y ^ k] = ref[...]


def spread_ff_kernel(*refs):
    up_ref, down_ref = refs[4:]
    xl, core = lax.axis_index("xl"), lax.axis_index(CORE)
    for index, ref in enumerate(refs[:4]):
        chip_xl = xl ^ (index % 2)
        owner = core ^ (index // 2)
        for y in range(4):
            chip = y * 2 + chip_xl
            block = ref[y].astype(F32)
            up_ref[pl.ds(pl.multiple_of((chip * 2 + owner) * 48, 16), 48)] = block[:, :384]
            down_ref[
                pl.ds(pl.multiple_of(chip * 48, 16), 48), pl.ds(pl.multiple_of(owner * 384, 128), 384)
            ] = block[:, 384:]


def input_kernel(
    own_ref, one_ref, two_ref, three_ref, tok_ref, gain_ref, grad_ref, result_ref, unused_ref, out_ref, buf, x_buf, sem, x_sem
):
    start = pl.multiple_of(group_index() * BLK, BLK)
    load = pltpu.make_async_copy(tok_ref.at[lax.axis_index(MICRO), pl.ds(start, BLK)], x_buf, x_sem)
    load.start()
    load.wait()
    total = own_ref[...]
    for ref in (one_ref, two_ref, three_ref):
        total = total + ref[...].astype(F32)
    unit, inverse = normalized(x_buf[...].astype(F32))
    grad = grad_ref[...] + norm_back(total, unit, inverse, gain_ref[...].reshape(1, D))
    buf[:BLK] = grad.astype(BF)
    buf[BLK:] = result_ref[...]
    wait_all(send_copies(buf, out_ref, range(8), sem))


def unpack_kernel(in_ref, unused_ref, other_ref, grad_ref, result_ref):
    for index in range(8):
        rows = slice(index % 4 * BLK, (index % 4 + 1) * BLK)
        grad_ref[index // 4, rows] = in_ref[index, :BLK].astype(F32)
        result_ref[index // 4, rows] = in_ref[index, BLK:]


def exchange(value, axes):
    return lax.all_to_all(value, axes, 0, 0, tiled=True)


def swap(value):
    return lax.ppermute(value, CORE, [(0, 1), (1, 0)])


def after(value, *others):
    return pl.pallas_call(
        lambda *refs: None,
        out_shape=jax.ShapeDtypeStruct(value.shape, value.dtype),
        in_specs=[pl.BlockSpec(memory_space=pl.ANY)] * (1 + len(others)),
        out_specs=pl.BlockSpec(memory_space=pl.ANY),
        input_output_aliases={0: 0},
        cost_estimate=pl.CostEstimate(flops=1, bytes_accessed=1, transcendentals=0),
        compiler_params=pltpu.CompilerParams(vmem_limit_bytes=2**20),
    )(value, *others)


def flip(value, axes, count, bits):
    return lax.ppermute(value, axes, [(index, index ^ bits) for index in range(count)])


def shards(
    tokens, scene_of_block, ln1_gain, ln1_shift, w_qkv, w_out, ln2_gain, ln2_shift, w_up, w_down, out_grad
):
    w_out_pad = jnp.pad(w_out.reshape(4, 192, D), ((0, 0), (HD, 0), (0, 0)))
    kv_send, normed = call(
        project_kernel,
        [((8, TOK, 384), BF, "H"), ((TOK, D), BF, "L")],
        [(tokens, "H"), (ln1_gain, "H"), (ln1_shift, "H"), (w_qkv, "H")],
        1000,
        [
            pltpu.VMEM((TOK, D), BF), pltpu.VMEM((2, D, 384), BF), pltpu.VMEM((TOK, 384), BF),
            pltpu.VMEM((D,), F32), pltpu.VMEM((D,), F32), DMA, DMA((2,)), DMA((8,)), DMA, DMA,
        ],
    )
    (query,) = call(
        query_kernel,
        [((TOK, 256), BF, "L")],
        [(normed, "L"), (w_qkv, "H")],
        1000,
        [pltpu.VMEM((1, D, 384), BF), DMA((1,))],
    )
    kv_same = exchange(kv_send, CHIP)
    kv_same = after(kv_same, pin(query))
    kv_other = swap(kv_same)
    (mixed_send,) = call(
        attend_kernel,
        [((8, TOK, 256), BF, "H")],
        [(scene_of_block, "S"), (query, "H"), (kv_same, "V"), (kv_other, "V")],
        1000,
        [pltpu.VMEM((TOK, 256), BF), pltpu.VMEM((TOK, 256), BF), DMA((8,)), DMA],
    )
    mixed = exchange(mixed_send, NARROW)
    (block_query,) = call(
        block_query_kernel,
        [((4, BLK, 256), BF, "L")],
        [(normed, "H"), (w_qkv, "H")],
        1000,
        [pltpu.VMEM((BLK, D), BF), pltpu.VMEM((D, D), BF), DMA, DMA],
    )
    ff_send, middle, normed2, act, grad_pre = call(
        forward_kernel,
        [
            ((8, 2 * BLK, D), BF, "H"), ((BLK, D), F32, "H"), ((2 * TOK, D), BF, "V"),
            ((2 * TOK, FFL), BF, "V"), ((2 * TOK, FFL), BF, "V"),
        ],
        [
            (mixed, "V"), (tokens, "H"), (out_grad, "H"), (w_out_pad, "V"), (ln2_gain, "H"), (ln2_shift, "H"),
            (w_up, "H"), (w_down, "H"),
        ],
        1000,
        [
            pltpu.VMEM((2, TOK, D), BF), pltpu.VMEM((2, TOK, D), BF), pltpu.VMEM((D, FFL), BF),
            pltpu.VMEM((FFL, D), BF), pltpu.VMEM((D,), F32), pltpu.VMEM((D,), F32), pltpu.VMEM((8, BLK, D), BF),
            pltpu.VMEM((8, BLK, D), BF), pltpu.VMEM((8, BLK, D), F32), DMA((6,)), DMA((3,)),
        ],
    )
    ff_sums = exchange(ff_send, NARROW)
    keep, send = call(
        ff_grads_kernel,
        [((8, 48, D), BF, "V")] * 2,
        [(normed2, "V"), (act, "V"), (grad_pre, "V"), (out_grad, "L")],
        1000,
        [pltpu.VMEM((D, FFL), F32), pltpu.VMEM((FFL, D), F32)],
    )
    pieces = call(
        split_kernel, [((2, 48, D), BF, "L")] * 4, [(keep, "V"), (swap(send), "V")], 1000
    )
    pieces = [pieces[0]] + [flip(pieces[k], "y", 4, k) for k in (1, 2, 3)]
    ff_keep, ff_send = call(
        halve_kernel,
        [((48, D), BF, "L")] * 2,
        [(pieces[0], "L")] + [(piece, "V") for piece in pieces[1:]],
        1000,
    )
    ff_sums = after(ff_sums, pin(ff_keep))
    grad_send, low, grad_mid, result_part, vec2 = call(
        middle_kernel,
        [
            ((8, 4, BLK, 512), BF, "H"), ((BLK, D), BF, "H"), ((BLK, D), F32, "H"), ((BLK, D), BF, "H"),
            ((8, D), F32, "H"),
        ],
        [
            (ff_sums, "V"), (middle, "H"), (out_grad, "H"), (mixed, "H"), (w_out_pad, "V"), (ln2_gain, "H"),
            (block_query, "H"),
        ],
        1000,
        [
            pltpu.VMEM((4, BLK, 512), BF), pltpu.VMEM((BLK, D), F32), pltpu.VMEM((BLK, D), BF),
            pltpu.VMEM((4, BLK, 256), BF), pltpu.VMEM((D,), F32), pltpu.VMEM((4, BLK, 256), BF), pltpu.VMEM((BLK, D), BF), pltpu.VMEM((BLK, D), F32),
            pltpu.VMEM((BLK, D), BF), pltpu.VMEM((8, D), F32), DMA((5,)), DMA((8,)), DMA((4,)),
        ],
    )
    far = flip(after(pin(ff_send), pin(low)), "xl", 2, 1)
    (ff_part,) = call(pair_kernel, [((48, D), BF, "L")], [(ff_keep, "L"), (far, "V")], 1000)
    ff_parts = [flip(ff_part, "y", 4, k) for k in (1, 2, 3)]
    grad_same = exchange(grad_send.reshape(32, BLK, 512), (*CHIP, *GROUP)).reshape(8, TOK, 512)
    lows = [flip(low, GROUP, 4, k) for k in (1, 2, 3)]
    grad_same = after(grad_same, *lows, pin(ff_part))
    grad_other = swap(grad_same)
    gqkv, w_own, keep, send = call(
        attend_back_kernel,
        [((TOK, 640), BF, "V"), ((3, D, 384), BF, "V")] + [((16, 48, 384), BF, "V")] * 2,
        [
            (scene_of_block, "S"), (kv_same, "H"), (kv_other, "H"), (grad_same, "V"), (grad_other, "V"),
            (normed, "H"), (mixed, "H"), (low, "H"), *[(value, "V") for value in lows], (w_qkv, "H"),
        ],
        10**9,
        [
            pltpu.VMEM((2, 5, TOK, 384), BF), pltpu.VMEM((D, 640), F32),
            pltpu.VMEM((TOK, 256), BF), pltpu.VMEM((TOK, D), BF), pltpu.VMEM((BLK, D), BF),
            DMA((2,)), DMA((3,)), DMA((3,)),
        ],
        vmem=24,
    )
    own, *sends, sums = call(
        normed_grad_kernel,
        [((BLK, D), F32, "H")] + [((BLK, D), BF, "H")] * 3 + [((8, D), F32, "H")],
        [(gqkv, "V"), (w_own, "V"), (tokens, "H"), (vec2, "H")],
        1000,
        [
            pltpu.VMEM((TOK, D), BF), pltpu.VMEM((8, D), F32), pltpu.VMEM((TOK, D), F32), pltpu.VMEM((TOK, D), BF),
            pltpu.VMEM((8, D), F32), DMA((2,)), DMA((5,)),
        ],
    )
    (weight_send,) = call(
        add_kernel,
        [((16, 48, 384), BF, "H")],
        [(keep, "V"), (swap(send), "V"), (own, "H")],
        1000,
        [pltpu.VMEM((16, 48, 384), BF), DMA],
    )
    weight_parts = exchange(weight_send, (*CHIP, MICRO))
    parts = [flip(value, GROUP, 4, k + 1) for k, value in enumerate(sends)]
    weight_parts = after(weight_parts, pin(sums), *parts, *ff_parts)
    (weight_total,) = call(
        sum_kernel,
        [((8, 8, 56, 384), BF, "H")],
        [(weight_parts, "V"), (sums, "H")],
        1000,
        [pltpu.VMEM((8, 56, 384), BF), pltpu.VMEM((8, D), F32), DMA((8,)), DMA],
    )
    (packed,) = call(
        input_kernel,
        [((8, 2 * BLK, D), BF, "H")],
        [
            (own, "L"), *[(value, "V") for value in parts], (tokens, "H"), (ln1_gain, "L"), (grad_mid, "L"),
            (result_part, "L"), (weight_total, "H"),
        ],
        1000,
        [pltpu.VMEM((2 * BLK, D), BF), pltpu.VMEM((BLK, D), BF), DMA((8,)), DMA],
    )
    (ff_near,) = call(
        stack_kernel,
        [((4, 48, D), BF, "L")],
        [(ff_part, "L"), *[(value, "V") for value in ff_parts]],
        1000,
    )
    ff_far = flip(ff_near, "xl", 2, 1)
    weight_same = exchange(weight_total.reshape(64, 56, 384), (*CHIP, *NARROW)).reshape(8, 8, 56, 384)
    weight_same = after(weight_same, pin(packed), ff_far)
    everyone = exchange(after(pin(packed), weight_same), NARROW)
    weight_other = swap(weight_same)
    up_grad, down_grad = call(
        spread_ff_kernel,
        [((D, FFL), F32, "L"), ((FFL, D), F32, "L")],
        [(ff_near, "L"), (ff_far, "V"), (swap(ff_near), "V"), (swap(ff_far), "V")],
        1000,
    )
    scratch = [
        pltpu.VMEM((8, 48, 3 * D), F32), pltpu.VMEM((4, 2, 48, D), F32), DMA((8,)), DMA((4, 2)),
    ]
    grads = [((D, 3 * D), F32, "H"), ((D, D), F32, "H")]
    half = call(
        functools.partial(spread_kernel, False),
        grads + [((8, 384), F32, "V")],
        [(weight_same, "V")],
        1000,
        scratch,
    )
    qkv_grad, out_proj_grad, *vectors = call(
        functools.partial(spread_kernel, True),
        grads + [((D,), F32, "L")] * 4,
        [(weight_other, "V"), (half[2], "V"), (half[0], "H"), (half[1], "H")],
        1000,
        scratch,
        aliases={2: 0, 3: 1},
    )
    input_grad, result = call(
        unpack_kernel, [((2, TOK, D), F32, "L"), ((2, TOK, D), BF, "L")], [(everyone, "V"), (vectors[0], "H"), (up_grad, "H")], 1000
    )
    return (
        result, input_grad, qkv_grad, out_proj_grad, *vectors, up_grad, down_grad
    )


def solution(mesh):
    names = ("y", "xl", "c", "zh", "zl", "xh")
    fine = Mesh(mesh.devices.reshape(4, 2, 2, 2, 2, 2), names)
    tokens = P(None, WIDE, None)
    placed = (
        tokens, P(), P(), P(), P(), P(), P(), P(), P(None, NARROW), P(NARROW, None), tokens
    )
    return jax.shard_map(
        shards,
        mesh=fine,
        in_specs=placed,
        out_specs=(
            tokens, tokens, P(), P(), P(), P(), P(), P(), P(None, NARROW), P(NARROW, None)
        ),
        check_vma=False,
    )
```

```python
import functools

import jax
import jax.numpy as jnp
from jax import lax
from jax.experimental import pallas as pl
from jax.experimental.pallas import tpu as pltpu
from jax.sharding import Mesh
from jax.sharding import PartitionSpec as P

D = 768
HD = 64
FFL = 384
TOK = 128
BLK = 32
EPS = 1e-05
BF = jnp.bfloat16
F32 = jnp.float32

CHIP = ("y", "xl")
CORE = "c"
MICRO = "zh"
GROUP = ("zl", "xh")
NARROW = (MICRO, *GROUP)
WIDE = (*CHIP, CORE)


def chip_index():
    return lax.axis_index("y") * 2 + lax.axis_index("xl")


def group_index():
    return lax.axis_index("zl") * 2 + lax.axis_index("xh")


def mm(left, right):
    return lax.dot_general(left, right, (((1,), (0,)), ((), ())), preferred_element_type=F32)


def mm_nt(left, right):
    return lax.dot_general(left, right, (((1,), (1,)), ((), ())), preferred_element_type=F32)


def mm_tn(left, right):
    return lax.dot_general(left, right, (((0,), (0,)), ((), ())), preferred_element_type=F32)


def normalized(values):
    center = values - jnp.mean(values, axis=-1, keepdims=True)
    spread = jnp.mean(center * center, axis=-1, keepdims=True)
    inverse = lax.rsqrt(spread + EPS)
    return center * inverse, inverse


def norm_back(grad, unit, inverse, gain):
    scaled = grad * gain
    first = jnp.mean(scaled, axis=-1, keepdims=True)
    second = jnp.mean(scaled * unit, axis=-1, keepdims=True)
    return inverse * (scaled - first - unit * second)


def halves(block):
    lane = lax.broadcasted_iota(jnp.int32, block.shape, 1)
    zero = jnp.zeros_like(block)
    return jnp.where(lane < HD, block, zero), jnp.where(lane < HD, zero, block)


def join(low, high):
    lane = lax.broadcasted_iota(jnp.int32, low.shape, 1)
    return jnp.where(lane < HD, low, high)


def span(scene_ref):
    micro = lax.axis_index(MICRO)
    own = scene_ref[micro, chip_index() * 4]
    first = jnp.int32(0)
    count = jnp.int32(0)
    for index in range(8):
        other = scene_ref[micro, index * 4]
        first += (other < own).astype(jnp.int32)
        count += (other == own).astype(jnp.int32)
    return first, count > 1


def three(value):
    a = value.astype(BF).astype(F32)
    b = (value - a).astype(BF).astype(F32)
    c = value - a - b
    return a, b, c


def put_columns(width, rows, start, columns):
    lane = lax.broadcasted_iota(jnp.int32, (rows, width), 1)
    out = jnp.zeros((rows, width), F32)
    for offset, column in enumerate(columns):
        out = jnp.where(lane == start + offset, column, out)
    return out


def pin(value):
    return pltpu.with_memory_space_constraint(value, pltpu.HBM)


def call(kernel, outs, ins, cost, scratch=(), vmem=16, aliases=None):
    places = {"V": pltpu.VMEM, "H": pltpu.HBM, "S": pltpu.SMEM, "L": pltpu.VMEM}
    return pl.pallas_call(
        kernel,
        out_shape=[
            (pltpu.HBM if place in "HL" else jax.ShapeDtypeStruct)(shape, dtype) for shape, dtype, place in outs
        ],
        in_specs=[pl.BlockSpec(memory_space=places[place]) for _, place in ins],
        out_specs=[pl.BlockSpec(memory_space=places[place]) for _, _, place in outs],
        scratch_shapes=list(scratch),
        input_output_aliases=aliases or {},
        cost_estimate=pl.CostEstimate(flops=cost, bytes_accessed=1000, transcendentals=0),
        compiler_params=pltpu.CompilerParams(vmem_limit_bytes=vmem * 2**20),
    )(*[pin(value) if place in "HL" else value for value, place in ins])


DMA = pltpu.SemaphoreType.DMA


def send_copies(source, target, indices, sem):
    copies = [pltpu.make_async_copy(source, target.at[index], sem.at[index]) for index in indices]
    for copy in copies:
        copy.start()
    return copies


def wait_all(copies):
    for copy in copies:
        copy.wait()


def weight_copies(w_ref, w_buf, w_sem, parts=(1, 2, 0), start=True):
    group = group_index()
    copies = []
    for slot, part in enumerate(parts):
        column = pl.multiple_of(part * D + (group // 2) * 384, 128)
        copy = pltpu.make_async_copy(w_ref.at[:, pl.ds(column, 384)], w_buf.at[slot], w_sem.at[slot])
        if start:
            copy.start()
        copies.append(copy)
    return copies


def own_heads(full):
    odd = (group_index() % 2) == 1
    return jnp.where(odd, full[:, 192:], full[:, :192]).astype(BF)


def project_kernel(
    tok_ref, gain_ref, shift_ref, w_ref, kv_ref, normed_ref,
    x_buf, w_buf, kv_buf, gain_buf, shift_buf, x_sem, w_sem, kv_sem, gain_sem, shift_sem,
):
    copy_x = pltpu.make_async_copy(tok_ref.at[lax.axis_index(MICRO)], x_buf, x_sem)
    copy_x.start()
    copy_gain = pltpu.make_async_copy(gain_ref, gain_buf, gain_sem)
    copy_gain.start()
    copy_shift = pltpu.make_async_copy(shift_ref, shift_buf, shift_sem)
    copy_shift.start()
    copies = weight_copies(w_ref, w_buf, w_sem, (1, 2))
    wait_all([copy_x, copy_gain, copy_shift])
    unit, _ = normalized(x_buf[...].astype(F32))
    normed = (unit * gain_buf[...].reshape(1, D) + shift_buf[...].reshape(1, D)).astype(BF)
    normed_ref[...] = normed
    parts = []
    for slot in range(2):
        copies[slot].wait()
        parts.append(own_heads(mm(normed, w_buf[slot])))
    kv_buf[...] = jnp.concatenate(parts, axis=1)
    wait_all(send_copies(kv_buf, kv_ref, range(8), kv_sem))


def query_kernel(normed_ref, w_ref, q_ref, w_buf, w_sem):
    weight_copies(w_ref, w_buf, w_sem, (0,))[0].wait()
    part = own_heads(mm(normed_ref[...], w_buf[0]))
    q_ref[...] = jnp.concatenate([part, jnp.zeros((TOK, HD), BF)], axis=1)


def block_query_kernel(normed_ref, w_ref, out_ref, x_buf, w_buf, x_sem, w_sem):
    block = pl.ds(pl.multiple_of(group_index() * BLK, BLK), BLK)
    loads = [
        pltpu.make_async_copy(normed_ref.at[block], x_buf, x_sem),
        pltpu.make_async_copy(w_ref.at[:, pl.ds(0, D)], w_buf, w_sem),
    ]
    for load in loads:
        load.start()
    wait_all(loads)
    query = mm(x_buf[...], w_buf[...]).astype(BF)
    zero = jnp.zeros((BLK, HD), BF)
    for group in range(4):
        out_ref[group] = jnp.concatenate([query[:, group * 192:(group + 1) * 192], zero], axis=1)


def attend_kernel(scene_ref, q_ref, same_ref, other_ref, out_ref, buf, q_buf, sem, q_sem):
    load = pltpu.make_async_copy(q_ref, q_buf, q_sem)
    load.start()
    first, big = span(scene_ref)

    def run(count):
        rows = count * TOK
        keys = jnp.concatenate(
            [ref[pl.ds(first, count)].reshape(rows, 384) for ref in (same_ref, other_ref)], axis=0
        )
        load.wait()
        query = q_buf[...]
        q0, q1 = halves(query[:, :128])
        blocks = [keys[:, :128], keys[:, 128:256], keys[:, 256:]]
        mixed = []
        columns = []
        for qh, kb, vb in ((q0, 0, 1), (q1, 0, 2), (query[:, 128:], 1, 2)):
            scores = mm_nt(qh, blocks[kb]) * (HD**-0.5)
            top = jnp.max(scores, axis=-1, keepdims=True)
            weights = jnp.exp(scores - top)
            total = jnp.sum(weights, axis=-1, keepdims=True)
            probs = (weights * (1.0 / total)).astype(BF)
            mixed.append(mm(probs, blocks[vb]))
            columns += three(top + jnp.log(total))
        stats = put_columns(128, TOK, 0, columns)
        buf[...] = jnp.concatenate([join(stats, mixed[0]), join(mixed[1], mixed[2])], axis=1).astype(BF)

    @pl.when(big)
    def _():
        run(5)

    @pl.when(jnp.logical_not(big))
    def _():
        run(1)

    wait_all(send_copies(buf, out_ref, range(8), sem))


def forward_kernel(
    mixed_ref, tok_ref, og_ref, wo_ref, gain_ref, shift_ref, up_ref, down_ref,
    out_ref, middle_ref, normed_ref, act_ref, gpre_ref,
    tok_buf, og_buf, up_buf, down_buf, gain_buf, shift_buf, grad_buf, branch_buf, middle_buf, in_sem, sem,
):
    loads = [
        pltpu.make_async_copy(ref, buf, in_sem.at[index])
        for index, (ref, buf) in enumerate(
            (
                (tok_ref, tok_buf), (up_ref, up_buf), (og_ref, og_buf), (down_ref, down_buf), (gain_ref, gain_buf),
                (shift_ref, shift_buf),
            )
        )
    ]
    for load in loads:
        load.start()
    total = jnp.zeros((2 * TOK, D), F32)
    for group in range(4):
        rows = jnp.concatenate([mixed_ref[group], mixed_ref[4 + group]], axis=0)
        total = total + mm(rows, wo_ref[group])
    loads[0].wait()
    total = total + tok_buf[...].reshape(2 * TOK, D).astype(F32)
    middle_buf[...] = total.reshape(8, BLK, D)
    third = pltpu.make_async_copy(
        middle_buf.at[lax.axis_index(MICRO) * 4 + group_index()], middle_ref, sem.at[2]
    )
    third.start()
    unit, _ = normalized(total)
    wait_all(loads[4:])
    normed = (unit * gain_buf[...].reshape(1, D) + shift_buf[...].reshape(1, D)).astype(BF)
    normed_ref[...] = normed
    loads[1].wait()
    pre = mm(normed, up_buf[...])
    cdf = 0.5 * (1.0 + lax.erf(pre * (0.5**0.5)))
    slope = cdf + pre * jnp.exp(-0.5 * pre * pre) * 0.3989422804014327
    loads[2].wait()
    loads[3].wait()
    grad_out = og_buf[...].reshape(2 * TOK, D)
    gpre = (mm_nt(grad_out, down_buf[...]) * slope).astype(BF)
    gpre_ref[...] = gpre
    grad_buf[...] = mm_nt(gpre, up_buf[...]).astype(BF).reshape(8, BLK, D)
    first = pltpu.make_async_copy(grad_buf, out_ref.at[:, pl.ds(BLK, BLK)], sem.at[0])
    first.start()
    act = (pre * cdf).astype(BF)
    act_ref[...] = act
    branch_buf[...] = mm(act, down_buf[...]).astype(BF).reshape(8, BLK, D)
    second = pltpu.make_async_copy(branch_buf, out_ref.at[:, pl.ds(0, BLK)], sem.at[1])
    second.start()
    wait_all([first, second, third])


def ff_grads_kernel(normed_ref, act_ref, gpre_ref, og_ref, keep_ref, send_ref, up_buf, down_buf):
    core = lax.axis_index(CORE)
    up_buf[...] = mm_tn(normed_ref[...], gpre_ref[...])
    down_buf[...] = mm_tn(act_ref[...], og_ref[...].reshape(2 * TOK, D))
    for ref, owner in ((keep_ref, core), (send_ref, 1 - core)):
        column = pl.multiple_of(owner * 384, 128)
        for tile in range(8):
            rows = pl.ds(pl.multiple_of((2 * tile + owner) * 48, 16), 48)
            ref[tile, :, :384] = up_buf[rows].astype(BF)
            ref[tile, :, 384:] = down_buf[tile * 48:(tile + 1) * 48, pl.ds(column, 384)].astype(BF)


def split_kernel(one_ref, two_ref, *refs):
    y = lax.axis_index("y")
    for k, ref in enumerate(refs):
        for xl in range(2):
            at = (y ^ k) * 2 + xl
            ref[xl] = (one_ref[at].astype(F32) + two_ref[at].astype(F32)).astype(BF)


def total_kernel(*refs):
    total = refs[0][...].astype(F32)
    for ref in refs[1:4]:
        total = total + ref[...].astype(F32)
    refs[4][...] = total.astype(BF)


def middle_kernel(
    sums_ref, middle_ref, og_ref, mixed_ref, wo_ref, gain_ref, query_ref,
    out_ref, low_ref, grad_ref, result_ref, vec_ref,
    buf, middle_buf, og_buf, mixed_buf, gain_buf, query_buf, low_buf, grad_buf, result_buf, vec_buf, in_sem, sem, rest_sem,
):
    micro = lax.axis_index(MICRO)
    group = group_index()
    block = pl.ds(pl.multiple_of(group * BLK, BLK), BLK)
    loads = [
        pltpu.make_async_copy(middle_ref, middle_buf, in_sem.at[0]),
        pltpu.make_async_copy(og_ref.at[micro, block], og_buf, in_sem.at[1]),
        pltpu.make_async_copy(mixed_ref.at[pl.ds(micro * 4, 4), block], mixed_buf, in_sem.at[2]),
        pltpu.make_async_copy(gain_ref, gain_buf, in_sem.at[3]),
        pltpu.make_async_copy(query_ref, query_buf, in_sem.at[4]),
    ]
    for load in loads:
        load.start()
    total = sums_ref[0].astype(F32)
    for index in range(1, 8):
        total = total + sums_ref[index].astype(F32)
    branch, grad = total[:BLK], total[BLK:]
    wait_all(loads)
    middle = middle_buf[...]
    unit, inverse = normalized(middle)
    grad_mid = og_buf[...].astype(F32) + norm_back(grad, unit, inverse, gain_buf[...].reshape(1, D))
    low = grad_mid.astype(BF)
    low_buf[...] = low
    grad_buf[...] = grad_mid
    result_buf[...] = (middle + branch).astype(BF)
    gain_grad = jnp.sum(grad * unit, axis=0, keepdims=True)
    shift_grad = jnp.sum(grad, axis=0, keepdims=True)
    vec_buf[...] = jnp.concatenate([gain_grad, shift_grad, jnp.zeros((6, D), F32)], axis=0)
    stores = [
        pltpu.make_async_copy(source, target, rest_sem.at[index])
        for index, (source, target) in enumerate(
            ((low_buf, low_ref), (grad_buf, grad_ref), (result_buf, result_ref), (vec_buf, vec_ref))
        )
    ]
    for store in stores:
        store.start()
    lane = lax.broadcasted_iota(jnp.int32, (BLK, 256), 1)
    for head_group in range(4):
        mixed = mixed_buf[head_group].astype(F32)
        back = mm_nt(low, wo_ref[head_group]).astype(BF).astype(F32)
        product = mixed * back
        columns = []
        for head in range(3):
            inside = (lane >= (head + 1) * HD) & (lane < (head + 2) * HD)
            columns += three(jnp.sum(jnp.where(inside, product, 0.0), axis=-1, keepdims=True))
        stats = put_columns(256, BLK, 9, columns)
        buf[head_group, :, :256] = jnp.where(lane < 9, mixed, jnp.where(lane < HD, stats, back)).astype(BF)
        buf[head_group, :, 256:] = query_buf[head_group]
    sends = send_copies(buf, out_ref, range(8), sem)
    wait_all(stores)
    wait_all(sends)


def attend_back_kernel(
    scene_ref, kvs_ref, kvo_ref, gs_ref, go_ref, normed_ref, mixed_ref, low_ref, low1_ref, low2_ref, low3_ref,
    w_ref, gqkv_ref, w_out_ref, keep_ref, send_ref,
    kv_buf, grad_buf, mixed_buf, normed_buf, low_buf, kv_sem, in_sem, w_sem,
):
    first, big = span(scene_ref)
    chip = chip_index()
    core = lax.axis_index(CORE)
    group = group_index()
    index = lax.axis_index(MICRO) * 4 + group
    first_loads = [
        pltpu.make_async_copy(source, target, in_sem.at[slot])
        for slot, (source, target) in enumerate(
            ((normed_ref, normed_buf), (mixed_ref.at[index], mixed_buf), (low_ref, low_buf))
        )
    ]
    scale = HD**-0.5

    def run(count):
        rows = count * TOK
        loads = [
            pltpu.make_async_copy(ref.at[pl.ds(first, count)], kv_buf.at[slot, pl.ds(0, count)], kv_sem.at[slot])
            for slot, ref in enumerate((kvs_ref, kvo_ref))
        ]
        for load in loads + first_loads:
            load.start()
        weight_copies(w_ref, w_out_ref, w_sem)

        def cut(value):
            return [value[:, at:at + 128] for at in range(0, value.shape[1], 128)]

        every = cut(jnp.concatenate(
            [ref[pl.ds(first, count)].reshape(rows, 512) for ref in (gs_ref, go_ref)], axis=0
        ))
        grad, query = every[:2], every[2:]
        g_own = cut(gs_ref[chip])
        g_heads = [halves(g_own[0])[1], *halves(g_own[1])]
        own_stats = g_own[0].astype(F32)
        all_stats = grad[0].astype(F32).T
        wait_all(loads)
        kv = cut(jnp.concatenate([kv_buf[slot, :count].reshape(rows, 384) for slot in range(2)], axis=0))
        own = cut(kv_buf[0, chip - first]) + g_own[2:]
        q_heads = [*halves(own[3]), own[4]]
        k_heads = [*halves(own[0]), halves(own[1])[0]]
        v_heads = [halves(own[1])[1], *halves(own[2])]

        def column(at):
            return own_stats[:, at:at + 1] + own_stats[:, at + 1:at + 2] + own_stats[:, at + 2:at + 3]

        def row(at):
            return all_stats[at:at + 1] + all_stats[at + 1:at + 2] + all_stats[at + 2:at + 3]

        dq, dk, dv = [], [], []
        for head, (kb, vb) in enumerate(((0, 1), (0, 2), (1, 2))):
            qb, gb = (0, 0, 1)[head], (0, 1, 1)[head]
            probs = jnp.exp(mm_nt(q_heads[head], kv[kb]) * scale - column(3 * head))
            gap = mm_nt(g_heads[head], kv[vb]) - column(9 + 3 * head)
            dq.append(mm((probs * gap).astype(BF), kv[kb]) * scale)
            probs = jnp.exp(mm_nt(k_heads[head], query[qb]) * scale - row(3 * head))
            gap = mm_nt(v_heads[head], grad[gb]) - row(9 + 3 * head)
            dv.append(mm(probs.astype(BF), grad[gb]))
            dk.append(mm((probs * gap).astype(BF), query[qb]) * scale)
        tail = dq[2]
        gqkv_ref[...] = jnp.concatenate(
            [join(dk[0], dk[1]), join(dk[2], dv[0]), join(dv[1], dv[2]), join(dq[0], dq[1]),
             join(tail, jnp.zeros_like(tail))],
            axis=1,
        ).astype(BF)


    @pl.when(big)
    def _():
        run(5)

    @pl.when(jnp.logical_not(big))
    def _():
        run(1)

    wait_all(first_loads)

    grad_buf[...] = mm_tn(normed_buf[...], gqkv_ref[...])
    low = jnp.concatenate([ref[...] for ref in (low_buf, low1_ref, low2_ref, low3_ref)], axis=0)
    mixed = jnp.concatenate(
        [mixed_buf[pl.ds(pl.multiple_of((group ^ k) * BLK, BLK), BLK)] for k in range(4)], axis=0
    )
    out = mm_tn(mixed, low)[HD:]
    for ref, owner in ((keep_ref, core), (send_ref, 1 - core)):
        for tile in range(8):
            rows = grad_buf[pl.ds(pl.multiple_of((2 * tile + owner) * 48, 16), 48)]
            at = (tile // 4) * 96
            pieces = [
                out[at + row * 48:at + (row + 1) * 48, (tile % 4) * 192:(tile % 4 + 1) * 192] for row in range(2)
            ]
            ref[2 * tile] = rows[:, :384].astype(BF)
            ref[2 * tile + 1] = jnp.concatenate(
                [rows[:, 384:576], jnp.where(owner == 1, pieces[1], pieces[0])], axis=1
            ).astype(BF)
    wait_all(weight_copies(w_ref, w_out_ref, w_sem, start=False))


def normed_grad_kernel(
    gqkv_ref, w_ref, tok_ref, vec_ref, near_ref, far_ref, own_ref, one_ref, two_ref, three_ref, sums_ref, ff_ref,
    x_buf, vec_buf, near_buf, part_buf, low_buf, sums_buf, ff_buf, in_sem, out_sem,
):
    loads = [
        pltpu.make_async_copy(tok_ref.at[lax.axis_index(MICRO)], x_buf, in_sem.at[0]),
        pltpu.make_async_copy(vec_ref, vec_buf, in_sem.at[1]),
        pltpu.make_async_copy(near_ref, near_buf, in_sem.at[2]),
    ]
    for load in loads:
        load.start()
    group = group_index()
    odd = (group % 2) == 1
    total = jnp.zeros((TOK, D), F32)
    for slot in range(3):
        part = gqkv_ref[:, slot * 192:(slot + 1) * 192]
        zero = jnp.zeros_like(part)
        wide = jnp.where(
            odd, jnp.concatenate([zero, part], axis=1), jnp.concatenate([part, zero], axis=1)
        )
        total = total + mm_nt(wide, w_ref[slot])
    part_buf[...] = total
    low_buf[...] = total.astype(BF)
    stores = []
    for k, ref in enumerate((own_ref, one_ref, two_ref, three_ref)):
        rows = pl.ds(pl.multiple_of((group ^ k) * BLK, BLK), BLK)
        stores.append(pltpu.make_async_copy((low_buf if k else part_buf).at[rows], ref, out_sem.at[k]))
        stores[-1].start()
    wait_all(loads)
    ff_buf[...] = (near_buf[...].astype(F32) + far_ref[...].astype(F32)).astype(BF)
    stores.append(pltpu.make_async_copy(ff_buf, ff_ref, out_sem.at[5]))
    stores[-1].start()
    unit, _ = normalized(x_buf[...].astype(F32))
    gain1 = jnp.sum(total * unit, axis=0, keepdims=True)
    shift1 = jnp.sum(total, axis=0, keepdims=True)
    sums_buf[...] = jnp.concatenate([gain1, shift1, vec_buf[...][:2], jnp.zeros((4, D), F32)], axis=0)
    stores.append(pltpu.make_async_copy(sums_buf, sums_ref, out_sem.at[4]))
    stores[-1].start()
    wait_all(stores)


def add_kernel(one_ref, two_ref, unused_ref, out_ref, buf, sem):
    buf[...] = (one_ref[...].astype(F32) + two_ref[...].astype(F32)).astype(BF)
    copy = pltpu.make_async_copy(buf, out_ref, sem)
    copy.start()
    copy.wait()


def sum_kernel(in_ref, vec_ref, out_ref, buf, vec_buf, sem, vec_sem):
    load = pltpu.make_async_copy(vec_ref, vec_buf, vec_sem)
    load.start()
    total = in_ref[0].astype(F32)
    for index in range(1, 16):
        total = total + in_ref[index].astype(F32)
    load.wait()
    vectors = vec_buf[...][:4]
    block = jnp.concatenate([total, vectors[:, :384], vectors[:, 384:]], axis=0).astype(BF)
    for index in range(8):
        buf[index] = block
    wait_all(send_copies(buf, out_ref, range(8), sem))


def spread_kernel(turn, in_ref, *refs):
    qkv_buf, out_buf, sem, out_sem = refs[-4:]
    qkv_ref, out_ref, *vec_refs = refs[3:-4] if turn else refs[:-4]
    owner = lax.axis_index(CORE)
    owner = 1 - owner if turn else owner
    copies = []
    vectors = jnp.zeros((8, 384), F32)
    for tile in range(8):
        whole = [in_ref[tile, index].astype(F32) for index in range(8)]
        block = [value[:48] for value in whole]
        for value in whole:
            vectors = vectors + value[48:]
        for part, half, at in ((1, 0, 0), (2, 0, 192), (0, 4, 0)):
            qkv_buf[tile, :, part * D:(part + 1) * D] = jnp.concatenate(
                [block[half + group][:, at:at + 192] for group in range(4)], axis=1
            )
        start = pl.multiple_of((2 * tile + owner) * 48, 16)
        copy = pltpu.make_async_copy(qkv_buf.at[tile], qkv_ref.at[pl.ds(start, 48)], sem.at[tile])
        copy.start()
        copies.append(copy)
        for group in range(4):
            out_buf[group, tile // 4, :, (tile % 4) * 192:(tile % 4 + 1) * 192] = block[4 + group][:, 192:]
    for group in range(4):
        for pair in range(2):
            start = pl.multiple_of(group * 192 + (pair * 2 + owner) * 48, 16)
            copy = pltpu.make_async_copy(
                out_buf.at[group, pair], out_ref.at[pl.ds(start, 48)], out_sem.at[group, pair]
            )
            copy.start()
            copies.append(copy)
    if turn:
        vectors = vectors + refs[0][...]
        for k, ref in enumerate(vec_refs):
            ref[...] = jnp.concatenate([vectors[k:k + 1], vectors[4 + k:5 + k]], axis=1).reshape(D)
    else:
        vec_refs[0][...] = vectors
    wait_all(copies)


def stack_kernel(*refs):
    y = lax.axis_index("y")
    for k, ref in enumerate(refs[:4]):
        refs[5][pl.ds((y ^ k) * 2, 2)] = ref[...]


def spread_ff_kernel(same_ref, other_ref, up_ref, down_ref):
    core = lax.axis_index(CORE)
    for ref, owner in ((same_ref, core), (other_ref, 1 - core)):
        for chip in range(8):
            block = ref[chip].astype(F32)
            up_ref[pl.ds(pl.multiple_of((chip * 2 + owner) * 48, 16), 48)] = block[:, :384]
            down_ref[chip * 48:(chip + 1) * 48, pl.ds(pl.multiple_of(owner * 384, 128), 384)] = block[:, 384:]


def input_kernel(
    own_ref, one_ref, two_ref, three_ref, tok_ref, gain_ref, grad_ref, result_ref, unused_ref, out_ref, buf, x_buf, sem, x_sem
):
    start = pl.multiple_of(group_index() * BLK, BLK)
    load = pltpu.make_async_copy(tok_ref.at[lax.axis_index(MICRO), pl.ds(start, BLK)], x_buf, x_sem)
    load.start()
    load.wait()
    total = own_ref[...]
    for ref in (one_ref, two_ref, three_ref):
        total = total + ref[...].astype(F32)
    unit, inverse = normalized(x_buf[...].astype(F32))
    grad = grad_ref[...] + norm_back(total, unit, inverse, gain_ref[...].reshape(1, D))
    buf[:BLK] = grad.astype(BF)
    buf[BLK:] = result_ref[...]
    wait_all(send_copies(buf, out_ref, range(8), sem))


def unpack_kernel(in_ref, unused_ref, other_ref, grad_ref, result_ref):
    for index in range(8):
        rows = slice(index % 4 * BLK, (index % 4 + 1) * BLK)
        grad_ref[index // 4, rows] = in_ref[index, :BLK].astype(F32)
        result_ref[index // 4, rows] = in_ref[index, BLK:]


def exchange(value, axes):
    return lax.all_to_all(value, axes, 0, 0, tiled=True)


def swap(value):
    return lax.ppermute(value, CORE, [(0, 1), (1, 0)])


def after(value, *others):
    return pl.pallas_call(
        lambda *refs: None,
        out_shape=jax.ShapeDtypeStruct(value.shape, value.dtype),
        in_specs=[pl.BlockSpec(memory_space=pl.ANY)] * (1 + len(others)),
        out_specs=pl.BlockSpec(memory_space=pl.ANY),
        input_output_aliases={0: 0},
        cost_estimate=pl.CostEstimate(flops=1, bytes_accessed=1, transcendentals=0),
        compiler_params=pltpu.CompilerParams(vmem_limit_bytes=2**20),
    )(value, *others)


def flip(value, axes, count, bits):
    return lax.ppermute(value, axes, [(index, index ^ bits) for index in range(count)])


def shards(
    tokens, scene_of_block, ln1_gain, ln1_shift, w_qkv, w_out, ln2_gain, ln2_shift, w_up, w_down, out_grad
):
    w_out_pad = jnp.pad(w_out.reshape(4, 192, D), ((0, 0), (HD, 0), (0, 0)))
    kv_send, normed = call(
        project_kernel,
        [((8, TOK, 384), BF, "H"), ((TOK, D), BF, "L")],
        [(tokens, "H"), (ln1_gain, "H"), (ln1_shift, "H"), (w_qkv, "H")],
        1000,
        [
            pltpu.VMEM((TOK, D), BF), pltpu.VMEM((2, D, 384), BF), pltpu.VMEM((TOK, 384), BF),
            pltpu.VMEM((D,), F32), pltpu.VMEM((D,), F32), DMA, DMA((2,)), DMA((8,)), DMA, DMA,
        ],
    )
    (query,) = call(
        query_kernel,
        [((TOK, 256), BF, "L")],
        [(normed, "L"), (w_qkv, "H")],
        1000,
        [pltpu.VMEM((1, D, 384), BF), DMA((1,))],
    )
    kv_same = exchange(kv_send, CHIP)
    kv_same = after(kv_same, pin(query))
    kv_other = swap(kv_same)
    (mixed_send,) = call(
        attend_kernel,
        [((8, TOK, 256), BF, "H")],
        [(scene_of_block, "S"), (query, "H"), (kv_same, "V"), (kv_other, "V")],
        1000,
        [pltpu.VMEM((TOK, 256), BF), pltpu.VMEM((TOK, 256), BF), DMA((8,)), DMA],
    )
    mixed = exchange(mixed_send, NARROW)
    (block_query,) = call(
        block_query_kernel,
        [((4, BLK, 256), BF, "L")],
        [(normed, "H"), (w_qkv, "H")],
        1000,
        [pltpu.VMEM((BLK, D), BF), pltpu.VMEM((D, D), BF), DMA, DMA],
    )
    ff_send, middle, normed2, act, grad_pre = call(
        forward_kernel,
        [
            ((8, 2 * BLK, D), BF, "H"), ((BLK, D), F32, "H"), ((2 * TOK, D), BF, "V"),
            ((2 * TOK, FFL), BF, "V"), ((2 * TOK, FFL), BF, "V"),
        ],
        [
            (mixed, "V"), (tokens, "H"), (out_grad, "H"), (w_out_pad, "V"), (ln2_gain, "H"), (ln2_shift, "H"),
            (w_up, "H"), (w_down, "H"),
        ],
        1000,
        [
            pltpu.VMEM((2, TOK, D), BF), pltpu.VMEM((2, TOK, D), BF), pltpu.VMEM((D, FFL), BF),
            pltpu.VMEM((FFL, D), BF), pltpu.VMEM((D,), F32), pltpu.VMEM((D,), F32), pltpu.VMEM((8, BLK, D), BF),
            pltpu.VMEM((8, BLK, D), BF), pltpu.VMEM((8, BLK, D), F32), DMA((6,)), DMA((3,)),
        ],
    )
    ff_sums = exchange(ff_send, NARROW)
    keep, send = call(
        ff_grads_kernel,
        [((8, 48, D), BF, "V")] * 2,
        [(normed2, "V"), (act, "V"), (grad_pre, "V"), (out_grad, "L")],
        1000,
        [pltpu.VMEM((D, FFL), F32), pltpu.VMEM((FFL, D), F32)],
    )
    pieces = call(
        split_kernel, [((2, 48, D), BF, "L")] * 4, [(keep, "V"), (swap(send), "V")], 1000
    )
    pieces = [pieces[0]] + [flip(pieces[k], "y", 4, k) for k in (1, 2, 3)]
    (ff_near,) = call(
        total_kernel,
        [((2, 48, D), BF, "L")],
        [(pieces[0], "L")] + [(piece, "V") for piece in pieces[1:]],
        1000,
    )
    ff_sums = after(ff_sums, pin(ff_near))
    grad_send, low, grad_mid, result_part, vec2 = call(
        middle_kernel,
        [
            ((8, 4, BLK, 512), BF, "H"), ((BLK, D), BF, "H"), ((BLK, D), F32, "H"), ((BLK, D), BF, "H"),
            ((8, D), F32, "H"),
        ],
        [
            (ff_sums, "V"), (middle, "H"), (out_grad, "H"), (mixed, "H"), (w_out_pad, "V"), (ln2_gain, "H"),
            (block_query, "H"),
        ],
        1000,
        [
            pltpu.VMEM((4, BLK, 512), BF), pltpu.VMEM((BLK, D), F32), pltpu.VMEM((BLK, D), BF),
            pltpu.VMEM((4, BLK, 256), BF), pltpu.VMEM((D,), F32), pltpu.VMEM((4, BLK, 256), BF), pltpu.VMEM((BLK, D), BF), pltpu.VMEM((BLK, D), F32),
            pltpu.VMEM((BLK, D), BF), pltpu.VMEM((8, D), F32), DMA((5,)), DMA((8,)), DMA((4,)),
        ],
    )
    grad_same = exchange(grad_send.reshape(32, BLK, 512), (*CHIP, *GROUP)).reshape(8, TOK, 512)
    lows = [flip(low, GROUP, 4, k) for k in (1, 2, 3)]
    grad_same = after(grad_same, *lows)
    grad_other = swap(grad_same)
    ff_near = after(pin(ff_near), grad_other)
    ff_far = flip(ff_near, "xl", 2, 1)
    gqkv, w_own, keep, send = call(
        attend_back_kernel,
        [((TOK, 640), BF, "V"), ((3, D, 384), BF, "V")] + [((16, 48, 384), BF, "V")] * 2,
        [
            (scene_of_block, "S"), (kv_same, "H"), (kv_other, "H"), (grad_same, "V"), (grad_other, "V"),
            (normed, "H"), (mixed, "H"), (low, "H"), *[(value, "V") for value in lows], (w_qkv, "H"),
        ],
        1000,
        [
            pltpu.VMEM((2, 5, TOK, 384), BF), pltpu.VMEM((D, 640), F32),
            pltpu.VMEM((TOK, 256), BF), pltpu.VMEM((TOK, D), BF), pltpu.VMEM((BLK, D), BF),
            DMA((2,)), DMA((3,)), DMA((3,)),
        ],
        vmem=24,
    )
    own, *sends, sums, ff_part = call(
        normed_grad_kernel,
        [((BLK, D), F32, "H")] + [((BLK, D), BF, "H")] * 3 + [((8, D), F32, "H"), ((2, 48, D), BF, "H")],
        [(gqkv, "V"), (w_own, "V"), (tokens, "H"), (vec2, "H"), (ff_near, "H"), (ff_far, "V")],
        1000,
        [
            pltpu.VMEM((TOK, D), BF), pltpu.VMEM((8, D), F32), pltpu.VMEM((2, 48, D), BF), pltpu.VMEM((TOK, D), F32),
            pltpu.VMEM((TOK, D), BF), pltpu.VMEM((8, D), F32), pltpu.VMEM((2, 48, D), BF), DMA((3,)), DMA((6,)),
        ],
    )
    (weight_send,) = call(
        add_kernel,
        [((16, 48, 384), BF, "H")],
        [(keep, "V"), (swap(after(send, ff_far)), "V"), (own, "H")],
        1000,
        [pltpu.VMEM((16, 48, 384), BF), DMA],
    )
    weight_parts = exchange(weight_send, (*CHIP, MICRO))
    parts = [flip(value, GROUP, 4, k + 1) for k, value in enumerate(sends)]
    weight_parts = after(weight_parts, pin(sums), *parts)
    ff_parts = [flip(ff_part, "y", 4, k) for k in (1, 2, 3)]
    (weight_total,) = call(
        sum_kernel,
        [((8, 8, 56, 384), BF, "H")],
        [(weight_parts, "V"), (sums, "H")],
        1000,
        [pltpu.VMEM((8, 56, 384), BF), pltpu.VMEM((8, D), F32), DMA((8,)), DMA],
    )
    (packed,) = call(
        input_kernel,
        [((8, 2 * BLK, D), BF, "H")],
        [
            (own, "L"), *[(value, "V") for value in parts], (tokens, "H"), (ln1_gain, "L"), (grad_mid, "L"),
            (result_part, "L"), (weight_total, "H"),
        ],
        1000,
        [pltpu.VMEM((2 * BLK, D), BF), pltpu.VMEM((BLK, D), BF), DMA((8,)), DMA],
    )
    weight_same = exchange(weight_total.reshape(64, 56, 384), (*CHIP, *NARROW)).reshape(8, 8, 56, 384)
    (ff_same,) = call(
        stack_kernel,
        [((8, 48, D), BF, "L")],
        [(ff_part, "L"), *[(value, "V") for value in ff_parts], (packed, "H")],
        1000,
    )
    weight_same = after(weight_same, pin(packed), pin(ff_same))
    everyone = exchange(after(pin(packed), weight_same), NARROW)
    weight_other = swap(weight_same)
    up_grad, down_grad = call(
        spread_ff_kernel,
        [((D, FFL), F32, "L"), ((FFL, D), F32, "L")],
        [(ff_same, "L"), (swap(ff_same), "V")],
        1000,
    )
    scratch = [
        pltpu.VMEM((8, 48, 3 * D), F32), pltpu.VMEM((4, 2, 48, D), F32), DMA((8,)), DMA((4, 2)),
    ]
    grads = [((D, 3 * D), F32, "H"), ((D, D), F32, "H")]
    half = call(
        functools.partial(spread_kernel, False),
        grads + [((8, 384), F32, "V")],
        [(weight_same, "V")],
        1000,
        scratch,
    )
    qkv_grad, out_proj_grad, *vectors = call(
        functools.partial(spread_kernel, True),
        grads + [((D,), F32, "L")] * 4,
        [(weight_other, "V"), (half[2], "V"), (half[0], "H"), (half[1], "H")],
        1000,
        scratch,
        aliases={2: 0, 3: 1},
    )
    input_grad, result = call(
        unpack_kernel, [((2, TOK, D), F32, "L"), ((2, TOK, D), BF, "L")], [(everyone, "V"), (vectors[0], "H"), (up_grad, "H")], 1000
    )
    return (
        result, input_grad, qkv_grad, out_proj_grad, *vectors, up_grad, down_grad
    )


def solution(mesh):
    names = ("y", "xl", "c", "zh", "zl", "xh")
    fine = Mesh(mesh.devices.reshape(4, 2, 2, 2, 2, 2), names)
    tokens = P(None, WIDE, None)
    placed = (
        tokens, P(), P(), P(), P(), P(), P(), P(), P(None, NARROW), P(NARROW, None), tokens
    )
    return jax.shard_map(
        shards,
        mesh=fine,
        in_specs=placed,
        out_specs=(
            tokens, tokens, P(), P(), P(), P(), P(), P(), P(None, NARROW), P(NARROW, None)
        ),
        check_vma=False,
    )
```

```python
import functools

import jax
import jax.numpy as jnp
from jax import lax
from jax.experimental import pallas as pl
from jax.experimental.pallas import tpu as pltpu
from jax.sharding import Mesh
from jax.sharding import PartitionSpec as P

D = 768
HD = 64
FFL = 384
TOK = 128
BLK = 32
EPS = 1e-05
BF = jnp.bfloat16
F32 = jnp.float32

CHIP = ("y", "xl")
CORE = "c"
MICRO = "zh"
GROUP = ("zl", "xh")
NARROW = (MICRO, *GROUP)
WIDE = (*CHIP, CORE)


def chip_index():
    return lax.axis_index("y") * 2 + lax.axis_index("xl")


def group_index():
    return lax.axis_index("zl") * 2 + lax.axis_index("xh")


def mm(left, right):
    return lax.dot_general(left, right, (((1,), (0,)), ((), ())), preferred_element_type=F32)


def mm_nt(left, right):
    return lax.dot_general(left, right, (((1,), (1,)), ((), ())), preferred_element_type=F32)


def mm_tn(left, right):
    return lax.dot_general(left, right, (((0,), (0,)), ((), ())), preferred_element_type=F32)


def normalized(values):
    center = values - jnp.mean(values, axis=-1, keepdims=True)
    spread = jnp.mean(center * center, axis=-1, keepdims=True)
    inverse = lax.rsqrt(spread + EPS)
    return center * inverse, inverse


def norm_back(grad, unit, inverse, gain):
    scaled = grad * gain
    first = jnp.mean(scaled, axis=-1, keepdims=True)
    second = jnp.mean(scaled * unit, axis=-1, keepdims=True)
    return inverse * (scaled - first - unit * second)


def halves(block):
    lane = lax.broadcasted_iota(jnp.int32, block.shape, 1)
    zero = jnp.zeros_like(block)
    return jnp.where(lane < HD, block, zero), jnp.where(lane < HD, zero, block)


def join(low, high):
    lane = lax.broadcasted_iota(jnp.int32, low.shape, 1)
    return jnp.where(lane < HD, low, high)


def span(scene_ref):
    micro = lax.axis_index(MICRO)
    own = scene_ref[micro, chip_index() * 4]
    first = jnp.int32(0)
    count = jnp.int32(0)
    for index in range(8):
        other = scene_ref[micro, index * 4]
        first += (other < own).astype(jnp.int32)
        count += (other == own).astype(jnp.int32)
    return first, count > 1


def three(value):
    a = value.astype(BF).astype(F32)
    b = (value - a).astype(BF).astype(F32)
    c = value - a - b
    return a, b, c


def put_columns(width, rows, start, columns):
    lane = lax.broadcasted_iota(jnp.int32, (rows, width), 1)
    out = jnp.zeros((rows, width), F32)
    for offset, column in enumerate(columns):
        out = jnp.where(lane == start + offset, column, out)
    return out


def pin(value):
    return pltpu.with_memory_space_constraint(value, pltpu.HBM)


def call(kernel, outs, ins, cost, scratch=(), vmem=16, aliases=None):
    places = {"V": pltpu.VMEM, "H": pltpu.HBM, "S": pltpu.SMEM, "L": pltpu.VMEM}
    return pl.pallas_call(
        kernel,
        out_shape=[
            (pltpu.HBM if place in "HL" else jax.ShapeDtypeStruct)(shape, dtype) for shape, dtype, place in outs
        ],
        in_specs=[pl.BlockSpec(memory_space=places[place]) for _, place in ins],
        out_specs=[pl.BlockSpec(memory_space=places[place]) for _, _, place in outs],
        scratch_shapes=list(scratch),
        input_output_aliases=aliases or {},
        cost_estimate=pl.CostEstimate(flops=cost, bytes_accessed=1000, transcendentals=0),
        compiler_params=pltpu.CompilerParams(vmem_limit_bytes=vmem * 2**20),
    )(*[pin(value) if place in "HL" else value for value, place in ins])


DMA = pltpu.SemaphoreType.DMA


def send_copies(source, target, indices, sem):
    copies = [pltpu.make_async_copy(source, target.at[index], sem.at[index]) for index in indices]
    for copy in copies:
        copy.start()
    return copies


def wait_all(copies):
    for copy in copies:
        copy.wait()


def weight_copies(w_ref, w_buf, w_sem, parts=(1, 2, 0), start=True):
    group = group_index()
    copies = []
    for slot, part in enumerate(parts):
        column = pl.multiple_of(part * D + (group // 2) * 384, 128)
        copy = pltpu.make_async_copy(w_ref.at[:, pl.ds(column, 384)], w_buf.at[slot], w_sem.at[slot])
        if start:
            copy.start()
        copies.append(copy)
    return copies


def own_heads(full):
    odd = (group_index() % 2) == 1
    return jnp.where(odd, full[:, 192:], full[:, :192]).astype(BF)


def project_kernel(
    tok_ref, gain_ref, shift_ref, w_ref, kv_ref, normed_ref,
    x_buf, w_buf, kv_buf, gain_buf, shift_buf, x_sem, w_sem, kv_sem, gain_sem, shift_sem,
):
    copy_x = pltpu.make_async_copy(tok_ref.at[lax.axis_index(MICRO)], x_buf, x_sem)
    copy_x.start()
    copy_gain = pltpu.make_async_copy(gain_ref, gain_buf, gain_sem)
    copy_gain.start()
    copy_shift = pltpu.make_async_copy(shift_ref, shift_buf, shift_sem)
    copy_shift.start()
    copies = weight_copies(w_ref, w_buf, w_sem, (1, 2))
    wait_all([copy_x, copy_gain, copy_shift])
    unit, _ = normalized(x_buf[...].astype(F32))
    normed = (unit * gain_buf[...].reshape(1, D) + shift_buf[...].reshape(1, D)).astype(BF)
    normed_ref[...] = normed
    parts = []
    for slot in range(2):
        copies[slot].wait()
        parts.append(own_heads(mm(normed, w_buf[slot])))
    kv_buf[...] = jnp.concatenate(parts, axis=1)
    wait_all(send_copies(kv_buf, kv_ref, range(8), kv_sem))


def query_kernel(normed_ref, w_ref, q_ref, w_buf, w_sem):
    weight_copies(w_ref, w_buf, w_sem, (0,))[0].wait()
    part = own_heads(mm(normed_ref[...], w_buf[0]))
    q_ref[...] = jnp.concatenate([part, jnp.zeros((TOK, HD), BF)], axis=1)


def block_query_kernel(normed_ref, w_ref, out_ref, x_buf, w_buf, x_sem, w_sem):
    block = pl.ds(pl.multiple_of(group_index() * BLK, BLK), BLK)
    loads = [
        pltpu.make_async_copy(normed_ref.at[block], x_buf, x_sem),
        pltpu.make_async_copy(w_ref.at[:, pl.ds(0, D)], w_buf, w_sem),
    ]
    for load in loads:
        load.start()
    wait_all(loads)
    query = mm(x_buf[...], w_buf[...]).astype(BF)
    zero = jnp.zeros((BLK, HD), BF)
    for group in range(4):
        out_ref[group] = jnp.concatenate([query[:, group * 192:(group + 1) * 192], zero], axis=1)


def attend_kernel(scene_ref, q_ref, same_ref, other_ref, out_ref, buf, q_buf, sem, q_sem):
    load = pltpu.make_async_copy(q_ref, q_buf, q_sem)
    load.start()
    first, big = span(scene_ref)

    def run(count):
        rows = count * TOK
        keys = jnp.concatenate(
            [ref[pl.ds(first, count)].reshape(rows, 384) for ref in (same_ref, other_ref)], axis=0
        )
        load.wait()
        query = q_buf[...]
        q0, q1 = halves(query[:, :128])
        blocks = [keys[:, :128], keys[:, 128:256], keys[:, 256:]]
        mixed = []
        columns = []
        for qh, kb, vb in ((q0, 0, 1), (q1, 0, 2), (query[:, 128:], 1, 2)):
            scores = mm_nt(qh, blocks[kb]) * (HD**-0.5)
            top = jnp.max(scores, axis=-1, keepdims=True)
            weights = jnp.exp(scores - top)
            total = jnp.sum(weights, axis=-1, keepdims=True)
            probs = (weights * (1.0 / total)).astype(BF)
            mixed.append(mm(probs, blocks[vb]))
            columns += three(top + jnp.log(total))
        stats = put_columns(128, TOK, 0, columns)
        buf[...] = jnp.concatenate([join(stats, mixed[0]), join(mixed[1], mixed[2])], axis=1).astype(BF)

    @pl.when(big)
    def _():
        run(5)

    @pl.when(jnp.logical_not(big))
    def _():
        run(1)

    wait_all(send_copies(buf, out_ref, range(8), sem))


def forward_kernel(
    mixed_ref, tok_ref, og_ref, wo_ref, gain_ref, shift_ref, up_ref, down_ref,
    out_ref, middle_ref, normed_ref, act_ref, gpre_ref,
    tok_buf, og_buf, up_buf, down_buf, gain_buf, shift_buf, grad_buf, branch_buf, middle_buf, in_sem, sem,
):
    loads = [
        pltpu.make_async_copy(ref, buf, in_sem.at[index])
        for index, (ref, buf) in enumerate(
            (
                (tok_ref, tok_buf), (up_ref, up_buf), (og_ref, og_buf), (down_ref, down_buf), (gain_ref, gain_buf),
                (shift_ref, shift_buf),
            )
        )
    ]
    for load in loads:
        load.start()
    total = jnp.zeros((2 * TOK, D), F32)
    for group in range(4):
        rows = jnp.concatenate([mixed_ref[group], mixed_ref[4 + group]], axis=0)
        total = total + mm(rows, wo_ref[group])
    loads[0].wait()
    total = total + tok_buf[...].reshape(2 * TOK, D).astype(F32)
    middle_buf[...] = total.reshape(8, BLK, D)
    third = pltpu.make_async_copy(
        middle_buf.at[lax.axis_index(MICRO) * 4 + group_index()], middle_ref, sem.at[2]
    )
    third.start()
    unit, _ = normalized(total)
    wait_all(loads[4:])
    normed = (unit * gain_buf[...].reshape(1, D) + shift_buf[...].reshape(1, D)).astype(BF)
    normed_ref[...] = normed
    loads[1].wait()
    pre = mm(normed, up_buf[...])
    cdf = 0.5 * (1.0 + lax.erf(pre * (0.5**0.5)))
    slope = cdf + pre * jnp.exp(-0.5 * pre * pre) * 0.3989422804014327
    loads[2].wait()
    loads[3].wait()
    grad_out = og_buf[...].reshape(2 * TOK, D)
    gpre = (mm_nt(grad_out, down_buf[...]) * slope).astype(BF)
    gpre_ref[...] = gpre
    grad_buf[...] = mm_nt(gpre, up_buf[...]).astype(BF).reshape(8, BLK, D)
    first = pltpu.make_async_copy(grad_buf, out_ref.at[:, pl.ds(BLK, BLK)], sem.at[0])
    first.start()
    act = (pre * cdf).astype(BF)
    act_ref[...] = act
    branch_buf[...] = mm(act, down_buf[...]).astype(BF).reshape(8, BLK, D)
    second = pltpu.make_async_copy(branch_buf, out_ref.at[:, pl.ds(0, BLK)], sem.at[1])
    second.start()
    wait_all([first, second, third])


def ff_grads_kernel(normed_ref, act_ref, gpre_ref, og_ref, keep_ref, send_ref, up_buf, down_buf):
    core = lax.axis_index(CORE)
    up_buf[...] = mm_tn(normed_ref[...], gpre_ref[...])
    down_buf[...] = mm_tn(act_ref[...], og_ref[...].reshape(2 * TOK, D))
    for ref, owner in ((keep_ref, core), (send_ref, 1 - core)):
        column = pl.multiple_of(owner * 384, 128)
        for tile in range(8):
            rows = pl.ds(pl.multiple_of((2 * tile + owner) * 48, 16), 48)
            ref[tile, :, :384] = up_buf[rows].astype(BF)
            ref[tile, :, 384:] = down_buf[tile * 48:(tile + 1) * 48, pl.ds(column, 384)].astype(BF)


def split_kernel(one_ref, two_ref, *refs):
    y = lax.axis_index("y")
    for k, ref in enumerate(refs):
        for xl in range(2):
            at = (y ^ k) * 2 + xl
            ref[xl] = (one_ref[at].astype(F32) + two_ref[at].astype(F32)).astype(BF)


def total_kernel(*refs):
    total = refs[0][...].astype(F32)
    for ref in refs[1:4]:
        total = total + ref[...].astype(F32)
    refs[4][...] = total.astype(BF)


def middle_kernel(
    sums_ref, middle_ref, og_ref, mixed_ref, wo_ref, gain_ref, query_ref,
    out_ref, low_ref, grad_ref, result_ref, vec_ref,
    buf, middle_buf, og_buf, mixed_buf, gain_buf, query_buf, low_buf, grad_buf, result_buf, vec_buf, in_sem, sem, rest_sem,
):
    micro = lax.axis_index(MICRO)
    group = group_index()
    block = pl.ds(pl.multiple_of(group * BLK, BLK), BLK)
    loads = [
        pltpu.make_async_copy(middle_ref, middle_buf, in_sem.at[0]),
        pltpu.make_async_copy(og_ref.at[micro, block], og_buf, in_sem.at[1]),
        pltpu.make_async_copy(mixed_ref.at[pl.ds(micro * 4, 4), block], mixed_buf, in_sem.at[2]),
        pltpu.make_async_copy(gain_ref, gain_buf, in_sem.at[3]),
        pltpu.make_async_copy(query_ref, query_buf, in_sem.at[4]),
    ]
    for load in loads:
        load.start()
    total = sums_ref[0].astype(F32)
    for index in range(1, 8):
        total = total + sums_ref[index].astype(F32)
    branch, grad = total[:BLK], total[BLK:]
    wait_all(loads)
    middle = middle_buf[...]
    unit, inverse = normalized(middle)
    grad_mid = og_buf[...].astype(F32) + norm_back(grad, unit, inverse, gain_buf[...].reshape(1, D))
    low = grad_mid.astype(BF)
    low_buf[...] = low
    grad_buf[...] = grad_mid
    result_buf[...] = (middle + branch).astype(BF)
    gain_grad = jnp.sum(grad * unit, axis=0, keepdims=True)
    shift_grad = jnp.sum(grad, axis=0, keepdims=True)
    vec_buf[...] = jnp.concatenate([gain_grad, shift_grad, jnp.zeros((6, D), F32)], axis=0)
    stores = [
        pltpu.make_async_copy(source, target, rest_sem.at[index])
        for index, (source, target) in enumerate(
            ((low_buf, low_ref), (grad_buf, grad_ref), (result_buf, result_ref), (vec_buf, vec_ref))
        )
    ]
    for store in stores:
        store.start()
    lane = lax.broadcasted_iota(jnp.int32, (BLK, 256), 1)
    for head_group in range(4):
        mixed = mixed_buf[head_group].astype(F32)
        back = mm_nt(low, wo_ref[head_group]).astype(BF).astype(F32)
        product = mixed * back
        columns = []
        for head in range(3):
            inside = (lane >= (head + 1) * HD) & (lane < (head + 2) * HD)
            columns += three(jnp.sum(jnp.where(inside, product, 0.0), axis=-1, keepdims=True))
        stats = put_columns(256, BLK, 9, columns)
        buf[head_group, :, :256] = jnp.where(lane < 9, mixed, jnp.where(lane < HD, stats, back)).astype(BF)
        buf[head_group, :, 256:] = query_buf[head_group]
    sends = send_copies(buf, out_ref, range(8), sem)
    wait_all(stores)
    wait_all(sends)


def attend_back_kernel(
    scene_ref, kvs_ref, kvo_ref, gs_ref, go_ref, normed_ref, mixed_ref, low_ref, low1_ref, low2_ref, low3_ref,
    w_ref, gqkv_ref, w_out_ref, keep_ref, send_ref,
    kv_buf, grad_buf, mixed_buf, normed_buf, low_buf, kv_sem, in_sem, w_sem,
):
    first, big = span(scene_ref)
    chip = chip_index()
    core = lax.axis_index(CORE)
    group = group_index()
    index = lax.axis_index(MICRO) * 4 + group
    first_loads = [
        pltpu.make_async_copy(source, target, in_sem.at[slot])
        for slot, (source, target) in enumerate(
            ((normed_ref, normed_buf), (mixed_ref.at[index], mixed_buf), (low_ref, low_buf))
        )
    ]
    scale = HD**-0.5

    def run(count):
        rows = count * TOK
        loads = [pltpu.make_async_copy(kvs_ref.at[pl.ds(first, count)], kv_buf.at[pl.ds(0, count)], kv_sem)]
        for load in loads + first_loads:
            load.start()
        weight_copies(w_ref, w_out_ref, w_sem)

        def cut(value):
            return [value[:, at:at + 128] for at in range(0, value.shape[1], 128)]

        every = cut(jnp.concatenate(
            [ref[pl.ds(first, count)].reshape(rows, 512) for ref in (gs_ref, go_ref)], axis=0
        ))
        grad, query = every[:2], every[2:]
        g_own = cut(gs_ref[chip])
        g_heads = [halves(g_own[0])[1], *halves(g_own[1])]
        own_stats = g_own[0].astype(F32)
        all_stats = grad[0].astype(F32).T
        wait_all(loads)
        kv = cut(jnp.concatenate(
            [kv_buf[:count].reshape(rows, 384), kvo_ref[pl.ds(first, count)].reshape(rows, 384)], axis=0
        ))
        own = cut(kv_buf[chip - first]) + g_own[2:]
        q_heads = [*halves(own[3]), own[4]]
        k_heads = [*halves(own[0]), halves(own[1])[0]]
        v_heads = [halves(own[1])[1], *halves(own[2])]

        def column(at):
            return own_stats[:, at:at + 1] + own_stats[:, at + 1:at + 2] + own_stats[:, at + 2:at + 3]

        def row(at):
            return all_stats[at:at + 1] + all_stats[at + 1:at + 2] + all_stats[at + 2:at + 3]

        dq, dk, dv = [], [], []
        for head, (kb, vb) in enumerate(((0, 1), (0, 2), (1, 2))):
            qb, gb = (0, 0, 1)[head], (0, 1, 1)[head]
            probs = jnp.exp(mm_nt(q_heads[head], kv[kb]) * scale - column(3 * head))
            gap = mm_nt(g_heads[head], kv[vb]) - column(9 + 3 * head)
            dq.append(mm((probs * gap).astype(BF), kv[kb]) * scale)
            probs = jnp.exp(mm_nt(k_heads[head], query[qb]) * scale - row(3 * head))
            gap = mm_nt(v_heads[head], grad[gb]) - row(9 + 3 * head)
            dv.append(mm(probs.astype(BF), grad[gb]))
            dk.append(mm((probs * gap).astype(BF), query[qb]) * scale)
        tail = dq[2]
        gqkv_ref[...] = jnp.concatenate(
            [join(dk[0], dk[1]), join(dk[2], dv[0]), join(dv[1], dv[2]), join(dq[0], dq[1]),
             join(tail, jnp.zeros_like(tail))],
            axis=1,
        ).astype(BF)


    @pl.when(big)
    def _():
        run(5)

    @pl.when(jnp.logical_not(big))
    def _():
        run(1)

    wait_all(first_loads)

    grad_buf[...] = mm_tn(normed_buf[...], gqkv_ref[...])
    low = jnp.concatenate([ref[...] for ref in (low_buf, low1_ref, low2_ref, low3_ref)], axis=0)
    mixed = jnp.concatenate(
        [mixed_buf[pl.ds(pl.multiple_of((group ^ k) * BLK, BLK), BLK)] for k in range(4)], axis=0
    )
    out = mm_tn(mixed, low)[HD:]
    for ref, owner in ((keep_ref, core), (send_ref, 1 - core)):
        for tile in range(8):
            rows = grad_buf[pl.ds(pl.multiple_of((2 * tile + owner) * 48, 16), 48)]
            at = (tile // 4) * 96
            pieces = [
                out[at + row * 48:at + (row + 1) * 48, (tile % 4) * 192:(tile % 4 + 1) * 192] for row in range(2)
            ]
            ref[2 * tile] = rows[:, :384].astype(BF)
            ref[2 * tile + 1] = jnp.concatenate(
                [rows[:, 384:576], jnp.where(owner == 1, pieces[1], pieces[0])], axis=1
            ).astype(BF)
    wait_all(weight_copies(w_ref, w_out_ref, w_sem, start=False))


def normed_grad_kernel(
    gqkv_ref, w_ref, tok_ref, vec_ref, near_ref, far_ref, own_ref, one_ref, two_ref, three_ref, sums_ref, ff_ref,
    x_buf, vec_buf, near_buf, part_buf, low_buf, sums_buf, ff_buf, in_sem, out_sem,
):
    loads = [
        pltpu.make_async_copy(tok_ref.at[lax.axis_index(MICRO)], x_buf, in_sem.at[0]),
        pltpu.make_async_copy(vec_ref, vec_buf, in_sem.at[1]),
        pltpu.make_async_copy(near_ref, near_buf, in_sem.at[2]),
    ]
    for load in loads:
        load.start()
    group = group_index()
    odd = (group % 2) == 1
    total = jnp.zeros((TOK, D), F32)
    for slot in range(3):
        part = gqkv_ref[:, slot * 192:(slot + 1) * 192]
        zero = jnp.zeros_like(part)
        wide = jnp.where(
            odd, jnp.concatenate([zero, part], axis=1), jnp.concatenate([part, zero], axis=1)
        )
        total = total + mm_nt(wide, w_ref[slot])
    part_buf[...] = total
    low_buf[...] = total.astype(BF)
    stores = []
    for k, ref in enumerate((own_ref, one_ref, two_ref, three_ref)):
        rows = pl.ds(pl.multiple_of((group ^ k) * BLK, BLK), BLK)
        stores.append(pltpu.make_async_copy((low_buf if k else part_buf).at[rows], ref, out_sem.at[k]))
        stores[-1].start()
    wait_all(loads)
    ff_buf[...] = (near_buf[...].astype(F32) + far_ref[...].astype(F32)).astype(BF)
    stores.append(pltpu.make_async_copy(ff_buf, ff_ref, out_sem.at[5]))
    stores[-1].start()
    unit, _ = normalized(x_buf[...].astype(F32))
    gain1 = jnp.sum(total * unit, axis=0, keepdims=True)
    shift1 = jnp.sum(total, axis=0, keepdims=True)
    sums_buf[...] = jnp.concatenate([gain1, shift1, vec_buf[...][:2], jnp.zeros((4, D), F32)], axis=0)
    stores.append(pltpu.make_async_copy(sums_buf, sums_ref, out_sem.at[4]))
    stores[-1].start()
    wait_all(stores)


def add_kernel(one_ref, two_ref, unused_ref, out_ref, buf, sem):
    buf[...] = (one_ref[...].astype(F32) + two_ref[...].astype(F32)).astype(BF)
    copy = pltpu.make_async_copy(buf, out_ref, sem)
    copy.start()
    copy.wait()


def sum_kernel(in_ref, vec_ref, out_ref, buf, vec_buf, sem, vec_sem):
    load = pltpu.make_async_copy(vec_ref, vec_buf, vec_sem)
    load.start()
    total = in_ref[0].astype(F32)
    for index in range(1, 16):
        total = total + in_ref[index].astype(F32)
    load.wait()
    vectors = vec_buf[...][:4]
    block = jnp.concatenate([total, vectors[:, :384], vectors[:, 384:]], axis=0).astype(BF)
    for index in range(8):
        buf[index] = block
    wait_all(send_copies(buf, out_ref, range(8), sem))


def spread_kernel(turn, in_ref, *refs):
    qkv_buf, out_buf, sem, out_sem = refs[-4:]
    qkv_ref, out_ref, *vec_refs = refs[3:-4] if turn else refs[:-4]
    owner = lax.axis_index(CORE)
    owner = 1 - owner if turn else owner
    copies = []
    vectors = jnp.zeros((8, 384), F32)
    for tile in range(8):
        whole = [in_ref[tile, index].astype(F32) for index in range(8)]
        block = [value[:48] for value in whole]
        for value in whole:
            vectors = vectors + value[48:]
        for part, half, at in ((1, 0, 0), (2, 0, 192), (0, 4, 0)):
            qkv_buf[tile, :, part * D:(part + 1) * D] = jnp.concatenate(
                [block[half + group][:, at:at + 192] for group in range(4)], axis=1
            )
        start = pl.multiple_of((2 * tile + owner) * 48, 16)
        copy = pltpu.make_async_copy(qkv_buf.at[tile], qkv_ref.at[pl.ds(start, 48)], sem.at[tile])
        copy.start()
        copies.append(copy)
        for group in range(4):
            out_buf[group, tile // 4, :, (tile % 4) * 192:(tile % 4 + 1) * 192] = block[4 + group][:, 192:]
    for group in range(4):
        for pair in range(2):
            start = pl.multiple_of(group * 192 + (pair * 2 + owner) * 48, 16)
            copy = pltpu.make_async_copy(
                out_buf.at[group, pair], out_ref.at[pl.ds(start, 48)], out_sem.at[group, pair]
            )
            copy.start()
            copies.append(copy)
    if turn:
        vectors = vectors + refs[0][...]
        for k, ref in enumerate(vec_refs):
            ref[...] = jnp.concatenate([vectors[k:k + 1], vectors[4 + k:5 + k]], axis=1).reshape(D)
    else:
        vec_refs[0][...] = vectors
    wait_all(copies)


def stack_kernel(*refs):
    y = lax.axis_index("y")
    for k, ref in enumerate(refs[:4]):
        refs[5][pl.ds((y ^ k) * 2, 2)] = ref[...]


def spread_ff_kernel(same_ref, other_ref, up_ref, down_ref):
    core = lax.axis_index(CORE)
    for ref, owner in ((same_ref, core), (other_ref, 1 - core)):
        for chip in range(8):
            block = ref[chip].astype(F32)
            up_ref[pl.ds(pl.multiple_of((chip * 2 + owner) * 48, 16), 48)] = block[:, :384]
            down_ref[chip * 48:(chip + 1) * 48, pl.ds(pl.multiple_of(owner * 384, 128), 384)] = block[:, 384:]


def input_kernel(
    own_ref, one_ref, two_ref, three_ref, tok_ref, gain_ref, grad_ref, result_ref, unused_ref, out_ref, buf, x_buf, sem, x_sem
):
    start = pl.multiple_of(group_index() * BLK, BLK)
    load = pltpu.make_async_copy(tok_ref.at[lax.axis_index(MICRO), pl.ds(start, BLK)], x_buf, x_sem)
    load.start()
    load.wait()
    total = own_ref[...]
    for ref in (one_ref, two_ref, three_ref):
        total = total + ref[...].astype(F32)
    unit, inverse = normalized(x_buf[...].astype(F32))
    grad = grad_ref[...] + norm_back(total, unit, inverse, gain_ref[...].reshape(1, D))
    buf[:BLK] = grad.astype(BF)
    buf[BLK:] = result_ref[...]
    wait_all(send_copies(buf, out_ref, range(8), sem))


def unpack_kernel(in_ref, unused_ref, other_ref, grad_ref, result_ref):
    for index in range(8):
        rows = slice(index % 4 * BLK, (index % 4 + 1) * BLK)
        grad_ref[index // 4, rows] = in_ref[index, :BLK].astype(F32)
        result_ref[index // 4, rows] = in_ref[index, BLK:]


def exchange(value, axes):
    return lax.all_to_all(value, axes, 0, 0, tiled=True)


def swap(value):
    return lax.ppermute(value, CORE, [(0, 1), (1, 0)])


def after(value, *others):
    return pl.pallas_call(
        lambda *refs: None,
        out_shape=jax.ShapeDtypeStruct(value.shape, value.dtype),
        in_specs=[pl.BlockSpec(memory_space=pl.ANY)] * (1 + len(others)),
        out_specs=pl.BlockSpec(memory_space=pl.ANY),
        input_output_aliases={0: 0},
        cost_estimate=pl.CostEstimate(flops=1, bytes_accessed=1, transcendentals=0),
        compiler_params=pltpu.CompilerParams(vmem_limit_bytes=2**20),
    )(value, *others)


def flip(value, axes, count, bits):
    return lax.ppermute(value, axes, [(index, index ^ bits) for index in range(count)])


def shards(
    tokens, scene_of_block, ln1_gain, ln1_shift, w_qkv, w_out, ln2_gain, ln2_shift, w_up, w_down, out_grad
):
    w_out_pad = jnp.pad(w_out.reshape(4, 192, D), ((0, 0), (HD, 0), (0, 0)))
    kv_send, normed = call(
        project_kernel,
        [((8, TOK, 384), BF, "H"), ((TOK, D), BF, "L")],
        [(tokens, "H"), (ln1_gain, "H"), (ln1_shift, "H"), (w_qkv, "H")],
        1000,
        [
            pltpu.VMEM((TOK, D), BF), pltpu.VMEM((2, D, 384), BF), pltpu.VMEM((TOK, 384), BF),
            pltpu.VMEM((D,), F32), pltpu.VMEM((D,), F32), DMA, DMA((2,)), DMA((8,)), DMA, DMA,
        ],
    )
    (query,) = call(
        query_kernel,
        [((TOK, 256), BF, "L")],
        [(normed, "L"), (w_qkv, "H")],
        1000,
        [pltpu.VMEM((1, D, 384), BF), DMA((1,))],
    )
    kv_same = exchange(kv_send, CHIP)
    kv_same = after(kv_same, pin(query))
    kv_other = swap(kv_same)
    (mixed_send,) = call(
        attend_kernel,
        [((8, TOK, 256), BF, "H")],
        [(scene_of_block, "S"), (query, "H"), (kv_same, "V"), (kv_other, "V")],
        1000,
        [pltpu.VMEM((TOK, 256), BF), pltpu.VMEM((TOK, 256), BF), DMA((8,)), DMA],
    )
    mixed = exchange(mixed_send, NARROW)
    (block_query,) = call(
        block_query_kernel,
        [((4, BLK, 256), BF, "L")],
        [(normed, "H"), (w_qkv, "H")],
        1000,
        [pltpu.VMEM((BLK, D), BF), pltpu.VMEM((D, D), BF), DMA, DMA],
    )
    ff_send, middle, normed2, act, grad_pre = call(
        forward_kernel,
        [
            ((8, 2 * BLK, D), BF, "H"), ((BLK, D), F32, "H"), ((2 * TOK, D), BF, "V"),
            ((2 * TOK, FFL), BF, "V"), ((2 * TOK, FFL), BF, "V"),
        ],
        [
            (mixed, "V"), (tokens, "H"), (out_grad, "H"), (w_out_pad, "V"), (ln2_gain, "H"), (ln2_shift, "H"),
            (w_up, "H"), (w_down, "H"),
        ],
        1000,
        [
            pltpu.VMEM((2, TOK, D), BF), pltpu.VMEM((2, TOK, D), BF), pltpu.VMEM((D, FFL), BF),
            pltpu.VMEM((FFL, D), BF), pltpu.VMEM((D,), F32), pltpu.VMEM((D,), F32), pltpu.VMEM((8, BLK, D), BF),
            pltpu.VMEM((8, BLK, D), BF), pltpu.VMEM((8, BLK, D), F32), DMA((6,)), DMA((3,)),
        ],
    )
    ff_sums = exchange(ff_send, NARROW)
    keep, send = call(
        ff_grads_kernel,
        [((8, 48, D), BF, "V")] * 2,
        [(normed2, "V"), (act, "V"), (grad_pre, "V"), (out_grad, "L")],
        1000,
        [pltpu.VMEM((D, FFL), F32), pltpu.VMEM((FFL, D), F32)],
    )
    pieces = call(
        split_kernel, [((2, 48, D), BF, "L")] * 4, [(keep, "V"), (swap(send), "V")], 1000
    )
    pieces = [pieces[0]] + [flip(pieces[k], "y", 4, k) for k in (1, 2, 3)]
    (ff_near,) = call(
        total_kernel,
        [((2, 48, D), BF, "L")],
        [(pieces[0], "L")] + [(piece, "V") for piece in pieces[1:]],
        1000,
    )
    grad_send, low, grad_mid, result_part, vec2 = call(
        middle_kernel,
        [
            ((8, 4, BLK, 512), BF, "H"), ((BLK, D), BF, "H"), ((BLK, D), F32, "H"), ((BLK, D), BF, "H"),
            ((8, D), F32, "H"),
        ],
        [
            (ff_sums, "V"), (middle, "H"), (out_grad, "H"), (mixed, "H"), (w_out_pad, "V"), (ln2_gain, "H"),
            (block_query, "H"),
        ],
        1000,
        [
            pltpu.VMEM((4, BLK, 512), BF), pltpu.VMEM((BLK, D), F32), pltpu.VMEM((BLK, D), BF),
            pltpu.VMEM((4, BLK, 256), BF), pltpu.VMEM((D,), F32), pltpu.VMEM((4, BLK, 256), BF), pltpu.VMEM((BLK, D), BF), pltpu.VMEM((BLK, D), F32),
            pltpu.VMEM((BLK, D), BF), pltpu.VMEM((8, D), F32), DMA((5,)), DMA((8,)), DMA((4,)),
        ],
    )
    grad_send = after(pin(grad_send), *pieces[1:])
    grad_same = exchange(grad_send.reshape(32, BLK, 512), (*CHIP, *GROUP)).reshape(8, TOK, 512)
    lows = [flip(low, GROUP, 4, k) for k in (1, 2, 3)]
    kv_same = after(pin(kv_same), low)
    kv_other = swap(kv_same)
    grad_same = after(grad_same, *lows, kv_other, pin(ff_near))
    grad_other = swap(grad_same)
    ff_near = after(pin(ff_near), grad_other)
    ff_far = flip(ff_near, "xl", 2, 1)
    gqkv, w_own, keep, send = call(
        attend_back_kernel,
        [((TOK, 640), BF, "V"), ((3, D, 384), BF, "V")] + [((16, 48, 384), BF, "V")] * 2,
        [
            (scene_of_block, "S"), (kv_same, "H"), (kv_other, "V"), (grad_same, "V"), (grad_other, "V"),
            (normed, "H"), (mixed, "H"), (low, "H"), *[(value, "V") for value in lows], (w_qkv, "H"),
        ],
        1000,
        [
            pltpu.VMEM((5, TOK, 384), BF), pltpu.VMEM((D, 640), F32),
            pltpu.VMEM((TOK, 256), BF), pltpu.VMEM((TOK, D), BF), pltpu.VMEM((BLK, D), BF),
            DMA, DMA((3,)), DMA((3,)),
        ],
        vmem=24,
    )
    own, *sends, sums, ff_part = call(
        normed_grad_kernel,
        [((BLK, D), F32, "H")] + [((BLK, D), BF, "H")] * 3 + [((8, D), F32, "H"), ((2, 48, D), BF, "H")],
        [(gqkv, "V"), (w_own, "V"), (tokens, "H"), (vec2, "H"), (ff_near, "H"), (ff_far, "V")],
        1000,
        [
            pltpu.VMEM((TOK, D), BF), pltpu.VMEM((8, D), F32), pltpu.VMEM((2, 48, D), BF), pltpu.VMEM((TOK, D), F32),
            pltpu.VMEM((TOK, D), BF), pltpu.VMEM((8, D), F32), pltpu.VMEM((2, 48, D), BF), DMA((3,)), DMA((6,)),
        ],
    )
    (weight_send,) = call(
        add_kernel,
        [((16, 48, 384), BF, "H")],
        [(keep, "V"), (swap(after(send, ff_far)), "V"), (own, "H")],
        1000,
        [pltpu.VMEM((16, 48, 384), BF), DMA],
    )
    weight_parts = exchange(weight_send, (*CHIP, MICRO))
    parts = [flip(value, GROUP, 4, k + 1) for k, value in enumerate(sends)]
    weight_parts = after(weight_parts, pin(sums), *parts)
    ff_parts = [flip(ff_part, "y", 4, k) for k in (1, 2, 3)]
    (weight_total,) = call(
        sum_kernel,
        [((8, 8, 56, 384), BF, "H")],
        [(weight_parts, "V"), (sums, "H")],
        1000,
        [pltpu.VMEM((8, 56, 384), BF), pltpu.VMEM((8, D), F32), DMA((8,)), DMA],
    )
    (packed,) = call(
        input_kernel,
        [((8, 2 * BLK, D), BF, "H")],
        [
            (own, "L"), *[(value, "V") for value in parts], (tokens, "H"), (ln1_gain, "L"), (grad_mid, "L"),
            (result_part, "L"), (weight_total, "H"),
        ],
        1000,
        [pltpu.VMEM((2 * BLK, D), BF), pltpu.VMEM((BLK, D), BF), DMA((8,)), DMA],
    )
    weight_same = exchange(weight_total.reshape(64, 56, 384), (*CHIP, *NARROW)).reshape(8, 8, 56, 384)
    (ff_same,) = call(
        stack_kernel,
        [((8, 48, D), BF, "L")],
        [(ff_part, "L"), *[(value, "V") for value in ff_parts], (packed, "H")],
        1000,
    )
    weight_same = after(weight_same, pin(packed), pin(ff_same))
    everyone = exchange(after(pin(packed), weight_same), NARROW)
    weight_other = swap(weight_same)
    up_grad, down_grad = call(
        spread_ff_kernel,
        [((D, FFL), F32, "L"), ((FFL, D), F32, "L")],
        [(ff_same, "L"), (swap(ff_same), "V")],
        1000,
    )
    scratch = [
        pltpu.VMEM((8, 48, 3 * D), F32), pltpu.VMEM((4, 2, 48, D), F32), DMA((8,)), DMA((4, 2)),
    ]
    grads = [((D, 3 * D), F32, "H"), ((D, D), F32, "H")]
    half = call(
        functools.partial(spread_kernel, False),
        grads + [((8, 384), F32, "V")],
        [(weight_same, "V")],
        1000,
        scratch,
    )
    qkv_grad, out_proj_grad, *vectors = call(
        functools.partial(spread_kernel, True),
        grads + [((D,), F32, "L")] * 4,
        [(weight_other, "V"), (half[2], "V"), (half[0], "H"), (half[1], "H")],
        1000,
        scratch,
        aliases={2: 0, 3: 1},
    )
    input_grad, result = call(
        unpack_kernel, [((2, TOK, D), F32, "L"), ((2, TOK, D), BF, "L")], [(everyone, "V"), (vectors[0], "H"), (up_grad, "H")], 1000
    )
    return (
        result, input_grad, qkv_grad, out_proj_grad, *vectors, up_grad, down_grad
    )


def solution(mesh):
    names = ("y", "xl", "c", "zh", "zl", "xh")
    fine = Mesh(mesh.devices.reshape(4, 2, 2, 2, 2, 2), names)
    tokens = P(None, WIDE, None)
    placed = (
        tokens, P(), P(), P(), P(), P(), P(), P(), P(None, NARROW), P(NARROW, None), tokens
    )
    return jax.shard_map(
        shards,
        mesh=fine,
        in_specs=placed,
        out_specs=(
            tokens, tokens, P(), P(), P(), P(), P(), P(), P(None, NARROW), P(NARROW, None)
        ),
        check_vma=False,
    )
```

```python
import functools

import jax
import jax.numpy as jnp
from jax import lax
from jax.experimental import pallas as pl
from jax.experimental.pallas import tpu as pltpu
from jax.sharding import Mesh
from jax.sharding import PartitionSpec as P

D = 768
HD = 64
FFL = 384
TOK = 128
BLK = 32
EPS = 1e-05
BF = jnp.bfloat16
F32 = jnp.float32

CHIP = ("y", "xl")
CORE = "c"
MICRO = "zh"
GROUP = ("zl", "xh")
NARROW = (MICRO, *GROUP)
WIDE = (*CHIP, CORE)


def chip_index():
    return lax.axis_index("y") * 2 + lax.axis_index("xl")


def group_index():
    return lax.axis_index("zl") * 2 + lax.axis_index("xh")


def mm(left, right):
    return lax.dot_general(left, right, (((1,), (0,)), ((), ())), preferred_element_type=F32)


def mm_nt(left, right):
    return lax.dot_general(left, right, (((1,), (1,)), ((), ())), preferred_element_type=F32)


def mm_tn(left, right):
    return lax.dot_general(left, right, (((0,), (0,)), ((), ())), preferred_element_type=F32)


def normalized(values):
    center = values - jnp.mean(values, axis=-1, keepdims=True)
    spread = jnp.mean(center * center, axis=-1, keepdims=True)
    inverse = lax.rsqrt(spread + EPS)
    return center * inverse, inverse


def norm_back(grad, unit, inverse, gain):
    scaled = grad * gain
    first = jnp.mean(scaled, axis=-1, keepdims=True)
    second = jnp.mean(scaled * unit, axis=-1, keepdims=True)
    return inverse * (scaled - first - unit * second)


def halves(block):
    lane = lax.broadcasted_iota(jnp.int32, block.shape, 1)
    zero = jnp.zeros_like(block)
    return jnp.where(lane < HD, block, zero), jnp.where(lane < HD, zero, block)


def join(low, high):
    lane = lax.broadcasted_iota(jnp.int32, low.shape, 1)
    return jnp.where(lane < HD, low, high)


def span(scene_ref):
    micro = lax.axis_index(MICRO)
    own = scene_ref[micro, chip_index() * 4]
    first = jnp.int32(0)
    count = jnp.int32(0)
    for index in range(8):
        other = scene_ref[micro, index * 4]
        first += (other < own).astype(jnp.int32)
        count += (other == own).astype(jnp.int32)
    return first, count > 1


def three(value):
    a = value.astype(BF).astype(F32)
    b = (value - a).astype(BF).astype(F32)
    c = value - a - b
    return a, b, c


def put_columns(width, rows, start, columns):
    lane = lax.broadcasted_iota(jnp.int32, (rows, width), 1)
    out = jnp.zeros((rows, width), F32)
    for offset, column in enumerate(columns):
        out = jnp.where(lane == start + offset, column, out)
    return out


def pin(value):
    return pltpu.with_memory_space_constraint(value, pltpu.HBM)


def call(kernel, outs, ins, cost, scratch=(), vmem=16, aliases=None):
    places = {"V": pltpu.VMEM, "H": pltpu.HBM, "S": pltpu.SMEM, "L": pltpu.VMEM}
    return pl.pallas_call(
        kernel,
        out_shape=[
            (pltpu.HBM if place in "HL" else jax.ShapeDtypeStruct)(shape, dtype) for shape, dtype, place in outs
        ],
        in_specs=[pl.BlockSpec(memory_space=places[place]) for _, place in ins],
        out_specs=[pl.BlockSpec(memory_space=places[place]) for _, _, place in outs],
        scratch_shapes=list(scratch),
        input_output_aliases=aliases or {},
        cost_estimate=pl.CostEstimate(flops=cost, bytes_accessed=1000, transcendentals=0),
        compiler_params=pltpu.CompilerParams(vmem_limit_bytes=vmem * 2**20),
    )(*[pin(value) if place in "HL" else value for value, place in ins])


DMA = pltpu.SemaphoreType.DMA


def send_copies(source, target, indices, sem):
    copies = [pltpu.make_async_copy(source, target.at[index], sem.at[index]) for index in indices]
    for copy in copies:
        copy.start()
    return copies


def wait_all(copies):
    for copy in copies:
        copy.wait()


def weight_copies(w_ref, w_buf, w_sem, parts=(1, 2, 0), start=True):
    group = group_index()
    copies = []
    for slot, part in enumerate(parts):
        column = pl.multiple_of(part * D + (group // 2) * 384, 128)
        copy = pltpu.make_async_copy(w_ref.at[:, pl.ds(column, 384)], w_buf.at[slot], w_sem.at[slot])
        if start:
            copy.start()
        copies.append(copy)
    return copies


def own_heads(full):
    odd = (group_index() % 2) == 1
    return jnp.where(odd, full[:, 192:], full[:, :192]).astype(BF)


def project_kernel(
    tok_ref, gain_ref, shift_ref, w_ref, kv_ref, normed_ref,
    x_buf, w_buf, kv_buf, gain_buf, shift_buf, x_sem, w_sem, kv_sem, gain_sem, shift_sem,
):
    copy_x = pltpu.make_async_copy(tok_ref.at[lax.axis_index(MICRO)], x_buf, x_sem)
    copy_x.start()
    copy_gain = pltpu.make_async_copy(gain_ref, gain_buf, gain_sem)
    copy_gain.start()
    copy_shift = pltpu.make_async_copy(shift_ref, shift_buf, shift_sem)
    copy_shift.start()
    copies = weight_copies(w_ref, w_buf, w_sem, (1, 2))
    wait_all([copy_x, copy_gain, copy_shift])
    unit, _ = normalized(x_buf[...].astype(F32))
    normed = (unit * gain_buf[...].reshape(1, D) + shift_buf[...].reshape(1, D)).astype(BF)
    normed_ref[...] = normed
    parts = []
    for slot in range(2):
        copies[slot].wait()
        parts.append(own_heads(mm(normed, w_buf[slot])))
    kv_buf[...] = jnp.concatenate(parts, axis=1)
    wait_all(send_copies(kv_buf, kv_ref, range(8), kv_sem))


def query_kernel(normed_ref, w_ref, q_ref, w_buf, w_sem):
    weight_copies(w_ref, w_buf, w_sem, (0,))[0].wait()
    part = own_heads(mm(normed_ref[...], w_buf[0]))
    q_ref[...] = jnp.concatenate([part, jnp.zeros((TOK, HD), BF)], axis=1)


def block_query_kernel(normed_ref, w_ref, out_ref, x_buf, w_buf, x_sem, w_sem):
    block = pl.ds(pl.multiple_of(group_index() * BLK, BLK), BLK)
    loads = [
        pltpu.make_async_copy(normed_ref.at[block], x_buf, x_sem),
        pltpu.make_async_copy(w_ref.at[:, pl.ds(0, D)], w_buf, w_sem),
    ]
    for load in loads:
        load.start()
    wait_all(loads)
    query = mm(x_buf[...], w_buf[...]).astype(BF)
    zero = jnp.zeros((BLK, HD), BF)
    for group in range(4):
        out_ref[group] = jnp.concatenate([query[:, group * 192:(group + 1) * 192], zero], axis=1)


def attend_kernel(scene_ref, q_ref, same_ref, other_ref, out_ref, buf, q_buf, sem, q_sem):
    load = pltpu.make_async_copy(q_ref, q_buf, q_sem)
    load.start()
    first, big = span(scene_ref)

    def run(count):
        rows = count * TOK
        keys = jnp.concatenate(
            [ref[pl.ds(first, count)].reshape(rows, 384) for ref in (same_ref, other_ref)], axis=0
        )
        load.wait()
        query = q_buf[...]
        q0, q1 = halves(query[:, :128])
        blocks = [keys[:, :128], keys[:, 128:256], keys[:, 256:]]
        mixed = []
        columns = []
        for qh, kb, vb in ((q0, 0, 1), (q1, 0, 2), (query[:, 128:], 1, 2)):
            scores = mm_nt(qh, blocks[kb]) * (HD**-0.5)
            top = jnp.max(scores, axis=-1, keepdims=True)
            weights = jnp.exp(scores - top)
            total = jnp.sum(weights, axis=-1, keepdims=True)
            probs = (weights * (1.0 / total)).astype(BF)
            mixed.append(mm(probs, blocks[vb]))
            columns += three(top + jnp.log(total))
        stats = put_columns(128, TOK, 0, columns)
        buf[...] = jnp.concatenate([join(stats, mixed[0]), join(mixed[1], mixed[2])], axis=1).astype(BF)

    @pl.when(big)
    def _():
        run(5)

    @pl.when(jnp.logical_not(big))
    def _():
        run(1)

    wait_all(send_copies(buf, out_ref, range(8), sem))


def forward_kernel(
    mixed_ref, tok_ref, og_ref, wo_ref, gain_ref, shift_ref, up_ref, down_ref,
    out_ref, middle_ref, normed_ref, act_ref, gpre_ref,
    tok_buf, og_buf, up_buf, down_buf, gain_buf, shift_buf, grad_buf, branch_buf, middle_buf, in_sem, sem,
):
    loads = [
        pltpu.make_async_copy(ref, buf, in_sem.at[index])
        for index, (ref, buf) in enumerate(
            (
                (tok_ref, tok_buf), (up_ref, up_buf), (og_ref, og_buf), (down_ref, down_buf), (gain_ref, gain_buf),
                (shift_ref, shift_buf),
            )
        )
    ]
    for load in loads:
        load.start()
    total = jnp.zeros((2 * TOK, D), F32)
    for group in range(4):
        rows = jnp.concatenate([mixed_ref[group], mixed_ref[4 + group]], axis=0)
        total = total + mm(rows, wo_ref[group])
    loads[0].wait()
    total = total + tok_buf[...].reshape(2 * TOK, D).astype(F32)
    middle_buf[...] = total.reshape(8, BLK, D)
    third = pltpu.make_async_copy(
        middle_buf.at[lax.axis_index(MICRO) * 4 + group_index()], middle_ref, sem.at[2]
    )
    third.start()
    unit, _ = normalized(total)
    wait_all(loads[4:])
    normed = (unit * gain_buf[...].reshape(1, D) + shift_buf[...].reshape(1, D)).astype(BF)
    normed_ref[...] = normed
    loads[1].wait()
    pre = mm(normed, up_buf[...])
    cdf = 0.5 * (1.0 + lax.erf(pre * (0.5**0.5)))
    slope = cdf + pre * jnp.exp(-0.5 * pre * pre) * 0.3989422804014327
    loads[2].wait()
    loads[3].wait()
    grad_out = og_buf[...].reshape(2 * TOK, D)
    gpre = (mm_nt(grad_out, down_buf[...]) * slope).astype(BF)
    gpre_ref[...] = gpre
    grad_buf[...] = mm_nt(gpre, up_buf[...]).astype(BF).reshape(8, BLK, D)
    first = pltpu.make_async_copy(grad_buf, out_ref.at[:, pl.ds(BLK, BLK)], sem.at[0])
    first.start()
    act = (pre * cdf).astype(BF)
    act_ref[...] = act
    branch_buf[...] = mm(act, down_buf[...]).astype(BF).reshape(8, BLK, D)
    second = pltpu.make_async_copy(branch_buf, out_ref.at[:, pl.ds(0, BLK)], sem.at[1])
    second.start()
    wait_all([first, second, third])


def ff_grads_kernel(normed_ref, act_ref, gpre_ref, og_ref, keep_ref, send_ref, up_buf, down_buf):
    core = lax.axis_index(CORE)
    up_buf[...] = mm_tn(normed_ref[...], gpre_ref[...])
    down_buf[...] = mm_tn(act_ref[...], og_ref[...].reshape(2 * TOK, D))
    for ref, owner in ((keep_ref, core), (send_ref, 1 - core)):
        column = pl.multiple_of(owner * 384, 128)
        for tile in range(8):
            rows = pl.ds(pl.multiple_of((2 * tile + owner) * 48, 16), 48)
            ref[tile, :, :384] = up_buf[rows].astype(BF)
            ref[tile, :, 384:] = down_buf[tile * 48:(tile + 1) * 48, pl.ds(column, 384)].astype(BF)


def split_kernel(one_ref, two_ref, *refs):
    y = lax.axis_index("y")
    for k, ref in enumerate(refs):
        for xl in range(2):
            at = (y ^ k) * 2 + xl
            ref[xl] = (one_ref[at].astype(F32) + two_ref[at].astype(F32)).astype(BF)


def total_kernel(*refs):
    total = refs[0][...].astype(F32)
    for ref in refs[1:4]:
        total = total + ref[...].astype(F32)
    refs[4][...] = total.astype(BF)


def middle_kernel(
    sums_ref, middle_ref, og_ref, mixed_ref, wo_ref, gain_ref, query_ref,
    out_ref, low_ref, grad_ref, result_ref, vec_ref,
    buf, middle_buf, og_buf, mixed_buf, gain_buf, query_buf, low_buf, grad_buf, result_buf, vec_buf, in_sem, sem, rest_sem,
):
    micro = lax.axis_index(MICRO)
    group = group_index()
    block = pl.ds(pl.multiple_of(group * BLK, BLK), BLK)
    loads = [
        pltpu.make_async_copy(middle_ref, middle_buf, in_sem.at[0]),
        pltpu.make_async_copy(og_ref.at[micro, block], og_buf, in_sem.at[1]),
        pltpu.make_async_copy(mixed_ref.at[pl.ds(micro * 4, 4), block], mixed_buf, in_sem.at[2]),
        pltpu.make_async_copy(gain_ref, gain_buf, in_sem.at[3]),
        pltpu.make_async_copy(query_ref, query_buf, in_sem.at[4]),
    ]
    for load in loads:
        load.start()
    total = sums_ref[0].astype(F32)
    for index in range(1, 8):
        total = total + sums_ref[index].astype(F32)
    branch, grad = total[:BLK], total[BLK:]
    wait_all(loads)
    middle = middle_buf[...]
    unit, inverse = normalized(middle)
    grad_mid = og_buf[...].astype(F32) + norm_back(grad, unit, inverse, gain_buf[...].reshape(1, D))
    low = grad_mid.astype(BF)
    low_buf[...] = low
    grad_buf[...] = grad_mid
    result_buf[...] = (middle + branch).astype(BF)
    gain_grad = jnp.sum(grad * unit, axis=0, keepdims=True)
    shift_grad = jnp.sum(grad, axis=0, keepdims=True)
    vec_buf[...] = jnp.concatenate([gain_grad, shift_grad, jnp.zeros((6, D), F32)], axis=0)
    stores = [
        pltpu.make_async_copy(source, target, rest_sem.at[index])
        for index, (source, target) in enumerate(
            ((low_buf, low_ref), (grad_buf, grad_ref), (result_buf, result_ref), (vec_buf, vec_ref))
        )
    ]
    for store in stores:
        store.start()
    lane = lax.broadcasted_iota(jnp.int32, (BLK, 256), 1)
    for head_group in range(4):
        mixed = mixed_buf[head_group].astype(F32)
        back = mm_nt(low, wo_ref[head_group]).astype(BF).astype(F32)
        product = mixed * back
        columns = []
        for head in range(3):
            inside = (lane >= (head + 1) * HD) & (lane < (head + 2) * HD)
            columns += three(jnp.sum(jnp.where(inside, product, 0.0), axis=-1, keepdims=True))
        stats = put_columns(256, BLK, 9, columns)
        buf[head_group, :, :256] = jnp.where(lane < 9, mixed, jnp.where(lane < HD, stats, back)).astype(BF)
        buf[head_group, :, 256:] = query_buf[head_group]
    sends = send_copies(buf, out_ref, range(8), sem)
    wait_all(stores)
    wait_all(sends)


def attend_back_kernel(
    scene_ref, kvs_ref, kvo_ref, gs_ref, go_ref, normed_ref, mixed_ref, low_ref, low1_ref, low2_ref, low3_ref,
    w_ref, gqkv_ref, w_out_ref, keep_ref, send_ref,
    kv_buf, grad_buf, mixed_buf, normed_buf, low_buf, kv_sem, in_sem, w_sem,
):
    first, big = span(scene_ref)
    chip = chip_index()
    core = lax.axis_index(CORE)
    group = group_index()
    index = lax.axis_index(MICRO) * 4 + group
    first_loads = [
        pltpu.make_async_copy(source, target, in_sem.at[slot])
        for slot, (source, target) in enumerate(
            ((normed_ref, normed_buf), (mixed_ref.at[index], mixed_buf), (low_ref, low_buf))
        )
    ]
    scale = HD**-0.5

    def run(count):
        rows = count * TOK
        loads = [pltpu.make_async_copy(kvs_ref.at[pl.ds(first, count)], kv_buf.at[pl.ds(0, count)], kv_sem)]
        for load in loads + first_loads:
            load.start()
        weight_copies(w_ref, w_out_ref, w_sem)

        def cut(value):
            return [value[:, at:at + 128] for at in range(0, value.shape[1], 128)]

        every = cut(jnp.concatenate(
            [ref[pl.ds(first, count)].reshape(rows, 512) for ref in (gs_ref, go_ref)], axis=0
        ))
        grad, query = every[:2], every[2:]
        g_own = cut(gs_ref[chip])
        g_heads = [halves(g_own[0])[1], *halves(g_own[1])]
        own_stats = g_own[0].astype(F32)
        all_stats = grad[0].astype(F32).T
        wait_all(loads)
        kv = cut(jnp.concatenate(
            [kv_buf[:count].reshape(rows, 384), kvo_ref[pl.ds(first, count)].reshape(rows, 384)], axis=0
        ))
        own = cut(kv_buf[chip - first]) + g_own[2:]
        q_heads = [*halves(own[3]), own[4]]
        k_heads = [*halves(own[0]), halves(own[1])[0]]
        v_heads = [halves(own[1])[1], *halves(own[2])]

        def column(at):
            return own_stats[:, at:at + 1] + own_stats[:, at + 1:at + 2] + own_stats[:, at + 2:at + 3]

        def row(at):
            return all_stats[at:at + 1] + all_stats[at + 1:at + 2] + all_stats[at + 2:at + 3]

        dq, dk, dv = [], [], []
        for head, (kb, vb) in enumerate(((0, 1), (0, 2), (1, 2))):
            qb, gb = (0, 0, 1)[head], (0, 1, 1)[head]
            probs = jnp.exp(mm_nt(q_heads[head], kv[kb]) * scale - column(3 * head))
            gap = mm_nt(g_heads[head], kv[vb]) - column(9 + 3 * head)
            dq.append(mm((probs * gap).astype(BF), kv[kb]) * scale)
            probs = jnp.exp(mm_nt(k_heads[head], query[qb]) * scale - row(3 * head))
            gap = mm_nt(v_heads[head], grad[gb]) - row(9 + 3 * head)
            dv.append(mm(probs.astype(BF), grad[gb]))
            dk.append(mm((probs * gap).astype(BF), query[qb]) * scale)
        tail = dq[2]
        gqkv_ref[...] = jnp.concatenate(
            [join(dk[0], dk[1]), join(dk[2], dv[0]), join(dv[1], dv[2]), join(dq[0], dq[1]),
             join(tail, jnp.zeros_like(tail))],
            axis=1,
        ).astype(BF)


    @pl.when(big)
    def _():
        run(5)

    @pl.when(jnp.logical_not(big))
    def _():
        run(1)

    wait_all(first_loads)

    grad_buf[...] = mm_tn(normed_buf[...], gqkv_ref[...])
    low = jnp.concatenate([ref[...] for ref in (low_buf, low1_ref, low2_ref, low3_ref)], axis=0)
    mixed = jnp.concatenate(
        [mixed_buf[pl.ds(pl.multiple_of((group ^ k) * BLK, BLK), BLK)] for k in range(4)], axis=0
    )
    out = mm_tn(mixed, low)[HD:]
    for ref, owner in ((keep_ref, core), (send_ref, 1 - core)):
        for tile in range(8):
            rows = grad_buf[pl.ds(pl.multiple_of((2 * tile + owner) * 48, 16), 48)]
            at = (tile // 4) * 96
            pieces = [
                out[at + row * 48:at + (row + 1) * 48, (tile % 4) * 192:(tile % 4 + 1) * 192] for row in range(2)
            ]
            ref[2 * tile] = rows[:, :384].astype(BF)
            ref[2 * tile + 1] = jnp.concatenate(
                [rows[:, 384:576], jnp.where(owner == 1, pieces[1], pieces[0])], axis=1
            ).astype(BF)
    wait_all(weight_copies(w_ref, w_out_ref, w_sem, start=False))


def normed_grad_kernel(
    gqkv_ref, w_ref, tok_ref, vec_ref, near_ref, far_ref, own_ref, one_ref, two_ref, three_ref, sums_ref, ff_ref,
    x_buf, vec_buf, near_buf, part_buf, low_buf, sums_buf, ff_buf, in_sem, out_sem,
):
    loads = [
        pltpu.make_async_copy(tok_ref.at[lax.axis_index(MICRO)], x_buf, in_sem.at[0]),
        pltpu.make_async_copy(vec_ref, vec_buf, in_sem.at[1]),
        pltpu.make_async_copy(near_ref, near_buf, in_sem.at[2]),
    ]
    for load in loads:
        load.start()
    group = group_index()
    odd = (group % 2) == 1
    total = jnp.zeros((TOK, D), F32)
    for slot in range(3):
        part = gqkv_ref[:, slot * 192:(slot + 1) * 192]
        zero = jnp.zeros_like(part)
        wide = jnp.where(
            odd, jnp.concatenate([zero, part], axis=1), jnp.concatenate([part, zero], axis=1)
        )
        total = total + mm_nt(wide, w_ref[slot])
    part_buf[...] = total
    low_buf[...] = total.astype(BF)
    stores = []
    for k, ref in enumerate((own_ref, one_ref, two_ref, three_ref)):
        rows = pl.ds(pl.multiple_of((group ^ k) * BLK, BLK), BLK)
        stores.append(pltpu.make_async_copy((low_buf if k else part_buf).at[rows], ref, out_sem.at[k]))
        stores[-1].start()
    wait_all(loads)
    ff_buf[...] = (near_buf[...].astype(F32) + far_ref[...].astype(F32)).astype(BF)
    stores.append(pltpu.make_async_copy(ff_buf, ff_ref, out_sem.at[5]))
    stores[-1].start()
    unit, _ = normalized(x_buf[...].astype(F32))
    gain1 = jnp.sum(total * unit, axis=0, keepdims=True)
    shift1 = jnp.sum(total, axis=0, keepdims=True)
    sums_buf[...] = jnp.concatenate([gain1, shift1, vec_buf[...][:2], jnp.zeros((4, D), F32)], axis=0)
    stores.append(pltpu.make_async_copy(sums_buf, sums_ref, out_sem.at[4]))
    stores[-1].start()
    wait_all(stores)


def add_kernel(one_ref, two_ref, unused_ref, out_ref, buf, sem):
    buf[...] = (one_ref[...].astype(F32) + two_ref[...].astype(F32)).astype(BF)
    copy = pltpu.make_async_copy(buf, out_ref, sem)
    copy.start()
    copy.wait()


def sum_kernel(in_ref, vec_ref, out_ref, buf, vec_buf, sem, vec_sem):
    load = pltpu.make_async_copy(vec_ref, vec_buf, vec_sem)
    load.start()
    total = in_ref[0].astype(F32)
    for index in range(1, 16):
        total = total + in_ref[index].astype(F32)
    load.wait()
    vectors = vec_buf[...][:4]
    block = jnp.concatenate([total, vectors[:, :384], vectors[:, 384:]], axis=0).astype(BF)
    for index in range(8):
        buf[index] = block
    wait_all(send_copies(buf, out_ref, range(8), sem))


def spread_kernel(turn, in_ref, *refs):
    qkv_buf, out_buf, sem, out_sem = refs[-4:]
    qkv_ref, out_ref, *vec_refs = refs[3:-4] if turn else refs[:-4]
    owner = lax.axis_index(CORE)
    owner = 1 - owner if turn else owner
    copies = []
    vectors = jnp.zeros((8, 384), F32)
    for tile in range(8):
        whole = [in_ref[tile, index].astype(F32) for index in range(8)]
        block = [value[:48] for value in whole]
        for value in whole:
            vectors = vectors + value[48:]
        for part, half, at in ((1, 0, 0), (2, 0, 192), (0, 4, 0)):
            qkv_buf[tile, :, part * D:(part + 1) * D] = jnp.concatenate(
                [block[half + group][:, at:at + 192] for group in range(4)], axis=1
            )
        start = pl.multiple_of((2 * tile + owner) * 48, 16)
        copy = pltpu.make_async_copy(qkv_buf.at[tile], qkv_ref.at[pl.ds(start, 48)], sem.at[tile])
        copy.start()
        copies.append(copy)
        for group in range(4):
            out_buf[group, tile // 4, :, (tile % 4) * 192:(tile % 4 + 1) * 192] = block[4 + group][:, 192:]
    for group in range(4):
        for pair in range(2):
            start = pl.multiple_of(group * 192 + (pair * 2 + owner) * 48, 16)
            copy = pltpu.make_async_copy(
                out_buf.at[group, pair], out_ref.at[pl.ds(start, 48)], out_sem.at[group, pair]
            )
            copy.start()
            copies.append(copy)
    if turn:
        vectors = vectors + refs[0][...]
        for k, ref in enumerate(vec_refs):
            ref[...] = jnp.concatenate([vectors[k:k + 1], vectors[4 + k:5 + k]], axis=1).reshape(D)
    else:
        vec_refs[0][...] = vectors
    wait_all(copies)


def spread_ff_kernel(*refs):
    up_ref, down_ref = refs[8:]
    y, core = lax.axis_index("y"), lax.axis_index(CORE)
    for index, ref in enumerate(refs[:8]):
        owner = core ^ (index // 4)
        for xl in range(2):
            chip = (y ^ (index % 4)) * 2 + xl
            block = ref[xl].astype(F32)
            up_ref[pl.ds(pl.multiple_of((chip * 2 + owner) * 48, 16), 48)] = block[:, :384]
            down_ref[
                pl.ds(pl.multiple_of(chip * 48, 16), 48), pl.ds(pl.multiple_of(owner * 384, 128), 384)
            ] = block[:, 384:]


def input_kernel(
    own_ref, one_ref, two_ref, three_ref, tok_ref, gain_ref, grad_ref, result_ref, unused_ref, out_ref, buf, x_buf, sem, x_sem
):
    start = pl.multiple_of(group_index() * BLK, BLK)
    load = pltpu.make_async_copy(tok_ref.at[lax.axis_index(MICRO), pl.ds(start, BLK)], x_buf, x_sem)
    load.start()
    load.wait()
    total = own_ref[...]
    for ref in (one_ref, two_ref, three_ref):
        total = total + ref[...].astype(F32)
    unit, inverse = normalized(x_buf[...].astype(F32))
    grad = grad_ref[...] + norm_back(total, unit, inverse, gain_ref[...].reshape(1, D))
    buf[:BLK] = grad.astype(BF)
    buf[BLK:] = result_ref[...]
    wait_all(send_copies(buf, out_ref, range(8), sem))


def unpack_kernel(in_ref, unused_ref, other_ref, grad_ref, result_ref):
    for index in range(8):
        rows = slice(index % 4 * BLK, (index % 4 + 1) * BLK)
        grad_ref[index // 4, rows] = in_ref[index, :BLK].astype(F32)
        result_ref[index // 4, rows] = in_ref[index, BLK:]


def exchange(value, axes):
    return lax.all_to_all(value, axes, 0, 0, tiled=True)


def swap(value):
    return lax.ppermute(value, CORE, [(0, 1), (1, 0)])


def after(value, *others):
    return pl.pallas_call(
        lambda *refs: None,
        out_shape=jax.ShapeDtypeStruct(value.shape, value.dtype),
        in_specs=[pl.BlockSpec(memory_space=pl.ANY)] * (1 + len(others)),
        out_specs=pl.BlockSpec(memory_space=pl.ANY),
        input_output_aliases={0: 0},
        cost_estimate=pl.CostEstimate(flops=1, bytes_accessed=1, transcendentals=0),
        compiler_params=pltpu.CompilerParams(vmem_limit_bytes=2**20),
    )(value, *others)


def flip(value, axes, count, bits):
    return lax.ppermute(value, axes, [(index, index ^ bits) for index in range(count)])


def shards(
    tokens, scene_of_block, ln1_gain, ln1_shift, w_qkv, w_out, ln2_gain, ln2_shift, w_up, w_down, out_grad
):
    w_out_pad = jnp.pad(w_out.reshape(4, 192, D), ((0, 0), (HD, 0), (0, 0)))
    kv_send, normed = call(
        project_kernel,
        [((8, TOK, 384), BF, "H"), ((TOK, D), BF, "L")],
        [(tokens, "H"), (ln1_gain, "H"), (ln1_shift, "H"), (w_qkv, "H")],
        1000,
        [
            pltpu.VMEM((TOK, D), BF), pltpu.VMEM((2, D, 384), BF), pltpu.VMEM((TOK, 384), BF),
            pltpu.VMEM((D,), F32), pltpu.VMEM((D,), F32), DMA, DMA((2,)), DMA((8,)), DMA, DMA,
        ],
    )
    (query,) = call(
        query_kernel,
        [((TOK, 256), BF, "L")],
        [(normed, "L"), (w_qkv, "H")],
        1000,
        [pltpu.VMEM((1, D, 384), BF), DMA((1,))],
    )
    kv_same = exchange(kv_send, CHIP)
    kv_same = after(kv_same, pin(query))
    kv_other = swap(kv_same)
    (mixed_send,) = call(
        attend_kernel,
        [((8, TOK, 256), BF, "H")],
        [(scene_of_block, "S"), (query, "H"), (kv_same, "V"), (kv_other, "V")],
        1000,
        [pltpu.VMEM((TOK, 256), BF), pltpu.VMEM((TOK, 256), BF), DMA((8,)), DMA],
    )
    mixed = exchange(mixed_send, NARROW)
    (block_query,) = call(
        block_query_kernel,
        [((4, BLK, 256), BF, "L")],
        [(normed, "H"), (w_qkv, "H")],
        1000,
        [pltpu.VMEM((BLK, D), BF), pltpu.VMEM((D, D), BF), DMA, DMA],
    )
    ff_send, middle, normed2, act, grad_pre = call(
        forward_kernel,
        [
            ((8, 2 * BLK, D), BF, "H"), ((BLK, D), F32, "H"), ((2 * TOK, D), BF, "V"),
            ((2 * TOK, FFL), BF, "V"), ((2 * TOK, FFL), BF, "V"),
        ],
        [
            (mixed, "V"), (tokens, "H"), (out_grad, "H"), (w_out_pad, "V"), (ln2_gain, "H"), (ln2_shift, "H"),
            (w_up, "H"), (w_down, "H"),
        ],
        1000,
        [
            pltpu.VMEM((2, TOK, D), BF), pltpu.VMEM((2, TOK, D), BF), pltpu.VMEM((D, FFL), BF),
            pltpu.VMEM((FFL, D), BF), pltpu.VMEM((D,), F32), pltpu.VMEM((D,), F32), pltpu.VMEM((8, BLK, D), BF),
            pltpu.VMEM((8, BLK, D), BF), pltpu.VMEM((8, BLK, D), F32), DMA((6,)), DMA((3,)),
        ],
    )
    ff_sums = exchange(ff_send, NARROW)
    keep, send = call(
        ff_grads_kernel,
        [((8, 48, D), BF, "V")] * 2,
        [(normed2, "V"), (act, "V"), (grad_pre, "V"), (out_grad, "L")],
        1000,
        [pltpu.VMEM((D, FFL), F32), pltpu.VMEM((FFL, D), F32)],
    )
    pieces = call(
        split_kernel, [((2, 48, D), BF, "L")] * 4, [(keep, "V"), (swap(send), "V")], 1000
    )
    pieces = [pieces[0]] + [flip(pieces[k], "y", 4, k) for k in (1, 2, 3)]
    (ff_near,) = call(
        total_kernel,
        [((2, 48, D), BF, "L")],
        [(pieces[0], "L")] + [(piece, "V") for piece in pieces[1:]],
        1000,
    )
    grad_send, low, grad_mid, result_part, vec2 = call(
        middle_kernel,
        [
            ((8, 4, BLK, 512), BF, "H"), ((BLK, D), BF, "H"), ((BLK, D), F32, "H"), ((BLK, D), BF, "H"),
            ((8, D), F32, "H"),
        ],
        [
            (ff_sums, "V"), (middle, "H"), (out_grad, "H"), (mixed, "H"), (w_out_pad, "V"), (ln2_gain, "H"),
            (block_query, "H"),
        ],
        1000,
        [
            pltpu.VMEM((4, BLK, 512), BF), pltpu.VMEM((BLK, D), F32), pltpu.VMEM((BLK, D), BF),
            pltpu.VMEM((4, BLK, 256), BF), pltpu.VMEM((D,), F32), pltpu.VMEM((4, BLK, 256), BF), pltpu.VMEM((BLK, D), BF), pltpu.VMEM((BLK, D), F32),
            pltpu.VMEM((BLK, D), BF), pltpu.VMEM((8, D), F32), DMA((5,)), DMA((8,)), DMA((4,)),
        ],
    )
    grad_send = after(pin(grad_send), *pieces[1:])
    grad_same = exchange(grad_send.reshape(32, BLK, 512), (*CHIP, *GROUP)).reshape(8, TOK, 512)
    lows = [flip(low, GROUP, 4, k) for k in (1, 2, 3)]
    kv_same = after(pin(kv_same), low)
    kv_other = swap(kv_same)
    grad_same = after(grad_same, *lows, kv_other, pin(ff_near))
    grad_other = swap(grad_same)
    ff_near = after(pin(ff_near), grad_other)
    ff_far = flip(ff_near, "xl", 2, 1)
    gqkv, w_own, keep, send = call(
        attend_back_kernel,
        [((TOK, 640), BF, "V"), ((3, D, 384), BF, "V")] + [((16, 48, 384), BF, "V")] * 2,
        [
            (scene_of_block, "S"), (kv_same, "H"), (kv_other, "V"), (grad_same, "V"), (grad_other, "V"),
            (normed, "H"), (mixed, "H"), (low, "H"), *[(value, "V") for value in lows], (w_qkv, "H"),
        ],
        1000,
        [
            pltpu.VMEM((5, TOK, 384), BF), pltpu.VMEM((D, 640), F32),
            pltpu.VMEM((TOK, 256), BF), pltpu.VMEM((TOK, D), BF), pltpu.VMEM((BLK, D), BF),
            DMA, DMA((3,)), DMA((3,)),
        ],
        vmem=24,
    )
    own, *sends, sums, ff_part = call(
        normed_grad_kernel,
        [((BLK, D), F32, "H")] + [((BLK, D), BF, "H")] * 3 + [((8, D), F32, "H"), ((2, 48, D), BF, "H")],
        [(gqkv, "V"), (w_own, "V"), (tokens, "H"), (vec2, "H"), (ff_near, "H"), (ff_far, "V")],
        1000,
        [
            pltpu.VMEM((TOK, D), BF), pltpu.VMEM((8, D), F32), pltpu.VMEM((2, 48, D), BF), pltpu.VMEM((TOK, D), F32),
            pltpu.VMEM((TOK, D), BF), pltpu.VMEM((8, D), F32), pltpu.VMEM((2, 48, D), BF), DMA((3,)), DMA((6,)),
        ],
    )
    (weight_send,) = call(
        add_kernel,
        [((16, 48, 384), BF, "H")],
        [(keep, "V"), (swap(after(send, ff_far)), "V"), (own, "H")],
        1000,
        [pltpu.VMEM((16, 48, 384), BF), DMA],
    )
    weight_parts = exchange(weight_send, (*CHIP, MICRO))
    parts = [flip(value, GROUP, 4, k + 1) for k, value in enumerate(sends)]
    weight_parts = after(weight_parts, pin(sums), *parts)
    ff_parts = [flip(ff_part, "y", 4, k) for k in (1, 2, 3)]
    (weight_total,) = call(
        sum_kernel,
        [((8, 8, 56, 384), BF, "H")],
        [(weight_parts, "V"), (sums, "H")],
        1000,
        [pltpu.VMEM((8, 56, 384), BF), pltpu.VMEM((8, D), F32), DMA((8,)), DMA],
    )
    (packed,) = call(
        input_kernel,
        [((8, 2 * BLK, D), BF, "H")],
        [
            (own, "L"), *[(value, "V") for value in parts], (tokens, "H"), (ln1_gain, "L"), (grad_mid, "L"),
            (result_part, "L"), (weight_total, "H"),
        ],
        1000,
        [pltpu.VMEM((2 * BLK, D), BF), pltpu.VMEM((BLK, D), BF), DMA((8,)), DMA],
    )
    weight_same = exchange(weight_total.reshape(64, 56, 384), (*CHIP, *NARROW)).reshape(8, 8, 56, 384)
    weight_same = after(weight_same, pin(packed))
    everyone = exchange(after(pin(packed), weight_same), NARROW)
    weight_other = swap(weight_same)
    scratch = [
        pltpu.VMEM((8, 48, 3 * D), F32), pltpu.VMEM((4, 2, 48, D), F32), DMA((8,)), DMA((4, 2)),
    ]
    grads = [((D, 3 * D), F32, "H"), ((D, D), F32, "H")]
    half = call(
        functools.partial(spread_kernel, False),
        grads + [((8, 384), F32, "V")],
        [(weight_same, "V")],
        1000,
        scratch,
    )
    qkv_grad, out_proj_grad, *vectors = call(
        functools.partial(spread_kernel, True),
        grads + [((D,), F32, "L")] * 4,
        [(weight_other, "V"), (half[2], "V"), (half[0], "H"), (half[1], "H")],
        1000,
        scratch,
        aliases={2: 0, 3: 1},
    )
    ff_parts = [after(value, pin(vectors[0])) for value in ff_parts]
    ff_swapped = [swap(value) for value in (ff_part, *ff_parts)]
    up_grad, down_grad = call(
        spread_ff_kernel,
        [((D, FFL), F32, "L"), ((FFL, D), F32, "L")],
        [(ff_part, "L"), *[(value, "V") for value in ff_parts], *[(value, "V") for value in ff_swapped]],
        1000,
    )
    input_grad, result = call(
        unpack_kernel, [((2, TOK, D), F32, "L"), ((2, TOK, D), BF, "L")], [(everyone, "V"), (vectors[0], "H"), (up_grad, "H")], 1000
    )
    return (
        result, input_grad, qkv_grad, out_proj_grad, *vectors, up_grad, down_grad
    )


def solution(mesh):
    names = ("y", "xl", "c", "zh", "zl", "xh")
    fine = Mesh(mesh.devices.reshape(4, 2, 2, 2, 2, 2), names)
    tokens = P(None, WIDE, None)
    placed = (
        tokens, P(), P(), P(), P(), P(), P(), P(), P(None, NARROW), P(NARROW, None), tokens
    )
    return jax.shard_map(
        shards,
        mesh=fine,
        in_specs=placed,
        out_specs=(
            tokens, tokens, P(), P(), P(), P(), P(), P(), P(None, NARROW), P(NARROW, None)
        ),
        check_vma=False,
    )
```

```python
import functools

import jax
import jax.numpy as jnp
from jax import lax
from jax.experimental import pallas as pl
from jax.experimental.pallas import tpu as pltpu
from jax.sharding import Mesh
from jax.sharding import PartitionSpec as P

D = 768
HD = 64
FFL = 384
TOK = 128
BLK = 32
EPS = 1e-05
BF = jnp.bfloat16
F32 = jnp.float32

CHIP = ("y", "xl")
CORE = "c"
MICRO = "zh"
GROUP = ("zl", "xh")
NARROW = (MICRO, *GROUP)
WIDE = (*CHIP, CORE)


def chip_index():
    return lax.axis_index("y") * 2 + lax.axis_index("xl")


def group_index():
    return lax.axis_index("zl") * 2 + lax.axis_index("xh")


def mm(left, right):
    return lax.dot_general(left, right, (((1,), (0,)), ((), ())), preferred_element_type=F32)


def mm_nt(left, right):
    return lax.dot_general(left, right, (((1,), (1,)), ((), ())), preferred_element_type=F32)


def mm_tn(left, right):
    return lax.dot_general(left, right, (((0,), (0,)), ((), ())), preferred_element_type=F32)


def normalized(values):
    center = values - jnp.mean(values, axis=-1, keepdims=True)
    spread = jnp.mean(center * center, axis=-1, keepdims=True)
    inverse = lax.rsqrt(spread + EPS)
    return center * inverse, inverse


def norm_back(grad, unit, inverse, gain):
    scaled = grad * gain
    first = jnp.mean(scaled, axis=-1, keepdims=True)
    second = jnp.mean(scaled * unit, axis=-1, keepdims=True)
    return inverse * (scaled - first - unit * second)


def halves(block):
    lane = lax.broadcasted_iota(jnp.int32, block.shape, 1)
    zero = jnp.zeros_like(block)
    return jnp.where(lane < HD, block, zero), jnp.where(lane < HD, zero, block)


def join(low, high):
    lane = lax.broadcasted_iota(jnp.int32, low.shape, 1)
    return jnp.where(lane < HD, low, high)


def span(scene_ref):
    micro = lax.axis_index(MICRO)
    own = scene_ref[micro, chip_index() * 4]
    first = jnp.int32(0)
    count = jnp.int32(0)
    for index in range(8):
        other = scene_ref[micro, index * 4]
        first += (other < own).astype(jnp.int32)
        count += (other == own).astype(jnp.int32)
    return first, count > 1


def three(value):
    a = value.astype(BF).astype(F32)
    b = (value - a).astype(BF).astype(F32)
    c = value - a - b
    return a, b, c


def put_columns(width, rows, start, columns):
    lane = lax.broadcasted_iota(jnp.int32, (rows, width), 1)
    out = jnp.zeros((rows, width), F32)
    for offset, column in enumerate(columns):
        out = jnp.where(lane == start + offset, column, out)
    return out


def pin(value):
    return pltpu.with_memory_space_constraint(value, pltpu.HBM)


def call(kernel, outs, ins, cost, scratch=(), vmem=16, aliases=None):
    places = {"V": pltpu.VMEM, "H": pltpu.HBM, "S": pltpu.SMEM, "L": pltpu.VMEM}
    return pl.pallas_call(
        kernel,
        out_shape=[
            (pltpu.HBM if place in "HL" else jax.ShapeDtypeStruct)(shape, dtype) for shape, dtype, place in outs
        ],
        in_specs=[pl.BlockSpec(memory_space=places[place]) for _, place in ins],
        out_specs=[pl.BlockSpec(memory_space=places[place]) for _, _, place in outs],
        scratch_shapes=list(scratch),
        input_output_aliases=aliases or {},
        cost_estimate=pl.CostEstimate(flops=cost, bytes_accessed=1000, transcendentals=0),
        compiler_params=pltpu.CompilerParams(vmem_limit_bytes=vmem * 2**20),
    )(*[pin(value) if place in "HL" else value for value, place in ins])


DMA = pltpu.SemaphoreType.DMA


def send_copies(source, target, indices, sem):
    copies = [pltpu.make_async_copy(source, target.at[index], sem.at[index]) for index in indices]
    for copy in copies:
        copy.start()
    return copies


def wait_all(copies):
    for copy in copies:
        copy.wait()


def weight_copies(w_ref, w_buf, w_sem, parts=(1, 2, 0), start=True):
    group = group_index()
    copies = []
    for slot, part in enumerate(parts):
        column = pl.multiple_of(part * D + (group // 2) * 384, 128)
        copy = pltpu.make_async_copy(w_ref.at[:, pl.ds(column, 384)], w_buf.at[slot], w_sem.at[slot])
        if start:
            copy.start()
        copies.append(copy)
    return copies


def own_heads(full):
    odd = (group_index() % 2) == 1
    return jnp.where(odd, full[:, 192:], full[:, :192]).astype(BF)


def project_kernel(
    tok_ref, gain_ref, shift_ref, w_ref, kv_ref, normed_ref,
    x_buf, w_buf, kv_buf, gain_buf, shift_buf, x_sem, w_sem, kv_sem, gain_sem, shift_sem,
):
    copy_x = pltpu.make_async_copy(tok_ref.at[lax.axis_index(MICRO)], x_buf, x_sem)
    copy_x.start()
    copy_gain = pltpu.make_async_copy(gain_ref, gain_buf, gain_sem)
    copy_gain.start()
    copy_shift = pltpu.make_async_copy(shift_ref, shift_buf, shift_sem)
    copy_shift.start()
    copies = weight_copies(w_ref, w_buf, w_sem, (1, 2))
    wait_all([copy_x, copy_gain, copy_shift])
    unit, _ = normalized(x_buf[...].astype(F32))
    normed = (unit * gain_buf[...].reshape(1, D) + shift_buf[...].reshape(1, D)).astype(BF)
    normed_ref[...] = normed
    parts = []
    for slot in range(2):
        copies[slot].wait()
        parts.append(own_heads(mm(normed, w_buf[slot])))
    kv_buf[...] = jnp.concatenate(parts, axis=1)
    wait_all(send_copies(kv_buf, kv_ref, range(8), kv_sem))


def query_kernel(normed_ref, w_ref, q_ref, w_buf, w_sem):
    weight_copies(w_ref, w_buf, w_sem, (0,))[0].wait()
    part = own_heads(mm(normed_ref[...], w_buf[0]))
    q_ref[...] = jnp.concatenate([part, jnp.zeros((TOK, HD), BF)], axis=1)


def block_query_kernel(normed_ref, w_ref, out_ref, x_buf, w_buf, x_sem, w_sem):
    block = pl.ds(pl.multiple_of(group_index() * BLK, BLK), BLK)
    loads = [
        pltpu.make_async_copy(normed_ref.at[block], x_buf, x_sem),
        pltpu.make_async_copy(w_ref.at[:, pl.ds(0, D)], w_buf, w_sem),
    ]
    for load in loads:
        load.start()
    wait_all(loads)
    query = mm(x_buf[...], w_buf[...]).astype(BF)
    zero = jnp.zeros((BLK, HD), BF)
    for group in range(4):
        out_ref[group] = jnp.concatenate([query[:, group * 192:(group + 1) * 192], zero], axis=1)


def attend_kernel(scene_ref, q_ref, same_ref, other_ref, out_ref, buf, q_buf, sem, q_sem):
    load = pltpu.make_async_copy(q_ref, q_buf, q_sem)
    load.start()
    first, big = span(scene_ref)

    def run(count):
        rows = count * TOK
        keys = jnp.concatenate(
            [ref[pl.ds(first, count)].reshape(rows, 384) for ref in (same_ref, other_ref)], axis=0
        )
        load.wait()
        query = q_buf[...]
        q0, q1 = halves(query[:, :128])
        blocks = [keys[:, :128], keys[:, 128:256], keys[:, 256:]]
        mixed = []
        columns = []
        for qh, kb, vb in ((q0, 0, 1), (q1, 0, 2), (query[:, 128:], 1, 2)):
            scores = mm_nt(qh, blocks[kb]) * (HD**-0.5)
            top = jnp.max(scores, axis=-1, keepdims=True)
            weights = jnp.exp(scores - top)
            total = jnp.sum(weights, axis=-1, keepdims=True)
            probs = (weights * (1.0 / total)).astype(BF)
            mixed.append(mm(probs, blocks[vb]))
            columns += three(top + jnp.log(total))
        stats = put_columns(128, TOK, 0, columns)
        buf[...] = jnp.concatenate([join(stats, mixed[0]), join(mixed[1], mixed[2])], axis=1).astype(BF)

    @pl.when(big)
    def _():
        run(5)

    @pl.when(jnp.logical_not(big))
    def _():
        run(1)

    wait_all(send_copies(buf, out_ref, range(8), sem))


def forward_kernel(
    mixed_ref, tok_ref, og_ref, wo_ref, gain_ref, shift_ref, up_ref, down_ref,
    out_ref, middle_ref, normed_ref, act_ref, gpre_ref,
    tok_buf, og_buf, up_buf, down_buf, gain_buf, shift_buf, grad_buf, branch_buf, middle_buf, in_sem, sem,
):
    loads = [
        pltpu.make_async_copy(ref, buf, in_sem.at[index])
        for index, (ref, buf) in enumerate(
            (
                (tok_ref, tok_buf), (up_ref, up_buf), (og_ref, og_buf), (down_ref, down_buf), (gain_ref, gain_buf),
                (shift_ref, shift_buf),
            )
        )
    ]
    for load in loads:
        load.start()
    total = jnp.zeros((2 * TOK, D), F32)
    for group in range(4):
        rows = jnp.concatenate([mixed_ref[group], mixed_ref[4 + group]], axis=0)
        total = total + mm(rows, wo_ref[group])
    loads[0].wait()
    total = total + tok_buf[...].reshape(2 * TOK, D).astype(F32)
    middle_buf[...] = total.reshape(8, BLK, D)
    third = pltpu.make_async_copy(
        middle_buf.at[lax.axis_index(MICRO) * 4 + group_index()], middle_ref, sem.at[2]
    )
    third.start()
    unit, _ = normalized(total)
    wait_all(loads[4:])
    normed = (unit * gain_buf[...].reshape(1, D) + shift_buf[...].reshape(1, D)).astype(BF)
    normed_ref[...] = normed
    loads[1].wait()
    pre = mm(normed, up_buf[...])
    cdf = 0.5 * (1.0 + lax.erf(pre * (0.5**0.5)))
    slope = cdf + pre * jnp.exp(-0.5 * pre * pre) * 0.3989422804014327
    loads[2].wait()
    loads[3].wait()
    grad_out = og_buf[...].reshape(2 * TOK, D)
    gpre = (mm_nt(grad_out, down_buf[...]) * slope).astype(BF)
    gpre_ref[...] = gpre
    grad_buf[...] = mm_nt(gpre, up_buf[...]).astype(BF).reshape(8, BLK, D)
    first = pltpu.make_async_copy(grad_buf, out_ref.at[:, pl.ds(BLK, BLK)], sem.at[0])
    first.start()
    act = (pre * cdf).astype(BF)
    act_ref[...] = act
    branch_buf[...] = mm(act, down_buf[...]).astype(BF).reshape(8, BLK, D)
    second = pltpu.make_async_copy(branch_buf, out_ref.at[:, pl.ds(0, BLK)], sem.at[1])
    second.start()
    wait_all([first, second, third])


def ff_grads_kernel(normed_ref, act_ref, gpre_ref, og_ref, keep_ref, send_ref, up_buf, down_buf):
    core = lax.axis_index(CORE)
    up_buf[...] = mm_tn(normed_ref[...], gpre_ref[...])
    down_buf[...] = mm_tn(act_ref[...], og_ref[...].reshape(2 * TOK, D))
    for ref, owner in ((keep_ref, core), (send_ref, 1 - core)):
        column = pl.multiple_of(owner * 384, 128)
        for tile in range(8):
            rows = pl.ds(pl.multiple_of((2 * tile + owner) * 48, 16), 48)
            ref[tile, :, :384] = up_buf[rows].astype(BF)
            ref[tile, :, 384:] = down_buf[tile * 48:(tile + 1) * 48, pl.ds(column, 384)].astype(BF)


def split_kernel(one_ref, two_ref, *refs):
    y = lax.axis_index("y")
    for k, ref in enumerate(refs):
        for xl in range(2):
            at = (y ^ k) * 2 + xl
            ref[xl] = (one_ref[at].astype(F32) + two_ref[at].astype(F32)).astype(BF)


def total_kernel(*refs):
    total = refs[0][...].astype(F32)
    for ref in refs[1:4]:
        total = total + ref[...].astype(F32)
    refs[4][...] = total.astype(BF)


def middle_kernel(
    sums_ref, middle_ref, og_ref, mixed_ref, wo_ref, gain_ref, query_ref,
    out_ref, low_ref, grad_ref, result_ref, vec_ref,
    buf, middle_buf, og_buf, mixed_buf, gain_buf, query_buf, low_buf, grad_buf, result_buf, vec_buf, in_sem, sem, rest_sem,
):
    micro = lax.axis_index(MICRO)
    group = group_index()
    block = pl.ds(pl.multiple_of(group * BLK, BLK), BLK)
    loads = [
        pltpu.make_async_copy(middle_ref, middle_buf, in_sem.at[0]),
        pltpu.make_async_copy(og_ref.at[micro, block], og_buf, in_sem.at[1]),
        pltpu.make_async_copy(mixed_ref.at[pl.ds(micro * 4, 4), block], mixed_buf, in_sem.at[2]),
        pltpu.make_async_copy(gain_ref, gain_buf, in_sem.at[3]),
        pltpu.make_async_copy(query_ref, query_buf, in_sem.at[4]),
    ]
    for load in loads:
        load.start()
    total = sums_ref[0].astype(F32)
    for index in range(1, 8):
        total = total + sums_ref[index].astype(F32)
    branch, grad = total[:BLK], total[BLK:]
    wait_all(loads)
    middle = middle_buf[...]
    unit, inverse = normalized(middle)
    grad_mid = og_buf[...].astype(F32) + norm_back(grad, unit, inverse, gain_buf[...].reshape(1, D))
    low = grad_mid.astype(BF)
    low_buf[...] = low
    grad_buf[...] = grad_mid
    result_buf[...] = (middle + branch).astype(BF)
    gain_grad = jnp.sum(grad * unit, axis=0, keepdims=True)
    shift_grad = jnp.sum(grad, axis=0, keepdims=True)
    vec_buf[...] = jnp.concatenate([gain_grad, shift_grad, jnp.zeros((6, D), F32)], axis=0)
    stores = [
        pltpu.make_async_copy(source, target, rest_sem.at[index])
        for index, (source, target) in enumerate(
            ((low_buf, low_ref), (grad_buf, grad_ref), (result_buf, result_ref), (vec_buf, vec_ref))
        )
    ]
    for store in stores:
        store.start()
    lane = lax.broadcasted_iota(jnp.int32, (BLK, 256), 1)
    for head_group in range(4):
        mixed = mixed_buf[head_group].astype(F32)
        back = mm_nt(low, wo_ref[head_group]).astype(BF).astype(F32)
        product = mixed * back
        columns = []
        for head in range(3):
            inside = (lane >= (head + 1) * HD) & (lane < (head + 2) * HD)
            columns += three(jnp.sum(jnp.where(inside, product, 0.0), axis=-1, keepdims=True))
        stats = put_columns(256, BLK, 9, columns)
        buf[head_group, :, :256] = jnp.where(lane < 9, mixed, jnp.where(lane < HD, stats, back)).astype(BF)
        buf[head_group, :, 256:] = query_buf[head_group]
    sends = send_copies(buf, out_ref, range(8), sem)
    wait_all(stores)
    wait_all(sends)


def attend_back_kernel(
    scene_ref, kvs_ref, kvo_ref, gs_ref, go_ref, normed_ref, mixed_ref, low_ref, low1_ref, low2_ref, low3_ref,
    w_ref, gqkv_ref, w_out_ref, keep_ref, send_ref,
    kv_buf, grad_buf, mixed_buf, normed_buf, low_buf, kv_sem, in_sem, w_sem,
):
    first, big = span(scene_ref)
    chip = chip_index()
    core = lax.axis_index(CORE)
    group = group_index()
    index = lax.axis_index(MICRO) * 4 + group
    first_loads = [
        pltpu.make_async_copy(source, target, in_sem.at[slot])
        for slot, (source, target) in enumerate(
            ((normed_ref, normed_buf), (mixed_ref.at[index], mixed_buf), (low_ref, low_buf))
        )
    ]
    scale = HD**-0.5

    def run(count):
        rows = count * TOK
        loads = [pltpu.make_async_copy(kvs_ref.at[pl.ds(first, count)], kv_buf.at[pl.ds(0, count)], kv_sem)]
        for load in loads + first_loads:
            load.start()
        weight_copies(w_ref, w_out_ref, w_sem)

        def cut(value):
            return [value[:, at:at + 128] for at in range(0, value.shape[1], 128)]

        every = cut(jnp.concatenate(
            [ref[pl.ds(first, count)].reshape(rows, 512) for ref in (gs_ref, go_ref)], axis=0
        ))
        grad, query = every[:2], every[2:]
        g_own = cut(gs_ref[chip])
        g_heads = [halves(g_own[0])[1], *halves(g_own[1])]
        own_stats = g_own[0].astype(F32)
        all_stats = grad[0].astype(F32).T
        wait_all(loads)
        kv = cut(jnp.concatenate(
            [kv_buf[:count].reshape(rows, 384), kvo_ref[pl.ds(first, count)].reshape(rows, 384)], axis=0
        ))
        own = cut(kv_buf[chip - first]) + g_own[2:]
        q_heads = [*halves(own[3]), own[4]]
        k_heads = [*halves(own[0]), halves(own[1])[0]]
        v_heads = [halves(own[1])[1], *halves(own[2])]

        def column(at):
            return own_stats[:, at:at + 1] + own_stats[:, at + 1:at + 2] + own_stats[:, at + 2:at + 3]

        def row(at):
            return all_stats[at:at + 1] + all_stats[at + 1:at + 2] + all_stats[at + 2:at + 3]

        dq, dk, dv = [], [], []
        for head, (kb, vb) in enumerate(((0, 1), (0, 2), (1, 2))):
            qb, gb = (0, 0, 1)[head], (0, 1, 1)[head]
            probs = jnp.exp(mm_nt(q_heads[head], kv[kb]) * scale - column(3 * head))
            gap = mm_nt(g_heads[head], kv[vb]) - column(9 + 3 * head)
            dq.append(mm((probs * gap).astype(BF), kv[kb]) * scale)
            probs = jnp.exp(mm_nt(k_heads[head], query[qb]) * scale - row(3 * head))
            gap = mm_nt(v_heads[head], grad[gb]) - row(9 + 3 * head)
            dv.append(mm(probs.astype(BF), grad[gb]))
            dk.append(mm((probs * gap).astype(BF), query[qb]) * scale)
        tail = dq[2]
        gqkv_ref[...] = jnp.concatenate(
            [join(dk[0], dk[1]), join(dk[2], dv[0]), join(dv[1], dv[2]), join(dq[0], dq[1]),
             join(tail, jnp.zeros_like(tail))],
            axis=1,
        ).astype(BF)


    @pl.when(big)
    def _():
        run(5)

    @pl.when(jnp.logical_not(big))
    def _():
        run(1)

    wait_all(first_loads)

    grad_buf[...] = mm_tn(normed_buf[...], gqkv_ref[...])
    low = jnp.concatenate([ref[...] for ref in (low_buf, low1_ref, low2_ref, low3_ref)], axis=0)
    mixed = jnp.concatenate(
        [mixed_buf[pl.ds(pl.multiple_of((group ^ k) * BLK, BLK), BLK)] for k in range(4)], axis=0
    )
    out = mm_tn(mixed, low)[HD:]
    for ref, owner in ((keep_ref, core), (send_ref, 1 - core)):
        for tile in range(8):
            rows = grad_buf[pl.ds(pl.multiple_of((2 * tile + owner) * 48, 16), 48)]
            at = (tile // 4) * 96
            pieces = [
                out[at + row * 48:at + (row + 1) * 48, (tile % 4) * 192:(tile % 4 + 1) * 192] for row in range(2)
            ]
            ref[2 * tile] = rows[:, :384].astype(BF)
            ref[2 * tile + 1] = jnp.concatenate(
                [rows[:, 384:576], jnp.where(owner == 1, pieces[1], pieces[0])], axis=1
            ).astype(BF)
    wait_all(weight_copies(w_ref, w_out_ref, w_sem, start=False))


def normed_grad_kernel(
    gqkv_ref, w_ref, tok_ref, vec_ref, near_ref, far_ref, own_ref, one_ref, two_ref, three_ref, sums_ref, ff_ref,
    x_buf, vec_buf, near_buf, part_buf, low_buf, sums_buf, ff_buf, in_sem, out_sem,
):
    loads = [
        pltpu.make_async_copy(tok_ref.at[lax.axis_index(MICRO)], x_buf, in_sem.at[0]),
        pltpu.make_async_copy(vec_ref, vec_buf, in_sem.at[1]),
        pltpu.make_async_copy(near_ref, near_buf, in_sem.at[2]),
    ]
    for load in loads:
        load.start()
    group = group_index()
    odd = (group % 2) == 1
    total = jnp.zeros((TOK, D), F32)
    for slot in range(3):
        part = gqkv_ref[:, slot * 192:(slot + 1) * 192]
        zero = jnp.zeros_like(part)
        wide = jnp.where(
            odd, jnp.concatenate([zero, part], axis=1), jnp.concatenate([part, zero], axis=1)
        )
        total = total + mm_nt(wide, w_ref[slot])
    part_buf[...] = total
    low_buf[...] = total.astype(BF)
    stores = []
    for k, ref in enumerate((own_ref, one_ref, two_ref, three_ref)):
        rows = pl.ds(pl.multiple_of((group ^ k) * BLK, BLK), BLK)
        stores.append(pltpu.make_async_copy((low_buf if k else part_buf).at[rows], ref, out_sem.at[k]))
        stores[-1].start()
    wait_all(loads)
    ff_buf[...] = (near_buf[...].astype(F32) + far_ref[...].astype(F32)).astype(BF)
    stores.append(pltpu.make_async_copy(ff_buf, ff_ref, out_sem.at[5]))
    stores[-1].start()
    unit, _ = normalized(x_buf[...].astype(F32))
    gain1 = jnp.sum(total * unit, axis=0, keepdims=True)
    shift1 = jnp.sum(total, axis=0, keepdims=True)
    sums_buf[...] = jnp.concatenate([gain1, shift1, vec_buf[...][:2], jnp.zeros((4, D), F32)], axis=0)
    stores.append(pltpu.make_async_copy(sums_buf, sums_ref, out_sem.at[4]))
    stores[-1].start()
    wait_all(stores)


def add_kernel(one_ref, two_ref, unused_ref, out_ref, buf, sem):
    buf[...] = (one_ref[...].astype(F32) + two_ref[...].astype(F32)).astype(BF)
    copy = pltpu.make_async_copy(buf, out_ref, sem)
    copy.start()
    copy.wait()


def sum_kernel(in_ref, vec_ref, out_ref, buf, vec_buf, sem, vec_sem):
    load = pltpu.make_async_copy(vec_ref, vec_buf, vec_sem)
    load.start()
    total = in_ref[0].astype(F32)
    for index in range(1, 16):
        total = total + in_ref[index].astype(F32)
    load.wait()
    vectors = vec_buf[...][:4]
    block = jnp.concatenate([total, vectors[:, :384], vectors[:, 384:]], axis=0).astype(BF)
    for index in range(8):
        buf[index] = block
    wait_all(send_copies(buf, out_ref, range(8), sem))


def spread_kernel(turn, in_ref, *refs):
    qkv_buf, out_buf, sem, out_sem = refs[-4:]
    if turn:
        in_buf, in_sem = refs[-6:-4]
        qkv_ref, out_ref, *vec_refs = refs[3:-6]
        loads = [pltpu.make_async_copy(in_ref.at[tile], in_buf.at[tile], in_sem.at[tile]) for tile in range(8)]
        for load in loads:
            load.start()
    else:
        qkv_ref, out_ref, *vec_refs = refs[:-4]
        in_buf = in_ref
    owner = lax.axis_index(CORE)
    owner = 1 - owner if turn else owner
    copies = []
    vectors = jnp.zeros((8, 384), F32)
    for tile in range(8):
        if turn:
            loads[tile].wait()
        whole = [in_buf[tile, index].astype(F32) for index in range(8)]
        block = [value[:48] for value in whole]
        for value in whole:
            vectors = vectors + value[48:]
        for part, half, at in ((1, 0, 0), (2, 0, 192), (0, 4, 0)):
            qkv_buf[tile, :, part * D:(part + 1) * D] = jnp.concatenate(
                [block[half + group][:, at:at + 192] for group in range(4)], axis=1
            )
        start = pl.multiple_of((2 * tile + owner) * 48, 16)
        copy = pltpu.make_async_copy(qkv_buf.at[tile], qkv_ref.at[pl.ds(start, 48)], sem.at[tile])
        copy.start()
        copies.append(copy)
        for group in range(4):
            out_buf[group, tile // 4, :, (tile % 4) * 192:(tile % 4 + 1) * 192] = block[4 + group][:, 192:]
    for group in range(4):
        for pair in range(2):
            start = pl.multiple_of(group * 192 + (pair * 2 + owner) * 48, 16)
            copy = pltpu.make_async_copy(
                out_buf.at[group, pair], out_ref.at[pl.ds(start, 48)], out_sem.at[group, pair]
            )
            copy.start()
            copies.append(copy)
    if turn:
        vectors = vectors + refs[0][...]
        for k, ref in enumerate(vec_refs):
            ref[...] = jnp.concatenate([vectors[k:k + 1], vectors[4 + k:5 + k]], axis=1).reshape(D)
    else:
        vec_refs[0][...] = vectors
    wait_all(copies)


def spread_ff_kernel(*refs):
    up_ref, down_ref, up_buf, down_buf, up_sem, down_sem = refs[8:]
    y, core = lax.axis_index("y"), lax.axis_index(CORE)
    copies = []
    for near in range(4):
        for xl in range(2):
            chip = (y ^ near) * 2 + xl
            for index in (near, near + 4):
                owner = core ^ (index // 4)
                block = refs[index][xl].astype(F32)
                up_buf[near, xl, pl.ds(pl.multiple_of(owner * 48, 16), 48)] = block[:, :384]
                down_buf[near, xl, :, pl.ds(pl.multiple_of(owner * 384, 128), 384)] = block[:, 384:]
            for source, target, rows, sem in ((up_buf, up_ref, 96, up_sem), (down_buf, down_ref, 48, down_sem)):
                copy = pltpu.make_async_copy(
                    source.at[near, xl],
                    target.at[pl.ds(pl.multiple_of(chip * rows, 16), rows)],
                    sem.at[near, xl],
                )
                copy.start()
                copies.append(copy)
    wait_all(copies)


def input_kernel(
    own_ref, one_ref, two_ref, three_ref, tok_ref, gain_ref, grad_ref, result_ref, unused_ref, out_ref, buf, x_buf, sem, x_sem
):
    start = pl.multiple_of(group_index() * BLK, BLK)
    load = pltpu.make_async_copy(tok_ref.at[lax.axis_index(MICRO), pl.ds(start, BLK)], x_buf, x_sem)
    load.start()
    load.wait()
    total = own_ref[...]
    for ref in (one_ref, two_ref, three_ref):
        total = total + ref[...].astype(F32)
    unit, inverse = normalized(x_buf[...].astype(F32))
    grad = grad_ref[...] + norm_back(total, unit, inverse, gain_ref[...].reshape(1, D))
    buf[:BLK] = grad.astype(BF)
    buf[BLK:] = result_ref[...]
    wait_all(send_copies(buf, out_ref, range(8), sem))


def unpack_kernel(in_ref, unused_ref, other_ref, grad_ref, result_ref):
    for index in range(8):
        rows = slice(index % 4 * BLK, (index % 4 + 1) * BLK)
        grad_ref[index // 4, rows] = in_ref[index, :BLK].astype(F32)
        result_ref[index // 4, rows] = in_ref[index, BLK:]


def exchange(value, axes):
    return lax.all_to_all(value, axes, 0, 0, tiled=True)


def swap(value):
    return lax.ppermute(value, CORE, [(0, 1), (1, 0)])


def after(value, *others):
    return pl.pallas_call(
        lambda *refs: None,
        out_shape=jax.ShapeDtypeStruct(value.shape, value.dtype),
        in_specs=[pl.BlockSpec(memory_space=pl.ANY)] * (1 + len(others)),
        out_specs=pl.BlockSpec(memory_space=pl.ANY),
        input_output_aliases={0: 0},
        cost_estimate=pl.CostEstimate(flops=1, bytes_accessed=1, transcendentals=0),
        compiler_params=pltpu.CompilerParams(vmem_limit_bytes=2**20),
    )(value, *others)


def flip(value, axes, count, bits):
    return lax.ppermute(value, axes, [(index, index ^ bits) for index in range(count)])


def shards(
    tokens, scene_of_block, ln1_gain, ln1_shift, w_qkv, w_out, ln2_gain, ln2_shift, w_up, w_down, out_grad
):
    w_out_pad = jnp.pad(w_out.reshape(4, 192, D), ((0, 0), (HD, 0), (0, 0)))
    kv_send, normed = call(
        project_kernel,
        [((8, TOK, 384), BF, "H"), ((TOK, D), BF, "L")],
        [(tokens, "H"), (ln1_gain, "H"), (ln1_shift, "H"), (w_qkv, "H")],
        1000,
        [
            pltpu.VMEM((TOK, D), BF), pltpu.VMEM((2, D, 384), BF), pltpu.VMEM((TOK, 384), BF),
            pltpu.VMEM((D,), F32), pltpu.VMEM((D,), F32), DMA, DMA((2,)), DMA((8,)), DMA, DMA,
        ],
    )
    (query,) = call(
        query_kernel,
        [((TOK, 256), BF, "L")],
        [(normed, "L"), (w_qkv, "H")],
        1000,
        [pltpu.VMEM((1, D, 384), BF), DMA((1,))],
    )
    kv_same = exchange(kv_send, CHIP)
    kv_same = after(kv_same, pin(query))
    kv_other = swap(kv_same)
    (mixed_send,) = call(
        attend_kernel,
        [((8, TOK, 256), BF, "H")],
        [(scene_of_block, "S"), (query, "H"), (kv_same, "V"), (kv_other, "V")],
        1000,
        [pltpu.VMEM((TOK, 256), BF), pltpu.VMEM((TOK, 256), BF), DMA((8,)), DMA],
    )
    mixed = exchange(mixed_send, NARROW)
    (block_query,) = call(
        block_query_kernel,
        [((4, BLK, 256), BF, "L")],
        [(normed, "H"), (w_qkv, "H")],
        1000,
        [pltpu.VMEM((BLK, D), BF), pltpu.VMEM((D, D), BF), DMA, DMA],
    )
    ff_send, middle, normed2, act, grad_pre = call(
        forward_kernel,
        [
            ((8, 2 * BLK, D), BF, "H"), ((BLK, D), F32, "H"), ((2 * TOK, D), BF, "V"),
            ((2 * TOK, FFL), BF, "V"), ((2 * TOK, FFL), BF, "V"),
        ],
        [
            (mixed, "V"), (tokens, "H"), (out_grad, "H"), (w_out_pad, "V"), (ln2_gain, "H"), (ln2_shift, "H"),
            (w_up, "H"), (w_down, "H"),
        ],
        1000,
        [
            pltpu.VMEM((2, TOK, D), BF), pltpu.VMEM((2, TOK, D), BF), pltpu.VMEM((D, FFL), BF),
            pltpu.VMEM((FFL, D), BF), pltpu.VMEM((D,), F32), pltpu.VMEM((D,), F32), pltpu.VMEM((8, BLK, D), BF),
            pltpu.VMEM((8, BLK, D), BF), pltpu.VMEM((8, BLK, D), F32), DMA((6,)), DMA((3,)),
        ],
    )
    ff_sums = exchange(ff_send, NARROW)
    keep, send = call(
        ff_grads_kernel,
        [((8, 48, D), BF, "V")] * 2,
        [(normed2, "V"), (act, "V"), (grad_pre, "V"), (out_grad, "L")],
        1000,
        [pltpu.VMEM((D, FFL), F32), pltpu.VMEM((FFL, D), F32)],
    )
    pieces = call(
        split_kernel, [((2, 48, D), BF, "L")] * 4, [(keep, "V"), (swap(send), "V")], 1000
    )
    pieces = [pieces[0]] + [flip(pieces[k], "y", 4, k) for k in (1, 2, 3)]
    (ff_near,) = call(
        total_kernel,
        [((2, 48, D), BF, "L")],
        [(pieces[0], "L")] + [(piece, "V") for piece in pieces[1:]],
        1000,
    )
    grad_send, low, grad_mid, result_part, vec2 = call(
        middle_kernel,
        [
            ((8, 4, BLK, 512), BF, "H"), ((BLK, D), BF, "H"), ((BLK, D), F32, "H"), ((BLK, D), BF, "H"),
            ((8, D), F32, "H"),
        ],
        [
            (ff_sums, "V"), (middle, "H"), (out_grad, "H"), (mixed, "H"), (w_out_pad, "V"), (ln2_gain, "H"),
            (block_query, "H"),
        ],
        1000,
        [
            pltpu.VMEM((4, BLK, 512), BF), pltpu.VMEM((BLK, D), F32), pltpu.VMEM((BLK, D), BF),
            pltpu.VMEM((4, BLK, 256), BF), pltpu.VMEM((D,), F32), pltpu.VMEM((4, BLK, 256), BF), pltpu.VMEM((BLK, D), BF), pltpu.VMEM((BLK, D), F32),
            pltpu.VMEM((BLK, D), BF), pltpu.VMEM((8, D), F32), DMA((5,)), DMA((8,)), DMA((4,)),
        ],
    )
    grad_send = after(pin(grad_send), *pieces[1:])
    grad_same = exchange(grad_send.reshape(32, BLK, 512), (*CHIP, *GROUP)).reshape(8, TOK, 512)
    lows = [flip(low, GROUP, 4, k) for k in (1, 2, 3)]
    kv_same = after(pin(kv_same), low)
    kv_other = swap(kv_same)
    grad_same = after(grad_same, *lows, kv_other, pin(ff_near))
    grad_other = swap(grad_same)
    ff_near = after(pin(ff_near), grad_other)
    ff_far = flip(ff_near, "xl", 2, 1)
    gqkv, w_own, keep, send = call(
        attend_back_kernel,
        [((TOK, 640), BF, "V"), ((3, D, 384), BF, "V")] + [((16, 48, 384), BF, "V")] * 2,
        [
            (scene_of_block, "S"), (kv_same, "H"), (kv_other, "V"), (grad_same, "V"), (grad_other, "V"),
            (normed, "H"), (mixed, "H"), (low, "H"), *[(value, "V") for value in lows], (w_qkv, "H"),
        ],
        1000,
        [
            pltpu.VMEM((5, TOK, 384), BF), pltpu.VMEM((D, 640), F32),
            pltpu.VMEM((TOK, 256), BF), pltpu.VMEM((TOK, D), BF), pltpu.VMEM((BLK, D), BF),
            DMA, DMA((3,)), DMA((3,)),
        ],
        vmem=24,
    )
    own, *sends, sums, ff_part = call(
        normed_grad_kernel,
        [((BLK, D), F32, "H")] + [((BLK, D), BF, "H")] * 3 + [((8, D), F32, "H"), ((2, 48, D), BF, "H")],
        [(gqkv, "V"), (w_own, "V"), (tokens, "H"), (vec2, "H"), (ff_near, "H"), (ff_far, "V")],
        1000,
        [
            pltpu.VMEM((TOK, D), BF), pltpu.VMEM((8, D), F32), pltpu.VMEM((2, 48, D), BF), pltpu.VMEM((TOK, D), F32),
            pltpu.VMEM((TOK, D), BF), pltpu.VMEM((8, D), F32), pltpu.VMEM((2, 48, D), BF), DMA((3,)), DMA((6,)),
        ],
    )
    (weight_send,) = call(
        add_kernel,
        [((16, 48, 384), BF, "H")],
        [(keep, "V"), (swap(after(send, ff_far)), "V"), (own, "H")],
        1000,
        [pltpu.VMEM((16, 48, 384), BF), DMA],
    )
    weight_parts = exchange(weight_send, (*CHIP, MICRO))
    parts = [flip(value, GROUP, 4, k + 1) for k, value in enumerate(sends)]
    weight_parts = after(weight_parts, pin(sums), *parts)
    ff_parts = [flip(ff_part, "y", 4, k) for k in (1, 2, 3)]
    (weight_total,) = call(
        sum_kernel,
        [((8, 8, 56, 384), BF, "H")],
        [(weight_parts, "V"), (sums, "H")],
        1000,
        [pltpu.VMEM((8, 56, 384), BF), pltpu.VMEM((8, D), F32), DMA((8,)), DMA],
    )
    (packed,) = call(
        input_kernel,
        [((8, 2 * BLK, D), BF, "H")],
        [
            (own, "L"), *[(value, "V") for value in parts], (tokens, "H"), (ln1_gain, "L"), (grad_mid, "L"),
            (result_part, "L"), (weight_total, "H"),
        ],
        1000,
        [pltpu.VMEM((2 * BLK, D), BF), pltpu.VMEM((BLK, D), BF), DMA((8,)), DMA],
    )
    weight_same = exchange(weight_total.reshape(64, 56, 384), (*CHIP, *NARROW)).reshape(8, 8, 56, 384)
    weight_same = after(weight_same, pin(packed))
    everyone = exchange(after(pin(packed), weight_same), NARROW)
    weight_other = swap(weight_same)
    scratch = [
        pltpu.VMEM((8, 48, 3 * D), F32), pltpu.VMEM((4, 2, 48, D), F32), DMA((8,)), DMA((4, 2)),
    ]
    grads = [((D, 3 * D), F32, "H"), ((D, D), F32, "H")]
    half = call(
        functools.partial(spread_kernel, False),
        grads + [((8, 384), F32, "V")],
        [(weight_same, "V")],
        1000,
        scratch,
    )
    qkv_grad, out_proj_grad, *vectors = call(
        functools.partial(spread_kernel, True),
        grads + [((D,), F32, "L")] * 4,
        [(weight_other, "H"), (half[2], "V"), (half[0], "H"), (half[1], "H")],
        1000,
        [pltpu.VMEM((8, 8, 56, 384), BF), DMA((8,))] + scratch,
        aliases={2: 0, 3: 1},
    )
    ff_parts = [after(value, pin(vectors[0])) for value in ff_parts]
    ff_swapped = [swap(value) for value in (ff_part, *ff_parts)]
    up_grad, down_grad = call(
        spread_ff_kernel,
        [((D, FFL), F32, "H"), ((FFL, D), F32, "H")],
        [(ff_part, "L"), *[(value, "V") for value in ff_parts], *[(value, "V") for value in ff_swapped]],
        1000,
        [pltpu.VMEM((4, 2, 96, FFL), F32), pltpu.VMEM((4, 2, 48, D), F32), DMA((4, 2)), DMA((4, 2))],
    )
    input_grad, result = call(
        unpack_kernel, [((2, TOK, D), F32, "L"), ((2, TOK, D), BF, "L")], [(everyone, "V"), (vectors[0], "H"), (up_grad, "H")], 1000
    )
    return (
        result, input_grad, qkv_grad, out_proj_grad, *vectors, up_grad, down_grad
    )


def solution(mesh):
    names = ("y", "xl", "c", "zh", "zl", "xh")
    fine = Mesh(mesh.devices.reshape(4, 2, 2, 2, 2, 2), names)
    tokens = P(None, WIDE, None)
    placed = (
        tokens, P(), P(), P(), P(), P(), P(), P(), P(None, NARROW), P(NARROW, None), tokens
    )
    return jax.shard_map(
        shards,
        mesh=fine,
        in_specs=placed,
        out_specs=(
            tokens, tokens, P(), P(), P(), P(), P(), P(), P(None, NARROW), P(NARROW, None)
        ),
        check_vma=False,
    )
```

```python
import functools

import jax
import jax.numpy as jnp
from jax import lax
from jax.experimental import pallas as pl
from jax.experimental.pallas import tpu as pltpu
from jax.sharding import Mesh
from jax.sharding import PartitionSpec as P

D = 768
HD = 64
FFL = 384
TOK = 128
BLK = 32
EPS = 1e-05
BF = jnp.bfloat16
F32 = jnp.float32

CHIP = ("y", "xl")
CORE = "c"
MICRO = "zh"
GROUP = ("zl", "xh")
NARROW = (MICRO, *GROUP)
WIDE = (*CHIP, CORE)


def chip_index():
    return lax.axis_index("y") * 2 + lax.axis_index("xl")


def group_index():
    return lax.axis_index("zl") * 2 + lax.axis_index("xh")


def mm(left, right):
    return lax.dot_general(left, right, (((1,), (0,)), ((), ())), preferred_element_type=F32)


def mm_nt(left, right):
    return lax.dot_general(left, right, (((1,), (1,)), ((), ())), preferred_element_type=F32)


def mm_tn(left, right):
    return lax.dot_general(left, right, (((0,), (0,)), ((), ())), preferred_element_type=F32)


def normalized(values):
    center = values - jnp.mean(values, axis=-1, keepdims=True)
    spread = jnp.mean(center * center, axis=-1, keepdims=True)
    inverse = lax.rsqrt(spread + EPS)
    return center * inverse, inverse


def norm_back(grad, unit, inverse, gain):
    scaled = grad * gain
    first = jnp.mean(scaled, axis=-1, keepdims=True)
    second = jnp.mean(scaled * unit, axis=-1, keepdims=True)
    return inverse * (scaled - first - unit * second)


def halves(block):
    lane = lax.broadcasted_iota(jnp.int32, block.shape, 1)
    zero = jnp.zeros_like(block)
    return jnp.where(lane < HD, block, zero), jnp.where(lane < HD, zero, block)


def join(low, high):
    lane = lax.broadcasted_iota(jnp.int32, low.shape, 1)
    return jnp.where(lane < HD, low, high)


def span(scene_ref):
    micro = lax.axis_index(MICRO)
    own = scene_ref[micro, chip_index() * 4]
    first = jnp.int32(0)
    count = jnp.int32(0)
    for index in range(8):
        other = scene_ref[micro, index * 4]
        first += (other < own).astype(jnp.int32)
        count += (other == own).astype(jnp.int32)
    return first, count > 1


def three(value):
    a = value.astype(BF).astype(F32)
    b = (value - a).astype(BF).astype(F32)
    c = value - a - b
    return a, b, c


def put_columns(width, rows, start, columns):
    lane = lax.broadcasted_iota(jnp.int32, (rows, width), 1)
    out = jnp.zeros((rows, width), F32)
    for offset, column in enumerate(columns):
        out = jnp.where(lane == start + offset, column, out)
    return out


def pin(value):
    return pltpu.with_memory_space_constraint(value, pltpu.HBM)


def call(kernel, outs, ins, cost, scratch=(), vmem=16, aliases=None):
    places = {"V": pltpu.VMEM, "H": pltpu.HBM, "S": pltpu.SMEM, "L": pltpu.VMEM, "A": pl.ANY}
    return pl.pallas_call(
        kernel,
        out_shape=[
            (pltpu.HBM if place in "HL" else jax.ShapeDtypeStruct)(shape, dtype) for shape, dtype, place in outs
        ],
        in_specs=[pl.BlockSpec(memory_space=places[place]) for _, place in ins],
        out_specs=[pl.BlockSpec(memory_space=places[place]) for _, _, place in outs],
        scratch_shapes=list(scratch),
        input_output_aliases=aliases or {},
        cost_estimate=pl.CostEstimate(flops=cost, bytes_accessed=1000, transcendentals=0),
        compiler_params=pltpu.CompilerParams(vmem_limit_bytes=vmem * 2**20),
    )(*[pin(value) if place in "HL" else value for value, place in ins])


DMA = pltpu.SemaphoreType.DMA


def send_copies(source, target, indices, sem):
    copies = [pltpu.make_async_copy(source, target.at[index], sem.at[index]) for index in indices]
    for copy in copies:
        copy.start()
    return copies


def wait_all(copies):
    for copy in copies:
        copy.wait()


def weight_copies(w_ref, w_buf, w_sem, parts=(1, 2, 0), start=True):
    group = group_index()
    copies = []
    for slot, part in enumerate(parts):
        column = pl.multiple_of(part * D + (group // 2) * 384, 128)
        copy = pltpu.make_async_copy(w_ref.at[:, pl.ds(column, 384)], w_buf.at[slot], w_sem.at[slot])
        if start:
            copy.start()
        copies.append(copy)
    return copies


def own_heads(full):
    odd = (group_index() % 2) == 1
    return jnp.where(odd, full[:, 192:], full[:, :192]).astype(BF)


def project_kernel(
    tok_ref, gain_ref, shift_ref, w_ref, kv_ref, normed_ref,
    x_buf, w_buf, kv_buf, gain_buf, shift_buf, x_sem, w_sem, kv_sem, gain_sem, shift_sem,
):
    copy_x = pltpu.make_async_copy(tok_ref.at[lax.axis_index(MICRO)], x_buf, x_sem)
    copy_x.start()
    copy_gain = pltpu.make_async_copy(gain_ref, gain_buf, gain_sem)
    copy_gain.start()
    copy_shift = pltpu.make_async_copy(shift_ref, shift_buf, shift_sem)
    copy_shift.start()
    copies = weight_copies(w_ref, w_buf, w_sem, (1, 2))
    wait_all([copy_x, copy_gain, copy_shift])
    unit, _ = normalized(x_buf[...].astype(F32))
    normed = (unit * gain_buf[...].reshape(1, D) + shift_buf[...].reshape(1, D)).astype(BF)
    normed_ref[...] = normed
    parts = []
    for slot in range(2):
        copies[slot].wait()
        parts.append(own_heads(mm(normed, w_buf[slot])))
    kv_buf[...] = jnp.concatenate(parts, axis=1)
    wait_all(send_copies(kv_buf, kv_ref, range(8), kv_sem))


def query_kernel(normed_ref, w_ref, q_ref, w_buf, w_sem):
    weight_copies(w_ref, w_buf, w_sem, (0,))[0].wait()
    part = own_heads(mm(normed_ref[...], w_buf[0]))
    q_ref[...] = jnp.concatenate([part, jnp.zeros((TOK, HD), BF)], axis=1)


def block_query_kernel(normed_ref, w_ref, out_ref, x_buf, w_buf, x_sem, w_sem):
    block = pl.ds(pl.multiple_of(group_index() * BLK, BLK), BLK)
    loads = [
        pltpu.make_async_copy(normed_ref.at[block], x_buf, x_sem),
        pltpu.make_async_copy(w_ref.at[:, pl.ds(0, D)], w_buf, w_sem),
    ]
    for load in loads:
        load.start()
    wait_all(loads)
    query = mm(x_buf[...], w_buf[...]).astype(BF)
    zero = jnp.zeros((BLK, HD), BF)
    for group in range(4):
        out_ref[group] = jnp.concatenate([query[:, group * 192:(group + 1) * 192], zero], axis=1)


def attend_kernel(scene_ref, q_ref, same_ref, other_ref, out_ref, buf, q_buf, sem, q_sem):
    load = pltpu.make_async_copy(q_ref, q_buf, q_sem)
    load.start()
    first, big = span(scene_ref)

    def run(count):
        rows = count * TOK
        keys = jnp.concatenate(
            [ref[pl.ds(first, count)].reshape(rows, 384) for ref in (same_ref, other_ref)], axis=0
        )
        load.wait()
        query = q_buf[...]
        q0, q1 = halves(query[:, :128])
        blocks = [keys[:, :128], keys[:, 128:256], keys[:, 256:]]
        mixed = []
        columns = []
        for qh, kb, vb in ((q0, 0, 1), (q1, 0, 2), (query[:, 128:], 1, 2)):
            scores = mm_nt(qh, blocks[kb]) * (HD**-0.5)
            top = jnp.max(scores, axis=-1, keepdims=True)
            weights = jnp.exp(scores - top)
            total = jnp.sum(weights, axis=-1, keepdims=True)
            probs = (weights * (1.0 / total)).astype(BF)
            mixed.append(mm(probs, blocks[vb]))
            columns += three(top + jnp.log(total))
        stats = put_columns(128, TOK, 0, columns)
        buf[...] = jnp.concatenate([join(stats, mixed[0]), join(mixed[1], mixed[2])], axis=1).astype(BF)

    @pl.when(big)
    def _():
        run(5)

    @pl.when(jnp.logical_not(big))
    def _():
        run(1)

    wait_all(send_copies(buf, out_ref, range(8), sem))


def forward_kernel(
    mixed_ref, tok_ref, og_ref, wo_ref, gain_ref, shift_ref, up_ref, down_ref,
    out_ref, middle_ref, normed_ref, act_ref, gpre_ref,
    tok_buf, og_buf, up_buf, down_buf, gain_buf, shift_buf, grad_buf, branch_buf, middle_buf, in_sem, sem,
):
    loads = [
        pltpu.make_async_copy(ref, buf, in_sem.at[index])
        for index, (ref, buf) in enumerate(
            (
                (tok_ref, tok_buf), (up_ref, up_buf), (og_ref, og_buf), (down_ref, down_buf), (gain_ref, gain_buf),
                (shift_ref, shift_buf),
            )
        )
    ]
    for load in loads:
        load.start()
    total = jnp.zeros((2 * TOK, D), F32)
    for group in range(4):
        rows = jnp.concatenate([mixed_ref[group], mixed_ref[4 + group]], axis=0)
        total = total + mm(rows, wo_ref[group])
    loads[0].wait()
    total = total + tok_buf[...].reshape(2 * TOK, D).astype(F32)
    middle_buf[...] = total.reshape(8, BLK, D)
    third = pltpu.make_async_copy(
        middle_buf.at[lax.axis_index(MICRO) * 4 + group_index()], middle_ref, sem.at[2]
    )
    third.start()
    unit, _ = normalized(total)
    wait_all(loads[4:])
    normed = (unit * gain_buf[...].reshape(1, D) + shift_buf[...].reshape(1, D)).astype(BF)
    normed_ref[...] = normed
    loads[1].wait()
    pre = mm(normed, up_buf[...])
    cdf = 0.5 * (1.0 + lax.erf(pre * (0.5**0.5)))
    slope = cdf + pre * jnp.exp(-0.5 * pre * pre) * 0.3989422804014327
    loads[2].wait()
    loads[3].wait()
    grad_out = og_buf[...].reshape(2 * TOK, D)
    gpre = (mm_nt(grad_out, down_buf[...]) * slope).astype(BF)
    gpre_ref[...] = gpre
    grad_buf[...] = mm_nt(gpre, up_buf[...]).astype(BF).reshape(8, BLK, D)
    first = pltpu.make_async_copy(grad_buf, out_ref.at[:, pl.ds(BLK, BLK)], sem.at[0])
    first.start()
    act = (pre * cdf).astype(BF)
    act_ref[...] = act
    branch_buf[...] = mm(act, down_buf[...]).astype(BF).reshape(8, BLK, D)
    second = pltpu.make_async_copy(branch_buf, out_ref.at[:, pl.ds(0, BLK)], sem.at[1])
    second.start()
    wait_all([first, second, third])


def ff_grads_kernel(normed_ref, act_ref, gpre_ref, og_ref, keep_ref, send_ref, up_buf, down_buf):
    core = lax.axis_index(CORE)
    up_buf[...] = mm_tn(normed_ref[...], gpre_ref[...])
    down_buf[...] = mm_tn(act_ref[...], og_ref[...].reshape(2 * TOK, D))
    for ref, owner in ((keep_ref, core), (send_ref, 1 - core)):
        column = pl.multiple_of(owner * 384, 128)
        for tile in range(8):
            rows = pl.ds(pl.multiple_of((2 * tile + owner) * 48, 16), 48)
            ref[tile, :, :384] = up_buf[rows].astype(BF)
            ref[tile, :, 384:] = down_buf[tile * 48:(tile + 1) * 48, pl.ds(column, 384)].astype(BF)


def split_kernel(one_ref, two_ref, *refs):
    y = lax.axis_index("y")
    for k, ref in enumerate(refs):
        for xl in range(2):
            at = (y ^ k) * 2 + xl
            ref[xl] = (one_ref[at].astype(F32) + two_ref[at].astype(F32)).astype(BF)


def total_kernel(*refs):
    total = refs[0][...].astype(F32)
    for ref in refs[1:4]:
        total = total + ref[...].astype(F32)
    refs[4][...] = total.astype(BF)


def middle_kernel(
    sums_ref, middle_ref, og_ref, mixed_ref, wo_ref, gain_ref, query_ref,
    out_ref, low_ref, grad_ref, result_ref, vec_ref,
    buf, middle_buf, og_buf, mixed_buf, gain_buf, query_buf, low_buf, grad_buf, result_buf, vec_buf, in_sem, sem, rest_sem,
):
    micro = lax.axis_index(MICRO)
    group = group_index()
    block = pl.ds(pl.multiple_of(group * BLK, BLK), BLK)
    loads = [
        pltpu.make_async_copy(middle_ref, middle_buf, in_sem.at[0]),
        pltpu.make_async_copy(og_ref.at[micro, block], og_buf, in_sem.at[1]),
        pltpu.make_async_copy(mixed_ref.at[pl.ds(micro * 4, 4), block], mixed_buf, in_sem.at[2]),
        pltpu.make_async_copy(gain_ref, gain_buf, in_sem.at[3]),
        pltpu.make_async_copy(query_ref, query_buf, in_sem.at[4]),
    ]
    for load in loads:
        load.start()
    total = sums_ref[0].astype(F32)
    for index in range(1, 8):
        total = total + sums_ref[index].astype(F32)
    branch, grad = total[:BLK], total[BLK:]
    wait_all(loads)
    middle = middle_buf[...]
    unit, inverse = normalized(middle)
    grad_mid = og_buf[...].astype(F32) + norm_back(grad, unit, inverse, gain_buf[...].reshape(1, D))
    low = grad_mid.astype(BF)
    low_buf[...] = low
    grad_buf[...] = grad_mid
    result_buf[...] = (middle + branch).astype(BF)
    gain_grad = jnp.sum(grad * unit, axis=0, keepdims=True)
    shift_grad = jnp.sum(grad, axis=0, keepdims=True)
    vec_buf[...] = jnp.concatenate([gain_grad, shift_grad, jnp.zeros((6, D), F32)], axis=0)
    stores = [
        pltpu.make_async_copy(source, target, rest_sem.at[index])
        for index, (source, target) in enumerate(
            ((low_buf, low_ref), (grad_buf, grad_ref), (result_buf, result_ref), (vec_buf, vec_ref))
        )
    ]
    for store in stores:
        store.start()
    lane = lax.broadcasted_iota(jnp.int32, (BLK, 256), 1)
    for head_group in range(4):
        mixed = mixed_buf[head_group].astype(F32)
        back = mm_nt(low, wo_ref[head_group]).astype(BF).astype(F32)
        product = mixed * back
        columns = []
        for head in range(3):
            inside = (lane >= (head + 1) * HD) & (lane < (head + 2) * HD)
            columns += three(jnp.sum(jnp.where(inside, product, 0.0), axis=-1, keepdims=True))
        stats = put_columns(256, BLK, 9, columns)
        buf[head_group, :, :256] = jnp.where(lane < 9, mixed, jnp.where(lane < HD, stats, back)).astype(BF)
        buf[head_group, :, 256:] = query_buf[head_group]
    sends = send_copies(buf, out_ref, range(8), sem)
    wait_all(stores)
    wait_all(sends)


def attend_back_kernel(
    scene_ref, kvs_ref, kvo_ref, gs_ref, go_ref, normed_ref, mixed_ref, low_ref, low1_ref, low2_ref, low3_ref,
    w_ref, gqkv_ref, w_out_ref, keep_ref, send_ref,
    kv_buf, grad_buf, mixed_buf, normed_buf, low_buf, kv_sem, in_sem, w_sem,
):
    first, big = span(scene_ref)
    chip = chip_index()
    core = lax.axis_index(CORE)
    group = group_index()
    index = lax.axis_index(MICRO) * 4 + group
    first_loads = [
        pltpu.make_async_copy(source, target, in_sem.at[slot])
        for slot, (source, target) in enumerate(
            ((normed_ref, normed_buf), (mixed_ref.at[index], mixed_buf), (low_ref, low_buf))
        )
    ]
    scale = HD**-0.5

    def run(count):
        rows = count * TOK
        loads = [pltpu.make_async_copy(kvs_ref.at[pl.ds(first, count)], kv_buf.at[pl.ds(0, count)], kv_sem)]
        for load in loads + first_loads:
            load.start()
        weight_copies(w_ref, w_out_ref, w_sem)

        def cut(value):
            return [value[:, at:at + 128] for at in range(0, value.shape[1], 128)]

        every = cut(jnp.concatenate(
            [ref[pl.ds(first, count)].reshape(rows, 512) for ref in (gs_ref, go_ref)], axis=0
        ))
        grad, query = every[:2], every[2:]
        g_own = cut(gs_ref[chip])
        g_heads = [halves(g_own[0])[1], *halves(g_own[1])]
        own_stats = g_own[0].astype(F32)
        all_stats = grad[0].astype(F32).T
        wait_all(loads)
        kv = cut(jnp.concatenate(
            [kv_buf[:count].reshape(rows, 384), kvo_ref[pl.ds(first, count)].reshape(rows, 384)], axis=0
        ))
        own = cut(kv_buf[chip - first]) + g_own[2:]
        q_heads = [*halves(own[3]), own[4]]
        k_heads = [*halves(own[0]), halves(own[1])[0]]
        v_heads = [halves(own[1])[1], *halves(own[2])]

        def column(at):
            return own_stats[:, at:at + 1] + own_stats[:, at + 1:at + 2] + own_stats[:, at + 2:at + 3]

        def row(at):
            return all_stats[at:at + 1] + all_stats[at + 1:at + 2] + all_stats[at + 2:at + 3]

        dq, dk, dv = [], [], []
        for head, (kb, vb) in enumerate(((0, 1), (0, 2), (1, 2))):
            qb, gb = (0, 0, 1)[head], (0, 1, 1)[head]
            probs = jnp.exp(mm_nt(q_heads[head], kv[kb]) * scale - column(3 * head))
            gap = mm_nt(g_heads[head], kv[vb]) - column(9 + 3 * head)
            dq.append(mm((probs * gap).astype(BF), kv[kb]) * scale)
            probs = jnp.exp(mm_nt(k_heads[head], query[qb]) * scale - row(3 * head))
            gap = mm_nt(v_heads[head], grad[gb]) - row(9 + 3 * head)
            dv.append(mm(probs.astype(BF), grad[gb]))
            dk.append(mm((probs * gap).astype(BF), query[qb]) * scale)
        tail = dq[2]
        gqkv_ref[...] = jnp.concatenate(
            [join(dk[0], dk[1]), join(dk[2], dv[0]), join(dv[1], dv[2]), join(dq[0], dq[1]),
             join(tail, jnp.zeros_like(tail))],
            axis=1,
        ).astype(BF)


    @pl.when(big)
    def _():
        run(5)

    @pl.when(jnp.logical_not(big))
    def _():
        run(1)

    wait_all(first_loads)

    grad_buf[...] = mm_tn(normed_buf[...], gqkv_ref[...])
    low = jnp.concatenate([ref[...] for ref in (low_buf, low1_ref, low2_ref, low3_ref)], axis=0)
    mixed = jnp.concatenate(
        [mixed_buf[pl.ds(pl.multiple_of((group ^ k) * BLK, BLK), BLK)] for k in range(4)], axis=0
    )
    out = mm_tn(mixed, low)[HD:]
    for ref, owner in ((keep_ref, core), (send_ref, 1 - core)):
        for tile in range(8):
            rows = grad_buf[pl.ds(pl.multiple_of((2 * tile + owner) * 48, 16), 48)]
            at = (tile // 4) * 96
            pieces = [
                out[at + row * 48:at + (row + 1) * 48, (tile % 4) * 192:(tile % 4 + 1) * 192] for row in range(2)
            ]
            ref[2 * tile] = rows[:, :384].astype(BF)
            ref[2 * tile + 1] = jnp.concatenate(
                [rows[:, 384:576], jnp.where(owner == 1, pieces[1], pieces[0])], axis=1
            ).astype(BF)
    wait_all(weight_copies(w_ref, w_out_ref, w_sem, start=False))


def normed_grad_kernel(
    gqkv_ref, w_ref, tok_ref, vec_ref, near_ref, far_ref, own_ref, one_ref, two_ref, three_ref, sums_ref, ff_ref,
    x_buf, vec_buf, near_buf, part_buf, low_buf, sums_buf, ff_buf, rows_buf, in_sem, out_sem, row_sem,
):
    loads = [
        pltpu.make_async_copy(tok_ref.at[lax.axis_index(MICRO)], x_buf, in_sem.at[0]),
        pltpu.make_async_copy(vec_ref, vec_buf, in_sem.at[1]),
        pltpu.make_async_copy(near_ref, near_buf, in_sem.at[2]),
    ]
    for load in loads:
        load.start()
    group = group_index()
    odd = (group % 2) == 1
    total = jnp.zeros((TOK, D), F32)
    for slot in range(3):
        part = gqkv_ref[:, slot * 192:(slot + 1) * 192]
        zero = jnp.zeros_like(part)
        wide = jnp.where(
            odd, jnp.concatenate([zero, part], axis=1), jnp.concatenate([part, zero], axis=1)
        )
        total = total + mm_nt(wide, w_ref[slot])
    part_buf[...] = total
    low_buf[...] = total.astype(BF)
    stores = []
    for k, ref in enumerate((own_ref, one_ref, two_ref, three_ref)):
        rows = pl.ds(pl.multiple_of((group ^ k) * BLK, BLK), BLK)
        target = ref.at[pl.ds(0, BLK)] if k else ref
        stores.append(pltpu.make_async_copy((low_buf if k else part_buf).at[rows], target, out_sem.at[k]))
        stores[-1].start()
    wait_all(loads)
    ff_buf[...] = (near_buf[...].astype(F32) + far_ref[...].astype(F32)).astype(BF)
    stores.append(pltpu.make_async_copy(ff_buf, ff_ref, out_sem.at[5]))
    stores[-1].start()
    unit, _ = normalized(x_buf[...].astype(F32))
    gain1 = jnp.sum(total * unit, axis=0, keepdims=True)
    shift1 = jnp.sum(total, axis=0, keepdims=True)
    vectors = jnp.concatenate([gain1, shift1, vec_buf[...][:2], jnp.zeros((4, D), F32)], axis=0)
    sums_buf[...] = vectors
    for index in range(4):
        rows_buf[index] = jnp.concatenate(
            [vectors[index:index + 1], jnp.zeros((15, D), F32)], axis=0
        ).astype(BF)
    for k, ref in enumerate((one_ref, two_ref, three_ref)):
        stores.append(
            pltpu.make_async_copy(rows_buf.at[group ^ (k + 1)], ref.at[pl.ds(BLK, 16)], row_sem.at[k])
        )
        stores[-1].start()
    stores.append(pltpu.make_async_copy(sums_buf, sums_ref, out_sem.at[4]))
    stores[-1].start()
    wait_all(stores)


def add_kernel(one_ref, two_ref, unused_ref, out_ref, buf, sem):
    buf[...] = (one_ref[...].astype(F32) + two_ref[...].astype(F32)).astype(BF)
    copy = pltpu.make_async_copy(buf, out_ref, sem)
    copy.start()
    copy.wait()


def sum_kernel(in_ref, vec_ref, one_ref, two_ref, three_ref, out_ref, buf, vec_buf, row_buf, sem, vec_sem, row_sem):
    loads = [pltpu.make_async_copy(vec_ref, vec_buf, vec_sem)] + [
        pltpu.make_async_copy(ref.at[pl.ds(BLK, 16)], row_buf.at[k], row_sem.at[k])
        for k, ref in enumerate((one_ref, two_ref, three_ref))
    ]
    for load in loads:
        load.start()
    total = in_ref[0].astype(F32)
    for index in range(1, 16):
        total = total + in_ref[index].astype(F32)
    wait_all(loads)
    vector = vec_buf[pl.ds(group_index(), 1)]
    for k in range(3):
        vector = vector + row_buf[k].astype(F32)[:1]
    rows = [vector[:, at:at + 128] for at in range(0, D, 128)] + [jnp.zeros((2, 128), F32)]
    pieces = [total[at:at + 8] for at in range(0, 48, 8)] + [jnp.concatenate(rows, axis=0)]
    block = jnp.concatenate(pieces, axis=1).astype(BF)
    for index in range(8):
        buf[index] = block
    wait_all(send_copies(buf, out_ref, range(8), sem))


def spread_kernel(turn, in_ref, *refs):
    qkv_buf, out_buf, sem, out_sem = refs[-4:]
    if turn:
        in_buf, in_sem = refs[-6:-4]
        qkv_ref, out_ref, *vec_refs = refs[3:-6]
        loads = [pltpu.make_async_copy(in_ref.at[tile], in_buf.at[tile], in_sem.at[tile]) for tile in range(8)]
        for load in loads:
            load.start()
    else:
        qkv_ref, out_ref, *vec_refs = refs[:-4]
        in_buf = in_ref
    owner = lax.axis_index(CORE)
    owner = 1 - owner if turn else owner
    copies = []
    vectors = [jnp.zeros((8, 128), F32)] * 4
    for tile in range(8):
        if turn:
            loads[tile].wait()
        whole = [in_buf[tile, index].astype(F32) for index in range(8)]
        block = [
            jnp.concatenate([value[:, at:at + 384] for at in range(0, 2304, 384)], axis=0) for value in whole
        ]
        vectors = [total + whole[k][:, 2304:] + whole[4 + k][:, 2304:] for k, total in enumerate(vectors)]
        for part, half, at in ((1, 0, 0), (2, 0, 192), (0, 4, 0)):
            qkv_buf[tile, :, part * D:(part + 1) * D] = jnp.concatenate(
                [block[half + group][:, at:at + 192] for group in range(4)], axis=1
            )
        start = pl.multiple_of((2 * tile + owner) * 48, 16)
        copy = pltpu.make_async_copy(qkv_buf.at[tile], qkv_ref.at[pl.ds(start, 48)], sem.at[tile])
        copy.start()
        copies.append(copy)
        for group in range(4):
            out_buf[group, tile // 4, :, (tile % 4) * 192:(tile % 4 + 1) * 192] = block[4 + group][:, 192:]
    for group in range(4):
        for pair in range(2):
            start = pl.multiple_of(group * 192 + (pair * 2 + owner) * 48, 16)
            copy = pltpu.make_async_copy(
                out_buf.at[group, pair], out_ref.at[pl.ds(start, 48)], out_sem.at[group, pair]
            )
            copy.start()
            copies.append(copy)
    if turn:
        for k, ref in enumerate(vec_refs):
            total = vectors[k] + refs[0][k]
            ref[...] = jnp.concatenate([total[row:row + 1] for row in range(6)], axis=1).reshape(D)
    else:
        for k, total in enumerate(vectors):
            vec_refs[0][k] = total
    wait_all(copies)


def spread_ff_kernel(*refs):
    up_ref, down_ref, up_buf, down_buf, up_sem, down_sem = refs[8:]
    y, core = lax.axis_index("y"), lax.axis_index(CORE)
    copies = []
    for near in range(4):
        for xl in range(2):
            chip = (y ^ near) * 2 + xl
            for index in (near, near + 4):
                owner = core ^ (index // 4)
                block = refs[index][xl].astype(F32)
                up_buf[near, xl, pl.ds(pl.multiple_of(owner * 48, 16), 48)] = block[:, :384]
                down_buf[near, xl, :, pl.ds(pl.multiple_of(owner * 384, 128), 384)] = block[:, 384:]
            for source, target, rows, sem in ((up_buf, up_ref, 96, up_sem), (down_buf, down_ref, 48, down_sem)):
                copy = pltpu.make_async_copy(
                    source.at[near, xl],
                    target.at[pl.ds(pl.multiple_of(chip * rows, 16), rows)],
                    sem.at[near, xl],
                )
                copy.start()
                copies.append(copy)
    wait_all(copies)


def input_kernel(
    own_ref, one_ref, two_ref, three_ref, tok_ref, gain_ref, grad_ref, result_ref, unused_ref, out_ref, buf, x_buf, sem, x_sem
):
    start = pl.multiple_of(group_index() * BLK, BLK)
    load = pltpu.make_async_copy(tok_ref.at[lax.axis_index(MICRO), pl.ds(start, BLK)], x_buf, x_sem)
    load.start()
    load.wait()
    total = own_ref[...]
    for ref in (one_ref, two_ref, three_ref):
        total = total + ref[:BLK].astype(F32)
    unit, inverse = normalized(x_buf[...].astype(F32))
    grad = grad_ref[...] + norm_back(total, unit, inverse, gain_ref[...].reshape(1, D))
    buf[:BLK] = grad.astype(BF)
    buf[BLK:] = result_ref[...]
    wait_all(send_copies(buf, out_ref, range(8), sem))


def unpack_kernel(in_ref, unused_ref, other_ref, grad_ref, result_ref):
    for index in range(8):
        rows = slice(index % 4 * BLK, (index % 4 + 1) * BLK)
        grad_ref[index // 4, rows] = in_ref[index, :BLK].astype(F32)
        result_ref[index // 4, rows] = in_ref[index, BLK:]


def exchange(value, axes):
    return lax.all_to_all(value, axes, 0, 0, tiled=True)


def swap(value):
    return lax.ppermute(value, CORE, [(0, 1), (1, 0)])


def after(value, *others):
    return pl.pallas_call(
        lambda *refs: None,
        out_shape=jax.ShapeDtypeStruct(value.shape, value.dtype),
        in_specs=[pl.BlockSpec(memory_space=pl.ANY)] * (1 + len(others)),
        out_specs=pl.BlockSpec(memory_space=pl.ANY),
        input_output_aliases={0: 0},
        cost_estimate=pl.CostEstimate(flops=1, bytes_accessed=1, transcendentals=0),
        compiler_params=pltpu.CompilerParams(vmem_limit_bytes=2**20),
    )(value, *others)


def flip(value, axes, count, bits):
    return lax.ppermute(value, axes, [(index, index ^ bits) for index in range(count)])


def shards(
    tokens, scene_of_block, ln1_gain, ln1_shift, w_qkv, w_out, ln2_gain, ln2_shift, w_up, w_down, out_grad
):
    w_out_pad = jnp.pad(w_out.reshape(4, 192, D), ((0, 0), (HD, 0), (0, 0)))
    kv_send, normed = call(
        project_kernel,
        [((8, TOK, 384), BF, "H"), ((TOK, D), BF, "L")],
        [(tokens, "H"), (ln1_gain, "H"), (ln1_shift, "H"), (w_qkv, "H")],
        1000,
        [
            pltpu.VMEM((TOK, D), BF), pltpu.VMEM((2, D, 384), BF), pltpu.VMEM((TOK, 384), BF),
            pltpu.VMEM((D,), F32), pltpu.VMEM((D,), F32), DMA, DMA((2,)), DMA((8,)), DMA, DMA,
        ],
    )
    (query,) = call(
        query_kernel,
        [((TOK, 256), BF, "L")],
        [(normed, "L"), (w_qkv, "H")],
        1000,
        [pltpu.VMEM((1, D, 384), BF), DMA((1,))],
    )
    kv_same = exchange(kv_send, CHIP)
    kv_same = after(kv_same, pin(query))
    kv_other = swap(kv_same)
    (mixed_send,) = call(
        attend_kernel,
        [((8, TOK, 256), BF, "H")],
        [(scene_of_block, "S"), (query, "H"), (kv_same, "V"), (kv_other, "V")],
        1000,
        [pltpu.VMEM((TOK, 256), BF), pltpu.VMEM((TOK, 256), BF), DMA((8,)), DMA],
    )
    mixed = exchange(mixed_send, NARROW)
    (block_query,) = call(
        block_query_kernel,
        [((4, BLK, 256), BF, "L")],
        [(normed, "H"), (w_qkv, "H")],
        1000,
        [pltpu.VMEM((BLK, D), BF), pltpu.VMEM((D, D), BF), DMA, DMA],
    )
    ff_send, middle, normed2, act, grad_pre = call(
        forward_kernel,
        [
            ((8, 2 * BLK, D), BF, "H"), ((BLK, D), F32, "H"), ((2 * TOK, D), BF, "V"),
            ((2 * TOK, FFL), BF, "V"), ((2 * TOK, FFL), BF, "V"),
        ],
        [
            (mixed, "V"), (tokens, "H"), (out_grad, "H"), (w_out_pad, "V"), (ln2_gain, "H"), (ln2_shift, "H"),
            (w_up, "H"), (w_down, "H"),
        ],
        1000,
        [
            pltpu.VMEM((2, TOK, D), BF), pltpu.VMEM((2, TOK, D), BF), pltpu.VMEM((D, FFL), BF),
            pltpu.VMEM((FFL, D), BF), pltpu.VMEM((D,), F32), pltpu.VMEM((D,), F32), pltpu.VMEM((8, BLK, D), BF),
            pltpu.VMEM((8, BLK, D), BF), pltpu.VMEM((8, BLK, D), F32), DMA((6,)), DMA((3,)),
        ],
    )
    ff_sums = exchange(ff_send, NARROW)
    keep, send = call(
        ff_grads_kernel,
        [((8, 48, D), BF, "V")] * 2,
        [(normed2, "V"), (act, "V"), (grad_pre, "V"), (out_grad, "L")],
        1000,
        [pltpu.VMEM((D, FFL), F32), pltpu.VMEM((FFL, D), F32)],
    )
    pieces = call(
        split_kernel, [((2, 48, D), BF, "L")] * 4, [(keep, "V"), (swap(send), "V")], 1000
    )
    pieces = [pieces[0]] + [flip(pieces[k], "y", 4, k) for k in (1, 2, 3)]
    (ff_near,) = call(
        total_kernel,
        [((2, 48, D), BF, "L")],
        [(pieces[0], "L")] + [(piece, "V") for piece in pieces[1:]],
        1000,
    )
    grad_send, low, grad_mid, result_part, vec2 = call(
        middle_kernel,
        [
            ((8, 4, BLK, 512), BF, "H"), ((BLK, D), BF, "H"), ((BLK, D), F32, "H"), ((BLK, D), BF, "H"),
            ((8, D), F32, "H"),
        ],
        [
            (ff_sums, "V"), (middle, "H"), (out_grad, "H"), (mixed, "H"), (w_out_pad, "V"), (ln2_gain, "H"),
            (block_query, "H"),
        ],
        1000,
        [
            pltpu.VMEM((4, BLK, 512), BF), pltpu.VMEM((BLK, D), F32), pltpu.VMEM((BLK, D), BF),
            pltpu.VMEM((4, BLK, 256), BF), pltpu.VMEM((D,), F32), pltpu.VMEM((4, BLK, 256), BF), pltpu.VMEM((BLK, D), BF), pltpu.VMEM((BLK, D), F32),
            pltpu.VMEM((BLK, D), BF), pltpu.VMEM((8, D), F32), DMA((5,)), DMA((8,)), DMA((4,)),
        ],
    )
    grad_send = after(pin(grad_send), *pieces[1:])
    grad_same = exchange(grad_send.reshape(32, BLK, 512), (*CHIP, *GROUP)).reshape(8, TOK, 512)
    lows = [flip(low, GROUP, 4, k) for k in (1, 2, 3)]
    kv_same = after(pin(kv_same), low)
    kv_other = swap(kv_same)
    grad_same = after(grad_same, *lows, kv_other, pin(ff_near))
    grad_other = swap(grad_same)
    ff_near = after(pin(ff_near), grad_other)
    ff_far = flip(ff_near, "xl", 2, 1)
    gqkv, w_own, keep, send = call(
        attend_back_kernel,
        [((TOK, 640), BF, "V"), ((3, D, 384), BF, "V")] + [((16, 48, 384), BF, "V")] * 2,
        [
            (scene_of_block, "S"), (kv_same, "H"), (kv_other, "V"), (grad_same, "V"), (grad_other, "V"),
            (normed, "H"), (mixed, "H"), (low, "H"), *[(value, "V") for value in lows], (w_qkv, "H"),
        ],
        1000,
        [
            pltpu.VMEM((5, TOK, 384), BF), pltpu.VMEM((D, 640), F32),
            pltpu.VMEM((TOK, 256), BF), pltpu.VMEM((TOK, D), BF), pltpu.VMEM((BLK, D), BF),
            DMA, DMA((3,)), DMA((3,)),
        ],
        vmem=24,
    )
    own, *sends, sums, ff_part = call(
        normed_grad_kernel,
        [((BLK, D), F32, "H")] + [((BLK + 16, D), BF, "H")] * 3 + [((8, D), F32, "H"), ((2, 48, D), BF, "H")],
        [(gqkv, "V"), (w_own, "V"), (tokens, "H"), (vec2, "H"), (ff_near, "H"), (ff_far, "V")],
        1000,
        [
            pltpu.VMEM((TOK, D), BF), pltpu.VMEM((8, D), F32), pltpu.VMEM((2, 48, D), BF), pltpu.VMEM((TOK, D), F32),
            pltpu.VMEM((TOK, D), BF), pltpu.VMEM((8, D), F32), pltpu.VMEM((2, 48, D), BF), pltpu.VMEM((4, 16, D), BF),
            DMA((3,)), DMA((6,)), DMA((3,)),
        ],
    )
    (weight_send,) = call(
        add_kernel,
        [((16, 48, 384), BF, "H")],
        [(keep, "V"), (swap(after(send, ff_far)), "V"), (own, "H")],
        1000,
        [pltpu.VMEM((16, 48, 384), BF), DMA],
    )
    weight_parts = exchange(weight_send, (*CHIP, MICRO))
    parts = [flip(value, GROUP, 4, k + 1) for k, value in enumerate(sends)]
    weight_parts = after(weight_parts, pin(sums), *parts)
    ff_parts = [flip(ff_part, "y", 4, k) for k in (1, 2, 3)]
    (weight_total,) = call(
        sum_kernel,
        [((8, 8, 8, 2432), BF, "H")],
        [(weight_parts, "V"), (sums, "H"), *[(value, "A") for value in parts]],
        1000,
        [
            pltpu.VMEM((8, 8, 2432), BF), pltpu.VMEM((8, D), F32), pltpu.VMEM((3, 16, D), BF), DMA((8,)), DMA,
            DMA((3,)),
        ],
    )
    (packed,) = call(
        input_kernel,
        [((8, 2 * BLK, D), BF, "H")],
        [
            (own, "L"), *[(value, "V") for value in parts], (tokens, "H"), (ln1_gain, "L"), (grad_mid, "L"),
            (result_part, "L"), (weight_total, "H"),
        ],
        1000,
        [pltpu.VMEM((2 * BLK, D), BF), pltpu.VMEM((BLK, D), BF), DMA((8,)), DMA],
    )
    weight_same = exchange(weight_total.reshape(64, 8, 2432), (*CHIP, *NARROW)).reshape(8, 8, 8, 2432)
    weight_same = after(weight_same, pin(packed))
    everyone = exchange(after(pin(packed), weight_same), NARROW)
    weight_other = swap(weight_same)
    scratch = [
        pltpu.VMEM((8, 48, 3 * D), F32), pltpu.VMEM((4, 2, 48, D), F32), DMA((8,)), DMA((4, 2)),
    ]
    grads = [((D, 3 * D), F32, "H"), ((D, D), F32, "H")]
    half = call(
        functools.partial(spread_kernel, False),
        grads + [((4, 8, 128), F32, "V")],
        [(weight_same, "V")],
        1000,
        scratch,
    )
    qkv_grad, out_proj_grad, *vectors = call(
        functools.partial(spread_kernel, True),
        grads + [((D,), F32, "L")] * 4,
        [(weight_other, "H"), (half[2], "V"), (half[0], "H"), (half[1], "H")],
        1000,
        [pltpu.VMEM((8, 8, 8, 2432), BF), DMA((8,))] + scratch,
        aliases={2: 0, 3: 1},
    )
    ff_parts = [after(value, pin(vectors[0])) for value in ff_parts]
    ff_swapped = [swap(value) for value in (ff_part, *ff_parts)]
    up_grad, down_grad = call(
        spread_ff_kernel,
        [((D, FFL), F32, "H"), ((FFL, D), F32, "H")],
        [(ff_part, "L"), *[(value, "V") for value in ff_parts], *[(value, "V") for value in ff_swapped]],
        1000,
        [pltpu.VMEM((4, 2, 96, FFL), F32), pltpu.VMEM((4, 2, 48, D), F32), DMA((4, 2)), DMA((4, 2))],
    )
    input_grad, result = call(
        unpack_kernel, [((2, TOK, D), F32, "L"), ((2, TOK, D), BF, "L")], [(everyone, "V"), (vectors[0], "H"), (up_grad, "H")], 1000
    )
    return (
        result, input_grad, qkv_grad, out_proj_grad, *vectors, up_grad, down_grad
    )


def solution(mesh):
    names = ("y", "xl", "c", "zh", "zl", "xh")
    fine = Mesh(mesh.devices.reshape(4, 2, 2, 2, 2, 2), names)
    tokens = P(None, WIDE, None)
    placed = (
        tokens, P(), P(), P(), P(), P(), P(), P(), P(None, NARROW), P(NARROW, None), tokens
    )
    return jax.shard_map(
        shards,
        mesh=fine,
        in_specs=placed,
        out_specs=(
            tokens, tokens, P(), P(), P(), P(), P(), P(), P(None, NARROW), P(NARROW, None)
        ),
        check_vma=False,
    )
```

```python
import functools

import jax
import jax.numpy as jnp
from jax import lax
from jax.experimental import pallas as pl
from jax.experimental.pallas import tpu as pltpu
from jax.sharding import Mesh
from jax.sharding import PartitionSpec as P

D = 768
HD = 64
FFL = 384
TOK = 128
BLK = 32
EPS = 1e-05
BF = jnp.bfloat16
F32 = jnp.float32

CHIP = ("y", "xl")
CORE = "c"
MICRO = "zh"
GROUP = ("zl", "xh")
NARROW = (MICRO, *GROUP)
WIDE = (*CHIP, CORE)


def chip_index():
    return lax.axis_index("y") * 2 + lax.axis_index("xl")


def group_index():
    return lax.axis_index("zl") * 2 + lax.axis_index("xh")


def mm(left, right):
    return lax.dot_general(left, right, (((1,), (0,)), ((), ())), preferred_element_type=F32)


def mm_nt(left, right):
    return lax.dot_general(left, right, (((1,), (1,)), ((), ())), preferred_element_type=F32)


def mm_tn(left, right):
    return lax.dot_general(left, right, (((0,), (0,)), ((), ())), preferred_element_type=F32)


def normalized(values):
    center = values - jnp.mean(values, axis=-1, keepdims=True)
    spread = jnp.mean(center * center, axis=-1, keepdims=True)
    inverse = lax.rsqrt(spread + EPS)
    return center * inverse, inverse


def norm_back(grad, unit, inverse, gain):
    scaled = grad * gain
    first = jnp.mean(scaled, axis=-1, keepdims=True)
    second = jnp.mean(scaled * unit, axis=-1, keepdims=True)
    return inverse * (scaled - first - unit * second)


def halves(block):
    lane = lax.broadcasted_iota(jnp.int32, block.shape, 1)
    zero = jnp.zeros_like(block)
    return jnp.where(lane < HD, block, zero), jnp.where(lane < HD, zero, block)


def join(low, high):
    lane = lax.broadcasted_iota(jnp.int32, low.shape, 1)
    return jnp.where(lane < HD, low, high)


def span(scene_ref):
    micro = lax.axis_index(MICRO)
    own = scene_ref[micro, chip_index() * 4]
    first = jnp.int32(0)
    count = jnp.int32(0)
    for index in range(8):
        other = scene_ref[micro, index * 4]
        first += (other < own).astype(jnp.int32)
        count += (other == own).astype(jnp.int32)
    return first, count > 1


def three(value):
    a = value.astype(BF).astype(F32)
    b = (value - a).astype(BF).astype(F32)
    c = value - a - b
    return a, b, c


def put_columns(width, rows, start, columns):
    lane = lax.broadcasted_iota(jnp.int32, (rows, width), 1)
    out = jnp.zeros((rows, width), F32)
    for offset, column in enumerate(columns):
        out = jnp.where(lane == start + offset, column, out)
    return out


def pin(value):
    return pltpu.with_memory_space_constraint(value, pltpu.HBM)


def call(kernel, outs, ins, cost, scratch=(), vmem=16, aliases=None):
    places = {"V": pltpu.VMEM, "H": pltpu.HBM, "S": pltpu.SMEM, "L": pltpu.VMEM, "A": pl.ANY}
    return pl.pallas_call(
        kernel,
        out_shape=[
            (pltpu.HBM if place in "HL" else jax.ShapeDtypeStruct)(shape, dtype) for shape, dtype, place in outs
        ],
        in_specs=[pl.BlockSpec(memory_space=places[place]) for _, place in ins],
        out_specs=[pl.BlockSpec(memory_space=places[place]) for _, _, place in outs],
        scratch_shapes=list(scratch),
        input_output_aliases=aliases or {},
        cost_estimate=pl.CostEstimate(flops=cost, bytes_accessed=1000, transcendentals=0),
        compiler_params=pltpu.CompilerParams(vmem_limit_bytes=vmem * 2**20),
    )(*[pin(value) if place in "HL" else value for value, place in ins])


DMA = pltpu.SemaphoreType.DMA


def send_copies(source, target, indices, sem):
    copies = [pltpu.make_async_copy(source, target.at[index], sem.at[index]) for index in indices]
    for copy in copies:
        copy.start()
    return copies


def wait_all(copies):
    for copy in copies:
        copy.wait()


def weight_copies(w_ref, w_buf, w_sem, parts=(1, 2, 0), start=True):
    group = group_index()
    copies = []
    for slot, part in enumerate(parts):
        column = pl.multiple_of(part * D + (group // 2) * 384, 128)
        copy = pltpu.make_async_copy(w_ref.at[:, pl.ds(column, 384)], w_buf.at[slot], w_sem.at[slot])
        if start:
            copy.start()
        copies.append(copy)
    return copies


def own_heads(full):
    odd = (group_index() % 2) == 1
    return jnp.where(odd, full[:, 192:], full[:, :192]).astype(BF)


def project_kernel(
    tok_ref, gain_ref, shift_ref, w_ref, kv_ref, normed_ref,
    x_buf, w_buf, kv_buf, gain_buf, shift_buf, x_sem, w_sem, kv_sem, gain_sem, shift_sem,
):
    copy_x = pltpu.make_async_copy(tok_ref.at[lax.axis_index(MICRO)], x_buf, x_sem)
    copy_x.start()
    copy_gain = pltpu.make_async_copy(gain_ref, gain_buf, gain_sem)
    copy_gain.start()
    copy_shift = pltpu.make_async_copy(shift_ref, shift_buf, shift_sem)
    copy_shift.start()
    copies = weight_copies(w_ref, w_buf, w_sem, (1, 2))
    wait_all([copy_x, copy_gain, copy_shift])
    unit, _ = normalized(x_buf[...].astype(F32))
    normed = (unit * gain_buf[...].reshape(1, D) + shift_buf[...].reshape(1, D)).astype(BF)
    normed_ref[...] = normed
    parts = []
    for slot in range(2):
        copies[slot].wait()
        parts.append(own_heads(mm(normed, w_buf[slot])))
    kv_buf[...] = jnp.concatenate(parts, axis=1)
    wait_all(send_copies(kv_buf, kv_ref, range(8), kv_sem))


def query_kernel(normed_ref, w_ref, q_ref, w_buf, w_sem):
    weight_copies(w_ref, w_buf, w_sem, (0,))[0].wait()
    part = own_heads(mm(normed_ref[...], w_buf[0]))
    q_ref[...] = jnp.concatenate([part, jnp.zeros((TOK, HD), BF)], axis=1)


def block_query_kernel(normed_ref, w_ref, out_ref, x_buf, w_buf, x_sem, w_sem):
    block = pl.ds(pl.multiple_of(group_index() * BLK, BLK), BLK)
    loads = [
        pltpu.make_async_copy(normed_ref.at[block], x_buf, x_sem),
        pltpu.make_async_copy(w_ref.at[:, pl.ds(0, D)], w_buf, w_sem),
    ]
    for load in loads:
        load.start()
    wait_all(loads)
    query = mm(x_buf[...], w_buf[...]).astype(BF)
    zero = jnp.zeros((BLK, HD), BF)
    for group in range(4):
        out_ref[group] = jnp.concatenate([query[:, group * 192:(group + 1) * 192], zero], axis=1)


def attend_kernel(scene_ref, q_ref, same_ref, other_ref, out_ref, buf, q_buf, sem, q_sem):
    load = pltpu.make_async_copy(q_ref, q_buf, q_sem)
    load.start()
    first, big = span(scene_ref)

    def run(count):
        rows = count * TOK
        keys = jnp.concatenate(
            [ref[pl.ds(first, count)].reshape(rows, 384) for ref in (same_ref, other_ref)], axis=0
        )
        load.wait()
        query = q_buf[...]
        q0, q1 = halves(query[:, :128])
        blocks = [keys[:, :128], keys[:, 128:256], keys[:, 256:]]
        mixed = []
        columns = []
        for qh, kb, vb in ((q0, 0, 1), (q1, 0, 2), (query[:, 128:], 1, 2)):
            scores = mm_nt(qh, blocks[kb]) * (HD**-0.5)
            top = jnp.max(scores, axis=-1, keepdims=True)
            weights = jnp.exp(scores - top)
            total = jnp.sum(weights, axis=-1, keepdims=True)
            probs = (weights * (1.0 / total)).astype(BF)
            mixed.append(mm(probs, blocks[vb]))
            columns += three(top + jnp.log(total))
        stats = put_columns(128, TOK, 0, columns)
        buf[...] = jnp.concatenate([join(stats, mixed[0]), join(mixed[1], mixed[2])], axis=1).astype(BF)

    @pl.when(big)
    def _():
        run(5)

    @pl.when(jnp.logical_not(big))
    def _():
        run(1)

    wait_all(send_copies(buf, out_ref, range(8), sem))


def forward_kernel(
    mixed_ref, tok_ref, og_ref, wo_ref, gain_ref, shift_ref, up_ref, down_ref,
    out_ref, middle_ref, normed_ref, act_ref, gpre_ref,
    tok_buf, og_buf, up_buf, down_buf, gain_buf, shift_buf, grad_buf, branch_buf, middle_buf, in_sem, sem,
):
    loads = [
        pltpu.make_async_copy(ref, buf, in_sem.at[index])
        for index, (ref, buf) in enumerate(
            (
                (tok_ref, tok_buf), (up_ref, up_buf), (og_ref, og_buf), (down_ref, down_buf), (gain_ref, gain_buf),
                (shift_ref, shift_buf),
            )
        )
    ]
    for load in loads:
        load.start()
    total = jnp.zeros((2 * TOK, D), F32)
    for group in range(4):
        rows = jnp.concatenate([mixed_ref[group], mixed_ref[4 + group]], axis=0)
        total = total + mm(rows, wo_ref[group])
    loads[0].wait()
    total = total + tok_buf[...].reshape(2 * TOK, D).astype(F32)
    middle_buf[...] = total.reshape(8, BLK, D)
    third = pltpu.make_async_copy(
        middle_buf.at[lax.axis_index(MICRO) * 4 + group_index()], middle_ref, sem.at[2]
    )
    third.start()
    unit, _ = normalized(total)
    wait_all(loads[4:])
    normed = (unit * gain_buf[...].reshape(1, D) + shift_buf[...].reshape(1, D)).astype(BF)
    normed_ref[...] = normed
    loads[1].wait()
    pre = mm(normed, up_buf[...])
    cdf = 0.5 * (1.0 + lax.erf(pre * (0.5**0.5)))
    slope = cdf + pre * jnp.exp(-0.5 * pre * pre) * 0.3989422804014327
    loads[2].wait()
    loads[3].wait()
    grad_out = og_buf[...].reshape(2 * TOK, D)
    gpre = (mm_nt(grad_out, down_buf[...]) * slope).astype(BF)
    gpre_ref[...] = gpre
    grad_buf[...] = mm_nt(gpre, up_buf[...]).astype(BF).reshape(8, BLK, D)
    first = pltpu.make_async_copy(grad_buf, out_ref.at[:, pl.ds(BLK, BLK)], sem.at[0])
    first.start()
    act = (pre * cdf).astype(BF)
    act_ref[...] = act
    branch_buf[...] = mm(act, down_buf[...]).astype(BF).reshape(8, BLK, D)
    second = pltpu.make_async_copy(branch_buf, out_ref.at[:, pl.ds(0, BLK)], sem.at[1])
    second.start()
    wait_all([first, second, third])


def ff_grads_kernel(normed_ref, act_ref, gpre_ref, og_ref, keep_ref, send_ref, up_buf, down_buf):
    core = lax.axis_index(CORE)
    up_buf[...] = mm_tn(normed_ref[...], gpre_ref[...])
    down_buf[...] = mm_tn(act_ref[...], og_ref[...].reshape(2 * TOK, D))
    for ref, owner in ((keep_ref, core), (send_ref, 1 - core)):
        column = pl.multiple_of(owner * 384, 128)
        for tile in range(8):
            rows = pl.ds(pl.multiple_of((2 * tile + owner) * 48, 16), 48)
            ref[tile, :, :384] = up_buf[rows].astype(BF)
            ref[tile, :, 384:] = down_buf[tile * 48:(tile + 1) * 48, pl.ds(column, 384)].astype(BF)


def split_kernel(one_ref, two_ref, *refs):
    y = lax.axis_index("y")
    for k, ref in enumerate(refs):
        for xl in range(2):
            at = (y ^ k) * 2 + xl
            ref[xl] = (one_ref[at].astype(F32) + two_ref[at].astype(F32)).astype(BF)


def total_kernel(*refs):
    total = refs[0][...].astype(F32)
    for ref in refs[1:4]:
        total = total + ref[...].astype(F32)
    refs[4][...] = total.astype(BF)


def middle_kernel(
    sums_ref, middle_ref, og_ref, mixed_ref, wo_ref, gain_ref, query_ref,
    out_ref, low_ref, grad_ref, result_ref, vec_ref,
    buf, middle_buf, og_buf, mixed_buf, gain_buf, query_buf, low_buf, grad_buf, result_buf, vec_buf, in_sem, sem, rest_sem,
):
    micro = lax.axis_index(MICRO)
    group = group_index()
    block = pl.ds(pl.multiple_of(group * BLK, BLK), BLK)
    loads = [
        pltpu.make_async_copy(middle_ref, middle_buf, in_sem.at[0]),
        pltpu.make_async_copy(og_ref.at[micro, block], og_buf, in_sem.at[1]),
        pltpu.make_async_copy(mixed_ref.at[pl.ds(micro * 4, 4), block], mixed_buf, in_sem.at[2]),
        pltpu.make_async_copy(gain_ref, gain_buf, in_sem.at[3]),
        pltpu.make_async_copy(query_ref, query_buf, in_sem.at[4]),
    ]
    for load in loads:
        load.start()
    total = sums_ref[0].astype(F32)
    for index in range(1, 8):
        total = total + sums_ref[index].astype(F32)
    branch, grad = total[:BLK], total[BLK:]
    wait_all(loads)
    middle = middle_buf[...]
    unit, inverse = normalized(middle)
    grad_mid = og_buf[...].astype(F32) + norm_back(grad, unit, inverse, gain_buf[...].reshape(1, D))
    low = grad_mid.astype(BF)
    low_buf[...] = low
    grad_buf[...] = grad_mid
    result_buf[...] = (middle + branch).astype(BF)
    gain_grad = jnp.sum(grad * unit, axis=0, keepdims=True)
    shift_grad = jnp.sum(grad, axis=0, keepdims=True)
    vec_buf[...] = jnp.concatenate([gain_grad, shift_grad, jnp.zeros((6, D), F32)], axis=0)
    stores = [
        pltpu.make_async_copy(source, target, rest_sem.at[index])
        for index, (source, target) in enumerate(
            ((low_buf, low_ref), (grad_buf, grad_ref), (result_buf, result_ref), (vec_buf, vec_ref))
        )
    ]
    for store in stores:
        store.start()
    lane = lax.broadcasted_iota(jnp.int32, (BLK, 256), 1)
    for head_group in range(4):
        mixed = mixed_buf[head_group].astype(F32)
        back = mm_nt(low, wo_ref[head_group]).astype(BF).astype(F32)
        product = mixed * back
        columns = []
        for head in range(3):
            inside = (lane >= (head + 1) * HD) & (lane < (head + 2) * HD)
            columns += three(jnp.sum(jnp.where(inside, product, 0.0), axis=-1, keepdims=True))
        stats = put_columns(256, BLK, 9, columns)
        buf[head_group, :, :256] = jnp.where(lane < 9, mixed, jnp.where(lane < HD, stats, back)).astype(BF)
        buf[head_group, :, 256:] = query_buf[head_group]
    sends = send_copies(buf, out_ref, range(8), sem)
    wait_all(stores)
    wait_all(sends)


def attend_back_kernel(
    scene_ref, kvs_ref, kvo_ref, gs_ref, go_ref, normed_ref, mixed_ref, low_ref, low1_ref, low2_ref, low3_ref,
    w_ref, gqkv_ref, w_out_ref, keep_ref, send_ref,
    kv_buf, grad_buf, mixed_buf, normed_buf, low_buf, kv_sem, in_sem, w_sem,
):
    first, big = span(scene_ref)
    chip = chip_index()
    core = lax.axis_index(CORE)
    group = group_index()
    index = lax.axis_index(MICRO) * 4 + group
    first_loads = [
        pltpu.make_async_copy(source, target, in_sem.at[slot])
        for slot, (source, target) in enumerate(
            ((normed_ref, normed_buf), (mixed_ref.at[index], mixed_buf), (low_ref, low_buf))
        )
    ]
    scale = HD**-0.5

    def run(count):
        rows = count * TOK
        loads = [pltpu.make_async_copy(kvs_ref.at[pl.ds(first, count)], kv_buf.at[pl.ds(0, count)], kv_sem)]
        for load in loads + first_loads:
            load.start()
        weight_copies(w_ref, w_out_ref, w_sem)

        def cut(value):
            return [value[:, at:at + 128] for at in range(0, value.shape[1], 128)]

        every = cut(jnp.concatenate(
            [ref[pl.ds(first, count)].reshape(rows, 512) for ref in (gs_ref, go_ref)], axis=0
        ))
        grad, query = every[:2], every[2:]
        g_own = cut(gs_ref[chip])
        g_heads = [halves(g_own[0])[1], *halves(g_own[1])]
        own_stats = g_own[0].astype(F32)
        all_stats = grad[0].astype(F32).T
        wait_all(loads)
        kv = cut(jnp.concatenate(
            [kv_buf[:count].reshape(rows, 384), kvo_ref[pl.ds(first, count)].reshape(rows, 384)], axis=0
        ))
        own = cut(kv_buf[chip - first]) + g_own[2:]
        q_heads = [*halves(own[3]), own[4]]
        k_heads = [*halves(own[0]), halves(own[1])[0]]
        v_heads = [halves(own[1])[1], *halves(own[2])]

        def column(at):
            return own_stats[:, at:at + 1] + own_stats[:, at + 1:at + 2] + own_stats[:, at + 2:at + 3]

        def row(at):
            return all_stats[at:at + 1] + all_stats[at + 1:at + 2] + all_stats[at + 2:at + 3]

        dq, dk, dv = [], [], []
        for head, (kb, vb) in enumerate(((0, 1), (0, 2), (1, 2))):
            qb, gb = (0, 0, 1)[head], (0, 1, 1)[head]
            probs = jnp.exp(mm_nt(q_heads[head], kv[kb]) * scale - column(3 * head))
            gap = mm_nt(g_heads[head], kv[vb]) - column(9 + 3 * head)
            dq.append(mm((probs * gap).astype(BF), kv[kb]) * scale)
            probs = jnp.exp(mm_nt(k_heads[head], query[qb]) * scale - row(3 * head))
            gap = mm_nt(v_heads[head], grad[gb]) - row(9 + 3 * head)
            dv.append(mm(probs.astype(BF), grad[gb]))
            dk.append(mm((probs * gap).astype(BF), query[qb]) * scale)
        tail = dq[2]
        gqkv_ref[...] = jnp.concatenate(
            [join(dk[0], dk[1]), join(dk[2], dv[0]), join(dv[1], dv[2]), join(dq[0], dq[1]),
             join(tail, jnp.zeros_like(tail))],
            axis=1,
        ).astype(BF)


    @pl.when(big)
    def _():
        run(5)

    @pl.when(jnp.logical_not(big))
    def _():
        run(1)

    wait_all(first_loads)

    grad_buf[...] = mm_tn(normed_buf[...], gqkv_ref[...])
    low = jnp.concatenate([ref[...] for ref in (low_buf, low1_ref, low2_ref, low3_ref)], axis=0)
    mixed = jnp.concatenate(
        [mixed_buf[pl.ds(pl.multiple_of((group ^ k) * BLK, BLK), BLK)] for k in range(4)], axis=0
    )
    out = mm_tn(mixed, low)[HD:]
    for ref, owner in ((keep_ref, core), (send_ref, 1 - core)):
        for tile in range(8):
            rows = grad_buf[pl.ds(pl.multiple_of((2 * tile + owner) * 48, 16), 48)]
            at = (tile // 4) * 96
            pieces = [
                out[at + row * 48:at + (row + 1) * 48, (tile % 4) * 192:(tile % 4 + 1) * 192] for row in range(2)
            ]
            ref[2 * tile] = rows[:, :384].astype(BF)
            ref[2 * tile + 1] = jnp.concatenate(
                [rows[:, 384:576], jnp.where(owner == 1, pieces[1], pieces[0])], axis=1
            ).astype(BF)
    wait_all(weight_copies(w_ref, w_out_ref, w_sem, start=False))


def normed_grad_kernel(
    gqkv_ref, w_ref, tok_ref, vec_ref, near_ref, far_ref, own_ref, one_ref, two_ref, three_ref, sums_ref, ff_ref,
    x_buf, vec_buf, near_buf, part_buf, low_buf, sums_buf, ff_buf, rows_buf, in_sem, out_sem, row_sem,
):
    loads = [
        pltpu.make_async_copy(tok_ref.at[lax.axis_index(MICRO)], x_buf, in_sem.at[0]),
        pltpu.make_async_copy(vec_ref, vec_buf, in_sem.at[1]),
        pltpu.make_async_copy(near_ref, near_buf, in_sem.at[2]),
    ]
    for load in loads:
        load.start()
    group = group_index()
    odd = (group % 2) == 1
    total = jnp.zeros((TOK, D), F32)
    for slot in range(3):
        part = gqkv_ref[:, slot * 192:(slot + 1) * 192]
        zero = jnp.zeros_like(part)
        wide = jnp.where(
            odd, jnp.concatenate([zero, part], axis=1), jnp.concatenate([part, zero], axis=1)
        )
        total = total + mm_nt(wide, w_ref[slot])
    part_buf[...] = total
    low_buf[...] = total.astype(BF)
    stores = []
    for k, ref in enumerate((own_ref, one_ref, two_ref, three_ref)):
        rows = pl.ds(pl.multiple_of((group ^ k) * BLK, BLK), BLK)
        target = ref.at[pl.ds(0, BLK)] if k else ref
        stores.append(pltpu.make_async_copy((low_buf if k else part_buf).at[rows], target, out_sem.at[k]))
        stores[-1].start()
    wait_all(loads)
    ff_buf[...] = (near_buf[...].astype(F32) + far_ref[...].astype(F32)).astype(BF)
    stores.append(pltpu.make_async_copy(ff_buf, ff_ref, out_sem.at[5]))
    stores[-1].start()
    unit, _ = normalized(x_buf[...].astype(F32))
    gain1 = jnp.sum(total * unit, axis=0, keepdims=True)
    shift1 = jnp.sum(total, axis=0, keepdims=True)
    vectors = jnp.concatenate([gain1, shift1, vec_buf[...][:2], jnp.zeros((4, D), F32)], axis=0)
    sums_buf[...] = vectors
    for index in range(4):
        rows_buf[index] = jnp.concatenate(
            [vectors[index:index + 1], jnp.zeros((15, D), F32)], axis=0
        ).astype(BF)
    for k, ref in enumerate((one_ref, two_ref, three_ref)):
        stores.append(
            pltpu.make_async_copy(rows_buf.at[group ^ (k + 1)], ref.at[pl.ds(BLK, 16)], row_sem.at[k])
        )
        stores[-1].start()
    stores.append(pltpu.make_async_copy(sums_buf, sums_ref, out_sem.at[4]))
    stores[-1].start()
    wait_all(stores)


def add_kernel(one_ref, two_ref, unused_ref, out_ref, buf, sem):
    buf[...] = (one_ref[...].astype(F32) + two_ref[...].astype(F32)).astype(BF)
    copy = pltpu.make_async_copy(buf, out_ref, sem)
    copy.start()
    copy.wait()


def sum_kernel(in_ref, vec_ref, one_ref, two_ref, three_ref, out_ref, buf, vec_buf, row_buf, sem, vec_sem, row_sem):
    loads = [pltpu.make_async_copy(vec_ref, vec_buf, vec_sem)] + [
        pltpu.make_async_copy(ref.at[pl.ds(BLK, 16)], row_buf.at[k], row_sem.at[k])
        for k, ref in enumerate((one_ref, two_ref, three_ref))
    ]
    for load in loads:
        load.start()
    total = in_ref[0].astype(F32)
    for index in range(1, 16):
        total = total + in_ref[index].astype(F32)
    wait_all(loads)
    vector = vec_buf[pl.ds(group_index(), 1)]
    for k in range(3):
        vector = vector + row_buf[k].astype(F32)[:1]
    rows = [vector[:, at:at + 128] for at in range(0, D, 128)] + [jnp.zeros((2, 128), F32)]
    pieces = [total[at:at + 8] for at in range(0, 48, 8)] + [jnp.concatenate(rows, axis=0)]
    block = jnp.concatenate(pieces, axis=1).astype(BF)
    for index in range(8):
        buf[index] = block
    wait_all(send_copies(buf, out_ref, range(8), sem))


def spread_kernel(turn, in_ref, *refs):
    qkv_buf, out_buf, sem, out_sem = refs[-4:]
    if turn:
        in_buf, in_sem = refs[-6:-4]
        qkv_ref, out_ref, *vec_refs = refs[3:-6]
        loads = [pltpu.make_async_copy(in_ref.at[tile], in_buf.at[tile], in_sem.at[tile]) for tile in range(8)]
        for load in loads:
            load.start()
    else:
        qkv_ref, out_ref, *vec_refs = refs[:-4]
        in_buf = in_ref
    owner = lax.axis_index(CORE)
    owner = 1 - owner if turn else owner
    copies = []
    vectors = [jnp.zeros((8, 128), F32)] * 4
    for tile in range(8):
        if turn:
            loads[tile].wait()
        whole = [in_buf[tile, index].astype(F32) for index in range(8)]
        block = [
            jnp.concatenate([value[:, at:at + 384] for at in range(0, 2304, 384)], axis=0) for value in whole
        ]
        vectors = [total + whole[k][:, 2304:] + whole[4 + k][:, 2304:] for k, total in enumerate(vectors)]
        for part, half, at in ((1, 0, 0), (2, 0, 192), (0, 4, 0)):
            qkv_buf[tile, :, part * D:(part + 1) * D] = jnp.concatenate(
                [block[half + group][:, at:at + 192] for group in range(4)], axis=1
            )
        start = pl.multiple_of((2 * tile + owner) * 48, 16)
        copy = pltpu.make_async_copy(qkv_buf.at[tile], qkv_ref.at[pl.ds(start, 48)], sem.at[tile])
        copy.start()
        copies.append(copy)
        for group in range(4):
            out_buf[group, tile // 4, :, (tile % 4) * 192:(tile % 4 + 1) * 192] = block[4 + group][:, 192:]
    for group in range(4):
        for pair in range(2):
            start = pl.multiple_of(group * 192 + (pair * 2 + owner) * 48, 16)
            copy = pltpu.make_async_copy(
                out_buf.at[group, pair], out_ref.at[pl.ds(start, 48)], out_sem.at[group, pair]
            )
            copy.start()
            copies.append(copy)
    if turn:
        for k, ref in enumerate(vec_refs):
            total = vectors[k] + refs[0][k]
            ref[...] = jnp.concatenate([total[row:row + 1] for row in range(6)], axis=1).reshape(D)
    else:
        for k, total in enumerate(vectors):
            vec_refs[0][k] = total
    wait_all(copies)


def spread_ff_kernel(turn, *refs):
    up_ref, down_ref, up_buf, down_buf, up_sem, down_sem = refs[-6:]
    y, core = lax.axis_index("y"), lax.axis_index(CORE)
    owner = 1 - core if turn else core
    copies = []
    for near in range(4):
        for xl in range(2):
            chip = (y ^ near) * 2 + xl
            block = refs[near][xl].astype(F32)
            up_buf[near, xl] = block[:, :384]
            down_buf[near, xl] = block[:, 384:]
            up_rows = pl.ds(pl.multiple_of((chip * 2 + owner) * 48, 16), 48)
            down_rows = pl.ds(pl.multiple_of(chip * 48, 16), 48)
            columns = pl.ds(pl.multiple_of(owner * 384, 128), 384)
            copies.append(pltpu.make_async_copy(up_buf.at[near, xl], up_ref.at[up_rows], up_sem.at[near, xl]))
            copies.append(
                pltpu.make_async_copy(down_buf.at[near, xl], down_ref.at[down_rows, columns], down_sem.at[near, xl])
            )
            copies[-2].start()
            copies[-1].start()
    wait_all(copies)


def input_kernel(
    own_ref, one_ref, two_ref, three_ref, tok_ref, gain_ref, grad_ref, result_ref, unused_ref, out_ref, buf, x_buf, sem, x_sem
):
    start = pl.multiple_of(group_index() * BLK, BLK)
    load = pltpu.make_async_copy(tok_ref.at[lax.axis_index(MICRO), pl.ds(start, BLK)], x_buf, x_sem)
    load.start()
    load.wait()
    total = own_ref[...]
    for ref in (one_ref, two_ref, three_ref):
        total = total + ref[:BLK].astype(F32)
    unit, inverse = normalized(x_buf[...].astype(F32))
    grad = grad_ref[...] + norm_back(total, unit, inverse, gain_ref[...].reshape(1, D))
    buf[:BLK] = grad.astype(BF)
    buf[BLK:] = result_ref[...]
    wait_all(send_copies(buf, out_ref, range(8), sem))


def unpack_kernel(in_ref, unused_ref, other_ref, grad_ref, result_ref):
    for index in range(8):
        rows = slice(index % 4 * BLK, (index % 4 + 1) * BLK)
        grad_ref[index // 4, rows] = in_ref[index, :BLK].astype(F32)
        result_ref[index // 4, rows] = in_ref[index, BLK:]


def exchange(value, axes):
    return lax.all_to_all(value, axes, 0, 0, tiled=True)


def swap(value):
    return lax.ppermute(value, CORE, [(0, 1), (1, 0)])


def after(value, *others):
    return pl.pallas_call(
        lambda *refs: None,
        out_shape=jax.ShapeDtypeStruct(value.shape, value.dtype),
        in_specs=[pl.BlockSpec(memory_space=pl.ANY)] * (1 + len(others)),
        out_specs=pl.BlockSpec(memory_space=pl.ANY),
        input_output_aliases={0: 0},
        cost_estimate=pl.CostEstimate(flops=1, bytes_accessed=1, transcendentals=0),
        compiler_params=pltpu.CompilerParams(vmem_limit_bytes=2**20),
    )(value, *others)


def flip(value, axes, count, bits):
    return lax.ppermute(value, axes, [(index, index ^ bits) for index in range(count)])


def shards(
    tokens, scene_of_block, ln1_gain, ln1_shift, w_qkv, w_out, ln2_gain, ln2_shift, w_up, w_down, out_grad
):
    w_out_pad = jnp.pad(w_out.reshape(4, 192, D), ((0, 0), (HD, 0), (0, 0)))
    kv_send, normed = call(
        project_kernel,
        [((8, TOK, 384), BF, "H"), ((TOK, D), BF, "L")],
        [(tokens, "H"), (ln1_gain, "H"), (ln1_shift, "H"), (w_qkv, "H")],
        1000,
        [
            pltpu.VMEM((TOK, D), BF), pltpu.VMEM((2, D, 384), BF), pltpu.VMEM((TOK, 384), BF),
            pltpu.VMEM((D,), F32), pltpu.VMEM((D,), F32), DMA, DMA((2,)), DMA((8,)), DMA, DMA,
        ],
    )
    (query,) = call(
        query_kernel,
        [((TOK, 256), BF, "L")],
        [(normed, "L"), (w_qkv, "H")],
        1000,
        [pltpu.VMEM((1, D, 384), BF), DMA((1,))],
    )
    kv_same = exchange(kv_send, CHIP)
    kv_same = after(kv_same, pin(query))
    kv_other = swap(kv_same)
    (mixed_send,) = call(
        attend_kernel,
        [((8, TOK, 256), BF, "H")],
        [(scene_of_block, "S"), (query, "H"), (kv_same, "V"), (kv_other, "V")],
        1000,
        [pltpu.VMEM((TOK, 256), BF), pltpu.VMEM((TOK, 256), BF), DMA((8,)), DMA],
    )
    mixed = exchange(mixed_send, NARROW)
    (block_query,) = call(
        block_query_kernel,
        [((4, BLK, 256), BF, "L")],
        [(normed, "H"), (w_qkv, "H")],
        1000,
        [pltpu.VMEM((BLK, D), BF), pltpu.VMEM((D, D), BF), DMA, DMA],
    )
    ff_send, middle, normed2, act, grad_pre = call(
        forward_kernel,
        [
            ((8, 2 * BLK, D), BF, "H"), ((BLK, D), F32, "H"), ((2 * TOK, D), BF, "V"),
            ((2 * TOK, FFL), BF, "V"), ((2 * TOK, FFL), BF, "V"),
        ],
        [
            (mixed, "V"), (tokens, "H"), (out_grad, "H"), (w_out_pad, "V"), (ln2_gain, "H"), (ln2_shift, "H"),
            (w_up, "H"), (w_down, "H"),
        ],
        1000,
        [
            pltpu.VMEM((2, TOK, D), BF), pltpu.VMEM((2, TOK, D), BF), pltpu.VMEM((D, FFL), BF),
            pltpu.VMEM((FFL, D), BF), pltpu.VMEM((D,), F32), pltpu.VMEM((D,), F32), pltpu.VMEM((8, BLK, D), BF),
            pltpu.VMEM((8, BLK, D), BF), pltpu.VMEM((8, BLK, D), F32), DMA((6,)), DMA((3,)),
        ],
    )
    ff_sums = exchange(ff_send, NARROW)
    keep, send = call(
        ff_grads_kernel,
        [((8, 48, D), BF, "V")] * 2,
        [(normed2, "V"), (act, "V"), (grad_pre, "V"), (out_grad, "L")],
        1000,
        [pltpu.VMEM((D, FFL), F32), pltpu.VMEM((FFL, D), F32)],
    )
    pieces = call(
        split_kernel, [((2, 48, D), BF, "L")] * 4, [(keep, "V"), (swap(send), "V")], 1000
    )
    pieces = [pieces[0]] + [flip(pieces[k], "y", 4, k) for k in (1, 2, 3)]
    (ff_near,) = call(
        total_kernel,
        [((2, 48, D), BF, "L")],
        [(pieces[0], "L")] + [(piece, "V") for piece in pieces[1:]],
        1000,
    )
    grad_send, low, grad_mid, result_part, vec2 = call(
        middle_kernel,
        [
            ((8, 4, BLK, 512), BF, "H"), ((BLK, D), BF, "H"), ((BLK, D), F32, "H"), ((BLK, D), BF, "H"),
            ((8, D), F32, "H"),
        ],
        [
            (ff_sums, "V"), (middle, "H"), (out_grad, "H"), (mixed, "H"), (w_out_pad, "V"), (ln2_gain, "H"),
            (block_query, "H"),
        ],
        1000,
        [
            pltpu.VMEM((4, BLK, 512), BF), pltpu.VMEM((BLK, D), F32), pltpu.VMEM((BLK, D), BF),
            pltpu.VMEM((4, BLK, 256), BF), pltpu.VMEM((D,), F32), pltpu.VMEM((4, BLK, 256), BF), pltpu.VMEM((BLK, D), BF), pltpu.VMEM((BLK, D), F32),
            pltpu.VMEM((BLK, D), BF), pltpu.VMEM((8, D), F32), DMA((5,)), DMA((8,)), DMA((4,)),
        ],
    )
    grad_send = after(pin(grad_send), *pieces[1:])
    grad_same = exchange(grad_send.reshape(32, BLK, 512), (*CHIP, *GROUP)).reshape(8, TOK, 512)
    lows = [flip(low, GROUP, 4, k) for k in (1, 2, 3)]
    kv_same = after(pin(kv_same), low)
    kv_other = swap(kv_same)
    grad_same = after(grad_same, *lows, kv_other, pin(ff_near))
    grad_other = swap(grad_same)
    ff_near = after(pin(ff_near), grad_other)
    ff_far = flip(ff_near, "xl", 2, 1)
    gqkv, w_own, keep, send = call(
        attend_back_kernel,
        [((TOK, 640), BF, "V"), ((3, D, 384), BF, "V")] + [((16, 48, 384), BF, "V")] * 2,
        [
            (scene_of_block, "S"), (kv_same, "H"), (kv_other, "V"), (grad_same, "V"), (grad_other, "V"),
            (normed, "H"), (mixed, "H"), (low, "H"), *[(value, "V") for value in lows], (w_qkv, "H"),
        ],
        1000,
        [
            pltpu.VMEM((5, TOK, 384), BF), pltpu.VMEM((D, 640), F32),
            pltpu.VMEM((TOK, 256), BF), pltpu.VMEM((TOK, D), BF), pltpu.VMEM((BLK, D), BF),
            DMA, DMA((3,)), DMA((3,)),
        ],
        vmem=24,
    )
    own, *sends, sums, ff_part = call(
        normed_grad_kernel,
        [((BLK, D), F32, "H")] + [((BLK + 16, D), BF, "H")] * 3 + [((8, D), F32, "H"), ((2, 48, D), BF, "H")],
        [(gqkv, "V"), (w_own, "V"), (tokens, "H"), (vec2, "H"), (ff_near, "H"), (ff_far, "V")],
        1000,
        [
            pltpu.VMEM((TOK, D), BF), pltpu.VMEM((8, D), F32), pltpu.VMEM((2, 48, D), BF), pltpu.VMEM((TOK, D), F32),
            pltpu.VMEM((TOK, D), BF), pltpu.VMEM((8, D), F32), pltpu.VMEM((2, 48, D), BF), pltpu.VMEM((4, 16, D), BF),
            DMA((3,)), DMA((6,)), DMA((3,)),
        ],
    )
    (weight_send,) = call(
        add_kernel,
        [((16, 48, 384), BF, "H")],
        [(keep, "V"), (swap(after(send, ff_far)), "V"), (own, "H")],
        1000,
        [pltpu.VMEM((16, 48, 384), BF), DMA],
    )
    weight_parts = exchange(weight_send, (*CHIP, MICRO))
    parts = [flip(value, GROUP, 4, k + 1) for k, value in enumerate(sends)]
    weight_parts = after(weight_parts, pin(sums), *parts)
    ff_parts = [flip(ff_part, "y", 4, k) for k in (1, 2, 3)]
    (weight_total,) = call(
        sum_kernel,
        [((8, 8, 8, 2432), BF, "H")],
        [(weight_parts, "V"), (sums, "H"), *[(value, "A") for value in parts]],
        1000,
        [
            pltpu.VMEM((8, 8, 2432), BF), pltpu.VMEM((8, D), F32), pltpu.VMEM((3, 16, D), BF), DMA((8,)), DMA,
            DMA((3,)),
        ],
    )
    (packed,) = call(
        input_kernel,
        [((8, 2 * BLK, D), BF, "H")],
        [
            (own, "L"), *[(value, "V") for value in parts], (tokens, "H"), (ln1_gain, "L"), (grad_mid, "L"),
            (result_part, "L"), (weight_total, "H"),
        ],
        1000,
        [pltpu.VMEM((2 * BLK, D), BF), pltpu.VMEM((BLK, D), BF), DMA((8,)), DMA],
    )
    weight_same = exchange(weight_total.reshape(64, 8, 2432), (*CHIP, *NARROW)).reshape(8, 8, 8, 2432)
    weight_same = after(weight_same, pin(packed))
    everyone = exchange(after(pin(packed), weight_same), NARROW)
    weight_other = swap(weight_same)
    scratch = [
        pltpu.VMEM((8, 48, 3 * D), F32), pltpu.VMEM((4, 2, 48, D), F32), DMA((8,)), DMA((4, 2)),
    ]
    grads = [((D, 3 * D), F32, "H"), ((D, D), F32, "H")]
    half = call(
        functools.partial(spread_kernel, False),
        grads + [((4, 8, 128), F32, "V")],
        [(weight_same, "V")],
        1000,
        scratch,
    )
    qkv_grad, out_proj_grad, *vectors = call(
        functools.partial(spread_kernel, True),
        grads + [((D,), F32, "L")] * 4,
        [(weight_other, "H"), (half[2], "V"), (half[0], "H"), (half[1], "H")],
        1000,
        [pltpu.VMEM((8, 8, 8, 2432), BF), DMA((8,))] + scratch,
        aliases={2: 0, 3: 1},
    )
    ff_parts = [after(value, pin(vectors[0])) for value in ff_parts]
    ff_swapped = [swap(value) for value in (ff_part, *ff_parts)]
    ff_grads = [((D, FFL), F32, "H"), ((FFL, D), F32, "H")]
    ff_scratch = [
        pltpu.VMEM((4, 2, 48, FFL), F32), pltpu.VMEM((4, 2, 48, FFL), F32), DMA((4, 2)), DMA((4, 2)),
    ]
    ff_half = call(
        functools.partial(spread_ff_kernel, False),
        ff_grads,
        [(ff_part, "L"), *[(value, "V") for value in ff_parts]],
        1000,
        ff_scratch,
    )
    up_grad, down_grad = call(
        functools.partial(spread_ff_kernel, True),
        ff_grads,
        [*[(value, "V") for value in ff_swapped], (ff_half[0], "H"), (ff_half[1], "H")],
        1000,
        ff_scratch,
        aliases={4: 0, 5: 1},
    )
    input_grad, result = call(
        unpack_kernel, [((2, TOK, D), F32, "L"), ((2, TOK, D), BF, "L")], [(everyone, "V"), (vectors[0], "H"), (up_grad, "H")], 1000
    )
    return (
        result, input_grad, qkv_grad, out_proj_grad, *vectors, up_grad, down_grad
    )


def solution(mesh):
    names = ("y", "xl", "c", "zh", "zl", "xh")
    fine = Mesh(mesh.devices.reshape(4, 2, 2, 2, 2, 2), names)
    tokens = P(None, WIDE, None)
    placed = (
        tokens, P(), P(), P(), P(), P(), P(), P(), P(None, NARROW), P(NARROW, None), tokens
    )
    return jax.shard_map(
        shards,
        mesh=fine,
        in_specs=placed,
        out_specs=(
            tokens, tokens, P(), P(), P(), P(), P(), P(), P(None, NARROW), P(NARROW, None)
        ),
        check_vma=False,
    )
```

```python
import functools

import jax
import jax.numpy as jnp
from jax import lax
from jax.experimental import pallas as pl
from jax.experimental.pallas import tpu as pltpu
from jax.sharding import Mesh
from jax.sharding import PartitionSpec as P

D = 768
HD = 64
FFL = 384
TOK = 128
BLK = 32
EPS = 1e-05
BF = jnp.bfloat16
F32 = jnp.float32

CHIP = ("y", "xl")
CORE = "c"
MICRO = "zh"
GROUP = ("zl", "xh")
NARROW = (MICRO, *GROUP)
WIDE = (*CHIP, CORE)


def chip_index():
    return lax.axis_index("y") * 2 + lax.axis_index("xl")


def group_index():
    return lax.axis_index("zl") * 2 + lax.axis_index("xh")


def mm(left, right):
    return lax.dot_general(left, right, (((1,), (0,)), ((), ())), preferred_element_type=F32)


def mm_nt(left, right):
    return lax.dot_general(left, right, (((1,), (1,)), ((), ())), preferred_element_type=F32)


def mm_tn(left, right):
    return lax.dot_general(left, right, (((0,), (0,)), ((), ())), preferred_element_type=F32)


def normalized(values):
    center = values - jnp.mean(values, axis=-1, keepdims=True)
    spread = jnp.mean(center * center, axis=-1, keepdims=True)
    inverse = lax.rsqrt(spread + EPS)
    return center * inverse, inverse


def norm_back(grad, unit, inverse, gain):
    scaled = grad * gain
    first = jnp.mean(scaled, axis=-1, keepdims=True)
    second = jnp.mean(scaled * unit, axis=-1, keepdims=True)
    return inverse * (scaled - first - unit * second)


def halves(block):
    lane = lax.broadcasted_iota(jnp.int32, block.shape, 1)
    zero = jnp.zeros_like(block)
    return jnp.where(lane < HD, block, zero), jnp.where(lane < HD, zero, block)


def join(low, high):
    lane = lax.broadcasted_iota(jnp.int32, low.shape, 1)
    return jnp.where(lane < HD, low, high)


def span(scene_ref):
    micro = lax.axis_index(MICRO)
    own = scene_ref[micro, chip_index() * 4]
    first = jnp.int32(0)
    count = jnp.int32(0)
    for index in range(8):
        other = scene_ref[micro, index * 4]
        first += (other < own).astype(jnp.int32)
        count += (other == own).astype(jnp.int32)
    return first, count > 1


def three(value):
    a = value.astype(BF).astype(F32)
    b = (value - a).astype(BF).astype(F32)
    c = value - a - b
    return a, b, c


def put_columns(width, rows, start, columns):
    lane = lax.broadcasted_iota(jnp.int32, (rows, width), 1)
    out = jnp.zeros((rows, width), F32)
    for offset, column in enumerate(columns):
        out = jnp.where(lane == start + offset, column, out)
    return out


def pin(value):
    return pltpu.with_memory_space_constraint(value, pltpu.HBM)


def call(kernel, outs, ins, cost, scratch=(), vmem=16, aliases=None):
    places = {"V": pltpu.VMEM, "H": pltpu.HBM, "S": pltpu.SMEM, "L": pltpu.VMEM, "A": pl.ANY}
    return pl.pallas_call(
        kernel,
        out_shape=[
            (pltpu.HBM if place in "HL" else jax.ShapeDtypeStruct)(shape, dtype) for shape, dtype, place in outs
        ],
        in_specs=[pl.BlockSpec(memory_space=places[place]) for _, place in ins],
        out_specs=[pl.BlockSpec(memory_space=places[place]) for _, _, place in outs],
        scratch_shapes=list(scratch),
        input_output_aliases=aliases or {},
        cost_estimate=pl.CostEstimate(flops=cost, bytes_accessed=1000, transcendentals=0),
        compiler_params=pltpu.CompilerParams(vmem_limit_bytes=vmem * 2**20),
    )(*[pin(value) if place in "HL" else value for value, place in ins])


DMA = pltpu.SemaphoreType.DMA


def send_copies(source, target, indices, sem):
    copies = [pltpu.make_async_copy(source, target.at[index], sem.at[index]) for index in indices]
    for copy in copies:
        copy.start()
    return copies


def wait_all(copies):
    for copy in copies:
        copy.wait()


def weight_copies(w_ref, w_buf, w_sem, parts=(1, 2, 0), start=True):
    group = group_index()
    copies = []
    for slot, part in enumerate(parts):
        column = pl.multiple_of(part * D + (group // 2) * 384, 128)
        copy = pltpu.make_async_copy(w_ref.at[:, pl.ds(column, 384)], w_buf.at[slot], w_sem.at[slot])
        if start:
            copy.start()
        copies.append(copy)
    return copies


def own_heads(full):
    odd = (group_index() % 2) == 1
    return jnp.where(odd, full[:, 192:], full[:, :192]).astype(BF)


def project_kernel(
    tok_ref, gain_ref, shift_ref, w_ref, kv_ref, normed_ref,
    x_buf, w_buf, kv_buf, gain_buf, shift_buf, x_sem, w_sem, kv_sem, gain_sem, shift_sem,
):
    copy_x = pltpu.make_async_copy(tok_ref.at[lax.axis_index(MICRO)], x_buf, x_sem)
    copy_x.start()
    copy_gain = pltpu.make_async_copy(gain_ref, gain_buf, gain_sem)
    copy_gain.start()
    copy_shift = pltpu.make_async_copy(shift_ref, shift_buf, shift_sem)
    copy_shift.start()
    copies = weight_copies(w_ref, w_buf, w_sem, (1, 2))
    wait_all([copy_x, copy_gain, copy_shift])
    unit, _ = normalized(x_buf[...].astype(F32))
    normed = (unit * gain_buf[...].reshape(1, D) + shift_buf[...].reshape(1, D)).astype(BF)
    normed_ref[...] = normed
    parts = []
    for slot in range(2):
        copies[slot].wait()
        parts.append(own_heads(mm(normed, w_buf[slot])))
    kv_buf[...] = jnp.concatenate(parts, axis=1)
    wait_all(send_copies(kv_buf, kv_ref, range(8), kv_sem))


def query_kernel(normed_ref, w_ref, q_ref, w_buf, w_sem):
    weight_copies(w_ref, w_buf, w_sem, (0,))[0].wait()
    part = own_heads(mm(normed_ref[...], w_buf[0]))
    q_ref[...] = jnp.concatenate([part, jnp.zeros((TOK, HD), BF)], axis=1)


def block_query_kernel(normed_ref, w_ref, out_ref, x_buf, w_buf, x_sem, w_sem):
    block = pl.ds(pl.multiple_of(group_index() * BLK, BLK), BLK)
    loads = [
        pltpu.make_async_copy(normed_ref.at[block], x_buf, x_sem),
        pltpu.make_async_copy(w_ref.at[:, pl.ds(0, D)], w_buf, w_sem),
    ]
    for load in loads:
        load.start()
    wait_all(loads)
    query = mm(x_buf[...], w_buf[...]).astype(BF)
    zero = jnp.zeros((BLK, HD), BF)
    for group in range(4):
        out_ref[group] = jnp.concatenate([query[:, group * 192:(group + 1) * 192], zero], axis=1)


def attend_kernel(scene_ref, q_ref, same_ref, other_ref, out_ref, buf, q_buf, sem, q_sem):
    load = pltpu.make_async_copy(q_ref, q_buf, q_sem)
    load.start()
    first, big = span(scene_ref)

    def run(count):
        rows = count * TOK
        keys = jnp.concatenate(
            [ref[pl.ds(first, count)].reshape(rows, 384) for ref in (same_ref, other_ref)], axis=0
        )
        load.wait()
        query = q_buf[...]
        q0, q1 = halves(query[:, :128])
        blocks = [keys[:, :128], keys[:, 128:256], keys[:, 256:]]
        mixed = []
        columns = []
        for qh, kb, vb in ((q0, 0, 1), (q1, 0, 2), (query[:, 128:], 1, 2)):
            scores = mm_nt(qh, blocks[kb]) * (HD**-0.5)
            top = jnp.max(scores, axis=-1, keepdims=True)
            weights = jnp.exp(scores - top)
            total = jnp.sum(weights, axis=-1, keepdims=True)
            probs = (weights * (1.0 / total)).astype(BF)
            mixed.append(mm(probs, blocks[vb]))
            columns += three(top + jnp.log(total))
        stats = put_columns(128, TOK, 0, columns)
        buf[...] = jnp.concatenate([join(stats, mixed[0]), join(mixed[1], mixed[2])], axis=1).astype(BF)

    @pl.when(big)
    def _():
        run(5)

    @pl.when(jnp.logical_not(big))
    def _():
        run(1)

    wait_all(send_copies(buf, out_ref, range(8), sem))


def forward_kernel(
    mixed_ref, tok_ref, og_ref, wo_ref, gain_ref, shift_ref, up_ref, down_ref,
    out_ref, middle_ref, normed_ref, act_ref, gpre_ref,
    tok_buf, og_buf, up_buf, down_buf, gain_buf, shift_buf, grad_buf, branch_buf, middle_buf, in_sem, sem,
):
    loads = [
        pltpu.make_async_copy(ref, buf, in_sem.at[index])
        for index, (ref, buf) in enumerate(
            (
                (tok_ref, tok_buf), (up_ref, up_buf), (og_ref, og_buf), (down_ref, down_buf), (gain_ref, gain_buf),
                (shift_ref, shift_buf),
            )
        )
    ]
    for load in loads:
        load.start()
    total = jnp.zeros((2 * TOK, D), F32)
    for group in range(4):
        rows = jnp.concatenate([mixed_ref[group], mixed_ref[4 + group]], axis=0)
        total = total + mm(rows, wo_ref[group])
    loads[0].wait()
    total = total + tok_buf[...].reshape(2 * TOK, D).astype(F32)
    middle_buf[...] = total.reshape(8, BLK, D)
    third = pltpu.make_async_copy(
        middle_buf.at[lax.axis_index(MICRO) * 4 + group_index()], middle_ref, sem.at[2]
    )
    third.start()
    unit, _ = normalized(total)
    wait_all(loads[4:])
    normed = (unit * gain_buf[...].reshape(1, D) + shift_buf[...].reshape(1, D)).astype(BF)
    normed_ref[...] = normed
    loads[1].wait()
    pre = mm(normed, up_buf[...])
    cdf = 0.5 * (1.0 + lax.erf(pre * (0.5**0.5)))
    slope = cdf + pre * jnp.exp(-0.5 * pre * pre) * 0.3989422804014327
    loads[2].wait()
    loads[3].wait()
    grad_out = og_buf[...].reshape(2 * TOK, D)
    gpre = (mm_nt(grad_out, down_buf[...]) * slope).astype(BF)
    gpre_ref[...] = gpre
    grad_buf[...] = mm_nt(gpre, up_buf[...]).astype(BF).reshape(8, BLK, D)
    first = pltpu.make_async_copy(grad_buf, out_ref.at[:, pl.ds(BLK, BLK)], sem.at[0])
    first.start()
    act = (pre * cdf).astype(BF)
    act_ref[...] = act
    branch_buf[...] = mm(act, down_buf[...]).astype(BF).reshape(8, BLK, D)
    second = pltpu.make_async_copy(branch_buf, out_ref.at[:, pl.ds(0, BLK)], sem.at[1])
    second.start()
    wait_all([first, second, third])


def ff_grads_kernel(normed_ref, act_ref, gpre_ref, og_ref, keep_ref, send_ref, up_buf, down_buf):
    core = lax.axis_index(CORE)
    up_buf[...] = mm_tn(normed_ref[...], gpre_ref[...])
    down_buf[...] = mm_tn(act_ref[...], og_ref[...].reshape(2 * TOK, D))
    for ref, owner in ((keep_ref, core), (send_ref, 1 - core)):
        column = pl.multiple_of(owner * 384, 128)
        for tile in range(8):
            rows = pl.ds(pl.multiple_of((2 * tile + owner) * 48, 16), 48)
            ref[tile, :, :384] = up_buf[rows].astype(BF)
            ref[tile, :, 384:] = down_buf[tile * 48:(tile + 1) * 48, pl.ds(column, 384)].astype(BF)


def split_kernel(one_ref, two_ref, *refs):
    y = lax.axis_index("y")
    for k, ref in enumerate(refs):
        for xl in range(2):
            at = (y ^ k) * 2 + xl
            ref[xl] = (one_ref[at].astype(F32) + two_ref[at].astype(F32)).astype(BF)


def total_kernel(*refs):
    total = refs[0][...].astype(F32)
    for ref in refs[1:4]:
        total = total + ref[...].astype(F32)
    refs[4][...] = total.astype(BF)


def middle_kernel(
    sums_ref, middle_ref, og_ref, mixed_ref, wo_ref, gain_ref, query_ref,
    out_ref, low_ref, grad_ref, result_ref, vec_ref,
    buf, middle_buf, og_buf, mixed_buf, gain_buf, query_buf, low_buf, grad_buf, result_buf, vec_buf, in_sem, sem, rest_sem,
):
    micro = lax.axis_index(MICRO)
    group = group_index()
    block = pl.ds(pl.multiple_of(group * BLK, BLK), BLK)
    loads = [
        pltpu.make_async_copy(middle_ref, middle_buf, in_sem.at[0]),
        pltpu.make_async_copy(og_ref.at[micro, block], og_buf, in_sem.at[1]),
        pltpu.make_async_copy(mixed_ref.at[pl.ds(micro * 4, 4), block], mixed_buf, in_sem.at[2]),
        pltpu.make_async_copy(gain_ref, gain_buf, in_sem.at[3]),
        pltpu.make_async_copy(query_ref, query_buf, in_sem.at[4]),
    ]
    for load in loads:
        load.start()
    total = sums_ref[0].astype(F32)
    for index in range(1, 8):
        total = total + sums_ref[index].astype(F32)
    branch, grad = total[:BLK], total[BLK:]
    wait_all(loads)
    middle = middle_buf[...]
    unit, inverse = normalized(middle)
    grad_mid = og_buf[...].astype(F32) + norm_back(grad, unit, inverse, gain_buf[...].reshape(1, D))
    low = grad_mid.astype(BF)
    low_buf[...] = low
    grad_buf[...] = grad_mid
    result_buf[...] = (middle + branch).astype(BF)
    gain_grad = jnp.sum(grad * unit, axis=0, keepdims=True)
    shift_grad = jnp.sum(grad, axis=0, keepdims=True)
    vec_buf[...] = jnp.concatenate([gain_grad, shift_grad, jnp.zeros((6, D), F32)], axis=0)
    stores = [
        pltpu.make_async_copy(source, target, rest_sem.at[index])
        for index, (source, target) in enumerate(
            ((low_buf, low_ref), (grad_buf, grad_ref), (result_buf, result_ref), (vec_buf, vec_ref))
        )
    ]
    for store in stores:
        store.start()
    lane = lax.broadcasted_iota(jnp.int32, (BLK, 256), 1)
    for head_group in range(4):
        mixed = mixed_buf[head_group].astype(F32)
        back = mm_nt(low, wo_ref[head_group]).astype(BF).astype(F32)
        product = mixed * back
        columns = []
        for head in range(3):
            inside = (lane >= (head + 1) * HD) & (lane < (head + 2) * HD)
            columns += three(jnp.sum(jnp.where(inside, product, 0.0), axis=-1, keepdims=True))
        stats = put_columns(256, BLK, 9, columns)
        packed = jnp.where(lane < 9, mixed, jnp.where(lane < HD, stats, back)).astype(BF)
        query = query_buf[head_group]
        last = query[:, 128:192]
        buf[head_group, :32] = packed[:, :128]
        buf[head_group, 32:64] = packed[:, 128:]
        buf[head_group, 64:96] = query[:, :128]
        buf[head_group, 96:] = jnp.concatenate([last[:16], last[16:]], axis=1)
    sends = send_copies(buf, out_ref, range(8), sem)
    wait_all(stores)
    wait_all(sends)


def attend_back_kernel(
    scene_ref, kvs_ref, kvo_ref, gs_ref, go_ref, normed_ref, mixed_ref, low_ref, low1_ref, low2_ref, low3_ref,
    w_ref, gqkv_ref, w_out_ref, keep_ref, send_ref,
    kv_buf, grad_buf, mixed_buf, normed_buf, low_buf, kv_sem, in_sem, w_sem,
):
    first, big = span(scene_ref)
    chip = chip_index()
    core = lax.axis_index(CORE)
    group = group_index()
    index = lax.axis_index(MICRO) * 4 + group
    first_loads = [
        pltpu.make_async_copy(source, target, in_sem.at[slot])
        for slot, (source, target) in enumerate(
            ((normed_ref, normed_buf), (mixed_ref.at[index], mixed_buf), (low_ref, low_buf))
        )
    ]
    scale = HD**-0.5

    def run(count):
        rows = count * TOK
        loads = [pltpu.make_async_copy(kvs_ref.at[pl.ds(first, count)], kv_buf.at[pl.ds(0, count)], kv_sem)]
        for load in loads + first_loads:
            load.start()
        weight_copies(w_ref, w_out_ref, w_sem)

        def cut(value):
            return [value[:, at:at + 128] for at in range(0, value.shape[1], 128)]

        def unpacked(ref, start, tiles):
            blocks = [ref[pl.ds(start, tiles), :, at:at + 32] for at in (0, 32, 64)]
            last = ref[pl.ds(start, tiles), :, 96:]
            turned = jnp.concatenate([last[..., HD:], last[..., :HD]], axis=-1)
            blocks.append(jnp.concatenate([last, turned], axis=2))
            return [block.reshape(tiles * TOK, 128) for block in blocks]

        every = [
            jnp.concatenate(pair, axis=0)
            for pair in zip(*[unpacked(ref, first, count) for ref in (gs_ref, go_ref)])
        ]
        grad, query = every[:2], every[2:]
        g_own = unpacked(gs_ref, chip, 1)
        g_heads = [halves(g_own[0])[1], *halves(g_own[1])]
        own_stats = g_own[0].astype(F32)
        all_stats = grad[0].astype(F32).T
        wait_all(loads)
        kv = cut(jnp.concatenate(
            [kv_buf[:count].reshape(rows, 384), kvo_ref[pl.ds(first, count)].reshape(rows, 384)], axis=0
        ))
        own = cut(kv_buf[chip - first]) + g_own[2:]
        q_heads = [*halves(own[3]), halves(own[4])[0]]
        k_heads = [*halves(own[0]), halves(own[1])[0]]
        v_heads = [halves(own[1])[1], *halves(own[2])]

        def column(at):
            return own_stats[:, at:at + 1] + own_stats[:, at + 1:at + 2] + own_stats[:, at + 2:at + 3]

        def row(at):
            return all_stats[at:at + 1] + all_stats[at + 1:at + 2] + all_stats[at + 2:at + 3]

        dq, dk, dv = [], [], []
        for head, (kb, vb) in enumerate(((0, 1), (0, 2), (1, 2))):
            qb, gb = (0, 0, 1)[head], (0, 1, 1)[head]
            probs = jnp.exp(mm_nt(q_heads[head], kv[kb]) * scale - column(3 * head))
            gap = mm_nt(g_heads[head], kv[vb]) - column(9 + 3 * head)
            dq.append(mm((probs * gap).astype(BF), kv[kb]) * scale)
            probs = jnp.exp(mm_nt(k_heads[head], query[qb]) * scale - row(3 * head))
            gap = mm_nt(v_heads[head], grad[gb]) - row(9 + 3 * head)
            dv.append(mm(probs.astype(BF), grad[gb]))
            dk.append(mm((probs * gap).astype(BF), query[qb]) * scale)
        tail = dq[2]
        gqkv_ref[...] = jnp.concatenate(
            [join(dk[0], dk[1]), join(dk[2], dv[0]), join(dv[1], dv[2]), join(dq[0], dq[1]),
             join(tail, jnp.zeros_like(tail))],
            axis=1,
        ).astype(BF)


    @pl.when(big)
    def _():
        run(5)

    @pl.when(jnp.logical_not(big))
    def _():
        run(1)

    wait_all(first_loads)

    grad_buf[...] = mm_tn(normed_buf[...], gqkv_ref[...])
    low = jnp.concatenate([ref[...] for ref in (low_buf, low1_ref, low2_ref, low3_ref)], axis=0)
    mixed = jnp.concatenate(
        [mixed_buf[pl.ds(pl.multiple_of((group ^ k) * BLK, BLK), BLK)] for k in range(4)], axis=0
    )
    out = mm_tn(mixed, low)[HD:]
    for ref, owner in ((keep_ref, core), (send_ref, 1 - core)):
        for tile in range(8):
            rows = grad_buf[pl.ds(pl.multiple_of((2 * tile + owner) * 48, 16), 48)]
            at = (tile // 4) * 96
            pieces = [
                out[at + row * 48:at + (row + 1) * 48, (tile % 4) * 192:(tile % 4 + 1) * 192] for row in range(2)
            ]
            ref[2 * tile] = rows[:, :384].astype(BF)
            ref[2 * tile + 1] = jnp.concatenate(
                [rows[:, 384:576], jnp.where(owner == 1, pieces[1], pieces[0])], axis=1
            ).astype(BF)
    wait_all(weight_copies(w_ref, w_out_ref, w_sem, start=False))


def normed_grad_kernel(
    gqkv_ref, w_ref, tok_ref, vec_ref, near_ref, far_ref, own_ref, one_ref, two_ref, three_ref, sums_ref, ff_ref,
    x_buf, vec_buf, near_buf, part_buf, low_buf, sums_buf, ff_buf, rows_buf, in_sem, out_sem, row_sem,
):
    loads = [
        pltpu.make_async_copy(tok_ref.at[lax.axis_index(MICRO)], x_buf, in_sem.at[0]),
        pltpu.make_async_copy(vec_ref, vec_buf, in_sem.at[1]),
        pltpu.make_async_copy(near_ref, near_buf, in_sem.at[2]),
    ]
    for load in loads:
        load.start()
    group = group_index()
    odd = (group % 2) == 1
    total = jnp.zeros((TOK, D), F32)
    for slot in range(3):
        part = gqkv_ref[:, slot * 192:(slot + 1) * 192]
        zero = jnp.zeros_like(part)
        wide = jnp.where(
            odd, jnp.concatenate([zero, part], axis=1), jnp.concatenate([part, zero], axis=1)
        )
        total = total + mm_nt(wide, w_ref[slot])
    part_buf[...] = total
    low_buf[...] = total.astype(BF)
    stores = []
    for k, ref in enumerate((own_ref, one_ref, two_ref, three_ref)):
        rows = pl.ds(pl.multiple_of((group ^ k) * BLK, BLK), BLK)
        target = ref.at[pl.ds(0, BLK)] if k else ref
        stores.append(pltpu.make_async_copy((low_buf if k else part_buf).at[rows], target, out_sem.at[k]))
        stores[-1].start()
    wait_all(loads)
    ff_buf[...] = (near_buf[...].astype(F32) + far_ref[...].astype(F32)).astype(BF)
    stores.append(pltpu.make_async_copy(ff_buf, ff_ref, out_sem.at[5]))
    stores[-1].start()
    unit, _ = normalized(x_buf[...].astype(F32))
    gain1 = jnp.sum(total * unit, axis=0, keepdims=True)
    shift1 = jnp.sum(total, axis=0, keepdims=True)
    vectors = jnp.concatenate([gain1, shift1, vec_buf[...][:2], jnp.zeros((4, D), F32)], axis=0)
    sums_buf[...] = vectors
    for index in range(4):
        rows_buf[index] = jnp.concatenate(
            [vectors[index:index + 1], jnp.zeros((15, D), F32)], axis=0
        ).astype(BF)
    for k, ref in enumerate((one_ref, two_ref, three_ref)):
        stores.append(
            pltpu.make_async_copy(rows_buf.at[group ^ (k + 1)], ref.at[pl.ds(BLK, 16)], row_sem.at[k])
        )
        stores[-1].start()
    stores.append(pltpu.make_async_copy(sums_buf, sums_ref, out_sem.at[4]))
    stores[-1].start()
    wait_all(stores)


def add_kernel(one_ref, two_ref, unused_ref, out_ref, buf, sem):
    buf[...] = (one_ref[...].astype(F32) + two_ref[...].astype(F32)).astype(BF)
    copy = pltpu.make_async_copy(buf, out_ref, sem)
    copy.start()
    copy.wait()


def sum_kernel(in_ref, vec_ref, one_ref, two_ref, three_ref, out_ref, buf, vec_buf, row_buf, sem, vec_sem, row_sem):
    loads = [pltpu.make_async_copy(vec_ref, vec_buf, vec_sem)] + [
        pltpu.make_async_copy(ref.at[pl.ds(BLK, 16)], row_buf.at[k], row_sem.at[k])
        for k, ref in enumerate((one_ref, two_ref, three_ref))
    ]
    for load in loads:
        load.start()
    total = in_ref[0].astype(F32)
    for index in range(1, 16):
        total = total + in_ref[index].astype(F32)
    wait_all(loads)
    vector = vec_buf[pl.ds(group_index(), 1)]
    for k in range(3):
        vector = vector + row_buf[k].astype(F32)[:1]
    rows = [vector[:, at:at + 128] for at in range(0, D, 128)] + [jnp.zeros((2, 128), F32)]
    pieces = [total[at:at + 8] for at in range(0, 48, 8)] + [jnp.concatenate(rows, axis=0)]
    block = jnp.concatenate(pieces, axis=1).astype(BF)
    for index in range(8):
        buf[index] = block
    wait_all(send_copies(buf, out_ref, range(8), sem))


def spread_kernel(turn, in_ref, *refs):
    qkv_buf, out_buf, sem, out_sem = refs[-4:]
    if turn:
        in_buf, in_sem = refs[-6:-4]
        qkv_ref, out_ref, *vec_refs = refs[3:-6]
        loads = [pltpu.make_async_copy(in_ref.at[tile], in_buf.at[tile], in_sem.at[tile]) for tile in range(8)]
        for load in loads:
            load.start()
    else:
        qkv_ref, out_ref, *vec_refs = refs[:-4]
        in_buf = in_ref
    owner = lax.axis_index(CORE)
    owner = 1 - owner if turn else owner
    copies = []
    vectors = [jnp.zeros((8, 128), F32)] * 4
    for tile in range(8):
        if turn:
            loads[tile].wait()
        whole = [in_buf[tile, index].astype(F32) for index in range(8)]
        block = [
            jnp.concatenate([value[:, at:at + 384] for at in range(0, 2304, 384)], axis=0) for value in whole
        ]
        vectors = [total + whole[k][:, 2304:] + whole[4 + k][:, 2304:] for k, total in enumerate(vectors)]
        for part, half, at in ((1, 0, 0), (2, 0, 192), (0, 4, 0)):
            qkv_buf[tile, :, part * D:(part + 1) * D] = jnp.concatenate(
                [block[half + group][:, at:at + 192] for group in range(4)], axis=1
            )
        start = pl.multiple_of((2 * tile + owner) * 48, 16)
        copy = pltpu.make_async_copy(qkv_buf.at[tile], qkv_ref.at[pl.ds(start, 48)], sem.at[tile])
        copy.start()
        copies.append(copy)
        for group in range(4):
            out_buf[group, tile // 4, :, (tile % 4) * 192:(tile % 4 + 1) * 192] = block[4 + group][:, 192:]
    for group in range(4):
        for pair in range(2):
            start = pl.multiple_of(group * 192 + (pair * 2 + owner) * 48, 16)
            copy = pltpu.make_async_copy(
                out_buf.at[group, pair], out_ref.at[pl.ds(start, 48)], out_sem.at[group, pair]
            )
            copy.start()
            copies.append(copy)
    if turn:
        for k, ref in enumerate(vec_refs):
            total = vectors[k] + refs[0][k]
            ref[...] = jnp.concatenate([total[row:row + 1] for row in range(6)], axis=1).reshape(D)
    else:
        for k, total in enumerate(vectors):
            vec_refs[0][k] = total
    wait_all(copies)


def spread_ff_kernel(turn, *refs):
    up_ref, down_ref, up_buf, down_buf, up_sem, down_sem = refs[-6:]
    y, core = lax.axis_index("y"), lax.axis_index(CORE)
    owner = 1 - core if turn else core
    copies = []
    for near in range(4):
        for xl in range(2):
            chip = (y ^ near) * 2 + xl
            block = refs[near][xl].astype(F32)
            up_buf[near, xl] = block[:, :384]
            down_buf[near, xl] = block[:, 384:]
            up_rows = pl.ds(pl.multiple_of((chip * 2 + owner) * 48, 16), 48)
            down_rows = pl.ds(pl.multiple_of(chip * 48, 16), 48)
            columns = pl.ds(pl.multiple_of(owner * 384, 128), 384)
            copies.append(pltpu.make_async_copy(up_buf.at[near, xl], up_ref.at[up_rows], up_sem.at[near, xl]))
            copies.append(
                pltpu.make_async_copy(down_buf.at[near, xl], down_ref.at[down_rows, columns], down_sem.at[near, xl])
            )
            copies[-2].start()
            copies[-1].start()
    wait_all(copies)


def input_kernel(
    own_ref, one_ref, two_ref, three_ref, tok_ref, gain_ref, grad_ref, result_ref, unused_ref, out_ref, buf, x_buf, sem, x_sem
):
    start = pl.multiple_of(group_index() * BLK, BLK)
    load = pltpu.make_async_copy(tok_ref.at[lax.axis_index(MICRO), pl.ds(start, BLK)], x_buf, x_sem)
    load.start()
    load.wait()
    total = own_ref[...]
    for ref in (one_ref, two_ref, three_ref):
        total = total + ref[:BLK].astype(F32)
    unit, inverse = normalized(x_buf[...].astype(F32))
    grad = grad_ref[...] + norm_back(total, unit, inverse, gain_ref[...].reshape(1, D))
    buf[:BLK] = grad.astype(BF)
    buf[BLK:] = result_ref[...]
    wait_all(send_copies(buf, out_ref, range(8), sem))


def unpack_kernel(in_ref, unused_ref, other_ref, grad_ref, result_ref):
    for index in range(8):
        rows = slice(index % 4 * BLK, (index % 4 + 1) * BLK)
        grad_ref[index // 4, rows] = in_ref[index, :BLK].astype(F32)
        result_ref[index // 4, rows] = in_ref[index, BLK:]


def exchange(value, axes):
    return lax.all_to_all(value, axes, 0, 0, tiled=True)


def swap(value):
    return lax.ppermute(value, CORE, [(0, 1), (1, 0)])


def after(value, *others):
    return pl.pallas_call(
        lambda *refs: None,
        out_shape=jax.ShapeDtypeStruct(value.shape, value.dtype),
        in_specs=[pl.BlockSpec(memory_space=pl.ANY)] * (1 + len(others)),
        out_specs=pl.BlockSpec(memory_space=pl.ANY),
        input_output_aliases={0: 0},
        cost_estimate=pl.CostEstimate(flops=1, bytes_accessed=1, transcendentals=0),
        compiler_params=pltpu.CompilerParams(vmem_limit_bytes=2**20),
    )(value, *others)


def flip(value, axes, count, bits):
    return lax.ppermute(value, axes, [(index, index ^ bits) for index in range(count)])


def shards(
    tokens, scene_of_block, ln1_gain, ln1_shift, w_qkv, w_out, ln2_gain, ln2_shift, w_up, w_down, out_grad
):
    w_out_pad = jnp.pad(w_out.reshape(4, 192, D), ((0, 0), (HD, 0), (0, 0)))
    kv_send, normed = call(
        project_kernel,
        [((8, TOK, 384), BF, "H"), ((TOK, D), BF, "L")],
        [(tokens, "H"), (ln1_gain, "H"), (ln1_shift, "H"), (w_qkv, "H")],
        1000,
        [
            pltpu.VMEM((TOK, D), BF), pltpu.VMEM((2, D, 384), BF), pltpu.VMEM((TOK, 384), BF),
            pltpu.VMEM((D,), F32), pltpu.VMEM((D,), F32), DMA, DMA((2,)), DMA((8,)), DMA, DMA,
        ],
    )
    (query,) = call(
        query_kernel,
        [((TOK, 256), BF, "L")],
        [(normed, "L"), (w_qkv, "H")],
        1000,
        [pltpu.VMEM((1, D, 384), BF), DMA((1,))],
    )
    kv_same = exchange(kv_send, CHIP)
    kv_same = after(kv_same, pin(query))
    kv_other = swap(kv_same)
    (mixed_send,) = call(
        attend_kernel,
        [((8, TOK, 256), BF, "H")],
        [(scene_of_block, "S"), (query, "H"), (kv_same, "V"), (kv_other, "V")],
        1000,
        [pltpu.VMEM((TOK, 256), BF), pltpu.VMEM((TOK, 256), BF), DMA((8,)), DMA],
    )
    mixed = exchange(mixed_send, NARROW)
    (block_query,) = call(
        block_query_kernel,
        [((4, BLK, 256), BF, "L")],
        [(normed, "H"), (w_qkv, "H")],
        1000,
        [pltpu.VMEM((BLK, D), BF), pltpu.VMEM((D, D), BF), DMA, DMA],
    )
    ff_send, middle, normed2, act, grad_pre = call(
        forward_kernel,
        [
            ((8, 2 * BLK, D), BF, "H"), ((BLK, D), F32, "H"), ((2 * TOK, D), BF, "V"),
            ((2 * TOK, FFL), BF, "V"), ((2 * TOK, FFL), BF, "V"),
        ],
        [
            (mixed, "V"), (tokens, "H"), (out_grad, "H"), (w_out_pad, "V"), (ln2_gain, "H"), (ln2_shift, "H"),
            (w_up, "H"), (w_down, "H"),
        ],
        1000,
        [
            pltpu.VMEM((2, TOK, D), BF), pltpu.VMEM((2, TOK, D), BF), pltpu.VMEM((D, FFL), BF),
            pltpu.VMEM((FFL, D), BF), pltpu.VMEM((D,), F32), pltpu.VMEM((D,), F32), pltpu.VMEM((8, BLK, D), BF),
            pltpu.VMEM((8, BLK, D), BF), pltpu.VMEM((8, BLK, D), F32), DMA((6,)), DMA((3,)),
        ],
    )
    ff_sums = exchange(ff_send, NARROW)
    keep, send = call(
        ff_grads_kernel,
        [((8, 48, D), BF, "V")] * 2,
        [(normed2, "V"), (act, "V"), (grad_pre, "V"), (out_grad, "L")],
        1000,
        [pltpu.VMEM((D, FFL), F32), pltpu.VMEM((FFL, D), F32)],
    )
    pieces = call(
        split_kernel, [((2, 48, D), BF, "L")] * 4, [(keep, "V"), (swap(send), "V")], 1000
    )
    pieces = [pieces[0]] + [flip(pieces[k], "y", 4, k) for k in (1, 2, 3)]
    (ff_near,) = call(
        total_kernel,
        [((2, 48, D), BF, "L")],
        [(pieces[0], "L")] + [(piece, "V") for piece in pieces[1:]],
        1000,
    )
    grad_send, low, grad_mid, result_part, vec2 = call(
        middle_kernel,
        [
            ((8, 4, 112, 128), BF, "H"), ((BLK, D), BF, "H"), ((BLK, D), F32, "H"), ((BLK, D), BF, "H"),
            ((8, D), F32, "H"),
        ],
        [
            (ff_sums, "V"), (middle, "H"), (out_grad, "H"), (mixed, "H"), (w_out_pad, "V"), (ln2_gain, "H"),
            (block_query, "H"),
        ],
        1000,
        [
            pltpu.VMEM((4, 112, 128), BF), pltpu.VMEM((BLK, D), F32), pltpu.VMEM((BLK, D), BF),
            pltpu.VMEM((4, BLK, 256), BF), pltpu.VMEM((D,), F32), pltpu.VMEM((4, BLK, 256), BF), pltpu.VMEM((BLK, D), BF), pltpu.VMEM((BLK, D), F32),
            pltpu.VMEM((BLK, D), BF), pltpu.VMEM((8, D), F32), DMA((5,)), DMA((8,)), DMA((4,)),
        ],
    )
    grad_send = after(pin(grad_send), *pieces[1:])
    grad_same = exchange(grad_send.reshape(32, 112, 128), (*CHIP, *GROUP)).reshape(8, 4, 112, 128)
    lows = [flip(low, GROUP, 4, k) for k in (1, 2, 3)]
    kv_same = after(pin(kv_same), low)
    kv_other = swap(kv_same)
    grad_same = after(grad_same, *lows, kv_other, pin(ff_near))
    grad_other = swap(grad_same)
    ff_near = after(pin(ff_near), grad_other)
    ff_far = flip(ff_near, "xl", 2, 1)
    gqkv, w_own, keep, send = call(
        attend_back_kernel,
        [((TOK, 640), BF, "V"), ((3, D, 384), BF, "V")] + [((16, 48, 384), BF, "V")] * 2,
        [
            (scene_of_block, "S"), (kv_same, "H"), (kv_other, "V"), (grad_same, "V"), (grad_other, "V"),
            (normed, "H"), (mixed, "H"), (low, "H"), *[(value, "V") for value in lows], (w_qkv, "H"),
        ],
        1000,
        [
            pltpu.VMEM((5, TOK, 384), BF), pltpu.VMEM((D, 640), F32),
            pltpu.VMEM((TOK, 256), BF), pltpu.VMEM((TOK, D), BF), pltpu.VMEM((BLK, D), BF),
            DMA, DMA((3,)), DMA((3,)),
        ],
        vmem=24,
    )
    own, *sends, sums, ff_part = call(
        normed_grad_kernel,
        [((BLK, D), F32, "H")] + [((BLK + 16, D), BF, "H")] * 3 + [((8, D), F32, "H"), ((2, 48, D), BF, "H")],
        [(gqkv, "V"), (w_own, "V"), (tokens, "H"), (vec2, "H"), (ff_near, "H"), (ff_far, "V")],
        1000,
        [
            pltpu.VMEM((TOK, D), BF), pltpu.VMEM((8, D), F32), pltpu.VMEM((2, 48, D), BF), pltpu.VMEM((TOK, D), F32),
            pltpu.VMEM((TOK, D), BF), pltpu.VMEM((8, D), F32), pltpu.VMEM((2, 48, D), BF), pltpu.VMEM((4, 16, D), BF),
            DMA((3,)), DMA((6,)), DMA((3,)),
        ],
    )
    (weight_send,) = call(
        add_kernel,
        [((16, 48, 384), BF, "H")],
        [(keep, "V"), (swap(after(send, ff_far)), "V"), (own, "H")],
        1000,
        [pltpu.VMEM((16, 48, 384), BF), DMA],
    )
    weight_parts = exchange(weight_send, (*CHIP, MICRO))
    parts = [flip(value, GROUP, 4, k + 1) for k, value in enumerate(sends)]
    weight_parts = after(weight_parts, pin(sums), *parts)
    ff_parts = [flip(ff_part, "y", 4, k) for k in (1, 2, 3)]
    (weight_total,) = call(
        sum_kernel,
        [((8, 8, 8, 2432), BF, "H")],
        [(weight_parts, "V"), (sums, "H"), *[(value, "A") for value in parts]],
        1000,
        [
            pltpu.VMEM((8, 8, 2432), BF), pltpu.VMEM((8, D), F32), pltpu.VMEM((3, 16, D), BF), DMA((8,)), DMA,
            DMA((3,)),
        ],
    )
    (packed,) = call(
        input_kernel,
        [((8, 2 * BLK, D), BF, "H")],
        [
            (own, "L"), *[(value, "V") for value in parts], (tokens, "H"), (ln1_gain, "L"), (grad_mid, "L"),
            (result_part, "L"), (weight_total, "H"),
        ],
        1000,
        [pltpu.VMEM((2 * BLK, D), BF), pltpu.VMEM((BLK, D), BF), DMA((8,)), DMA],
    )
    weight_same = exchange(weight_total.reshape(64, 8, 2432), (*CHIP, *NARROW)).reshape(8, 8, 8, 2432)
    weight_same = after(weight_same, pin(packed))
    everyone = exchange(after(pin(packed), weight_same), NARROW)
    weight_other = swap(weight_same)
    scratch = [
        pltpu.VMEM((8, 48, 3 * D), F32), pltpu.VMEM((4, 2, 48, D), F32), DMA((8,)), DMA((4, 2)),
    ]
    grads = [((D, 3 * D), F32, "H"), ((D, D), F32, "H")]
    half = call(
        functools.partial(spread_kernel, False),
        grads + [((4, 8, 128), F32, "V")],
        [(weight_same, "V")],
        1000,
        scratch,
    )
    qkv_grad, out_proj_grad, *vectors = call(
        functools.partial(spread_kernel, True),
        grads + [((D,), F32, "L")] * 4,
        [(weight_other, "H"), (half[2], "V"), (half[0], "H"), (half[1], "H")],
        1000,
        [pltpu.VMEM((8, 8, 8, 2432), BF), DMA((8,))] + scratch,
        aliases={2: 0, 3: 1},
    )
    ff_parts = [after(value, pin(vectors[0])) for value in ff_parts]
    ff_swapped = [swap(value) for value in (ff_part, *ff_parts)]
    ff_grads = [((D, FFL), F32, "H"), ((FFL, D), F32, "H")]
    ff_scratch = [
        pltpu.VMEM((4, 2, 48, FFL), F32), pltpu.VMEM((4, 2, 48, FFL), F32), DMA((4, 2)), DMA((4, 2)),
    ]
    ff_half = call(
        functools.partial(spread_ff_kernel, False),
        ff_grads,
        [(ff_part, "L"), *[(value, "V") for value in ff_parts]],
        1000,
        ff_scratch,
    )
    up_grad, down_grad = call(
        functools.partial(spread_ff_kernel, True),
        ff_grads,
        [*[(value, "V") for value in ff_swapped], (ff_half[0], "H"), (ff_half[1], "H")],
        1000,
        ff_scratch,
        aliases={4: 0, 5: 1},
    )
    input_grad, result = call(
        unpack_kernel, [((2, TOK, D), F32, "L"), ((2, TOK, D), BF, "L")], [(everyone, "V"), (vectors[0], "H"), (up_grad, "H")], 1000
    )
    return (
        result, input_grad, qkv_grad, out_proj_grad, *vectors, up_grad, down_grad
    )


def solution(mesh):
    names = ("y", "xl", "c", "zh", "zl", "xh")
    fine = Mesh(mesh.devices.reshape(4, 2, 2, 2, 2, 2), names)
    tokens = P(None, WIDE, None)
    placed = (
        tokens, P(), P(), P(), P(), P(), P(), P(), P(None, NARROW), P(NARROW, None), tokens
    )
    return jax.shard_map(
        shards,
        mesh=fine,
        in_specs=placed,
        out_specs=(
            tokens, tokens, P(), P(), P(), P(), P(), P(), P(None, NARROW), P(NARROW, None)
        ),
        check_vma=False,
    )
```

```python
import functools

import jax
import jax.numpy as jnp
from jax import lax
from jax.experimental import pallas as pl
from jax.experimental.pallas import tpu as pltpu
from jax.sharding import Mesh
from jax.sharding import PartitionSpec as P

D = 768
HD = 64
FFL = 384
TOK = 128
BLK = 32
EPS = 1e-05
BF = jnp.bfloat16
F32 = jnp.float32

CHIP = ("y", "xl")
CORE = "c"
MICRO = "zh"
GROUP = ("zl", "xh")
NARROW = (MICRO, *GROUP)
WIDE = (*CHIP, CORE)


def chip_index():
    return lax.axis_index("y") * 2 + lax.axis_index("xl")


def group_index():
    return lax.axis_index("zl") * 2 + lax.axis_index("xh")


def mm(left, right):
    return lax.dot_general(left, right, (((1,), (0,)), ((), ())), preferred_element_type=F32)


def mm_nt(left, right):
    return lax.dot_general(left, right, (((1,), (1,)), ((), ())), preferred_element_type=F32)


def mm_tn(left, right):
    return lax.dot_general(left, right, (((0,), (0,)), ((), ())), preferred_element_type=F32)


def normalized(values):
    center = values - jnp.mean(values, axis=-1, keepdims=True)
    spread = jnp.mean(center * center, axis=-1, keepdims=True)
    inverse = lax.rsqrt(spread + EPS)
    return center * inverse, inverse


def norm_back(grad, unit, inverse, gain):
    scaled = grad * gain
    first = jnp.mean(scaled, axis=-1, keepdims=True)
    second = jnp.mean(scaled * unit, axis=-1, keepdims=True)
    return inverse * (scaled - first - unit * second)


def halves(block):
    lane = lax.broadcasted_iota(jnp.int32, block.shape, 1)
    zero = jnp.zeros_like(block)
    return jnp.where(lane < HD, block, zero), jnp.where(lane < HD, zero, block)


def join(low, high):
    lane = lax.broadcasted_iota(jnp.int32, low.shape, 1)
    return jnp.where(lane < HD, low, high)


def span(scene_ref):
    micro = lax.axis_index(MICRO)
    own = scene_ref[micro, chip_index() * 4]
    first = jnp.int32(0)
    count = jnp.int32(0)
    for index in range(8):
        other = scene_ref[micro, index * 4]
        first += (other < own).astype(jnp.int32)
        count += (other == own).astype(jnp.int32)
    return first, count > 1


def three(value):
    a = value.astype(BF).astype(F32)
    b = (value - a).astype(BF).astype(F32)
    c = value - a - b
    return a, b, c


def put_columns(width, rows, start, columns):
    lane = lax.broadcasted_iota(jnp.int32, (rows, width), 1)
    out = jnp.zeros((rows, width), F32)
    for offset, column in enumerate(columns):
        out = jnp.where(lane == start + offset, column, out)
    return out


def pin(value):
    return pltpu.with_memory_space_constraint(value, pltpu.HBM)


def call(kernel, outs, ins, cost, scratch=(), vmem=16, aliases=None):
    places = {"V": pltpu.VMEM, "H": pltpu.HBM, "S": pltpu.SMEM, "L": pltpu.VMEM, "A": pl.ANY}
    return pl.pallas_call(
        kernel,
        out_shape=[
            (pltpu.HBM if place in "HL" else jax.ShapeDtypeStruct)(shape, dtype) for shape, dtype, place in outs
        ],
        in_specs=[pl.BlockSpec(memory_space=places[place]) for _, place in ins],
        out_specs=[pl.BlockSpec(memory_space=places[place]) for _, _, place in outs],
        scratch_shapes=list(scratch),
        input_output_aliases=aliases or {},
        cost_estimate=pl.CostEstimate(flops=cost, bytes_accessed=1000, transcendentals=0),
        compiler_params=pltpu.CompilerParams(vmem_limit_bytes=vmem * 2**20),
    )(*[pin(value) if place in "HL" else value for value, place in ins])


DMA = pltpu.SemaphoreType.DMA


def send_copies(source, target, indices, sem):
    copies = [pltpu.make_async_copy(source, target.at[index], sem.at[index]) for index in indices]
    for copy in copies:
        copy.start()
    return copies


def wait_all(copies):
    for copy in copies:
        copy.wait()


def weight_copies(w_ref, w_buf, w_sem, parts=(1, 2, 0), start=True):
    group = group_index()
    copies = []
    for slot, part in enumerate(parts):
        column = pl.multiple_of(part * D + (group // 2) * 384, 128)
        copy = pltpu.make_async_copy(w_ref.at[:, pl.ds(column, 384)], w_buf.at[slot], w_sem.at[slot])
        if start:
            copy.start()
        copies.append(copy)
    return copies


def own_heads(full):
    odd = (group_index() % 2) == 1
    return jnp.where(odd, full[:, 192:], full[:, :192]).astype(BF)


def project_kernel(
    tok_ref, gain_ref, shift_ref, w_ref, kv_ref, normed_ref,
    x_buf, w_buf, kv_buf, gain_buf, shift_buf, x_sem, w_sem, kv_sem, gain_sem, shift_sem,
):
    copy_x = pltpu.make_async_copy(tok_ref.at[lax.axis_index(MICRO)], x_buf, x_sem)
    copy_x.start()
    copy_gain = pltpu.make_async_copy(gain_ref, gain_buf, gain_sem)
    copy_gain.start()
    copy_shift = pltpu.make_async_copy(shift_ref, shift_buf, shift_sem)
    copy_shift.start()
    copies = weight_copies(w_ref, w_buf, w_sem, (1, 2))
    wait_all([copy_x, copy_gain, copy_shift])
    unit, _ = normalized(x_buf[...].astype(F32))
    normed = (unit * gain_buf[...].reshape(1, D) + shift_buf[...].reshape(1, D)).astype(BF)
    normed_ref[...] = normed
    parts = []
    for slot in range(2):
        copies[slot].wait()
        parts.append(own_heads(mm(normed, w_buf[slot])))
    kv_buf[...] = jnp.concatenate(parts, axis=1)
    wait_all(send_copies(kv_buf, kv_ref, range(8), kv_sem))


def query_kernel(normed_ref, w_ref, q_ref, w_buf, w_sem):
    weight_copies(w_ref, w_buf, w_sem, (0,))[0].wait()
    part = own_heads(mm(normed_ref[...], w_buf[0]))
    q_ref[...] = jnp.concatenate([part, jnp.zeros((TOK, HD), BF)], axis=1)


def block_query_kernel(normed_ref, w_ref, out_ref, x_buf, w_buf, x_sem, w_sem):
    block = pl.ds(pl.multiple_of(group_index() * BLK, BLK), BLK)
    loads = [
        pltpu.make_async_copy(normed_ref.at[block], x_buf, x_sem),
        pltpu.make_async_copy(w_ref.at[:, pl.ds(0, D)], w_buf, w_sem),
    ]
    for load in loads:
        load.start()
    wait_all(loads)
    query = mm(x_buf[...], w_buf[...]).astype(BF)
    zero = jnp.zeros((BLK, HD), BF)
    for group in range(4):
        out_ref[group] = jnp.concatenate([query[:, group * 192:(group + 1) * 192], zero], axis=1)


def attend_kernel(scene_ref, q_ref, same_ref, other_ref, out_ref, buf, q_buf, sem, q_sem):
    load = pltpu.make_async_copy(q_ref, q_buf, q_sem)
    load.start()
    first, big = span(scene_ref)

    def run(count):
        rows = count * TOK
        keys = jnp.concatenate(
            [ref[pl.ds(first, count)].reshape(rows, 384) for ref in (same_ref, other_ref)], axis=0
        )
        load.wait()
        query = q_buf[...] * jnp.asarray(HD**-0.5, BF)
        q0, q1 = halves(query[:, :128])
        blocks = [keys[:, :128], keys[:, 128:256], keys[:, 256:]]
        mixed = []
        columns = []
        for qh, kb, vb in ((q0, 0, 1), (q1, 0, 2), (query[:, 128:], 1, 2)):
            scores = mm_nt(qh, blocks[kb])
            top = jnp.max(scores, axis=-1, keepdims=True)
            weights = jnp.exp(scores - top)
            total = jnp.sum(weights, axis=-1, keepdims=True)
            probs = (weights * (1.0 / total)).astype(BF)
            mixed.append(mm(probs, blocks[vb]))
            columns += three(top + jnp.log(total))
        stats = put_columns(128, TOK, 0, columns)
        buf[...] = jnp.concatenate([join(stats, mixed[0]), join(mixed[1], mixed[2])], axis=1).astype(BF)

    @pl.when(big)
    def _():
        run(5)

    @pl.when(jnp.logical_not(big))
    def _():
        run(1)

    wait_all(send_copies(buf, out_ref, range(8), sem))


def forward_kernel(
    mixed_ref, tok_ref, og_ref, wo_ref, gain_ref, shift_ref, up_ref, down_ref,
    out_ref, middle_ref, normed_ref, act_ref, gpre_ref,
    tok_buf, og_buf, up_buf, down_buf, gain_buf, shift_buf, grad_buf, branch_buf, middle_buf, in_sem, sem,
):
    loads = [
        pltpu.make_async_copy(ref, buf, in_sem.at[index])
        for index, (ref, buf) in enumerate(
            (
                (tok_ref, tok_buf), (up_ref, up_buf), (og_ref, og_buf), (down_ref, down_buf), (gain_ref, gain_buf),
                (shift_ref, shift_buf),
            )
        )
    ]
    for load in loads:
        load.start()
    total = jnp.zeros((2 * TOK, D), F32)
    for group in range(4):
        rows = jnp.concatenate([mixed_ref[group], mixed_ref[4 + group]], axis=0)
        total = total + mm(rows, wo_ref[group])
    loads[0].wait()
    total = total + tok_buf[...].reshape(2 * TOK, D).astype(F32)
    middle_buf[...] = total.reshape(8, BLK, D)
    third = pltpu.make_async_copy(
        middle_buf.at[lax.axis_index(MICRO) * 4 + group_index()], middle_ref, sem.at[2]
    )
    third.start()
    unit, _ = normalized(total)
    wait_all(loads[4:])
    normed = (unit * gain_buf[...].reshape(1, D) + shift_buf[...].reshape(1, D)).astype(BF)
    normed_ref[...] = normed
    loads[1].wait()
    pre = mm(normed, up_buf[...])
    cdf = 0.5 * (1.0 + lax.erf(pre * (0.5**0.5)))
    slope = cdf + pre * jnp.exp(-0.5 * pre * pre) * 0.3989422804014327
    loads[2].wait()
    loads[3].wait()
    grad_out = og_buf[...].reshape(2 * TOK, D)
    gpre = (mm_nt(grad_out, down_buf[...]) * slope).astype(BF)
    gpre_ref[...] = gpre
    grad_buf[...] = mm_nt(gpre, up_buf[...]).astype(BF).reshape(8, BLK, D)
    first = pltpu.make_async_copy(grad_buf, out_ref.at[:, pl.ds(BLK, BLK)], sem.at[0])
    first.start()
    act = (pre * cdf).astype(BF)
    act_ref[...] = act
    branch_buf[...] = mm(act, down_buf[...]).astype(BF).reshape(8, BLK, D)
    second = pltpu.make_async_copy(branch_buf, out_ref.at[:, pl.ds(0, BLK)], sem.at[1])
    second.start()
    wait_all([first, second, third])


def ff_grads_kernel(normed_ref, act_ref, gpre_ref, og_ref, keep_ref, send_ref, up_buf, down_buf):
    core = lax.axis_index(CORE)
    up_buf[...] = mm_tn(normed_ref[...], gpre_ref[...])
    down_buf[...] = mm_tn(act_ref[...], og_ref[...].reshape(2 * TOK, D))
    for ref, owner in ((keep_ref, core), (send_ref, 1 - core)):
        column = pl.multiple_of(owner * 384, 128)
        for tile in range(8):
            rows = pl.ds(pl.multiple_of((2 * tile + owner) * 48, 16), 48)
            ref[tile, :, :384] = up_buf[rows].astype(BF)
            ref[tile, :, 384:] = down_buf[tile * 48:(tile + 1) * 48, pl.ds(column, 384)].astype(BF)


def split_kernel(one_ref, two_ref, *refs):
    y = lax.axis_index("y")
    for k, ref in enumerate(refs):
        for xl in range(2):
            at = (y ^ k) * 2 + xl
            ref[xl] = (one_ref[at].astype(F32) + two_ref[at].astype(F32)).astype(BF)


def total_kernel(*refs):
    total = refs[0][...].astype(F32)
    for ref in refs[1:4]:
        total = total + ref[...].astype(F32)
    refs[4][...] = total.astype(BF)


def middle_kernel(
    sums_ref, middle_ref, og_ref, mixed_ref, wo_ref, gain_ref, query_ref,
    out_ref, low_ref, grad_ref, result_ref, vec_ref,
    buf, middle_buf, og_buf, mixed_buf, gain_buf, query_buf, low_buf, grad_buf, result_buf, vec_buf, in_sem, sem, rest_sem,
):
    micro = lax.axis_index(MICRO)
    group = group_index()
    block = pl.ds(pl.multiple_of(group * BLK, BLK), BLK)
    loads = [
        pltpu.make_async_copy(middle_ref, middle_buf, in_sem.at[0]),
        pltpu.make_async_copy(og_ref.at[micro, block], og_buf, in_sem.at[1]),
        pltpu.make_async_copy(mixed_ref.at[pl.ds(micro * 4, 4), block], mixed_buf, in_sem.at[2]),
        pltpu.make_async_copy(gain_ref, gain_buf, in_sem.at[3]),
        pltpu.make_async_copy(query_ref, query_buf, in_sem.at[4]),
    ]
    for load in loads:
        load.start()
    total = sums_ref[0].astype(F32)
    for index in range(1, 8):
        total = total + sums_ref[index].astype(F32)
    branch, grad = total[:BLK], total[BLK:]
    wait_all(loads)
    middle = middle_buf[...]
    unit, inverse = normalized(middle)
    grad_mid = og_buf[...].astype(F32) + norm_back(grad, unit, inverse, gain_buf[...].reshape(1, D))
    low = grad_mid.astype(BF)
    low_buf[...] = low
    grad_buf[...] = grad_mid
    result_buf[...] = (middle + branch).astype(BF)
    gain_grad = jnp.sum(grad * unit, axis=0, keepdims=True)
    shift_grad = jnp.sum(grad, axis=0, keepdims=True)
    vec_buf[...] = jnp.concatenate([gain_grad, shift_grad, jnp.zeros((6, D), F32)], axis=0)
    stores = [
        pltpu.make_async_copy(source, target, rest_sem.at[index])
        for index, (source, target) in enumerate(
            ((low_buf, low_ref), (grad_buf, grad_ref), (result_buf, result_ref), (vec_buf, vec_ref))
        )
    ]
    for store in stores:
        store.start()
    lane = lax.broadcasted_iota(jnp.int32, (BLK, 256), 1)
    for head_group in range(4):
        mixed = mixed_buf[head_group].astype(F32)
        back = mm_nt(low, wo_ref[head_group]).astype(BF).astype(F32)
        product = mixed * back
        columns = []
        for head in range(3):
            inside = (lane >= (head + 1) * HD) & (lane < (head + 2) * HD)
            columns += three(jnp.sum(jnp.where(inside, product, 0.0), axis=-1, keepdims=True))
        stats = put_columns(256, BLK, 9, columns)
        packed = jnp.where(lane < 9, mixed, jnp.where(lane < HD, stats, back)).astype(BF)
        query = query_buf[head_group]
        last = query[:, 128:192]
        buf[head_group, :32] = packed[:, :128]
        buf[head_group, 32:64] = packed[:, 128:]
        buf[head_group, 64:96] = query[:, :128]
        buf[head_group, 96:] = jnp.concatenate([last[:16], last[16:]], axis=1)
    sends = send_copies(buf, out_ref, range(8), sem)
    wait_all(stores)
    wait_all(sends)


def attend_back_kernel(
    scene_ref, kvs_ref, kvo_ref, gs_ref, go_ref, normed_ref, mixed_ref, low_ref, low1_ref, low2_ref, low3_ref,
    w_ref, gqkv_ref, w_out_ref, keep_ref, send_ref,
    kv_buf, grad_buf, mixed_buf, normed_buf, low_buf, kv_sem, in_sem, w_sem,
):
    first, big = span(scene_ref)
    chip = chip_index()
    core = lax.axis_index(CORE)
    group = group_index()
    index = lax.axis_index(MICRO) * 4 + group
    first_loads = [
        pltpu.make_async_copy(source, target, in_sem.at[slot])
        for slot, (source, target) in enumerate(
            ((normed_ref, normed_buf), (mixed_ref.at[index], mixed_buf), (low_ref, low_buf))
        )
    ]
    scale = HD**-0.5

    def run(count):
        rows = count * TOK
        loads = [pltpu.make_async_copy(kvs_ref.at[pl.ds(first, count)], kv_buf.at[pl.ds(0, count)], kv_sem)]
        for load in loads + first_loads:
            load.start()
        weight_copies(w_ref, w_out_ref, w_sem)

        def cut(value):
            return [value[:, at:at + 128] for at in range(0, value.shape[1], 128)]

        def unpacked(ref, start, tiles):
            blocks = [ref[pl.ds(start, tiles), :, at:at + 32] for at in (0, 32, 64)]
            last = ref[pl.ds(start, tiles), :, 96:]
            turned = jnp.concatenate([last[..., HD:], last[..., :HD]], axis=-1)
            blocks.append(jnp.concatenate([last, turned], axis=2))
            return [block.reshape(tiles * TOK, 128) for block in blocks]

        every = [
            jnp.concatenate(pair, axis=0)
            for pair in zip(*[unpacked(ref, first, count) for ref in (gs_ref, go_ref)])
        ]
        grad, query = every[:2], every[2:]
        g_own = unpacked(gs_ref, chip, 1)
        g_heads = [halves(g_own[0])[1], *halves(g_own[1])]
        own_stats = g_own[0].astype(F32)
        all_stats = grad[0].astype(F32).T
        wait_all(loads)
        kv = cut(jnp.concatenate(
            [kv_buf[:count].reshape(rows, 384), kvo_ref[pl.ds(first, count)].reshape(rows, 384)], axis=0
        ))
        own = cut(kv_buf[chip - first]) + g_own[2:]
        small = jnp.asarray(scale, BF)
        q_heads = [*halves(own[3] * small), halves(own[4] * small)[0]]
        k_heads = [*halves(own[0] * small), halves(own[1] * small)[0]]
        v_heads = [halves(own[1])[1], *halves(own[2])]

        def column(at):
            return own_stats[:, at:at + 1] + own_stats[:, at + 1:at + 2] + own_stats[:, at + 2:at + 3]

        def row(at):
            return all_stats[at:at + 1] + all_stats[at + 1:at + 2] + all_stats[at + 2:at + 3]

        dq, dk, dv = [], [], []
        for head, (kb, vb) in enumerate(((0, 1), (0, 2), (1, 2))):
            qb, gb = (0, 0, 1)[head], (0, 1, 1)[head]
            probs = jnp.exp(mm_nt(q_heads[head], kv[kb]) - column(3 * head))
            gap = mm_nt(g_heads[head], kv[vb]) - column(9 + 3 * head)
            dq.append(mm((probs * gap).astype(BF), kv[kb]) * scale)
            probs = jnp.exp(mm_nt(k_heads[head], query[qb]) - row(3 * head))
            gap = mm_nt(v_heads[head], grad[gb]) - row(9 + 3 * head)
            dv.append(mm(probs.astype(BF), grad[gb]))
            dk.append(mm((probs * gap).astype(BF), query[qb]) * scale)
        tail = dq[2]
        gqkv_ref[...] = jnp.concatenate(
            [join(dk[0], dk[1]), join(dk[2], dv[0]), join(dv[1], dv[2]), join(dq[0], dq[1]),
             join(tail, jnp.zeros_like(tail))],
            axis=1,
        ).astype(BF)


    @pl.when(big)
    def _():
        run(5)

    @pl.when(jnp.logical_not(big))
    def _():
        run(1)

    wait_all(first_loads)

    grad_buf[...] = mm_tn(normed_buf[...], gqkv_ref[...])
    low = jnp.concatenate([ref[...] for ref in (low_buf, low1_ref, low2_ref, low3_ref)], axis=0)
    mixed = jnp.concatenate(
        [mixed_buf[pl.ds(pl.multiple_of((group ^ k) * BLK, BLK), BLK)] for k in range(4)], axis=0
    )
    out = mm_tn(mixed, low)[HD:]
    for ref, owner in ((keep_ref, core), (send_ref, 1 - core)):
        for tile in range(8):
            rows = grad_buf[pl.ds(pl.multiple_of((2 * tile + owner) * 48, 16), 48)]
            at = (tile // 4) * 96
            pieces = [
                out[at + row * 48:at + (row + 1) * 48, (tile % 4) * 192:(tile % 4 + 1) * 192] for row in range(2)
            ]
            ref[2 * tile] = rows[:, :384].astype(BF)
            ref[2 * tile + 1] = jnp.concatenate(
                [rows[:, 384:576], jnp.where(owner == 1, pieces[1], pieces[0])], axis=1
            ).astype(BF)
    wait_all(weight_copies(w_ref, w_out_ref, w_sem, start=False))


def normed_grad_kernel(
    gqkv_ref, w_ref, tok_ref, vec_ref, near_ref, far_ref, own_ref, one_ref, two_ref, three_ref, sums_ref, ff_ref,
    x_buf, vec_buf, near_buf, part_buf, low_buf, sums_buf, ff_buf, rows_buf, in_sem, out_sem, row_sem,
):
    loads = [
        pltpu.make_async_copy(tok_ref.at[lax.axis_index(MICRO)], x_buf, in_sem.at[0]),
        pltpu.make_async_copy(vec_ref, vec_buf, in_sem.at[1]),
        pltpu.make_async_copy(near_ref, near_buf, in_sem.at[2]),
    ]
    for load in loads:
        load.start()
    group = group_index()
    odd = (group % 2) == 1
    total = jnp.zeros((TOK, D), F32)
    for slot in range(3):
        part = gqkv_ref[:, slot * 192:(slot + 1) * 192]
        zero = jnp.zeros_like(part)
        wide = jnp.where(
            odd, jnp.concatenate([zero, part], axis=1), jnp.concatenate([part, zero], axis=1)
        )
        total = total + mm_nt(wide, w_ref[slot])
    part_buf[...] = total
    low_buf[...] = total.astype(BF)
    stores = []
    for k, ref in enumerate((own_ref, one_ref, two_ref, three_ref)):
        rows = pl.ds(pl.multiple_of((group ^ k) * BLK, BLK), BLK)
        target = ref.at[pl.ds(0, BLK)] if k else ref
        stores.append(pltpu.make_async_copy((low_buf if k else part_buf).at[rows], target, out_sem.at[k]))
        stores[-1].start()
    wait_all(loads)
    ff_buf[...] = (near_buf[...].astype(F32) + far_ref[...].astype(F32)).astype(BF)
    stores.append(pltpu.make_async_copy(ff_buf, ff_ref, out_sem.at[5]))
    stores[-1].start()
    unit, _ = normalized(x_buf[...].astype(F32))
    gain1 = jnp.sum(total * unit, axis=0, keepdims=True)
    shift1 = jnp.sum(total, axis=0, keepdims=True)
    vectors = jnp.concatenate([gain1, shift1, vec_buf[...][:2], jnp.zeros((4, D), F32)], axis=0)
    sums_buf[...] = vectors
    for index in range(4):
        rows_buf[index] = jnp.concatenate(
            [vectors[index:index + 1], jnp.zeros((15, D), F32)], axis=0
        ).astype(BF)
    for k, ref in enumerate((one_ref, two_ref, three_ref)):
        stores.append(
            pltpu.make_async_copy(rows_buf.at[group ^ (k + 1)], ref.at[pl.ds(BLK, 16)], row_sem.at[k])
        )
        stores[-1].start()
    stores.append(pltpu.make_async_copy(sums_buf, sums_ref, out_sem.at[4]))
    stores[-1].start()
    wait_all(stores)


def add_kernel(one_ref, two_ref, unused_ref, out_ref, buf, sem):
    buf[...] = (one_ref[...].astype(F32) + two_ref[...].astype(F32)).astype(BF)
    copy = pltpu.make_async_copy(buf, out_ref, sem)
    copy.start()
    copy.wait()


def sum_kernel(in_ref, vec_ref, one_ref, two_ref, three_ref, out_ref, buf, vec_buf, row_buf, sem, vec_sem, row_sem):
    loads = [pltpu.make_async_copy(vec_ref, vec_buf, vec_sem)] + [
        pltpu.make_async_copy(ref.at[pl.ds(BLK, 16)], row_buf.at[k], row_sem.at[k])
        for k, ref in enumerate((one_ref, two_ref, three_ref))
    ]
    for load in loads:
        load.start()
    total = in_ref[0].astype(F32)
    for index in range(1, 16):
        total = total + in_ref[index].astype(F32)
    wait_all(loads)
    vector = vec_buf[pl.ds(group_index(), 1)]
    for k in range(3):
        vector = vector + row_buf[k].astype(F32)[:1]
    rows = [vector[:, at:at + 128] for at in range(0, D, 128)] + [jnp.zeros((2, 128), F32)]
    pieces = [total[at:at + 8] for at in range(0, 48, 8)] + [jnp.concatenate(rows, axis=0)]
    block = jnp.concatenate(pieces, axis=1).astype(BF)
    for index in range(8):
        buf[index] = block
    wait_all(send_copies(buf, out_ref, range(8), sem))


def spread_kernel(turn, in_ref, *refs):
    qkv_buf, out_buf, sem, out_sem = refs[-4:]
    if turn:
        in_buf, in_sem = refs[-6:-4]
        qkv_ref, out_ref, *vec_refs = refs[3:-6]
        loads = [pltpu.make_async_copy(in_ref.at[tile], in_buf.at[tile], in_sem.at[tile]) for tile in range(8)]
        for load in loads:
            load.start()
    else:
        qkv_ref, out_ref, *vec_refs = refs[:-4]
        in_buf = in_ref
    owner = lax.axis_index(CORE)
    owner = 1 - owner if turn else owner
    copies = []
    vectors = [jnp.zeros((8, 128), F32)] * 4
    for tile in range(8):
        if turn:
            loads[tile].wait()
        whole = [in_buf[tile, index].astype(F32) for index in range(8)]
        block = [
            jnp.concatenate([value[:, at:at + 384] for at in range(0, 2304, 384)], axis=0) for value in whole
        ]
        vectors = [total + whole[k][:, 2304:] + whole[4 + k][:, 2304:] for k, total in enumerate(vectors)]
        for part, half, at in ((1, 0, 0), (2, 0, 192), (0, 4, 0)):
            qkv_buf[tile, :, part * D:(part + 1) * D] = jnp.concatenate(
                [block[half + group][:, at:at + 192] for group in range(4)], axis=1
            )
        start = pl.multiple_of((2 * tile + owner) * 48, 16)
        copy = pltpu.make_async_copy(qkv_buf.at[tile], qkv_ref.at[pl.ds(start, 48)], sem.at[tile])
        copy.start()
        copies.append(copy)
        for group in range(4):
            out_buf[group, tile // 4, :, (tile % 4) * 192:(tile % 4 + 1) * 192] = block[4 + group][:, 192:]
    for group in range(4):
        for pair in range(2):
            start = pl.multiple_of(group * 192 + (pair * 2 + owner) * 48, 16)
            copy = pltpu.make_async_copy(
                out_buf.at[group, pair], out_ref.at[pl.ds(start, 48)], out_sem.at[group, pair]
            )
            copy.start()
            copies.append(copy)
    if turn:
        for k, ref in enumerate(vec_refs):
            total = vectors[k] + refs[0][k]
            ref[...] = jnp.concatenate([total[row:row + 1] for row in range(6)], axis=1).reshape(D)
    else:
        for k, total in enumerate(vectors):
            vec_refs[0][k] = total
    wait_all(copies)


def spread_ff_kernel(turn, *refs):
    up_ref, down_ref, up_buf, down_buf, up_sem, down_sem = refs[-6:]
    y, core = lax.axis_index("y"), lax.axis_index(CORE)
    owner = 1 - core if turn else core
    copies = []
    for near in range(4):
        for xl in range(2):
            chip = (y ^ near) * 2 + xl
            block = refs[near][xl].astype(F32)
            up_buf[near, xl] = block[:, :384]
            down_buf[near, xl] = block[:, 384:]
            up_rows = pl.ds(pl.multiple_of((chip * 2 + owner) * 48, 16), 48)
            down_rows = pl.ds(pl.multiple_of(chip * 48, 16), 48)
            columns = pl.ds(pl.multiple_of(owner * 384, 128), 384)
            copies.append(pltpu.make_async_copy(up_buf.at[near, xl], up_ref.at[up_rows], up_sem.at[near, xl]))
            copies.append(
                pltpu.make_async_copy(down_buf.at[near, xl], down_ref.at[down_rows, columns], down_sem.at[near, xl])
            )
            copies[-2].start()
            copies[-1].start()
    wait_all(copies)


def input_kernel(
    own_ref, one_ref, two_ref, three_ref, tok_ref, gain_ref, grad_ref, result_ref, unused_ref, out_ref, buf, x_buf, sem, x_sem
):
    start = pl.multiple_of(group_index() * BLK, BLK)
    load = pltpu.make_async_copy(tok_ref.at[lax.axis_index(MICRO), pl.ds(start, BLK)], x_buf, x_sem)
    load.start()
    load.wait()
    total = own_ref[...]
    for ref in (one_ref, two_ref, three_ref):
        total = total + ref[:BLK].astype(F32)
    unit, inverse = normalized(x_buf[...].astype(F32))
    grad = grad_ref[...] + norm_back(total, unit, inverse, gain_ref[...].reshape(1, D))
    buf[:BLK] = grad.astype(BF)
    buf[BLK:] = result_ref[...]
    wait_all(send_copies(buf, out_ref, range(8), sem))


def unpack_kernel(in_ref, unused_ref, other_ref, grad_ref, result_ref):
    for index in range(8):
        rows = slice(index % 4 * BLK, (index % 4 + 1) * BLK)
        grad_ref[index // 4, rows] = in_ref[index, :BLK].astype(F32)
        result_ref[index // 4, rows] = in_ref[index, BLK:]


def exchange(value, axes):
    return lax.all_to_all(value, axes, 0, 0, tiled=True)


def swap(value):
    return lax.ppermute(value, CORE, [(0, 1), (1, 0)])


def after(value, *others):
    return pl.pallas_call(
        lambda *refs: None,
        out_shape=jax.ShapeDtypeStruct(value.shape, value.dtype),
        in_specs=[pl.BlockSpec(memory_space=pl.ANY)] * (1 + len(others)),
        out_specs=pl.BlockSpec(memory_space=pl.ANY),
        input_output_aliases={0: 0},
        cost_estimate=pl.CostEstimate(flops=1, bytes_accessed=1, transcendentals=0),
        compiler_params=pltpu.CompilerParams(vmem_limit_bytes=2**20),
    )(value, *others)


def flip(value, axes, count, bits):
    return lax.ppermute(value, axes, [(index, index ^ bits) for index in range(count)])


def shards(
    tokens, scene_of_block, ln1_gain, ln1_shift, w_qkv, w_out, ln2_gain, ln2_shift, w_up, w_down, out_grad
):
    w_out_pad = jnp.pad(w_out.reshape(4, 192, D), ((0, 0), (HD, 0), (0, 0)))
    kv_send, normed = call(
        project_kernel,
        [((8, TOK, 384), BF, "H"), ((TOK, D), BF, "L")],
        [(tokens, "H"), (ln1_gain, "H"), (ln1_shift, "H"), (w_qkv, "H")],
        1000,
        [
            pltpu.VMEM((TOK, D), BF), pltpu.VMEM((2, D, 384), BF), pltpu.VMEM((TOK, 384), BF),
            pltpu.VMEM((D,), F32), pltpu.VMEM((D,), F32), DMA, DMA((2,)), DMA((8,)), DMA, DMA,
        ],
    )
    (query,) = call(
        query_kernel,
        [((TOK, 256), BF, "L")],
        [(normed, "L"), (w_qkv, "H")],
        1000,
        [pltpu.VMEM((1, D, 384), BF), DMA((1,))],
    )
    kv_same = exchange(kv_send, CHIP)
    kv_same = after(kv_same, pin(query))
    kv_other = swap(kv_same)
    (mixed_send,) = call(
        attend_kernel,
        [((8, TOK, 256), BF, "H")],
        [(scene_of_block, "S"), (query, "H"), (kv_same, "V"), (kv_other, "V")],
        1000,
        [pltpu.VMEM((TOK, 256), BF), pltpu.VMEM((TOK, 256), BF), DMA((8,)), DMA],
    )
    mixed = exchange(mixed_send, NARROW)
    (block_query,) = call(
        block_query_kernel,
        [((4, BLK, 256), BF, "L")],
        [(normed, "H"), (w_qkv, "H")],
        1000,
        [pltpu.VMEM((BLK, D), BF), pltpu.VMEM((D, D), BF), DMA, DMA],
    )
    ff_send, middle, normed2, act, grad_pre = call(
        forward_kernel,
        [
            ((8, 2 * BLK, D), BF, "H"), ((BLK, D), F32, "H"), ((2 * TOK, D), BF, "V"),
            ((2 * TOK, FFL), BF, "V"), ((2 * TOK, FFL), BF, "V"),
        ],
        [
            (mixed, "V"), (tokens, "H"), (out_grad, "H"), (w_out_pad, "V"), (ln2_gain, "H"), (ln2_shift, "H"),
            (w_up, "H"), (w_down, "H"),
        ],
        1000,
        [
            pltpu.VMEM((2, TOK, D), BF), pltpu.VMEM((2, TOK, D), BF), pltpu.VMEM((D, FFL), BF),
            pltpu.VMEM((FFL, D), BF), pltpu.VMEM((D,), F32), pltpu.VMEM((D,), F32), pltpu.VMEM((8, BLK, D), BF),
            pltpu.VMEM((8, BLK, D), BF), pltpu.VMEM((8, BLK, D), F32), DMA((6,)), DMA((3,)),
        ],
    )
    ff_sums = exchange(ff_send, NARROW)
    keep, send = call(
        ff_grads_kernel,
        [((8, 48, D), BF, "V")] * 2,
        [(normed2, "V"), (act, "V"), (grad_pre, "V"), (out_grad, "L")],
        1000,
        [pltpu.VMEM((D, FFL), F32), pltpu.VMEM((FFL, D), F32)],
    )
    pieces = call(
        split_kernel, [((2, 48, D), BF, "L")] * 4, [(keep, "V"), (swap(send), "V")], 1000
    )
    pieces = [pieces[0]] + [flip(pieces[k], "y", 4, k) for k in (1, 2, 3)]
    (ff_near,) = call(
        total_kernel,
        [((2, 48, D), BF, "L")],
        [(pieces[0], "L")] + [(piece, "V") for piece in pieces[1:]],
        1000,
    )
    grad_send, low, grad_mid, result_part, vec2 = call(
        middle_kernel,
        [
            ((8, 4, 112, 128), BF, "H"), ((BLK, D), BF, "H"), ((BLK, D), F32, "H"), ((BLK, D), BF, "H"),
            ((8, D), F32, "H"),
        ],
        [
            (ff_sums, "V"), (middle, "H"), (out_grad, "H"), (mixed, "H"), (w_out_pad, "V"), (ln2_gain, "H"),
            (block_query, "H"),
        ],
        1000,
        [
            pltpu.VMEM((4, 112, 128), BF), pltpu.VMEM((BLK, D), F32), pltpu.VMEM((BLK, D), BF),
            pltpu.VMEM((4, BLK, 256), BF), pltpu.VMEM((D,), F32), pltpu.VMEM((4, BLK, 256), BF), pltpu.VMEM((BLK, D), BF), pltpu.VMEM((BLK, D), F32),
            pltpu.VMEM((BLK, D), BF), pltpu.VMEM((8, D), F32), DMA((5,)), DMA((8,)), DMA((4,)),
        ],
    )
    grad_send = after(pin(grad_send), *pieces[1:])
    grad_same = exchange(grad_send.reshape(32, 112, 128), (*CHIP, *GROUP)).reshape(8, 4, 112, 128)
    lows = [flip(low, GROUP, 4, k) for k in (1, 2, 3)]
    kv_same = after(pin(kv_same), low)
    kv_other = swap(kv_same)
    grad_same = after(grad_same, *lows, kv_other, pin(ff_near))
    grad_other = swap(grad_same)
    ff_near = after(pin(ff_near), grad_other)
    ff_far = flip(ff_near, "xl", 2, 1)
    gqkv, w_own, keep, send = call(
        attend_back_kernel,
        [((TOK, 640), BF, "V"), ((3, D, 384), BF, "V")] + [((16, 48, 384), BF, "V")] * 2,
        [
            (scene_of_block, "S"), (kv_same, "H"), (kv_other, "V"), (grad_same, "V"), (grad_other, "V"),
            (normed, "H"), (mixed, "H"), (low, "H"), *[(value, "V") for value in lows], (w_qkv, "H"),
        ],
        1000,
        [
            pltpu.VMEM((5, TOK, 384), BF), pltpu.VMEM((D, 640), F32),
            pltpu.VMEM((TOK, 256), BF), pltpu.VMEM((TOK, D), BF), pltpu.VMEM((BLK, D), BF),
            DMA, DMA((3,)), DMA((3,)),
        ],
        vmem=24,
    )
    own, *sends, sums, ff_part = call(
        normed_grad_kernel,
        [((BLK, D), F32, "H")] + [((BLK + 16, D), BF, "H")] * 3 + [((8, D), F32, "H"), ((2, 48, D), BF, "H")],
        [(gqkv, "V"), (w_own, "V"), (tokens, "H"), (vec2, "H"), (ff_near, "H"), (ff_far, "V")],
        1000,
        [
            pltpu.VMEM((TOK, D), BF), pltpu.VMEM((8, D), F32), pltpu.VMEM((2, 48, D), BF), pltpu.VMEM((TOK, D), F32),
            pltpu.VMEM((TOK, D), BF), pltpu.VMEM((8, D), F32), pltpu.VMEM((2, 48, D), BF), pltpu.VMEM((4, 16, D), BF),
            DMA((3,)), DMA((6,)), DMA((3,)),
        ],
    )
    (weight_send,) = call(
        add_kernel,
        [((16, 48, 384), BF, "H")],
        [(keep, "V"), (swap(after(send, ff_far)), "V"), (own, "H")],
        1000,
        [pltpu.VMEM((16, 48, 384), BF), DMA],
    )
    weight_parts = exchange(weight_send, (*CHIP, MICRO))
    parts = [flip(value, GROUP, 4, k + 1) for k, value in enumerate(sends)]
    weight_parts = after(weight_parts, pin(sums), *parts)
    ff_parts = [flip(ff_part, "y", 4, k) for k in (1, 2, 3)]
    (weight_total,) = call(
        sum_kernel,
        [((8, 8, 8, 2432), BF, "H")],
        [(weight_parts, "V"), (sums, "H"), *[(value, "A") for value in parts]],
        1000,
        [
            pltpu.VMEM((8, 8, 2432), BF), pltpu.VMEM((8, D), F32), pltpu.VMEM((3, 16, D), BF), DMA((8,)), DMA,
            DMA((3,)),
        ],
    )
    (packed,) = call(
        input_kernel,
        [((8, 2 * BLK, D), BF, "H")],
        [
            (own, "L"), *[(value, "V") for value in parts], (tokens, "H"), (ln1_gain, "L"), (grad_mid, "L"),
            (result_part, "L"), (weight_total, "H"),
        ],
        1000,
        [pltpu.VMEM((2 * BLK, D), BF), pltpu.VMEM((BLK, D), BF), DMA((8,)), DMA],
    )
    weight_same = exchange(weight_total.reshape(64, 8, 2432), (*CHIP, *NARROW)).reshape(8, 8, 8, 2432)
    weight_same = after(weight_same, pin(packed))
    everyone = exchange(after(pin(packed), weight_same), NARROW)
    weight_other = swap(weight_same)
    scratch = [
        pltpu.VMEM((8, 48, 3 * D), F32), pltpu.VMEM((4, 2, 48, D), F32), DMA((8,)), DMA((4, 2)),
    ]
    grads = [((D, 3 * D), F32, "H"), ((D, D), F32, "H")]
    half = call(
        functools.partial(spread_kernel, False),
        grads + [((4, 8, 128), F32, "V")],
        [(weight_same, "V")],
        1000,
        scratch,
    )
    qkv_grad, out_proj_grad, *vectors = call(
        functools.partial(spread_kernel, True),
        grads + [((D,), F32, "L")] * 4,
        [(weight_other, "H"), (half[2], "V"), (half[0], "H"), (half[1], "H")],
        1000,
        [pltpu.VMEM((8, 8, 8, 2432), BF), DMA((8,))] + scratch,
        aliases={2: 0, 3: 1},
    )
    ff_parts = [after(value, pin(vectors[0])) for value in ff_parts]
    ff_swapped = [swap(value) for value in (ff_part, *ff_parts)]
    ff_grads = [((D, FFL), F32, "H"), ((FFL, D), F32, "H")]
    ff_scratch = [
        pltpu.VMEM((4, 2, 48, FFL), F32), pltpu.VMEM((4, 2, 48, FFL), F32), DMA((4, 2)), DMA((4, 2)),
    ]
    ff_half = call(
        functools.partial(spread_ff_kernel, False),
        ff_grads,
        [(ff_part, "L"), *[(value, "V") for value in ff_parts]],
        1000,
        ff_scratch,
    )
    up_grad, down_grad = call(
        functools.partial(spread_ff_kernel, True),
        ff_grads,
        [*[(value, "V") for value in ff_swapped], (ff_half[0], "H"), (ff_half[1], "H")],
        1000,
        ff_scratch,
        aliases={4: 0, 5: 1},
    )
    input_grad, result = call(
        unpack_kernel, [((2, TOK, D), F32, "L"), ((2, TOK, D), BF, "L")], [(everyone, "V"), (vectors[0], "H"), (up_grad, "H")], 1000
    )
    return (
        result, input_grad, qkv_grad, out_proj_grad, *vectors, up_grad, down_grad
    )


def solution(mesh):
    names = ("y", "xl", "c", "zh", "zl", "xh")
    fine = Mesh(mesh.devices.reshape(4, 2, 2, 2, 2, 2), names)
    tokens = P(None, WIDE, None)
    placed = (
        tokens, P(), P(), P(), P(), P(), P(), P(), P(None, NARROW), P(NARROW, None), tokens
    )
    return jax.shard_map(
        shards,
        mesh=fine,
        in_specs=placed,
        out_specs=(
            tokens, tokens, P(), P(), P(), P(), P(), P(), P(None, NARROW), P(NARROW, None)
        ),
        check_vma=False,
    )
```

```python
import functools

import jax
import jax.numpy as jnp
from jax import lax
from jax.experimental import pallas as pl
from jax.experimental.pallas import tpu as pltpu
from jax.sharding import Mesh
from jax.sharding import PartitionSpec as P

D = 768
HD = 64
FFL = 384
TOK = 128
BLK = 32
EPS = 1e-05
BF = jnp.bfloat16
F32 = jnp.float32

CHIP = ("y", "xl")
CORE = "c"
MICRO = "zh"
GROUP = ("zl", "xh")
NARROW = (MICRO, *GROUP)
WIDE = (*CHIP, CORE)


def chip_index():
    return lax.axis_index("y") * 2 + lax.axis_index("xl")


def group_index():
    return lax.axis_index("zl") * 2 + lax.axis_index("xh")


def mm(left, right):
    return lax.dot_general(left, right, (((1,), (0,)), ((), ())), preferred_element_type=F32)


def mm_nt(left, right):
    return lax.dot_general(left, right, (((1,), (1,)), ((), ())), preferred_element_type=F32)


def mm_tn(left, right):
    return lax.dot_general(left, right, (((0,), (0,)), ((), ())), preferred_element_type=F32)


def normalized(values):
    center = values - jnp.mean(values, axis=-1, keepdims=True)
    spread = jnp.mean(center * center, axis=-1, keepdims=True)
    inverse = lax.rsqrt(spread + EPS)
    return center * inverse, inverse


def norm_back(grad, unit, inverse, gain):
    scaled = grad * gain
    first = jnp.mean(scaled, axis=-1, keepdims=True)
    second = jnp.mean(scaled * unit, axis=-1, keepdims=True)
    return inverse * (scaled - first - unit * second)


def halves(block):
    lane = lax.broadcasted_iota(jnp.int32, block.shape, 1)
    zero = jnp.zeros_like(block)
    return jnp.where(lane < HD, block, zero), jnp.where(lane < HD, zero, block)


def join(low, high):
    lane = lax.broadcasted_iota(jnp.int32, low.shape, 1)
    return jnp.where(lane < HD, low, high)


def span(scene_ref):
    micro = lax.axis_index(MICRO)
    own = scene_ref[micro, chip_index() * 4]
    first = jnp.int32(0)
    count = jnp.int32(0)
    for index in range(8):
        other = scene_ref[micro, index * 4]
        first += (other < own).astype(jnp.int32)
        count += (other == own).astype(jnp.int32)
    return first, count > 1


def three(value):
    a = value.astype(BF).astype(F32)
    b = (value - a).astype(BF).astype(F32)
    c = value - a - b
    return a, b, c


def put_columns(width, rows, start, columns):
    lane = lax.broadcasted_iota(jnp.int32, (rows, width), 1)
    out = jnp.zeros((rows, width), F32)
    for offset, column in enumerate(columns):
        out = jnp.where(lane == start + offset, column, out)
    return out


def pin(value):
    return pltpu.with_memory_space_constraint(value, pltpu.HBM)


def call(kernel, outs, ins, cost, scratch=(), vmem=16, aliases=None):
    places = {"V": pltpu.VMEM, "H": pltpu.HBM, "S": pltpu.SMEM, "L": pltpu.VMEM, "A": pl.ANY}
    return pl.pallas_call(
        kernel,
        out_shape=[
            (pltpu.HBM if place in "HL" else jax.ShapeDtypeStruct)(shape, dtype) for shape, dtype, place in outs
        ],
        in_specs=[pl.BlockSpec(memory_space=places[place]) for _, place in ins],
        out_specs=[pl.BlockSpec(memory_space=places[place]) for _, _, place in outs],
        scratch_shapes=list(scratch),
        input_output_aliases=aliases or {},
        cost_estimate=pl.CostEstimate(flops=cost, bytes_accessed=1000, transcendentals=0),
        compiler_params=pltpu.CompilerParams(vmem_limit_bytes=vmem * 2**20),
    )(*[pin(value) if place in "HL" else value for value, place in ins])


DMA = pltpu.SemaphoreType.DMA


def send_copies(source, target, indices, sem):
    copies = [pltpu.make_async_copy(source, target.at[index], sem.at[index]) for index in indices]
    for copy in copies:
        copy.start()
    return copies


def wait_all(copies):
    for copy in copies:
        copy.wait()


def weight_copies(w_ref, w_buf, w_sem, parts=(1, 2, 0), start=True):
    group = group_index()
    copies = []
    for slot, part in enumerate(parts):
        column = pl.multiple_of(part * D + (group // 2) * 384, 128)
        copy = pltpu.make_async_copy(w_ref.at[:, pl.ds(column, 384)], w_buf.at[slot], w_sem.at[slot])
        if start:
            copy.start()
        copies.append(copy)
    return copies


def own_heads(full):
    odd = (group_index() % 2) == 1
    return jnp.where(odd, full[:, 192:], full[:, :192]).astype(BF)


def project_kernel(
    tok_ref, gain_ref, shift_ref, w_ref, kv_ref, normed_ref,
    x_buf, w_buf, kv_buf, gain_buf, shift_buf, x_sem, w_sem, kv_sem, gain_sem, shift_sem,
):
    copy_x = pltpu.make_async_copy(tok_ref.at[lax.axis_index(MICRO)], x_buf, x_sem)
    copy_x.start()
    copy_gain = pltpu.make_async_copy(gain_ref, gain_buf, gain_sem)
    copy_gain.start()
    copy_shift = pltpu.make_async_copy(shift_ref, shift_buf, shift_sem)
    copy_shift.start()
    copies = weight_copies(w_ref, w_buf, w_sem, (1, 2))
    wait_all([copy_x, copy_gain, copy_shift])
    unit, _ = normalized(x_buf[...].astype(F32))
    normed = (unit * gain_buf[...].reshape(1, D) + shift_buf[...].reshape(1, D)).astype(BF)
    normed_ref[...] = normed
    parts = []
    for slot in range(2):
        copies[slot].wait()
        parts.append(own_heads(mm(normed, w_buf[slot])))
    kv_buf[...] = jnp.concatenate(parts, axis=1)
    wait_all(send_copies(kv_buf, kv_ref, range(8), kv_sem))


def query_kernel(normed_ref, w_ref, q_ref, w_buf, w_sem):
    weight_copies(w_ref, w_buf, w_sem, (0,))[0].wait()
    part = own_heads(mm(normed_ref[...], w_buf[0]))
    q_ref[...] = jnp.concatenate([part, jnp.zeros((TOK, HD), BF)], axis=1)


def block_query_kernel(normed_ref, w_ref, out_ref, x_buf, w_buf, x_sem, w_sem):
    block = pl.ds(pl.multiple_of(group_index() * BLK, BLK), BLK)
    loads = [
        pltpu.make_async_copy(normed_ref.at[block], x_buf, x_sem),
        pltpu.make_async_copy(w_ref.at[:, pl.ds(0, D)], w_buf, w_sem),
    ]
    for load in loads:
        load.start()
    wait_all(loads)
    query = mm(x_buf[...], w_buf[...]).astype(BF)
    zero = jnp.zeros((BLK, HD), BF)
    for group in range(4):
        out_ref[group] = jnp.concatenate([query[:, group * 192:(group + 1) * 192], zero], axis=1)


def attend_kernel(scene_ref, q_ref, same_ref, other_ref, out_ref, buf, q_buf, sem, q_sem):
    load = pltpu.make_async_copy(q_ref, q_buf, q_sem)
    load.start()
    first, big = span(scene_ref)

    def run(count):
        rows = count * TOK
        keys = jnp.concatenate(
            [ref[pl.ds(first, count)].reshape(rows, 384) for ref in (same_ref, other_ref)], axis=0
        )
        load.wait()
        query = q_buf[...]
        q0, q1 = halves(query[:, :128])
        blocks = [keys[:, :128], keys[:, 128:256], keys[:, 256:]]
        mixed = []
        columns = []
        for qh, kb, vb in ((q0, 0, 1), (q1, 0, 2), (query[:, 128:], 1, 2)):
            scores = mm_nt(qh, blocks[kb]) * (HD**-0.5)
            top = jnp.max(scores, axis=-1, keepdims=True)
            weights = jnp.exp(scores - top)
            total = jnp.sum(weights, axis=-1, keepdims=True)
            probs = (weights * (1.0 / total)).astype(BF)
            mixed.append(mm(probs, blocks[vb]))
            columns += three(top + jnp.log(total))
        stats = put_columns(128, TOK, 0, columns)
        buf[...] = jnp.concatenate([join(stats, mixed[0]), join(mixed[1], mixed[2])], axis=1).astype(BF)

    @pl.when(big)
    def _():
        run(5)

    @pl.when(jnp.logical_not(big))
    def _():
        run(1)

    wait_all(send_copies(buf, out_ref, range(8), sem))


def forward_kernel(
    mixed_ref, tok_ref, og_ref, wo_ref, gain_ref, shift_ref, up_ref, down_ref,
    out_ref, middle_ref, normed_ref, act_ref, gpre_ref,
    tok_buf, og_buf, up_buf, down_buf, gain_buf, shift_buf, grad_buf, branch_buf, middle_buf, in_sem, sem,
):
    loads = [
        pltpu.make_async_copy(ref, buf, in_sem.at[index])
        for index, (ref, buf) in enumerate(
            (
                (tok_ref, tok_buf), (up_ref, up_buf), (og_ref, og_buf), (down_ref, down_buf), (gain_ref, gain_buf),
                (shift_ref, shift_buf),
            )
        )
    ]
    for load in loads:
        load.start()
    total = jnp.zeros((2 * TOK, D), F32)
    for group in range(4):
        rows = jnp.concatenate([mixed_ref[group], mixed_ref[4 + group]], axis=0)
        total = total + mm(rows, wo_ref[group])
    loads[0].wait()
    total = total + tok_buf[...].reshape(2 * TOK, D).astype(F32)
    middle_buf[...] = total.reshape(8, BLK, D)
    third = pltpu.make_async_copy(
        middle_buf.at[lax.axis_index(MICRO) * 4 + group_index()], middle_ref, sem.at[2]
    )
    third.start()
    unit, _ = normalized(total)
    wait_all(loads[4:])
    normed = (unit * gain_buf[...].reshape(1, D) + shift_buf[...].reshape(1, D)).astype(BF)
    normed_ref[...] = normed
    loads[1].wait()
    pre = mm(normed, up_buf[...])
    cdf = 0.5 * (1.0 + lax.erf(pre * (0.5**0.5)))
    slope = cdf + pre * jnp.exp(-0.5 * pre * pre) * 0.3989422804014327
    loads[2].wait()
    loads[3].wait()
    grad_out = og_buf[...].reshape(2 * TOK, D)
    gpre = (mm_nt(grad_out, down_buf[...]) * slope).astype(BF)
    gpre_ref[...] = gpre
    grad_buf[...] = mm_nt(gpre, up_buf[...]).astype(BF).reshape(8, BLK, D)
    first = pltpu.make_async_copy(grad_buf, out_ref.at[:, pl.ds(BLK, BLK)], sem.at[0])
    first.start()
    act = (pre * cdf).astype(BF)
    act_ref[...] = act
    branch_buf[...] = mm(act, down_buf[...]).astype(BF).reshape(8, BLK, D)
    second = pltpu.make_async_copy(branch_buf, out_ref.at[:, pl.ds(0, BLK)], sem.at[1])
    second.start()
    wait_all([first, second, third])


def ff_grads_kernel(normed_ref, act_ref, gpre_ref, og_ref, keep_ref, send_ref, up_buf, down_buf):
    core = lax.axis_index(CORE)
    up_buf[...] = mm_tn(normed_ref[...], gpre_ref[...])
    down_buf[...] = mm_tn(act_ref[...], og_ref[...].reshape(2 * TOK, D))
    for ref, owner in ((keep_ref, core), (send_ref, 1 - core)):
        column = pl.multiple_of(owner * 384, 128)
        for tile in range(8):
            rows = pl.ds(pl.multiple_of((2 * tile + owner) * 48, 16), 48)
            ref[tile, :, :384] = up_buf[rows].astype(BF)
            ref[tile, :, 384:] = down_buf[tile * 48:(tile + 1) * 48, pl.ds(column, 384)].astype(BF)


def split_kernel(one_ref, two_ref, *refs):
    y = lax.axis_index("y")
    for k, ref in enumerate(refs):
        for xl in range(2):
            at = (y ^ k) * 2 + xl
            ref[xl] = (one_ref[at].astype(F32) + two_ref[at].astype(F32)).astype(BF)


def total_kernel(*refs):
    total = refs[0][...].astype(F32)
    for ref in refs[1:4]:
        total = total + ref[...].astype(F32)
    refs[4][...] = total.astype(BF)


def middle_kernel(
    sums_ref, middle_ref, og_ref, mixed_ref, wo_ref, gain_ref, query_ref,
    out_ref, low_ref, grad_ref, result_ref, vec_ref,
    buf, middle_buf, og_buf, mixed_buf, gain_buf, query_buf, low_buf, grad_buf, result_buf, vec_buf, in_sem, sem, rest_sem,
):
    micro = lax.axis_index(MICRO)
    group = group_index()
    block = pl.ds(pl.multiple_of(group * BLK, BLK), BLK)
    loads = [
        pltpu.make_async_copy(middle_ref, middle_buf, in_sem.at[0]),
        pltpu.make_async_copy(og_ref.at[micro, block], og_buf, in_sem.at[1]),
        pltpu.make_async_copy(mixed_ref.at[pl.ds(micro * 4, 4), block], mixed_buf, in_sem.at[2]),
        pltpu.make_async_copy(gain_ref, gain_buf, in_sem.at[3]),
        pltpu.make_async_copy(query_ref, query_buf, in_sem.at[4]),
    ]
    for load in loads:
        load.start()
    total = sums_ref[0].astype(F32)
    for index in range(1, 8):
        total = total + sums_ref[index].astype(F32)
    branch, grad = total[:BLK], total[BLK:]
    wait_all(loads)
    middle = middle_buf[...]
    unit, inverse = normalized(middle)
    grad_mid = og_buf[...].astype(F32) + norm_back(grad, unit, inverse, gain_buf[...].reshape(1, D))
    low = grad_mid.astype(BF)
    low_buf[...] = low
    grad_buf[...] = grad_mid
    result_buf[...] = (middle + branch).astype(BF)
    gain_grad = jnp.sum(grad * unit, axis=0, keepdims=True)
    shift_grad = jnp.sum(grad, axis=0, keepdims=True)
    vec_buf[...] = jnp.concatenate([gain_grad, shift_grad, jnp.zeros((6, D), F32)], axis=0)
    stores = [
        pltpu.make_async_copy(source, target, rest_sem.at[index])
        for index, (source, target) in enumerate(
            ((low_buf, low_ref), (grad_buf, grad_ref), (result_buf, result_ref), (vec_buf, vec_ref))
        )
    ]
    for store in stores:
        store.start()
    lane = lax.broadcasted_iota(jnp.int32, (BLK, 256), 1)
    for head_group in range(4):
        mixed = mixed_buf[head_group].astype(F32)
        back = mm_nt(low, wo_ref[head_group]).astype(BF).astype(F32)
        product = mixed * back
        columns = []
        for head in range(3):
            inside = (lane >= (head + 1) * HD) & (lane < (head + 2) * HD)
            columns += three(jnp.sum(jnp.where(inside, product, 0.0), axis=-1, keepdims=True))
        stats = put_columns(256, BLK, 9, columns)
        packed = jnp.where(lane < 9, mixed, jnp.where(lane < HD, stats, back)).astype(BF)
        query = query_buf[head_group]
        last = query[:, 128:192]
        buf[head_group, :32] = packed[:, :128]
        buf[head_group, 32:64] = packed[:, 128:]
        buf[head_group, 64:96] = query[:, :128]
        buf[head_group, 96:] = jnp.concatenate([last[:16], last[16:]], axis=1)
    sends = send_copies(buf, out_ref, range(8), sem)
    wait_all(stores)
    wait_all(sends)


def attend_back_kernel(
    scene_ref, kvs_ref, kvo_ref, gs_ref, go_ref, normed_ref, mixed_ref, low_ref, low1_ref, low2_ref, low3_ref,
    w_ref, gqkv_ref, w_out_ref, keep_ref, send_ref,
    kv_buf, grad_buf, mixed_buf, normed_buf, low_buf, kv_sem, in_sem, w_sem,
):
    first, big = span(scene_ref)
    chip = chip_index()
    core = lax.axis_index(CORE)
    group = group_index()
    index = lax.axis_index(MICRO) * 4 + group
    first_loads = [
        pltpu.make_async_copy(source, target, in_sem.at[slot])
        for slot, (source, target) in enumerate(
            ((normed_ref, normed_buf), (mixed_ref.at[index], mixed_buf), (low_ref, low_buf))
        )
    ]
    scale = HD**-0.5

    def run(count):
        rows = count * TOK
        loads = [pltpu.make_async_copy(kvs_ref.at[pl.ds(first, count)], kv_buf.at[pl.ds(0, count)], kv_sem)]
        for load in loads + first_loads:
            load.start()
        weight_copies(w_ref, w_out_ref, w_sem)

        def cut(value):
            return [value[:, at:at + 128] for at in range(0, value.shape[1], 128)]

        def unpacked(ref, start, tiles):
            blocks = [ref[pl.ds(start, tiles), :, at:at + 32] for at in (0, 32, 64)]
            last = ref[pl.ds(start, tiles), :, 96:]
            turned = jnp.concatenate([last[..., HD:], last[..., :HD]], axis=-1)
            blocks.append(jnp.concatenate([last, turned], axis=2))
            return [block.reshape(tiles * TOK, 128) for block in blocks]

        every = [
            jnp.concatenate(pair, axis=0)
            for pair in zip(*[unpacked(ref, first, count) for ref in (gs_ref, go_ref)])
        ]
        grad, query = every[:2], every[2:]
        g_own = unpacked(gs_ref, chip, 1)
        g_heads = [halves(g_own[0])[1], *halves(g_own[1])]
        own_stats = g_own[0].astype(F32)
        all_stats = grad[0].astype(F32).T
        wait_all(loads)
        kv = cut(jnp.concatenate(
            [kv_buf[:count].reshape(rows, 384), kvo_ref[pl.ds(first, count)].reshape(rows, 384)], axis=0
        ))
        own = cut(kv_buf[chip - first]) + g_own[2:]
        q_heads = [*halves(own[3]), halves(own[4])[0]]
        k_heads = [*halves(own[0]), halves(own[1])[0]]
        v_heads = [halves(own[1])[1], *halves(own[2])]

        def column(at):
            return own_stats[:, at:at + 1] + own_stats[:, at + 1:at + 2] + own_stats[:, at + 2:at + 3]

        def row(at):
            return all_stats[at:at + 1] + all_stats[at + 1:at + 2] + all_stats[at + 2:at + 3]

        dq, dk, dv = [], [], []
        for head, (kb, vb) in enumerate(((0, 1), (0, 2), (1, 2))):
            qb, gb = (0, 0, 1)[head], (0, 1, 1)[head]
            probs = jnp.exp(mm_nt(q_heads[head], kv[kb]) * scale - column(3 * head))
            gap = mm_nt(g_heads[head], kv[vb]) - column(9 + 3 * head)
            dq.append(mm((probs * gap).astype(BF), kv[kb]) * scale)
            probs = jnp.exp(mm_nt(k_heads[head], query[qb]) * scale - row(3 * head))
            gap = mm_nt(v_heads[head], grad[gb]) - row(9 + 3 * head)
            dv.append(mm(probs.astype(BF), grad[gb]))
            dk.append(mm((probs * gap).astype(BF), query[qb]) * scale)
        tail = dq[2]
        gqkv_ref[...] = jnp.concatenate(
            [join(dk[0], dk[1]), join(dk[2], dv[0]), join(dv[1], dv[2]), join(dq[0], dq[1]),
             join(tail, jnp.zeros_like(tail))],
            axis=1,
        ).astype(BF)


    @pl.when(big)
    def _():
        run(5)

    @pl.when(jnp.logical_not(big))
    def _():
        run(1)

    wait_all(first_loads)

    grad_buf[...] = mm_tn(normed_buf[...], gqkv_ref[...])
    low = jnp.concatenate([ref[...] for ref in (low_buf, low1_ref, low2_ref, low3_ref)], axis=0)
    mixed = jnp.concatenate(
        [mixed_buf[pl.ds(pl.multiple_of((group ^ k) * BLK, BLK), BLK)] for k in range(4)], axis=0
    )
    out = mm_tn(mixed, low)[HD:]
    for ref, owner in ((keep_ref, core), (send_ref, 1 - core)):
        for tile in range(8):
            rows = grad_buf[pl.ds(pl.multiple_of((2 * tile + owner) * 48, 16), 48)]
            at = (tile // 4) * 96
            pieces = [
                out[at + row * 48:at + (row + 1) * 48, (tile % 4) * 192:(tile % 4 + 1) * 192] for row in range(2)
            ]
            ref[2 * tile] = rows[:, :384].astype(BF)
            ref[2 * tile + 1] = jnp.concatenate(
                [rows[:, 384:576], jnp.where(owner == 1, pieces[1], pieces[0])], axis=1
            ).astype(BF)
    wait_all(weight_copies(w_ref, w_out_ref, w_sem, start=False))


def normed_grad_kernel(
    gqkv_ref, w_ref, tok_ref, vec_ref, near_ref, far_ref, own_ref, one_ref, two_ref, three_ref, sums_ref, ff_ref,
    x_buf, vec_buf, near_buf, part_buf, low_buf, sums_buf, ff_buf, rows_buf, in_sem, out_sem, row_sem,
):
    loads = [
        pltpu.make_async_copy(tok_ref.at[lax.axis_index(MICRO)], x_buf, in_sem.at[0]),
        pltpu.make_async_copy(vec_ref, vec_buf, in_sem.at[1]),
        pltpu.make_async_copy(near_ref, near_buf, in_sem.at[2]),
    ]
    for load in loads:
        load.start()
    group = group_index()
    odd = (group % 2) == 1
    total = jnp.zeros((TOK, D), F32)
    for slot in range(3):
        part = gqkv_ref[:, slot * 192:(slot + 1) * 192]
        zero = jnp.zeros_like(part)
        wide = jnp.where(
            odd, jnp.concatenate([zero, part], axis=1), jnp.concatenate([part, zero], axis=1)
        )
        total = total + mm_nt(wide, w_ref[slot])
    part_buf[...] = total
    low_buf[...] = total.astype(BF)
    stores = []
    for k, ref in enumerate((own_ref, one_ref, two_ref, three_ref)):
        rows = pl.ds(pl.multiple_of((group ^ k) * BLK, BLK), BLK)
        target = ref.at[pl.ds(0, BLK)] if k else ref
        stores.append(pltpu.make_async_copy((low_buf if k else part_buf).at[rows], target, out_sem.at[k]))
        stores[-1].start()
    wait_all(loads)
    ff_buf[...] = (near_buf[...].astype(F32) + far_ref[...].astype(F32)).astype(BF)
    stores.append(pltpu.make_async_copy(ff_buf, ff_ref, out_sem.at[5]))
    stores[-1].start()
    unit, _ = normalized(x_buf[...].astype(F32))
    gain1 = jnp.sum(total * unit, axis=0, keepdims=True)
    shift1 = jnp.sum(total, axis=0, keepdims=True)
    vectors = jnp.concatenate([gain1, shift1, vec_buf[...][:2], jnp.zeros((4, D), F32)], axis=0)
    sums_buf[...] = vectors
    for index in range(4):
        rows_buf[index] = jnp.concatenate(
            [vectors[index:index + 1], jnp.zeros((15, D), F32)], axis=0
        ).astype(BF)
    for k, ref in enumerate((one_ref, two_ref, three_ref)):
        stores.append(
            pltpu.make_async_copy(rows_buf.at[group ^ (k + 1)], ref.at[pl.ds(BLK, 16)], row_sem.at[k])
        )
        stores[-1].start()
    stores.append(pltpu.make_async_copy(sums_buf, sums_ref, out_sem.at[4]))
    stores[-1].start()
    wait_all(stores)


def add_kernel(one_ref, two_ref, unused_ref, out_ref, buf, sem):
    buf[...] = (one_ref[...].astype(F32) + two_ref[...].astype(F32)).astype(BF)
    copy = pltpu.make_async_copy(buf, out_ref, sem)
    copy.start()
    copy.wait()


def sum_kernel(in_ref, vec_ref, one_ref, two_ref, three_ref, out_ref, buf, vec_buf, row_buf, sem, vec_sem, row_sem):
    loads = [pltpu.make_async_copy(vec_ref, vec_buf, vec_sem)] + [
        pltpu.make_async_copy(ref.at[pl.ds(BLK, 16)], row_buf.at[k], row_sem.at[k])
        for k, ref in enumerate((one_ref, two_ref, three_ref))
    ]
    for load in loads:
        load.start()
    total = in_ref[0].astype(F32)
    for index in range(1, 16):
        total = total + in_ref[index].astype(F32)
    wait_all(loads)
    vector = vec_buf[pl.ds(group_index(), 1)]
    for k in range(3):
        vector = vector + row_buf[k].astype(F32)[:1]
    rows = [vector[:, at:at + 128] for at in range(0, D, 128)] + [jnp.zeros((2, 128), F32)]
    pieces = [total[at:at + 8] for at in range(0, 48, 8)] + [jnp.concatenate(rows, axis=0)]
    block = jnp.concatenate(pieces, axis=1).astype(BF)
    for index in range(8):
        buf[index] = block
    wait_all(send_copies(buf, out_ref, range(8), sem))


def spread_kernel(turn, in_ref, *refs):
    qkv_buf, out_buf, sem, out_sem = refs[-4:]
    if turn:
        in_buf, in_sem = refs[-6:-4]
        qkv_ref, out_ref, *vec_refs = refs[3:-6]
        loads = [pltpu.make_async_copy(in_ref.at[tile], in_buf.at[tile], in_sem.at[tile]) for tile in range(8)]
        for load in loads:
            load.start()
    else:
        qkv_ref, out_ref, *vec_refs = refs[:-4]
        in_buf = in_ref
    owner = lax.axis_index(CORE)
    owner = 1 - owner if turn else owner
    copies = []
    vectors = [jnp.zeros((8, 128), F32)] * 4
    for tile in range(8):
        if turn:
            loads[tile].wait()
        whole = [in_buf[tile, index].astype(F32) for index in range(8)]
        block = [
            jnp.concatenate([value[:, at:at + 384] for at in range(0, 2304, 384)], axis=0) for value in whole
        ]
        vectors = [total + whole[k][:, 2304:] + whole[4 + k][:, 2304:] for k, total in enumerate(vectors)]
        for part, half, at in ((1, 0, 0), (2, 0, 192), (0, 4, 0)):
            qkv_buf[tile, :, part * D:(part + 1) * D] = jnp.concatenate(
                [block[half + group][:, at:at + 192] for group in range(4)], axis=1
            )
        start = pl.multiple_of((2 * tile + owner) * 48, 16)
        copy = pltpu.make_async_copy(qkv_buf.at[tile], qkv_ref.at[pl.ds(start, 48)], sem.at[tile])
        copy.start()
        copies.append(copy)
        for group in range(4):
            out_buf[group, tile // 4, :, (tile % 4) * 192:(tile % 4 + 1) * 192] = block[4 + group][:, 192:]
    for group in range(4):
        for pair in range(2):
            start = pl.multiple_of(group * 192 + (pair * 2 + owner) * 48, 16)
            copy = pltpu.make_async_copy(
                out_buf.at[group, pair], out_ref.at[pl.ds(start, 48)], out_sem.at[group, pair]
            )
            copy.start()
            copies.append(copy)
    if turn:
        for k, ref in enumerate(vec_refs):
            total = vectors[k] + refs[0][k]
            ref[...] = jnp.concatenate([total[row:row + 1] for row in range(6)], axis=1).reshape(D)
    else:
        for k, total in enumerate(vectors):
            vec_refs[0][k] = total
    wait_all(copies)


def spread_ff_kernel(turn, *refs):
    up_ref, down_ref, up_buf, down_buf, up_sem, down_sem = refs[-6:]
    y, core = lax.axis_index("y"), lax.axis_index(CORE)
    owner = 1 - core if turn else core
    copies = []
    for near in range(4):
        for xl in range(2):
            chip = (y ^ near) * 2 + xl
            block = refs[near][xl].astype(F32)
            up_buf[near, xl] = block[:, :384]
            down_buf[near, xl] = block[:, 384:]
            up_rows = pl.ds(pl.multiple_of((chip * 2 + owner) * 48, 16), 48)
            down_rows = pl.ds(pl.multiple_of(chip * 48, 16), 48)
            columns = pl.ds(pl.multiple_of(owner * 384, 128), 384)
            copies.append(pltpu.make_async_copy(up_buf.at[near, xl], up_ref.at[up_rows], up_sem.at[near, xl]))
            copies.append(
                pltpu.make_async_copy(down_buf.at[near, xl], down_ref.at[down_rows, columns], down_sem.at[near, xl])
            )
            copies[-2].start()
            copies[-1].start()
    wait_all(copies)


def input_kernel(
    own_ref, one_ref, two_ref, three_ref, tok_ref, gain_ref, grad_ref, result_ref, unused_ref, out_ref, buf, x_buf, sem, x_sem
):
    start = pl.multiple_of(group_index() * BLK, BLK)
    load = pltpu.make_async_copy(tok_ref.at[lax.axis_index(MICRO), pl.ds(start, BLK)], x_buf, x_sem)
    load.start()
    load.wait()
    total = own_ref[...]
    for ref in (one_ref, two_ref, three_ref):
        total = total + ref[:BLK].astype(F32)
    unit, inverse = normalized(x_buf[...].astype(F32))
    grad = grad_ref[...] + norm_back(total, unit, inverse, gain_ref[...].reshape(1, D))
    buf[:BLK] = grad.astype(BF)
    buf[BLK:] = result_ref[...]
    wait_all(send_copies(buf, out_ref, range(8), sem))


def unpack_kernel(in_ref, unused_ref, other_ref, grad_ref, result_ref):
    for index in range(8):
        rows = slice(index % 4 * BLK, (index % 4 + 1) * BLK)
        grad_ref[index // 4, rows] = in_ref[index, :BLK].astype(F32)
        result_ref[index // 4, rows] = in_ref[index, BLK:]


def exchange(value, axes):
    return lax.all_to_all(value, axes, 0, 0, tiled=True)


def swap(value):
    return lax.ppermute(value, CORE, [(0, 1), (1, 0)])


def after(value, *others):
    return pl.pallas_call(
        lambda *refs: None,
        out_shape=jax.ShapeDtypeStruct(value.shape, value.dtype),
        in_specs=[pl.BlockSpec(memory_space=pl.ANY)] * (1 + len(others)),
        out_specs=pl.BlockSpec(memory_space=pl.ANY),
        input_output_aliases={0: 0},
        cost_estimate=pl.CostEstimate(flops=1, bytes_accessed=1, transcendentals=0),
        compiler_params=pltpu.CompilerParams(vmem_limit_bytes=2**20),
    )(value, *others)


def flip(value, axes, count, bits):
    return lax.ppermute(value, axes, [(index, index ^ bits) for index in range(count)])


def shards(
    tokens, scene_of_block, ln1_gain, ln1_shift, w_qkv, w_out, ln2_gain, ln2_shift, w_up, w_down, out_grad
):
    w_out_pad = jnp.pad(w_out.reshape(4, 192, D), ((0, 0), (HD, 0), (0, 0)))
    kv_send, normed = call(
        project_kernel,
        [((8, TOK, 384), BF, "H"), ((TOK, D), BF, "L")],
        [(tokens, "H"), (ln1_gain, "H"), (ln1_shift, "H"), (w_qkv, "H")],
        1000,
        [
            pltpu.VMEM((TOK, D), BF), pltpu.VMEM((2, D, 384), BF), pltpu.VMEM((TOK, 384), BF),
            pltpu.VMEM((D,), F32), pltpu.VMEM((D,), F32), DMA, DMA((2,)), DMA((8,)), DMA, DMA,
        ],
    )
    (query,) = call(
        query_kernel,
        [((TOK, 256), BF, "L")],
        [(normed, "L"), (w_qkv, "H")],
        1000,
        [pltpu.VMEM((1, D, 384), BF), DMA((1,))],
    )
    kv_same = exchange(kv_send, CHIP)
    kv_same = after(kv_same, pin(query))
    kv_other = swap(kv_same)
    (mixed_send,) = call(
        attend_kernel,
        [((8, TOK, 256), BF, "H")],
        [(scene_of_block, "S"), (query, "H"), (kv_same, "V"), (kv_other, "V")],
        1000,
        [pltpu.VMEM((TOK, 256), BF), pltpu.VMEM((TOK, 256), BF), DMA((8,)), DMA],
    )
    mixed = exchange(mixed_send, NARROW)
    (block_query,) = call(
        block_query_kernel,
        [((4, BLK, 256), BF, "L")],
        [(normed, "H"), (w_qkv, "H")],
        1000,
        [pltpu.VMEM((BLK, D), BF), pltpu.VMEM((D, D), BF), DMA, DMA],
    )
    ff_send, middle, normed2, act, grad_pre = call(
        forward_kernel,
        [
            ((8, 2 * BLK, D), BF, "H"), ((BLK, D), F32, "H"), ((2 * TOK, D), BF, "V"),
            ((2 * TOK, FFL), BF, "V"), ((2 * TOK, FFL), BF, "V"),
        ],
        [
            (mixed, "V"), (tokens, "H"), (out_grad, "H"), (w_out_pad, "V"), (ln2_gain, "H"), (ln2_shift, "H"),
            (w_up, "H"), (w_down, "H"),
        ],
        1000,
        [
            pltpu.VMEM((2, TOK, D), BF), pltpu.VMEM((2, TOK, D), BF), pltpu.VMEM((D, FFL), BF),
            pltpu.VMEM((FFL, D), BF), pltpu.VMEM((D,), F32), pltpu.VMEM((D,), F32), pltpu.VMEM((8, BLK, D), BF),
            pltpu.VMEM((8, BLK, D), BF), pltpu.VMEM((8, BLK, D), F32), DMA((6,)), DMA((3,)),
        ],
    )
    ff_sums = exchange(ff_send, NARROW)
    keep, send = call(
        ff_grads_kernel,
        [((8, 48, D), BF, "V")] * 2,
        [(normed2, "V"), (act, "V"), (grad_pre, "V"), (out_grad, "L")],
        1000,
        [pltpu.VMEM((D, FFL), F32), pltpu.VMEM((FFL, D), F32)],
    )
    pieces = call(
        split_kernel, [((2, 48, D), BF, "L")] * 4, [(keep, "V"), (swap(send), "V")], 1000
    )
    pieces = [pieces[0]] + [flip(pieces[k], "y", 4, k) for k in (1, 2, 3)]
    (ff_near,) = call(
        total_kernel,
        [((2, 48, D), BF, "L")],
        [(pieces[0], "L")] + [(piece, "V") for piece in pieces[1:]],
        1000,
    )
    grad_send, low, grad_mid, result_part, vec2 = call(
        middle_kernel,
        [
            ((8, 4, 112, 128), BF, "H"), ((BLK, D), BF, "H"), ((BLK, D), F32, "H"), ((BLK, D), BF, "H"),
            ((8, D), F32, "H"),
        ],
        [
            (ff_sums, "V"), (middle, "H"), (out_grad, "H"), (mixed, "H"), (w_out_pad, "V"), (ln2_gain, "H"),
            (block_query, "H"),
        ],
        1000,
        [
            pltpu.VMEM((4, 112, 128), BF), pltpu.VMEM((BLK, D), F32), pltpu.VMEM((BLK, D), BF),
            pltpu.VMEM((4, BLK, 256), BF), pltpu.VMEM((D,), F32), pltpu.VMEM((4, BLK, 256), BF), pltpu.VMEM((BLK, D), BF), pltpu.VMEM((BLK, D), F32),
            pltpu.VMEM((BLK, D), BF), pltpu.VMEM((8, D), F32), DMA((5,)), DMA((8,)), DMA((4,)),
        ],
    )
    grad_send = after(pin(grad_send), *pieces[1:])
    grad_same = exchange(grad_send.reshape(32, 112, 128), (*CHIP, *GROUP)).reshape(8, 4, 112, 128)
    lows = [flip(low, GROUP, 4, k) for k in (1, 2, 3)]
    kv_same = after(pin(kv_same), low)
    kv_other = swap(kv_same)
    grad_same = after(grad_same, *lows, kv_other, pin(ff_near))
    grad_other = swap(grad_same)
    ff_near = after(pin(ff_near), grad_other)
    ff_far = flip(ff_near, "xl", 2, 1)
    gqkv, w_own, keep, send = call(
        attend_back_kernel,
        [((TOK, 640), BF, "V"), ((3, D, 384), BF, "V")] + [((16, 48, 384), BF, "V")] * 2,
        [
            (scene_of_block, "S"), (kv_same, "H"), (kv_other, "V"), (grad_same, "V"), (grad_other, "V"),
            (normed, "H"), (mixed, "H"), (low, "H"), *[(value, "V") for value in lows], (w_qkv, "H"),
        ],
        1000,
        [
            pltpu.VMEM((5, TOK, 384), BF), pltpu.VMEM((D, 640), F32),
            pltpu.VMEM((TOK, 256), BF), pltpu.VMEM((TOK, D), BF), pltpu.VMEM((BLK, D), BF),
            DMA, DMA((3,)), DMA((3,)),
        ],
        vmem=24,
    )
    own, *sends, sums, ff_part = call(
        normed_grad_kernel,
        [((BLK, D), F32, "H")] + [((BLK + 16, D), BF, "H")] * 3 + [((8, D), F32, "H"), ((2, 48, D), BF, "H")],
        [(gqkv, "V"), (w_own, "V"), (tokens, "H"), (vec2, "H"), (ff_near, "H"), (ff_far, "V")],
        1000,
        [
            pltpu.VMEM((TOK, D), BF), pltpu.VMEM((8, D), F32), pltpu.VMEM((2, 48, D), BF), pltpu.VMEM((TOK, D), F32),
            pltpu.VMEM((TOK, D), BF), pltpu.VMEM((8, D), F32), pltpu.VMEM((2, 48, D), BF), pltpu.VMEM((4, 16, D), BF),
            DMA((3,)), DMA((6,)), DMA((3,)),
        ],
    )
    (weight_send,) = call(
        add_kernel,
        [((16, 48, 384), BF, "H")],
        [(keep, "V"), (swap(after(send, ff_far)), "V"), (own, "H")],
        1000,
        [pltpu.VMEM((16, 48, 384), BF), DMA],
    )
    weight_parts = exchange(weight_send, (*CHIP, MICRO))
    parts = [flip(value, GROUP, 4, k + 1) for k, value in enumerate(sends)]
    weight_parts = after(weight_parts, pin(sums), *parts)
    ff_parts = [flip(ff_part, "y", 4, k) for k in (1, 2, 3)]
    (weight_total,) = call(
        sum_kernel,
        [((8, 8, 8, 2432), BF, "H")],
        [(weight_parts, "V"), (sums, "H"), *[(value, "A") for value in parts]],
        1000,
        [
            pltpu.VMEM((8, 8, 2432), BF), pltpu.VMEM((8, D), F32), pltpu.VMEM((3, 16, D), BF), DMA((8,)), DMA,
            DMA((3,)),
        ],
    )
    (packed,) = call(
        input_kernel,
        [((8, 2 * BLK, D), BF, "H")],
        [
            (own, "L"), *[(value, "V") for value in parts], (tokens, "H"), (ln1_gain, "L"), (grad_mid, "L"),
            (result_part, "L"), (weight_total, "H"),
        ],
        1000,
        [pltpu.VMEM((2 * BLK, D), BF), pltpu.VMEM((BLK, D), BF), DMA((8,)), DMA],
    )
    weight_same = exchange(weight_total.reshape(64, 8, 2432), (*CHIP, *NARROW)).reshape(8, 8, 8, 2432)
    weight_same = after(weight_same, pin(packed))
    weight_other = swap(weight_same)
    scratch = [
        pltpu.VMEM((8, 48, 3 * D), F32), pltpu.VMEM((4, 2, 48, D), F32), DMA((8,)), DMA((4, 2)),
    ]
    grads = [((D, 3 * D), F32, "H"), ((D, D), F32, "H")]
    half = call(
        functools.partial(spread_kernel, False),
        grads + [((4, 8, 128), F32, "V")],
        [(weight_same, "V")],
        1000,
        scratch,
    )
    everyone = exchange(after(pin(packed), half[2]), NARROW)
    qkv_grad, out_proj_grad, *vectors = call(
        functools.partial(spread_kernel, True),
        grads + [((D,), F32, "L")] * 4,
        [(weight_other, "H"), (half[2], "V"), (half[0], "H"), (half[1], "H")],
        1000,
        [pltpu.VMEM((8, 8, 8, 2432), BF), DMA((8,))] + scratch,
        aliases={2: 0, 3: 1},
    )
    ff_parts = [after(value, pin(vectors[0])) for value in ff_parts]
    ff_swapped = [swap(value) for value in (ff_part, *ff_parts)]
    ff_grads = [((D, FFL), F32, "H"), ((FFL, D), F32, "H")]
    ff_scratch = [
        pltpu.VMEM((4, 2, 48, FFL), F32), pltpu.VMEM((4, 2, 48, FFL), F32), DMA((4, 2)), DMA((4, 2)),
    ]
    ff_half = call(
        functools.partial(spread_ff_kernel, False),
        ff_grads,
        [(ff_part, "L"), *[(value, "V") for value in ff_parts]],
        1000,
        ff_scratch,
    )
    up_grad, down_grad = call(
        functools.partial(spread_ff_kernel, True),
        ff_grads,
        [*[(value, "V") for value in ff_swapped], (ff_half[0], "H"), (ff_half[1], "H")],
        1000,
        ff_scratch,
        aliases={4: 0, 5: 1},
    )
    input_grad, result = call(
        unpack_kernel, [((2, TOK, D), F32, "L"), ((2, TOK, D), BF, "L")], [(everyone, "V"), (vectors[0], "H"), (up_grad, "H")], 1000
    )
    return (
        result, input_grad, qkv_grad, out_proj_grad, *vectors, up_grad, down_grad
    )


def solution(mesh):
    names = ("y", "xl", "c", "zh", "zl", "xh")
    fine = Mesh(mesh.devices.reshape(4, 2, 2, 2, 2, 2), names)
    tokens = P(None, WIDE, None)
    placed = (
        tokens, P(), P(), P(), P(), P(), P(), P(), P(None, NARROW), P(NARROW, None), tokens
    )
    return jax.shard_map(
        shards,
        mesh=fine,
        in_specs=placed,
        out_specs=(
            tokens, tokens, P(), P(), P(), P(), P(), P(), P(None, NARROW), P(NARROW, None)
        ),
        check_vma=False,
    )
```

```python
import functools

import jax
import jax.numpy as jnp
from jax import lax
from jax.experimental import pallas as pl
from jax.experimental.pallas import tpu as pltpu
from jax.sharding import Mesh
from jax.sharding import PartitionSpec as P

D = 768
HD = 64
FFL = 384
TOK = 128
BLK = 32
EPS = 1e-05
BF = jnp.bfloat16
F32 = jnp.float32

CHIP = ("y", "xl")
CORE = "c"
MICRO = "zh"
GROUP = ("zl", "xh")
NARROW = (MICRO, *GROUP)
WIDE = (*CHIP, CORE)


def chip_index():
    return lax.axis_index("y") * 2 + lax.axis_index("xl")


def group_index():
    return lax.axis_index("zl") * 2 + lax.axis_index("xh")


def mm(left, right):
    return lax.dot_general(left, right, (((1,), (0,)), ((), ())), preferred_element_type=F32)


def mm_nt(left, right):
    return lax.dot_general(left, right, (((1,), (1,)), ((), ())), preferred_element_type=F32)


def mm_tn(left, right):
    return lax.dot_general(left, right, (((0,), (0,)), ((), ())), preferred_element_type=F32)


def normalized(values):
    center = values - jnp.mean(values, axis=-1, keepdims=True)
    spread = jnp.mean(center * center, axis=-1, keepdims=True)
    inverse = lax.rsqrt(spread + EPS)
    return center * inverse, inverse


def norm_back(grad, unit, inverse, gain):
    scaled = grad * gain
    first = jnp.mean(scaled, axis=-1, keepdims=True)
    second = jnp.mean(scaled * unit, axis=-1, keepdims=True)
    return inverse * (scaled - first - unit * second)


def halves(block):
    lane = lax.broadcasted_iota(jnp.int32, block.shape, 1)
    zero = jnp.zeros_like(block)
    return jnp.where(lane < HD, block, zero), jnp.where(lane < HD, zero, block)


def join(low, high):
    lane = lax.broadcasted_iota(jnp.int32, low.shape, 1)
    return jnp.where(lane < HD, low, high)


def span(scene_ref):
    micro = lax.axis_index(MICRO)
    own = scene_ref[micro, chip_index() * 4]
    first = jnp.int32(0)
    count = jnp.int32(0)
    for index in range(8):
        other = scene_ref[micro, index * 4]
        first += (other < own).astype(jnp.int32)
        count += (other == own).astype(jnp.int32)
    return first, count > 1


def three(value):
    a = value.astype(BF).astype(F32)
    b = (value - a).astype(BF).astype(F32)
    c = value - a - b
    return a, b, c


def put_columns(width, rows, start, columns):
    lane = lax.broadcasted_iota(jnp.int32, (rows, width), 1)
    out = jnp.zeros((rows, width), F32)
    for offset, column in enumerate(columns):
        out = jnp.where(lane == start + offset, column, out)
    return out


def pin(value):
    return pltpu.with_memory_space_constraint(value, pltpu.HBM)


def call(kernel, outs, ins, cost, scratch=(), vmem=16, aliases=None):
    places = {"V": pltpu.VMEM, "H": pltpu.HBM, "S": pltpu.SMEM, "L": pltpu.VMEM, "A": pl.ANY}
    return pl.pallas_call(
        kernel,
        out_shape=[
            (pltpu.HBM if place in "HL" else jax.ShapeDtypeStruct)(shape, dtype) for shape, dtype, place in outs
        ],
        in_specs=[pl.BlockSpec(memory_space=places[place]) for _, place in ins],
        out_specs=[pl.BlockSpec(memory_space=places[place]) for _, _, place in outs],
        scratch_shapes=list(scratch),
        input_output_aliases=aliases or {},
        cost_estimate=pl.CostEstimate(flops=cost, bytes_accessed=1000, transcendentals=0),
        compiler_params=pltpu.CompilerParams(vmem_limit_bytes=vmem * 2**20),
    )(*[pin(value) if place in "HL" else value for value, place in ins])


DMA = pltpu.SemaphoreType.DMA


def send_copies(source, target, indices, sem):
    copies = [pltpu.make_async_copy(source, target.at[index], sem.at[index]) for index in indices]
    for copy in copies:
        copy.start()
    return copies


def wait_all(copies):
    for copy in copies:
        copy.wait()


def weight_copies(w_ref, w_buf, w_sem, parts=(1, 2, 0), start=True):
    group = group_index()
    copies = []
    for slot, part in enumerate(parts):
        column = pl.multiple_of(part * D + (group // 2) * 384, 128)
        copy = pltpu.make_async_copy(w_ref.at[:, pl.ds(column, 384)], w_buf.at[slot], w_sem.at[slot])
        if start:
            copy.start()
        copies.append(copy)
    return copies


def own_heads(full):
    odd = (group_index() % 2) == 1
    return jnp.where(odd, full[:, 192:], full[:, :192]).astype(BF)


def project_kernel(
    tok_ref, gain_ref, shift_ref, w_ref, kv_ref, normed_ref,
    x_buf, w_buf, kv_buf, gain_buf, shift_buf, x_sem, w_sem, kv_sem, gain_sem, shift_sem,
):
    copy_x = pltpu.make_async_copy(tok_ref.at[lax.axis_index(MICRO)], x_buf, x_sem)
    copy_x.start()
    copy_gain = pltpu.make_async_copy(gain_ref, gain_buf, gain_sem)
    copy_gain.start()
    copy_shift = pltpu.make_async_copy(shift_ref, shift_buf, shift_sem)
    copy_shift.start()
    copies = weight_copies(w_ref, w_buf, w_sem, (1, 2))
    wait_all([copy_x, copy_gain, copy_shift])
    unit, _ = normalized(x_buf[...].astype(F32))
    normed = (unit * gain_buf[...].reshape(1, D) + shift_buf[...].reshape(1, D)).astype(BF)
    normed_ref[...] = normed
    parts = []
    for slot in range(2):
        copies[slot].wait()
        parts.append(own_heads(mm(normed, w_buf[slot])))
    kv_buf[...] = jnp.concatenate(parts, axis=1)
    wait_all(send_copies(kv_buf, kv_ref, range(8), kv_sem))


def query_kernel(normed_ref, w_ref, q_ref, w_buf, w_sem):
    weight_copies(w_ref, w_buf, w_sem, (0,))[0].wait()
    part = own_heads(mm(normed_ref[...], w_buf[0]))
    q_ref[...] = jnp.concatenate([part, jnp.zeros((TOK, HD), BF)], axis=1)


def block_query_kernel(normed_ref, w_ref, out_ref, x_buf, w_buf, x_sem, w_sem):
    block = pl.ds(pl.multiple_of(group_index() * BLK, BLK), BLK)
    loads = [
        pltpu.make_async_copy(normed_ref.at[block], x_buf, x_sem),
        pltpu.make_async_copy(w_ref.at[:, pl.ds(0, D)], w_buf, w_sem),
    ]
    for load in loads:
        load.start()
    wait_all(loads)
    query = mm(x_buf[...], w_buf[...]).astype(BF)
    zero = jnp.zeros((BLK, HD), BF)
    for group in range(4):
        out_ref[group] = jnp.concatenate([query[:, group * 192:(group + 1) * 192], zero], axis=1)


def attend_kernel(scene_ref, q_ref, same_ref, other_ref, out_ref, buf, q_buf, sem, q_sem):
    load = pltpu.make_async_copy(q_ref, q_buf, q_sem)
    load.start()
    first, big = span(scene_ref)

    def run(count):
        rows = count * TOK
        keys = jnp.concatenate(
            [ref[pl.ds(first, count)].reshape(rows, 384) for ref in (same_ref, other_ref)], axis=0
        )
        load.wait()
        query = q_buf[...]
        q0, q1 = halves(query[:, :128])
        blocks = [keys[:, :128], keys[:, 128:256], keys[:, 256:]]
        mixed = []
        columns = []
        for qh, kb, vb in ((q0, 0, 1), (q1, 0, 2), (query[:, 128:], 1, 2)):
            scores = mm_nt(qh, blocks[kb]) * (HD**-0.5)
            top = jnp.max(scores, axis=-1, keepdims=True)
            weights = jnp.exp(scores - top)
            total = jnp.sum(weights, axis=-1, keepdims=True)
            probs = (weights * (1.0 / total)).astype(BF)
            mixed.append(mm(probs, blocks[vb]))
            columns += three(top + jnp.log(total))
        stats = put_columns(128, TOK, 0, columns)
        buf[...] = jnp.concatenate([join(stats, mixed[0]), join(mixed[1], mixed[2])], axis=1).astype(BF)

    @pl.when(big)
    def _():
        run(5)

    @pl.when(jnp.logical_not(big))
    def _():
        run(1)

    wait_all(send_copies(buf, out_ref, range(8), sem))


def forward_kernel(
    mixed_ref, tok_ref, og_ref, wo_ref, gain_ref, shift_ref, up_ref, down_ref,
    out_ref, middle_ref, normed_ref, act_ref, gpre_ref,
    tok_buf, og_buf, up_buf, down_buf, gain_buf, shift_buf, grad_buf, branch_buf, middle_buf, in_sem, sem,
):
    loads = [
        pltpu.make_async_copy(ref, buf, in_sem.at[index])
        for index, (ref, buf) in enumerate(
            (
                (tok_ref, tok_buf), (up_ref, up_buf), (og_ref, og_buf), (down_ref, down_buf), (gain_ref, gain_buf),
                (shift_ref, shift_buf),
            )
        )
    ]
    for load in loads:
        load.start()
    total = jnp.zeros((2 * TOK, D), F32)
    for group in range(4):
        rows = jnp.concatenate([mixed_ref[group], mixed_ref[4 + group]], axis=0)
        total = total + mm(rows, wo_ref[group])
    loads[0].wait()
    total = total + tok_buf[...].reshape(2 * TOK, D).astype(F32)
    middle_buf[...] = total.reshape(8, BLK, D)
    third = pltpu.make_async_copy(
        middle_buf.at[lax.axis_index(MICRO) * 4 + group_index()], middle_ref, sem.at[2]
    )
    third.start()
    unit, _ = normalized(total)
    wait_all(loads[4:])
    normed = (unit * gain_buf[...].reshape(1, D) + shift_buf[...].reshape(1, D)).astype(BF)
    normed_ref[...] = normed
    loads[1].wait()
    pre = mm(normed, up_buf[...])
    cdf = 0.5 * (1.0 + lax.erf(pre * (0.5**0.5)))
    slope = cdf + pre * jnp.exp(-0.5 * pre * pre) * 0.3989422804014327
    loads[2].wait()
    loads[3].wait()
    grad_out = og_buf[...].reshape(2 * TOK, D)
    gpre = (mm_nt(grad_out, down_buf[...]) * slope).astype(BF)
    gpre_ref[...] = gpre
    grad_buf[...] = mm_nt(gpre, up_buf[...]).astype(BF).reshape(8, BLK, D)
    first = pltpu.make_async_copy(grad_buf, out_ref.at[:, pl.ds(BLK, BLK)], sem.at[0])
    first.start()
    act = (pre * cdf).astype(BF)
    act_ref[...] = act
    branch_buf[...] = mm(act, down_buf[...]).astype(BF).reshape(8, BLK, D)
    second = pltpu.make_async_copy(branch_buf, out_ref.at[:, pl.ds(0, BLK)], sem.at[1])
    second.start()
    wait_all([first, second, third])


def ff_grads_kernel(normed_ref, act_ref, gpre_ref, og_ref, keep_ref, send_ref, up_buf, down_buf):
    core = lax.axis_index(CORE)
    up_buf[...] = mm_tn(normed_ref[...], gpre_ref[...])
    down_buf[...] = mm_tn(act_ref[...], og_ref[...].reshape(2 * TOK, D))
    for ref, owner in ((keep_ref, core), (send_ref, 1 - core)):
        column = pl.multiple_of(owner * 384, 128)
        for tile in range(8):
            rows = pl.ds(pl.multiple_of((2 * tile + owner) * 48, 16), 48)
            ref[tile, :, :384] = up_buf[rows].astype(BF)
            ref[tile, :, 384:] = down_buf[tile * 48:(tile + 1) * 48, pl.ds(column, 384)].astype(BF)


def split_kernel(one_ref, two_ref, *refs):
    y = lax.axis_index("y")
    for k, ref in enumerate(refs):
        for xl in range(2):
            at = (y ^ k) * 2 + xl
            ref[xl] = (one_ref[at].astype(F32) + two_ref[at].astype(F32)).astype(BF)


def total_kernel(*refs):
    total = refs[0][...].astype(F32)
    for ref in refs[1:4]:
        total = total + ref[...].astype(F32)
    refs[4][...] = total.astype(BF)


def middle_kernel(
    sums_ref, middle_ref, og_ref, mixed_ref, wo_ref, gain_ref, query_ref,
    out_ref, low_ref, grad_ref, result_ref, vec_ref,
    buf, middle_buf, og_buf, mixed_buf, gain_buf, query_buf, low_buf, grad_buf, result_buf, vec_buf, in_sem, sem, rest_sem,
):
    micro = lax.axis_index(MICRO)
    group = group_index()
    block = pl.ds(pl.multiple_of(group * BLK, BLK), BLK)
    loads = [
        pltpu.make_async_copy(middle_ref, middle_buf, in_sem.at[0]),
        pltpu.make_async_copy(og_ref.at[micro, block], og_buf, in_sem.at[1]),
        pltpu.make_async_copy(mixed_ref.at[pl.ds(micro * 4, 4), block], mixed_buf, in_sem.at[2]),
        pltpu.make_async_copy(gain_ref, gain_buf, in_sem.at[3]),
        pltpu.make_async_copy(query_ref, query_buf, in_sem.at[4]),
    ]
    for load in loads:
        load.start()
    total = sums_ref[0].astype(F32)
    for index in range(1, 8):
        total = total + sums_ref[index].astype(F32)
    branch, grad = total[:BLK], total[BLK:]
    wait_all(loads)
    middle = middle_buf[...]
    unit, inverse = normalized(middle)
    grad_mid = og_buf[...].astype(F32) + norm_back(grad, unit, inverse, gain_buf[...].reshape(1, D))
    low = grad_mid.astype(BF)
    low_buf[...] = low
    grad_buf[...] = grad_mid
    result_buf[...] = (middle + branch).astype(BF)
    gain_grad = jnp.sum(grad * unit, axis=0, keepdims=True)
    shift_grad = jnp.sum(grad, axis=0, keepdims=True)
    vec_buf[...] = jnp.concatenate([gain_grad, shift_grad, jnp.zeros((6, D), F32)], axis=0)
    stores = [
        pltpu.make_async_copy(source, target, rest_sem.at[index])
        for index, (source, target) in enumerate(
            ((low_buf, low_ref), (grad_buf, grad_ref), (result_buf, result_ref), (vec_buf, vec_ref))
        )
    ]
    for store in stores:
        store.start()
    lane = lax.broadcasted_iota(jnp.int32, (BLK, 256), 1)
    for head_group in range(4):
        mixed = mixed_buf[head_group].astype(F32)
        back = mm_nt(low, wo_ref[head_group]).astype(BF).astype(F32)
        product = mixed * back
        columns = []
        for head in range(3):
            inside = (lane >= (head + 1) * HD) & (lane < (head + 2) * HD)
            columns += three(jnp.sum(jnp.where(inside, product, 0.0), axis=-1, keepdims=True))
        stats = put_columns(256, BLK, 9, columns)
        packed = jnp.where(lane < 9, mixed, jnp.where(lane < HD, stats, back)).astype(BF)
        query = query_buf[head_group]
        last = query[:, 128:192]
        buf[head_group, :32] = packed[:, :128]
        buf[head_group, 32:64] = packed[:, 128:]
        buf[head_group, 64:96] = query[:, :128]
        buf[head_group, 96:] = jnp.concatenate([last[:16], last[16:]], axis=1)
    sends = send_copies(buf, out_ref, range(8), sem)
    wait_all(stores)
    wait_all(sends)


def attend_back_kernel(
    scene_ref, kvs_ref, kvo_ref, gs_ref, go_ref, normed_ref, mixed_ref, low_ref, low1_ref, low2_ref, low3_ref,
    w_ref, gqkv_ref, w_out_ref, keep_ref, send_ref,
    kv_buf, grad_buf, mixed_buf, normed_buf, low_buf, kv_sem, in_sem, w_sem,
):
    first, big = span(scene_ref)
    chip = chip_index()
    core = lax.axis_index(CORE)
    group = group_index()
    index = lax.axis_index(MICRO) * 4 + group
    first_loads = [
        pltpu.make_async_copy(source, target, in_sem.at[slot])
        for slot, (source, target) in enumerate(
            ((normed_ref, normed_buf), (mixed_ref.at[index], mixed_buf), (low_ref, low_buf))
        )
    ]
    scale = HD**-0.5

    def run(count):
        rows = count * TOK
        loads = [pltpu.make_async_copy(kvs_ref.at[pl.ds(first, count)], kv_buf.at[pl.ds(0, count)], kv_sem)]
        for load in loads + first_loads:
            load.start()
        weight_copies(w_ref, w_out_ref, w_sem)

        def cut(value):
            return [value[:, at:at + 128] for at in range(0, value.shape[1], 128)]

        def unpacked(ref, start, tiles):
            blocks = [ref[pl.ds(start, tiles), :, at:at + 32] for at in (0, 32, 64)]
            last = ref[pl.ds(start, tiles), :, 96:]
            turned = jnp.concatenate([last[..., HD:], last[..., :HD]], axis=-1)
            blocks.append(jnp.concatenate([last, turned], axis=2))
            return [block.reshape(tiles * TOK, 128) for block in blocks]

        every = [
            jnp.concatenate(pair, axis=0)
            for pair in zip(*[unpacked(ref, first, count) for ref in (gs_ref, go_ref)])
        ]
        grad, query = every[:2], every[2:]
        g_own = unpacked(gs_ref, chip, 1)
        g_heads = [halves(g_own[0])[1], *halves(g_own[1])]
        own_stats = g_own[0].astype(F32)
        all_stats = grad[0].astype(F32).T
        wait_all(loads)
        kv = cut(jnp.concatenate(
            [kv_buf[:count].reshape(rows, 384), kvo_ref[pl.ds(first, count)].reshape(rows, 384)], axis=0
        ))
        own = cut(kv_buf[chip - first]) + g_own[2:]
        q_heads = [*halves(own[3]), halves(own[4])[0]]
        k_heads = [*halves(own[0]), halves(own[1])[0]]
        v_heads = [halves(own[1])[1], *halves(own[2])]

        def column(at):
            return own_stats[:, at:at + 1] + own_stats[:, at + 1:at + 2] + own_stats[:, at + 2:at + 3]

        def row(at):
            return all_stats[at:at + 1] + all_stats[at + 1:at + 2] + all_stats[at + 2:at + 3]

        dq, dk, dv = [], [], []
        for head, (kb, vb) in enumerate(((0, 1), (0, 2), (1, 2))):
            qb, gb = (0, 0, 1)[head], (0, 1, 1)[head]
            probs = jnp.exp(mm_nt(q_heads[head], kv[kb]) * scale - column(3 * head))
            gap = mm_nt(g_heads[head], kv[vb]) - column(9 + 3 * head)
            dq.append(mm((probs * gap).astype(BF), kv[kb]) * scale)
            probs = jnp.exp(mm_nt(k_heads[head], query[qb]) * scale - row(3 * head))
            gap = mm_nt(v_heads[head], grad[gb]) - row(9 + 3 * head)
            dv.append(mm(probs.astype(BF), grad[gb]))
            dk.append(mm((probs * gap).astype(BF), query[qb]) * scale)
        tail = dq[2]
        gqkv_ref[...] = jnp.concatenate(
            [join(dk[0], dk[1]), join(dk[2], dv[0]), join(dv[1], dv[2]), join(dq[0], dq[1]),
             join(tail, jnp.zeros_like(tail))],
            axis=1,
        ).astype(BF)


    @pl.when(big)
    def _():
        run(5)

    @pl.when(jnp.logical_not(big))
    def _():
        run(1)

    wait_all(first_loads)

    grad_buf[...] = mm_tn(normed_buf[...], gqkv_ref[...])
    low = jnp.concatenate([ref[...] for ref in (low_buf, low1_ref, low2_ref, low3_ref)], axis=0)
    mixed = jnp.concatenate(
        [mixed_buf[pl.ds(pl.multiple_of((group ^ k) * BLK, BLK), BLK)] for k in range(4)], axis=0
    )
    out = mm_tn(mixed, low)[HD:]
    for ref, owner in ((keep_ref, core), (send_ref, 1 - core)):
        for tile in range(8):
            rows = grad_buf[pl.ds(pl.multiple_of((2 * tile + owner) * 48, 16), 48)]
            at = (tile // 4) * 96
            pieces = [
                out[at + row * 48:at + (row + 1) * 48, (tile % 4) * 192:(tile % 4 + 1) * 192] for row in range(2)
            ]
            ref[2 * tile] = rows[:, :384].astype(BF)
            ref[2 * tile + 1] = jnp.concatenate(
                [rows[:, 384:576], jnp.where(owner == 1, pieces[1], pieces[0])], axis=1
            ).astype(BF)
    wait_all(weight_copies(w_ref, w_out_ref, w_sem, start=False))


def normed_grad_kernel(
    gqkv_ref, w_ref, tok_ref, vec_ref, near_ref, far_ref, own_ref, one_ref, two_ref, three_ref, sums_ref, ff_ref,
    x_buf, vec_buf, near_buf, part_buf, low_buf, sums_buf, ff_buf, rows_buf, in_sem, out_sem, row_sem,
):
    loads = [
        pltpu.make_async_copy(tok_ref.at[lax.axis_index(MICRO)], x_buf, in_sem.at[0]),
        pltpu.make_async_copy(vec_ref, vec_buf, in_sem.at[1]),
        pltpu.make_async_copy(near_ref, near_buf, in_sem.at[2]),
    ]
    for load in loads:
        load.start()
    group = group_index()
    odd = (group % 2) == 1
    total = jnp.zeros((TOK, D), F32)
    for slot in range(3):
        part = gqkv_ref[:, slot * 192:(slot + 1) * 192]
        zero = jnp.zeros_like(part)
        wide = jnp.where(
            odd, jnp.concatenate([zero, part], axis=1), jnp.concatenate([part, zero], axis=1)
        )
        total = total + mm_nt(wide, w_ref[slot])
    part_buf[...] = total
    low_buf[...] = total.astype(BF)
    stores = []
    for k, ref in enumerate((own_ref, one_ref, two_ref, three_ref)):
        rows = pl.ds(pl.multiple_of((group ^ k) * BLK, BLK), BLK)
        target = ref.at[pl.ds(0, BLK)] if k else ref
        stores.append(pltpu.make_async_copy((low_buf if k else part_buf).at[rows], target, out_sem.at[k]))
        stores[-1].start()
    wait_all(loads)
    ff_buf[...] = (near_buf[...].astype(F32) + far_ref[...].astype(F32)).astype(BF)
    stores.append(pltpu.make_async_copy(ff_buf, ff_ref, out_sem.at[5]))
    stores[-1].start()
    unit, _ = normalized(x_buf[...].astype(F32))
    gain1 = jnp.sum(total * unit, axis=0, keepdims=True)
    shift1 = jnp.sum(total, axis=0, keepdims=True)
    vectors = jnp.concatenate([gain1, shift1, vec_buf[...][:2], jnp.zeros((4, D), F32)], axis=0)
    sums_buf[...] = vectors
    for index in range(4):
        rows_buf[index] = jnp.concatenate(
            [vectors[index:index + 1], jnp.zeros((15, D), F32)], axis=0
        ).astype(BF)
    for k, ref in enumerate((one_ref, two_ref, three_ref)):
        stores.append(
            pltpu.make_async_copy(rows_buf.at[group ^ (k + 1)], ref.at[pl.ds(BLK, 16)], row_sem.at[k])
        )
        stores[-1].start()
    stores.append(pltpu.make_async_copy(sums_buf, sums_ref, out_sem.at[4]))
    stores[-1].start()
    wait_all(stores)


def add_kernel(one_ref, two_ref, unused_ref, out_ref, buf, sem):
    buf[...] = (one_ref[...].astype(F32) + two_ref[...].astype(F32)).astype(BF)
    copy = pltpu.make_async_copy(buf, out_ref, sem)
    copy.start()
    copy.wait()


def sum_kernel(in_ref, vec_ref, one_ref, two_ref, three_ref, out_ref, buf, vec_buf, row_buf, sem, vec_sem, row_sem):
    loads = [pltpu.make_async_copy(vec_ref, vec_buf, vec_sem)] + [
        pltpu.make_async_copy(ref.at[pl.ds(BLK, 16)], row_buf.at[k], row_sem.at[k])
        for k, ref in enumerate((one_ref, two_ref, three_ref))
    ]
    for load in loads:
        load.start()
    total = in_ref[0].astype(F32)
    for index in range(1, 16):
        total = total + in_ref[index].astype(F32)
    wait_all(loads)
    vector = vec_buf[pl.ds(group_index(), 1)]
    for k in range(3):
        vector = vector + row_buf[k].astype(F32)[:1]
    rows = [vector[:, at:at + 128] for at in range(0, D, 128)] + [jnp.zeros((2, 128), F32)]
    pieces = [total[at:at + 8] for at in range(0, 48, 8)] + [jnp.concatenate(rows, axis=0)]
    block = jnp.concatenate(pieces, axis=1).astype(BF)
    for index in range(8):
        buf[index] = block
    wait_all(send_copies(buf, out_ref, range(8), sem))


def spread_kernel(turn, in_ref, *refs):
    qkv_buf, out_buf, sem, out_sem = refs[-4:]
    if turn:
        in_buf, in_sem = refs[-6:-4]
        qkv_ref, out_ref, *vec_refs = refs[3:-6]
        loads = [pltpu.make_async_copy(in_ref.at[tile], in_buf.at[tile], in_sem.at[tile]) for tile in range(8)]
        for load in loads:
            load.start()
    else:
        qkv_ref, out_ref, *vec_refs = refs[:-4]
        in_buf = in_ref
    owner = lax.axis_index(CORE)
    owner = 1 - owner if turn else owner
    copies = []
    vectors = [jnp.zeros((8, 128), F32)] * 4
    for tile in range(8):
        if turn:
            loads[tile].wait()
        whole = [in_buf[tile, index].astype(F32) for index in range(8)]
        block = [
            jnp.concatenate([value[:, at:at + 384] for at in range(0, 2304, 384)], axis=0) for value in whole
        ]
        vectors = [total + whole[k][:, 2304:] + whole[4 + k][:, 2304:] for k, total in enumerate(vectors)]
        for part, half, at in ((1, 0, 0), (2, 0, 192), (0, 4, 0)):
            qkv_buf[tile, :, part * D:(part + 1) * D] = jnp.concatenate(
                [block[half + group][:, at:at + 192] for group in range(4)], axis=1
            )
        start = pl.multiple_of((2 * tile + owner) * 48, 16)
        copy = pltpu.make_async_copy(qkv_buf.at[tile], qkv_ref.at[pl.ds(start, 48)], sem.at[tile])
        copy.start()
        copies.append(copy)
        for group in range(4):
            out_buf[group, tile // 4, :, (tile % 4) * 192:(tile % 4 + 1) * 192] = block[4 + group][:, 192:]
    for group in range(4):
        for pair in range(2):
            start = pl.multiple_of(group * 192 + (pair * 2 + owner) * 48, 16)
            copy = pltpu.make_async_copy(
                out_buf.at[group, pair], out_ref.at[pl.ds(start, 48)], out_sem.at[group, pair]
            )
            copy.start()
            copies.append(copy)
    if turn:
        for k, ref in enumerate(vec_refs):
            total = vectors[k] + refs[0][k]
            ref[...] = jnp.concatenate([total[row:row + 1] for row in range(6)], axis=1).reshape(D)
    else:
        for k, total in enumerate(vectors):
            vec_refs[0][k] = total
    wait_all(copies)


def spread_ff_kernel(*refs):
    up_ref, down_ref, up_buf, down_buf, up_sem, down_sem = refs[8:]
    y, core = lax.axis_index("y"), lax.axis_index(CORE)
    copies = []
    for near in range(4):
        for xl in range(2):
            chip = (y ^ near) * 2 + xl
            for index in (near, near + 4):
                owner = core ^ (index // 4)
                block = refs[index][xl].astype(F32)
                up_buf[near, xl, pl.ds(pl.multiple_of(owner * 48, 16), 48)] = block[:, :384]
                down_buf[near, xl, :, pl.ds(pl.multiple_of(owner * 384, 128), 384)] = block[:, 384:]
            for source, target, rows, sem in ((up_buf, up_ref, 96, up_sem), (down_buf, down_ref, 48, down_sem)):
                copy = pltpu.make_async_copy(
                    source.at[near, xl],
                    target.at[pl.ds(pl.multiple_of(chip * rows, 16), rows)],
                    sem.at[near, xl],
                )
                copy.start()
                copies.append(copy)
    wait_all(copies)


def input_kernel(
    own_ref, one_ref, two_ref, three_ref, tok_ref, gain_ref, grad_ref, result_ref, unused_ref, out_ref, buf, x_buf, sem, x_sem
):
    start = pl.multiple_of(group_index() * BLK, BLK)
    load = pltpu.make_async_copy(tok_ref.at[lax.axis_index(MICRO), pl.ds(start, BLK)], x_buf, x_sem)
    load.start()
    load.wait()
    total = own_ref[...]
    for ref in (one_ref, two_ref, three_ref):
        total = total + ref[:BLK].astype(F32)
    unit, inverse = normalized(x_buf[...].astype(F32))
    grad = grad_ref[...] + norm_back(total, unit, inverse, gain_ref[...].reshape(1, D))
    buf[:BLK] = grad.astype(BF)
    buf[BLK:] = result_ref[...]
    wait_all(send_copies(buf, out_ref, range(8), sem))


def unpack_kernel(in_ref, unused_ref, other_ref, grad_ref, result_ref):
    for index in range(8):
        rows = slice(index % 4 * BLK, (index % 4 + 1) * BLK)
        grad_ref[index // 4, rows] = in_ref[index, :BLK].astype(F32)
        result_ref[index // 4, rows] = in_ref[index, BLK:]


def exchange(value, axes):
    return lax.all_to_all(value, axes, 0, 0, tiled=True)


def swap(value):
    return lax.ppermute(value, CORE, [(0, 1), (1, 0)])


def after(value, *others):
    return pl.pallas_call(
        lambda *refs: None,
        out_shape=jax.ShapeDtypeStruct(value.shape, value.dtype),
        in_specs=[pl.BlockSpec(memory_space=pl.ANY)] * (1 + len(others)),
        out_specs=pl.BlockSpec(memory_space=pl.ANY),
        input_output_aliases={0: 0},
        cost_estimate=pl.CostEstimate(flops=1, bytes_accessed=1, transcendentals=0),
        compiler_params=pltpu.CompilerParams(vmem_limit_bytes=2**20),
    )(value, *others)


def flip(value, axes, count, bits):
    return lax.ppermute(value, axes, [(index, index ^ bits) for index in range(count)])


def shards(
    tokens, scene_of_block, ln1_gain, ln1_shift, w_qkv, w_out, ln2_gain, ln2_shift, w_up, w_down, out_grad
):
    w_out_pad = jnp.pad(w_out.reshape(4, 192, D), ((0, 0), (HD, 0), (0, 0)))
    kv_send, normed = call(
        project_kernel,
        [((8, TOK, 384), BF, "H"), ((TOK, D), BF, "L")],
        [(tokens, "H"), (ln1_gain, "H"), (ln1_shift, "H"), (w_qkv, "H")],
        1000,
        [
            pltpu.VMEM((TOK, D), BF), pltpu.VMEM((2, D, 384), BF), pltpu.VMEM((TOK, 384), BF),
            pltpu.VMEM((D,), F32), pltpu.VMEM((D,), F32), DMA, DMA((2,)), DMA((8,)), DMA, DMA,
        ],
    )
    (query,) = call(
        query_kernel,
        [((TOK, 256), BF, "L")],
        [(normed, "L"), (w_qkv, "H")],
        1000,
        [pltpu.VMEM((1, D, 384), BF), DMA((1,))],
    )
    kv_same = exchange(kv_send, CHIP)
    kv_same = after(kv_same, pin(query))
    kv_other = swap(kv_same)
    (mixed_send,) = call(
        attend_kernel,
        [((8, TOK, 256), BF, "H")],
        [(scene_of_block, "S"), (query, "H"), (kv_same, "V"), (kv_other, "V")],
        1000,
        [pltpu.VMEM((TOK, 256), BF), pltpu.VMEM((TOK, 256), BF), DMA((8,)), DMA],
    )
    mixed = exchange(mixed_send, NARROW)
    (block_query,) = call(
        block_query_kernel,
        [((4, BLK, 256), BF, "L")],
        [(normed, "H"), (w_qkv, "H")],
        1000,
        [pltpu.VMEM((BLK, D), BF), pltpu.VMEM((D, D), BF), DMA, DMA],
    )
    ff_send, middle, normed2, act, grad_pre = call(
        forward_kernel,
        [
            ((8, 2 * BLK, D), BF, "H"), ((BLK, D), F32, "H"), ((2 * TOK, D), BF, "V"),
            ((2 * TOK, FFL), BF, "V"), ((2 * TOK, FFL), BF, "V"),
        ],
        [
            (mixed, "V"), (tokens, "H"), (out_grad, "H"), (w_out_pad, "V"), (ln2_gain, "H"), (ln2_shift, "H"),
            (w_up, "H"), (w_down, "H"),
        ],
        1000,
        [
            pltpu.VMEM((2, TOK, D), BF), pltpu.VMEM((2, TOK, D), BF), pltpu.VMEM((D, FFL), BF),
            pltpu.VMEM((FFL, D), BF), pltpu.VMEM((D,), F32), pltpu.VMEM((D,), F32), pltpu.VMEM((8, BLK, D), BF),
            pltpu.VMEM((8, BLK, D), BF), pltpu.VMEM((8, BLK, D), F32), DMA((6,)), DMA((3,)),
        ],
    )
    ff_sums = exchange(ff_send, NARROW)
    keep, send = call(
        ff_grads_kernel,
        [((8, 48, D), BF, "V")] * 2,
        [(normed2, "V"), (act, "V"), (grad_pre, "V"), (out_grad, "L")],
        1000,
        [pltpu.VMEM((D, FFL), F32), pltpu.VMEM((FFL, D), F32)],
    )
    pieces = call(
        split_kernel, [((2, 48, D), BF, "L")] * 4, [(keep, "V"), (swap(send), "V")], 1000
    )
    pieces = [pieces[0]] + [flip(pieces[k], "y", 4, k) for k in (1, 2, 3)]
    (ff_near,) = call(
        total_kernel,
        [((2, 48, D), BF, "L")],
        [(pieces[0], "L")] + [(piece, "V") for piece in pieces[1:]],
        1000,
    )
    grad_send, low, grad_mid, result_part, vec2 = call(
        middle_kernel,
        [
            ((8, 4, 112, 128), BF, "H"), ((BLK, D), BF, "H"), ((BLK, D), F32, "H"), ((BLK, D), BF, "H"),
            ((8, D), F32, "H"),
        ],
        [
            (ff_sums, "V"), (middle, "H"), (out_grad, "H"), (mixed, "H"), (w_out_pad, "V"), (ln2_gain, "H"),
            (block_query, "H"),
        ],
        1000,
        [
            pltpu.VMEM((4, 112, 128), BF), pltpu.VMEM((BLK, D), F32), pltpu.VMEM((BLK, D), BF),
            pltpu.VMEM((4, BLK, 256), BF), pltpu.VMEM((D,), F32), pltpu.VMEM((4, BLK, 256), BF), pltpu.VMEM((BLK, D), BF), pltpu.VMEM((BLK, D), F32),
            pltpu.VMEM((BLK, D), BF), pltpu.VMEM((8, D), F32), DMA((5,)), DMA((8,)), DMA((4,)),
        ],
    )
    grad_send = after(pin(grad_send), *pieces[1:])
    grad_same = exchange(grad_send.reshape(32, 112, 128), (*CHIP, *GROUP)).reshape(8, 4, 112, 128)
    lows = [flip(low, GROUP, 4, k) for k in (1, 2, 3)]
    kv_same = after(pin(kv_same), low)
    kv_other = swap(kv_same)
    grad_same = after(grad_same, *lows, kv_other, pin(ff_near))
    grad_other = swap(grad_same)
    ff_near = after(pin(ff_near), grad_other)
    ff_far = flip(ff_near, "xl", 2, 1)
    gqkv, w_own, keep, send = call(
        attend_back_kernel,
        [((TOK, 640), BF, "V"), ((3, D, 384), BF, "V")] + [((16, 48, 384), BF, "V")] * 2,
        [
            (scene_of_block, "S"), (kv_same, "H"), (kv_other, "V"), (grad_same, "V"), (grad_other, "V"),
            (normed, "H"), (mixed, "H"), (low, "H"), *[(value, "V") for value in lows], (w_qkv, "H"),
        ],
        1000,
        [
            pltpu.VMEM((5, TOK, 384), BF), pltpu.VMEM((D, 640), F32),
            pltpu.VMEM((TOK, 256), BF), pltpu.VMEM((TOK, D), BF), pltpu.VMEM((BLK, D), BF),
            DMA, DMA((3,)), DMA((3,)),
        ],
        vmem=24,
    )
    own, *sends, sums, ff_part = call(
        normed_grad_kernel,
        [((BLK, D), F32, "H")] + [((BLK + 16, D), BF, "H")] * 3 + [((8, D), F32, "H"), ((2, 48, D), BF, "H")],
        [(gqkv, "V"), (w_own, "V"), (tokens, "H"), (vec2, "H"), (ff_near, "H"), (ff_far, "V")],
        1000,
        [
            pltpu.VMEM((TOK, D), BF), pltpu.VMEM((8, D), F32), pltpu.VMEM((2, 48, D), BF), pltpu.VMEM((TOK, D), F32),
            pltpu.VMEM((TOK, D), BF), pltpu.VMEM((8, D), F32), pltpu.VMEM((2, 48, D), BF), pltpu.VMEM((4, 16, D), BF),
            DMA((3,)), DMA((6,)), DMA((3,)),
        ],
    )
    (weight_send,) = call(
        add_kernel,
        [((16, 48, 384), BF, "H")],
        [(keep, "V"), (swap(after(send, ff_far)), "V"), (own, "H")],
        1000,
        [pltpu.VMEM((16, 48, 384), BF), DMA],
    )
    weight_parts = exchange(weight_send, (*CHIP, MICRO))
    parts = [flip(value, GROUP, 4, k + 1) for k, value in enumerate(sends)]
    weight_parts = after(weight_parts, pin(sums), *parts)
    ff_parts = [flip(ff_part, "y", 4, k) for k in (1, 2, 3)]
    (weight_total,) = call(
        sum_kernel,
        [((8, 8, 8, 2432), BF, "H")],
        [(weight_parts, "V"), (sums, "H"), *[(value, "A") for value in parts]],
        1000,
        [
            pltpu.VMEM((8, 8, 2432), BF), pltpu.VMEM((8, D), F32), pltpu.VMEM((3, 16, D), BF), DMA((8,)), DMA,
            DMA((3,)),
        ],
    )
    (packed,) = call(
        input_kernel,
        [((8, 2 * BLK, D), BF, "H")],
        [
            (own, "L"), *[(value, "V") for value in parts], (tokens, "H"), (ln1_gain, "L"), (grad_mid, "L"),
            (result_part, "L"), (weight_total, "H"),
        ],
        1000,
        [pltpu.VMEM((2 * BLK, D), BF), pltpu.VMEM((BLK, D), BF), DMA((8,)), DMA],
    )
    weight_same = exchange(weight_total.reshape(64, 8, 2432), (*CHIP, *NARROW)).reshape(8, 8, 8, 2432)
    weight_same = after(weight_same, pin(packed))
    everyone = exchange(after(pin(packed), weight_same), NARROW)
    weight_other = swap(weight_same)
    scratch = [
        pltpu.VMEM((8, 48, 3 * D), F32), pltpu.VMEM((4, 2, 48, D), F32), DMA((8,)), DMA((4, 2)),
    ]
    grads = [((D, 3 * D), F32, "H"), ((D, D), F32, "H")]
    half = call(
        functools.partial(spread_kernel, False),
        grads + [((4, 8, 128), F32, "V")],
        [(weight_same, "V")],
        1000,
        scratch,
    )
    qkv_grad, out_proj_grad, *vectors = call(
        functools.partial(spread_kernel, True),
        grads + [((D,), F32, "L")] * 4,
        [(weight_other, "H"), (half[2], "V"), (half[0], "H"), (half[1], "H")],
        1000,
        [pltpu.VMEM((8, 8, 8, 2432), BF), DMA((8,))] + scratch,
        aliases={2: 0, 3: 1},
    )
    ff_parts = [after(value, pin(vectors[0])) for value in ff_parts]
    ff_swapped = [swap(value) for value in (ff_part, *ff_parts)]
    up_grad, down_grad = call(
        spread_ff_kernel,
        [((D, FFL), F32, "H"), ((FFL, D), F32, "H")],
        [(ff_part, "L"), *[(value, "V") for value in ff_parts], *[(value, "V") for value in ff_swapped]],
        1000,
        [pltpu.VMEM((4, 2, 96, FFL), F32), pltpu.VMEM((4, 2, 48, D), F32), DMA((4, 2)), DMA((4, 2))],
    )
    input_grad, result = call(
        unpack_kernel, [((2, TOK, D), F32, "L"), ((2, TOK, D), BF, "L")], [(everyone, "V"), (vectors[0], "H"), (up_grad, "H")], 1000
    )
    return (
        result, input_grad, qkv_grad, out_proj_grad, *vectors, up_grad, down_grad
    )


def solution(mesh):
    names = ("y", "xl", "c", "zh", "zl", "xh")
    fine = Mesh(mesh.devices.reshape(4, 2, 2, 2, 2, 2), names)
    tokens = P(None, WIDE, None)
    placed = (
        tokens, P(), P(), P(), P(), P(), P(), P(), P(None, NARROW), P(NARROW, None), tokens
    )
    return jax.shard_map(
        shards,
        mesh=fine,
        in_specs=placed,
        out_specs=(
            tokens, tokens, P(), P(), P(), P(), P(), P(), P(None, NARROW), P(NARROW, None)
        ),
        check_vma=False,
    )
```
